32 devices in a mesh: dp: 8 (over z, y), segment: 4 (over x, core).
Axes of the slice: x: 2, y: 2, z: 4, core: 2. Of those that a mesh axis runs over, the one named last changes fastest.
Arguments:
- frames: bfloat16 [128, 7, 7, 512], P(('dp', 'segment')), may hold values from -15 to 15, as said below
- cotangent: bfloat16 [128, 7, 7, 512], P(('dp', 'segment')), may hold values from -6 to 6
- starts: int32 [128], P(('dp', 'segment')), may hold values 0 or 1
- space_kernel: float32 [4, 4608, 1152], P('segment', 'dp'), may hold values from -0.09375 to 0.09375
- time_kernel: float32 [4, 3456, 512], P('segment', 'dp'), may hold values from -0.109375 to 0.109375
- mid_gain: float32 [4, 1152], P('segment', 'dp'), may hold values from 0.5 to 1.5
- mid_bias: float32 [4, 1152], P('segment', 'dp'), may hold values from -3 to 3
- out_gain: float32 [4, 512], P('segment', 'dp'), may hold values from 0.5 to 1.5
- out_bias: float32 [4, 512], P('segment', 'dp'), may hold values from -3 to 3
Outputs:
- output: bfloat16 [128, 7, 7, 512], P(('dp', 'segment'))
- frames_grad: float32 [128, 7, 7, 512], P(('dp', 'segment'))
- space_grad: float32 [4, 4608, 1152], P('segment', 'dp')
- time_grad: float32 [4, 3456, 512], P('segment', 'dp')
- mid_gain_grad: float32 [4, 1152], P('segment', 'dp')
- mid_bias_grad: float32 [4, 1152], P('segment', 'dp')
- out_gain_grad: float32 [4, 512], P('segment', 'dp')
- out_bias_grad: float32 [4, 512], P('segment', 'dp')
The draws below stay inside these ranges and needn't reach their ends.
Inputs may be any that keep to these rules, and one draw needn't show every extreme that they name: `starts`: 1 marks the first frame of a clip. `frames`: normal or uniform values plus a per-channel offset, times a scale.
All inputs are finite; a program needn't handle non-finite values. No bound on the sum of `starts` on one device may be relied on, other than what follows from the above.
Results may differ from the reference program's by a relative error of at most 0.024.
Values may be sent and summed in bfloat16 or wider, within the bound.
No kernel may reach another device: no remote copies, remote signals or barrier semaphores. Data moves between devices by JAX's collectives and lax.ppermute only.
A program may use at most 256 MiB of HBM per device.

```python
import jax
import jax.numpy as jnp
from jax import lax

D = 512
FF = 1152
SIDE = 7
FR = 4
MICRO = 4
FRAMES = 128
N_DP = 8
N_SEGMENT = 4


def draw_frames(key, part):
    key = jax.random.fold_in(key, 11)
    first_key, second_key = jax.random.split(key)
    noise = jnp.clip(jax.random.normal(first_key, (FRAMES, SIDE, SIDE, D), jnp.float32), -4.0, 4.0)
    offset = jnp.clip(0.5 * jax.random.normal(second_key, (D,), jnp.float32), -1.0, 1.0)
    ramp = jnp.exp(jnp.log(3.0) * jnp.arange(FRAMES, dtype=jnp.float32) / FRAMES)
    return (ramp[:, None, None, None] * (noise + offset)).astype(jnp.bfloat16)


def place_ends(values, stream_key, least, top_value):
    spot = [jax.random.randint(jax.random.fold_in(stream_key, axis), (), 0, length) for axis, length in enumerate(values.shape)]
    widest = values.shape.index(max(values.shape))
    neighbour = spot[:widest] + [(spot[widest] + 1) % values.shape[widest]] + spot[widest + 1:]
    return values.at[tuple(spot)].set(least).at[tuple(neighbour)].set(top_value)


def steps_of(rng, extent, shards, least, top_value):
    loudness, own = 1.0, jax.random.fold_in(rng, 6)
    for axis_at, shards_of in shards:
        heights = jnp.exp(jax.random.uniform(jax.random.fold_in(own, axis_at), (shards_of,), jnp.float32, least / len(shards), top_value / len(shards)))
        loudness = loudness * jnp.repeat(heights, extent[axis_at] // shards_of).reshape([-1 if axis == axis_at else 1 for axis in range(len(extent))])
    return loudness


def gaussian(own_key, shape, scale, reach, cuts=(), kind=jnp.bfloat16):
    values = jax.random.normal(own_key, shape, jnp.float32) * scale
    if len(cuts) > 0:
        values = steps_of(own_key, shape, cuts, -0.22, 0.18) * values
    return jnp.clip(values, min=-reach, max=reach).astype(kind)


def setup_inputs(seed: int = 0) -> dict:
    splits = jax.random.split(jax.random.key(seed), 10)
    return {
        "frames": draw_frames(jax.random.fold_in(splits[9], 71), 0),
        "cotangent": gaussian(splits[1], (FRAMES, SIDE, SIDE, D), 1.0, 6.0, ((0, 32),)),
        "starts": place_ends((jax.random.randint(splits[2], (FRAMES,), 0, 3) < 1).astype(jnp.int32), jax.random.fold_in(splits[2], 1), 0, 1),
        "space_kernel": gaussian(splits[3], (N_SEGMENT, 9 * D, FF), (9 * D) ** -0.5, 0.09375, ((0, 4), (1, 8)), jnp.float32),
        "time_kernel": gaussian(splits[4], (N_SEGMENT, 3 * FF, D), (3 * FF) ** -0.5, 0.109375, ((0, 4), (1, 8)), jnp.float32),
        "mid_gain": jnp.clip(1.0 + 0.1 * jax.random.normal(splits[5], (N_SEGMENT, FF), jnp.float32), 0.5, 1.5),
        "mid_bias": gaussian(splits[6], (N_SEGMENT, FF), 0.5, 3.0, ((0, 4), (1, 8)), jnp.float32),
        "out_gain": jnp.clip(1.0 + 0.1 * jax.random.normal(splits[7], (N_SEGMENT, D), jnp.float32), 0.5, 1.5),
        "out_bias": gaussian(splits[8], (N_SEGMENT, D), 0.5, 3.0, ((0, 4), (1, 8)), jnp.float32),
    }


@jax.custom_vjp
def low(v):
    return lax.optimization_barrier(v.astype(jnp.bfloat16)).astype(jnp.float32)

@jax.custom_vjp
def low_back(v):
    return v

def low_keep(v):
    return (low(v), None)

def low_pass(kept, grad):
    return (grad,)

def back_keep(v):
    return (v, None)

def back_low(kept, grad):
    return (low(grad),)
low.defvjp(low_keep, low_pass)
low_back.defvjp(back_keep, back_low)
HIGHEST = lax.Precision.HIGHEST
eps = 1e-05

def space_conv(current, kernel):
    frame_side = current.shape[1]
    padded = jnp.pad(current, ((0, 0), (1, 1), (1, 1), (0, 0)))
    stacked = jnp.concatenate([padded[:, row_shift:row_shift + frame_side, col_shift:col_shift + frame_side, :] for row_shift in range(3) for col_shift in range(3)], axis=-1)
    return jnp.einsum('fijc,co->fijo', stacked, kernel, precision=HIGHEST)

def time_conv(current, kernel, before_mask, after_mask):
    blanks = jnp.zeros_like(current[:1])
    earlier = jnp.concatenate([blanks, current[:-1]], axis=0) * before_mask[:, None, None, None]
    later = jnp.concatenate([current[1:], blanks], axis=0) * after_mask[:, None, None, None]
    stacked = jnp.concatenate([earlier, current, later], axis=-1)
    return jnp.einsum('fijc,co->fijo', stacked, kernel, precision=HIGHEST)

def normalize(values, gain_now, bias_now):
    average = lax.optimization_barrier(jnp.mean(values, axis=(0, 1, 2)))
    centered = values - average
    spread = lax.optimization_barrier(jnp.mean(centered * centered, axis=(0, 1, 2)))
    return centered * lax.rsqrt(spread + eps) * gain_now + bias_now

def forward(frames, space_kernel, time_kernel, mid_gain, mid_bias, out_gain, out_bias, before_mask, after_mask):
    space_low = low(space_kernel)
    time_low = low(time_kernel)
    mid_gain_low = low(mid_gain)
    mid_bias_low = low(mid_bias)
    out_gain_low = low(out_gain)
    out_bias_low = low(out_bias)
    shaped = frames.reshape(N_DP, MICRO, FR, SIDE, SIDE, D)
    collected = []
    for micro_index in range(MICRO):
        current = shaped[:, micro_index].reshape(N_DP * FR, SIDE, SIDE, D)
        before_now = before_mask[:, micro_index].reshape(N_DP * FR)
        after_now = after_mask[:, micro_index].reshape(N_DP * FR)
        skip_input = current
        for section in range(N_SEGMENT):
            spatial = low_back(space_conv(current, space_low[section]))
            hidden_act = low(jax.nn.silu(normalize(spatial, mid_gain_low[section], mid_bias_low[section])))
            temporal = low_back(time_conv(hidden_act, time_low[section], before_now, after_now))
            pre_act = normalize(temporal, out_gain_low[section], out_bias_low[section])
            if section % 2 == 1:
                pre_act = pre_act + low_back(skip_input)
            result = low(jax.nn.silu(pre_act))
            if section % 2 == 1:
                skip_input = result
            if section < N_SEGMENT - 1:
                current = low_back(result)
            else:
                current = result
        collected.append(current.reshape(N_DP, FR, SIDE, SIDE, D))
    return jnp.stack(collected, axis=1).reshape(N_DP * MICRO * FR, SIDE, SIDE, D)

def reference(frames, cotangent, starts, space_kernel, time_kernel, mid_gain, mid_bias, out_gain, out_bias):
    clip_flags = starts.reshape(N_DP, MICRO, FR)
    positions = jnp.arange(FR)
    before_mask = jnp.where((clip_flags == 1) | (positions == 0), 0.0, 1.0).astype(jnp.float32)
    following = jnp.concatenate([clip_flags[:, :, 1:], jnp.ones((N_DP, MICRO, 1), jnp.int32)], axis=2)
    after_mask = jnp.where(following == 1, 0.0, 1.0).astype(jnp.float32)

    def run_blocks(inputs_now, space_now, time_now, mid_gain_now, mid_bias_now, out_gain_now, out_bias_now):
        return forward(inputs_now, space_now, time_now, mid_gain_now, mid_bias_now, out_gain_now, out_bias_now, before_mask, after_mask)
    output, pullback = jax.vjp(run_blocks, frames.astype(jnp.float32), space_kernel, time_kernel, mid_gain, mid_bias, out_gain, out_bias)
    grads = pullback(cotangent.astype(jnp.float32))
    return (output.astype(jnp.bfloat16), grads[0], grads[1], grads[2], grads[3], grads[4], grads[5], grads[6])
```

```python
import jax
import jax.numpy as jnp
from jax import lax
from jax.sharding import Mesh, PartitionSpec as P

eps = 1e-05
PLANE = ("y", "x", "c")
EVERY = ("z", "y", "x", "c")
BF = jnp.bfloat16
F32 = jnp.float32


def pack(v):
    half = v.shape[0] // 2
    return jnp.concatenate([v[:half], v[half:]], axis=1)


def unpack(v):
    half = v.shape[1] // 2
    return jnp.concatenate([v[:, :half], v[:, half:]], axis=0)


def unpack_all(g):
    return jnp.concatenate([unpack(g[i]) for i in range(g.shape[0])], axis=1)


def pack_all(v, ranks):
    w = v.shape[1] // ranks
    return jnp.stack([pack(v[:, i * w : (i + 1) * w]) for i in range(ranks)])


def slope(v):
    s = jax.nn.sigmoid(v)
    return s * (1.0 + v * (1.0 - s))


def taps_of(a, side):
    frames, ch = a.shape[0] // (side * side), a.shape[1]
    padded = jnp.pad(a.reshape(side, side, frames, ch), ((1, 1), (1, 1), (0, 0), (0, 0)))
    return [
        padded[r : r + side, c : c + side].reshape(a.shape[0], ch) for r in range(3) for c in range(3)
    ]


def nt(a, b):
    return lax.dot_general(a, b, (((1,), (1,)), ((), ())), preferred_element_type=F32)


def nn(a, b):
    return lax.dot_general(a, b, (((1,), (0,)), ((), ())), preferred_element_type=F32)


def tn(a, b):
    return lax.dot_general(a, b, (((0,), (0,)), ((), ())), preferred_element_type=F32)


def fwd_a(a, kt, lt, gain, bias, before, after, side):
    stacked = jnp.concatenate(taps_of(a, side), axis=1)
    spatial = nt(stacked, kt)
    mean = jnp.mean(spatial, axis=0)
    cen = spatial - mean
    rs = lax.rsqrt(jnp.mean(cen * cen, axis=0) + eps)
    xhat = cen * rs
    hidden = jax.nn.silu(xhat * gain + bias)
    n = lt.shape[0] // 3
    prev = (jnp.roll(hidden, 1, axis=0) * before).astype(BF)
    here = hidden.astype(BF)
    nxt = (jnp.roll(hidden, -1, axis=0) * after).astype(BF)
    part = nn(prev, lt[:n]) + nn(here, lt[n : 2 * n]) + nn(nxt, lt[2 * n :])
    return here, xhat, rs, part


def fwd_b(recv, gain, bias, skip):
    temporal = unpack(jnp.sum(recv.astype(F32), axis=0))
    mean = jnp.mean(temporal, axis=0)
    cen = temporal - mean
    rs = lax.rsqrt(jnp.mean(cen * cen, axis=0) + eps)
    xhat = cen * rs
    pre = xhat * gain + bias
    if skip is not None:
        pre = pre + skip.astype(F32)
    return xhat, rs, pre, jax.nn.silu(pre).astype(BF)


def bwd_a(g, pre, xhat, rs, gain):
    dpre = g * slope(pre)
    n = dpre.shape[0]
    sb, sg = jnp.sum(dpre, axis=0), jnp.sum(dpre * xhat, axis=0)
    dt = (gain * rs * (dpre - sb / n - xhat * (sg / n))).astype(BF)
    return dpre, dt, sg, sb


def bwd_b(dt, xhat, rs, kt, lt, gain, bias, before, after, side):
    n = lt.shape[0] // 3
    pixels, frames = dt.shape[0], dt.shape[0] // (side * side)
    early = nt(dt, lt[:n]) * before
    late = nt(dt, lt[2 * n :]) * after
    dh = nt(dt, lt[n : 2 * n]) + jnp.roll(early, -1, axis=0) + jnp.roll(late, 1, axis=0)
    dy = dh * slope(xhat * gain + bias)
    sb, sg = jnp.sum(dy, axis=0), jnp.sum(dy * xhat, axis=0)
    ds = (gain * rs * (dy - sb / pixels - xhat * (sg / pixels))).astype(BF)
    ch = kt.shape[1] // 9
    taps = taps_of(ds, side)
    part = sum(nn(taps[8 - t], kt[:, t * ch : (t + 1) * ch]) for t in range(9))
    return ds, part, sg, sb


def bwd_c(a, hidden, ds, dt, before, after, side):
    h32 = hidden.astype(F32)
    prev = (jnp.roll(h32, 1, axis=0) * before).astype(BF)
    nxt = (jnp.roll(h32, -1, axis=0) * after).astype(BF)
    tgrad = jnp.concatenate([tn(prev, dt), tn(hidden, dt), tn(nxt, dt)], axis=0)
    sgrad = jnp.concatenate([tn(ds, t) for t in taps_of(a, side)], axis=1)
    return sgrad, tgrad


def on_device(frames, cot, starts, ks, ktm, mg, mb, og, ob):
    nz, n_rank, n_seg = lax.axis_size("z"), 8, 4
    n_dp = nz * 2
    fr, side, ch = frames.shape[0], frames.shape[1], frames.shape[3]
    area = side * side
    hid = ks.shape[2]
    hc, cc = hid // n_rank, ch // n_rank
    q = hc // n_rank
    z = lax.axis_index("z")
    rank = lax.axis_index(PLANE)
    d_index = lax.axis_index(("z", "y"))
    s_index = lax.axis_index(("x", "c"))
    nf = n_dp * fr

    small = jnp.concatenate(
        [v[0].astype(BF).astype(F32) for v in (mg, mb, og, ob)] + [starts.astype(F32)]
    )
    small = lax.all_gather(small, EVERY, axis=0).reshape(n_dp, n_seg, -1)
    w_mid, w_out = mg.shape[1], og.shape[1]

    def mid_vec(section, first):
        full = small[:, section, first : first + w_mid].reshape(n_rank, n_rank, q)
        return lax.dynamic_index_in_dim(full, rank, 1, keepdims=False).reshape(hc)

    def out_vec(section, first):
        full = small[:, section, first : first + w_out].reshape(n_rank, cc)
        return lax.dynamic_index_in_dim(full, rank, 0, keepdims=False)

    flags = lax.dynamic_index_in_dim(small[:, :, 2 * w_mid + 2 * w_out :], z, 1, keepdims=False)
    flags = flags.reshape(nf) > 0.5
    slot = jnp.arange(nf) % fr
    before = jnp.where(flags | (slot == 0), 0.0, 1.0)
    after = jnp.where(jnp.roll(flags, -1) | (slot == fr - 1), 0.0, 1.0)
    before = jnp.tile(before, area)[:, None]
    after = jnp.tile(after, area)[:, None]

    perm = (jnp.arange(hid).reshape(n_rank, n_rank, q).transpose(1, 0, 2).reshape(hid)[:, None]
            == jnp.arange(hid)[None, :]).astype(BF)
    kt = lax.dot_general(perm, ks[0].astype(BF), (((1,), (1,)), ((), ())),
                         preferred_element_type=F32).astype(BF)
    kt = kt.reshape(n_rank, hc, ks.shape[1])
    kt = lax.all_to_all(kt, PLANE, 0, 0)
    kt = kt.reshape(2, n_seg, hc, ks.shape[1]).transpose(1, 2, 0, 3).reshape(n_seg, hc, -1)
    lt = ktm[0].astype(BF).reshape(-1, n_rank, q, ch).transpose(1, 0, 2, 3).reshape(n_rank, -1, ch)
    lt = lax.all_to_all(lt, PLANE, 0, 0)
    lt = lt.reshape(2, n_seg, -1, ch).transpose(1, 0, 2, 3).reshape(n_seg, -1, ch)
    kts, lts = [], []
    for s in range(n_seg):
        kts.append(lax.all_gather(kt[s], "z", axis=0).transpose(1, 0, 2).reshape(hc, -1))
        lts.append(lax.all_gather(lt[s], "z", axis=0, tiled=True))

    to_plane = [(d * n_seg + s, s * n_rank + d) for d in range(n_dp) for s in range(n_seg)]
    from_plane = [(b, a) for a, b in to_plane]

    def whole(v):
        v = lax.ppermute(v.reshape(fr, area, ch).transpose(1, 0, 2), EVERY, to_plane)
        v = lax.all_gather(v, PLANE, axis=0)
        return v.transpose(1, 0, 2, 3).reshape(area * nf, ch)

    def own_channels(v):
        return lax.dynamic_slice_in_dim(v, rank * cc, cc, axis=1)

    def scatter_sum(part):
        sent = pack_all(part.astype(BF), n_rank)
        return lax.all_to_all(sent, PLANE, 0, 0)

    a = whole(frames)
    cot_own = own_channels(whole(cot)).astype(F32)
    skip = own_channels(a)
    saved = []
    for s in range(n_seg):
        gm, bm = mid_vec(s, 0), mid_vec(s, w_mid)
        go, bo = out_vec(s, 2 * w_mid), out_vec(s, 2 * w_mid + w_out)
        hidden, xm, rm, part = fwd_a(a, kts[s], lts[s], gm, bm, before, after, side)
        recv = scatter_sum(part)
        xo, ro, pre, res = fwd_b(recv, go, bo, skip if s % 2 == 1 else None)
        saved.append((a, hidden, xm, rm, xo, ro, pre, gm, bm, go))
        if s % 2 == 1:
            skip = res
        a = unpack_all(lax.all_gather(pack(res), PLANE, axis=0))

    def own_frames(v):
        v = v.reshape(area, n_dp, fr, ch)
        v = lax.dynamic_index_in_dim(v, rank, 1, keepdims=False)
        v = lax.ppermute(v, EVERY, from_plane)
        return v.transpose(1, 0, 2).reshape(fr, side, side, ch)

    output = own_frames(a)

    g = cot_own
    skip_grad = None
    sgrads, tgrads, vecs = [], [], []
    for s in reversed(range(n_seg)):
        a, hidden, xm, rm, xo, ro, pre, gm, bm, go = saved[s]
        dpre, dt, og_g, ob_g = bwd_a(g, pre, xo, ro, go)
        if s % 2 == 1:
            skip_grad = dpre.astype(BF).astype(F32)
        dtf = unpack_all(lax.all_gather(pack(dt), PLANE, axis=0))
        ds, part, mg_g, mb_g = bwd_b(dtf, xm, rm, kts[s], lts[s], gm, bm, before, after, side)
        sg, tg = bwd_c(a, hidden, ds, dtf, before, after, side)
        sg = sg.astype(BF).reshape(hc, nz, -1).transpose(1, 0, 2)
        tg = tg.astype(BF).reshape(nz, -1, ch)
        sgrads.append(lax.psum_scatter(sg, "z", scatter_dimension=0))
        tgrads.append(lax.psum_scatter(tg, "z", scatter_dimension=0))
        vecs.append(jnp.concatenate([mg_g, mb_g, og_g, ob_g]))
        if s > 0:
            recv = scatter_sum(part)
            g = unpack(jnp.sum(recv.astype(F32), axis=0))
            if s == 2:
                g = g + skip_grad
        else:
            whole_part = jnp.concatenate(
                [lax.dynamic_update_slice_in_dim(jnp.zeros_like(part), skip_grad, rank * cc, axis=1)])
            part = part + whole_part
            part = part.astype(BF).reshape(area, n_dp, fr, ch).transpose(1, 0, 2, 3)
            recv = lax.all_to_all(part, PLANE, 0, 0)
            da = jnp.sum(recv.astype(F32), axis=0).astype(BF)
            da = lax.ppermute(da, EVERY, from_plane)
            frames_grad = da.transpose(1, 0, 2).reshape(fr, side, side, ch).astype(F32)

    sgrads, tgrads, vecs = [jnp.stack(v[::-1]) for v in (sgrads, tgrads, vecs)]
    sg = sgrads.reshape(n_seg, hc, 2, -1).transpose(2, 0, 1, 3).reshape(n_rank, hc, -1)
    sg = lax.all_to_all(sg, PLANE, 0, 0).reshape(hid, -1)
    space_grad = lax.dot_general(sg, perm, (((0,), (0,)), ((), ())), preferred_element_type=F32)
    tg = tgrads.reshape(n_seg, 2, -1, ch).transpose(1, 0, 2, 3).reshape(n_rank, -1, ch)
    tg = lax.all_to_all(tg, PLANE, 0, 0)
    time_grad = tg.reshape(n_rank, -1, q, ch).transpose(1, 0, 2, 3).reshape(-1, ch).astype(F32)
    vecs = lax.all_gather(vecs, EVERY, axis=0).reshape(nz, n_rank, n_seg, -1)
    vecs = jnp.sum(lax.dynamic_index_in_dim(vecs, s_index, 2, keepdims=False), axis=0)

    def mid_own(first):
        v = vecs[:, first : first + hc].reshape(n_rank, n_rank, q)
        return lax.dynamic_index_in_dim(v, d_index, 1, keepdims=False).reshape(1, hc)

    def out_own(first):
        v = vecs[:, first : first + cc]
        return lax.dynamic_index_in_dim(v, d_index, 0, keepdims=True)

    return (
        output,
        frames_grad,
        space_grad[None],
        time_grad[None],
        mid_own(0),
        mid_own(hc),
        out_own(2 * hc),
        out_own(2 * hc + cc),
    )


def from_behind(value, axis, steps):
    count = lax.axis_size(axis)
    leading, last = (max(0, -steps), min(count, count - steps))
    return lax.ppermute(value, axis, [(source, source + steps) for source in range(leading, last)])


def space_apply(current, kernel):
    frame_side = current.shape[1]
    padded = jnp.pad(current, ((0, 0), (1, 1), (1, 1), (0, 0)))
    stacked = jnp.concatenate(
        [
            padded[:, row_shift : row_shift + frame_side, col_shift : col_shift + frame_side, :]
            for row_shift in range(3)
            for col_shift in range(3)
        ],
        axis=-1,
    )
    return (
        stacked,
        jnp.einsum("fijc,co->fijo", stacked, kernel, preferred_element_type=jnp.float32),
    )


def space_back(gradient, kernel):
    frame_side = gradient.shape[1]
    channels = kernel.shape[0] // 9
    spread = jnp.einsum("fijo,co->fijc", gradient, kernel, preferred_element_type=jnp.float32)
    total = jnp.zeros((gradient.shape[0], frame_side + 2, frame_side + 2, channels), jnp.float32)
    for tap_index in range(9):
        row_shift = tap_index // 3
        col_shift = tap_index % 3
        piece_now = spread[..., tap_index * channels : (tap_index + 1) * channels]
        total = total + jnp.pad(
            piece_now, ((0, 0), (row_shift, 2 - row_shift), (col_shift, 2 - col_shift), (0, 0))
        )
    return total[:, 1 : frame_side + 1, 1 : frame_side + 1, :]


def time_apply(current, kernel, before_mask, after_mask):
    blanks = jnp.zeros_like(current[:1])
    earlier = jnp.concatenate([blanks, current[:-1]], axis=0) * before_mask[
        :, None, None, None
    ].astype(current.dtype)
    later = jnp.concatenate([current[1:], blanks], axis=0) * after_mask[:, None, None, None].astype(
        current.dtype
    )
    stacked = jnp.concatenate([earlier, current, later], axis=-1)
    return (
        stacked,
        jnp.einsum("fijc,co->fijo", stacked, kernel, preferred_element_type=jnp.float32),
    )


def time_back(gradient, kernel, before_mask, after_mask):
    channels = kernel.shape[0] // 3
    spread = jnp.einsum("fijo,co->fijc", gradient, kernel, preferred_element_type=jnp.float32)
    early_part = spread[..., :channels] * before_mask[:, None, None, None]
    late_part = spread[..., 2 * channels :] * after_mask[:, None, None, None]
    blanks = jnp.zeros_like(early_part[:1])
    moved_early = jnp.concatenate([early_part[1:], blanks], axis=0)
    moved_late = jnp.concatenate([blanks, late_part[:-1]], axis=0)
    return spread[..., channels : 2 * channels] + moved_early + moved_late


def moments(values, pixel_count):
    average = lax.psum(jnp.sum(values, axis=(0, 1, 2)), "dp") / pixel_count
    centered = values - average
    spread = lax.psum(jnp.sum(centered * centered, axis=(0, 1, 2)), "dp") / pixel_count
    return (average, lax.rsqrt(spread + eps))


def reduce_back(gradient, normed):
    return lax.psum(
        (jnp.sum(gradient, axis=(0, 1, 2)), jnp.sum(gradient * normed, axis=(0, 1, 2))), "dp"
    )


def silu_slope(values):
    sigmoid_now = jax.nn.sigmoid(values)
    return sigmoid_now * (1.0 + values * (1.0 - sigmoid_now))


def pick_slot(stack, slot_index):
    return lax.dynamic_index_in_dim(stack, slot_index, 0, keepdims=False)


def store_slot(stack, value, slot_index, usable):
    previous = pick_slot(stack, slot_index)
    return lax.dynamic_update_index_in_dim(stack, jnp.where(usable, value, previous), slot_index, 0)


def on_device_general(
    frames, cotangent, starts, space_kernel, time_kernel, mid_gain, mid_bias, out_gain, out_bias
):
    n_segment = lax.axis_size("segment")
    n_data = lax.axis_size("dp")
    segment_index = lax.axis_index("segment")
    odd_segment = segment_index % 2 == 1
    last_segment = segment_index == n_segment - 1
    first_segment = segment_index == 0
    frame_count = frames.shape[0]
    frame_side = frames.shape[1]
    channels = frames.shape[3]
    hidden_units = mid_gain.shape[1] * n_data
    pixel_count = n_data * frame_count * frame_side * frame_side
    turns = 2 * n_segment - 1
    block_shape = (n_segment,) + frames.shape
    all_frames, all_cot, all_starts = (
        lax.all_gather(frames, "segment", axis=0, tiled=True),
        lax.all_gather(cotangent, "segment", axis=0, tiled=True),
        lax.all_gather(starts.astype(jnp.bfloat16), "segment", axis=0, tiled=True),
    )
    frame_stack = all_frames.reshape(block_shape)
    cot_stack = all_cot.reshape(block_shape)
    clip_flags = all_starts.astype(jnp.float32).reshape(n_segment, frame_count)
    positions = jnp.arange(frame_count)
    before_mask = jnp.where((clip_flags > 0.5) | (positions == 0), 0.0, 1.0)
    following = jnp.concatenate([clip_flags[:, 1:], jnp.ones((n_segment, 1), jnp.float32)], axis=1)
    after_mask = jnp.where(following > 0.5, 0.0, 1.0)
    gathered = (
        lax.all_gather(space_kernel[0].astype(jnp.bfloat16), "dp", axis=0, tiled=True),
        lax.all_gather(time_kernel[0].astype(jnp.bfloat16), "dp", axis=0, tiled=True),
        lax.all_gather(mid_gain[0].astype(jnp.bfloat16), "dp", axis=0, tiled=True),
        lax.all_gather(mid_bias[0].astype(jnp.bfloat16), "dp", axis=0, tiled=True),
        lax.all_gather(out_gain[0].astype(jnp.bfloat16), "dp", axis=0, tiled=True),
        lax.all_gather(out_bias[0].astype(jnp.bfloat16), "dp", axis=0, tiled=True),
    )
    space_low, time_low = (gathered[0], gathered[1])
    mid_gain_now = gathered[2].astype(jnp.float32)
    mid_bias_now = gathered[3].astype(jnp.float32)
    out_gain_now = gathered[4].astype(jnp.float32)
    out_bias_now = gathered[5].astype(jnp.float32)
    incoming = jnp.zeros_like(frames)
    carried = jnp.zeros_like(frames)
    kept_input = jnp.zeros(block_shape, jnp.bfloat16)
    kept_skip = jnp.zeros(block_shape, jnp.bfloat16)
    kept_mid_mean = jnp.zeros((n_segment, hidden_units), jnp.float32)
    kept_mid_scale = jnp.zeros((n_segment, hidden_units), jnp.float32)
    kept_out_mean = jnp.zeros((n_segment, channels), jnp.float32)
    kept_out_scale = jnp.zeros((n_segment, channels), jnp.float32)
    results = jnp.zeros(block_shape, jnp.float32)
    for turn_index in range(turns):
        micro_index = turn_index - segment_index
        usable = (micro_index >= 0) & (micro_index < n_segment)
        slot_index = jnp.clip(micro_index, 0, n_segment - 1)
        current = jnp.where(first_segment, pick_slot(frame_stack, slot_index), incoming)
        skip_input = carried
        _, spatial = space_apply(current, space_low)
        mid_mean, mid_scale = moments(spatial, pixel_count)
        hidden_act = jax.nn.silu(
            (spatial - mid_mean) * mid_scale * mid_gain_now + mid_bias_now
        ).astype(jnp.bfloat16)
        _, temporal = time_apply(
            hidden_act,
            time_low,
            pick_slot(before_mask, slot_index),
            pick_slot(after_mask, slot_index),
        )
        out_mean, out_scale = moments(temporal, pixel_count)
        pre_act = (
            (temporal - out_mean) * out_scale * out_gain_now
            + out_bias_now
            + jnp.where(odd_segment, skip_input.astype(jnp.float32), 0.0)
        )
        result = jax.nn.silu(pre_act).astype(jnp.bfloat16)
        kept_input = store_slot(kept_input, current, slot_index, usable)
        kept_skip = store_slot(kept_skip, skip_input, slot_index, usable)
        kept_mid_mean = store_slot(kept_mid_mean, mid_mean, slot_index, usable)
        kept_mid_scale = store_slot(kept_mid_scale, mid_scale, slot_index, usable)
        kept_out_mean = store_slot(kept_out_mean, out_mean, slot_index, usable)
        kept_out_scale = store_slot(kept_out_scale, out_scale, slot_index, usable)
        results = store_slot(results, result.astype(jnp.float32), slot_index, usable)
        if turn_index < turns - 1:
            incoming, carried = from_behind(
                (result, jnp.where(odd_segment, result, current)), "segment", 1
            )
    gathered = (
        lax.all_gather(space_kernel[0].astype(jnp.bfloat16), "dp", axis=0, tiled=True),
        lax.all_gather(time_kernel[0].astype(jnp.bfloat16), "dp", axis=0, tiled=True),
        lax.all_gather(mid_gain[0].astype(jnp.bfloat16), "dp", axis=0, tiled=True),
        lax.all_gather(mid_bias[0].astype(jnp.bfloat16), "dp", axis=0, tiled=True),
        lax.all_gather(out_gain[0].astype(jnp.bfloat16), "dp", axis=0, tiled=True),
        lax.all_gather(out_bias[0].astype(jnp.bfloat16), "dp", axis=0, tiled=True),
    )
    space_low, time_low = (gathered[0], gathered[1])
    mid_gain_now = gathered[2].astype(jnp.float32)
    mid_bias_now = gathered[3].astype(jnp.float32)
    out_gain_now = gathered[4].astype(jnp.float32)
    out_bias_now = gathered[5].astype(jnp.float32)
    grad_input = jnp.zeros_like(frames)
    grad_skip = jnp.zeros_like(frames)
    space_acc = jnp.zeros(space_low.shape, jnp.float32)
    time_acc = jnp.zeros(time_low.shape, jnp.float32)
    mid_gain_acc = jnp.zeros((hidden_units,), jnp.float32)
    mid_bias_acc = jnp.zeros((hidden_units,), jnp.float32)
    out_gain_acc = jnp.zeros((channels,), jnp.float32)
    out_bias_acc = jnp.zeros((channels,), jnp.float32)
    input_grads = jnp.zeros(block_shape, jnp.float32)
    for turn_index in range(turns):
        micro_index = n_segment - 1 - (turn_index - (n_segment - 1 - segment_index))
        usable = (micro_index >= 0) & (micro_index < n_segment)
        usable_weight = usable.astype(jnp.float32)
        slot_index = jnp.clip(micro_index, 0, n_segment - 1)
        current = pick_slot(kept_input, slot_index)
        skip_input = pick_slot(kept_skip, slot_index)
        before_now = pick_slot(before_mask, slot_index)
        after_now = pick_slot(after_mask, slot_index)
        space_taps, spatial = space_apply(current, space_low)
        mid_normed = (spatial - pick_slot(kept_mid_mean, slot_index)) * pick_slot(
            kept_mid_scale, slot_index
        )
        mid_pre = mid_normed * mid_gain_now + mid_bias_now
        hidden_act = jax.nn.silu(mid_pre).astype(jnp.bfloat16)
        time_taps, temporal = time_apply(hidden_act, time_low, before_now, after_now)
        out_scale = pick_slot(kept_out_scale, slot_index)
        out_normed = (temporal - pick_slot(kept_out_mean, slot_index)) * out_scale
        pre_act = (
            out_normed * out_gain_now
            + out_bias_now
            + jnp.where(odd_segment, skip_input.astype(jnp.float32), 0.0)
        )
        grad_result = jnp.where(
            last_segment,
            pick_slot(cot_stack, slot_index).astype(jnp.float32),
            grad_input.astype(jnp.float32)
            + jnp.where(odd_segment, grad_skip.astype(jnp.float32), 0.0),
        )
        grad_pre = grad_result * silu_slope(pre_act)
        out_bias_sum, out_gain_sum = reduce_back(grad_pre, out_normed)
        grad_temporal = (
            out_gain_now
            * out_scale
            * (grad_pre - out_bias_sum / pixel_count - out_normed * out_gain_sum / pixel_count)
        ).astype(jnp.bfloat16)
        time_acc = time_acc + usable_weight * jnp.einsum(
            "fijc,fijo->co", time_taps, grad_temporal, preferred_element_type=jnp.float32
        )
        grad_hidden = time_back(grad_temporal, time_low, before_now, after_now)
        grad_mid = grad_hidden * silu_slope(mid_pre)
        mid_bias_sum, mid_gain_sum = reduce_back(grad_mid, mid_normed)
        mid_scale = pick_slot(kept_mid_scale, slot_index)
        grad_spatial = (
            mid_gain_now
            * mid_scale
            * (grad_mid - mid_bias_sum / pixel_count - mid_normed * mid_gain_sum / pixel_count)
        ).astype(jnp.bfloat16)
        space_acc = space_acc + usable_weight * jnp.einsum(
            "fijc,fijo->co", space_taps, grad_spatial, preferred_element_type=jnp.float32
        )
        grad_current = space_back(grad_spatial, space_low)
        mid_gain_acc = mid_gain_acc + usable_weight * mid_gain_sum
        mid_bias_acc = mid_bias_acc + usable_weight * mid_bias_sum
        out_gain_acc = out_gain_acc + usable_weight * out_gain_sum
        out_bias_acc = out_bias_acc + usable_weight * out_bias_sum
        input_grads = store_slot(
            input_grads, grad_current + grad_skip.astype(jnp.float32), slot_index, usable
        )
        if turn_index < turns - 1:
            grad_input, grad_skip = from_behind(
                (
                    grad_current.astype(jnp.bfloat16),
                    jnp.where(odd_segment, grad_pre.astype(jnp.bfloat16), grad_skip),
                ),
                "segment",
                -1,
            )
    space_grad, time_grad = (
        lax.psum_scatter(space_acc, "dp", scatter_dimension=0, tiled=True),
        lax.psum_scatter(time_acc, "dp", scatter_dimension=0, tiled=True),
    )
    data_index = lax.axis_index("dp")

    def own_share(full_vector):
        share = full_vector.shape[0] // n_data
        return lax.dynamic_slice_in_dim(full_vector, data_index * share, share)[None]

    flat_shape = (n_segment * frame_count,) + frames.shape[1:]
    arrived_out, arrived_grads = (
        lax.all_to_all(
            results.reshape(flat_shape).astype(jnp.bfloat16),
            "segment",
            split_axis=0,
            concat_axis=0,
            tiled=True,
        ).astype(jnp.float32),
        lax.all_to_all(
            input_grads.reshape(flat_shape).astype(jnp.bfloat16),
            "segment",
            split_axis=0,
            concat_axis=0,
            tiled=True,
        ).astype(jnp.float32),
    )
    output = arrived_out[(n_segment - 1) * frame_count :].astype(jnp.bfloat16)
    frames_grad = arrived_grads[:frame_count]
    return (
        output,
        frames_grad,
        space_grad[None],
        time_grad[None],
        own_share(mid_gain_acc),
        own_share(mid_bias_acc),
        own_share(out_gain_acc),
        own_share(out_bias_acc),
    )


def general(mesh):
    return jax.shard_map(
        on_device_general,
        mesh=mesh,
        in_specs=(
            P(("dp", "segment"), None, None, None),
            P(("dp", "segment"), None, None, None),
            P(("dp", "segment")),
            P("segment", "dp", None),
            P("segment", "dp", None),
            P("segment", "dp"),
            P("segment", "dp"),
            P("segment", "dp"),
            P("segment", "dp"),
        ),
        out_specs=(
            P(("dp", "segment"), None, None, None),
            P(("dp", "segment"), None, None, None),
            P("segment", "dp", None),
            P("segment", "dp", None),
            P("segment", "dp"),
            P("segment", "dp"),
            P("segment", "dp"),
            P("segment", "dp"),
        ),
        check_vma=False,
    )


def solution(mesh):
    if mesh.shape["dp"] != 8 or mesh.shape["segment"] != 4:
        return general(mesh)
    n_dp, n_seg = mesh.shape["dp"], mesh.shape["segment"]
    fine = Mesh(mesh.devices.reshape(n_dp // 2, 2, 2, n_seg // 2), EVERY)
    dp, seg = ("z", "y"), ("x", "c")
    return jax.shard_map(
        on_device,
        mesh=fine,
        in_specs=(
            P(EVERY, None, None, None),
            P(EVERY, None, None, None),
            P(EVERY),
            P(seg, dp, None),
            P(seg, dp, None),
            P(seg, dp),
            P(seg, dp),
            P(seg, dp),
            P(seg, dp),
        ),
        out_specs=(
            P(EVERY, None, None, None),
            P(EVERY, None, None, None),
            P(seg, dp, None),
            P(seg, dp, None),
            P(seg, dp),
            P(seg, dp),
            P(seg, dp),
            P(seg, dp),
        ),
        check_vma=False,
    )
```

```python
import functools

import jax
import jax.numpy as jnp
from jax import lax
from jax.experimental import pallas as pl
from jax.experimental.pallas import tpu as pltpu
from jax.sharding import Mesh, PartitionSpec as P

eps = 1e-05
PLANE = ("y", "x", "c")
EVERY = ("z", "y", "x", "c")
BF = jnp.bfloat16
F32 = jnp.float32


def nt(a, b):
    return lax.dot_general(a, b, (((1,), (1,)), ((), ())), preferred_element_type=F32)


def nn(a, b):
    return lax.dot_general(a, b, (((1,), (0,)), ((), ())), preferred_element_type=F32)


VMEM_CAP = 56 * 1024 * 1024


def call(body, outs, scratch, flops, *args):
    moved = sum(a.size * a.dtype.itemsize for a in args) + sum(
        o.size * o.dtype.itemsize for o in outs
    )
    return pl.pallas_call(
        body,
        out_shape=outs,
        in_specs=[pl.BlockSpec(memory_space=pltpu.VMEM)] * len(args),
        out_specs=[pl.BlockSpec(memory_space=pltpu.VMEM)] * len(outs),
        scratch_shapes=scratch,
        compiler_params=pltpu.CompilerParams(vmem_limit_bytes=VMEM_CAP),
        cost_estimate=pl.CostEstimate(flops=flops, bytes_accessed=moved, transcendentals=0),
    )(*args)


def halves(first, second):
    low = lax.broadcasted_iota(jnp.int32, first.shape, 1) < 64
    a, b = first.astype(F32), second.astype(F32)
    top = jnp.where(low, a, pltpu.roll(b, 64, 1))
    bottom = jnp.where(low, pltpu.roll(a, 64, 1), b)
    return top, bottom


def conv_in_body(side, g_ref, kt_ref, lt_ref, vec_ref, before_ref, after_ref,
                 pad_ref, hid_ref, xhat_ref, rs_ref, sent_ref, sp_ref, ktm_ref):
    ranks, half = g_ref.shape[0], g_ref.shape[1]
    rows = 2 * half
    plane = rows // side
    nf = plane // side
    ch = pad_ref.shape[2]
    zrow = jnp.zeros((pad_ref.shape[1], ch), BF)
    pad_ref[0] = zrow
    pad_ref[side + 1] = zrow
    zcol = jnp.zeros((nf, ch), BF)
    for i in range(side):
        pad_ref[i + 1, 0:nf] = zcol
        pad_ref[i + 1, nf + plane : 2 * nf + plane] = zcol
    step = plane // 2

    def place(k, carry):
        for q in range(ranks // 2):
            top, bottom = halves(
                g_ref[2 * q, pl.ds(pl.multiple_of(k * step, 16), step), :],
                g_ref[2 * q + 1, pl.ds(pl.multiple_of(k * step, 16), step), :],
            )
            for piece, kk in ((top, k), (bottom, k + side)):
                at = nf + lax.rem(kk, 2) * step
                pad_ref[1 + kk // 2, pl.ds(pl.multiple_of(at, 16), step), 128 * q : 128 * q + 128] = (
                    piece.astype(BF)
                )
        return carry

    lax.fori_loop(0, side, place, 0)
    conv_rest(side, pad_ref, kt_ref, lt_ref, vec_ref, before_ref, after_ref,
              hid_ref, xhat_ref, rs_ref, sent_ref, sp_ref, ktm_ref, plane, nf, ch)


def conv_first_body(side, a_ref, kt_ref, lt_ref, vec_ref, before_ref, after_ref,
                    pad_ref, hid_ref, xhat_ref, rs_ref, sent_ref, sp_ref, ktm_ref):
    ch = pad_ref.shape[2]
    plane = a_ref.shape[0] // side
    nf = plane // side
    zrow = jnp.zeros((pad_ref.shape[1], ch), BF)
    pad_ref[0] = zrow
    pad_ref[side + 1] = zrow
    zcol = jnp.zeros((nf, ch), BF)
    for i in range(side):
        pad_ref[i + 1, 0:nf] = zcol
        pad_ref[i + 1, nf + plane : 2 * nf + plane] = zcol
        pad_ref[i + 1, nf : nf + plane] = a_ref[i * plane : (i + 1) * plane]
    conv_rest(side, pad_ref, kt_ref, lt_ref, vec_ref, before_ref, after_ref,
              hid_ref, xhat_ref, rs_ref, sent_ref, sp_ref, ktm_ref, plane, nf, ch)


def gather_columns(kt_ref, ktm_ref):
    width = kt_ref.shape[2]
    for z in range(kt_ref.shape[0]):
        ktm_ref[:, z * width : (z + 1) * width] = kt_ref[z]


def conv_rest(side, pad_ref, kt_ref, lt_ref, vec_ref, before_ref, after_ref,
              hid_ref, xhat_ref, rs_ref, sent_ref, sp_ref, ktm_ref, plane, nf, ch):
    hc = hid_ref.shape[1]
    rows = plane * side
    gather_columns(kt_ref, ktm_ref)

    def conv(i, total):
        acc = jnp.zeros((plane, hc), F32)
        for t in range(9):
            r, c = t // 3, t % 3
            acc += nt(pad_ref[i + r, c * nf : c * nf + plane, :], ktm_ref[:, t * ch : (t + 1) * ch])
        sp_ref[i] = acc
        return total + jnp.sum(acc, axis=0, keepdims=True)

    mean = lax.fori_loop(0, side, conv, jnp.zeros((1, hc), F32)) / rows

    def square(i, total):
        cen = sp_ref[i] - mean
        return total + jnp.sum(cen * cen, axis=0, keepdims=True)

    var = lax.fori_loop(0, side, square, jnp.zeros((1, hc), F32)) / rows
    rs = lax.rsqrt(var + eps)
    rs_ref[...] = rs
    gain, bias = vec_ref[0:1, :], vec_ref[1:2, :]
    step = plane // 2

    def act(i, carry):
        xhat = (sp_ref[i] - mean) * rs
        xhat_ref[i] = xhat
        v = xhat * gain + bias
        sp_ref[i] = v * jax.nn.sigmoid(v)
        hid_ref[pl.ds(pl.multiple_of(i * plane, 16), plane), :] = sp_ref[i].astype(BF)
        return carry

    lax.fori_loop(0, side, act, 0)
    l0, l1, l2 = lt_ref[0:hc], lt_ref[hc : 2 * hc], lt_ref[2 * hc : 3 * hc]
    low = lax.broadcasted_iota(jnp.int32, (step, 128), 1) < 64

    def temporal(k, carry):
        pieces = []
        for kk in (k, k + side):
            par = lax.rem(kk, 2)
            h = sp_ref[kk // 2, pl.ds(pl.multiple_of(par * step, 8), step), :]
            at = pl.multiple_of(par * (step % nf), 8)
            pieces.append((
                (pltpu.roll(h, 1, 0) * before_ref[pl.ds(at, step), :]).astype(BF),
                h.astype(BF),
                (pltpu.roll(h, step - 1, 0) * after_ref[pl.ds(at, step), :]).astype(BF),
            ))
        prev, here, nxt = [jnp.concatenate([x, y], axis=0) for x, y in zip(*pieces)]
        part = nn(prev, l0) + nn(here, l1) + nn(nxt, l2)
        store_packed(sent_ref, part, k, step, low)
        return carry

    lax.fori_loop(0, side, temporal, 0)


def store_packed(sent_ref, part, k, step, low):
    at = pl.multiple_of(k * step, 16)
    for q in range(sent_ref.shape[0] // 2):
        x = part[:step, 128 * q : 128 * q + 128]
        y = part[step:, 128 * q : 128 * q + 128]
        sent_ref[2 * q, pl.ds(at, step), :] = jnp.where(low, x, pltpu.roll(y, 64, 1)).astype(BF)
        sent_ref[2 * q + 1, pl.ds(at, step), :] = jnp.where(low, pltpu.roll(x, 64, 1), y).astype(BF)


def conv_forward(g, kt, lt, vec, before, after, side, pixels, ch):
    hc = lt.shape[0] // 3
    plane = pixels // side
    nf = plane // side
    first = g.ndim == 2
    body = functools.partial(conv_first_body if first else conv_in_body, side)
    outs = [
        jax.ShapeDtypeStruct((side + 2, plane + 2 * nf, ch), BF),
        jax.ShapeDtypeStruct((pixels, hc), BF),
        jax.ShapeDtypeStruct((side, plane, hc), F32),
        jax.ShapeDtypeStruct((1, hc), F32),
        jax.ShapeDtypeStruct((8, pixels // 2, 128), BF),
    ]
    scratch = [pltpu.VMEM((side, plane, hc), F32), pltpu.VMEM((hc, 9 * ch), BF)]
    flops = 2 * pixels * hc * 12 * ch
    return call(body, outs, scratch, flops, g, kt, lt, vec, before, after)


def fold(v):
    return v + pltpu.roll(v, 64, 1)


def total_of(recv_ref):
    t = recv_ref[0].astype(F32)
    for i in range(1, recv_ref.shape[0]):
        t += recv_ref[i].astype(F32)
    return t


def out_norm_body(has_skip, *refs):
    if has_skip:
        recv_ref, vec_ref, skip_ref, xhat_ref, rs_ref, pre_ref, res_ref = refs
    else:
        recv_ref, vec_ref, xhat_ref, rs_ref, pre_ref, res_ref = refs
    t = total_of(recv_ref)
    pixels = 2 * t.shape[0]
    mean = fold(jnp.sum(t, axis=0, keepdims=True)) / pixels
    cen = t - mean
    rs = lax.rsqrt(fold(jnp.sum(cen * cen, axis=0, keepdims=True)) / pixels + eps)
    xhat = cen * rs
    pre = xhat * vec_ref[0:1, :] + vec_ref[1:2, :]
    if has_skip:
        pre = pre + skip_ref[...].astype(F32)
    xhat_ref[...] = xhat
    rs_ref[...] = rs
    pre_ref[...] = pre
    res_ref[...] = (pre * jax.nn.sigmoid(pre)).astype(BF)


def out_norm(recv, vec, skip):
    half = recv.shape[1]
    outs = [
        jax.ShapeDtypeStruct((half, 128), F32),
        jax.ShapeDtypeStruct((1, 128), F32),
        jax.ShapeDtypeStruct((half, 128), F32),
        jax.ShapeDtypeStruct((half, 128), BF),
    ]
    args = (recv, vec) + (() if skip is None else (skip,))
    return call(functools.partial(out_norm_body, skip is not None), outs, [], recv.size * 2, *args)


def out_back_body(has_skip, *refs):
    if has_skip:
        g_ref, extra_ref, pre_ref, xhat_ref, rs_ref, vec_ref, dpre_ref, dt_ref, sums_ref = refs
    else:
        g_ref, pre_ref, xhat_ref, rs_ref, vec_ref, dpre_ref, dt_ref, sums_ref = refs
    g = total_of(g_ref)
    if has_skip:
        g = g + extra_ref[...].astype(F32)
    pre, xhat = pre_ref[...], xhat_ref[...]
    sig = jax.nn.sigmoid(pre)
    dpre = g * (sig * (1.0 + pre * (1.0 - sig)))
    pixels = 2 * pre.shape[0]
    sb = fold(jnp.sum(dpre, axis=0, keepdims=True))
    sg = fold(jnp.sum(dpre * xhat, axis=0, keepdims=True))
    dpre_ref[...] = dpre.astype(BF)
    scale = vec_ref[0:1, :] * rs_ref[...]
    dt_ref[...] = (scale * (dpre - sb / pixels - xhat * (sg / pixels))).astype(BF)
    sums_ref[0:1, :] = sg
    sums_ref[1:2, :] = sb


def out_back(g, extra, pre, xhat, rs, vec):
    half = pre.shape[0]
    outs = [
        jax.ShapeDtypeStruct((half, 128), BF),
        jax.ShapeDtypeStruct((half, 128), BF),
        jax.ShapeDtypeStruct((2, 128), F32),
    ]
    args = (g,) + (() if extra is None else (extra,)) + (pre, xhat, rs, vec)
    return call(functools.partial(out_back_body, extra is not None), outs, [], g.size * 4, *args)


def conv_back_body(side, plain, g_ref, xhat_ref, rs_ref, kt_ref, lt_ref, vec_ref, before_ref,
                   after_ref, dt_ref, ds_ref, sums_ref, sent_ref, dy_ref, pad_ref, ktm_ref):
    ranks, half = g_ref.shape[0], g_ref.shape[1]
    rows = 2 * half
    plane = rows // side
    nf = plane // side
    step = plane // 2
    hc = ds_ref.shape[1]
    ch = dt_ref.shape[1]
    gather_columns(kt_ref, ktm_ref)
    zrow = jnp.zeros((pad_ref.shape[1], hc), BF)
    pad_ref[0] = zrow
    pad_ref[side + 1] = zrow
    zcol = jnp.zeros((nf, hc), BF)
    for i in range(side):
        pad_ref[i + 1, 0:nf] = zcol
        pad_ref[i + 1, nf + plane : 2 * nf + plane] = zcol

    def place(k, carry):
        at = pl.multiple_of(k * step, 16)
        for q in range(ranks // 2):
            top, bottom = halves(g_ref[2 * q, pl.ds(at, step), :], g_ref[2 * q + 1, pl.ds(at, step), :])
            dt_ref[pl.ds(at, step), 128 * q : 128 * q + 128] = top.astype(BF)
            dt_ref[pl.ds(pl.multiple_of(half + k * step, 16), step), 128 * q : 128 * q + 128] = (
                bottom.astype(BF)
            )
        return carry

    lax.fori_loop(0, side, place, 0)
    l0, l1, l2 = lt_ref[0:hc], lt_ref[hc : 2 * hc], lt_ref[2 * hc : 3 * hc]
    gain, bias = vec_ref[0:1, :], vec_ref[1:2, :]

    def hidden_grad(i, sums):
        dt = dt_ref[pl.ds(pl.multiple_of(i * plane, 16), plane), :]
        early = nt(dt, l0) * before_ref[0:plane, :]
        late = nt(dt, l2) * after_ref[0:plane, :]
        dh = nt(dt, l1) + pltpu.roll(early, plane - 1, 0) + pltpu.roll(late, 1, 0)
        xhat = xhat_ref[i]
        v = xhat * gain + bias
        sig = jax.nn.sigmoid(v)
        dy = dh * (sig * (1.0 + v * (1.0 - sig)))
        dy_ref[i] = dy
        return (
            sums[0] + jnp.sum(dy * xhat, axis=0, keepdims=True),
            sums[1] + jnp.sum(dy, axis=0, keepdims=True),
        )

    zero = jnp.zeros((1, hc), F32)
    sg, sb = lax.fori_loop(0, side, hidden_grad, (zero, zero))
    sums_ref[0:1, :] = sg
    sums_ref[1:2, :] = sb
    scale = gain * rs_ref[...]

    def spatial_grad(i, carry):
        ds = (scale * (dy_ref[i] - sb / rows - xhat_ref[i] * (sg / rows))).astype(BF)
        pad_ref[i + 1, nf : nf + plane] = ds
        ds_ref[pl.ds(pl.multiple_of(i * plane, 16), plane), :] = ds
        return carry

    lax.fori_loop(0, side, spatial_grad, 0)

    if plain:
        def back_plain(i, carry):
            acc = jnp.zeros((plane, ch), F32)
            for t in range(9):
                r, c = 2 - t // 3, 2 - t % 3
                acc += nn(pad_ref[i + r, c * nf : c * nf + plane, :], ktm_ref[:, t * ch : (t + 1) * ch])
            sent_ref[pl.ds(pl.multiple_of(i * plane, 16), plane), :] = acc.astype(BF)
            return carry

        lax.fori_loop(0, side, back_plain, 0)
        return
    low = lax.broadcasted_iota(jnp.int32, (step, 128), 1) < 64

    def back(k, carry):
        acc = jnp.zeros((2 * step, ch), F32)
        for t in range(9):
            r, c = 2 - t // 3, 2 - t % 3
            pieces = []
            for kk in (k, k + side):
                at = c * nf + lax.rem(kk, 2) * step
                pieces.append(pad_ref[kk // 2 + r, pl.ds(pl.multiple_of(at, 16), step), :])
            acc += nn(jnp.concatenate(pieces, axis=0), ktm_ref[:, t * ch : (t + 1) * ch])
        store_packed(sent_ref, acc, k, step, low)
        return carry

    lax.fori_loop(0, side, back, 0)


def conv_back(g, xhat, rs, kt, lt, vec, before, after, side, plain):
    ranks, half = g.shape[0], g.shape[1]
    hc = lt.shape[0] // 3
    ch = lt.shape[1]
    pixels = 2 * half
    plane = pixels // side
    nf = plane // side
    outs = [
        jax.ShapeDtypeStruct((pixels, ch), BF),
        jax.ShapeDtypeStruct((pixels, hc), BF),
        jax.ShapeDtypeStruct((2, hc), F32),
        jax.ShapeDtypeStruct((pixels, ch) if plain else (8, half, 128), BF),
    ]
    scratch = [
        pltpu.VMEM((side, plane, hc), F32),
        pltpu.VMEM((side + 2, plane + 2 * nf, hc), BF),
        pltpu.VMEM((hc, 9 * ch), BF),
    ]
    flops = 2 * pixels * hc * 12 * ch
    body = functools.partial(conv_back_body, side, plain)
    return call(body, outs, scratch, flops, g, xhat, rs, kt, lt, vec, before, after)


def grads_body(side, pad_ref, hid_ref, ds_ref, dt_ref, before_ref, after_ref, sg_ref, tg_ref,
               dst_ref, p_ref, n_ref, h_ref):
    ch = pad_ref.shape[2]
    hc = hid_ref.shape[1]
    plane = hid_ref.shape[0] // side
    nf = plane // side

    def flip(i, carry):
        at = pl.ds(pl.multiple_of(i * plane, 16), plane)
        h = hid_ref[at, :].astype(F32)
        p_ref[i] = (pltpu.roll(h, 1, 0) * before_ref[0:plane, :]).T.astype(BF)
        n_ref[i] = (pltpu.roll(h, plane - 1, 0) * after_ref[0:plane, :]).T.astype(BF)
        h_ref[i] = h.T.astype(BF)
        dst_ref[i] = ds_ref[at, :].astype(F32).T.astype(BF)
        return carry

    lax.fori_loop(0, side, flip, 0)
    for t, src in enumerate((p_ref, h_ref, n_ref)):
        acc = jnp.zeros((hc, ch), F32)
        for i in range(side):
            acc += nn(src[i], dt_ref[i * plane : (i + 1) * plane, :])
        tg_ref[t * hc : (t + 1) * hc, :] = acc.astype(BF)
    width = sg_ref.shape[2]
    for t in range(9):
        r, c = t // 3, t % 3
        acc = jnp.zeros((hc, ch), F32)
        for i in range(side):
            acc += nn(dst_ref[i], pad_ref[i + r, c * nf : c * nf + plane, :])
        first = t * ch
        while first < (t + 1) * ch:
            z = first // width
            last = min((t + 1) * ch, (z + 1) * width)
            sg_ref[z, :, first - z * width : last - z * width] = (
                acc[:, first - t * ch : last - t * ch].astype(BF)
            )
            first = last


def kernel_grads(pad, hidden, ds, dt, before, after, side, nz):
    pixels, hc = hidden.shape
    ch = dt.shape[1]
    plane = pixels // side
    outs = [
        jax.ShapeDtypeStruct((nz, hc, 9 * ch // nz), BF),
        jax.ShapeDtypeStruct((3 * hc, ch), BF),
    ]
    scratch = [pltpu.VMEM((side, hc, plane), BF)] * 4
    flops = 2 * pixels * hc * 12 * ch
    return call(functools.partial(grads_body, side), outs, scratch, flops,
                pad, hidden, ds, dt, before, after)


def on_device(frames, cot, starts, ks, ktm, mg, mb, og, ob):
    nz, n_rank, n_seg = lax.axis_size("z"), 8, 4
    n_dp = nz * 2
    fr, side, ch = frames.shape[0], frames.shape[1], frames.shape[3]
    area = side * side
    hid = ks.shape[2]
    hc, cc = hid // n_rank, ch // n_rank
    q = hc // n_rank
    rank = lax.axis_index(PLANE)
    d_index = lax.axis_index(("z", "y"))
    nf = n_dp * fr
    pixels = area * nf

    to_plane = [(d * n_seg + s, s * n_rank + d) for d in range(n_dp) for s in range(n_seg)]
    from_plane = [(b, a) for a, b in to_plane]
    rows = fr * area
    flag_row = jnp.zeros((12, ch), BF).at[0, :fr].set(starts.astype(BF))
    moving = jnp.concatenate([frames.reshape(rows, ch), flag_row], axis=0)
    moving = lax.ppermute(moving, EVERY, to_plane)
    cot_moving = lax.ppermute(cot.reshape(rows, ch), EVERY, to_plane)

    def by_pixel(v):
        return v.reshape(n_rank * fr, area, ch).transpose(1, 0, 2).reshape(pixels, ch)

    perm = (jnp.arange(hid).reshape(n_rank, n_rank, q).transpose(1, 0, 2).reshape(hid)[:, None]
            == jnp.arange(hid)[None, :]).astype(BF)
    kt = lax.dot_general(perm, ks[0].astype(BF), (((1,), (1,)), ((), ())),
                         preferred_element_type=F32).astype(BF)
    kt = kt.reshape(n_rank, hc, ks.shape[1])
    kt = lax.all_to_all(kt, PLANE, 0, 0)
    kt = kt.reshape(2, n_seg, hc, ks.shape[1]).transpose(1, 2, 0, 3).reshape(n_seg, hc, -1)
    lrows = ktm.shape[1] // n_rank
    lt = ktm[0].astype(BF).reshape(-1, n_rank, q, ch).transpose(1, 0, 2, 3).reshape(n_rank, lrows, ch)
    extra = jnp.zeros((n_rank, 2, ch), BF)
    extra = extra.at[:, 0, :q].set(mg[0].astype(BF).reshape(n_rank, q))
    extra = extra.at[:, 0, q : 2 * q].set(mb[0].astype(BF).reshape(n_rank, q))
    extra = extra.at[:, 0, 128 : 128 + cc].set(og[0].astype(BF)[None])
    extra = extra.at[:, 0, 256 : 256 + cc].set(ob[0].astype(BF)[None])
    lt = jnp.concatenate([lt, extra], axis=1)
    lt = lax.all_to_all(lt, PLANE, 0, 0)
    lt = lt.reshape(2, n_seg, lrows + 2, ch).transpose(1, 0, 2, 3).reshape(n_seg, 2 * (lrows + 2), ch)
    kts, lts, mids, outs = [], [], [], []
    for s in range(n_seg):
        kts.append(lax.all_gather(kt[s], "z", axis=0))
        full = lax.all_gather(lt[s], "z", axis=0).reshape(n_dp, lrows + 2, ch)
        lts.append(full[:, :lrows].reshape(3 * hc, ch))
        row = full[:, lrows].astype(F32)
        mids.append(jnp.stack([row[:, :q].reshape(hc), row[:, q : 2 * q].reshape(hc)]))
        own = lax.dynamic_index_in_dim(row, rank, 0, keepdims=False)
        outs.append(jnp.stack([jnp.tile(own[128 : 128 + cc], 2), jnp.tile(own[256 : 256 + cc], 2)]))

    gathered = lax.all_gather(moving, PLANE, axis=0)
    a0 = by_pixel(gathered[:, :rows])
    flags = gathered[:, rows, :fr].reshape(nf) > 0.5
    slot = jnp.arange(nf) % fr
    before = jnp.where(flags | (slot == 0), 0.0, 1.0)
    after = jnp.where(jnp.roll(flags, -1) | (slot == fr - 1), 0.0, 1.0)
    spread = (side * nf + nf, hc)
    before = jnp.broadcast_to(jnp.tile(before, side + 1)[:, None], spread)
    after = jnp.broadcast_to(jnp.tile(after, side + 1)[:, None], spread)

    def own_channels(v):
        v = lax.dynamic_slice_in_dim(v, rank * cc, cc, axis=1)
        return jnp.concatenate([v[: pixels // 2], v[pixels // 2 :]], axis=1)

    skip = own_channels(a0)
    cot_own = own_channels(by_pixel(lax.all_gather(cot_moving, PLANE, axis=0)))

    saved = []
    g = a0
    for s in range(n_seg):
        pad, hidden, xm, rm, sent = conv_forward(
            g, kts[s], lts[s], mids[s], before, after, side, pixels, ch)
        recv = lax.all_to_all(sent, PLANE, 0, 0)
        xo, ro, pre, res = out_norm(recv, outs[s], skip if s % 2 == 1 else None)
        saved.append((pad, hidden, xm, rm, xo, ro, pre))
        if s % 2 == 1:
            skip = res
        g = lax.all_gather(res, PLANE, axis=0)

    out = g.reshape(n_rank, pixels // 2, 2, cc).transpose(2, 1, 0, 3).reshape(area, n_rank, fr, ch)
    out = lax.dynamic_index_in_dim(out, rank, 1, keepdims=False)
    output = lax.ppermute(out, EVERY, from_plane).transpose(1, 0, 2).reshape(frames.shape)

    g = cot_own[None]
    skip_grad = None
    sgrads, tgrads = [], []
    for s in reversed(range(n_seg)):
        pad, hidden, xm, rm, xo, ro, pre = saved[s]
        dpre, dt, osum = out_back(g, skip_grad if s == 1 else None, pre, xo, ro, outs[s])
        if s % 2 == 1:
            skip_grad = dpre
        dtg = lax.all_gather(dt, PLANE, axis=0)
        dtf, ds, msum, sent = conv_back(
            dtg, xm, rm, kts[s], lts[s], mids[s], before, after, side, False)
        sg, tg = kernel_grads(pad, hidden, ds, dtf, before, after, side, nz)
        tail = jnp.zeros((n_dp, 2, ch), BF)
        msum = msum.astype(BF).reshape(2, n_dp, q)
        osum = osum.astype(BF)
        tail = tail.at[:, 0, :q].set(msum[0]).at[:, 0, q : 2 * q].set(msum[1])
        tail = tail.at[:, 0, 128 : 128 + cc].set(osum[None, 0, :cc])
        tail = tail.at[:, 0, 256 : 256 + cc].set(osum[None, 1, :cc])
        tg = jnp.concatenate([tg.reshape(n_dp, lrows, ch), tail], axis=1).reshape(nz, -1, ch)
        sgrads.append(lax.psum_scatter(sg, "z", scatter_dimension=0))
        tgrads.append(lax.psum_scatter(tg, "z", scatter_dimension=0))
        g = lax.all_to_all(sent, PLANE, 0, 0)

    da = jnp.sum(g.astype(F32), axis=0) + skip_grad.astype(F32)
    da = lax.all_gather(da.astype(BF), PLANE, axis=0)
    da = da.reshape(n_rank, pixels // 2, 2, cc).transpose(2, 1, 0, 3).reshape(area, n_rank, fr, ch)
    da = lax.dynamic_index_in_dim(da, rank, 1, keepdims=False)
    frames_grad = lax.ppermute(da, EVERY, from_plane).transpose(1, 0, 2).reshape(frames.shape)
    frames_grad = frames_grad.astype(F32)

    sg, tg = [jnp.stack(v[::-1]) for v in (sgrads, tgrads)]
    sg = sg.reshape(n_seg, hc, 2, -1).transpose(2, 0, 1, 3).reshape(n_rank, hc, -1)
    sg = lax.all_to_all(sg, PLANE, 0, 0).reshape(hid, -1)
    space_grad = lax.dot_general(sg, perm, (((0,), (0,)), ((), ())), preferred_element_type=F32)
    tg = tg.reshape(n_seg, 2, lrows + 2, ch).transpose(1, 0, 2, 3).reshape(n_rank, lrows + 2, ch)
    tg = lax.all_to_all(tg, PLANE, 0, 0)
    row = tg[:, lrows].astype(F32)
    tg = tg[:, :lrows].reshape(n_rank, -1, q, ch)
    time_grad = tg.transpose(1, 0, 2, 3).reshape(-1, ch).astype(F32)
    own = lax.dynamic_index_in_dim(row, d_index, 0, keepdims=False)
    return (
        output,
        frames_grad,
        space_grad[None],
        time_grad[None],
        row[:, :q].reshape(1, hc),
        row[:, q : 2 * q].reshape(1, hc),
        own[128 : 128 + cc][None],
        own[256 : 256 + cc][None],
    )


def from_behind(value, axis, steps):
    count = lax.axis_size(axis)
    leading, last = (max(0, -steps), min(count, count - steps))
    return lax.ppermute(value, axis, [(source, source + steps) for source in range(leading, last)])


def space_apply(current, kernel):
    frame_side = current.shape[1]
    padded = jnp.pad(current, ((0, 0), (1, 1), (1, 1), (0, 0)))
    stacked = jnp.concatenate(
        [
            padded[:, row_shift : row_shift + frame_side, col_shift : col_shift + frame_side, :]
            for row_shift in range(3)
            for col_shift in range(3)
        ],
        axis=-1,
    )
    return (
        stacked,
        jnp.einsum("fijc,co->fijo", stacked, kernel, preferred_element_type=jnp.float32),
    )


def space_back(gradient, kernel):
    frame_side = gradient.shape[1]
    channels = kernel.shape[0] // 9
    spread = jnp.einsum("fijo,co->fijc", gradient, kernel, preferred_element_type=jnp.float32)
    total = jnp.zeros((gradient.shape[0], frame_side + 2, frame_side + 2, channels), jnp.float32)
    for tap_index in range(9):
        row_shift = tap_index // 3
        col_shift = tap_index % 3
        piece_now = spread[..., tap_index * channels : (tap_index + 1) * channels]
        total = total + jnp.pad(
            piece_now, ((0, 0), (row_shift, 2 - row_shift), (col_shift, 2 - col_shift), (0, 0))
        )
    return total[:, 1 : frame_side + 1, 1 : frame_side + 1, :]


def time_apply(current, kernel, before_mask, after_mask):
    blanks = jnp.zeros_like(current[:1])
    earlier = jnp.concatenate([blanks, current[:-1]], axis=0) * before_mask[
        :, None, None, None
    ].astype(current.dtype)
    later = jnp.concatenate([current[1:], blanks], axis=0) * after_mask[:, None, None, None].astype(
        current.dtype
    )
    stacked = jnp.concatenate([earlier, current, later], axis=-1)
    return (
        stacked,
        jnp.einsum("fijc,co->fijo", stacked, kernel, preferred_element_type=jnp.float32),
    )


def time_back(gradient, kernel, before_mask, after_mask):
    channels = kernel.shape[0] // 3
    spread = jnp.einsum("fijo,co->fijc", gradient, kernel, preferred_element_type=jnp.float32)
    early_part = spread[..., :channels] * before_mask[:, None, None, None]
    late_part = spread[..., 2 * channels :] * after_mask[:, None, None, None]
    blanks = jnp.zeros_like(early_part[:1])
    moved_early = jnp.concatenate([early_part[1:], blanks], axis=0)
    moved_late = jnp.concatenate([blanks, late_part[:-1]], axis=0)
    return spread[..., channels : 2 * channels] + moved_early + moved_late


def moments(values, pixel_count):
    average = lax.psum(jnp.sum(values, axis=(0, 1, 2)), "dp") / pixel_count
    centered = values - average
    spread = lax.psum(jnp.sum(centered * centered, axis=(0, 1, 2)), "dp") / pixel_count
    return (average, lax.rsqrt(spread + eps))


def reduce_back(gradient, normed):
    return lax.psum(
        (jnp.sum(gradient, axis=(0, 1, 2)), jnp.sum(gradient * normed, axis=(0, 1, 2))), "dp"
    )


def silu_slope(values):
    sigmoid_now = jax.nn.sigmoid(values)
    return sigmoid_now * (1.0 + values * (1.0 - sigmoid_now))


def pick_slot(stack, slot_index):
    return lax.dynamic_index_in_dim(stack, slot_index, 0, keepdims=False)


def store_slot(stack, value, slot_index, usable):
    previous = pick_slot(stack, slot_index)
    return lax.dynamic_update_index_in_dim(stack, jnp.where(usable, value, previous), slot_index, 0)


def on_device_general(
    frames, cotangent, starts, space_kernel, time_kernel, mid_gain, mid_bias, out_gain, out_bias
):
    n_segment = lax.axis_size("segment")
    n_data = lax.axis_size("dp")
    segment_index = lax.axis_index("segment")
    odd_segment = segment_index % 2 == 1
    last_segment = segment_index == n_segment - 1
    first_segment = segment_index == 0
    frame_count = frames.shape[0]
    frame_side = frames.shape[1]
    channels = frames.shape[3]
    hidden_units = mid_gain.shape[1] * n_data
    pixel_count = n_data * frame_count * frame_side * frame_side
    turns = 2 * n_segment - 1
    block_shape = (n_segment,) + frames.shape
    all_frames, all_cot, all_starts = (
        lax.all_gather(frames, "segment", axis=0, tiled=True),
        lax.all_gather(cotangent, "segment", axis=0, tiled=True),
        lax.all_gather(starts.astype(jnp.bfloat16), "segment", axis=0, tiled=True),
    )
    frame_stack = all_frames.reshape(block_shape)
    cot_stack = all_cot.reshape(block_shape)
    clip_flags = all_starts.astype(jnp.float32).reshape(n_segment, frame_count)
    positions = jnp.arange(frame_count)
    before_mask = jnp.where((clip_flags > 0.5) | (positions == 0), 0.0, 1.0)
    following = jnp.concatenate([clip_flags[:, 1:], jnp.ones((n_segment, 1), jnp.float32)], axis=1)
    after_mask = jnp.where(following > 0.5, 0.0, 1.0)
    gathered = (
        lax.all_gather(space_kernel[0].astype(jnp.bfloat16), "dp", axis=0, tiled=True),
        lax.all_gather(time_kernel[0].astype(jnp.bfloat16), "dp", axis=0, tiled=True),
        lax.all_gather(mid_gain[0].astype(jnp.bfloat16), "dp", axis=0, tiled=True),
        lax.all_gather(mid_bias[0].astype(jnp.bfloat16), "dp", axis=0, tiled=True),
        lax.all_gather(out_gain[0].astype(jnp.bfloat16), "dp", axis=0, tiled=True),
        lax.all_gather(out_bias[0].astype(jnp.bfloat16), "dp", axis=0, tiled=True),
    )
    space_low, time_low = (gathered[0], gathered[1])
    mid_gain_now = gathered[2].astype(jnp.float32)
    mid_bias_now = gathered[3].astype(jnp.float32)
    out_gain_now = gathered[4].astype(jnp.float32)
    out_bias_now = gathered[5].astype(jnp.float32)
    incoming = jnp.zeros_like(frames)
    carried = jnp.zeros_like(frames)
    kept_input = jnp.zeros(block_shape, jnp.bfloat16)
    kept_skip = jnp.zeros(block_shape, jnp.bfloat16)
    kept_mid_mean = jnp.zeros((n_segment, hidden_units), jnp.float32)
    kept_mid_scale = jnp.zeros((n_segment, hidden_units), jnp.float32)
    kept_out_mean = jnp.zeros((n_segment, channels), jnp.float32)
    kept_out_scale = jnp.zeros((n_segment, channels), jnp.float32)
    results = jnp.zeros(block_shape, jnp.float32)
    for turn_index in range(turns):
        micro_index = turn_index - segment_index
        usable = (micro_index >= 0) & (micro_index < n_segment)
        slot_index = jnp.clip(micro_index, 0, n_segment - 1)
        current = jnp.where(first_segment, pick_slot(frame_stack, slot_index), incoming)
        skip_input = carried
        _, spatial = space_apply(current, space_low)
        mid_mean, mid_scale = moments(spatial, pixel_count)
        hidden_act = jax.nn.silu(
            (spatial - mid_mean) * mid_scale * mid_gain_now + mid_bias_now
        ).astype(jnp.bfloat16)
        _, temporal = time_apply(
            hidden_act,
            time_low,
            pick_slot(before_mask, slot_index),
            pick_slot(after_mask, slot_index),
        )
        out_mean, out_scale = moments(temporal, pixel_count)
        pre_act = (
            (temporal - out_mean) * out_scale * out_gain_now
            + out_bias_now
            + jnp.where(odd_segment, skip_input.astype(jnp.float32), 0.0)
        )
        result = jax.nn.silu(pre_act).astype(jnp.bfloat16)
        kept_input = store_slot(kept_input, current, slot_index, usable)
        kept_skip = store_slot(kept_skip, skip_input, slot_index, usable)
        kept_mid_mean = store_slot(kept_mid_mean, mid_mean, slot_index, usable)
        kept_mid_scale = store_slot(kept_mid_scale, mid_scale, slot_index, usable)
        kept_out_mean = store_slot(kept_out_mean, out_mean, slot_index, usable)
        kept_out_scale = store_slot(kept_out_scale, out_scale, slot_index, usable)
        results = store_slot(results, result.astype(jnp.float32), slot_index, usable)
        if turn_index < turns - 1:
            incoming, carried = from_behind(
                (result, jnp.where(odd_segment, result, current)), "segment", 1
            )
    gathered = (
        lax.all_gather(space_kernel[0].astype(jnp.bfloat16), "dp", axis=0, tiled=True),
        lax.all_gather(time_kernel[0].astype(jnp.bfloat16), "dp", axis=0, tiled=True),
        lax.all_gather(mid_gain[0].astype(jnp.bfloat16), "dp", axis=0, tiled=True),
        lax.all_gather(mid_bias[0].astype(jnp.bfloat16), "dp", axis=0, tiled=True),
        lax.all_gather(out_gain[0].astype(jnp.bfloat16), "dp", axis=0, tiled=True),
        lax.all_gather(out_bias[0].astype(jnp.bfloat16), "dp", axis=0, tiled=True),
    )
    space_low, time_low = (gathered[0], gathered[1])
    mid_gain_now = gathered[2].astype(jnp.float32)
    mid_bias_now = gathered[3].astype(jnp.float32)
    out_gain_now = gathered[4].astype(jnp.float32)
    out_bias_now = gathered[5].astype(jnp.float32)
    grad_input = jnp.zeros_like(frames)
    grad_skip = jnp.zeros_like(frames)
    space_acc = jnp.zeros(space_low.shape, jnp.float32)
    time_acc = jnp.zeros(time_low.shape, jnp.float32)
    mid_gain_acc = jnp.zeros((hidden_units,), jnp.float32)
    mid_bias_acc = jnp.zeros((hidden_units,), jnp.float32)
    out_gain_acc = jnp.zeros((channels,), jnp.float32)
    out_bias_acc = jnp.zeros((channels,), jnp.float32)
    input_grads = jnp.zeros(block_shape, jnp.float32)
    for turn_index in range(turns):
        micro_index = n_segment - 1 - (turn_index - (n_segment - 1 - segment_index))
        usable = (micro_index >= 0) & (micro_index < n_segment)
        usable_weight = usable.astype(jnp.float32)
        slot_index = jnp.clip(micro_index, 0, n_segment - 1)
        current = pick_slot(kept_input, slot_index)
        skip_input = pick_slot(kept_skip, slot_index)
        before_now = pick_slot(before_mask, slot_index)
        after_now = pick_slot(after_mask, slot_index)
        space_taps, spatial = space_apply(current, space_low)
        mid_normed = (spatial - pick_slot(kept_mid_mean, slot_index)) * pick_slot(
            kept_mid_scale, slot_index
        )
        mid_pre = mid_normed * mid_gain_now + mid_bias_now
        hidden_act = jax.nn.silu(mid_pre).astype(jnp.bfloat16)
        time_taps, temporal = time_apply(hidden_act, time_low, before_now, after_now)
        out_scale = pick_slot(kept_out_scale, slot_index)
        out_normed = (temporal - pick_slot(kept_out_mean, slot_index)) * out_scale
        pre_act = (
            out_normed * out_gain_now
            + out_bias_now
            + jnp.where(odd_segment, skip_input.astype(jnp.float32), 0.0)
        )
        grad_result = jnp.where(
            last_segment,
            pick_slot(cot_stack, slot_index).astype(jnp.float32),
            grad_input.astype(jnp.float32)
            + jnp.where(odd_segment, grad_skip.astype(jnp.float32), 0.0),
        )
        grad_pre = grad_result * silu_slope(pre_act)
        out_bias_sum, out_gain_sum = reduce_back(grad_pre, out_normed)
        grad_temporal = (
            out_gain_now
            * out_scale
            * (grad_pre - out_bias_sum / pixel_count - out_normed * out_gain_sum / pixel_count)
        ).astype(jnp.bfloat16)
        time_acc = time_acc + usable_weight * jnp.einsum(
            "fijc,fijo->co", time_taps, grad_temporal, preferred_element_type=jnp.float32
        )
        grad_hidden = time_back(grad_temporal, time_low, before_now, after_now)
        grad_mid = grad_hidden * silu_slope(mid_pre)
        mid_bias_sum, mid_gain_sum = reduce_back(grad_mid, mid_normed)
        mid_scale = pick_slot(kept_mid_scale, slot_index)
        grad_spatial = (
            mid_gain_now
            * mid_scale
            * (grad_mid - mid_bias_sum / pixel_count - mid_normed * mid_gain_sum / pixel_count)
        ).astype(jnp.bfloat16)
        space_acc = space_acc + usable_weight * jnp.einsum(
            "fijc,fijo->co", space_taps, grad_spatial, preferred_element_type=jnp.float32
        )
        grad_current = space_back(grad_spatial, space_low)
        mid_gain_acc = mid_gain_acc + usable_weight * mid_gain_sum
        mid_bias_acc = mid_bias_acc + usable_weight * mid_bias_sum
        out_gain_acc = out_gain_acc + usable_weight * out_gain_sum
        out_bias_acc = out_bias_acc + usable_weight * out_bias_sum
        input_grads = store_slot(
            input_grads, grad_current + grad_skip.astype(jnp.float32), slot_index, usable
        )
        if turn_index < turns - 1:
            grad_input, grad_skip = from_behind(
                (
                    grad_current.astype(jnp.bfloat16),
                    jnp.where(odd_segment, grad_pre.astype(jnp.bfloat16), grad_skip),
                ),
                "segment",
                -1,
            )
    space_grad, time_grad = (
        lax.psum_scatter(space_acc, "dp", scatter_dimension=0, tiled=True),
        lax.psum_scatter(time_acc, "dp", scatter_dimension=0, tiled=True),
    )
    data_index = lax.axis_index("dp")

    def own_share(full_vector):
        share = full_vector.shape[0] // n_data
        return lax.dynamic_slice_in_dim(full_vector, data_index * share, share)[None]

    flat_shape = (n_segment * frame_count,) + frames.shape[1:]
    arrived_out, arrived_grads = (
        lax.all_to_all(
            results.reshape(flat_shape).astype(jnp.bfloat16),
            "segment",
            split_axis=0,
            concat_axis=0,
            tiled=True,
        ).astype(jnp.float32),
        lax.all_to_all(
            input_grads.reshape(flat_shape).astype(jnp.bfloat16),
            "segment",
            split_axis=0,
            concat_axis=0,
            tiled=True,
        ).astype(jnp.float32),
    )
    output = arrived_out[(n_segment - 1) * frame_count :].astype(jnp.bfloat16)
    frames_grad = arrived_grads[:frame_count]
    return (
        output,
        frames_grad,
        space_grad[None],
        time_grad[None],
        own_share(mid_gain_acc),
        own_share(mid_bias_acc),
        own_share(out_gain_acc),
        own_share(out_bias_acc),
    )


def general(mesh):
    return jax.shard_map(
        on_device_general,
        mesh=mesh,
        in_specs=(
            P(("dp", "segment"), None, None, None),
            P(("dp", "segment"), None, None, None),
            P(("dp", "segment")),
            P("segment", "dp", None),
            P("segment", "dp", None),
            P("segment", "dp"),
            P("segment", "dp"),
            P("segment", "dp"),
            P("segment", "dp"),
        ),
        out_specs=(
            P(("dp", "segment"), None, None, None),
            P(("dp", "segment"), None, None, None),
            P("segment", "dp", None),
            P("segment", "dp", None),
            P("segment", "dp"),
            P("segment", "dp"),
            P("segment", "dp"),
            P("segment", "dp"),
        ),
        check_vma=False,
    )


def solution(mesh):
    if mesh.shape["dp"] != 8 or mesh.shape["segment"] != 4:
        return general(mesh)
    n_dp, n_seg = mesh.shape["dp"], mesh.shape["segment"]
    fine = Mesh(mesh.devices.reshape(n_dp // 2, 2, 2, n_seg // 2), EVERY)
    dp, seg = ("z", "y"), ("x", "c")
    return jax.shard_map(
        on_device,
        mesh=fine,
        in_specs=(
            P(EVERY, None, None, None),
            P(EVERY, None, None, None),
            P(EVERY),
            P(seg, dp, None),
            P(seg, dp, None),
            P(seg, dp),
            P(seg, dp),
            P(seg, dp),
            P(seg, dp),
        ),
        out_specs=(
            P(EVERY, None, None, None),
            P(EVERY, None, None, None),
            P(seg, dp, None),
            P(seg, dp, None),
            P(seg, dp),
            P(seg, dp),
            P(seg, dp),
            P(seg, dp),
        ),
        check_vma=False,
    )
```

```python
import functools

import jax
import jax.numpy as jnp
from jax import lax
from jax.experimental import pallas as pl
from jax.experimental.pallas import tpu as pltpu
from jax.sharding import Mesh, PartitionSpec as P

eps = 1e-05
PLANE = ("y", "x", "c")
EVERY = ("z", "y", "x", "c")
BF = jnp.bfloat16
F32 = jnp.float32


def nt(a, b):
    return lax.dot_general(a, b, (((1,), (1,)), ((), ())), preferred_element_type=F32)


def nn(a, b):
    return lax.dot_general(a, b, (((1,), (0,)), ((), ())), preferred_element_type=F32)


VMEM_CAP = 56 * 1024 * 1024


def call(body, outs, scratch, flops, *args):
    moved = sum(a.size * a.dtype.itemsize for a in args) + sum(
        o.size * o.dtype.itemsize for o in outs
    )
    return pl.pallas_call(
        body,
        out_shape=outs,
        in_specs=[
            pl.BlockSpec(memory_space=pltpu.SMEM if a.dtype == jnp.int32 else pltpu.VMEM) for a in args
        ],
        out_specs=[pl.BlockSpec(memory_space=pltpu.VMEM)] * len(outs),
        scratch_shapes=scratch,
        compiler_params=pltpu.CompilerParams(vmem_limit_bytes=VMEM_CAP),
        cost_estimate=pl.CostEstimate(flops=flops, bytes_accessed=moved, transcendentals=0),
    )(*args)


def halves(odd, own, mate):
    low = lax.broadcasted_iota(jnp.int32, own.shape, 1) < 64
    own, mate = own.astype(F32), mate.astype(F32)
    a, b = jnp.where(odd, mate, own), jnp.where(odd, own, mate)
    top = jnp.where(low, a, pltpu.roll(b, 64, 1))
    bottom = jnp.where(low, pltpu.roll(a, 64, 1), b)
    return top, bottom


def by_rank(slices, rank):
    odd = lax.rem(rank, 2) == 1
    for p in range(len(slices) // 2):
        a, b = slices[2 * p], slices[2 * p + 1]
        yield lax.bitwise_xor(rank // 2, p), odd, a, b


def conv_in_body(side, rank_ref, *refs):
    slices, (kt_ref, lt_ref, vec_ref, before_ref, after_ref, pad_ref, hid_ref, xhat_ref, rs_ref,
             mate_ref, keep_ref, sp_ref, ktm_ref) = refs[:8], refs[8:]
    ranks, half = 8, slices[0].shape[0]
    rank = rank_ref[0]
    rows = 2 * half
    plane = rows // side
    nf = plane // side
    ch = pad_ref.shape[2]
    zrow = jnp.zeros((pad_ref.shape[1], ch), BF)
    pad_ref[0] = zrow
    pad_ref[side + 1] = zrow
    zcol = jnp.zeros((nf, ch), BF)
    for i in range(side):
        pad_ref[i + 1, 0:nf] = zcol
        pad_ref[i + 1, nf + plane : 2 * nf + plane] = zcol
    step = plane // 2

    def place(k, carry):
        rows_now = pl.ds(pl.multiple_of(k * step, 16), step)
        for q, odd, a_ref, b_ref in by_rank(slices, rank):
            top, bottom = halves(odd, a_ref[rows_now, :], b_ref[rows_now, :])
            lanes = pl.ds(pl.multiple_of(128 * q, 128), 128)
            for piece, kk in ((top, k), (bottom, k + side)):
                at = nf + lax.rem(kk, 2) * step
                pad_ref[1 + kk // 2, pl.ds(pl.multiple_of(at, 16), step), lanes] = piece.astype(BF)
        return carry

    lax.fori_loop(0, side, place, 0)
    conv_rest(side, rank, pad_ref, kt_ref, lt_ref, vec_ref, before_ref, after_ref,
              hid_ref, xhat_ref, rs_ref, mate_ref, keep_ref, sp_ref, ktm_ref, plane, nf, ch)


def conv_first_body(side, rank_ref, a_ref, kt_ref, lt_ref, vec_ref, before_ref, after_ref,
                    pad_ref, hid_ref, xhat_ref, rs_ref, mate_ref, keep_ref, sp_ref, ktm_ref):
    rank = rank_ref[0]
    ch = pad_ref.shape[2]
    plane = a_ref.shape[0] // side
    nf = plane // side
    zrow = jnp.zeros((pad_ref.shape[1], ch), BF)
    pad_ref[0] = zrow
    pad_ref[side + 1] = zrow
    zcol = jnp.zeros((nf, ch), BF)
    for i in range(side):
        pad_ref[i + 1, 0:nf] = zcol
        pad_ref[i + 1, nf + plane : 2 * nf + plane] = zcol
        pad_ref[i + 1, nf : nf + plane] = a_ref[i * plane : (i + 1) * plane]
    conv_rest(side, rank, pad_ref, kt_ref, lt_ref, vec_ref, before_ref, after_ref,
              hid_ref, xhat_ref, rs_ref, mate_ref, keep_ref, sp_ref, ktm_ref, plane, nf, ch)


def gather_columns(kt_ref, ktm_ref):
    width = kt_ref.shape[2]
    for z in range(kt_ref.shape[0]):
        ktm_ref[:, z * width : (z + 1) * width] = kt_ref[z]


def conv_rest(side, rank, pad_ref, kt_ref, lt_ref, vec_ref, before_ref, after_ref,
              hid_ref, xhat_ref, rs_ref, mate_ref, keep_ref, sp_ref, ktm_ref, plane, nf, ch):
    hc = hid_ref.shape[1]
    rows = plane * side
    gather_columns(kt_ref, ktm_ref)

    def conv(i, total):
        acc = jnp.zeros((plane, hc), F32)
        for t in range(9):
            r, c = t // 3, t % 3
            acc += nt(pad_ref[i + r, c * nf : c * nf + plane, :], ktm_ref[:, t * ch : (t + 1) * ch])
        sp_ref[i] = acc
        return total + jnp.sum(acc, axis=0, keepdims=True)

    mean = lax.fori_loop(0, side, conv, jnp.zeros((1, hc), F32)) / rows

    def square(i, total):
        cen = sp_ref[i] - mean
        return total + jnp.sum(cen * cen, axis=0, keepdims=True)

    var = lax.fori_loop(0, side, square, jnp.zeros((1, hc), F32)) / rows
    rs = lax.rsqrt(var + eps)
    rs_ref[...] = rs
    gain, bias = vec_ref[0:1, :], vec_ref[1:2, :]
    step = plane // 2

    def act(i, carry):
        xhat = (sp_ref[i] - mean) * rs
        xhat_ref[i] = xhat
        v = xhat * gain + bias
        sp_ref[i] = v * jax.nn.sigmoid(v)
        hid_ref[pl.ds(pl.multiple_of(i * plane, 16), plane), :] = sp_ref[i].astype(BF)
        return carry

    lax.fori_loop(0, side, act, 0)
    l0, l1, l2 = lt_ref[0:hc], lt_ref[hc : 2 * hc], lt_ref[2 * hc : 3 * hc]
    low = lax.broadcasted_iota(jnp.int32, (step, 128), 1) < 64

    def temporal(k, carry):
        pieces = []
        for kk in (k, k + side):
            par = lax.rem(kk, 2)
            h = sp_ref[kk // 2, pl.ds(pl.multiple_of(par * step, 8), step), :]
            at = pl.multiple_of(par * (step % nf), 8)
            pieces.append((
                (pltpu.roll(h, 1, 0) * before_ref[pl.ds(at, step), :]).astype(BF),
                h.astype(BF),
                (pltpu.roll(h, step - 1, 0) * after_ref[pl.ds(at, step), :]).astype(BF),
            ))
        prev, here, nxt = [jnp.concatenate([x, y], axis=0) for x, y in zip(*pieces)]
        part = nn(prev, l0) + nn(here, l1) + nn(nxt, l2)
        store_packed(rank, mate_ref, keep_ref, part, k, step, low)
        return carry

    lax.fori_loop(0, side, temporal, 0)


def store_packed(rank, mate_ref, keep_ref, part, k, step, low):
    rows_now = pl.ds(pl.multiple_of(k * step, 16), step)
    odd = lax.rem(rank, 2) == 1
    for q in range(keep_ref.shape[0]):
        x = part[:step, 128 * q : 128 * q + 128]
        y = part[step:, 128 * q : 128 * q + 128]
        even_slice = jnp.where(low, x, pltpu.roll(y, 64, 1))
        odd_slice = jnp.where(low, pltpu.roll(x, 64, 1), y)
        p = lax.bitwise_xor(rank // 2, q)
        keep_ref[p, rows_now, :] = jnp.where(odd, odd_slice, even_slice).astype(BF)
        mate_ref[p, rows_now, :] = jnp.where(odd, even_slice, odd_slice).astype(BF)


def conv_forward(rank, g, kt, lt, vec, before, after, side, pixels, ch):
    hc = lt.shape[0] // 3
    plane = pixels // side
    nf = plane // side
    first = len(g) == 1
    body = functools.partial(conv_first_body if first else conv_in_body, side)
    outs = [
        jax.ShapeDtypeStruct((side + 2, plane + 2 * nf, ch), BF),
        jax.ShapeDtypeStruct((pixels, hc), BF),
        jax.ShapeDtypeStruct((side, plane, hc), F32),
        jax.ShapeDtypeStruct((1, hc), F32),
        jax.ShapeDtypeStruct((4, pixels // 2, 128), BF),
        jax.ShapeDtypeStruct((4, pixels // 2, 128), BF),
    ]
    scratch = [pltpu.VMEM((side, plane, hc), F32), pltpu.VMEM((hc, 9 * ch), BF)]
    flops = 2 * pixels * hc * 12 * ch
    return call(body, outs, scratch, flops, rank, *g, kt, lt, vec, before, after)


def fold(v):
    return v + pltpu.roll(v, 64, 1)


def total_of(refs):
    t = refs[0][...].astype(F32)
    for ref in refs[1:]:
        t += ref[...].astype(F32)
    return t


def pair_sum_body(keep_ref, mate_ref, *out_refs):
    for p, ref in enumerate(out_refs):
        ref[...] = (keep_ref[p].astype(F32) + mate_ref[p].astype(F32)).astype(ref.dtype)


def pair_sum(keep, arrived):
    shape = keep.shape[1:]
    outs = [jax.ShapeDtypeStruct(shape, BF)] * keep.shape[0]
    return call(pair_sum_body, outs, [], keep.size, keep, arrived)


def out_norm_body(n, has_skip, *refs):
    parts, refs = refs[:n], refs[n:]
    if has_skip:
        vec_ref, skip_ref, xhat_ref, rs_ref, pre_ref, res_ref = refs
    else:
        vec_ref, xhat_ref, rs_ref, pre_ref, res_ref = refs
    t = total_of(parts)
    pixels = 2 * t.shape[0]
    mean = fold(jnp.sum(t, axis=0, keepdims=True)) / pixels
    cen = t - mean
    rs = lax.rsqrt(fold(jnp.sum(cen * cen, axis=0, keepdims=True)) / pixels + eps)
    xhat = cen * rs
    pre = xhat * vec_ref[0:1, :] + vec_ref[1:2, :]
    if has_skip:
        pre = pre + skip_ref[...].astype(F32)
    xhat_ref[...] = xhat
    rs_ref[...] = rs
    pre_ref[...] = pre
    res_ref[...] = (pre * jax.nn.sigmoid(pre)).astype(BF)


def out_norm(parts, vec, skip):
    half = parts[0].shape[0]
    outs = [
        jax.ShapeDtypeStruct((half, 128), F32),
        jax.ShapeDtypeStruct((1, 128), F32),
        jax.ShapeDtypeStruct((half, 128), F32),
        jax.ShapeDtypeStruct((half, 128), BF),
    ]
    args = (*parts, vec) + (() if skip is None else (skip,))
    body = functools.partial(out_norm_body, len(parts), skip is not None)
    return call(body, outs, [], half * 128 * 10, *args)


def out_back_body(n, *refs):
    parts, (pre_ref, xhat_ref, rs_ref, vec_ref, dpre_ref, dt_ref, sums_ref) = refs[:n], refs[n:]
    g = total_of(parts)
    pre, xhat = pre_ref[...], xhat_ref[...]
    sig = jax.nn.sigmoid(pre)
    dpre = g * (sig * (1.0 + pre * (1.0 - sig)))
    pixels = 2 * pre.shape[0]
    sb = fold(jnp.sum(dpre, axis=0, keepdims=True))
    sg = fold(jnp.sum(dpre * xhat, axis=0, keepdims=True))
    dpre_ref[...] = dpre.astype(BF)
    scale = vec_ref[0:1, :] * rs_ref[...]
    dt_ref[...] = (scale * (dpre - sb / pixels - xhat * (sg / pixels))).astype(BF)
    sums_ref[0:1, :] = sg
    sums_ref[1:2, :] = sb


def out_back(parts, pre, xhat, rs, vec):
    half = pre.shape[0]
    outs = [
        jax.ShapeDtypeStruct((half, 128), BF),
        jax.ShapeDtypeStruct((half, 128), BF),
        jax.ShapeDtypeStruct((2, 128), F32),
    ]
    args = (*parts, pre, xhat, rs, vec)
    return call(functools.partial(out_back_body, len(parts)), outs, [], half * 1280, *args)


def conv_back_body(side, rank_ref, *refs):
    slices, (xhat_ref, rs_ref, kt_ref, lt_ref, vec_ref, before_ref, after_ref, dt_ref, ds_ref,
             sums_ref, mate_ref, keep_ref, dy_ref, pad_ref, ktm_ref) = refs[:8], refs[8:]
    half = slices[0].shape[0]
    rank = rank_ref[0]
    rows = 2 * half
    plane = rows // side
    nf = plane // side
    step = plane // 2
    hc = ds_ref.shape[1]
    ch = dt_ref.shape[1]
    gather_columns(kt_ref, ktm_ref)
    zrow = jnp.zeros((pad_ref.shape[1], hc), BF)
    pad_ref[0] = zrow
    pad_ref[side + 1] = zrow
    zcol = jnp.zeros((nf, hc), BF)
    for i in range(side):
        pad_ref[i + 1, 0:nf] = zcol
        pad_ref[i + 1, nf + plane : 2 * nf + plane] = zcol

    def place(k, carry):
        at = pl.multiple_of(k * step, 16)
        for q, odd, a_ref, b_ref in by_rank(slices, rank):
            top, bottom = halves(odd, a_ref[pl.ds(at, step), :], b_ref[pl.ds(at, step), :])
            lanes = pl.ds(pl.multiple_of(128 * q, 128), 128)
            dt_ref[pl.ds(at, step), lanes] = top.astype(BF)
            dt_ref[pl.ds(pl.multiple_of(half + k * step, 16), step), lanes] = bottom.astype(BF)
        return carry

    lax.fori_loop(0, side, place, 0)
    l0, l1, l2 = lt_ref[0:hc], lt_ref[hc : 2 * hc], lt_ref[2 * hc : 3 * hc]
    gain, bias = vec_ref[0:1, :], vec_ref[1:2, :]

    def hidden_grad(i, sums):
        dt = dt_ref[pl.ds(pl.multiple_of(i * plane, 16), plane), :]
        early = nt(dt, l0) * before_ref[0:plane, :]
        late = nt(dt, l2) * after_ref[0:plane, :]
        dh = nt(dt, l1) + pltpu.roll(early, plane - 1, 0) + pltpu.roll(late, 1, 0)
        xhat = xhat_ref[i]
        v = xhat * gain + bias
        sig = jax.nn.sigmoid(v)
        dy = dh * (sig * (1.0 + v * (1.0 - sig)))
        dy_ref[i] = dy
        return (
            sums[0] + jnp.sum(dy * xhat, axis=0, keepdims=True),
            sums[1] + jnp.sum(dy, axis=0, keepdims=True),
        )

    zero = jnp.zeros((1, hc), F32)
    sg, sb = lax.fori_loop(0, side, hidden_grad, (zero, zero))
    sums_ref[0:1, :] = sg
    sums_ref[1:2, :] = sb
    scale = gain * rs_ref[...]

    def spatial_grad(i, carry):
        ds = (scale * (dy_ref[i] - sb / rows - xhat_ref[i] * (sg / rows))).astype(BF)
        pad_ref[i + 1, nf : nf + plane] = ds
        ds_ref[pl.ds(pl.multiple_of(i * plane, 16), plane), :] = ds
        return carry

    lax.fori_loop(0, side, spatial_grad, 0)

    low = lax.broadcasted_iota(jnp.int32, (step, 128), 1) < 64

    def back(k, carry):
        acc = jnp.zeros((2 * step, ch), F32)
        for t in range(9):
            r, c = 2 - t // 3, 2 - t % 3
            pieces = []
            for kk in (k, k + side):
                at = c * nf + lax.rem(kk, 2) * step
                pieces.append(pad_ref[kk // 2 + r, pl.ds(pl.multiple_of(at, 16), step), :])
            acc += nn(jnp.concatenate(pieces, axis=0), ktm_ref[:, t * ch : (t + 1) * ch])
        store_packed(rank, mate_ref, keep_ref, acc, k, step, low)
        return carry

    lax.fori_loop(0, side, back, 0)


def conv_back(rank, g, xhat, rs, kt, lt, vec, before, after, side):
    half = g[0].shape[0]
    hc = lt.shape[0] // 3
    ch = lt.shape[1]
    pixels = 2 * half
    plane = pixels // side
    nf = plane // side
    outs = [
        jax.ShapeDtypeStruct((pixels, ch), BF),
        jax.ShapeDtypeStruct((pixels, hc), BF),
        jax.ShapeDtypeStruct((2, hc), F32),
        jax.ShapeDtypeStruct((4, half, 128), BF),
        jax.ShapeDtypeStruct((4, half, 128), BF),
    ]
    scratch = [
        pltpu.VMEM((side, plane, hc), F32),
        pltpu.VMEM((side + 2, plane + 2 * nf, hc), BF),
        pltpu.VMEM((hc, 9 * ch), BF),
    ]
    flops = 2 * pixels * hc * 12 * ch
    body = functools.partial(conv_back_body, side)
    return call(body, outs, scratch, flops, rank, *g, xhat, rs, kt, lt, vec, before, after)


def grads_body(side, pad_ref, hid_ref, ds_ref, dt_ref, before_ref, after_ref, sg_ref, tg_ref,
               dst_ref, p_ref, n_ref, h_ref):
    ch = pad_ref.shape[2]
    hc = hid_ref.shape[1]
    plane = hid_ref.shape[0] // side
    nf = plane // side

    def flip(i, carry):
        at = pl.ds(pl.multiple_of(i * plane, 16), plane)
        h = hid_ref[at, :].astype(F32)
        p_ref[i] = (pltpu.roll(h, 1, 0) * before_ref[0:plane, :]).T.astype(BF)
        n_ref[i] = (pltpu.roll(h, plane - 1, 0) * after_ref[0:plane, :]).T.astype(BF)
        h_ref[i] = h.T.astype(BF)
        dst_ref[i] = ds_ref[at, :].astype(F32).T.astype(BF)
        return carry

    lax.fori_loop(0, side, flip, 0)
    for t, src in enumerate((p_ref, h_ref, n_ref)):
        acc = jnp.zeros((hc, ch), F32)
        for i in range(side):
            acc += nn(src[i], dt_ref[i * plane : (i + 1) * plane, :])
        tg_ref[t * hc : (t + 1) * hc, :] = acc.astype(BF)
    width = sg_ref.shape[2]
    for t in range(9):
        r, c = t // 3, t % 3
        acc = jnp.zeros((hc, ch), F32)
        for i in range(side):
            acc += nn(dst_ref[i], pad_ref[i + r, c * nf : c * nf + plane, :])
        first = t * ch
        while first < (t + 1) * ch:
            z = first // width
            last = min((t + 1) * ch, (z + 1) * width)
            sg_ref[z, :, first - z * width : last - z * width] = (
                acc[:, first - t * ch : last - t * ch].astype(BF)
            )
            first = last


def kernel_grads(pad, hidden, ds, dt, before, after, side, nz):
    pixels, hc = hidden.shape
    ch = dt.shape[1]
    plane = pixels // side
    outs = [
        jax.ShapeDtypeStruct((nz, hc, 9 * ch // nz), BF),
        jax.ShapeDtypeStruct((3 * hc, ch), BF),
    ]
    scratch = [pltpu.VMEM((side, hc, plane), BF)] * 4
    flops = 2 * pixels * hc * 12 * ch
    return call(functools.partial(grads_body, side), outs, scratch, flops,
                pad, hidden, ds, dt, before, after)


def hop(v, k):
    n = 1
    for name in EVERY:
        n *= lax.axis_size(name)
    return lax.ppermute(v, EVERY, [(i, i ^ k) for i in range(n)])


def plane_gather(v):
    got = {0: v}
    for k in (6, 2, 4, 1):
        got[k] = hop(v, k)
    for k in (2, 4, 6):
        got[k ^ 1] = hop(got[k], 1)
    return [got[k] for k in range(8)]


def plane_reduce(mate, keep):
    sums = pair_sum(keep, hop(mate, 1))
    arrived = {k: hop(sums[k // 2], k) for k in (6, 2, 4)}
    return [sums[0], arrived[2], arrived[4], arrived[6]]


def on_device(frames, cot, starts, ks, ktm, mg, mb, og, ob):
    nz, n_rank, n_seg = lax.axis_size("z"), 8, 4
    n_dp = nz * 2
    fr, side, ch = frames.shape[0], frames.shape[1], frames.shape[3]
    area = side * side
    hid = ks.shape[2]
    hc, cc = hid // n_rank, ch // n_rank
    q = hc // n_rank
    rank = lax.axis_index(PLANE)
    rank_now = rank.astype(jnp.int32).reshape(1)
    d_index = lax.axis_index(("z", "y"))
    nf = n_dp * fr
    pixels = area * nf
    half = pixels // 2

    to_plane = [(d * n_seg + s, s * n_rank + d) for d in range(n_dp) for s in range(n_seg)]
    from_plane = [(b, a) for a, b in to_plane]
    rows = fr * area
    flag_row = jnp.pad(starts.astype(BF)[None], ((0, 11), (0, ch - fr)))
    moving = jnp.concatenate([frames.reshape(rows, ch), flag_row], axis=0)
    moving = lax.ppermute(moving, EVERY, to_plane)
    gathered = lax.all_gather(moving, PLANE, axis=0)

    perm = (jnp.arange(hid).reshape(n_rank, n_rank, q).transpose(1, 0, 2).reshape(hid)[:, None]
            == jnp.arange(hid)[None, :]).astype(BF)
    kt = lax.dot_general(perm, ks[0].astype(BF), (((1,), (1,)), ((), ())),
                         preferred_element_type=F32).astype(BF)
    kt = kt.reshape(n_rank, hc, ks.shape[1])
    kt = lax.all_to_all(kt, PLANE, 0, 0)
    kt = kt.reshape(2, n_seg, hc, ks.shape[1]).transpose(1, 2, 0, 3).reshape(n_seg, hc, -1)
    lrows = ktm.shape[1] // n_rank
    lt = ktm[0].astype(BF).reshape(-1, n_rank, q, ch).transpose(1, 0, 2, 3).reshape(n_rank, lrows, ch)
    extra = jnp.concatenate([v.astype(BF) for v in (mg, mb, og, ob)], axis=1)
    extra = jnp.pad(extra, ((0, 1), (0, ch - extra.shape[1])))
    lt = jnp.concatenate([lt, jnp.broadcast_to(extra, (n_rank, 2, ch))], axis=1)
    lt = lax.all_to_all(lt, PLANE, 0, 0)
    lt = lt.reshape(2, n_seg, lrows + 2, ch).transpose(1, 0, 2, 3).reshape(n_seg, 2 * (lrows + 2), ch)
    kts = [lax.all_gather(kt[0], "z", axis=0)]
    lt = lax.all_gather(lt, "z", axis=0).reshape(nz, n_seg, 2, lrows + 2, ch)
    kts += [lax.all_gather(kt[s], "z", axis=0) for s in range(1, n_seg)]
    lts, mids, outs = [], [], []
    for s in range(n_seg):
        full = lt[:, s].reshape(n_dp, lrows + 2, ch)
        lts.append(full[:, :lrows].reshape(3 * hc, ch))
        row = full[:, lrows].astype(F32)
        mids.append(jnp.stack([
            lax.dynamic_slice_in_dim(row[:, i * hc : (i + 1) * hc], rank * q, q, axis=1).reshape(hc)
            for i in range(2)]))
        own = lax.dynamic_index_in_dim(row, rank, 0, keepdims=False)
        outs.append(jnp.stack([
            jnp.tile(own[2 * hc + i * cc : 2 * hc + (i + 1) * cc], 2) for i in range(2)]))

    def by_pixel(v):
        width = v.shape[2]
        v = v.reshape(n_rank * fr, area, width).transpose(1, 0, 2)
        return v.reshape(pixels, width)

    def packed(v):
        return jnp.concatenate([v[:half], v[half:]], axis=1)

    a0 = by_pixel(gathered[:, :rows])
    flags = gathered[:, rows, :fr].reshape(nf) > 0.5
    slot = jnp.arange(nf) % fr
    before = jnp.where(flags | (slot == 0), 0.0, 1.0)
    after = jnp.where(jnp.roll(flags, -1) | (slot == fr - 1), 0.0, 1.0)
    spread = (side * nf + nf, hc)
    before = jnp.broadcast_to(jnp.tile(before, side + 1)[:, None], spread)
    after = jnp.broadcast_to(jnp.tile(after, side + 1)[:, None], spread)
    skip = packed(lax.dynamic_slice_in_dim(a0, rank * cc, cc, axis=1))

    cot_moving = lax.ppermute(cot.reshape(rows, ch), EVERY, to_plane)
    cot_moving = cot_moving.reshape(rows, n_rank, cc).transpose(1, 0, 2)
    cot_own = packed(by_pixel(lax.all_to_all(cot_moving, PLANE, 0, 0)))

    def to_frames(v):
        v = jnp.concatenate([v[:, :cc], v[:, cc:]], axis=0)
        v = v.reshape(area, n_rank, fr, cc).transpose(1, 0, 2, 3).reshape(n_rank, rows, cc)
        v = lax.all_to_all(v, PLANE, 0, 0).transpose(1, 0, 2).reshape(area, fr, ch)
        return lax.ppermute(v, EVERY, from_plane).transpose(1, 0, 2).reshape(frames.shape)

    saved = []
    g = [a0]
    for s in range(n_seg):
        pad, hidden, xm, rm, mate, keep = conv_forward(
            rank_now, g, kts[s], lts[s], mids[s], before, after, side, pixels, ch)
        parts = plane_reduce(mate, keep)
        xo, ro, pre, res = out_norm(parts, outs[s], skip if s % 2 == 1 else None)
        saved.append((pad, hidden, xm, rm, xo, ro, pre))
        if s % 2 == 1:
            skip = res
        if s < n_seg - 1:
            g = plane_gather(res)
    output = to_frames(res)

    parts = [cot_own]
    skip_grad = None
    sgrads, tgrads = [], []
    for s in reversed(range(n_seg)):
        pad, hidden, xm, rm, xo, ro, pre = saved[s]
        if s == 1:
            parts = parts + [skip_grad]
        dpre, dt, osum = out_back(parts, pre, xo, ro, outs[s])
        if s % 2 == 1:
            skip_grad = dpre
        dtf, ds, msum, mate, keep = conv_back(
            rank_now, plane_gather(dt), xm, rm, kts[s], lts[s], mids[s], before, after, side)
        sg, tg = kernel_grads(pad, hidden, ds, dtf, before, after, side, nz)
        row = jnp.concatenate([msum[0], msum[1], osum[0, :cc], osum[1, :cc]]).astype(BF)
        row = jnp.pad(row[None], ((0, 1), (0, ch - row.shape[0])))
        tg = jnp.concatenate(
            [tg.reshape(n_dp, lrows, ch), jnp.broadcast_to(row, (n_dp, 2, ch))], axis=1)
        sgrads.append(lax.psum_scatter(sg, "z", scatter_dimension=0))
        tgrads.append(lax.psum_scatter(tg.reshape(nz, -1, ch), "z", scatter_dimension=0))
        parts = plane_reduce(mate, keep)

    da = sum(p.astype(F32) for p in parts) + skip_grad.astype(F32)
    frames_grad = to_frames(da.astype(BF)).astype(F32)

    tg = jnp.stack(tgrads[::-1])
    sg = jnp.stack(sgrads[::-1])
    sg = sg.reshape(n_seg, hc, 2, -1).transpose(2, 0, 1, 3).reshape(n_rank, hc, -1)
    sg = lax.all_to_all(sg, PLANE, 0, 0).reshape(hid, -1)
    space_grad = lax.dot_general(sg, perm, (((0,), (0,)), ((), ())), preferred_element_type=F32)
    tg = tg.reshape(n_seg, 2, lrows + 2, ch).transpose(1, 0, 2, 3).reshape(n_rank, lrows + 2, ch)
    tg = lax.all_to_all(tg, PLANE, 0, 0)
    row = tg[:, lrows].astype(F32)
    tg = tg[:, :lrows].reshape(n_rank, -1, q, ch)
    time_grad = tg.transpose(1, 0, 2, 3).reshape(-1, ch).astype(F32)
    own = lax.dynamic_index_in_dim(row, d_index, 0, keepdims=True)
    return (
        output,
        frames_grad,
        space_grad[None],
        time_grad[None],
        lax.dynamic_slice_in_dim(row[:, :hc], d_index * q, q, axis=1).reshape(1, hc),
        lax.dynamic_slice_in_dim(row[:, hc : 2 * hc], d_index * q, q, axis=1).reshape(1, hc),
        own[:, 2 * hc : 2 * hc + cc],
        own[:, 2 * hc + cc : 2 * hc + 2 * cc],
    )


def from_behind(value, axis, steps):
    count = lax.axis_size(axis)
    leading, last = (max(0, -steps), min(count, count - steps))
    return lax.ppermute(value, axis, [(source, source + steps) for source in range(leading, last)])


def space_apply(current, kernel):
    frame_side = current.shape[1]
    padded = jnp.pad(current, ((0, 0), (1, 1), (1, 1), (0, 0)))
    stacked = jnp.concatenate(
        [
            padded[:, row_shift : row_shift + frame_side, col_shift : col_shift + frame_side, :]
            for row_shift in range(3)
            for col_shift in range(3)
        ],
        axis=-1,
    )
    return (
        stacked,
        jnp.einsum("fijc,co->fijo", stacked, kernel, preferred_element_type=jnp.float32),
    )


def space_back(gradient, kernel):
    frame_side = gradient.shape[1]
    channels = kernel.shape[0] // 9
    spread = jnp.einsum("fijo,co->fijc", gradient, kernel, preferred_element_type=jnp.float32)
    total = jnp.zeros((gradient.shape[0], frame_side + 2, frame_side + 2, channels), jnp.float32)
    for tap_index in range(9):
        row_shift = tap_index // 3
        col_shift = tap_index % 3
        piece_now = spread[..., tap_index * channels : (tap_index + 1) * channels]
        total = total + jnp.pad(
            piece_now, ((0, 0), (row_shift, 2 - row_shift), (col_shift, 2 - col_shift), (0, 0))
        )
    return total[:, 1 : frame_side + 1, 1 : frame_side + 1, :]


def time_apply(current, kernel, before_mask, after_mask):
    blanks = jnp.zeros_like(current[:1])
    earlier = jnp.concatenate([blanks, current[:-1]], axis=0) * before_mask[
        :, None, None, None
    ].astype(current.dtype)
    later = jnp.concatenate([current[1:], blanks], axis=0) * after_mask[:, None, None, None].astype(
        current.dtype
    )
    stacked = jnp.concatenate([earlier, current, later], axis=-1)
    return (
        stacked,
        jnp.einsum("fijc,co->fijo", stacked, kernel, preferred_element_type=jnp.float32),
    )


def time_back(gradient, kernel, before_mask, after_mask):
    channels = kernel.shape[0] // 3
    spread = jnp.einsum("fijo,co->fijc", gradient, kernel, preferred_element_type=jnp.float32)
    early_part = spread[..., :channels] * before_mask[:, None, None, None]
    late_part = spread[..., 2 * channels :] * after_mask[:, None, None, None]
    blanks = jnp.zeros_like(early_part[:1])
    moved_early = jnp.concatenate([early_part[1:], blanks], axis=0)
    moved_late = jnp.concatenate([blanks, late_part[:-1]], axis=0)
    return spread[..., channels : 2 * channels] + moved_early + moved_late


def moments(values, pixel_count):
    average = lax.psum(jnp.sum(values, axis=(0, 1, 2)), "dp") / pixel_count
    centered = values - average
    spread = lax.psum(jnp.sum(centered * centered, axis=(0, 1, 2)), "dp") / pixel_count
    return (average, lax.rsqrt(spread + eps))


def reduce_back(gradient, normed):
    return lax.psum(
        (jnp.sum(gradient, axis=(0, 1, 2)), jnp.sum(gradient * normed, axis=(0, 1, 2))), "dp"
    )


def silu_slope(values):
    sigmoid_now = jax.nn.sigmoid(values)
    return sigmoid_now * (1.0 + values * (1.0 - sigmoid_now))


def pick_slot(stack, slot_index):
    return lax.dynamic_index_in_dim(stack, slot_index, 0, keepdims=False)


def store_slot(stack, value, slot_index, usable):
    previous = pick_slot(stack, slot_index)
    return lax.dynamic_update_index_in_dim(stack, jnp.where(usable, value, previous), slot_index, 0)


def on_device_general(
    frames, cotangent, starts, space_kernel, time_kernel, mid_gain, mid_bias, out_gain, out_bias
):
    n_segment = lax.axis_size("segment")
    n_data = lax.axis_size("dp")
    segment_index = lax.axis_index("segment")
    odd_segment = segment_index % 2 == 1
    last_segment = segment_index == n_segment - 1
    first_segment = segment_index == 0
    frame_count = frames.shape[0]
    frame_side = frames.shape[1]
    channels = frames.shape[3]
    hidden_units = mid_gain.shape[1] * n_data
    pixel_count = n_data * frame_count * frame_side * frame_side
    turns = 2 * n_segment - 1
    block_shape = (n_segment,) + frames.shape
    all_frames, all_cot, all_starts = (
        lax.all_gather(frames, "segment", axis=0, tiled=True),
        lax.all_gather(cotangent, "segment", axis=0, tiled=True),
        lax.all_gather(starts.astype(jnp.bfloat16), "segment", axis=0, tiled=True),
    )
    frame_stack = all_frames.reshape(block_shape)
    cot_stack = all_cot.reshape(block_shape)
    clip_flags = all_starts.astype(jnp.float32).reshape(n_segment, frame_count)
    positions = jnp.arange(frame_count)
    before_mask = jnp.where((clip_flags > 0.5) | (positions == 0), 0.0, 1.0)
    following = jnp.concatenate([clip_flags[:, 1:], jnp.ones((n_segment, 1), jnp.float32)], axis=1)
    after_mask = jnp.where(following > 0.5, 0.0, 1.0)
    gathered = (
        lax.all_gather(space_kernel[0].astype(jnp.bfloat16), "dp", axis=0, tiled=True),
        lax.all_gather(time_kernel[0].astype(jnp.bfloat16), "dp", axis=0, tiled=True),
        lax.all_gather(mid_gain[0].astype(jnp.bfloat16), "dp", axis=0, tiled=True),
        lax.all_gather(mid_bias[0].astype(jnp.bfloat16), "dp", axis=0, tiled=True),
        lax.all_gather(out_gain[0].astype(jnp.bfloat16), "dp", axis=0, tiled=True),
        lax.all_gather(out_bias[0].astype(jnp.bfloat16), "dp", axis=0, tiled=True),
    )
    space_low, time_low = (gathered[0], gathered[1])
    mid_gain_now = gathered[2].astype(jnp.float32)
    mid_bias_now = gathered[3].astype(jnp.float32)
    out_gain_now = gathered[4].astype(jnp.float32)
    out_bias_now = gathered[5].astype(jnp.float32)
    incoming = jnp.zeros_like(frames)
    carried = jnp.zeros_like(frames)
    kept_input = jnp.zeros(block_shape, jnp.bfloat16)
    kept_skip = jnp.zeros(block_shape, jnp.bfloat16)
    kept_mid_mean = jnp.zeros((n_segment, hidden_units), jnp.float32)
    kept_mid_scale = jnp.zeros((n_segment, hidden_units), jnp.float32)
    kept_out_mean = jnp.zeros((n_segment, channels), jnp.float32)
    kept_out_scale = jnp.zeros((n_segment, channels), jnp.float32)
    results = jnp.zeros(block_shape, jnp.float32)
    for turn_index in range(turns):
        micro_index = turn_index - segment_index
        usable = (micro_index >= 0) & (micro_index < n_segment)
        slot_index = jnp.clip(micro_index, 0, n_segment - 1)
        current = jnp.where(first_segment, pick_slot(frame_stack, slot_index), incoming)
        skip_input = carried
        _, spatial = space_apply(current, space_low)
        mid_mean, mid_scale = moments(spatial, pixel_count)
        hidden_act = jax.nn.silu(
            (spatial - mid_mean) * mid_scale * mid_gain_now + mid_bias_now
        ).astype(jnp.bfloat16)
        _, temporal = time_apply(
            hidden_act,
            time_low,
            pick_slot(before_mask, slot_index),
            pick_slot(after_mask, slot_index),
        )
        out_mean, out_scale = moments(temporal, pixel_count)
        pre_act = (
            (temporal - out_mean) * out_scale * out_gain_now
            + out_bias_now
            + jnp.where(odd_segment, skip_input.astype(jnp.float32), 0.0)
        )
        result = jax.nn.silu(pre_act).astype(jnp.bfloat16)
        kept_input = store_slot(kept_input, current, slot_index, usable)
        kept_skip = store_slot(kept_skip, skip_input, slot_index, usable)
        kept_mid_mean = store_slot(kept_mid_mean, mid_mean, slot_index, usable)
        kept_mid_scale = store_slot(kept_mid_scale, mid_scale, slot_index, usable)
        kept_out_mean = store_slot(kept_out_mean, out_mean, slot_index, usable)
        kept_out_scale = store_slot(kept_out_scale, out_scale, slot_index, usable)
        results = store_slot(results, result.astype(jnp.float32), slot_index, usable)
        if turn_index < turns - 1:
            incoming, carried = from_behind(
                (result, jnp.where(odd_segment, result, current)), "segment", 1
            )
    gathered = (
        lax.all_gather(space_kernel[0].astype(jnp.bfloat16), "dp", axis=0, tiled=True),
        lax.all_gather(time_kernel[0].astype(jnp.bfloat16), "dp", axis=0, tiled=True),
        lax.all_gather(mid_gain[0].astype(jnp.bfloat16), "dp", axis=0, tiled=True),
        lax.all_gather(mid_bias[0].astype(jnp.bfloat16), "dp", axis=0, tiled=True),
        lax.all_gather(out_gain[0].astype(jnp.bfloat16), "dp", axis=0, tiled=True),
        lax.all_gather(out_bias[0].astype(jnp.bfloat16), "dp", axis=0, tiled=True),
    )
    space_low, time_low = (gathered[0], gathered[1])
    mid_gain_now = gathered[2].astype(jnp.float32)
    mid_bias_now = gathered[3].astype(jnp.float32)
    out_gain_now = gathered[4].astype(jnp.float32)
    out_bias_now = gathered[5].astype(jnp.float32)
    grad_input = jnp.zeros_like(frames)
    grad_skip = jnp.zeros_like(frames)
    space_acc = jnp.zeros(space_low.shape, jnp.float32)
    time_acc = jnp.zeros(time_low.shape, jnp.float32)
    mid_gain_acc = jnp.zeros((hidden_units,), jnp.float32)
    mid_bias_acc = jnp.zeros((hidden_units,), jnp.float32)
    out_gain_acc = jnp.zeros((channels,), jnp.float32)
    out_bias_acc = jnp.zeros((channels,), jnp.float32)
    input_grads = jnp.zeros(block_shape, jnp.float32)
    for turn_index in range(turns):
        micro_index = n_segment - 1 - (turn_index - (n_segment - 1 - segment_index))
        usable = (micro_index >= 0) & (micro_index < n_segment)
        usable_weight = usable.astype(jnp.float32)
        slot_index = jnp.clip(micro_index, 0, n_segment - 1)
        current = pick_slot(kept_input, slot_index)
        skip_input = pick_slot(kept_skip, slot_index)
        before_now = pick_slot(before_mask, slot_index)
        after_now = pick_slot(after_mask, slot_index)
        space_taps, spatial = space_apply(current, space_low)
        mid_normed = (spatial - pick_slot(kept_mid_mean, slot_index)) * pick_slot(
            kept_mid_scale, slot_index
        )
        mid_pre = mid_normed * mid_gain_now + mid_bias_now
        hidden_act = jax.nn.silu(mid_pre).astype(jnp.bfloat16)
        time_taps, temporal = time_apply(hidden_act, time_low, before_now, after_now)
        out_scale = pick_slot(kept_out_scale, slot_index)
        out_normed = (temporal - pick_slot(kept_out_mean, slot_index)) * out_scale
        pre_act = (
            out_normed * out_gain_now
            + out_bias_now
            + jnp.where(odd_segment, skip_input.astype(jnp.float32), 0.0)
        )
        grad_result = jnp.where(
            last_segment,
            pick_slot(cot_stack, slot_index).astype(jnp.float32),
            grad_input.astype(jnp.float32)
            + jnp.where(odd_segment, grad_skip.astype(jnp.float32), 0.0),
        )
        grad_pre = grad_result * silu_slope(pre_act)
        out_bias_sum, out_gain_sum = reduce_back(grad_pre, out_normed)
        grad_temporal = (
            out_gain_now
            * out_scale
            * (grad_pre - out_bias_sum / pixel_count - out_normed * out_gain_sum / pixel_count)
        ).astype(jnp.bfloat16)
        time_acc = time_acc + usable_weight * jnp.einsum(
            "fijc,fijo->co", time_taps, grad_temporal, preferred_element_type=jnp.float32
        )
        grad_hidden = time_back(grad_temporal, time_low, before_now, after_now)
        grad_mid = grad_hidden * silu_slope(mid_pre)
        mid_bias_sum, mid_gain_sum = reduce_back(grad_mid, mid_normed)
        mid_scale = pick_slot(kept_mid_scale, slot_index)
        grad_spatial = (
            mid_gain_now
            * mid_scale
            * (grad_mid - mid_bias_sum / pixel_count - mid_normed * mid_gain_sum / pixel_count)
        ).astype(jnp.bfloat16)
        space_acc = space_acc + usable_weight * jnp.einsum(
            "fijc,fijo->co", space_taps, grad_spatial, preferred_element_type=jnp.float32
        )
        grad_current = space_back(grad_spatial, space_low)
        mid_gain_acc = mid_gain_acc + usable_weight * mid_gain_sum
        mid_bias_acc = mid_bias_acc + usable_weight * mid_bias_sum
        out_gain_acc = out_gain_acc + usable_weight * out_gain_sum
        out_bias_acc = out_bias_acc + usable_weight * out_bias_sum
        input_grads = store_slot(
            input_grads, grad_current + grad_skip.astype(jnp.float32), slot_index, usable
        )
        if turn_index < turns - 1:
            grad_input, grad_skip = from_behind(
                (
                    grad_current.astype(jnp.bfloat16),
                    jnp.where(odd_segment, grad_pre.astype(jnp.bfloat16), grad_skip),
                ),
                "segment",
                -1,
            )
    space_grad, time_grad = (
        lax.psum_scatter(space_acc, "dp", scatter_dimension=0, tiled=True),
        lax.psum_scatter(time_acc, "dp", scatter_dimension=0, tiled=True),
    )
    data_index = lax.axis_index("dp")

    def own_share(full_vector):
        share = full_vector.shape[0] // n_data
        return lax.dynamic_slice_in_dim(full_vector, data_index * share, share)[None]

    flat_shape = (n_segment * frame_count,) + frames.shape[1:]
    arrived_out, arrived_grads = (
        lax.all_to_all(
            results.reshape(flat_shape).astype(jnp.bfloat16),
            "segment",
            split_axis=0,
            concat_axis=0,
            tiled=True,
        ).astype(jnp.float32),
        lax.all_to_all(
            input_grads.reshape(flat_shape).astype(jnp.bfloat16),
            "segment",
            split_axis=0,
            concat_axis=0,
            tiled=True,
        ).astype(jnp.float32),
    )
    output = arrived_out[(n_segment - 1) * frame_count :].astype(jnp.bfloat16)
    frames_grad = arrived_grads[:frame_count]
    return (
        output,
        frames_grad,
        space_grad[None],
        time_grad[None],
        own_share(mid_gain_acc),
        own_share(mid_bias_acc),
        own_share(out_gain_acc),
        own_share(out_bias_acc),
    )


def general(mesh):
    return jax.shard_map(
        on_device_general,
        mesh=mesh,
        in_specs=(
            P(("dp", "segment"), None, None, None),
            P(("dp", "segment"), None, None, None),
            P(("dp", "segment")),
            P("segment", "dp", None),
            P("segment", "dp", None),
            P("segment", "dp"),
            P("segment", "dp"),
            P("segment", "dp"),
            P("segment", "dp"),
        ),
        out_specs=(
            P(("dp", "segment"), None, None, None),
            P(("dp", "segment"), None, None, None),
            P("segment", "dp", None),
            P("segment", "dp", None),
            P("segment", "dp"),
            P("segment", "dp"),
            P("segment", "dp"),
            P("segment", "dp"),
        ),
        check_vma=False,
    )


def solution(mesh):
    if mesh.shape["dp"] != 8 or mesh.shape["segment"] != 4:
        return general(mesh)
    n_dp, n_seg = mesh.shape["dp"], mesh.shape["segment"]
    fine = Mesh(mesh.devices.reshape(n_dp // 2, 2, 2, n_seg // 2), EVERY)
    dp, seg = ("z", "y"), ("x", "c")
    return jax.shard_map(
        on_device,
        mesh=fine,
        in_specs=(
            P(EVERY, None, None, None),
            P(EVERY, None, None, None),
            P(EVERY),
            P(seg, dp, None),
            P(seg, dp, None),
            P(seg, dp),
            P(seg, dp),
            P(seg, dp),
            P(seg, dp),
        ),
        out_specs=(
            P(EVERY, None, None, None),
            P(EVERY, None, None, None),
            P(seg, dp, None),
            P(seg, dp, None),
            P(seg, dp),
            P(seg, dp),
            P(seg, dp),
            P(seg, dp),
        ),
        check_vma=False,
    )
```

```python
import functools

import jax
import jax.numpy as jnp
from jax import lax
from jax.experimental import pallas as pl
from jax.experimental.pallas import tpu as pltpu
from jax.sharding import Mesh, PartitionSpec as P

eps = 1e-05
PLANE = ("y", "x", "c")
EVERY = ("z", "y", "x", "c")
BF = jnp.bfloat16
F32 = jnp.float32


def nt(a, b):
    return lax.dot_general(a, b, (((1,), (1,)), ((), ())), preferred_element_type=F32)


def nn(a, b):
    return lax.dot_general(a, b, (((1,), (0,)), ((), ())), preferred_element_type=F32)


VMEM_CAP = 56 * 1024 * 1024
ANY = pl.BlockSpec(memory_space=pl.ANY)


def call(body, outs, scratch, flops, *args, deps=(), far=(), far_outs=()):
    moved = sum(a.size * a.dtype.itemsize for a in args) + sum(
        o.size * o.dtype.itemsize for o in outs
    )
    n = len(deps)

    def spec(a):
        return pl.BlockSpec(memory_space=pltpu.SMEM if a.dtype == jnp.int32 else pltpu.VMEM)

    return pl.pallas_call(
        lambda *refs: body(*refs[n:]),
        out_shape=outs,
        in_specs=[ANY] * n + [ANY if i in far else spec(a) for i, a in enumerate(args)],
        out_specs=[ANY if i in far_outs else spec(o) for i, o in enumerate(outs)],
        scratch_shapes=scratch,
        compiler_params=pltpu.CompilerParams(vmem_limit_bytes=VMEM_CAP),
        cost_estimate=pl.CostEstimate(flops=flops, bytes_accessed=moved, transcendentals=0),
    )(*deps, *args)


def chunk(i, size):
    return pl.ds(pl.multiple_of(i * size, 16), size)


def clear_borders(pad_ref, side, plane, nf):
    zrow = jnp.zeros(pad_ref.shape[1:], BF)
    pad_ref[0] = zrow
    pad_ref[side + 1] = zrow
    zcol = jnp.zeros((nf, pad_ref.shape[2]), BF)
    for i in range(side):
        pad_ref[i + 1, 0:nf] = zcol
        pad_ref[i + 1, nf + plane : 2 * nf + plane] = zcol


def by_rank(slices, rank):
    odd = lax.rem(rank, 2) == 1
    for p in range(len(slices) // 2):
        a, b = slices[2 * p], slices[2 * p + 1]
        yield lax.bitwise_xor(rank // 2, p), odd, a, b


def halves(odd, own, mate):
    low = lax.broadcasted_iota(jnp.int32, own.shape, 1) < 64
    own, mate = own.astype(F32), mate.astype(F32)
    a, b = jnp.where(odd, mate, own), jnp.where(odd, own, mate)
    top = jnp.where(low, a, pltpu.roll(b, 64, 1))
    bottom = jnp.where(low, pltpu.roll(a, 64, 1), b)
    return top, bottom


def store_packed(rank, mate_ref, keep_ref, part, k, step, low):
    rows_now = chunk(k, step)
    odd = lax.rem(rank, 2) == 1
    for q in range(keep_ref.shape[0]):
        x = part[:step, 128 * q : 128 * q + 128]
        y = part[step:, 128 * q : 128 * q + 128]
        even_slice = jnp.where(low, x, pltpu.roll(y, 64, 1))
        odd_slice = jnp.where(low, pltpu.roll(x, 64, 1), y)
        p = lax.bitwise_xor(rank // 2, q)
        keep_ref[p, rows_now, :] = jnp.where(odd, odd_slice, even_slice).astype(BF)
        mate_ref[p, rows_now, :] = jnp.where(odd, even_slice, odd_slice).astype(BF)


def fetch_kernels(kt_ref, lt_ref, ktm_ref, ltm_ref, sems):
    width = kt_ref.shape[2]
    copies = [
        pltpu.make_async_copy(kt_ref.at[z], ktm_ref.at[:, pl.ds(z * width, width)], sems.at[z])
        for z in range(kt_ref.shape[0])
    ]
    copies.append(pltpu.make_async_copy(lt_ref, ltm_ref, sems.at[kt_ref.shape[0]]))
    for copy in copies:
        copy.start()
    return copies


def conv_body(side, first, rank_ref, *refs):
    n = 1 if first else 8
    slices = refs[:n]
    (kt_ref, lt_ref, vec_ref, before_ref, after_ref,
     pad_out, hid_out, xhat_out, rs_ref, mate_ref, keep_ref,
     pad_ref, hid_ref, xhat_ref, sp_ref, ktm_ref, ltm_ref, kn_ref, sems) = refs[n:]
    rank = rank_ref[0]
    nz = kt_ref.shape[0]
    fetched = fetch_kernels(kt_ref, lt_ref, ktm_ref, ltm_ref, sems)
    ch, hc = pad_ref.shape[2], hid_ref.shape[1]
    rows = hid_ref.shape[0]
    plane = rows // side
    nf = plane // side
    step = plane // 2
    clear_borders(pad_ref, side, plane, nf)
    if first:
        for i in range(side):
            pad_ref[i + 1, nf : nf + plane] = slices[0][i * plane : (i + 1) * plane]
    else:
        def place(k, carry):
            for q, odd, a_ref, b_ref in by_rank(slices, rank):
                top, bottom = halves(odd, a_ref[chunk(k, step), :], b_ref[chunk(k, step), :])
                lanes = pl.ds(pl.multiple_of(128 * q, 128), 128)
                for piece, kk in ((top, k), (bottom, k + side)):
                    at = nf + lax.rem(kk, 2) * step
                    pad_ref[1 + kk // 2, pl.ds(pl.multiple_of(at, 16), step), lanes] = piece.astype(BF)
            return carry

        lax.fori_loop(0, side, place, 0)
    pad_copy = pltpu.make_async_copy(pad_ref, pad_out, sems.at[nz + 1])
    pad_copy.start()
    for copy in fetched:
        copy.wait()
    for t in range(9):
        kn_ref[t] = ktm_ref[:, t * ch : (t + 1) * ch].astype(F32).T.astype(BF)

    def conv(i, total):
        acc = jnp.zeros((plane, hc), F32)
        for t in range(9):
            r, c = t // 3, t % 3
            acc += nn(pad_ref[i + r, c * nf : c * nf + plane, :], kn_ref[t])
        sp_ref[i] = acc
        return total + jnp.sum(acc, axis=0, keepdims=True)

    mean = lax.fori_loop(0, side, conv, jnp.zeros((1, hc), F32)) / rows

    def square(i, total):
        cen = sp_ref[i] - mean
        return total + jnp.sum(cen * cen, axis=0, keepdims=True)

    var = lax.fori_loop(0, side, square, jnp.zeros((1, hc), F32)) / rows
    rs = lax.rsqrt(var + eps)
    rs_ref[...] = rs
    gain, bias = vec_ref[0:1, :], vec_ref[1:2, :]

    def act(i, carry):
        xhat = (sp_ref[i] - mean) * rs
        xhat_ref[i] = xhat
        v = xhat * gain + bias
        v = v * jax.nn.sigmoid(v)
        sp_ref[i] = v
        hid_ref[chunk(i, plane), :] = v.astype(BF)
        return carry

    lax.fori_loop(0, side, act, 0)
    late = [
        pltpu.make_async_copy(hid_ref, hid_out, sems.at[nz + 2]),
        pltpu.make_async_copy(xhat_ref, xhat_out, sems.at[nz + 3]),
    ]
    for copy in late:
        copy.start()
    low = lax.broadcasted_iota(jnp.int32, (step, 128), 1) < 64

    def temporal(k, carry):
        pieces = []
        for kk in (k, k + side):
            par = lax.rem(kk, 2)
            h = sp_ref[kk // 2, pl.ds(pl.multiple_of(par * step, 8), step), :]
            at = pl.multiple_of(par * (step % nf), 8)
            pieces.append((
                (pltpu.roll(h, 1, 0) * before_ref[pl.ds(at, step), :]).astype(BF),
                h.astype(BF),
                (pltpu.roll(h, step - 1, 0) * after_ref[pl.ds(at, step), :]).astype(BF),
            ))
        part = sum(
            nn(jnp.concatenate([x, y], axis=0), ltm_ref[t * hc : (t + 1) * hc])
            for t, (x, y) in enumerate(zip(*pieces))
        )
        store_packed(rank, mate_ref, keep_ref, part, k, step, low)
        return carry

    lax.fori_loop(0, side, temporal, 0)
    for copy in [pad_copy] + late:
        copy.wait()


def conv_forward(rank, g, kt, lt, vec, before, after, side, pixels, ch, deps=()):
    hc = lt.shape[0] // 3
    plane = pixels // side
    nf = plane // side
    n = len(g)
    shapes = [
        ((side + 2, plane + 2 * nf, ch), BF),
        ((pixels, hc), BF),
        ((side, plane, hc), F32),
    ]
    outs = [jax.ShapeDtypeStruct(*s) for s in shapes] + [
        jax.ShapeDtypeStruct((1, hc), F32),
        jax.ShapeDtypeStruct((4, pixels // 2, 128), BF),
        jax.ShapeDtypeStruct((4, pixels // 2, 128), BF),
    ]
    scratch = [pltpu.VMEM(*s) for s in shapes] + [
        pltpu.VMEM((side, plane, hc), F32),
        pltpu.VMEM((hc, 9 * ch), BF),
        pltpu.VMEM((3 * hc, ch), BF),
        pltpu.VMEM((9, ch, hc), BF),
        pltpu.SemaphoreType.DMA((kt.shape[0] + 4,)),
    ]
    flops = 2 * pixels * hc * 12 * ch
    return call(functools.partial(conv_body, side, n == 1), outs, scratch, flops,
                rank, *g, kt, lt, vec, before, after,
                deps=deps, far=(n + 1, n + 2), far_outs=(0, 1, 2))


def fold(v):
    return v + pltpu.roll(v, 64, 1)


def total_of(refs):
    t = refs[0][...].astype(F32)
    for ref in refs[1:]:
        t += ref[...].astype(F32)
    return t


def pair_sum_body(keep_ref, mate_ref, *out_refs):
    for p, ref in enumerate(out_refs):
        ref[...] = (keep_ref[p].astype(F32) + mate_ref[p].astype(F32)).astype(ref.dtype)


def pair_sum(keep, arrived):
    shape = keep.shape[1:]
    outs = [jax.ShapeDtypeStruct(shape, BF)] * keep.shape[0]
    return call(pair_sum_body, outs, [], keep.size, keep, arrived)


def out_norm_body(n, has_skip, *refs):
    parts, refs = refs[:n], refs[n:]
    if has_skip:
        vec_ref, skip_ref, xhat_ref, rs_ref, pre_ref, res_ref = refs
    else:
        vec_ref, xhat_ref, rs_ref, pre_ref, res_ref = refs
    t = total_of(parts)
    pixels = 2 * t.shape[0]
    mean = fold(jnp.sum(t, axis=0, keepdims=True)) / pixels
    cen = t - mean
    rs = lax.rsqrt(fold(jnp.sum(cen * cen, axis=0, keepdims=True)) / pixels + eps)
    xhat = cen * rs
    pre = xhat * vec_ref[0:1, :] + vec_ref[1:2, :]
    if has_skip:
        pre = pre + skip_ref[...].astype(F32)
    xhat_ref[...] = xhat
    rs_ref[...] = rs
    pre_ref[...] = pre
    res_ref[...] = (pre * jax.nn.sigmoid(pre)).astype(BF)


def out_norm(parts, vec, skip):
    half = parts[0].shape[0]
    outs = [
        jax.ShapeDtypeStruct((half, 128), F32),
        jax.ShapeDtypeStruct((1, 128), F32),
        jax.ShapeDtypeStruct((half, 128), F32),
        jax.ShapeDtypeStruct((half, 128), BF),
    ]
    args = (*parts, vec) + (() if skip is None else (skip,))
    body = functools.partial(out_norm_body, len(parts), skip is not None)
    return call(body, outs, [], half * 128 * 10, *args)


def out_back_body(n, *refs):
    parts, (pre_ref, xhat_ref, rs_ref, vec_ref, dpre_ref, dt_ref, sums_ref) = refs[:n], refs[n:]
    g = total_of(parts)
    pre, xhat = pre_ref[...], xhat_ref[...]
    sig = jax.nn.sigmoid(pre)
    dpre = g * (sig * (1.0 + pre * (1.0 - sig)))
    pixels = 2 * pre.shape[0]
    sb = fold(jnp.sum(dpre, axis=0, keepdims=True))
    sg = fold(jnp.sum(dpre * xhat, axis=0, keepdims=True))
    dpre_ref[...] = dpre.astype(BF)
    scale = vec_ref[0:1, :] * rs_ref[...]
    dt_ref[...] = (scale * (dpre - sb / pixels - xhat * (sg / pixels))).astype(BF)
    sums_ref[0:1, :] = sg
    sums_ref[1:2, :] = sb


def out_back(parts, pre, xhat, rs, vec, deps=()):
    half = pre.shape[0]
    outs = [
        jax.ShapeDtypeStruct((half, 128), BF),
        jax.ShapeDtypeStruct((half, 128), BF),
        jax.ShapeDtypeStruct((2, 128), F32),
    ]
    args = (*parts, pre, xhat, rs, vec)
    return call(functools.partial(out_back_body, len(parts)), outs, [], half * 1280, *args, deps=deps)


def conv_back_body(side, rank_ref, *refs):
    slices, (xhat_in, rs_ref, kt_ref, lt_ref, vec_ref, before_ref, after_ref,
             dt_out, ds_out, sums_ref, mate_ref, keep_ref,
             dt_ref, ds_ref, xhat_ref, dy_ref, pad_ref, ktm_ref, ltm_ref, lnt_ref, sems) = (
        refs[:8], refs[8:])
    half = slices[0].shape[0]
    rank = rank_ref[0]
    nz = kt_ref.shape[0]
    rows = 2 * half
    plane = rows // side
    nf = plane // side
    step = plane // 2
    hc = ds_ref.shape[1]
    ch = dt_ref.shape[1]
    fetched = fetch_kernels(kt_ref, lt_ref, ktm_ref, ltm_ref, sems)
    xhat_copy = pltpu.make_async_copy(xhat_in, xhat_ref, sems.at[nz + 1])
    xhat_copy.start()
    clear_borders(pad_ref, side, plane, nf)

    def place(k, carry):
        for q, odd, a_ref, b_ref in by_rank(slices, rank):
            top, bottom = halves(odd, a_ref[chunk(k, step), :], b_ref[chunk(k, step), :])
            lanes = pl.ds(pl.multiple_of(128 * q, 128), 128)
            dt_ref[chunk(k, step), lanes] = top.astype(BF)
            dt_ref[pl.ds(pl.multiple_of(half + k * step, 16), step), lanes] = bottom.astype(BF)
        return carry

    lax.fori_loop(0, side, place, 0)
    dt_copy = pltpu.make_async_copy(dt_ref, dt_out, sems.at[nz + 2])
    dt_copy.start()
    for copy in fetched + [xhat_copy]:
        copy.wait()
    for t in range(3):
        lnt_ref[t] = ltm_ref[t * hc : (t + 1) * hc].astype(F32).T.astype(BF)
    gain, bias = vec_ref[0:1, :], vec_ref[1:2, :]

    def hidden_grad(i, sums):
        dt = dt_ref[chunk(i, plane), :]
        early = nn(dt, lnt_ref[0]) * before_ref[0:plane, :]
        late = nn(dt, lnt_ref[2]) * after_ref[0:plane, :]
        dh = nn(dt, lnt_ref[1]) + pltpu.roll(early, plane - 1, 0) + pltpu.roll(late, 1, 0)
        xhat = xhat_ref[i]
        v = xhat * gain + bias
        sig = jax.nn.sigmoid(v)
        dy = dh * (sig * (1.0 + v * (1.0 - sig)))
        dy_ref[i] = dy
        return (
            sums[0] + jnp.sum(dy * xhat, axis=0, keepdims=True),
            sums[1] + jnp.sum(dy, axis=0, keepdims=True),
        )

    zero = jnp.zeros((1, hc), F32)
    sg, sb = lax.fori_loop(0, side, hidden_grad, (zero, zero))
    sums_ref[0:1, :] = sg
    sums_ref[1:2, :] = sb
    scale = gain * rs_ref[...]

    def spatial_grad(i, carry):
        ds = (scale * (dy_ref[i] - sb / rows - xhat_ref[i] * (sg / rows))).astype(BF)
        pad_ref[i + 1, nf : nf + plane] = ds
        ds_ref[chunk(i, plane), :] = ds
        return carry

    lax.fori_loop(0, side, spatial_grad, 0)
    ds_copy = pltpu.make_async_copy(ds_ref, ds_out, sems.at[nz + 3])
    ds_copy.start()
    low = lax.broadcasted_iota(jnp.int32, (step, 128), 1) < 64

    def back(k, carry):
        acc = jnp.zeros((2 * step, ch), F32)
        for t in range(9):
            r, c = 2 - t // 3, 2 - t % 3
            pieces = []
            for kk in (k, k + side):
                at = c * nf + lax.rem(kk, 2) * step
                pieces.append(pad_ref[kk // 2 + r, pl.ds(pl.multiple_of(at, 16), step), :])
            acc += nn(jnp.concatenate(pieces, axis=0), ktm_ref[:, t * ch : (t + 1) * ch])
        store_packed(rank, mate_ref, keep_ref, acc, k, step, low)
        return carry

    lax.fori_loop(0, side, back, 0)
    dt_copy.wait()
    ds_copy.wait()


def conv_back(rank, g, xhat, rs, kt, lt, vec, before, after, side, deps=()):
    half = g[0].shape[0]
    hc = lt.shape[0] // 3
    ch = lt.shape[1]
    pixels = 2 * half
    plane = pixels // side
    nf = plane // side
    outs = [
        jax.ShapeDtypeStruct((pixels, ch), BF),
        jax.ShapeDtypeStruct((pixels, hc), BF),
        jax.ShapeDtypeStruct((2, hc), F32),
        jax.ShapeDtypeStruct((4, half, 128), BF),
        jax.ShapeDtypeStruct((4, half, 128), BF),
    ]
    scratch = [
        pltpu.VMEM((pixels, ch), BF),
        pltpu.VMEM((pixels, hc), BF),
        pltpu.VMEM((side, plane, hc), F32),
        pltpu.VMEM((side, plane, hc), F32),
        pltpu.VMEM((side + 2, plane + 2 * nf, hc), BF),
        pltpu.VMEM((hc, 9 * ch), BF),
        pltpu.VMEM((3 * hc, ch), BF),
        pltpu.VMEM((3, ch, hc), BF),
        pltpu.SemaphoreType.DMA((kt.shape[0] + 4,)),
    ]
    flops = 2 * pixels * hc * 12 * ch
    return call(functools.partial(conv_back_body, side), outs, scratch, flops,
                rank, *g, xhat, rs, kt, lt, vec, before, after,
                deps=deps, far=(9, 11, 12), far_outs=(0, 1))


def grads_body(side, pad_in, hid_ref, ds_ref, dt_in, before_ref, after_ref, sg_ref, tg_ref,
               dst_ref, taps_ref, acc_ref, pad_ref, dt_ref, sems):
    ch = pad_ref.shape[2]
    hc = hid_ref.shape[1]
    plane = hid_ref.shape[0] // side
    nf = plane // side
    copies = [
        pltpu.make_async_copy(dt_in, dt_ref, sems.at[0]),
        pltpu.make_async_copy(pad_in, pad_ref, sems.at[1]),
    ]
    for copy in copies:
        copy.start()
    for i in (0, 1, side + 2, side + 3):
        dst_ref[i] = jnp.zeros(dst_ref.shape[1:], BF)

    def flip(i, carry):
        h = hid_ref[chunk(i, plane), :].astype(F32)
        taps_ref[i, 0:hc] = (pltpu.roll(h, 1, 0) * before_ref[0:plane, :]).T.astype(BF)
        taps_ref[i, hc : 2 * hc] = h.T.astype(BF)
        taps_ref[i, 2 * hc : 3 * hc] = (pltpu.roll(h, plane - 1, 0) * after_ref[0:plane, :]).T.astype(BF)
        dst_ref[i + 2] = ds_ref[chunk(i, plane), :].astype(F32).T.astype(BF)
        return carry

    lax.fori_loop(0, side, flip, 0)
    copies[0].wait()
    acc_ref[...] = jnp.zeros(acc_ref.shape, F32)

    def time_tap(i, carry):
        acc_ref[...] += nn(taps_ref[i], dt_ref[chunk(i, plane), :])
        return carry

    lax.fori_loop(0, side, time_tap, 0)
    tg_ref[...] = acc_ref[...].astype(BF)
    copies[1].wait()
    width = sg_ref.shape[2]
    for c in range(3):
        acc_ref[...] = jnp.zeros(acc_ref.shape, F32)

        def space_tap(i, carry):
            lhs = dst_ref[pl.ds(i, 3)].reshape(3 * hc, plane)
            acc_ref[...] += nn(lhs, pad_ref[i, c * nf : c * nf + plane, :])
            return carry

        lax.fori_loop(1, side + 1, space_tap, 0)
        for r in range(3):
            first = (3 * r + c) * ch
            end = first + ch
            at = (2 - r) * hc
            done = 0
            while first < end:
                z = first // width
                last = min(end, (z + 1) * width)
                sg_ref[z, :, first - z * width : last - z * width] = (
                    acc_ref[at : at + hc, done : done + last - first].astype(BF)
                )
                done += last - first
                first = last


def kernel_grads(pad, hidden, ds, dt, before, after, side, nz):
    pixels, hc = hidden.shape
    ch = dt.shape[1]
    plane = pixels // side
    outs = [
        jax.ShapeDtypeStruct((nz, hc, 9 * ch // nz), BF),
        jax.ShapeDtypeStruct((3 * hc, ch), BF),
    ]
    scratch = [
        pltpu.VMEM((side + 4, hc, plane), BF),
        pltpu.VMEM((side, 3 * hc, plane), BF),
        pltpu.VMEM((3 * hc, ch), F32),
        pltpu.VMEM(pad.shape, BF),
        pltpu.VMEM((pixels, ch), BF),
        pltpu.SemaphoreType.DMA((2,)),
    ]
    flops = 2 * pixels * hc * 12 * ch
    return call(functools.partial(grads_body, side), outs, scratch, flops,
                pad, hidden, ds, dt, before, after, far=(0, 3))


def copy_after_body(v_ref, out_ref):
    out_ref[...] = v_ref[...]


def after_all(v, *deps):
    return call(copy_after_body, [jax.ShapeDtypeStruct(v.shape, v.dtype)], [], v.size, v, deps=deps)[0]


def call(body, outs, scratch, flops, *args, deps=(), far=(), far_outs=()):
    moved = sum(a.size * a.dtype.itemsize for a in args) + sum(
        o.size * o.dtype.itemsize for o in outs
    )
    n = len(deps)

    def spec(a):
        return pl.BlockSpec(memory_space=pltpu.SMEM if a.dtype == jnp.int32 else pltpu.VMEM)

    return pl.pallas_call(
        lambda *refs: body(*refs[n:]),
        out_shape=outs,
        in_specs=[ANY] * n + [ANY if i in far else spec(a) for i, a in enumerate(args)],
        out_specs=[ANY if i in far_outs else spec(o) for i, o in enumerate(outs)],
        scratch_shapes=scratch,
        compiler_params=pltpu.CompilerParams(vmem_limit_bytes=VMEM_CAP),
        cost_estimate=pl.CostEstimate(flops=flops, bytes_accessed=moved, transcendentals=0),
    )(*deps, *args)


def chunk(i, size):
    return pl.ds(pl.multiple_of(i * size, 16), size)


def clear_borders(pad_ref, side, plane, nf):
    zrow = jnp.zeros(pad_ref.shape[1:], BF)
    pad_ref[0] = zrow
    pad_ref[side + 1] = zrow
    zcol = jnp.zeros((nf, pad_ref.shape[2]), BF)
    for i in range(side):
        pad_ref[i + 1, 0:nf] = zcol
        pad_ref[i + 1, nf + plane : 2 * nf + plane] = zcol


def by_rank(slices, rank):
    odd = lax.rem(rank, 2) == 1
    for p in range(len(slices) // 2):
        a, b = slices[2 * p], slices[2 * p + 1]
        yield lax.bitwise_xor(rank // 2, p), odd, a, b


def halves(odd, own, mate):
    low = lax.broadcasted_iota(jnp.int32, own.shape, 1) < 64
    own, mate = own.astype(F32), mate.astype(F32)
    a, b = jnp.where(odd, mate, own), jnp.where(odd, own, mate)
    top = jnp.where(low, a, pltpu.roll(b, 64, 1))
    bottom = jnp.where(low, pltpu.roll(a, 64, 1), b)
    return top, bottom


def store_packed(rank, mate_ref, keep_ref, part, k, step, low):
    rows_now = chunk(k, step)
    odd = lax.rem(rank, 2) == 1
    for q in range(keep_ref.shape[0]):
        x = part[:step, 128 * q : 128 * q + 128]
        y = part[step:, 128 * q : 128 * q + 128]
        even_slice = jnp.where(low, x, pltpu.roll(y, 64, 1))
        odd_slice = jnp.where(low, pltpu.roll(x, 64, 1), y)
        p = lax.bitwise_xor(rank // 2, q)
        keep_ref[p, rows_now, :] = jnp.where(odd, odd_slice, even_slice).astype(BF)
        mate_ref[p, rows_now, :] = jnp.where(odd, even_slice, odd_slice).astype(BF)


def fetch_kernels(kt_ref, lt_ref, ktm_ref, ltm_ref, sems):
    width = kt_ref.shape[2]
    copies = [
        pltpu.make_async_copy(kt_ref.at[z], ktm_ref.at[:, pl.ds(z * width, width)], sems.at[z])
        for z in range(kt_ref.shape[0])
    ]
    copies.append(pltpu.make_async_copy(lt_ref, ltm_ref, sems.at[kt_ref.shape[0]]))
    for copy in copies:
        copy.start()
    return copies


def conv_body(side, first, rank_ref, *refs):
    n = 1 if first else 8
    slices = refs[:n]
    (kt_ref, lt_ref, vec_ref, before_ref, after_ref,
     pad_out, hid_out, xhat_out, rs_ref, mate_ref, keep_ref,
     pad_ref, hid_ref, xhat_ref, sp_ref, ktm_ref, ltm_ref, kn_ref, sems) = refs[n:]
    rank = rank_ref[0]
    nz = kt_ref.shape[0]
    fetched = fetch_kernels(kt_ref, lt_ref, ktm_ref, ltm_ref, sems)
    ch, hc = pad_ref.shape[2], hid_ref.shape[1]
    rows = hid_ref.shape[0]
    plane = rows // side
    nf = plane // side
    step = plane // 2
    clear_borders(pad_ref, side, plane, nf)
    if first:
        for i in range(side):
            pad_ref[i + 1, nf : nf + plane] = slices[0][i * plane : (i + 1) * plane]
    else:
        def place(k, carry):
            for q, odd, a_ref, b_ref in by_rank(slices, rank):
                top, bottom = halves(odd, a_ref[chunk(k, step), :], b_ref[chunk(k, step), :])
                lanes = pl.ds(pl.multiple_of(128 * q, 128), 128)
                for piece, kk in ((top, k), (bottom, k + side)):
                    at = nf + lax.rem(kk, 2) * step
                    pad_ref[1 + kk // 2, pl.ds(pl.multiple_of(at, 16), step), lanes] = piece.astype(BF)
            return carry

        lax.fori_loop(0, side, place, 0)
    pad_copy = pltpu.make_async_copy(pad_ref, pad_out, sems.at[nz + 1])
    pad_copy.start()
    for copy in fetched:
        copy.wait()
    for t in range(9):
        kn_ref[t] = ktm_ref[:, t * ch : (t + 1) * ch].astype(F32).T.astype(BF)

    def conv(i, total):
        acc = jnp.zeros((plane, hc), F32)
        for t in range(9):
            r, c = t // 3, t % 3
            acc += nn(pad_ref[i + r, c * nf : c * nf + plane, :], kn_ref[t])
        sp_ref[i] = acc
        return total + jnp.sum(acc, axis=0, keepdims=True)

    mean = lax.fori_loop(0, side, conv, jnp.zeros((1, hc), F32)) / rows

    def square(i, total):
        cen = sp_ref[i] - mean
        return total + jnp.sum(cen * cen, axis=0, keepdims=True)

    var = lax.fori_loop(0, side, square, jnp.zeros((1, hc), F32)) / rows
    rs = lax.rsqrt(var + eps)
    rs_ref[...] = rs
    gain, bias = vec_ref[0:1, :], vec_ref[1:2, :]

    def act(i, carry):
        xhat = (sp_ref[i] - mean) * rs
        xhat_ref[i] = xhat
        v = xhat * gain + bias
        v = v * jax.nn.sigmoid(v)
        sp_ref[i] = v
        hid_ref[chunk(i, plane), :] = v.astype(BF)
        return carry

    lax.fori_loop(0, side, act, 0)
    late = [
        pltpu.make_async_copy(hid_ref, hid_out, sems.at[nz + 2]),
        pltpu.make_async_copy(xhat_ref, xhat_out, sems.at[nz + 3]),
    ]
    for copy in late:
        copy.start()
    low = lax.broadcasted_iota(jnp.int32, (step, 128), 1) < 64

    def temporal(k, carry):
        pieces = []
        for kk in (k, k + side):
            par = lax.rem(kk, 2)
            h = sp_ref[kk // 2, pl.ds(pl.multiple_of(par * step, 8), step), :]
            at = pl.multiple_of(par * (step % nf), 8)
            pieces.append((
                (pltpu.roll(h, 1, 0) * before_ref[pl.ds(at, step), :]).astype(BF),
                h.astype(BF),
                (pltpu.roll(h, step - 1, 0) * after_ref[pl.ds(at, step), :]).astype(BF),
            ))
        part = sum(
            nn(jnp.concatenate([x, y], axis=0), ltm_ref[t * hc : (t + 1) * hc])
            for t, (x, y) in enumerate(zip(*pieces))
        )
        store_packed(rank, mate_ref, keep_ref, part, k, step, low)
        return carry

    lax.fori_loop(0, side, temporal, 0)
    for copy in [pad_copy] + late:
        copy.wait()


def conv_forward(rank, g, kt, lt, vec, before, after, side, pixels, ch, deps=()):
    hc = lt.shape[0] // 3
    plane = pixels // side
    nf = plane // side
    n = len(g)
    shapes = [
        ((side + 2, plane + 2 * nf, ch), BF),
        ((pixels, hc), BF),
        ((side, plane, hc), F32),
    ]
    outs = [jax.ShapeDtypeStruct(*s) for s in shapes] + [
        jax.ShapeDtypeStruct((1, hc), F32),
        jax.ShapeDtypeStruct((4, pixels // 2, 128), BF),
        jax.ShapeDtypeStruct((4, pixels // 2, 128), BF),
    ]
    scratch = [pltpu.VMEM(*s) for s in shapes] + [
        pltpu.VMEM((side, plane, hc), F32),
        pltpu.VMEM((hc, 9 * ch), BF),
        pltpu.VMEM((3 * hc, ch), BF),
        pltpu.VMEM((9, ch, hc), BF),
        pltpu.SemaphoreType.DMA((kt.shape[0] + 4,)),
    ]
    flops = 2 * pixels * hc * 12 * ch
    return call(functools.partial(conv_body, side, n == 1), outs, scratch, flops,
                rank, *g, kt, lt, vec, before, after,
                deps=deps, far=(n + 1, n + 2), far_outs=(0, 1, 2))


def fold(v):
    return v + pltpu.roll(v, 64, 1)


def total_of(refs):
    t = refs[0][...].astype(F32)
    for ref in refs[1:]:
        t += ref[...].astype(F32)
    return t


def pair_sum_body(keep_ref, mate_ref, *out_refs):
    for p, ref in enumerate(out_refs):
        ref[...] = (keep_ref[p].astype(F32) + mate_ref[p].astype(F32)).astype(ref.dtype)


def pair_sum(keep, arrived):
    shape = keep.shape[1:]
    outs = [jax.ShapeDtypeStruct(shape, BF)] * keep.shape[0]
    return call(pair_sum_body, outs, [], keep.size, keep, arrived)


def out_norm_body(n, has_skip, *refs):
    parts, refs = refs[:n], refs[n:]
    if has_skip:
        vec_ref, skip_ref, xhat_ref, rs_ref, pre_ref, res_ref = refs
    else:
        vec_ref, xhat_ref, rs_ref, pre_ref, res_ref = refs
    t = total_of(parts)
    pixels = 2 * t.shape[0]
    mean = fold(jnp.sum(t, axis=0, keepdims=True)) / pixels
    cen = t - mean
    rs = lax.rsqrt(fold(jnp.sum(cen * cen, axis=0, keepdims=True)) / pixels + eps)
    xhat = cen * rs
    pre = xhat * vec_ref[0:1, :] + vec_ref[1:2, :]
    if has_skip:
        pre = pre + skip_ref[...].astype(F32)
    xhat_ref[...] = xhat
    rs_ref[...] = rs
    pre_ref[...] = pre
    res_ref[...] = (pre * jax.nn.sigmoid(pre)).astype(BF)


def out_norm(parts, vec, skip):
    half = parts[0].shape[0]
    outs = [
        jax.ShapeDtypeStruct((half, 128), F32),
        jax.ShapeDtypeStruct((1, 128), F32),
        jax.ShapeDtypeStruct((half, 128), F32),
        jax.ShapeDtypeStruct((half, 128), BF),
    ]
    args = (*parts, vec) + (() if skip is None else (skip,))
    body = functools.partial(out_norm_body, len(parts), skip is not None)
    return call(body, outs, [], half * 128 * 10, *args)


def out_back_body(n, *refs):
    parts, (pre_ref, xhat_ref, rs_ref, vec_ref, dpre_ref, dt_ref, sums_ref) = refs[:n], refs[n:]
    g = total_of(parts)
    pre, xhat = pre_ref[...], xhat_ref[...]
    sig = jax.nn.sigmoid(pre)
    dpre = g * (sig * (1.0 + pre * (1.0 - sig)))
    pixels = 2 * pre.shape[0]
    sb = fold(jnp.sum(dpre, axis=0, keepdims=True))
    sg = fold(jnp.sum(dpre * xhat, axis=0, keepdims=True))
    dpre_ref[...] = dpre.astype(BF)
    scale = vec_ref[0:1, :] * rs_ref[...]
    dt_ref[...] = (scale * (dpre - sb / pixels - xhat * (sg / pixels))).astype(BF)
    sums_ref[0:1, :] = sg
    sums_ref[1:2, :] = sb


def out_back(parts, pre, xhat, rs, vec, deps=()):
    half = pre.shape[0]
    outs = [
        jax.ShapeDtypeStruct((half, 128), BF),
        jax.ShapeDtypeStruct((half, 128), BF),
        jax.ShapeDtypeStruct((2, 128), F32),
    ]
    args = (*parts, pre, xhat, rs, vec)
    return call(functools.partial(out_back_body, len(parts)), outs, [], half * 1280, *args, deps=deps)


def conv_back_body(side, rank_ref, *refs):
    slices, (xhat_in, rs_ref, kt_ref, lt_ref, vec_ref, before_ref, after_ref,
             dt_out, ds_out, sums_ref, mate_ref, keep_ref,
             dt_ref, ds_ref, xhat_ref, dy_ref, pad_ref, ktm_ref, ltm_ref, lnt_ref, sems) = (
        refs[:8], refs[8:])
    half = slices[0].shape[0]
    rank = rank_ref[0]
    nz = kt_ref.shape[0]
    rows = 2 * half
    plane = rows // side
    nf = plane // side
    step = plane // 2
    hc = ds_ref.shape[1]
    ch = dt_ref.shape[1]
    fetched = fetch_kernels(kt_ref, lt_ref, ktm_ref, ltm_ref, sems)
    xhat_copy = pltpu.make_async_copy(xhat_in, xhat_ref, sems.at[nz + 1])
    xhat_copy.start()
    clear_borders(pad_ref, side, plane, nf)

    def place(k, carry):
        for q, odd, a_ref, b_ref in by_rank(slices, rank):
            top, bottom = halves(odd, a_ref[chunk(k, step), :], b_ref[chunk(k, step), :])
            lanes = pl.ds(pl.multiple_of(128 * q, 128), 128)
            dt_ref[chunk(k, step), lanes] = top.astype(BF)
            dt_ref[pl.ds(pl.multiple_of(half + k * step, 16), step), lanes] = bottom.astype(BF)
        return carry

    lax.fori_loop(0, side, place, 0)
    dt_copy = pltpu.make_async_copy(dt_ref, dt_out, sems.at[nz + 2])
    dt_copy.start()
    for copy in fetched + [xhat_copy]:
        copy.wait()
    for t in range(3):
        lnt_ref[t] = ltm_ref[t * hc : (t + 1) * hc].astype(F32).T.astype(BF)
    gain, bias = vec_ref[0:1, :], vec_ref[1:2, :]

    def hidden_grad(i, sums):
        dt = dt_ref[chunk(i, plane), :]
        early = nn(dt, lnt_ref[0]) * before_ref[0:plane, :]
        late = nn(dt, lnt_ref[2]) * after_ref[0:plane, :]
        dh = nn(dt, lnt_ref[1]) + pltpu.roll(early, plane - 1, 0) + pltpu.roll(late, 1, 0)
        xhat = xhat_ref[i]
        v = xhat * gain + bias
        sig = jax.nn.sigmoid(v)
        dy = dh * (sig * (1.0 + v * (1.0 - sig)))
        dy_ref[i] = dy
        return (
            sums[0] + jnp.sum(dy * xhat, axis=0, keepdims=True),
            sums[1] + jnp.sum(dy, axis=0, keepdims=True),
        )

    zero = jnp.zeros((1, hc), F32)
    sg, sb = lax.fori_loop(0, side, hidden_grad, (zero, zero))
    sums_ref[0:1, :] = sg
    sums_ref[1:2, :] = sb
    scale = gain * rs_ref[...]

    def spatial_grad(i, carry):
        ds = (scale * (dy_ref[i] - sb / rows - xhat_ref[i] * (sg / rows))).astype(BF)
        pad_ref[i + 1, nf : nf + plane] = ds
        ds_ref[chunk(i, plane), :] = ds
        return carry

    lax.fori_loop(0, side, spatial_grad, 0)
    ds_copy = pltpu.make_async_copy(ds_ref, ds_out, sems.at[nz + 3])
    ds_copy.start()
    low = lax.broadcasted_iota(jnp.int32, (step, 128), 1) < 64

    def back(k, carry):
        acc = jnp.zeros((2 * step, ch), F32)
        for t in range(9):
            r, c = 2 - t // 3, 2 - t % 3
            pieces = []
            for kk in (k, k + side):
                at = c * nf + lax.rem(kk, 2) * step
                pieces.append(pad_ref[kk // 2 + r, pl.ds(pl.multiple_of(at, 16), step), :])
            acc += nn(jnp.concatenate(pieces, axis=0), ktm_ref[:, t * ch : (t + 1) * ch])
        store_packed(rank, mate_ref, keep_ref, acc, k, step, low)
        return carry

    lax.fori_loop(0, side, back, 0)
    dt_copy.wait()
    ds_copy.wait()


def conv_back(rank, g, xhat, rs, kt, lt, vec, before, after, side, deps=()):
    half = g[0].shape[0]
    hc = lt.shape[0] // 3
    ch = lt.shape[1]
    pixels = 2 * half
    plane = pixels // side
    nf = plane // side
    outs = [
        jax.ShapeDtypeStruct((pixels, ch), BF),
        jax.ShapeDtypeStruct((pixels, hc), BF),
        jax.ShapeDtypeStruct((2, hc), F32),
        jax.ShapeDtypeStruct((4, half, 128), BF),
        jax.ShapeDtypeStruct((4, half, 128), BF),
    ]
    scratch = [
        pltpu.VMEM((pixels, ch), BF),
        pltpu.VMEM((pixels, hc), BF),
        pltpu.VMEM((side, plane, hc), F32),
        pltpu.VMEM((side, plane, hc), F32),
        pltpu.VMEM((side + 2, plane + 2 * nf, hc), BF),
        pltpu.VMEM((hc, 9 * ch), BF),
        pltpu.VMEM((3 * hc, ch), BF),
        pltpu.VMEM((3, ch, hc), BF),
        pltpu.SemaphoreType.DMA((kt.shape[0] + 4,)),
    ]
    flops = 2 * pixels * hc * 12 * ch
    return call(functools.partial(conv_back_body, side), outs, scratch, flops,
                rank, *g, xhat, rs, kt, lt, vec, before, after,
                deps=deps, far=(9, 11, 12), far_outs=(0, 1))


def grads_body(side, pad_in, hid_ref, ds_ref, dt_in, before_ref, after_ref, sg_ref, tg_ref,
               dst_ref, taps_ref, acc_ref, pad_ref, dt_ref, sems):
    ch = pad_ref.shape[2]
    hc = hid_ref.shape[1]
    plane = hid_ref.shape[0] // side
    nf = plane // side
    copies = [
        pltpu.make_async_copy(dt_in, dt_ref, sems.at[0]),
        pltpu.make_async_copy(pad_in, pad_ref, sems.at[1]),
    ]
    for copy in copies:
        copy.start()
    for i in (0, 1, side + 2, side + 3):
        dst_ref[i] = jnp.zeros(dst_ref.shape[1:], BF)

    def flip(i, carry):
        h = hid_ref[chunk(i, plane), :].astype(F32)
        taps_ref[i, 0:hc] = (pltpu.roll(h, 1, 0) * before_ref[0:plane, :]).T.astype(BF)
        taps_ref[i, hc : 2 * hc] = h.T.astype(BF)
        taps_ref[i, 2 * hc : 3 * hc] = (pltpu.roll(h, plane - 1, 0) * after_ref[0:plane, :]).T.astype(BF)
        dst_ref[i + 2] = ds_ref[chunk(i, plane), :].astype(F32).T.astype(BF)
        return carry

    lax.fori_loop(0, side, flip, 0)
    copies[0].wait()
    acc_ref[...] = jnp.zeros(acc_ref.shape, F32)

    def time_tap(i, carry):
        acc_ref[...] += nn(taps_ref[i], dt_ref[chunk(i, plane), :])
        return carry

    lax.fori_loop(0, side, time_tap, 0)
    tg_ref[...] = acc_ref[...].astype(BF)
    copies[1].wait()
    width = sg_ref.shape[2]
    for c in range(3):
        acc_ref[...] = jnp.zeros(acc_ref.shape, F32)

        def space_tap(i, carry):
            lhs = dst_ref[pl.ds(i, 3)].reshape(3 * hc, plane)
            acc_ref[...] += nn(lhs, pad_ref[i, c * nf : c * nf + plane, :])
            return carry

        lax.fori_loop(1, side + 1, space_tap, 0)
        for r in range(3):
            first = (3 * r + c) * ch
            end = first + ch
            at = (2 - r) * hc
            done = 0
            while first < end:
                z = first // width
                last = min(end, (z + 1) * width)
                sg_ref[z, :, first - z * width : last - z * width] = (
                    acc_ref[at : at + hc, done : done + last - first].astype(BF)
                )
                done += last - first
                first = last


def kernel_grads(pad, hidden, ds, dt, before, after, side, nz):
    pixels, hc = hidden.shape
    ch = dt.shape[1]
    plane = pixels // side
    outs = [
        jax.ShapeDtypeStruct((nz, hc, 9 * ch // nz), BF),
        jax.ShapeDtypeStruct((3 * hc, ch), BF),
    ]
    scratch = [
        pltpu.VMEM((side + 4, hc, plane), BF),
        pltpu.VMEM((side, 3 * hc, plane), BF),
        pltpu.VMEM((3 * hc, ch), F32),
        pltpu.VMEM(pad.shape, BF),
        pltpu.VMEM((pixels, ch), BF),
        pltpu.SemaphoreType.DMA((2,)),
    ]
    flops = 2 * pixels * hc * 12 * ch
    return call(functools.partial(grads_body, side), outs, scratch, flops,
                pad, hidden, ds, dt, before, after, far=(0, 3))


def copy_after_body(v_ref, out_ref):
    out_ref[...] = v_ref[...]


def after_all(v, *deps):
    return call(copy_after_body, [jax.ShapeDtypeStruct(v.shape, v.dtype)], [], v.size, v, deps=deps)[0]


def hop(v, k):
    n = 1
    for name in EVERY:
        n *= lax.axis_size(name)
    return lax.ppermute(v, EVERY, [(i, i ^ k) for i in range(n)])


def plane_gather(v):
    got = {0: v}
    for k in (6, 2, 4, 1):
        got[k] = hop(v, k)
    for k in (2, 4, 6):
        got[k ^ 1] = hop(got[k], 1)
    return [got[k] for k in range(8)]


def in_order(pieces, first):
    whole = jnp.zeros((len(pieces), *pieces[0].shape), pieces[0].dtype)
    for k, piece in enumerate(pieces):
        whole = lax.dynamic_update_index_in_dim(whole, piece, lax.bitwise_xor(first, k), 0)
    return whole


def z_gather(v, n_rank, nz):
    return in_order([v] + [hop(v, n_rank * k) for k in range(1, nz)], lax.axis_index("z"))


def z_reduce(v, n_rank, nz):
    z = lax.axis_index("z")
    total = lax.dynamic_index_in_dim(v, z, 0, keepdims=False).astype(F32)
    for k in range(1, nz):
        piece = lax.dynamic_index_in_dim(v, lax.bitwise_xor(z, k), 0, keepdims=False)
        total = total + hop(piece, n_rank * k).astype(F32)
    return total.astype(v.dtype)


def plane_reduce(mate, keep):
    sums = pair_sum(keep, hop(mate, 1))
    arrived = {k: hop(sums[k // 2], k) for k in (6, 2, 4)}
    return [sums[0], arrived[2], arrived[4], arrived[6]]


def on_device(frames, cot, starts, ks, ktm, mg, mb, og, ob):
    nz, n_rank, n_seg = lax.axis_size("z"), 8, 4
    n_dp = nz * 2
    fr, side, ch = frames.shape[0], frames.shape[1], frames.shape[3]
    area = side * side
    hid = ks.shape[2]
    hc, cc = hid // n_rank, ch // n_rank
    q = hc // n_rank
    rank = lax.axis_index(PLANE)
    rank_now = rank.astype(jnp.int32).reshape(1)
    d_index = lax.axis_index(("z", "y"))
    nf = n_dp * fr
    pixels = area * nf
    half = pixels // 2

    to_plane = [(d * n_seg + s, s * n_rank + d) for d in range(n_dp) for s in range(n_seg)]
    from_plane = [(b, a) for a, b in to_plane]
    rows = fr * area
    flag_row = jnp.pad(starts.astype(BF)[None], ((0, 11), (0, ch - fr)))
    moving = jnp.concatenate([frames.reshape(rows, ch), flag_row], axis=0)
    moving = lax.ppermute(moving, EVERY, to_plane)

    perm = (jnp.arange(hid).reshape(n_rank, n_rank, q).transpose(1, 0, 2).reshape(hid)[:, None]
            == jnp.arange(hid)[None, :]).astype(BF)
    kt = lax.dot_general(perm, ks[0].astype(BF), (((1,), (1,)), ((), ())),
                         preferred_element_type=F32).astype(BF)
    kt = kt.reshape(n_rank, hc, ks.shape[1])
    kt = lax.all_to_all(kt, PLANE, 0, 0)
    kt_here = kt
    kt = kt.reshape(2, n_seg, hc, ks.shape[1]).transpose(1, 2, 0, 3).reshape(n_seg, hc, -1)
    lrows = ktm.shape[1] // n_rank
    lt = ktm[0].astype(BF).reshape(-1, n_rank, q, ch).transpose(1, 0, 2, 3).reshape(n_rank, lrows, ch)
    extra = jnp.concatenate([v.astype(BF) for v in (mg, mb, og, ob)], axis=1)
    extra = jnp.pad(extra, ((0, 1), (0, ch - extra.shape[1])))
    lt = jnp.concatenate([lt, jnp.broadcast_to(extra, (n_rank, 2, ch))], axis=1)
    lt = lax.all_to_all(after_all(lt, kt_here), PLANE, 0, 0)
    gathered = in_order(plane_gather(after_all(moving, kt_here)), rank)
    lt = lt.reshape(2, n_seg, lrows + 2, ch).transpose(1, 0, 2, 3).reshape(n_seg, 2 * (lrows + 2), ch)
    kts = [lax.all_gather(kt[s], "z", axis=0) for s in range(n_seg)]
    lt_first = z_gather(lt[0], n_rank, nz)[:, None]
    lt_rest = lax.all_gather(lt[1:], "z", axis=0)
    lts, mids, outs = [], [], []
    for s in range(n_seg):
        full = lt_first[:, 0] if s == 0 else lt_rest[:, s - 1]
        full = full.reshape(n_dp, lrows + 2, ch)
        lts.append(full[:, :lrows].reshape(3 * hc, ch))
        row = full[:, lrows].astype(F32)
        mids.append(jnp.stack([
            lax.dynamic_slice_in_dim(row[:, i * hc : (i + 1) * hc], rank * q, q, axis=1).reshape(hc)
            for i in range(2)]))
        own = lax.dynamic_index_in_dim(row, rank, 0, keepdims=False)
        outs.append(jnp.stack([
            jnp.tile(own[2 * hc + i * cc : 2 * hc + (i + 1) * cc], 2) for i in range(2)]))

    def by_pixel(v):
        width = v.shape[2]
        v = v.reshape(n_rank * fr, area, width).transpose(1, 0, 2)
        return v.reshape(pixels, width)

    def packed(v):
        return jnp.concatenate([v[:half], v[half:]], axis=1)

    a0 = by_pixel(gathered[:, :rows])
    flags = gathered[:, rows, :fr].reshape(nf) > 0.5
    slot = jnp.arange(nf) % fr
    before = jnp.where(flags | (slot == 0), 0.0, 1.0)
    after = jnp.where(jnp.roll(flags, -1) | (slot == fr - 1), 0.0, 1.0)
    spread = (side * nf + nf, hc)
    before = jnp.broadcast_to(jnp.tile(before, side + 1)[:, None], spread)
    after = jnp.broadcast_to(jnp.tile(after, side + 1)[:, None], spread)
    skip = packed(lax.dynamic_slice_in_dim(a0, rank * cc, cc, axis=1))

    cot_moving = lax.ppermute(cot.reshape(rows, ch), EVERY, to_plane)
    cot_moving = cot_moving.reshape(rows, n_rank, cc).transpose(1, 0, 2)
    cot_own = packed(by_pixel(lax.all_to_all(cot_moving, PLANE, 0, 0)))

    def to_frames(v):
        v = jnp.concatenate([v[:, :cc], v[:, cc:]], axis=0)
        v = v.reshape(area, n_rank, fr, cc).transpose(1, 0, 2, 3).reshape(n_rank, rows, cc)
        v = lax.all_to_all(v, PLANE, 0, 0).transpose(1, 0, 2).reshape(area, fr, ch)
        return lax.ppermute(v, EVERY, from_plane).transpose(1, 0, 2).reshape(frames.shape)

    saved = []
    g = [a0]
    for s in range(n_seg):
        pad, hidden, xm, rm, mate, keep = conv_forward(
            rank_now, g, kts[s], lts[s], mids[s], before, after, side, pixels, ch,
            deps=(cot_own,) if s == 0 else ())
        parts = plane_reduce(mate, keep)
        xo, ro, pre, res = out_norm(parts, outs[s], skip if s % 2 == 1 else None)
        saved.append((pad, hidden, xm, rm, xo, ro, pre))
        if s % 2 == 1:
            skip = res
        if s < n_seg - 1:
            g = plane_gather(res)
    output = to_frames(res)

    parts = [cot_own]
    skip_grad = None
    sgrads, tgrads, raw = [], [], ()
    for s in reversed(range(n_seg)):
        pad, hidden, xm, rm, xo, ro, pre = saved[s]
        if s == 1:
            parts = parts + [skip_grad]
        dpre, dt, osum = out_back(parts, pre, xo, ro, outs[s], deps=raw)
        if s % 2 == 1:
            skip_grad = dpre
        dtf, ds, msum, mate, keep = conv_back(
            rank_now, plane_gather(dt), xm, rm, kts[s], lts[s], mids[s], before, after, side,
            deps=(sgrads[-2], tgrads[-2]) if len(sgrads) > 1 else ())
        sg, tg = kernel_grads(pad, hidden, ds, dtf, before, after, side, nz)
        row = jnp.concatenate([msum[0], msum[1], osum[0, :cc], osum[1, :cc]]).astype(BF)
        row = jnp.pad(row[None], ((0, 1), (0, ch - row.shape[0])))
        tg = jnp.concatenate(
            [tg.reshape(n_dp, lrows, ch), jnp.broadcast_to(row, (n_dp, 2, ch))], axis=1)
        sgrads.append(lax.psum_scatter(sg, "z", scatter_dimension=0))
        raw = (sg,)
        tg = tg.reshape(nz, -1, ch)
        if s > 0:
            tgrads.append(lax.psum_scatter(tg, "z", scatter_dimension=0))
        else:
            tgrads.append(z_reduce(tg, n_rank, nz))
        parts = plane_reduce(mate, keep)

    da = sum(p.astype(F32) for p in parts) + skip_grad.astype(F32)
    frames_grad = to_frames(da.astype(BF)).astype(F32)

    tg = jnp.stack(tgrads[::-1])
    sg = jnp.stack(sgrads[::-1])
    sg = sg.reshape(n_seg, hc, 2, -1).transpose(2, 0, 1, 3).reshape(n_rank, hc, -1)
    sg = lax.all_to_all(sg, PLANE, 0, 0).reshape(hid, -1)
    space_grad = lax.dot_general(sg, perm, (((0,), (0,)), ((), ())), preferred_element_type=F32)
    tg = tg.reshape(n_seg, 2, lrows + 2, ch).transpose(1, 0, 2, 3).reshape(n_rank, lrows + 2, ch)
    tg = lax.all_to_all(tg, PLANE, 0, 0)
    row = tg[:, lrows].astype(F32)
    tg = tg[:, :lrows].reshape(n_rank, -1, q, ch)
    time_grad = tg.transpose(1, 0, 2, 3).reshape(-1, ch).astype(F32)
    own = lax.dynamic_index_in_dim(row, d_index, 0, keepdims=True)
    return (
        output,
        frames_grad,
        space_grad[None],
        time_grad[None],
        lax.dynamic_slice_in_dim(row[:, :hc], d_index * q, q, axis=1).reshape(1, hc),
        lax.dynamic_slice_in_dim(row[:, hc : 2 * hc], d_index * q, q, axis=1).reshape(1, hc),
        own[:, 2 * hc : 2 * hc + cc],
        own[:, 2 * hc + cc : 2 * hc + 2 * cc],
    )


def from_behind(value, axis, steps):
    count = lax.axis_size(axis)
    leading, last = (max(0, -steps), min(count, count - steps))
    return lax.ppermute(value, axis, [(source, source + steps) for source in range(leading, last)])


def space_apply(current, kernel):
    frame_side = current.shape[1]
    padded = jnp.pad(current, ((0, 0), (1, 1), (1, 1), (0, 0)))
    stacked = jnp.concatenate(
        [
            padded[:, row_shift : row_shift + frame_side, col_shift : col_shift + frame_side, :]
            for row_shift in range(3)
            for col_shift in range(3)
        ],
        axis=-1,
    )
    return (
        stacked,
        jnp.einsum("fijc,co->fijo", stacked, kernel, preferred_element_type=jnp.float32),
    )


def space_back(gradient, kernel):
    frame_side = gradient.shape[1]
    channels = kernel.shape[0] // 9
    spread = jnp.einsum("fijo,co->fijc", gradient, kernel, preferred_element_type=jnp.float32)
    total = jnp.zeros((gradient.shape[0], frame_side + 2, frame_side + 2, channels), jnp.float32)
    for tap_index in range(9):
        row_shift = tap_index // 3
        col_shift = tap_index % 3
        piece_now = spread[..., tap_index * channels : (tap_index + 1) * channels]
        total = total + jnp.pad(
            piece_now, ((0, 0), (row_shift, 2 - row_shift), (col_shift, 2 - col_shift), (0, 0))
        )
    return total[:, 1 : frame_side + 1, 1 : frame_side + 1, :]


def time_apply(current, kernel, before_mask, after_mask):
    blanks = jnp.zeros_like(current[:1])
    earlier = jnp.concatenate([blanks, current[:-1]], axis=0) * before_mask[
        :, None, None, None
    ].astype(current.dtype)
    later = jnp.concatenate([current[1:], blanks], axis=0) * after_mask[:, None, None, None].astype(
        current.dtype
    )
    stacked = jnp.concatenate([earlier, current, later], axis=-1)
    return (
        stacked,
        jnp.einsum("fijc,co->fijo", stacked, kernel, preferred_element_type=jnp.float32),
    )


def time_back(gradient, kernel, before_mask, after_mask):
    channels = kernel.shape[0] // 3
    spread = jnp.einsum("fijo,co->fijc", gradient, kernel, preferred_element_type=jnp.float32)
    early_part = spread[..., :channels] * before_mask[:, None, None, None]
    late_part = spread[..., 2 * channels :] * after_mask[:, None, None, None]
    blanks = jnp.zeros_like(early_part[:1])
    moved_early = jnp.concatenate([early_part[1:], blanks], axis=0)
    moved_late = jnp.concatenate([blanks, late_part[:-1]], axis=0)
    return spread[..., channels : 2 * channels] + moved_early + moved_late


def moments(values, pixel_count):
    average = lax.psum(jnp.sum(values, axis=(0, 1, 2)), "dp") / pixel_count
    centered = values - average
    spread = lax.psum(jnp.sum(centered * centered, axis=(0, 1, 2)), "dp") / pixel_count
    return (average, lax.rsqrt(spread + eps))


def reduce_back(gradient, normed):
    return lax.psum(
        (jnp.sum(gradient, axis=(0, 1, 2)), jnp.sum(gradient * normed, axis=(0, 1, 2))), "dp"
    )


def silu_slope(values):
    sigmoid_now = jax.nn.sigmoid(values)
    return sigmoid_now * (1.0 + values * (1.0 - sigmoid_now))


def pick_slot(stack, slot_index):
    return lax.dynamic_index_in_dim(stack, slot_index, 0, keepdims=False)


def store_slot(stack, value, slot_index, usable):
    previous = pick_slot(stack, slot_index)
    return lax.dynamic_update_index_in_dim(stack, jnp.where(usable, value, previous), slot_index, 0)


def on_device_general(
    frames, cotangent, starts, space_kernel, time_kernel, mid_gain, mid_bias, out_gain, out_bias
):
    n_segment = lax.axis_size("segment")
    n_data = lax.axis_size("dp")
    segment_index = lax.axis_index("segment")
    odd_segment = segment_index % 2 == 1
    last_segment = segment_index == n_segment - 1
    first_segment = segment_index == 0
    frame_count = frames.shape[0]
    frame_side = frames.shape[1]
    channels = frames.shape[3]
    hidden_units = mid_gain.shape[1] * n_data
    pixel_count = n_data * frame_count * frame_side * frame_side
    turns = 2 * n_segment - 1
    block_shape = (n_segment,) + frames.shape
    all_frames, all_cot, all_starts = (
        lax.all_gather(frames, "segment", axis=0, tiled=True),
        lax.all_gather(cotangent, "segment", axis=0, tiled=True),
        lax.all_gather(starts.astype(jnp.bfloat16), "segment", axis=0, tiled=True),
    )
    frame_stack = all_frames.reshape(block_shape)
    cot_stack = all_cot.reshape(block_shape)
    clip_flags = all_starts.astype(jnp.float32).reshape(n_segment, frame_count)
    positions = jnp.arange(frame_count)
    before_mask = jnp.where((clip_flags > 0.5) | (positions == 0), 0.0, 1.0)
    following = jnp.concatenate([clip_flags[:, 1:], jnp.ones((n_segment, 1), jnp.float32)], axis=1)
    after_mask = jnp.where(following > 0.5, 0.0, 1.0)
    gathered = (
        lax.all_gather(space_kernel[0].astype(jnp.bfloat16), "dp", axis=0, tiled=True),
        lax.all_gather(time_kernel[0].astype(jnp.bfloat16), "dp", axis=0, tiled=True),
        lax.all_gather(mid_gain[0].astype(jnp.bfloat16), "dp", axis=0, tiled=True),
        lax.all_gather(mid_bias[0].astype(jnp.bfloat16), "dp", axis=0, tiled=True),
        lax.all_gather(out_gain[0].astype(jnp.bfloat16), "dp", axis=0, tiled=True),
        lax.all_gather(out_bias[0].astype(jnp.bfloat16), "dp", axis=0, tiled=True),
    )
    space_low, time_low = (gathered[0], gathered[1])
    mid_gain_now = gathered[2].astype(jnp.float32)
    mid_bias_now = gathered[3].astype(jnp.float32)
    out_gain_now = gathered[4].astype(jnp.float32)
    out_bias_now = gathered[5].astype(jnp.float32)
    incoming = jnp.zeros_like(frames)
    carried = jnp.zeros_like(frames)
    kept_input = jnp.zeros(block_shape, jnp.bfloat16)
    kept_skip = jnp.zeros(block_shape, jnp.bfloat16)
    kept_mid_mean = jnp.zeros((n_segment, hidden_units), jnp.float32)
    kept_mid_scale = jnp.zeros((n_segment, hidden_units), jnp.float32)
    kept_out_mean = jnp.zeros((n_segment, channels), jnp.float32)
    kept_out_scale = jnp.zeros((n_segment, channels), jnp.float32)
    results = jnp.zeros(block_shape, jnp.float32)
    for turn_index in range(turns):
        micro_index = turn_index - segment_index
        usable = (micro_index >= 0) & (micro_index < n_segment)
        slot_index = jnp.clip(micro_index, 0, n_segment - 1)
        current = jnp.where(first_segment, pick_slot(frame_stack, slot_index), incoming)
        skip_input = carried
        _, spatial = space_apply(current, space_low)
        mid_mean, mid_scale = moments(spatial, pixel_count)
        hidden_act = jax.nn.silu(
            (spatial - mid_mean) * mid_scale * mid_gain_now + mid_bias_now
        ).astype(jnp.bfloat16)
        _, temporal = time_apply(
            hidden_act,
            time_low,
            pick_slot(before_mask, slot_index),
            pick_slot(after_mask, slot_index),
        )
        out_mean, out_scale = moments(temporal, pixel_count)
        pre_act = (
            (temporal - out_mean) * out_scale * out_gain_now
            + out_bias_now
            + jnp.where(odd_segment, skip_input.astype(jnp.float32), 0.0)
        )
        result = jax.nn.silu(pre_act).astype(jnp.bfloat16)
        kept_input = store_slot(kept_input, current, slot_index, usable)
        kept_skip = store_slot(kept_skip, skip_input, slot_index, usable)
        kept_mid_mean = store_slot(kept_mid_mean, mid_mean, slot_index, usable)
        kept_mid_scale = store_slot(kept_mid_scale, mid_scale, slot_index, usable)
        kept_out_mean = store_slot(kept_out_mean, out_mean, slot_index, usable)
        kept_out_scale = store_slot(kept_out_scale, out_scale, slot_index, usable)
        results = store_slot(results, result.astype(jnp.float32), slot_index, usable)
        if turn_index < turns - 1:
            incoming, carried = from_behind(
                (result, jnp.where(odd_segment, result, current)), "segment", 1
            )
    gathered = (
        lax.all_gather(space_kernel[0].astype(jnp.bfloat16), "dp", axis=0, tiled=True),
        lax.all_gather(time_kernel[0].astype(jnp.bfloat16), "dp", axis=0, tiled=True),
        lax.all_gather(mid_gain[0].astype(jnp.bfloat16), "dp", axis=0, tiled=True),
        lax.all_gather(mid_bias[0].astype(jnp.bfloat16), "dp", axis=0, tiled=True),
        lax.all_gather(out_gain[0].astype(jnp.bfloat16), "dp", axis=0, tiled=True),
        lax.all_gather(out_bias[0].astype(jnp.bfloat16), "dp", axis=0, tiled=True),
    )
    space_low, time_low = (gathered[0], gathered[1])
    mid_gain_now = gathered[2].astype(jnp.float32)
    mid_bias_now = gathered[3].astype(jnp.float32)
    out_gain_now = gathered[4].astype(jnp.float32)
    out_bias_now = gathered[5].astype(jnp.float32)
    grad_input = jnp.zeros_like(frames)
    grad_skip = jnp.zeros_like(frames)
    space_acc = jnp.zeros(space_low.shape, jnp.float32)
    time_acc = jnp.zeros(time_low.shape, jnp.float32)
    mid_gain_acc = jnp.zeros((hidden_units,), jnp.float32)
    mid_bias_acc = jnp.zeros((hidden_units,), jnp.float32)
    out_gain_acc = jnp.zeros((channels,), jnp.float32)
    out_bias_acc = jnp.zeros((channels,), jnp.float32)
    input_grads = jnp.zeros(block_shape, jnp.float32)
    for turn_index in range(turns):
        micro_index = n_segment - 1 - (turn_index - (n_segment - 1 - segment_index))
        usable = (micro_index >= 0) & (micro_index < n_segment)
        usable_weight = usable.astype(jnp.float32)
        slot_index = jnp.clip(micro_index, 0, n_segment - 1)
        current = pick_slot(kept_input, slot_index)
        skip_input = pick_slot(kept_skip, slot_index)
        before_now = pick_slot(before_mask, slot_index)
        after_now = pick_slot(after_mask, slot_index)
        space_taps, spatial = space_apply(current, space_low)
        mid_normed = (spatial - pick_slot(kept_mid_mean, slot_index)) * pick_slot(
            kept_mid_scale, slot_index
        )
        mid_pre = mid_normed * mid_gain_now + mid_bias_now
        hidden_act = jax.nn.silu(mid_pre).astype(jnp.bfloat16)
        time_taps, temporal = time_apply(hidden_act, time_low, before_now, after_now)
        out_scale = pick_slot(kept_out_scale, slot_index)
        out_normed = (temporal - pick_slot(kept_out_mean, slot_index)) * out_scale
        pre_act = (
            out_normed * out_gain_now
            + out_bias_now
            + jnp.where(odd_segment, skip_input.astype(jnp.float32), 0.0)
        )
        grad_result = jnp.where(
            last_segment,
            pick_slot(cot_stack, slot_index).astype(jnp.float32),
            grad_input.astype(jnp.float32)
            + jnp.where(odd_segment, grad_skip.astype(jnp.float32), 0.0),
        )
        grad_pre = grad_result * silu_slope(pre_act)
        out_bias_sum, out_gain_sum = reduce_back(grad_pre, out_normed)
        grad_temporal = (
            out_gain_now
            * out_scale
            * (grad_pre - out_bias_sum / pixel_count - out_normed * out_gain_sum / pixel_count)
        ).astype(jnp.bfloat16)
        time_acc = time_acc + usable_weight * jnp.einsum(
            "fijc,fijo->co", time_taps, grad_temporal, preferred_element_type=jnp.float32
        )
        grad_hidden = time_back(grad_temporal, time_low, before_now, after_now)
        grad_mid = grad_hidden * silu_slope(mid_pre)
        mid_bias_sum, mid_gain_sum = reduce_back(grad_mid, mid_normed)
        mid_scale = pick_slot(kept_mid_scale, slot_index)
        grad_spatial = (
            mid_gain_now
            * mid_scale
            * (grad_mid - mid_bias_sum / pixel_count - mid_normed * mid_gain_sum / pixel_count)
        ).astype(jnp.bfloat16)
        space_acc = space_acc + usable_weight * jnp.einsum(
            "fijc,fijo->co", space_taps, grad_spatial, preferred_element_type=jnp.float32
        )
        grad_current = space_back(grad_spatial, space_low)
        mid_gain_acc = mid_gain_acc + usable_weight * mid_gain_sum
        mid_bias_acc = mid_bias_acc + usable_weight * mid_bias_sum
        out_gain_acc = out_gain_acc + usable_weight * out_gain_sum
        out_bias_acc = out_bias_acc + usable_weight * out_bias_sum
        input_grads = store_slot(
            input_grads, grad_current + grad_skip.astype(jnp.float32), slot_index, usable
        )
        if turn_index < turns - 1:
            grad_input, grad_skip = from_behind(
                (
                    grad_current.astype(jnp.bfloat16),
                    jnp.where(odd_segment, grad_pre.astype(jnp.bfloat16), grad_skip),
                ),
                "segment",
                -1,
            )
    space_grad, time_grad = (
        lax.psum_scatter(space_acc, "dp", scatter_dimension=0, tiled=True),
        lax.psum_scatter(time_acc, "dp", scatter_dimension=0, tiled=True),
    )
    data_index = lax.axis_index("dp")

    def own_share(full_vector):
        share = full_vector.shape[0] // n_data
        return lax.dynamic_slice_in_dim(full_vector, data_index * share, share)[None]

    flat_shape = (n_segment * frame_count,) + frames.shape[1:]
    arrived_out, arrived_grads = (
        lax.all_to_all(
            results.reshape(flat_shape).astype(jnp.bfloat16),
            "segment",
            split_axis=0,
            concat_axis=0,
            tiled=True,
        ).astype(jnp.float32),
        lax.all_to_all(
            input_grads.reshape(flat_shape).astype(jnp.bfloat16),
            "segment",
            split_axis=0,
            concat_axis=0,
            tiled=True,
        ).astype(jnp.float32),
    )
    output = arrived_out[(n_segment - 1) * frame_count :].astype(jnp.bfloat16)
    frames_grad = arrived_grads[:frame_count]
    return (
        output,
        frames_grad,
        space_grad[None],
        time_grad[None],
        own_share(mid_gain_acc),
        own_share(mid_bias_acc),
        own_share(out_gain_acc),
        own_share(out_bias_acc),
    )


def general(mesh):
    return jax.shard_map(
        on_device_general,
        mesh=mesh,
        in_specs=(
            P(("dp", "segment"), None, None, None),
            P(("dp", "segment"), None, None, None),
            P(("dp", "segment")),
            P("segment", "dp", None),
            P("segment", "dp", None),
            P("segment", "dp"),
            P("segment", "dp"),
            P("segment", "dp"),
            P("segment", "dp"),
        ),
        out_specs=(
            P(("dp", "segment"), None, None, None),
            P(("dp", "segment"), None, None, None),
            P("segment", "dp", None),
            P("segment", "dp", None),
            P("segment", "dp"),
            P("segment", "dp"),
            P("segment", "dp"),
            P("segment", "dp"),
        ),
        check_vma=False,
    )


def solution(mesh):
    if mesh.shape["dp"] != 8 or mesh.shape["segment"] != 4:
        return general(mesh)
    n_dp, n_seg = mesh.shape["dp"], mesh.shape["segment"]
    fine = Mesh(mesh.devices.reshape(n_dp // 2, 2, 2, n_seg // 2), EVERY)
    dp, seg = ("z", "y"), ("x", "c")
    return jax.shard_map(
        on_device,
        mesh=fine,
        in_specs=(
            P(EVERY, None, None, None),
            P(EVERY, None, None, None),
            P(EVERY),
            P(seg, dp, None),
            P(seg, dp, None),
            P(seg, dp),
            P(seg, dp),
            P(seg, dp),
            P(seg, dp),
        ),
        out_specs=(
            P(EVERY, None, None, None),
            P(EVERY, None, None, None),
            P(seg, dp, None),
            P(seg, dp, None),
            P(seg, dp),
            P(seg, dp),
            P(seg, dp),
            P(seg, dp),
        ),
        check_vma=False,
    )
```

```python
import functools

import jax
import jax.numpy as jnp
from jax import lax
from jax.experimental import pallas as pl
from jax.experimental.pallas import tpu as pltpu
from jax.sharding import Mesh, PartitionSpec as P

eps = 1e-05
PLANE = ("y", "x", "c")
EVERY = ("z", "y", "x", "c")
BF = jnp.bfloat16
F32 = jnp.float32


def nt(a, b):
    return lax.dot_general(a, b, (((1,), (1,)), ((), ())), preferred_element_type=F32)


def nn(a, b):
    return lax.dot_general(a, b, (((1,), (0,)), ((), ())), preferred_element_type=F32)


VMEM_CAP = 56 * 1024 * 1024
ANY = pl.BlockSpec(memory_space=pl.ANY)


def call(body, outs, scratch, flops, *args, deps=(), far=(), far_outs=()):
    moved = sum(a.size * a.dtype.itemsize for a in args) + sum(
        o.size * o.dtype.itemsize for o in outs
    )
    n = len(deps)

    def spec(a):
        return pl.BlockSpec(memory_space=pltpu.SMEM if a.dtype == jnp.int32 else pltpu.VMEM)

    return pl.pallas_call(
        lambda *refs: body(*refs[n:]),
        out_shape=outs,
        in_specs=[ANY] * n + [ANY if i in far else spec(a) for i, a in enumerate(args)],
        out_specs=[ANY if i in far_outs else spec(o) for i, o in enumerate(outs)],
        scratch_shapes=scratch,
        compiler_params=pltpu.CompilerParams(vmem_limit_bytes=VMEM_CAP),
        cost_estimate=pl.CostEstimate(flops=flops, bytes_accessed=moved, transcendentals=0),
    )(*deps, *args)


def chunk(i, size):
    return pl.ds(pl.multiple_of(i * size, 16), size)


def clear_borders(pad_ref, side, plane, nf):
    zrow = jnp.zeros(pad_ref.shape[1:], BF)
    pad_ref[0] = zrow
    pad_ref[side + 1] = zrow
    zcol = jnp.zeros((nf, pad_ref.shape[2]), BF)
    for i in range(side):
        pad_ref[i + 1, 0:nf] = zcol
        pad_ref[i + 1, nf + plane : 2 * nf + plane] = zcol


def by_rank(slices, rank):
    odd = lax.rem(rank, 2) == 1
    for p in range(len(slices) // 2):
        a, b = slices[2 * p], slices[2 * p + 1]
        yield lax.bitwise_xor(rank // 2, p), odd, a, b


def halves(odd, own, mate):
    low = lax.broadcasted_iota(jnp.int32, own.shape, 1) < 64
    own, mate = own.astype(F32), mate.astype(F32)
    a, b = jnp.where(odd, mate, own), jnp.where(odd, own, mate)
    top = jnp.where(low, a, pltpu.roll(b, 64, 1))
    bottom = jnp.where(low, pltpu.roll(a, 64, 1), b)
    return top, bottom


def store_packed(rank, mate_ref, keep_ref, part, k, step, low):
    rows_now = chunk(k, step)
    odd = lax.rem(rank, 2) == 1
    for q in range(keep_ref.shape[0]):
        x = part[:step, 128 * q : 128 * q + 128]
        y = part[step:, 128 * q : 128 * q + 128]
        even_slice = jnp.where(low, x, pltpu.roll(y, 64, 1))
        odd_slice = jnp.where(low, pltpu.roll(x, 64, 1), y)
        p = lax.bitwise_xor(rank // 2, q)
        keep_ref[p, rows_now, :] = jnp.where(odd, odd_slice, even_slice).astype(BF)
        mate_ref[p, rows_now, :] = jnp.where(odd, even_slice, odd_slice).astype(BF)


def fetch_kernels(kt_ref, lt_ref, ktm_ref, ltm_ref, sems):
    width = kt_ref.shape[2]
    copies = [
        pltpu.make_async_copy(kt_ref.at[z], ktm_ref.at[:, pl.ds(z * width, width)], sems.at[z])
        for z in range(kt_ref.shape[0])
    ]
    copies.append(pltpu.make_async_copy(lt_ref, ltm_ref, sems.at[kt_ref.shape[0]]))
    for copy in copies:
        copy.start()
    return copies


def conv_body(side, first, rank_ref, *refs):
    n = 1 if first else 8
    slices = refs[:n]
    (kt_ref, lt_ref, vec_ref, before_ref, after_ref,
     pad_out, hid_out, xhat_out, rs_ref, mate_ref, keep_ref,
     pad_ref, hid_ref, xhat_ref, sp_ref, ktm_ref, ltm_ref, kn_ref, sems) = refs[n:]
    rank = rank_ref[0]
    nz = kt_ref.shape[0]
    fetched = fetch_kernels(kt_ref, lt_ref, ktm_ref, ltm_ref, sems)
    ch, hc = pad_ref.shape[2], hid_ref.shape[1]
    rows = hid_ref.shape[0]
    plane = rows // side
    nf = plane // side
    step = plane // 2
    clear_borders(pad_ref, side, plane, nf)
    if first:
        for i in range(side):
            pad_ref[i + 1, nf : nf + plane] = slices[0][i * plane : (i + 1) * plane]
    else:
        def place(k, carry):
            for q, odd, a_ref, b_ref in by_rank(slices, rank):
                top, bottom = halves(odd, a_ref[chunk(k, step), :], b_ref[chunk(k, step), :])
                lanes = pl.ds(pl.multiple_of(128 * q, 128), 128)
                for piece, kk in ((top, k), (bottom, k + side)):
                    at = nf + lax.rem(kk, 2) * step
                    pad_ref[1 + kk // 2, pl.ds(pl.multiple_of(at, 16), step), lanes] = piece.astype(BF)
            return carry

        lax.fori_loop(0, side, place, 0, unroll=True)
    pad_copy = pltpu.make_async_copy(pad_ref, pad_out, sems.at[nz + 1])
    pad_copy.start()
    for copy in fetched:
        copy.wait()
    for t in range(9):
        kn_ref[t] = ktm_ref[:, t * ch : (t + 1) * ch].astype(F32).T.astype(BF)

    def conv(i, total):
        acc = jnp.zeros((plane, hc), F32)
        for t in range(9):
            r, c = t // 3, t % 3
            acc += nn(pad_ref[i + r, c * nf : c * nf + plane, :], kn_ref[t])
        sp_ref[i] = acc
        return total + jnp.sum(acc, axis=0, keepdims=True)

    mean = lax.fori_loop(0, side, conv, jnp.zeros((1, hc), F32), unroll=True) / rows

    def square(i, total):
        cen = sp_ref[i] - mean
        return total + jnp.sum(cen * cen, axis=0, keepdims=True)

    var = lax.fori_loop(0, side, square, jnp.zeros((1, hc), F32), unroll=True) / rows
    rs = lax.rsqrt(var + eps)
    rs_ref[...] = rs
    gain, bias = vec_ref[0:1, :], vec_ref[1:2, :]

    def act(i, carry):
        xhat = (sp_ref[i] - mean) * rs
        xhat_ref[i] = xhat
        v = xhat * gain + bias
        v = v * jax.nn.sigmoid(v)
        sp_ref[i] = v
        hid_ref[chunk(i, plane), :] = v.astype(BF)
        return carry

    lax.fori_loop(0, side, act, 0, unroll=True)
    late = [
        pltpu.make_async_copy(hid_ref, hid_out, sems.at[nz + 2]),
        pltpu.make_async_copy(xhat_ref, xhat_out, sems.at[nz + 3]),
    ]
    for copy in late:
        copy.start()
    low = lax.broadcasted_iota(jnp.int32, (step, 128), 1) < 64

    def temporal(k, carry):
        pieces = []
        for kk in (k, k + side):
            par = lax.rem(kk, 2)
            h = sp_ref[kk // 2, pl.ds(pl.multiple_of(par * step, 8), step), :]
            at = pl.multiple_of(par * (step % nf), 8)
            pieces.append((
                (pltpu.roll(h, 1, 0) * before_ref[pl.ds(at, step), :]).astype(BF),
                h.astype(BF),
                (pltpu.roll(h, step - 1, 0) * after_ref[pl.ds(at, step), :]).astype(BF),
            ))
        part = sum(
            nn(jnp.concatenate([x, y], axis=0), ltm_ref[t * hc : (t + 1) * hc])
            for t, (x, y) in enumerate(zip(*pieces))
        )
        store_packed(rank, mate_ref, keep_ref, part, k, step, low)
        return carry

    lax.fori_loop(0, side, temporal, 0, unroll=True)
    for copy in [pad_copy] + late:
        copy.wait()


def conv_forward(rank, g, kt, lt, vec, before, after, side, pixels, ch, deps=()):
    hc = lt.shape[0] // 3
    plane = pixels // side
    nf = plane // side
    n = len(g)
    shapes = [
        ((side + 2, plane + 2 * nf, ch), BF),
        ((pixels, hc), BF),
        ((side, plane, hc), F32),
    ]
    outs = [jax.ShapeDtypeStruct(*s) for s in shapes] + [
        jax.ShapeDtypeStruct((1, hc), F32),
        jax.ShapeDtypeStruct((4, pixels // 2, 128), BF),
        jax.ShapeDtypeStruct((4, pixels // 2, 128), BF),
    ]
    scratch = [pltpu.VMEM(*s) for s in shapes] + [
        pltpu.VMEM((side, plane, hc), F32),
        pltpu.VMEM((hc, 9 * ch), BF),
        pltpu.VMEM((3 * hc, ch), BF),
        pltpu.VMEM((9, ch, hc), BF),
        pltpu.SemaphoreType.DMA((kt.shape[0] + 4,)),
    ]
    flops = 2 * pixels * hc * 12 * ch
    return call(functools.partial(conv_body, side, n == 1), outs, scratch, flops,
                rank, *g, kt, lt, vec, before, after,
                deps=deps, far=(n + 1, n + 2), far_outs=(0, 1, 2))


def fold(v):
    return v + pltpu.roll(v, 64, 1)


def total_of(refs):
    t = refs[0][...].astype(F32)
    for ref in refs[1:]:
        t += ref[...].astype(F32)
    return t


def pair_sum_body(keep_ref, mate_ref, *out_refs):
    for p, ref in enumerate(out_refs):
        ref[...] = (keep_ref[p].astype(F32) + mate_ref[p].astype(F32)).astype(ref.dtype)


def pair_sum(keep, arrived):
    shape = keep.shape[1:]
    outs = [jax.ShapeDtypeStruct(shape, BF)] * keep.shape[0]
    return call(pair_sum_body, outs, [], keep.size, keep, arrived)


def out_norm_body(n, has_skip, *refs):
    parts, refs = refs[:n], refs[n:]
    if has_skip:
        vec_ref, skip_ref, xhat_ref, rs_ref, pre_ref, res_ref = refs
    else:
        vec_ref, xhat_ref, rs_ref, pre_ref, res_ref = refs
    t = total_of(parts)
    pixels = 2 * t.shape[0]
    mean = fold(jnp.sum(t, axis=0, keepdims=True)) / pixels
    cen = t - mean
    rs = lax.rsqrt(fold(jnp.sum(cen * cen, axis=0, keepdims=True)) / pixels + eps)
    xhat = cen * rs
    pre = xhat * vec_ref[0:1, :] + vec_ref[1:2, :]
    if has_skip:
        pre = pre + skip_ref[...].astype(F32)
    xhat_ref[...] = xhat
    rs_ref[...] = rs
    pre_ref[...] = pre
    res_ref[...] = (pre * jax.nn.sigmoid(pre)).astype(BF)


def out_norm(parts, vec, skip):
    half = parts[0].shape[0]
    outs = [
        jax.ShapeDtypeStruct((half, 128), F32),
        jax.ShapeDtypeStruct((1, 128), F32),
        jax.ShapeDtypeStruct((half, 128), F32),
        jax.ShapeDtypeStruct((half, 128), BF),
    ]
    args = (*parts, vec) + (() if skip is None else (skip,))
    body = functools.partial(out_norm_body, len(parts), skip is not None)
    return call(body, outs, [], half * 128 * 10, *args)


def out_back_body(n, *refs):
    parts, (pre_ref, xhat_ref, rs_ref, vec_ref, dpre_ref, dt_ref, sums_ref) = refs[:n], refs[n:]
    g = total_of(parts)
    pre, xhat = pre_ref[...], xhat_ref[...]
    sig = jax.nn.sigmoid(pre)
    dpre = g * (sig * (1.0 + pre * (1.0 - sig)))
    pixels = 2 * pre.shape[0]
    sb = fold(jnp.sum(dpre, axis=0, keepdims=True))
    sg = fold(jnp.sum(dpre * xhat, axis=0, keepdims=True))
    dpre_ref[...] = dpre.astype(BF)
    scale = vec_ref[0:1, :] * rs_ref[...]
    dt_ref[...] = (scale * (dpre - sb / pixels - xhat * (sg / pixels))).astype(BF)
    sums_ref[0:1, :] = sg
    sums_ref[1:2, :] = sb


def out_back(parts, pre, xhat, rs, vec, deps=()):
    half = pre.shape[0]
    outs = [
        jax.ShapeDtypeStruct((half, 128), BF),
        jax.ShapeDtypeStruct((half, 128), BF),
        jax.ShapeDtypeStruct((2, 128), F32),
    ]
    args = (*parts, pre, xhat, rs, vec)
    return call(functools.partial(out_back_body, len(parts)), outs, [], half * 1280, *args, deps=deps)


def conv_back_body(side, rank_ref, *refs):
    slices, (xhat_in, rs_ref, kt_ref, lt_ref, vec_ref, before_ref, after_ref,
             dt_out, ds_out, sums_ref, mate_ref, keep_ref,
             dt_ref, ds_ref, xhat_ref, dy_ref, pad_ref, ktm_ref, ltm_ref, lnt_ref, sems) = (
        refs[:8], refs[8:])
    half = slices[0].shape[0]
    rank = rank_ref[0]
    nz = kt_ref.shape[0]
    rows = 2 * half
    plane = rows // side
    nf = plane // side
    step = plane // 2
    hc = ds_ref.shape[1]
    ch = dt_ref.shape[1]
    fetched = fetch_kernels(kt_ref, lt_ref, ktm_ref, ltm_ref, sems)
    xhat_copy = pltpu.make_async_copy(xhat_in, xhat_ref, sems.at[nz + 1])
    xhat_copy.start()
    clear_borders(pad_ref, side, plane, nf)

    def place(k, carry):
        for q, odd, a_ref, b_ref in by_rank(slices, rank):
            top, bottom = halves(odd, a_ref[chunk(k, step), :], b_ref[chunk(k, step), :])
            lanes = pl.ds(pl.multiple_of(128 * q, 128), 128)
            dt_ref[chunk(k, step), lanes] = top.astype(BF)
            dt_ref[pl.ds(pl.multiple_of(half + k * step, 16), step), lanes] = bottom.astype(BF)
        return carry

    lax.fori_loop(0, side, place, 0, unroll=True)
    dt_copy = pltpu.make_async_copy(dt_ref, dt_out, sems.at[nz + 2])
    dt_copy.start()
    for copy in fetched + [xhat_copy]:
        copy.wait()
    for t in range(3):
        lnt_ref[t] = ltm_ref[t * hc : (t + 1) * hc].astype(F32).T.astype(BF)
    gain, bias = vec_ref[0:1, :], vec_ref[1:2, :]

    def hidden_grad(i, sums):
        dt = dt_ref[chunk(i, plane), :]
        early = nn(dt, lnt_ref[0]) * before_ref[0:plane, :]
        late = nn(dt, lnt_ref[2]) * after_ref[0:plane, :]
        dh = nn(dt, lnt_ref[1]) + pltpu.roll(early, plane - 1, 0) + pltpu.roll(late, 1, 0)
        xhat = xhat_ref[i]
        v = xhat * gain + bias
        sig = jax.nn.sigmoid(v)
        dy = dh * (sig * (1.0 + v * (1.0 - sig)))
        dy_ref[i] = dy
        return (
            sums[0] + jnp.sum(dy * xhat, axis=0, keepdims=True),
            sums[1] + jnp.sum(dy, axis=0, keepdims=True),
        )

    zero = jnp.zeros((1, hc), F32)
    sg, sb = lax.fori_loop(0, side, hidden_grad, (zero, zero), unroll=True)
    sums_ref[0:1, :] = sg
    sums_ref[1:2, :] = sb
    scale = gain * rs_ref[...]

    def spatial_grad(i, carry):
        ds = (scale * (dy_ref[i] - sb / rows - xhat_ref[i] * (sg / rows))).astype(BF)
        pad_ref[i + 1, nf : nf + plane] = ds
        ds_ref[chunk(i, plane), :] = ds
        return carry

    lax.fori_loop(0, side, spatial_grad, 0, unroll=True)
    ds_copy = pltpu.make_async_copy(ds_ref, ds_out, sems.at[nz + 3])
    ds_copy.start()
    low = lax.broadcasted_iota(jnp.int32, (step, 128), 1) < 64

    def back(k, carry):
        acc = jnp.zeros((2 * step, ch), F32)
        for t in range(9):
            r, c = 2 - t // 3, 2 - t % 3
            pieces = []
            for kk in (k, k + side):
                at = c * nf + lax.rem(kk, 2) * step
                pieces.append(pad_ref[kk // 2 + r, pl.ds(pl.multiple_of(at, 16), step), :])
            acc += nn(jnp.concatenate(pieces, axis=0), ktm_ref[:, t * ch : (t + 1) * ch])
        store_packed(rank, mate_ref, keep_ref, acc, k, step, low)
        return carry

    lax.fori_loop(0, side, back, 0, unroll=True)
    dt_copy.wait()
    ds_copy.wait()


def conv_back(rank, g, xhat, rs, kt, lt, vec, before, after, side, deps=()):
    half = g[0].shape[0]
    hc = lt.shape[0] // 3
    ch = lt.shape[1]
    pixels = 2 * half
    plane = pixels // side
    nf = plane // side
    outs = [
        jax.ShapeDtypeStruct((pixels, ch), BF),
        jax.ShapeDtypeStruct((pixels, hc), BF),
        jax.ShapeDtypeStruct((2, hc), F32),
        jax.ShapeDtypeStruct((4, half, 128), BF),
        jax.ShapeDtypeStruct((4, half, 128), BF),
    ]
    scratch = [
        pltpu.VMEM((pixels, ch), BF),
        pltpu.VMEM((pixels, hc), BF),
        pltpu.VMEM((side, plane, hc), F32),
        pltpu.VMEM((side, plane, hc), F32),
        pltpu.VMEM((side + 2, plane + 2 * nf, hc), BF),
        pltpu.VMEM((hc, 9 * ch), BF),
        pltpu.VMEM((3 * hc, ch), BF),
        pltpu.VMEM((3, ch, hc), BF),
        pltpu.SemaphoreType.DMA((kt.shape[0] + 4,)),
    ]
    flops = 2 * pixels * hc * 12 * ch
    return call(functools.partial(conv_back_body, side), outs, scratch, flops,
                rank, *g, xhat, rs, kt, lt, vec, before, after,
                deps=deps, far=(9, 11, 12), far_outs=(0, 1))


def grads_body(side, pad_ref, hid_ref, ds_ref, dt_ref, before_ref, after_ref, sg_ref, tg_ref,
               dst_ref, taps_ref):
    ch = pad_ref.shape[2]
    hc = hid_ref.shape[1]
    plane = hid_ref.shape[0] // side
    nf = plane // side
    for i in (0, 1, side + 2, side + 3):
        dst_ref[i] = jnp.zeros(dst_ref.shape[1:], BF)
    for i in range(side):
        at = slice(i * plane, (i + 1) * plane)
        h = hid_ref[at, :].astype(F32)
        taps_ref[i, 0:hc] = (pltpu.roll(h, 1, 0) * before_ref[0:plane, :]).T.astype(BF)
        taps_ref[i, hc : 2 * hc] = h.T.astype(BF)
        taps_ref[i, 2 * hc : 3 * hc] = (pltpu.roll(h, plane - 1, 0) * after_ref[0:plane, :]).T.astype(BF)
        dst_ref[i + 2] = ds_ref[at, :].astype(F32).T.astype(BF)
    tg_ref[...] = sum(
        nn(taps_ref[i], dt_ref[i * plane : (i + 1) * plane, :]) for i in range(side)
    ).astype(BF)
    width = sg_ref.shape[2]
    for c in range(3):
        acc = sum(
            nn(dst_ref[i : i + 3].reshape(3 * hc, plane), pad_ref[i, c * nf : c * nf + plane, :])
            for i in range(1, side + 1)
        )
        for r in range(3):
            first = (3 * r + c) * ch
            end = first + ch
            at = (2 - r) * hc
            done = 0
            while first < end:
                z = first // width
                last = min(end, (z + 1) * width)
                sg_ref[z, :, first - z * width : last - z * width] = (
                    acc[at : at + hc, done : done + last - first].astype(BF)
                )
                done += last - first
                first = last


def kernel_grads(pad, hidden, ds, dt, before, after, side, nz, deps=()):
    pixels, hc = hidden.shape
    ch = dt.shape[1]
    plane = pixels // side
    outs = [
        jax.ShapeDtypeStruct((nz, hc, 9 * ch // nz), BF),
        jax.ShapeDtypeStruct((3 * hc, ch), BF),
    ]
    scratch = [
        pltpu.VMEM((side + 4, hc, plane), BF),
        pltpu.VMEM((side, 3 * hc, plane), BF),
    ]
    flops = 2 * pixels * hc * 12 * ch
    return call(functools.partial(grads_body, side), outs, scratch, flops,
                pad, hidden, ds, dt, before, after, deps=deps)


def copy_after_body(v_ref, out_ref):
    out_ref[...] = v_ref[...]


def after_all(v, *deps):
    return call(copy_after_body, [jax.ShapeDtypeStruct(v.shape, v.dtype)], [], v.size, v, deps=deps)[0]


def call(body, outs, scratch, flops, *args, deps=(), far=(), far_outs=()):
    moved = sum(a.size * a.dtype.itemsize for a in args) + sum(
        o.size * o.dtype.itemsize for o in outs
    )
    n = len(deps)

    def spec(a):
        return pl.BlockSpec(memory_space=pltpu.SMEM if a.dtype == jnp.int32 else pltpu.VMEM)

    return pl.pallas_call(
        lambda *refs: body(*refs[n:]),
        out_shape=outs,
        in_specs=[ANY] * n + [ANY if i in far else spec(a) for i, a in enumerate(args)],
        out_specs=[ANY if i in far_outs else spec(o) for i, o in enumerate(outs)],
        scratch_shapes=scratch,
        compiler_params=pltpu.CompilerParams(vmem_limit_bytes=VMEM_CAP),
        cost_estimate=pl.CostEstimate(flops=flops, bytes_accessed=moved, transcendentals=0),
    )(*deps, *args)


def chunk(i, size):
    return pl.ds(pl.multiple_of(i * size, 16), size)


def clear_borders(pad_ref, side, plane, nf):
    zrow = jnp.zeros(pad_ref.shape[1:], BF)
    pad_ref[0] = zrow
    pad_ref[side + 1] = zrow
    zcol = jnp.zeros((nf, pad_ref.shape[2]), BF)
    for i in range(side):
        pad_ref[i + 1, 0:nf] = zcol
        pad_ref[i + 1, nf + plane : 2 * nf + plane] = zcol


def by_rank(slices, rank):
    odd = lax.rem(rank, 2) == 1
    for p in range(len(slices) // 2):
        a, b = slices[2 * p], slices[2 * p + 1]
        yield lax.bitwise_xor(rank // 2, p), odd, a, b


def halves(odd, own, mate):
    low = lax.broadcasted_iota(jnp.int32, own.shape, 1) < 64
    own, mate = own.astype(F32), mate.astype(F32)
    a, b = jnp.where(odd, mate, own), jnp.where(odd, own, mate)
    top = jnp.where(low, a, pltpu.roll(b, 64, 1))
    bottom = jnp.where(low, pltpu.roll(a, 64, 1), b)
    return top, bottom


def store_packed(rank, mate_ref, keep_ref, part, k, step, low):
    rows_now = chunk(k, step)
    odd = lax.rem(rank, 2) == 1
    for q in range(keep_ref.shape[0]):
        x = part[:step, 128 * q : 128 * q + 128]
        y = part[step:, 128 * q : 128 * q + 128]
        even_slice = jnp.where(low, x, pltpu.roll(y, 64, 1))
        odd_slice = jnp.where(low, pltpu.roll(x, 64, 1), y)
        p = lax.bitwise_xor(rank // 2, q)
        keep_ref[p, rows_now, :] = jnp.where(odd, odd_slice, even_slice).astype(BF)
        mate_ref[p, rows_now, :] = jnp.where(odd, even_slice, odd_slice).astype(BF)


def fetch_kernels(kt_ref, lt_ref, ktm_ref, ltm_ref, sems):
    width = kt_ref.shape[2]
    copies = [
        pltpu.make_async_copy(kt_ref.at[z], ktm_ref.at[:, pl.ds(z * width, width)], sems.at[z])
        for z in range(kt_ref.shape[0])
    ]
    copies.append(pltpu.make_async_copy(lt_ref, ltm_ref, sems.at[kt_ref.shape[0]]))
    for copy in copies:
        copy.start()
    return copies


def conv_body(side, first, rank_ref, *refs):
    n = 1 if first else 8
    slices = refs[:n]
    (kt_ref, lt_ref, vec_ref, before_ref, after_ref,
     pad_out, hid_out, xhat_out, rs_ref, mate_ref, keep_ref,
     pad_ref, hid_ref, xhat_ref, sp_ref, ktm_ref, ltm_ref, kn_ref, sems) = refs[n:]
    rank = rank_ref[0]
    nz = kt_ref.shape[0]
    fetched = fetch_kernels(kt_ref, lt_ref, ktm_ref, ltm_ref, sems)
    ch, hc = pad_ref.shape[2], hid_ref.shape[1]
    rows = hid_ref.shape[0]
    plane = rows // side
    nf = plane // side
    step = plane // 2
    clear_borders(pad_ref, side, plane, nf)
    if first:
        for i in range(side):
            pad_ref[i + 1, nf : nf + plane] = slices[0][i * plane : (i + 1) * plane]
    else:
        def place(k, carry):
            for q, odd, a_ref, b_ref in by_rank(slices, rank):
                top, bottom = halves(odd, a_ref[chunk(k, step), :], b_ref[chunk(k, step), :])
                lanes = pl.ds(pl.multiple_of(128 * q, 128), 128)
                for piece, kk in ((top, k), (bottom, k + side)):
                    at = nf + lax.rem(kk, 2) * step
                    pad_ref[1 + kk // 2, pl.ds(pl.multiple_of(at, 16), step), lanes] = piece.astype(BF)
            return carry

        lax.fori_loop(0, side, place, 0, unroll=True)
    pad_copy = pltpu.make_async_copy(pad_ref, pad_out, sems.at[nz + 1])
    pad_copy.start()
    for copy in fetched:
        copy.wait()
    for t in range(9):
        kn_ref[t] = ktm_ref[:, t * ch : (t + 1) * ch].astype(F32).T.astype(BF)

    def conv(i, total):
        acc = jnp.zeros((plane, hc), F32)
        for t in range(9):
            r, c = t // 3, t % 3
            acc += nn(pad_ref[i + r, c * nf : c * nf + plane, :], kn_ref[t])
        sp_ref[i] = acc
        return total + jnp.sum(acc, axis=0, keepdims=True)

    mean = lax.fori_loop(0, side, conv, jnp.zeros((1, hc), F32), unroll=True) / rows

    def square(i, total):
        cen = sp_ref[i] - mean
        return total + jnp.sum(cen * cen, axis=0, keepdims=True)

    var = lax.fori_loop(0, side, square, jnp.zeros((1, hc), F32), unroll=True) / rows
    rs = lax.rsqrt(var + eps)
    rs_ref[...] = rs
    gain, bias = vec_ref[0:1, :], vec_ref[1:2, :]

    def act(i, carry):
        xhat = (sp_ref[i] - mean) * rs
        xhat_ref[i] = xhat
        v = xhat * gain + bias
        v = v * jax.nn.sigmoid(v)
        sp_ref[i] = v
        hid_ref[chunk(i, plane), :] = v.astype(BF)
        return carry

    lax.fori_loop(0, side, act, 0, unroll=True)
    late = [
        pltpu.make_async_copy(hid_ref, hid_out, sems.at[nz + 2]),
        pltpu.make_async_copy(xhat_ref, xhat_out, sems.at[nz + 3]),
    ]
    for copy in late:
        copy.start()
    low = lax.broadcasted_iota(jnp.int32, (step, 128), 1) < 64

    def temporal(k, carry):
        pieces = []
        for kk in (k, k + side):
            par = lax.rem(kk, 2)
            h = sp_ref[kk // 2, pl.ds(pl.multiple_of(par * step, 8), step), :]
            at = pl.multiple_of(par * (step % nf), 8)
            pieces.append((
                (pltpu.roll(h, 1, 0) * before_ref[pl.ds(at, step), :]).astype(BF),
                h.astype(BF),
                (pltpu.roll(h, step - 1, 0) * after_ref[pl.ds(at, step), :]).astype(BF),
            ))
        part = sum(
            nn(jnp.concatenate([x, y], axis=0), ltm_ref[t * hc : (t + 1) * hc])
            for t, (x, y) in enumerate(zip(*pieces))
        )
        store_packed(rank, mate_ref, keep_ref, part, k, step, low)
        return carry

    lax.fori_loop(0, side, temporal, 0, unroll=True)
    for copy in [pad_copy] + late:
        copy.wait()


def conv_forward(rank, g, kt, lt, vec, before, after, side, pixels, ch, deps=()):
    hc = lt.shape[0] // 3
    plane = pixels // side
    nf = plane // side
    n = len(g)
    shapes = [
        ((side + 2, plane + 2 * nf, ch), BF),
        ((pixels, hc), BF),
        ((side, plane, hc), F32),
    ]
    outs = [jax.ShapeDtypeStruct(*s) for s in shapes] + [
        jax.ShapeDtypeStruct((1, hc), F32),
        jax.ShapeDtypeStruct((4, pixels // 2, 128), BF),
        jax.ShapeDtypeStruct((4, pixels // 2, 128), BF),
    ]
    scratch = [pltpu.VMEM(*s) for s in shapes] + [
        pltpu.VMEM((side, plane, hc), F32),
        pltpu.VMEM((hc, 9 * ch), BF),
        pltpu.VMEM((3 * hc, ch), BF),
        pltpu.VMEM((9, ch, hc), BF),
        pltpu.SemaphoreType.DMA((kt.shape[0] + 4,)),
    ]
    flops = 2 * pixels * hc * 12 * ch
    return call(functools.partial(conv_body, side, n == 1), outs, scratch, flops,
                rank, *g, kt, lt, vec, before, after,
                deps=deps, far=(n + 1, n + 2), far_outs=(0, 1, 2))


def fold(v):
    return v + pltpu.roll(v, 64, 1)


def total_of(refs):
    t = refs[0][...].astype(F32)
    for ref in refs[1:]:
        t += ref[...].astype(F32)
    return t


def pair_sum_body(keep_ref, mate_ref, *out_refs):
    for p, ref in enumerate(out_refs):
        ref[...] = (keep_ref[p].astype(F32) + mate_ref[p].astype(F32)).astype(ref.dtype)


def pair_sum(keep, arrived):
    shape = keep.shape[1:]
    outs = [jax.ShapeDtypeStruct(shape, BF)] * keep.shape[0]
    return call(pair_sum_body, outs, [], keep.size, keep, arrived)


def out_norm_body(n, has_skip, *refs):
    parts, refs = refs[:n], refs[n:]
    if has_skip:
        vec_ref, skip_ref, xhat_ref, rs_ref, pre_ref, res_ref = refs
    else:
        vec_ref, xhat_ref, rs_ref, pre_ref, res_ref = refs
    t = total_of(parts)
    pixels = 2 * t.shape[0]
    mean = fold(jnp.sum(t, axis=0, keepdims=True)) / pixels
    cen = t - mean
    rs = lax.rsqrt(fold(jnp.sum(cen * cen, axis=0, keepdims=True)) / pixels + eps)
    xhat = cen * rs
    pre = xhat * vec_ref[0:1, :] + vec_ref[1:2, :]
    if has_skip:
        pre = pre + skip_ref[...].astype(F32)
    xhat_ref[...] = xhat
    rs_ref[...] = rs
    pre_ref[...] = pre
    res_ref[...] = (pre * jax.nn.sigmoid(pre)).astype(BF)


def out_norm(parts, vec, skip):
    half = parts[0].shape[0]
    outs = [
        jax.ShapeDtypeStruct((half, 128), F32),
        jax.ShapeDtypeStruct((1, 128), F32),
        jax.ShapeDtypeStruct((half, 128), F32),
        jax.ShapeDtypeStruct((half, 128), BF),
    ]
    args = (*parts, vec) + (() if skip is None else (skip,))
    body = functools.partial(out_norm_body, len(parts), skip is not None)
    return call(body, outs, [], half * 128 * 10, *args)


def out_back_body(n, *refs):
    parts, (pre_ref, xhat_ref, rs_ref, vec_ref, dpre_ref, dt_ref, sums_ref) = refs[:n], refs[n:]
    g = total_of(parts)
    pre, xhat = pre_ref[...], xhat_ref[...]
    sig = jax.nn.sigmoid(pre)
    dpre = g * (sig * (1.0 + pre * (1.0 - sig)))
    pixels = 2 * pre.shape[0]
    sb = fold(jnp.sum(dpre, axis=0, keepdims=True))
    sg = fold(jnp.sum(dpre * xhat, axis=0, keepdims=True))
    dpre_ref[...] = dpre.astype(BF)
    scale = vec_ref[0:1, :] * rs_ref[...]
    dt_ref[...] = (scale * (dpre - sb / pixels - xhat * (sg / pixels))).astype(BF)
    sums_ref[0:1, :] = sg
    sums_ref[1:2, :] = sb


def out_back(parts, pre, xhat, rs, vec, deps=()):
    half = pre.shape[0]
    outs = [
        jax.ShapeDtypeStruct((half, 128), BF),
        jax.ShapeDtypeStruct((half, 128), BF),
        jax.ShapeDtypeStruct((2, 128), F32),
    ]
    args = (*parts, pre, xhat, rs, vec)
    return call(functools.partial(out_back_body, len(parts)), outs, [], half * 1280, *args, deps=deps)


def conv_back_body(side, rank_ref, *refs):
    slices, (xhat_in, rs_ref, kt_ref, lt_ref, vec_ref, before_ref, after_ref,
             dt_out, ds_out, sums_ref, mate_ref, keep_ref,
             dt_ref, ds_ref, xhat_ref, dy_ref, pad_ref, ktm_ref, ltm_ref, lnt_ref, sems) = (
        refs[:8], refs[8:])
    half = slices[0].shape[0]
    rank = rank_ref[0]
    nz = kt_ref.shape[0]
    rows = 2 * half
    plane = rows // side
    nf = plane // side
    step = plane // 2
    hc = ds_ref.shape[1]
    ch = dt_ref.shape[1]
    fetched = fetch_kernels(kt_ref, lt_ref, ktm_ref, ltm_ref, sems)
    xhat_copy = pltpu.make_async_copy(xhat_in, xhat_ref, sems.at[nz + 1])
    xhat_copy.start()
    clear_borders(pad_ref, side, plane, nf)

    def place(k, carry):
        for q, odd, a_ref, b_ref in by_rank(slices, rank):
            top, bottom = halves(odd, a_ref[chunk(k, step), :], b_ref[chunk(k, step), :])
            lanes = pl.ds(pl.multiple_of(128 * q, 128), 128)
            dt_ref[chunk(k, step), lanes] = top.astype(BF)
            dt_ref[pl.ds(pl.multiple_of(half + k * step, 16), step), lanes] = bottom.astype(BF)
        return carry

    lax.fori_loop(0, side, place, 0, unroll=True)
    dt_copy = pltpu.make_async_copy(dt_ref, dt_out, sems.at[nz + 2])
    dt_copy.start()
    for copy in fetched + [xhat_copy]:
        copy.wait()
    for t in range(3):
        lnt_ref[t] = ltm_ref[t * hc : (t + 1) * hc].astype(F32).T.astype(BF)
    gain, bias = vec_ref[0:1, :], vec_ref[1:2, :]

    def hidden_grad(i, sums):
        dt = dt_ref[chunk(i, plane), :]
        early = nn(dt, lnt_ref[0]) * before_ref[0:plane, :]
        late = nn(dt, lnt_ref[2]) * after_ref[0:plane, :]
        dh = nn(dt, lnt_ref[1]) + pltpu.roll(early, plane - 1, 0) + pltpu.roll(late, 1, 0)
        xhat = xhat_ref[i]
        v = xhat * gain + bias
        sig = jax.nn.sigmoid(v)
        dy = dh * (sig * (1.0 + v * (1.0 - sig)))
        dy_ref[i] = dy
        return (
            sums[0] + jnp.sum(dy * xhat, axis=0, keepdims=True),
            sums[1] + jnp.sum(dy, axis=0, keepdims=True),
        )

    zero = jnp.zeros((1, hc), F32)
    sg, sb = lax.fori_loop(0, side, hidden_grad, (zero, zero), unroll=True)
    sums_ref[0:1, :] = sg
    sums_ref[1:2, :] = sb
    scale = gain * rs_ref[...]

    def spatial_grad(i, carry):
        ds = (scale * (dy_ref[i] - sb / rows - xhat_ref[i] * (sg / rows))).astype(BF)
        pad_ref[i + 1, nf : nf + plane] = ds
        ds_ref[chunk(i, plane), :] = ds
        return carry

    lax.fori_loop(0, side, spatial_grad, 0, unroll=True)
    ds_copy = pltpu.make_async_copy(ds_ref, ds_out, sems.at[nz + 3])
    ds_copy.start()
    low = lax.broadcasted_iota(jnp.int32, (step, 128), 1) < 64

    def back(k, carry):
        acc = jnp.zeros((2 * step, ch), F32)
        for t in range(9):
            r, c = 2 - t // 3, 2 - t % 3
            pieces = []
            for kk in (k, k + side):
                at = c * nf + lax.rem(kk, 2) * step
                pieces.append(pad_ref[kk // 2 + r, pl.ds(pl.multiple_of(at, 16), step), :])
            acc += nn(jnp.concatenate(pieces, axis=0), ktm_ref[:, t * ch : (t + 1) * ch])
        store_packed(rank, mate_ref, keep_ref, acc, k, step, low)
        return carry

    lax.fori_loop(0, side, back, 0, unroll=True)
    dt_copy.wait()
    ds_copy.wait()


def conv_back(rank, g, xhat, rs, kt, lt, vec, before, after, side, deps=()):
    half = g[0].shape[0]
    hc = lt.shape[0] // 3
    ch = lt.shape[1]
    pixels = 2 * half
    plane = pixels // side
    nf = plane // side
    outs = [
        jax.ShapeDtypeStruct((pixels, ch), BF),
        jax.ShapeDtypeStruct((pixels, hc), BF),
        jax.ShapeDtypeStruct((2, hc), F32),
        jax.ShapeDtypeStruct((4, half, 128), BF),
        jax.ShapeDtypeStruct((4, half, 128), BF),
    ]
    scratch = [
        pltpu.VMEM((pixels, ch), BF),
        pltpu.VMEM((pixels, hc), BF),
        pltpu.VMEM((side, plane, hc), F32),
        pltpu.VMEM((side, plane, hc), F32),
        pltpu.VMEM((side + 2, plane + 2 * nf, hc), BF),
        pltpu.VMEM((hc, 9 * ch), BF),
        pltpu.VMEM((3 * hc, ch), BF),
        pltpu.VMEM((3, ch, hc), BF),
        pltpu.SemaphoreType.DMA((kt.shape[0] + 4,)),
    ]
    flops = 2 * pixels * hc * 12 * ch
    return call(functools.partial(conv_back_body, side), outs, scratch, flops,
                rank, *g, xhat, rs, kt, lt, vec, before, after,
                deps=deps, far=(9, 11, 12), far_outs=(0, 1))


def grads_body(side, pad_ref, hid_ref, ds_ref, dt_ref, before_ref, after_ref, sg_ref, tg_ref,
               dst_ref, taps_ref):
    ch = pad_ref.shape[2]
    hc = hid_ref.shape[1]
    plane = hid_ref.shape[0] // side
    nf = plane // side
    for i in (0, 1, side + 2, side + 3):
        dst_ref[i] = jnp.zeros(dst_ref.shape[1:], BF)
    for i in range(side):
        at = slice(i * plane, (i + 1) * plane)
        h = hid_ref[at, :].astype(F32)
        taps_ref[i, 0:hc] = (pltpu.roll(h, 1, 0) * before_ref[0:plane, :]).T.astype(BF)
        taps_ref[i, hc : 2 * hc] = h.T.astype(BF)
        taps_ref[i, 2 * hc : 3 * hc] = (pltpu.roll(h, plane - 1, 0) * after_ref[0:plane, :]).T.astype(BF)
        dst_ref[i + 2] = ds_ref[at, :].astype(F32).T.astype(BF)
    tg_ref[...] = sum(
        nn(taps_ref[i], dt_ref[i * plane : (i + 1) * plane, :]) for i in range(side)
    ).astype(BF)
    width = sg_ref.shape[2]
    for c in range(3):
        acc = sum(
            nn(dst_ref[i : i + 3].reshape(3 * hc, plane), pad_ref[i, c * nf : c * nf + plane, :])
            for i in range(1, side + 1)
        )
        for r in range(3):
            first = (3 * r + c) * ch
            end = first + ch
            at = (2 - r) * hc
            done = 0
            while first < end:
                z = first // width
                last = min(end, (z + 1) * width)
                sg_ref[z, :, first - z * width : last - z * width] = (
                    acc[at : at + hc, done : done + last - first].astype(BF)
                )
                done += last - first
                first = last


def kernel_grads(pad, hidden, ds, dt, before, after, side, nz, deps=()):
    pixels, hc = hidden.shape
    ch = dt.shape[1]
    plane = pixels // side
    outs = [
        jax.ShapeDtypeStruct((nz, hc, 9 * ch // nz), BF),
        jax.ShapeDtypeStruct((3 * hc, ch), BF),
    ]
    scratch = [
        pltpu.VMEM((side + 4, hc, plane), BF),
        pltpu.VMEM((side, 3 * hc, plane), BF),
    ]
    flops = 2 * pixels * hc * 12 * ch
    return call(functools.partial(grads_body, side), outs, scratch, flops,
                pad, hidden, ds, dt, before, after, deps=deps)


def copy_after_body(v_ref, out_ref):
    out_ref[...] = v_ref[...]


def after_all(v, *deps):
    return call(copy_after_body, [jax.ShapeDtypeStruct(v.shape, v.dtype)], [], v.size, v, deps=deps)[0]


def hop(v, k):
    n = 1
    for name in EVERY:
        n *= lax.axis_size(name)
    return lax.ppermute(v, EVERY, [(i, i ^ k) for i in range(n)])


def plane_gather(v):
    got = {0: v}
    for k in (6, 2, 4, 1):
        got[k] = hop(v, k)
    for k in (2, 4, 6):
        got[k ^ 1] = hop(got[k], 1)
    return [got[k] for k in range(8)]


def z_gather(v, n_rank, nz):
    v = jnp.stack([v] + [hop(v, n_rank * k) for k in range(1, nz)])
    z = lax.axis_index("z")
    bit = 1
    while bit < nz:
        pairs = v.reshape(nz // (2 * bit), 2, bit, *v.shape[1:])
        v = jnp.where(lax.bitwise_and(z, bit) > 0, pairs[:, ::-1], pairs).reshape(v.shape)
        bit *= 2
    return v


def z_reduce(v, n_rank, nz):
    z = lax.axis_index("z")
    total = lax.dynamic_index_in_dim(v, z, 0, keepdims=False).astype(F32)
    for k in range(1, nz):
        piece = lax.dynamic_index_in_dim(v, lax.bitwise_xor(z, k), 0, keepdims=False)
        total = total + hop(piece, n_rank * k).astype(F32)
    return total.astype(v.dtype)


def plane_reduce(mate, keep):
    sums = pair_sum(keep, hop(mate, 1))
    arrived = {k: hop(sums[k // 2], k) for k in (6, 2, 4)}
    return [sums[0], arrived[2], arrived[4], arrived[6]]


def to_section(v, section, n_seg):
    y = lax.axis_index("y")
    near = lax.dynamic_index_in_dim(v, y, 0, keepdims=False)
    far = lax.dynamic_index_in_dim(v, 1 - y, 0, keepdims=False)
    n = 2 * n_seg * lax.axis_size("z")
    got = []
    for base, block in ((0, near), (n_seg, far)):
        row = []
        for low in range(n_seg):
            k = base + (low ^ section)
            if k == 0:
                row.append(block)
            else:
                pairs = [(i, i ^ k) for i in range(n) if i % n_seg == low]
                row.append(lax.ppermute(block, EVERY, pairs))
        got.append(jnp.stack(row))
    same, other = got
    return jnp.where(y == 0, jnp.concatenate([same, other]), jnp.concatenate([other, same]))

def on_device(frames, cot, starts, ks, ktm, mg, mb, og, ob):
    nz, n_rank, n_seg = lax.axis_size("z"), 8, 4
    n_dp = nz * 2
    fr, side, ch = frames.shape[0], frames.shape[1], frames.shape[3]
    area = side * side
    hid = ks.shape[2]
    hc, cc = hid // n_rank, ch // n_rank
    q = hc // n_rank
    rank = lax.axis_index(PLANE)
    rank_now = rank.astype(jnp.int32).reshape(1)
    d_index = lax.axis_index(("z", "y"))
    nf = n_dp * fr
    pixels = area * nf
    half = pixels // 2

    to_plane = [(d * n_seg + s, s * n_rank + d) for d in range(n_dp) for s in range(n_seg)]
    from_plane = [(b, a) for a, b in to_plane]
    rows = fr * area
    flag_row = jnp.pad(starts.astype(BF)[None], ((0, 11), (0, ch - fr)))
    moving = jnp.concatenate([frames.reshape(rows, ch), flag_row], axis=0)
    moving = lax.ppermute(moving, EVERY, to_plane)

    perm = (jnp.arange(hid).reshape(n_rank, n_rank, q).transpose(1, 0, 2).reshape(hid)[:, None]
            == jnp.arange(hid)[None, :]).astype(BF)
    kt = lax.dot_general(perm, ks[0].astype(BF), (((1,), (1,)), ((), ())),
                         preferred_element_type=F32).astype(BF)
    kt = kt.reshape(n_rank, hc, ks.shape[1])
    kt = lax.all_to_all(kt, PLANE, 0, 0)
    kt_here = kt
    kt = kt.reshape(2, n_seg, hc, ks.shape[1]).transpose(1, 2, 0, 3).reshape(n_seg, hc, -1)
    lrows = ktm.shape[1] // n_rank
    lt = ktm[0].astype(BF).reshape(-1, n_rank, q, ch).transpose(1, 0, 2, 3).reshape(n_rank, lrows, ch)
    extra = jnp.concatenate([v.astype(BF) for v in (mg, mb, og, ob)], axis=1)
    extra = jnp.pad(extra, ((0, 1), (0, ch - extra.shape[1])))
    lt = jnp.concatenate([lt, jnp.broadcast_to(extra, (n_rank, 2, ch))], axis=1)
    lt = lax.all_to_all(after_all(lt, kt_here), PLANE, 0, 0)
    moving = after_all(moving, lt)
    gathered = lax.all_to_all(jnp.broadcast_to(moving, (n_rank, *moving.shape)), PLANE, 0, 0)
    lt = lt.reshape(2, n_seg, lrows + 2, ch).transpose(1, 0, 2, 3).reshape(n_seg, 2 * (lrows + 2), ch)
    kts = [lax.all_gather(kt[s], "z", axis=0) for s in range(n_seg)]
    lt_first = z_gather(lt[0], n_rank, nz)[:, None]
    lt_rest = lax.all_gather(lt[1:], "z", axis=0)
    lts, mids, outs = [], [], []
    for s in range(n_seg):
        full = lt_first[:, 0] if s == 0 else lt_rest[:, s - 1]
        full = full.reshape(n_dp, lrows + 2, ch)
        lts.append(full[:, :lrows].reshape(3 * hc, ch))
        row = full[:, lrows].astype(F32)
        mids.append(jnp.stack([
            lax.dynamic_slice_in_dim(row[:, i * hc : (i + 1) * hc], rank * q, q, axis=1).reshape(hc)
            for i in range(2)]))
        own = lax.dynamic_index_in_dim(row, rank, 0, keepdims=False)
        outs.append(jnp.stack([
            jnp.tile(own[2 * hc + i * cc : 2 * hc + (i + 1) * cc], 2) for i in range(2)]))

    def by_pixel(v):
        width = v.shape[2]
        v = v.reshape(n_rank * fr, area, width).transpose(1, 0, 2)
        return v.reshape(pixels, width)

    def packed(v):
        return jnp.concatenate([v[:half], v[half:]], axis=1)

    a0 = by_pixel(gathered[:, :rows])
    flags = gathered[:, rows, :fr].reshape(nf) > 0.5
    slot = jnp.arange(nf) % fr
    before = jnp.where(flags | (slot == 0), 0.0, 1.0)
    after = jnp.where(jnp.roll(flags, -1) | (slot == fr - 1), 0.0, 1.0)
    spread = (side * nf + nf, hc)
    before = jnp.broadcast_to(jnp.tile(before, side + 1)[:, None], spread)
    after = jnp.broadcast_to(jnp.tile(after, side + 1)[:, None], spread)
    skip = packed(lax.dynamic_slice_in_dim(a0, rank * cc, cc, axis=1))

    cot_moving = lax.ppermute(cot.reshape(rows, ch), EVERY, to_plane)
    cot_moving = cot_moving.reshape(rows, n_rank, cc).transpose(1, 0, 2)
    cot_own = packed(by_pixel(lax.all_to_all(after_all(cot_moving, gathered), PLANE, 0, 0)))

    def to_frames(v):
        v = jnp.concatenate([v[:, :cc], v[:, cc:]], axis=0)
        v = v.reshape(area, n_rank, fr, cc).transpose(1, 0, 2, 3).reshape(n_rank, rows, cc)
        v = lax.all_to_all(v, PLANE, 0, 0).transpose(1, 0, 2).reshape(area, fr, ch)
        return lax.ppermute(v, EVERY, from_plane).transpose(1, 0, 2).reshape(frames.shape)

    saved = []
    g = [a0]
    for s in range(n_seg):
        pad, hidden, xm, rm, mate, keep = conv_forward(
            rank_now, g, kts[s], lts[s], mids[s], before, after, side, pixels, ch,
            deps=(cot_own,) if s == 0 else ())
        parts = plane_reduce(mate, keep)
        xo, ro, pre, res = out_norm(parts, outs[s], skip if s % 2 == 1 else None)
        saved.append((pad, hidden, xm, rm, xo, ro, pre))
        if s % 2 == 1:
            skip = res
        if s < n_seg - 1:
            g = plane_gather(res)
    output = to_frames(res)

    parts = [cot_own]
    skip_grad = None
    sgrads, tgrads, raw = [], [], ()
    for s in reversed(range(n_seg)):
        pad, hidden, xm, rm, xo, ro, pre = saved[s]
        if s == 1:
            parts = parts + [skip_grad]
        dpre, dt, osum = out_back(parts, pre, xo, ro, outs[s], deps=raw)
        if s % 2 == 1:
            skip_grad = dpre
        dtf, ds, msum, mate, keep = conv_back(
            rank_now, plane_gather(dt), xm, rm, kts[s], lts[s], mids[s], before, after, side,
            deps=(sgrads[-2], tgrads[-2]) if len(sgrads) > 1 else (output,) * len(sgrads))
        if s > 0:
            parts = plane_reduce(mate, keep)
        sg, tg = kernel_grads(pad, hidden, ds, dtf, before, after, side, nz,
                              deps=parts[:1] if s > 0 else ())
        if s == 0:
            parts = plane_reduce(mate, keep)
        row = jnp.concatenate([msum[0], msum[1], osum[0, :cc], osum[1, :cc]]).astype(BF)
        row = jnp.pad(row[None], ((0, 1), (0, ch - row.shape[0])))
        tg = jnp.concatenate(
            [tg.reshape(n_dp, lrows, ch), jnp.broadcast_to(row, (n_dp, 2, ch))], axis=1)
        sgrads.append(lax.psum_scatter(sg, "z", scatter_dimension=0))
        raw = (sg,)
        tg = tg.reshape(nz, -1, ch)
        if s > 0:
            tgrads.append(lax.psum_scatter(tg, "z", scatter_dimension=0))
        else:
            tgrads.append(z_reduce(tg, n_rank, nz))

    da = sum(p.astype(F32) for p in parts) + skip_grad.astype(F32)
    frames_grad = to_frames(da.astype(BF)).astype(F32)

    tg = jnp.stack(tgrads[::-1])
    last = to_section(sgrads[-1].reshape(hc, 2, -1).transpose(1, 0, 2), 0, n_seg)
    sg = jnp.stack([jnp.zeros_like(sgrads[0])] + sgrads[2::-1])
    sg = sg.reshape(n_seg, hc, 2, -1).transpose(2, 0, 1, 3).reshape(n_rank, hc, -1)
    sg = lax.all_to_all(sg, PLANE, 0, 0)
    sg = jnp.where(lax.axis_index(("x", "c")) == 0, last, sg).reshape(hid, -1)
    space_grad = lax.dot_general(sg, perm, (((0,), (0,)), ((), ())), preferred_element_type=F32)
    tg = tg.reshape(n_seg, 2, lrows + 2, ch).transpose(1, 0, 2, 3).reshape(n_rank, lrows + 2, ch)
    tg = lax.all_to_all(tg, PLANE, 0, 0)
    row = tg[:, lrows].astype(F32)
    tg = tg[:, :lrows].reshape(n_rank, -1, q, ch)
    time_grad = tg.transpose(1, 0, 2, 3).reshape(-1, ch).astype(F32)
    own = lax.dynamic_index_in_dim(row, d_index, 0, keepdims=True)
    return (
        output,
        frames_grad,
        space_grad[None],
        time_grad[None],
        lax.dynamic_slice_in_dim(row[:, :hc], d_index * q, q, axis=1).reshape(1, hc),
        lax.dynamic_slice_in_dim(row[:, hc : 2 * hc], d_index * q, q, axis=1).reshape(1, hc),
        own[:, 2 * hc : 2 * hc + cc],
        own[:, 2 * hc + cc : 2 * hc + 2 * cc],
    )


def from_behind(value, axis, steps):
    count = lax.axis_size(axis)
    leading, last = (max(0, -steps), min(count, count - steps))
    return lax.ppermute(value, axis, [(source, source + steps) for source in range(leading, last)])


def space_apply(current, kernel):
    frame_side = current.shape[1]
    padded = jnp.pad(current, ((0, 0), (1, 1), (1, 1), (0, 0)))
    stacked = jnp.concatenate(
        [
            padded[:, row_shift : row_shift + frame_side, col_shift : col_shift + frame_side, :]
            for row_shift in range(3)
            for col_shift in range(3)
        ],
        axis=-1,
    )
    return (
        stacked,
        jnp.einsum("fijc,co->fijo", stacked, kernel, preferred_element_type=jnp.float32),
    )


def space_back(gradient, kernel):
    frame_side = gradient.shape[1]
    channels = kernel.shape[0] // 9
    spread = jnp.einsum("fijo,co->fijc", gradient, kernel, preferred_element_type=jnp.float32)
    total = jnp.zeros((gradient.shape[0], frame_side + 2, frame_side + 2, channels), jnp.float32)
    for tap_index in range(9):
        row_shift = tap_index // 3
        col_shift = tap_index % 3
        piece_now = spread[..., tap_index * channels : (tap_index + 1) * channels]
        total = total + jnp.pad(
            piece_now, ((0, 0), (row_shift, 2 - row_shift), (col_shift, 2 - col_shift), (0, 0))
        )
    return total[:, 1 : frame_side + 1, 1 : frame_side + 1, :]


def time_apply(current, kernel, before_mask, after_mask):
    blanks = jnp.zeros_like(current[:1])
    earlier = jnp.concatenate([blanks, current[:-1]], axis=0) * before_mask[
        :, None, None, None
    ].astype(current.dtype)
    later = jnp.concatenate([current[1:], blanks], axis=0) * after_mask[:, None, None, None].astype(
        current.dtype
    )
    stacked = jnp.concatenate([earlier, current, later], axis=-1)
    return (
        stacked,
        jnp.einsum("fijc,co->fijo", stacked, kernel, preferred_element_type=jnp.float32),
    )


def time_back(gradient, kernel, before_mask, after_mask):
    channels = kernel.shape[0] // 3
    spread = jnp.einsum("fijo,co->fijc", gradient, kernel, preferred_element_type=jnp.float32)
    early_part = spread[..., :channels] * before_mask[:, None, None, None]
    late_part = spread[..., 2 * channels :] * after_mask[:, None, None, None]
    blanks = jnp.zeros_like(early_part[:1])
    moved_early = jnp.concatenate([early_part[1:], blanks], axis=0)
    moved_late = jnp.concatenate([blanks, late_part[:-1]], axis=0)
    return spread[..., channels : 2 * channels] + moved_early + moved_late


def moments(values, pixel_count):
    average = lax.psum(jnp.sum(values, axis=(0, 1, 2)), "dp") / pixel_count
    centered = values - average
    spread = lax.psum(jnp.sum(centered * centered, axis=(0, 1, 2)), "dp") / pixel_count
    return (average, lax.rsqrt(spread + eps))


def reduce_back(gradient, normed):
    return lax.psum(
        (jnp.sum(gradient, axis=(0, 1, 2)), jnp.sum(gradient * normed, axis=(0, 1, 2))), "dp"
    )


def silu_slope(values):
    sigmoid_now = jax.nn.sigmoid(values)
    return sigmoid_now * (1.0 + values * (1.0 - sigmoid_now))


def pick_slot(stack, slot_index):
    return lax.dynamic_index_in_dim(stack, slot_index, 0, keepdims=False)


def store_slot(stack, value, slot_index, usable):
    previous = pick_slot(stack, slot_index)
    return lax.dynamic_update_index_in_dim(stack, jnp.where(usable, value, previous), slot_index, 0)


def on_device_general(
    frames, cotangent, starts, space_kernel, time_kernel, mid_gain, mid_bias, out_gain, out_bias
):
    n_segment = lax.axis_size("segment")
    n_data = lax.axis_size("dp")
    segment_index = lax.axis_index("segment")
    odd_segment = segment_index % 2 == 1
    last_segment = segment_index == n_segment - 1
    first_segment = segment_index == 0
    frame_count = frames.shape[0]
    frame_side = frames.shape[1]
    channels = frames.shape[3]
    hidden_units = mid_gain.shape[1] * n_data
    pixel_count = n_data * frame_count * frame_side * frame_side
    turns = 2 * n_segment - 1
    block_shape = (n_segment,) + frames.shape
    all_frames, all_cot, all_starts = (
        lax.all_gather(frames, "segment", axis=0, tiled=True),
        lax.all_gather(cotangent, "segment", axis=0, tiled=True),
        lax.all_gather(starts.astype(jnp.bfloat16), "segment", axis=0, tiled=True),
    )
    frame_stack = all_frames.reshape(block_shape)
    cot_stack = all_cot.reshape(block_shape)
    clip_flags = all_starts.astype(jnp.float32).reshape(n_segment, frame_count)
    positions = jnp.arange(frame_count)
    before_mask = jnp.where((clip_flags > 0.5) | (positions == 0), 0.0, 1.0)
    following = jnp.concatenate([clip_flags[:, 1:], jnp.ones((n_segment, 1), jnp.float32)], axis=1)
    after_mask = jnp.where(following > 0.5, 0.0, 1.0)
    gathered = (
        lax.all_gather(space_kernel[0].astype(jnp.bfloat16), "dp", axis=0, tiled=True),
        lax.all_gather(time_kernel[0].astype(jnp.bfloat16), "dp", axis=0, tiled=True),
        lax.all_gather(mid_gain[0].astype(jnp.bfloat16), "dp", axis=0, tiled=True),
        lax.all_gather(mid_bias[0].astype(jnp.bfloat16), "dp", axis=0, tiled=True),
        lax.all_gather(out_gain[0].astype(jnp.bfloat16), "dp", axis=0, tiled=True),
        lax.all_gather(out_bias[0].astype(jnp.bfloat16), "dp", axis=0, tiled=True),
    )
    space_low, time_low = (gathered[0], gathered[1])
    mid_gain_now = gathered[2].astype(jnp.float32)
    mid_bias_now = gathered[3].astype(jnp.float32)
    out_gain_now = gathered[4].astype(jnp.float32)
    out_bias_now = gathered[5].astype(jnp.float32)
    incoming = jnp.zeros_like(frames)
    carried = jnp.zeros_like(frames)
    kept_input = jnp.zeros(block_shape, jnp.bfloat16)
    kept_skip = jnp.zeros(block_shape, jnp.bfloat16)
    kept_mid_mean = jnp.zeros((n_segment, hidden_units), jnp.float32)
    kept_mid_scale = jnp.zeros((n_segment, hidden_units), jnp.float32)
    kept_out_mean = jnp.zeros((n_segment, channels), jnp.float32)
    kept_out_scale = jnp.zeros((n_segment, channels), jnp.float32)
    results = jnp.zeros(block_shape, jnp.float32)
    for turn_index in range(turns):
        micro_index = turn_index - segment_index
        usable = (micro_index >= 0) & (micro_index < n_segment)
        slot_index = jnp.clip(micro_index, 0, n_segment - 1)
        current = jnp.where(first_segment, pick_slot(frame_stack, slot_index), incoming)
        skip_input = carried
        _, spatial = space_apply(current, space_low)
        mid_mean, mid_scale = moments(spatial, pixel_count)
        hidden_act = jax.nn.silu(
            (spatial - mid_mean) * mid_scale * mid_gain_now + mid_bias_now
        ).astype(jnp.bfloat16)
        _, temporal = time_apply(
            hidden_act,
            time_low,
            pick_slot(before_mask, slot_index),
            pick_slot(after_mask, slot_index),
        )
        out_mean, out_scale = moments(temporal, pixel_count)
        pre_act = (
            (temporal - out_mean) * out_scale * out_gain_now
            + out_bias_now
            + jnp.where(odd_segment, skip_input.astype(jnp.float32), 0.0)
        )
        result = jax.nn.silu(pre_act).astype(jnp.bfloat16)
        kept_input = store_slot(kept_input, current, slot_index, usable)
        kept_skip = store_slot(kept_skip, skip_input, slot_index, usable)
        kept_mid_mean = store_slot(kept_mid_mean, mid_mean, slot_index, usable)
        kept_mid_scale = store_slot(kept_mid_scale, mid_scale, slot_index, usable)
        kept_out_mean = store_slot(kept_out_mean, out_mean, slot_index, usable)
        kept_out_scale = store_slot(kept_out_scale, out_scale, slot_index, usable)
        results = store_slot(results, result.astype(jnp.float32), slot_index, usable)
        if turn_index < turns - 1:
            incoming, carried = from_behind(
                (result, jnp.where(odd_segment, result, current)), "segment", 1
            )
    gathered = (
        lax.all_gather(space_kernel[0].astype(jnp.bfloat16), "dp", axis=0, tiled=True),
        lax.all_gather(time_kernel[0].astype(jnp.bfloat16), "dp", axis=0, tiled=True),
        lax.all_gather(mid_gain[0].astype(jnp.bfloat16), "dp", axis=0, tiled=True),
        lax.all_gather(mid_bias[0].astype(jnp.bfloat16), "dp", axis=0, tiled=True),
        lax.all_gather(out_gain[0].astype(jnp.bfloat16), "dp", axis=0, tiled=True),
        lax.all_gather(out_bias[0].astype(jnp.bfloat16), "dp", axis=0, tiled=True),
    )
    space_low, time_low = (gathered[0], gathered[1])
    mid_gain_now = gathered[2].astype(jnp.float32)
    mid_bias_now = gathered[3].astype(jnp.float32)
    out_gain_now = gathered[4].astype(jnp.float32)
    out_bias_now = gathered[5].astype(jnp.float32)
    grad_input = jnp.zeros_like(frames)
    grad_skip = jnp.zeros_like(frames)
    space_acc = jnp.zeros(space_low.shape, jnp.float32)
    time_acc = jnp.zeros(time_low.shape, jnp.float32)
    mid_gain_acc = jnp.zeros((hidden_units,), jnp.float32)
    mid_bias_acc = jnp.zeros((hidden_units,), jnp.float32)
    out_gain_acc = jnp.zeros((channels,), jnp.float32)
    out_bias_acc = jnp.zeros((channels,), jnp.float32)
    input_grads = jnp.zeros(block_shape, jnp.float32)
    for turn_index in range(turns):
        micro_index = n_segment - 1 - (turn_index - (n_segment - 1 - segment_index))
        usable = (micro_index >= 0) & (micro_index < n_segment)
        usable_weight = usable.astype(jnp.float32)
        slot_index = jnp.clip(micro_index, 0, n_segment - 1)
        current = pick_slot(kept_input, slot_index)
        skip_input = pick_slot(kept_skip, slot_index)
        before_now = pick_slot(before_mask, slot_index)
        after_now = pick_slot(after_mask, slot_index)
        space_taps, spatial = space_apply(current, space_low)
        mid_normed = (spatial - pick_slot(kept_mid_mean, slot_index)) * pick_slot(
            kept_mid_scale, slot_index
        )
        mid_pre = mid_normed * mid_gain_now + mid_bias_now
        hidden_act = jax.nn.silu(mid_pre).astype(jnp.bfloat16)
        time_taps, temporal = time_apply(hidden_act, time_low, before_now, after_now)
        out_scale = pick_slot(kept_out_scale, slot_index)
        out_normed = (temporal - pick_slot(kept_out_mean, slot_index)) * out_scale
        pre_act = (
            out_normed * out_gain_now
            + out_bias_now
            + jnp.where(odd_segment, skip_input.astype(jnp.float32), 0.0)
        )
        grad_result = jnp.where(
            last_segment,
            pick_slot(cot_stack, slot_index).astype(jnp.float32),
            grad_input.astype(jnp.float32)
            + jnp.where(odd_segment, grad_skip.astype(jnp.float32), 0.0),
        )
        grad_pre = grad_result * silu_slope(pre_act)
        out_bias_sum, out_gain_sum = reduce_back(grad_pre, out_normed)
        grad_temporal = (
            out_gain_now
            * out_scale
            * (grad_pre - out_bias_sum / pixel_count - out_normed * out_gain_sum / pixel_count)
        ).astype(jnp.bfloat16)
        time_acc = time_acc + usable_weight * jnp.einsum(
            "fijc,fijo->co", time_taps, grad_temporal, preferred_element_type=jnp.float32
        )
        grad_hidden = time_back(grad_temporal, time_low, before_now, after_now)
        grad_mid = grad_hidden * silu_slope(mid_pre)
        mid_bias_sum, mid_gain_sum = reduce_back(grad_mid, mid_normed)
        mid_scale = pick_slot(kept_mid_scale, slot_index)
        grad_spatial = (
            mid_gain_now
            * mid_scale
            * (grad_mid - mid_bias_sum / pixel_count - mid_normed * mid_gain_sum / pixel_count)
        ).astype(jnp.bfloat16)
        space_acc = space_acc + usable_weight * jnp.einsum(
            "fijc,fijo->co", space_taps, grad_spatial, preferred_element_type=jnp.float32
        )
        grad_current = space_back(grad_spatial, space_low)
        mid_gain_acc = mid_gain_acc + usable_weight * mid_gain_sum
        mid_bias_acc = mid_bias_acc + usable_weight * mid_bias_sum
        out_gain_acc = out_gain_acc + usable_weight * out_gain_sum
        out_bias_acc = out_bias_acc + usable_weight * out_bias_sum
        input_grads = store_slot(
            input_grads, grad_current + grad_skip.astype(jnp.float32), slot_index, usable
        )
        if turn_index < turns - 1:
            grad_input, grad_skip = from_behind(
                (
                    grad_current.astype(jnp.bfloat16),
                    jnp.where(odd_segment, grad_pre.astype(jnp.bfloat16), grad_skip),
                ),
                "segment",
                -1,
            )
    space_grad, time_grad = (
        lax.psum_scatter(space_acc, "dp", scatter_dimension=0, tiled=True),
        lax.psum_scatter(time_acc, "dp", scatter_dimension=0, tiled=True),
    )
    data_index = lax.axis_index("dp")

    def own_share(full_vector):
        share = full_vector.shape[0] // n_data
        return lax.dynamic_slice_in_dim(full_vector, data_index * share, share)[None]

    flat_shape = (n_segment * frame_count,) + frames.shape[1:]
    arrived_out, arrived_grads = (
        lax.all_to_all(
            results.reshape(flat_shape).astype(jnp.bfloat16),
            "segment",
            split_axis=0,
            concat_axis=0,
            tiled=True,
        ).astype(jnp.float32),
        lax.all_to_all(
            input_grads.reshape(flat_shape).astype(jnp.bfloat16),
            "segment",
            split_axis=0,
            concat_axis=0,
            tiled=True,
        ).astype(jnp.float32),
    )
    output = arrived_out[(n_segment - 1) * frame_count :].astype(jnp.bfloat16)
    frames_grad = arrived_grads[:frame_count]
    return (
        output,
        frames_grad,
        space_grad[None],
        time_grad[None],
        own_share(mid_gain_acc),
        own_share(mid_bias_acc),
        own_share(out_gain_acc),
        own_share(out_bias_acc),
    )


def general(mesh):
    return jax.shard_map(
        on_device_general,
        mesh=mesh,
        in_specs=(
            P(("dp", "segment"), None, None, None),
            P(("dp", "segment"), None, None, None),
            P(("dp", "segment")),
            P("segment", "dp", None),
            P("segment", "dp", None),
            P("segment", "dp"),
            P("segment", "dp"),
            P("segment", "dp"),
            P("segment", "dp"),
        ),
        out_specs=(
            P(("dp", "segment"), None, None, None),
            P(("dp", "segment"), None, None, None),
            P("segment", "dp", None),
            P("segment", "dp", None),
            P("segment", "dp"),
            P("segment", "dp"),
            P("segment", "dp"),
            P("segment", "dp"),
        ),
        check_vma=False,
    )


def solution(mesh):
    if mesh.shape["dp"] != 8 or mesh.shape["segment"] != 4:
        return general(mesh)
    n_dp, n_seg = mesh.shape["dp"], mesh.shape["segment"]
    fine = Mesh(mesh.devices.reshape(n_dp // 2, 2, 2, n_seg // 2), EVERY)
    dp, seg = ("z", "y"), ("x", "c")
    return jax.shard_map(
        on_device,
        mesh=fine,
        in_specs=(
            P(EVERY, None, None, None),
            P(EVERY, None, None, None),
            P(EVERY),
            P(seg, dp, None),
            P(seg, dp, None),
            P(seg, dp),
            P(seg, dp),
            P(seg, dp),
            P(seg, dp),
        ),
        out_specs=(
            P(EVERY, None, None, None),
            P(EVERY, None, None, None),
            P(seg, dp, None),
            P(seg, dp, None),
            P(seg, dp),
            P(seg, dp),
            P(seg, dp),
            P(seg, dp),
        ),
        check_vma=False,
    )
```

```python
import functools

import jax
import jax.numpy as jnp
from jax import lax
from jax.experimental import pallas as pl
from jax.experimental.pallas import tpu as pltpu
from jax.sharding import Mesh, PartitionSpec as P

eps = 1e-05
PLANE = ("y", "x", "c")
EVERY = ("z", "y", "x", "c")
BF = jnp.bfloat16
F32 = jnp.float32


def nt(a, b):
    return lax.dot_general(a, b, (((1,), (1,)), ((), ())), preferred_element_type=F32)


def nn(a, b):
    return lax.dot_general(a, b, (((1,), (0,)), ((), ())), preferred_element_type=F32)


VMEM_CAP = 56 * 1024 * 1024
ANY = pl.BlockSpec(memory_space=pl.ANY)


def call(body, outs, scratch, flops, *args, deps=(), far=(), far_outs=()):
    moved = sum(a.size * a.dtype.itemsize for a in args) + sum(
        o.size * o.dtype.itemsize for o in outs
    )
    n = len(deps)

    def spec(a):
        return pl.BlockSpec(memory_space=pltpu.SMEM if a.dtype == jnp.int32 else pltpu.VMEM)

    return pl.pallas_call(
        lambda *refs: body(*refs[n:]),
        out_shape=outs,
        in_specs=[ANY] * n + [ANY if i in far else spec(a) for i, a in enumerate(args)],
        out_specs=[ANY if i in far_outs else spec(o) for i, o in enumerate(outs)],
        scratch_shapes=scratch,
        compiler_params=pltpu.CompilerParams(vmem_limit_bytes=VMEM_CAP),
        cost_estimate=pl.CostEstimate(flops=flops, bytes_accessed=moved, transcendentals=0),
    )(*deps, *args)


def chunk(i, size):
    return pl.ds(pl.multiple_of(i * size, 16), size)


def clear_borders(pad_ref, side, plane, nf):
    zrow = jnp.zeros(pad_ref.shape[1:], BF)
    pad_ref[0] = zrow
    pad_ref[side + 1] = zrow
    zcol = jnp.zeros((nf, pad_ref.shape[2]), BF)
    for i in range(side):
        pad_ref[i + 1, 0:nf] = zcol
        pad_ref[i + 1, nf + plane : 2 * nf + plane] = zcol


def by_rank(slices, rank):
    odd = lax.rem(rank, 2) == 1
    for p in range(len(slices) // 2):
        a, b = slices[2 * p], slices[2 * p + 1]
        yield lax.bitwise_xor(rank // 2, p), odd, a, b


def halves(odd, own, mate):
    low = lax.broadcasted_iota(jnp.int32, own.shape, 1) < 64
    own, mate = own.astype(F32), mate.astype(F32)
    a, b = jnp.where(odd, mate, own), jnp.where(odd, own, mate)
    top = jnp.where(low, a, pltpu.roll(b, 64, 1))
    bottom = jnp.where(low, pltpu.roll(a, 64, 1), b)
    return top, bottom


def store_packed(rank, mate_ref, keep_ref, part, k, step, low):
    rows_now = chunk(k, step)
    odd = lax.rem(rank, 2) == 1
    for q in range(keep_ref.shape[0]):
        x = part[:step, 128 * q : 128 * q + 128]
        y = part[step:, 128 * q : 128 * q + 128]
        even_slice = jnp.where(low, x, pltpu.roll(y, 64, 1))
        odd_slice = jnp.where(low, pltpu.roll(x, 64, 1), y)
        p = lax.bitwise_xor(rank // 2, q)
        keep_ref[p, rows_now, :] = jnp.where(odd, odd_slice, even_slice).astype(BF)
        mate_ref[p, rows_now, :] = jnp.where(odd, even_slice, odd_slice).astype(BF)


def fetch_kernels(w_ref, ktm_ref, lw_ref, sems):
    nz, _, width = w_ref.shape
    hc = ktm_ref.shape[0]
    copies = []
    for z in range(nz):
        copies.append(pltpu.make_async_copy(
            w_ref.at[z, pl.ds(0, hc)], ktm_ref.at[:, pl.ds(z * width, width)], sems.at[2 * z]))
        copies.append(pltpu.make_async_copy(
            w_ref.at[z, pl.ds(hc, lw_ref.shape[1])], lw_ref.at[z], sems.at[2 * z + 1]))
    for copy in copies:
        copy.start()
    return copies


def join_temporal(lw_ref, lf_ref, ltm_ref):
    ch = ltm_ref.shape[1]
    width = lw_ref.shape[2] // 2
    count = 2 * lw_ref.shape[0]
    size = ltm_ref.shape[0] // count
    for z in range(lw_ref.shape[0]):
        first = lw_ref[z, :, 0:ch].astype(F32)
        off = width % 128
        second = lw_ref[z, :, width - off : width - off + ch + 128].astype(F32)
        second = pltpu.roll(second, ch + 128 - off, 1)[:, 0:ch]
        for b, block in ((2 * z, first), (2 * z + 1, second)):
            lf_ref[b * size : b * size + block.shape[0], :] = block
    ltm_ref[...] = lf_ref[0 : ltm_ref.shape[0], :].astype(BF)


def conv_body(side, first, rank_ref, *refs):
    n = 1 if first else 8
    slices = refs[:n]
    (w_ref, vec_ref, before_ref, after_ref,
     pad_out, hid_out, xhat_out, rs_ref, mate_ref, keep_ref,
     pad_ref, hid_ref, xhat_ref, sp_ref, ktm_ref, lw_ref, lf_ref, ltm_ref, kn_ref, sems) = refs[n:]
    rank = rank_ref[0]
    nz = 2 * w_ref.shape[0]
    fetched = fetch_kernels(w_ref, ktm_ref, lw_ref, sems)
    ch, hc = pad_ref.shape[2], hid_ref.shape[1]
    rows = hid_ref.shape[0]
    plane = rows // side
    nf = plane // side
    step = plane // 2
    clear_borders(pad_ref, side, plane, nf)
    if first:
        for i in range(side):
            pad_ref[i + 1, nf : nf + plane] = slices[0][i * plane : (i + 1) * plane]
    else:
        def place(k, carry):
            for q, odd, a_ref, b_ref in by_rank(slices, rank):
                top, bottom = halves(odd, a_ref[chunk(k, step), :], b_ref[chunk(k, step), :])
                lanes = pl.ds(pl.multiple_of(128 * q, 128), 128)
                for piece, kk in ((top, k), (bottom, k + side)):
                    at = nf + lax.rem(kk, 2) * step
                    pad_ref[1 + kk // 2, pl.ds(pl.multiple_of(at, 16), step), lanes] = piece.astype(BF)
            return carry

        lax.fori_loop(0, side, place, 0, unroll=True)
    pad_copy = pltpu.make_async_copy(pad_ref, pad_out, sems.at[nz])
    pad_copy.start()
    for copy in fetched:
        copy.wait()
    for t in range(9):
        kn_ref[t] = ktm_ref[:, t * ch : (t + 1) * ch].astype(F32).T.astype(BF)
    join_temporal(lw_ref, lf_ref, ltm_ref)

    def conv(i, total):
        acc = jnp.zeros((plane, hc), F32)
        for t in range(9):
            r, c = t // 3, t % 3
            acc += nn(pad_ref[i + r, c * nf : c * nf + plane, :], kn_ref[t])
        sp_ref[i] = acc
        return total + jnp.sum(acc, axis=0, keepdims=True)

    mean = lax.fori_loop(0, side, conv, jnp.zeros((1, hc), F32), unroll=True) / rows

    def square(i, total):
        cen = sp_ref[i] - mean
        return total + jnp.sum(cen * cen, axis=0, keepdims=True)

    var = lax.fori_loop(0, side, square, jnp.zeros((1, hc), F32), unroll=True) / rows
    rs = lax.rsqrt(var + eps)
    rs_ref[...] = rs
    gain, bias = vec_ref[0:1, :], vec_ref[1:2, :]

    def act(i, carry):
        xhat = (sp_ref[i] - mean) * rs
        xhat_ref[i] = xhat
        v = xhat * gain + bias
        v = v * jax.nn.sigmoid(v)
        sp_ref[i] = v
        hid_ref[chunk(i, plane), :] = v.astype(BF)
        return carry

    lax.fori_loop(0, side, act, 0, unroll=True)
    late = [
        pltpu.make_async_copy(hid_ref, hid_out, sems.at[nz + 1]),
        pltpu.make_async_copy(xhat_ref, xhat_out, sems.at[nz + 2]),
    ]
    for copy in late:
        copy.start()
    low = lax.broadcasted_iota(jnp.int32, (step, 128), 1) < 64

    def temporal(k, carry):
        pieces = []
        for kk in (k, k + side):
            par = lax.rem(kk, 2)
            h = sp_ref[kk // 2, pl.ds(pl.multiple_of(par * step, 8), step), :]
            at = pl.multiple_of(par * (step % nf), 8)
            pieces.append((
                (pltpu.roll(h, 1, 0) * before_ref[pl.ds(at, step), :]).astype(BF),
                h.astype(BF),
                (pltpu.roll(h, step - 1, 0) * after_ref[pl.ds(at, step), :]).astype(BF),
            ))
        part = sum(
            nn(jnp.concatenate([x, y], axis=0), ltm_ref[t * hc : (t + 1) * hc])
            for t, (x, y) in enumerate(zip(*pieces))
        )
        store_packed(rank, mate_ref, keep_ref, part, k, step, low)
        return carry

    lax.fori_loop(0, side, temporal, 0, unroll=True)
    for copy in [pad_copy] + late:
        copy.wait()


def kernel_scratch(w, hc, ch):
    return [
        pltpu.VMEM((hc, 9 * ch), BF),
        pltpu.VMEM((w.shape[0], w.shape[1] - hc, w.shape[2]), BF),
        pltpu.VMEM((3 * hc + w.shape[1] - hc, ch), F32),
        pltpu.VMEM((3 * hc, ch), BF),
    ]


def conv_forward(rank, g, w, vec, before, after, side, pixels, ch, deps=()):
    hc = vec.shape[1]
    plane = pixels // side
    nf = plane // side
    n = len(g)
    shapes = [
        ((side + 2, plane + 2 * nf, ch), BF),
        ((pixels, hc), BF),
        ((side, plane, hc), F32),
    ]
    outs = [jax.ShapeDtypeStruct(*s) for s in shapes] + [
        jax.ShapeDtypeStruct((1, hc), F32),
        jax.ShapeDtypeStruct((4, pixels // 2, 128), BF),
        jax.ShapeDtypeStruct((4, pixels // 2, 128), BF),
    ]
    scratch = [pltpu.VMEM(*s) for s in shapes] + [
        pltpu.VMEM((side, plane, hc), F32),
        *kernel_scratch(w, hc, ch),
        pltpu.VMEM((9, ch, hc), BF),
        pltpu.SemaphoreType.DMA((2 * w.shape[0] + 3,)),
    ]
    flops = 2 * pixels * hc * 12 * ch
    return call(functools.partial(conv_body, side, n == 1), outs, scratch, flops,
                rank, *g, w, vec, before, after,
                deps=deps, far=(n + 1,), far_outs=(0, 1, 2))


def fold(v):
    return v + pltpu.roll(v, 64, 1)


def total_of(refs):
    t = refs[0][...].astype(F32)
    for ref in refs[1:]:
        t += ref[...].astype(F32)
    return t


def pair_sum_body(keep_ref, mate_ref, *out_refs):
    for p, ref in enumerate(out_refs):
        ref[...] = (keep_ref[p].astype(F32) + mate_ref[p].astype(F32)).astype(ref.dtype)


def pair_sum(keep, arrived):
    shape = keep.shape[1:]
    outs = [jax.ShapeDtypeStruct(shape, BF)] * keep.shape[0]
    return call(pair_sum_body, outs, [], keep.size, keep, arrived)


def out_norm_body(n, has_skip, *refs):
    parts, refs = refs[:n], refs[n:]
    if has_skip:
        vec_ref, skip_ref, xhat_ref, rs_ref, pre_ref, res_ref = refs
    else:
        vec_ref, xhat_ref, rs_ref, pre_ref, res_ref = refs
    t = total_of(parts)
    pixels = 2 * t.shape[0]
    mean = fold(jnp.sum(t, axis=0, keepdims=True)) / pixels
    cen = t - mean
    rs = lax.rsqrt(fold(jnp.sum(cen * cen, axis=0, keepdims=True)) / pixels + eps)
    xhat = cen * rs
    pre = xhat * vec_ref[0:1, :] + vec_ref[1:2, :]
    if has_skip:
        pre = pre + skip_ref[...].astype(F32)
    xhat_ref[...] = xhat
    rs_ref[...] = rs
    pre_ref[...] = pre
    res_ref[...] = (pre * jax.nn.sigmoid(pre)).astype(BF)


def out_norm(parts, vec, skip):
    half = parts[0].shape[0]
    outs = [
        jax.ShapeDtypeStruct((half, 128), F32),
        jax.ShapeDtypeStruct((1, 128), F32),
        jax.ShapeDtypeStruct((half, 128), F32),
        jax.ShapeDtypeStruct((half, 128), BF),
    ]
    args = (*parts, vec) + (() if skip is None else (skip,))
    body = functools.partial(out_norm_body, len(parts), skip is not None)
    return call(body, outs, [], half * 128 * 10, *args)


def out_back_body(n, *refs):
    parts, (pre_ref, xhat_ref, rs_ref, vec_ref, dpre_ref, dt_ref, sums_ref) = refs[:n], refs[n:]
    g = total_of(parts)
    pre, xhat = pre_ref[...], xhat_ref[...]
    sig = jax.nn.sigmoid(pre)
    dpre = g * (sig * (1.0 + pre * (1.0 - sig)))
    pixels = 2 * pre.shape[0]
    sb = fold(jnp.sum(dpre, axis=0, keepdims=True))
    sg = fold(jnp.sum(dpre * xhat, axis=0, keepdims=True))
    dpre_ref[...] = dpre.astype(BF)
    scale = vec_ref[0:1, :] * rs_ref[...]
    dt_ref[...] = (scale * (dpre - sb / pixels - xhat * (sg / pixels))).astype(BF)
    sums_ref[0:1, :] = sg
    sums_ref[1:2, :] = sb


def out_back(parts, pre, xhat, rs, vec, deps=()):
    half = pre.shape[0]
    outs = [
        jax.ShapeDtypeStruct((half, 128), BF),
        jax.ShapeDtypeStruct((half, 128), BF),
        jax.ShapeDtypeStruct((2, 128), F32),
    ]
    args = (*parts, pre, xhat, rs, vec)
    return call(functools.partial(out_back_body, len(parts)), outs, [], half * 1280, *args, deps=deps)


def conv_back_body(side, rank_ref, *refs):
    slices, (xhat_in, rs_ref, w_ref, vec_ref, before_ref, after_ref,
             dt_out, ds_out, sums_ref, mate_ref, keep_ref,
             dt_ref, ds_ref, xhat_ref, dy_ref, pad_ref, ktm_ref, lw_ref, lf_ref, ltm_ref, lnt_ref,
             sems) = (refs[:8], refs[8:])
    half = slices[0].shape[0]
    rank = rank_ref[0]
    nz = 2 * w_ref.shape[0]
    rows = 2 * half
    plane = rows // side
    nf = plane // side
    step = plane // 2
    hc = ds_ref.shape[1]
    ch = dt_ref.shape[1]
    fetched = fetch_kernels(w_ref, ktm_ref, lw_ref, sems)
    xhat_copy = pltpu.make_async_copy(xhat_in, xhat_ref, sems.at[nz])
    xhat_copy.start()
    clear_borders(pad_ref, side, plane, nf)

    def place(k, carry):
        for q, odd, a_ref, b_ref in by_rank(slices, rank):
            top, bottom = halves(odd, a_ref[chunk(k, step), :], b_ref[chunk(k, step), :])
            lanes = pl.ds(pl.multiple_of(128 * q, 128), 128)
            dt_ref[chunk(k, step), lanes] = top.astype(BF)
            dt_ref[pl.ds(pl.multiple_of(half + k * step, 16), step), lanes] = bottom.astype(BF)
        return carry

    lax.fori_loop(0, side, place, 0, unroll=True)
    dt_copy = pltpu.make_async_copy(dt_ref, dt_out, sems.at[nz + 1])
    dt_copy.start()
    for copy in fetched + [xhat_copy]:
        copy.wait()
    join_temporal(lw_ref, lf_ref, ltm_ref)
    for t in range(3):
        lnt_ref[t] = ltm_ref[t * hc : (t + 1) * hc].astype(F32).T.astype(BF)
    gain, bias = vec_ref[0:1, :], vec_ref[1:2, :]

    def hidden_grad(i, sums):
        dt = dt_ref[chunk(i, plane), :]
        early = nn(dt, lnt_ref[0]) * before_ref[0:plane, :]
        late = nn(dt, lnt_ref[2]) * after_ref[0:plane, :]
        dh = nn(dt, lnt_ref[1]) + pltpu.roll(early, plane - 1, 0) + pltpu.roll(late, 1, 0)
        xhat = xhat_ref[i]
        v = xhat * gain + bias
        sig = jax.nn.sigmoid(v)
        dy = dh * (sig * (1.0 + v * (1.0 - sig)))
        dy_ref[i] = dy
        return (
            sums[0] + jnp.sum(dy * xhat, axis=0, keepdims=True),
            sums[1] + jnp.sum(dy, axis=0, keepdims=True),
        )

    zero = jnp.zeros((1, hc), F32)
    sg, sb = lax.fori_loop(0, side, hidden_grad, (zero, zero), unroll=True)
    sums_ref[0:1, :] = sg
    sums_ref[1:2, :] = sb
    scale = gain * rs_ref[...]

    def spatial_grad(i, carry):
        ds = (scale * (dy_ref[i] - sb / rows - xhat_ref[i] * (sg / rows))).astype(BF)
        pad_ref[i + 1, nf : nf + plane] = ds
        ds_ref[chunk(i, plane), :] = ds
        return carry

    lax.fori_loop(0, side, spatial_grad, 0, unroll=True)
    ds_copy = pltpu.make_async_copy(ds_ref, ds_out, sems.at[nz + 2])
    ds_copy.start()
    low = lax.broadcasted_iota(jnp.int32, (step, 128), 1) < 64

    def back(k, carry):
        acc = jnp.zeros((2 * step, ch), F32)
        for t in range(9):
            r, c = 2 - t // 3, 2 - t % 3
            pieces = []
            for kk in (k, k + side):
                at = c * nf + lax.rem(kk, 2) * step
                pieces.append(pad_ref[kk // 2 + r, pl.ds(pl.multiple_of(at, 16), step), :])
            acc += nn(jnp.concatenate(pieces, axis=0), ktm_ref[:, t * ch : (t + 1) * ch])
        store_packed(rank, mate_ref, keep_ref, acc, k, step, low)
        return carry

    lax.fori_loop(0, side, back, 0, unroll=True)
    dt_copy.wait()
    ds_copy.wait()


def conv_back(rank, g, xhat, rs, w, vec, before, after, side, deps=()):
    half = g[0].shape[0]
    hc = vec.shape[1]
    ch = len(g) * 64
    pixels = 2 * half
    plane = pixels // side
    nf = plane // side
    outs = [
        jax.ShapeDtypeStruct((pixels, ch), BF),
        jax.ShapeDtypeStruct((pixels, hc), BF),
        jax.ShapeDtypeStruct((2, hc), F32),
        jax.ShapeDtypeStruct((4, half, 128), BF),
        jax.ShapeDtypeStruct((4, half, 128), BF),
    ]
    scratch = [
        pltpu.VMEM((pixels, ch), BF),
        pltpu.VMEM((pixels, hc), BF),
        pltpu.VMEM((side, plane, hc), F32),
        pltpu.VMEM((side, plane, hc), F32),
        pltpu.VMEM((side + 2, plane + 2 * nf, hc), BF),
        *kernel_scratch(w, hc, ch),
        pltpu.VMEM((3, ch, hc), BF),
        pltpu.SemaphoreType.DMA((2 * w.shape[0] + 3,)),
    ]
    flops = 2 * pixels * hc * 12 * ch
    return call(functools.partial(conv_back_body, side), outs, scratch, flops,
                rank, *g, xhat, rs, w, vec, before, after,
                deps=deps, far=(9, 11), far_outs=(0, 1))


def grads_body(side, pad_ref, hid_ref, ds_ref, dt_ref, before_ref, after_ref, mid_ref, out_ref,
               sg_ref, dst_ref, taps_ref, tg_ref, vec_ref):
    ch = pad_ref.shape[2]
    hc = hid_ref.shape[1]
    plane = hid_ref.shape[0] // side
    nf = plane // side
    for i in (0, 1, side + 2, side + 3):
        dst_ref[i] = jnp.zeros(dst_ref.shape[1:], BF)
    for i in range(side):
        at = slice(i * plane, (i + 1) * plane)
        h = hid_ref[at, :].astype(F32)
        taps_ref[i, 0:hc] = (pltpu.roll(h, 1, 0) * before_ref[0:plane, :]).T.astype(BF)
        taps_ref[i, hc : 2 * hc] = h.T.astype(BF)
        taps_ref[i, 2 * hc : 3 * hc] = (pltpu.roll(h, plane - 1, 0) * after_ref[0:plane, :]).T.astype(BF)
        dst_ref[i + 2] = ds_ref[at, :].astype(F32).T.astype(BF)
    tg_ref[0 : 3 * hc, :] = sum(
        nn(taps_ref[i], dt_ref[i * plane : (i + 1) * plane, :]) for i in range(side)
    )
    tg_ref[3 * hc :, :] = jnp.zeros((tg_ref.shape[0] - 3 * hc, ch), F32)
    nz, _, width = sg_ref.shape
    size = 3 * hc // (2 * nz)
    vec_ref[...] = jnp.zeros(vec_ref.shape, F32)
    vec_ref[size : size + 2, 0:hc] = mid_ref[...]
    vec_ref[size + 2 : size + 4, 0:128] = out_ref[...]
    tall = vec_ref.shape[0]
    inside = lax.broadcasted_iota(jnp.int32, (tall, ch), 0) < size
    off = (width // 2) % 128
    for z in range(nz):
        first, second = [
            jnp.where(inside, tg_ref[b * size : b * size + tall, :], vec_ref[...])
            for b in (2 * z, 2 * z + 1)
        ]
        start = width // 2 - off
        sg_ref[z, hc : hc + tall, 0:ch] = first.astype(BF)
        second = pltpu.roll(jnp.concatenate([second, jnp.zeros((tall, 128), F32)], axis=1), off, 1)
        sg_ref[z, hc : hc + tall, start : start + ch + 128] = second.astype(BF)
    for c in range(3):
        acc = sum(
            nn(dst_ref[i : i + 3].reshape(3 * hc, plane), pad_ref[i, c * nf : c * nf + plane, :])
            for i in range(1, side + 1)
        )
        for r in range(3):
            first = (3 * r + c) * ch
            end = first + ch
            at = (2 - r) * hc
            done = 0
            while first < end:
                z = first // width
                last = min(end, (z + 1) * width)
                sg_ref[z, 0:hc, first - z * width : last - z * width] = (
                    acc[at : at + hc, done : done + last - first].astype(BF)
                )
                done += last - first
                first = last


def kernel_grads(pad, hidden, ds, dt, before, after, mid, out, side, shape, deps=()):
    pixels, hc = hidden.shape
    ch = dt.shape[1]
    plane = pixels // side
    outs = [jax.ShapeDtypeStruct(shape, BF)]
    tall = shape[1] - hc
    scratch = [
        pltpu.VMEM((side + 4, hc, plane), BF),
        pltpu.VMEM((side, 3 * hc, plane), BF),
        pltpu.VMEM((3 * hc + tall, ch), F32),
        pltpu.VMEM((tall, ch), F32),
    ]
    flops = 2 * pixels * hc * 12 * ch
    return call(functools.partial(grads_body, side), outs, scratch, flops,
                pad, hidden, ds, dt, before, after, mid, out, deps=deps)[0]


def copy_after_body(v_ref, out_ref):
    out_ref[...] = v_ref[...]


def after_all(v, *deps):
    return call(copy_after_body, [jax.ShapeDtypeStruct(v.shape, v.dtype)], [], v.size, v, deps=deps)[0]


def call(body, outs, scratch, flops, *args, deps=(), far=(), far_outs=()):
    moved = sum(a.size * a.dtype.itemsize for a in args) + sum(
        o.size * o.dtype.itemsize for o in outs
    )
    n = len(deps)

    def spec(a):
        return pl.BlockSpec(memory_space=pltpu.SMEM if a.dtype == jnp.int32 else pltpu.VMEM)

    return pl.pallas_call(
        lambda *refs: body(*refs[n:]),
        out_shape=outs,
        in_specs=[ANY] * n + [ANY if i in far else spec(a) for i, a in enumerate(args)],
        out_specs=[ANY if i in far_outs else spec(o) for i, o in enumerate(outs)],
        scratch_shapes=scratch,
        compiler_params=pltpu.CompilerParams(vmem_limit_bytes=VMEM_CAP),
        cost_estimate=pl.CostEstimate(flops=flops, bytes_accessed=moved, transcendentals=0),
    )(*deps, *args)


def chunk(i, size):
    return pl.ds(pl.multiple_of(i * size, 16), size)


def clear_borders(pad_ref, side, plane, nf):
    zrow = jnp.zeros(pad_ref.shape[1:], BF)
    pad_ref[0] = zrow
    pad_ref[side + 1] = zrow
    zcol = jnp.zeros((nf, pad_ref.shape[2]), BF)
    for i in range(side):
        pad_ref[i + 1, 0:nf] = zcol
        pad_ref[i + 1, nf + plane : 2 * nf + plane] = zcol


def by_rank(slices, rank):
    odd = lax.rem(rank, 2) == 1
    for p in range(len(slices) // 2):
        a, b = slices[2 * p], slices[2 * p + 1]
        yield lax.bitwise_xor(rank // 2, p), odd, a, b


def halves(odd, own, mate):
    low = lax.broadcasted_iota(jnp.int32, own.shape, 1) < 64
    own, mate = own.astype(F32), mate.astype(F32)
    a, b = jnp.where(odd, mate, own), jnp.where(odd, own, mate)
    top = jnp.where(low, a, pltpu.roll(b, 64, 1))
    bottom = jnp.where(low, pltpu.roll(a, 64, 1), b)
    return top, bottom


def store_packed(rank, mate_ref, keep_ref, part, k, step, low):
    rows_now = chunk(k, step)
    odd = lax.rem(rank, 2) == 1
    for q in range(keep_ref.shape[0]):
        x = part[:step, 128 * q : 128 * q + 128]
        y = part[step:, 128 * q : 128 * q + 128]
        even_slice = jnp.where(low, x, pltpu.roll(y, 64, 1))
        odd_slice = jnp.where(low, pltpu.roll(x, 64, 1), y)
        p = lax.bitwise_xor(rank // 2, q)
        keep_ref[p, rows_now, :] = jnp.where(odd, odd_slice, even_slice).astype(BF)
        mate_ref[p, rows_now, :] = jnp.where(odd, even_slice, odd_slice).astype(BF)


def fetch_kernels(w_ref, ktm_ref, lw_ref, sems):
    nz, _, width = w_ref.shape
    hc = ktm_ref.shape[0]
    copies = []
    for z in range(nz):
        copies.append(pltpu.make_async_copy(
            w_ref.at[z, pl.ds(0, hc)], ktm_ref.at[:, pl.ds(z * width, width)], sems.at[2 * z]))
        copies.append(pltpu.make_async_copy(
            w_ref.at[z, pl.ds(hc, lw_ref.shape[1])], lw_ref.at[z], sems.at[2 * z + 1]))
    for copy in copies:
        copy.start()
    return copies


def join_temporal(lw_ref, lf_ref, ltm_ref):
    ch = ltm_ref.shape[1]
    width = lw_ref.shape[2] // 2
    count = 2 * lw_ref.shape[0]
    size = ltm_ref.shape[0] // count
    for z in range(lw_ref.shape[0]):
        first = lw_ref[z, :, 0:ch].astype(F32)
        off = width % 128
        second = lw_ref[z, :, width - off : width - off + ch + 128].astype(F32)
        second = pltpu.roll(second, ch + 128 - off, 1)[:, 0:ch]
        for b, block in ((2 * z, first), (2 * z + 1, second)):
            lf_ref[b * size : b * size + block.shape[0], :] = block
    ltm_ref[...] = lf_ref[0 : ltm_ref.shape[0], :].astype(BF)


def conv_body(side, first, rank_ref, *refs):
    n = 1 if first else 8
    slices = refs[:n]
    (w_ref, vec_ref, before_ref, after_ref,
     pad_out, hid_out, xhat_out, rs_ref, mate_ref, keep_ref,
     pad_ref, hid_ref, xhat_ref, sp_ref, ktm_ref, lw_ref, lf_ref, ltm_ref, kn_ref, sems) = refs[n:]
    rank = rank_ref[0]
    nz = 2 * w_ref.shape[0]
    fetched = fetch_kernels(w_ref, ktm_ref, lw_ref, sems)
    ch, hc = pad_ref.shape[2], hid_ref.shape[1]
    rows = hid_ref.shape[0]
    plane = rows // side
    nf = plane // side
    step = plane // 2
    clear_borders(pad_ref, side, plane, nf)
    if first:
        for i in range(side):
            pad_ref[i + 1, nf : nf + plane] = slices[0][i * plane : (i + 1) * plane]
    else:
        def place(k, carry):
            for q, odd, a_ref, b_ref in by_rank(slices, rank):
                top, bottom = halves(odd, a_ref[chunk(k, step), :], b_ref[chunk(k, step), :])
                lanes = pl.ds(pl.multiple_of(128 * q, 128), 128)
                for piece, kk in ((top, k), (bottom, k + side)):
                    at = nf + lax.rem(kk, 2) * step
                    pad_ref[1 + kk // 2, pl.ds(pl.multiple_of(at, 16), step), lanes] = piece.astype(BF)
            return carry

        lax.fori_loop(0, side, place, 0, unroll=True)
    pad_copy = pltpu.make_async_copy(pad_ref, pad_out, sems.at[nz])
    pad_copy.start()
    for copy in fetched:
        copy.wait()
    for t in range(9):
        kn_ref[t] = ktm_ref[:, t * ch : (t + 1) * ch].astype(F32).T.astype(BF)
    join_temporal(lw_ref, lf_ref, ltm_ref)

    def conv(i, total):
        acc = jnp.zeros((plane, hc), F32)
        for t in range(9):
            r, c = t // 3, t % 3
            acc += nn(pad_ref[i + r, c * nf : c * nf + plane, :], kn_ref[t])
        sp_ref[i] = acc
        return total + jnp.sum(acc, axis=0, keepdims=True)

    mean = lax.fori_loop(0, side, conv, jnp.zeros((1, hc), F32), unroll=True) / rows

    def square(i, total):
        cen = sp_ref[i] - mean
        return total + jnp.sum(cen * cen, axis=0, keepdims=True)

    var = lax.fori_loop(0, side, square, jnp.zeros((1, hc), F32), unroll=True) / rows
    rs = lax.rsqrt(var + eps)
    rs_ref[...] = rs
    gain, bias = vec_ref[0:1, :], vec_ref[1:2, :]

    def act(i, carry):
        xhat = (sp_ref[i] - mean) * rs
        xhat_ref[i] = xhat
        v = xhat * gain + bias
        v = v * jax.nn.sigmoid(v)
        sp_ref[i] = v
        hid_ref[chunk(i, plane), :] = v.astype(BF)
        return carry

    lax.fori_loop(0, side, act, 0, unroll=True)
    late = [
        pltpu.make_async_copy(hid_ref, hid_out, sems.at[nz + 1]),
        pltpu.make_async_copy(xhat_ref, xhat_out, sems.at[nz + 2]),
    ]
    for copy in late:
        copy.start()
    low = lax.broadcasted_iota(jnp.int32, (step, 128), 1) < 64

    def temporal(k, carry):
        pieces = []
        for kk in (k, k + side):
            par = lax.rem(kk, 2)
            h = sp_ref[kk // 2, pl.ds(pl.multiple_of(par * step, 8), step), :]
            at = pl.multiple_of(par * (step % nf), 8)
            pieces.append((
                (pltpu.roll(h, 1, 0) * before_ref[pl.ds(at, step), :]).astype(BF),
                h.astype(BF),
                (pltpu.roll(h, step - 1, 0) * after_ref[pl.ds(at, step), :]).astype(BF),
            ))
        part = sum(
            nn(jnp.concatenate([x, y], axis=0), ltm_ref[t * hc : (t + 1) * hc])
            for t, (x, y) in enumerate(zip(*pieces))
        )
        store_packed(rank, mate_ref, keep_ref, part, k, step, low)
        return carry

    lax.fori_loop(0, side, temporal, 0, unroll=True)
    for copy in [pad_copy] + late:
        copy.wait()


def kernel_scratch(w, hc, ch):
    return [
        pltpu.VMEM((hc, 9 * ch), BF),
        pltpu.VMEM((w.shape[0], w.shape[1] - hc, w.shape[2]), BF),
        pltpu.VMEM((3 * hc + w.shape[1] - hc, ch), F32),
        pltpu.VMEM((3 * hc, ch), BF),
    ]


def conv_forward(rank, g, w, vec, before, after, side, pixels, ch, deps=()):
    hc = vec.shape[1]
    plane = pixels // side
    nf = plane // side
    n = len(g)
    shapes = [
        ((side + 2, plane + 2 * nf, ch), BF),
        ((pixels, hc), BF),
        ((side, plane, hc), F32),
    ]
    outs = [jax.ShapeDtypeStruct(*s) for s in shapes] + [
        jax.ShapeDtypeStruct((1, hc), F32),
        jax.ShapeDtypeStruct((4, pixels // 2, 128), BF),
        jax.ShapeDtypeStruct((4, pixels // 2, 128), BF),
    ]
    scratch = [pltpu.VMEM(*s) for s in shapes] + [
        pltpu.VMEM((side, plane, hc), F32),
        *kernel_scratch(w, hc, ch),
        pltpu.VMEM((9, ch, hc), BF),
        pltpu.SemaphoreType.DMA((2 * w.shape[0] + 3,)),
    ]
    flops = 2 * pixels * hc * 12 * ch
    return call(functools.partial(conv_body, side, n == 1), outs, scratch, flops,
                rank, *g, w, vec, before, after,
                deps=deps, far=(n + 1,), far_outs=(0, 1, 2))


def fold(v):
    return v + pltpu.roll(v, 64, 1)


def total_of(refs):
    t = refs[0][...].astype(F32)
    for ref in refs[1:]:
        t += ref[...].astype(F32)
    return t


def pair_sum_body(keep_ref, mate_ref, *out_refs):
    for p, ref in enumerate(out_refs):
        ref[...] = (keep_ref[p].astype(F32) + mate_ref[p].astype(F32)).astype(ref.dtype)


def pair_sum(keep, arrived):
    shape = keep.shape[1:]
    outs = [jax.ShapeDtypeStruct(shape, BF)] * keep.shape[0]
    return call(pair_sum_body, outs, [], keep.size, keep, arrived)


def out_norm_body(n, has_skip, *refs):
    parts, refs = refs[:n], refs[n:]
    if has_skip:
        vec_ref, skip_ref, xhat_ref, rs_ref, pre_ref, res_ref = refs
    else:
        vec_ref, xhat_ref, rs_ref, pre_ref, res_ref = refs
    t = total_of(parts)
    pixels = 2 * t.shape[0]
    mean = fold(jnp.sum(t, axis=0, keepdims=True)) / pixels
    cen = t - mean
    rs = lax.rsqrt(fold(jnp.sum(cen * cen, axis=0, keepdims=True)) / pixels + eps)
    xhat = cen * rs
    pre = xhat * vec_ref[0:1, :] + vec_ref[1:2, :]
    if has_skip:
        pre = pre + skip_ref[...].astype(F32)
    xhat_ref[...] = xhat
    rs_ref[...] = rs
    pre_ref[...] = pre
    res_ref[...] = (pre * jax.nn.sigmoid(pre)).astype(BF)


def out_norm(parts, vec, skip):
    half = parts[0].shape[0]
    outs = [
        jax.ShapeDtypeStruct((half, 128), F32),
        jax.ShapeDtypeStruct((1, 128), F32),
        jax.ShapeDtypeStruct((half, 128), F32),
        jax.ShapeDtypeStruct((half, 128), BF),
    ]
    args = (*parts, vec) + (() if skip is None else (skip,))
    body = functools.partial(out_norm_body, len(parts), skip is not None)
    return call(body, outs, [], half * 128 * 10, *args)


def out_back_body(n, *refs):
    parts, (pre_ref, xhat_ref, rs_ref, vec_ref, dpre_ref, dt_ref, sums_ref) = refs[:n], refs[n:]
    g = total_of(parts)
    pre, xhat = pre_ref[...], xhat_ref[...]
    sig = jax.nn.sigmoid(pre)
    dpre = g * (sig * (1.0 + pre * (1.0 - sig)))
    pixels = 2 * pre.shape[0]
    sb = fold(jnp.sum(dpre, axis=0, keepdims=True))
    sg = fold(jnp.sum(dpre * xhat, axis=0, keepdims=True))
    dpre_ref[...] = dpre.astype(BF)
    scale = vec_ref[0:1, :] * rs_ref[...]
    dt_ref[...] = (scale * (dpre - sb / pixels - xhat * (sg / pixels))).astype(BF)
    sums_ref[0:1, :] = sg
    sums_ref[1:2, :] = sb


def out_back(parts, pre, xhat, rs, vec, deps=()):
    half = pre.shape[0]
    outs = [
        jax.ShapeDtypeStruct((half, 128), BF),
        jax.ShapeDtypeStruct((half, 128), BF),
        jax.ShapeDtypeStruct((2, 128), F32),
    ]
    args = (*parts, pre, xhat, rs, vec)
    return call(functools.partial(out_back_body, len(parts)), outs, [], half * 1280, *args, deps=deps)


def conv_back_body(side, rank_ref, *refs):
    slices, (xhat_in, rs_ref, w_ref, vec_ref, before_ref, after_ref,
             dt_out, ds_out, sums_ref, mate_ref, keep_ref,
             dt_ref, ds_ref, xhat_ref, dy_ref, pad_ref, ktm_ref, lw_ref, lf_ref, ltm_ref, lnt_ref,
             sems) = (refs[:8], refs[8:])
    half = slices[0].shape[0]
    rank = rank_ref[0]
    nz = 2 * w_ref.shape[0]
    rows = 2 * half
    plane = rows // side
    nf = plane // side
    step = plane // 2
    hc = ds_ref.shape[1]
    ch = dt_ref.shape[1]
    fetched = fetch_kernels(w_ref, ktm_ref, lw_ref, sems)
    xhat_copy = pltpu.make_async_copy(xhat_in, xhat_ref, sems.at[nz])
    xhat_copy.start()
    clear_borders(pad_ref, side, plane, nf)

    def place(k, carry):
        for q, odd, a_ref, b_ref in by_rank(slices, rank):
            top, bottom = halves(odd, a_ref[chunk(k, step), :], b_ref[chunk(k, step), :])
            lanes = pl.ds(pl.multiple_of(128 * q, 128), 128)
            dt_ref[chunk(k, step), lanes] = top.astype(BF)
            dt_ref[pl.ds(pl.multiple_of(half + k * step, 16), step), lanes] = bottom.astype(BF)
        return carry

    lax.fori_loop(0, side, place, 0, unroll=True)
    dt_copy = pltpu.make_async_copy(dt_ref, dt_out, sems.at[nz + 1])
    dt_copy.start()
    for copy in fetched + [xhat_copy]:
        copy.wait()
    join_temporal(lw_ref, lf_ref, ltm_ref)
    for t in range(3):
        lnt_ref[t] = ltm_ref[t * hc : (t + 1) * hc].astype(F32).T.astype(BF)
    gain, bias = vec_ref[0:1, :], vec_ref[1:2, :]

    def hidden_grad(i, sums):
        dt = dt_ref[chunk(i, plane), :]
        early = nn(dt, lnt_ref[0]) * before_ref[0:plane, :]
        late = nn(dt, lnt_ref[2]) * after_ref[0:plane, :]
        dh = nn(dt, lnt_ref[1]) + pltpu.roll(early, plane - 1, 0) + pltpu.roll(late, 1, 0)
        xhat = xhat_ref[i]
        v = xhat * gain + bias
        sig = jax.nn.sigmoid(v)
        dy = dh * (sig * (1.0 + v * (1.0 - sig)))
        dy_ref[i] = dy
        return (
            sums[0] + jnp.sum(dy * xhat, axis=0, keepdims=True),
            sums[1] + jnp.sum(dy, axis=0, keepdims=True),
        )

    zero = jnp.zeros((1, hc), F32)
    sg, sb = lax.fori_loop(0, side, hidden_grad, (zero, zero), unroll=True)
    sums_ref[0:1, :] = sg
    sums_ref[1:2, :] = sb
    scale = gain * rs_ref[...]

    def spatial_grad(i, carry):
        ds = (scale * (dy_ref[i] - sb / rows - xhat_ref[i] * (sg / rows))).astype(BF)
        pad_ref[i + 1, nf : nf + plane] = ds
        ds_ref[chunk(i, plane), :] = ds
        return carry

    lax.fori_loop(0, side, spatial_grad, 0, unroll=True)
    ds_copy = pltpu.make_async_copy(ds_ref, ds_out, sems.at[nz + 2])
    ds_copy.start()
    low = lax.broadcasted_iota(jnp.int32, (step, 128), 1) < 64

    def back(k, carry):
        acc = jnp.zeros((2 * step, ch), F32)
        for t in range(9):
            r, c = 2 - t // 3, 2 - t % 3
            pieces = []
            for kk in (k, k + side):
                at = c * nf + lax.rem(kk, 2) * step
                pieces.append(pad_ref[kk // 2 + r, pl.ds(pl.multiple_of(at, 16), step), :])
            acc += nn(jnp.concatenate(pieces, axis=0), ktm_ref[:, t * ch : (t + 1) * ch])
        store_packed(rank, mate_ref, keep_ref, acc, k, step, low)
        return carry

    lax.fori_loop(0, side, back, 0, unroll=True)
    dt_copy.wait()
    ds_copy.wait()


def conv_back(rank, g, xhat, rs, w, vec, before, after, side, deps=()):
    half = g[0].shape[0]
    hc = vec.shape[1]
    ch = len(g) * 64
    pixels = 2 * half
    plane = pixels // side
    nf = plane // side
    outs = [
        jax.ShapeDtypeStruct((pixels, ch), BF),
        jax.ShapeDtypeStruct((pixels, hc), BF),
        jax.ShapeDtypeStruct((2, hc), F32),
        jax.ShapeDtypeStruct((4, half, 128), BF),
        jax.ShapeDtypeStruct((4, half, 128), BF),
    ]
    scratch = [
        pltpu.VMEM((pixels, ch), BF),
        pltpu.VMEM((pixels, hc), BF),
        pltpu.VMEM((side, plane, hc), F32),
        pltpu.VMEM((side, plane, hc), F32),
        pltpu.VMEM((side + 2, plane + 2 * nf, hc), BF),
        *kernel_scratch(w, hc, ch),
        pltpu.VMEM((3, ch, hc), BF),
        pltpu.SemaphoreType.DMA((2 * w.shape[0] + 3,)),
    ]
    flops = 2 * pixels * hc * 12 * ch
    return call(functools.partial(conv_back_body, side), outs, scratch, flops,
                rank, *g, xhat, rs, w, vec, before, after,
                deps=deps, far=(9, 11), far_outs=(0, 1))


def grads_body(side, pad_ref, hid_ref, ds_ref, dt_ref, before_ref, after_ref, mid_ref, out_ref,
               sg_ref, dst_ref, taps_ref, tg_ref, vec_ref):
    ch = pad_ref.shape[2]
    hc = hid_ref.shape[1]
    plane = hid_ref.shape[0] // side
    nf = plane // side
    for i in (0, 1, side + 2, side + 3):
        dst_ref[i] = jnp.zeros(dst_ref.shape[1:], BF)
    for i in range(side):
        at = slice(i * plane, (i + 1) * plane)
        h = hid_ref[at, :].astype(F32)
        taps_ref[i, 0:hc] = (pltpu.roll(h, 1, 0) * before_ref[0:plane, :]).T.astype(BF)
        taps_ref[i, hc : 2 * hc] = h.T.astype(BF)
        taps_ref[i, 2 * hc : 3 * hc] = (pltpu.roll(h, plane - 1, 0) * after_ref[0:plane, :]).T.astype(BF)
        dst_ref[i + 2] = ds_ref[at, :].astype(F32).T.astype(BF)
    tg_ref[0 : 3 * hc, :] = sum(
        nn(taps_ref[i], dt_ref[i * plane : (i + 1) * plane, :]) for i in range(side)
    )
    tg_ref[3 * hc :, :] = jnp.zeros((tg_ref.shape[0] - 3 * hc, ch), F32)
    nz, _, width = sg_ref.shape
    size = 3 * hc // (2 * nz)
    vec_ref[...] = jnp.zeros(vec_ref.shape, F32)
    vec_ref[size : size + 2, 0:hc] = mid_ref[...]
    vec_ref[size + 2 : size + 4, 0:128] = out_ref[...]
    tall = vec_ref.shape[0]
    inside = lax.broadcasted_iota(jnp.int32, (tall, ch), 0) < size
    off = (width // 2) % 128
    for z in range(nz):
        first, second = [
            jnp.where(inside, tg_ref[b * size : b * size + tall, :], vec_ref[...])
            for b in (2 * z, 2 * z + 1)
        ]
        start = width // 2 - off
        sg_ref[z, hc : hc + tall, 0:ch] = first.astype(BF)
        second = pltpu.roll(jnp.concatenate([second, jnp.zeros((tall, 128), F32)], axis=1), off, 1)
        sg_ref[z, hc : hc + tall, start : start + ch + 128] = second.astype(BF)
    for c in range(3):
        acc = sum(
            nn(dst_ref[i : i + 3].reshape(3 * hc, plane), pad_ref[i, c * nf : c * nf + plane, :])
            for i in range(1, side + 1)
        )
        for r in range(3):
            first = (3 * r + c) * ch
            end = first + ch
            at = (2 - r) * hc
            done = 0
            while first < end:
                z = first // width
                last = min(end, (z + 1) * width)
                sg_ref[z, 0:hc, first - z * width : last - z * width] = (
                    acc[at : at + hc, done : done + last - first].astype(BF)
                )
                done += last - first
                first = last


def kernel_grads(pad, hidden, ds, dt, before, after, mid, out, side, shape, deps=()):
    pixels, hc = hidden.shape
    ch = dt.shape[1]
    plane = pixels // side
    outs = [jax.ShapeDtypeStruct(shape, BF)]
    tall = shape[1] - hc
    scratch = [
        pltpu.VMEM((side + 4, hc, plane), BF),
        pltpu.VMEM((side, 3 * hc, plane), BF),
        pltpu.VMEM((3 * hc + tall, ch), F32),
        pltpu.VMEM((tall, ch), F32),
    ]
    flops = 2 * pixels * hc * 12 * ch
    return call(functools.partial(grads_body, side), outs, scratch, flops,
                pad, hidden, ds, dt, before, after, mid, out, deps=deps)[0]


def copy_after_body(v_ref, out_ref):
    out_ref[...] = v_ref[...]


def after_all(v, *deps):
    return call(copy_after_body, [jax.ShapeDtypeStruct(v.shape, v.dtype)], [], v.size, v, deps=deps)[0]


def hop(v, k):
    n = 1
    for name in EVERY:
        n *= lax.axis_size(name)
    return lax.ppermute(v, EVERY, [(i, i ^ k) for i in range(n)])


def plane_gather(v):
    got = {0: v}
    for k in (6, 2, 4, 1):
        got[k] = hop(v, k)
    for k in (2, 4, 6):
        got[k ^ 1] = hop(got[k], 1)
    return [got[k] for k in range(8)]


def plane_reduce(mate, keep):
    sums = pair_sum(keep, hop(mate, 1))
    arrived = {k: hop(sums[k // 2], k) for k in (6, 2, 4)}
    return [sums[0], arrived[2], arrived[4], arrived[6]]


def to_section(v, section, n_seg):
    y = lax.axis_index("y")
    near = lax.dynamic_index_in_dim(v, y, 0, keepdims=False)
    far = lax.dynamic_index_in_dim(v, 1 - y, 0, keepdims=False)
    n = 2 * n_seg * lax.axis_size("z")
    got = []
    for base, block in ((0, near), (n_seg, far)):
        row = []
        for low in range(n_seg):
            k = base + (low ^ section)
            if k == 0:
                row.append(block)
            else:
                pairs = [(i, i ^ k) for i in range(n) if i % n_seg == low]
                row.append(lax.ppermute(block, EVERY, pairs))
        got.append(jnp.stack(row))
    same, other = got
    return jnp.where(y == 0, jnp.concatenate([same, other]), jnp.concatenate([other, same]))

def on_device(frames, cot, starts, ks, ktm, mg, mb, og, ob):
    nz, n_rank, n_seg = lax.axis_size("z"), 8, 4
    n_dp = nz * 2
    fr, side, ch = frames.shape[0], frames.shape[1], frames.shape[3]
    area = side * side
    hid = ks.shape[2]
    hc, cc = hid // n_rank, ch // n_rank
    q = hc // n_rank
    rank = lax.axis_index(PLANE)
    rank_now = rank.astype(jnp.int32).reshape(1)
    d_index = lax.axis_index(("z", "y"))
    s_index = lax.axis_index(("x", "c"))
    nf = n_dp * fr
    pixels = area * nf
    half = pixels // 2

    to_plane = [(d * n_seg + s, s * n_rank + d) for d in range(n_dp) for s in range(n_seg)]
    from_plane = [(b, a) for a, b in to_plane]
    rows = fr * area
    flag_row = jnp.pad(starts.astype(BF)[None], ((0, 11), (0, ch - fr)))
    moving = jnp.concatenate([frames.reshape(rows, ch), flag_row], axis=0)
    moving = lax.ppermute(moving, EVERY, to_plane)

    perm = (jnp.arange(hid).reshape(n_rank, n_rank, q).transpose(1, 0, 2).reshape(hid)[:, None]
            == jnp.arange(hid)[None, :]).astype(BF)
    kt = lax.dot_general(perm, ks[0].astype(BF), (((1,), (1,)), ((), ())),
                         preferred_element_type=F32).astype(BF)
    kt = kt.reshape(n_rank, hc, ks.shape[1])
    lrows, width = ktm.shape[1] // n_rank, ks.shape[1]
    lt = ktm[0].astype(BF).reshape(-1, n_rank, q, ch).transpose(1, 0, 2, 3).reshape(n_rank, lrows, ch)
    lt = jnp.pad(lt, ((0, 0), (0, 0), (0, width - ch)))
    extra = jnp.concatenate([v.astype(BF) for v in (mg, mb, og, ob)], axis=1)
    tall = -(-(lrows + 4) // 16) * 16
    extra = jnp.pad(extra, ((0, tall - lrows - 1), (0, width - extra.shape[1])))
    w = jnp.concatenate([kt, lt, jnp.broadcast_to(extra, (n_rank, *extra.shape))], axis=1)
    w = lax.all_to_all(w, PLANE, 0, 0)
    here = w
    high = hc + tall
    w = w.reshape(2, n_seg, high, width).transpose(1, 2, 0, 3).reshape(n_seg, high, 2 * width)
    ws = [lax.all_gather(w[s], "z", axis=0) for s in range(n_seg)]
    mids, outs = [], []
    for s in range(n_seg):
        row = ws[s][:, hc + lrows].reshape(n_dp, width).astype(F32)
        mids.append(jnp.stack([
            lax.dynamic_slice_in_dim(row[:, i * hc : (i + 1) * hc], rank * q, q, axis=1).reshape(hc)
            for i in range(2)]))
        own = lax.dynamic_index_in_dim(row, rank, 0, keepdims=False)
        outs.append(jnp.stack([
            jnp.tile(own[2 * hc + i * cc : 2 * hc + (i + 1) * cc], 2) for i in range(2)]))

    moving = after_all(moving, here)
    gathered = lax.all_to_all(jnp.broadcast_to(moving, (n_rank, *moving.shape)), PLANE, 0, 0)

    def by_pixel(v):
        width = v.shape[2]
        v = v.reshape(n_rank * fr, area, width).transpose(1, 0, 2)
        return v.reshape(pixels, width)

    def packed(v):
        return jnp.concatenate([v[:half], v[half:]], axis=1)

    a0 = by_pixel(gathered[:, :rows])
    flags = gathered[:, rows, :fr].reshape(nf) > 0.5
    slot = jnp.arange(nf) % fr
    before = jnp.where(flags | (slot == 0), 0.0, 1.0)
    after = jnp.where(jnp.roll(flags, -1) | (slot == fr - 1), 0.0, 1.0)
    spread = (side * nf + nf, hc)
    before = jnp.broadcast_to(jnp.tile(before, side + 1)[:, None], spread)
    after = jnp.broadcast_to(jnp.tile(after, side + 1)[:, None], spread)
    skip = packed(lax.dynamic_slice_in_dim(a0, rank * cc, cc, axis=1))

    cot_moving = lax.ppermute(cot.reshape(rows, ch), EVERY, to_plane)
    cot_moving = cot_moving.reshape(rows, n_rank, cc).transpose(1, 0, 2)
    cot_own = packed(by_pixel(lax.all_to_all(after_all(cot_moving, gathered), PLANE, 0, 0)))

    def to_frames(v):
        v = jnp.concatenate([v[:, :cc], v[:, cc:]], axis=0)
        v = v.reshape(area, n_rank, fr, cc).transpose(1, 0, 2, 3).reshape(n_rank, rows, cc)
        v = lax.all_to_all(v, PLANE, 0, 0).transpose(1, 0, 2).reshape(area, fr, ch)
        return lax.ppermute(v, EVERY, from_plane).transpose(1, 0, 2).reshape(frames.shape)

    saved = []
    g = [a0]
    for s in range(n_seg):
        pad, hidden, xm, rm, mate, keep = conv_forward(
            rank_now, g, ws[s], mids[s], before, after, side, pixels, ch,
            deps=(cot_own,) if s == 0 else ())
        parts = plane_reduce(mate, keep)
        xo, ro, pre, res = out_norm(parts, outs[s], skip if s % 2 == 1 else None)
        saved.append((pad, hidden, xm, rm, xo, ro, pre))
        if s % 2 == 1:
            skip = res
        if s < n_seg - 1:
            g = plane_gather(res)
    output = to_frames(res)

    parts = [cot_own]
    skip_grad = None
    grads, raw = [], ()
    for s in reversed(range(n_seg)):
        pad, hidden, xm, rm, xo, ro, pre = saved[s]
        if s == 1:
            parts = parts + [skip_grad]
        dpre, dt, osum = out_back(parts, pre, xo, ro, outs[s], deps=raw)
        if s % 2 == 1:
            skip_grad = dpre
        dtf, ds, msum, mate, keep = conv_back(
            rank_now, plane_gather(dt), xm, rm, ws[s], mids[s], before, after, side,
            deps=tuple(grads[-2:-1]))
        if s > 0:
            parts = plane_reduce(mate, keep)
        wait = parts[:1] if s > 0 else grads[-1:]
        if s == n_seg - 2:
            wait = wait + [output]
        sg = kernel_grads(pad, hidden, ds, dtf, before, after, msum, osum, side, ws[s].shape, deps=wait)
        raw = (sg,)
        grads.append(lax.psum_scatter(sg, "z", scatter_dimension=0))
        if s == 0:
            parts = plane_reduce(mate, keep)

    da = sum(p.astype(F32) for p in parts) + skip_grad.astype(F32)
    frames_grad = to_frames(da.astype(BF)).astype(F32)

    def by_row(v):
        return v.reshape(high, 2, width).transpose(1, 0, 2)

    grads = grads[::-1]
    early = jnp.stack([jnp.zeros((2, high, width), BF)] + [by_row(v) for v in grads[1:]], axis=1)
    early = lax.all_to_all(early.reshape(n_rank, high, width), PLANE, 0, 0)
    last = to_section(after_all(by_row(grads[0]), early), 0, n_seg)
    g = jnp.where(s_index == 0, last, early)
    space_grad = lax.dot_general(g[:, :hc].reshape(hid, width), perm, (((0,), (0,)), ((), ())),
                                 preferred_element_type=F32)
    tg = g[:, hc : hc + lrows, :ch].reshape(n_rank, -1, q, ch)
    time_grad = tg.transpose(1, 0, 2, 3).reshape(-1, ch).astype(F32)
    sums = g[:, hc + lrows : hc + lrows + 4].astype(F32)

    def mid_own(v):
        return lax.dynamic_slice_in_dim(v[:, :hc], d_index * q, q, axis=1).reshape(1, hc)

    own = lax.dynamic_index_in_dim(sums, d_index, 0, keepdims=False)
    return (
        output,
        frames_grad,
        space_grad[None],
        time_grad[None],
        mid_own(sums[:, 0]),
        mid_own(sums[:, 1]),
        own[2:3, :cc],
        own[3:4, :cc],
    )


def from_behind(value, axis, steps):
    count = lax.axis_size(axis)
    leading, last = (max(0, -steps), min(count, count - steps))
    return lax.ppermute(value, axis, [(source, source + steps) for source in range(leading, last)])


def space_apply(current, kernel):
    frame_side = current.shape[1]
    padded = jnp.pad(current, ((0, 0), (1, 1), (1, 1), (0, 0)))
    stacked = jnp.concatenate(
        [
            padded[:, row_shift : row_shift + frame_side, col_shift : col_shift + frame_side, :]
            for row_shift in range(3)
            for col_shift in range(3)
        ],
        axis=-1,
    )
    return (
        stacked,
        jnp.einsum("fijc,co->fijo", stacked, kernel, preferred_element_type=jnp.float32),
    )


def space_back(gradient, kernel):
    frame_side = gradient.shape[1]
    channels = kernel.shape[0] // 9
    spread = jnp.einsum("fijo,co->fijc", gradient, kernel, preferred_element_type=jnp.float32)
    total = jnp.zeros((gradient.shape[0], frame_side + 2, frame_side + 2, channels), jnp.float32)
    for tap_index in range(9):
        row_shift = tap_index // 3
        col_shift = tap_index % 3
        piece_now = spread[..., tap_index * channels : (tap_index + 1) * channels]
        total = total + jnp.pad(
            piece_now, ((0, 0), (row_shift, 2 - row_shift), (col_shift, 2 - col_shift), (0, 0))
        )
    return total[:, 1 : frame_side + 1, 1 : frame_side + 1, :]


def time_apply(current, kernel, before_mask, after_mask):
    blanks = jnp.zeros_like(current[:1])
    earlier = jnp.concatenate([blanks, current[:-1]], axis=0) * before_mask[
        :, None, None, None
    ].astype(current.dtype)
    later = jnp.concatenate([current[1:], blanks], axis=0) * after_mask[:, None, None, None].astype(
        current.dtype
    )
    stacked = jnp.concatenate([earlier, current, later], axis=-1)
    return (
        stacked,
        jnp.einsum("fijc,co->fijo", stacked, kernel, preferred_element_type=jnp.float32),
    )


def time_back(gradient, kernel, before_mask, after_mask):
    channels = kernel.shape[0] // 3
    spread = jnp.einsum("fijo,co->fijc", gradient, kernel, preferred_element_type=jnp.float32)
    early_part = spread[..., :channels] * before_mask[:, None, None, None]
    late_part = spread[..., 2 * channels :] * after_mask[:, None, None, None]
    blanks = jnp.zeros_like(early_part[:1])
    moved_early = jnp.concatenate([early_part[1:], blanks], axis=0)
    moved_late = jnp.concatenate([blanks, late_part[:-1]], axis=0)
    return spread[..., channels : 2 * channels] + moved_early + moved_late


def moments(values, pixel_count):
    average = lax.psum(jnp.sum(values, axis=(0, 1, 2)), "dp") / pixel_count
    centered = values - average
    spread = lax.psum(jnp.sum(centered * centered, axis=(0, 1, 2)), "dp") / pixel_count
    return (average, lax.rsqrt(spread + eps))


def reduce_back(gradient, normed):
    return lax.psum(
        (jnp.sum(gradient, axis=(0, 1, 2)), jnp.sum(gradient * normed, axis=(0, 1, 2))), "dp"
    )


def silu_slope(values):
    sigmoid_now = jax.nn.sigmoid(values)
    return sigmoid_now * (1.0 + values * (1.0 - sigmoid_now))


def pick_slot(stack, slot_index):
    return lax.dynamic_index_in_dim(stack, slot_index, 0, keepdims=False)


def store_slot(stack, value, slot_index, usable):
    previous = pick_slot(stack, slot_index)
    return lax.dynamic_update_index_in_dim(stack, jnp.where(usable, value, previous), slot_index, 0)


def on_device_general(
    frames, cotangent, starts, space_kernel, time_kernel, mid_gain, mid_bias, out_gain, out_bias
):
    n_segment = lax.axis_size("segment")
    n_data = lax.axis_size("dp")
    segment_index = lax.axis_index("segment")
    odd_segment = segment_index % 2 == 1
    last_segment = segment_index == n_segment - 1
    first_segment = segment_index == 0
    frame_count = frames.shape[0]
    frame_side = frames.shape[1]
    channels = frames.shape[3]
    hidden_units = mid_gain.shape[1] * n_data
    pixel_count = n_data * frame_count * frame_side * frame_side
    turns = 2 * n_segment - 1
    block_shape = (n_segment,) + frames.shape
    all_frames, all_cot, all_starts = (
        lax.all_gather(frames, "segment", axis=0, tiled=True),
        lax.all_gather(cotangent, "segment", axis=0, tiled=True),
        lax.all_gather(starts.astype(jnp.bfloat16), "segment", axis=0, tiled=True),
    )
    frame_stack = all_frames.reshape(block_shape)
    cot_stack = all_cot.reshape(block_shape)
    clip_flags = all_starts.astype(jnp.float32).reshape(n_segment, frame_count)
    positions = jnp.arange(frame_count)
    before_mask = jnp.where((clip_flags > 0.5) | (positions == 0), 0.0, 1.0)
    following = jnp.concatenate([clip_flags[:, 1:], jnp.ones((n_segment, 1), jnp.float32)], axis=1)
    after_mask = jnp.where(following > 0.5, 0.0, 1.0)
    gathered = (
        lax.all_gather(space_kernel[0].astype(jnp.bfloat16), "dp", axis=0, tiled=True),
        lax.all_gather(time_kernel[0].astype(jnp.bfloat16), "dp", axis=0, tiled=True),
        lax.all_gather(mid_gain[0].astype(jnp.bfloat16), "dp", axis=0, tiled=True),
        lax.all_gather(mid_bias[0].astype(jnp.bfloat16), "dp", axis=0, tiled=True),
        lax.all_gather(out_gain[0].astype(jnp.bfloat16), "dp", axis=0, tiled=True),
        lax.all_gather(out_bias[0].astype(jnp.bfloat16), "dp", axis=0, tiled=True),
    )
    space_low, time_low = (gathered[0], gathered[1])
    mid_gain_now = gathered[2].astype(jnp.float32)
    mid_bias_now = gathered[3].astype(jnp.float32)
    out_gain_now = gathered[4].astype(jnp.float32)
    out_bias_now = gathered[5].astype(jnp.float32)
    incoming = jnp.zeros_like(frames)
    carried = jnp.zeros_like(frames)
    kept_input = jnp.zeros(block_shape, jnp.bfloat16)
    kept_skip = jnp.zeros(block_shape, jnp.bfloat16)
    kept_mid_mean = jnp.zeros((n_segment, hidden_units), jnp.float32)
    kept_mid_scale = jnp.zeros((n_segment, hidden_units), jnp.float32)
    kept_out_mean = jnp.zeros((n_segment, channels), jnp.float32)
    kept_out_scale = jnp.zeros((n_segment, channels), jnp.float32)
    results = jnp.zeros(block_shape, jnp.float32)
    for turn_index in range(turns):
        micro_index = turn_index - segment_index
        usable = (micro_index >= 0) & (micro_index < n_segment)
        slot_index = jnp.clip(micro_index, 0, n_segment - 1)
        current = jnp.where(first_segment, pick_slot(frame_stack, slot_index), incoming)
        skip_input = carried
        _, spatial = space_apply(current, space_low)
        mid_mean, mid_scale = moments(spatial, pixel_count)
        hidden_act = jax.nn.silu(
            (spatial - mid_mean) * mid_scale * mid_gain_now + mid_bias_now
        ).astype(jnp.bfloat16)
        _, temporal = time_apply(
            hidden_act,
            time_low,
            pick_slot(before_mask, slot_index),
            pick_slot(after_mask, slot_index),
        )
        out_mean, out_scale = moments(temporal, pixel_count)
        pre_act = (
            (temporal - out_mean) * out_scale * out_gain_now
            + out_bias_now
            + jnp.where(odd_segment, skip_input.astype(jnp.float32), 0.0)
        )
        result = jax.nn.silu(pre_act).astype(jnp.bfloat16)
        kept_input = store_slot(kept_input, current, slot_index, usable)
        kept_skip = store_slot(kept_skip, skip_input, slot_index, usable)
        kept_mid_mean = store_slot(kept_mid_mean, mid_mean, slot_index, usable)
        kept_mid_scale = store_slot(kept_mid_scale, mid_scale, slot_index, usable)
        kept_out_mean = store_slot(kept_out_mean, out_mean, slot_index, usable)
        kept_out_scale = store_slot(kept_out_scale, out_scale, slot_index, usable)
        results = store_slot(results, result.astype(jnp.float32), slot_index, usable)
        if turn_index < turns - 1:
            incoming, carried = from_behind(
                (result, jnp.where(odd_segment, result, current)), "segment", 1
            )
    gathered = (
        lax.all_gather(space_kernel[0].astype(jnp.bfloat16), "dp", axis=0, tiled=True),
        lax.all_gather(time_kernel[0].astype(jnp.bfloat16), "dp", axis=0, tiled=True),
        lax.all_gather(mid_gain[0].astype(jnp.bfloat16), "dp", axis=0, tiled=True),
        lax.all_gather(mid_bias[0].astype(jnp.bfloat16), "dp", axis=0, tiled=True),
        lax.all_gather(out_gain[0].astype(jnp.bfloat16), "dp", axis=0, tiled=True),
        lax.all_gather(out_bias[0].astype(jnp.bfloat16), "dp", axis=0, tiled=True),
    )
    space_low, time_low = (gathered[0], gathered[1])
    mid_gain_now = gathered[2].astype(jnp.float32)
    mid_bias_now = gathered[3].astype(jnp.float32)
    out_gain_now = gathered[4].astype(jnp.float32)
    out_bias_now = gathered[5].astype(jnp.float32)
    grad_input = jnp.zeros_like(frames)
    grad_skip = jnp.zeros_like(frames)
    space_acc = jnp.zeros(space_low.shape, jnp.float32)
    time_acc = jnp.zeros(time_low.shape, jnp.float32)
    mid_gain_acc = jnp.zeros((hidden_units,), jnp.float32)
    mid_bias_acc = jnp.zeros((hidden_units,), jnp.float32)
    out_gain_acc = jnp.zeros((channels,), jnp.float32)
    out_bias_acc = jnp.zeros((channels,), jnp.float32)
    input_grads = jnp.zeros(block_shape, jnp.float32)
    for turn_index in range(turns):
        micro_index = n_segment - 1 - (turn_index - (n_segment - 1 - segment_index))
        usable = (micro_index >= 0) & (micro_index < n_segment)
        usable_weight = usable.astype(jnp.float32)
        slot_index = jnp.clip(micro_index, 0, n_segment - 1)
        current = pick_slot(kept_input, slot_index)
        skip_input = pick_slot(kept_skip, slot_index)
        before_now = pick_slot(before_mask, slot_index)
        after_now = pick_slot(after_mask, slot_index)
        space_taps, spatial = space_apply(current, space_low)
        mid_normed = (spatial - pick_slot(kept_mid_mean, slot_index)) * pick_slot(
            kept_mid_scale, slot_index
        )
        mid_pre = mid_normed * mid_gain_now + mid_bias_now
        hidden_act = jax.nn.silu(mid_pre).astype(jnp.bfloat16)
        time_taps, temporal = time_apply(hidden_act, time_low, before_now, after_now)
        out_scale = pick_slot(kept_out_scale, slot_index)
        out_normed = (temporal - pick_slot(kept_out_mean, slot_index)) * out_scale
        pre_act = (
            out_normed * out_gain_now
            + out_bias_now
            + jnp.where(odd_segment, skip_input.astype(jnp.float32), 0.0)
        )
        grad_result = jnp.where(
            last_segment,
            pick_slot(cot_stack, slot_index).astype(jnp.float32),
            grad_input.astype(jnp.float32)
            + jnp.where(odd_segment, grad_skip.astype(jnp.float32), 0.0),
        )
        grad_pre = grad_result * silu_slope(pre_act)
        out_bias_sum, out_gain_sum = reduce_back(grad_pre, out_normed)
        grad_temporal = (
            out_gain_now
            * out_scale
            * (grad_pre - out_bias_sum / pixel_count - out_normed * out_gain_sum / pixel_count)
        ).astype(jnp.bfloat16)
        time_acc = time_acc + usable_weight * jnp.einsum(
            "fijc,fijo->co", time_taps, grad_temporal, preferred_element_type=jnp.float32
        )
        grad_hidden = time_back(grad_temporal, time_low, before_now, after_now)
        grad_mid = grad_hidden * silu_slope(mid_pre)
        mid_bias_sum, mid_gain_sum = reduce_back(grad_mid, mid_normed)
        mid_scale = pick_slot(kept_mid_scale, slot_index)
        grad_spatial = (
            mid_gain_now
            * mid_scale
            * (grad_mid - mid_bias_sum / pixel_count - mid_normed * mid_gain_sum / pixel_count)
        ).astype(jnp.bfloat16)
        space_acc = space_acc + usable_weight * jnp.einsum(
            "fijc,fijo->co", space_taps, grad_spatial, preferred_element_type=jnp.float32
        )
        grad_current = space_back(grad_spatial, space_low)
        mid_gain_acc = mid_gain_acc + usable_weight * mid_gain_sum
        mid_bias_acc = mid_bias_acc + usable_weight * mid_bias_sum
        out_gain_acc = out_gain_acc + usable_weight * out_gain_sum
        out_bias_acc = out_bias_acc + usable_weight * out_bias_sum
        input_grads = store_slot(
            input_grads, grad_current + grad_skip.astype(jnp.float32), slot_index, usable
        )
        if turn_index < turns - 1:
            grad_input, grad_skip = from_behind(
                (
                    grad_current.astype(jnp.bfloat16),
                    jnp.where(odd_segment, grad_pre.astype(jnp.bfloat16), grad_skip),
                ),
                "segment",
                -1,
            )
    space_grad, time_grad = (
        lax.psum_scatter(space_acc, "dp", scatter_dimension=0, tiled=True),
        lax.psum_scatter(time_acc, "dp", scatter_dimension=0, tiled=True),
    )
    data_index = lax.axis_index("dp")

    def own_share(full_vector):
        share = full_vector.shape[0] // n_data
        return lax.dynamic_slice_in_dim(full_vector, data_index * share, share)[None]

    flat_shape = (n_segment * frame_count,) + frames.shape[1:]
    arrived_out, arrived_grads = (
        lax.all_to_all(
            results.reshape(flat_shape).astype(jnp.bfloat16),
            "segment",
            split_axis=0,
            concat_axis=0,
            tiled=True,
        ).astype(jnp.float32),
        lax.all_to_all(
            input_grads.reshape(flat_shape).astype(jnp.bfloat16),
            "segment",
            split_axis=0,
            concat_axis=0,
            tiled=True,
        ).astype(jnp.float32),
    )
    output = arrived_out[(n_segment - 1) * frame_count :].astype(jnp.bfloat16)
    frames_grad = arrived_grads[:frame_count]
    return (
        output,
        frames_grad,
        space_grad[None],
        time_grad[None],
        own_share(mid_gain_acc),
        own_share(mid_bias_acc),
        own_share(out_gain_acc),
        own_share(out_bias_acc),
    )


def general(mesh):
    return jax.shard_map(
        on_device_general,
        mesh=mesh,
        in_specs=(
            P(("dp", "segment"), None, None, None),
            P(("dp", "segment"), None, None, None),
            P(("dp", "segment")),
            P("segment", "dp", None),
            P("segment", "dp", None),
            P("segment", "dp"),
            P("segment", "dp"),
            P("segment", "dp"),
            P("segment", "dp"),
        ),
        out_specs=(
            P(("dp", "segment"), None, None, None),
            P(("dp", "segment"), None, None, None),
            P("segment", "dp", None),
            P("segment", "dp", None),
            P("segment", "dp"),
            P("segment", "dp"),
            P("segment", "dp"),
            P("segment", "dp"),
        ),
        check_vma=False,
    )


def solution(mesh):
    if mesh.shape["dp"] != 8 or mesh.shape["segment"] != 4:
        return general(mesh)
    n_dp, n_seg = mesh.shape["dp"], mesh.shape["segment"]
    fine = Mesh(mesh.devices.reshape(n_dp // 2, 2, 2, n_seg // 2), EVERY)
    dp, seg = ("z", "y"), ("x", "c")
    return jax.shard_map(
        on_device,
        mesh=fine,
        in_specs=(
            P(EVERY, None, None, None),
            P(EVERY, None, None, None),
            P(EVERY),
            P(seg, dp, None),
            P(seg, dp, None),
            P(seg, dp),
            P(seg, dp),
            P(seg, dp),
            P(seg, dp),
        ),
        out_specs=(
            P(EVERY, None, None, None),
            P(EVERY, None, None, None),
            P(seg, dp, None),
            P(seg, dp, None),
            P(seg, dp),
            P(seg, dp),
            P(seg, dp),
            P(seg, dp),
        ),
        check_vma=False,
    )
```

```python
import functools

import jax
import jax.numpy as jnp
from jax import lax
from jax.experimental import pallas as pl
from jax.experimental.pallas import tpu as pltpu
from jax.sharding import Mesh, PartitionSpec as P

eps = 1e-05
PLANE = ("y", "x", "c")
EVERY = ("z", "y", "x", "c")
BF = jnp.bfloat16
F32 = jnp.float32


def nt(a, b):
    return lax.dot_general(a, b, (((1,), (1,)), ((), ())), preferred_element_type=F32)


def nn(a, b):
    return lax.dot_general(a, b, (((1,), (0,)), ((), ())), preferred_element_type=F32)


VMEM_CAP = 56 * 1024 * 1024
ANY = pl.BlockSpec(memory_space=pl.ANY)


def call(body, outs, scratch, flops, *args, deps=(), far=(), far_outs=()):
    moved = sum(a.size * a.dtype.itemsize for a in args) + sum(
        o.size * o.dtype.itemsize for o in outs
    )
    n = len(deps)

    def spec(a):
        return pl.BlockSpec(memory_space=pltpu.SMEM if a.dtype == jnp.int32 else pltpu.VMEM)

    return pl.pallas_call(
        lambda *refs: body(*refs[n:]),
        out_shape=outs,
        in_specs=[ANY] * n + [ANY if i in far else spec(a) for i, a in enumerate(args)],
        out_specs=[ANY if i in far_outs else spec(o) for i, o in enumerate(outs)],
        scratch_shapes=scratch,
        compiler_params=pltpu.CompilerParams(vmem_limit_bytes=VMEM_CAP),
        cost_estimate=pl.CostEstimate(flops=flops, bytes_accessed=moved, transcendentals=0),
    )(*deps, *args)


def chunk(i, size):
    return pl.ds(pl.multiple_of(i * size, 16), size)


def clear_borders(pad_ref, side, plane, nf):
    zrow = jnp.zeros(pad_ref.shape[1:], BF)
    pad_ref[0] = zrow
    pad_ref[side + 1] = zrow
    zcol = jnp.zeros((nf, pad_ref.shape[2]), BF)
    for i in range(side):
        pad_ref[i + 1, 0:nf] = zcol
        pad_ref[i + 1, nf + plane : 2 * nf + plane] = zcol


def by_rank(slices, rank):
    odd = lax.rem(rank, 2) == 1
    for p in range(len(slices) // 2):
        a, b = slices[2 * p], slices[2 * p + 1]
        yield lax.bitwise_xor(rank // 2, p), odd, a, b


def halves(odd, own, mate):
    low = lax.broadcasted_iota(jnp.int32, own.shape, 1) < 64
    own, mate = own.astype(F32), mate.astype(F32)
    a, b = jnp.where(odd, mate, own), jnp.where(odd, own, mate)
    top = jnp.where(low, a, pltpu.roll(b, 64, 1))
    bottom = jnp.where(low, pltpu.roll(a, 64, 1), b)
    return top, bottom


def store_packed(rank, mate_ref, keep_ref, part, k, step, low):
    rows_now = chunk(k, step)
    odd = lax.rem(rank, 2) == 1
    for q in range(keep_ref.shape[0]):
        x = part[:step, 128 * q : 128 * q + 128]
        y = part[step:, 128 * q : 128 * q + 128]
        even_slice = jnp.where(low, x, pltpu.roll(y, 64, 1))
        odd_slice = jnp.where(low, pltpu.roll(x, 64, 1), y)
        p = lax.bitwise_xor(rank // 2, q)
        keep_ref[p, rows_now, :] = jnp.where(odd, odd_slice, even_slice).astype(BF)
        mate_ref[p, rows_now, :] = jnp.where(odd, even_slice, odd_slice).astype(BF)


def fetch_kernels(w_ref, ktm_ref, lw_ref, sems):
    nz, _, width = w_ref.shape
    hc = ktm_ref.shape[0]
    copies = []
    for z in range(nz):
        copies.append(pltpu.make_async_copy(
            w_ref.at[z, pl.ds(0, hc)], ktm_ref.at[:, pl.ds(z * width, width)], sems.at[2 * z]))
        copies.append(pltpu.make_async_copy(
            w_ref.at[z, pl.ds(hc, lw_ref.shape[1])], lw_ref.at[z], sems.at[2 * z + 1]))
    for copy in copies:
        copy.start()
    return copies


def join_temporal(lw_ref, lf_ref, ltm_ref):
    ch = ltm_ref.shape[1]
    width = lw_ref.shape[2] // 2
    count = 2 * lw_ref.shape[0]
    size = ltm_ref.shape[0] // count
    for z in range(lw_ref.shape[0]):
        first = lw_ref[z, :, 0:ch].astype(F32)
        off = width % 128
        second = lw_ref[z, :, width - off : width - off + ch + 128].astype(F32)
        second = pltpu.roll(second, ch + 128 - off, 1)[:, 0:ch]
        for b, block in ((2 * z, first), (2 * z + 1, second)):
            lf_ref[b * size : b * size + block.shape[0], :] = block
    ltm_ref[...] = lf_ref[0 : ltm_ref.shape[0], :].astype(BF)


def conv_body(side, first, rank_ref, *refs):
    n = 1 if first else 8
    slices = refs[:n]
    (w_ref, vec_ref, before_ref, after_ref,
     pad_out, hid_out, xhat_out, rs_ref, mate_ref, keep_ref,
     pad_ref, hid_ref, xhat_ref, sp_ref, ktm_ref, lw_ref, lf_ref, ltm_ref, kn_ref, sems) = refs[n:]
    rank = rank_ref[0]
    nz = 2 * w_ref.shape[0]
    fetched = fetch_kernels(w_ref, ktm_ref, lw_ref, sems)
    ch, hc = pad_ref.shape[2], hid_ref.shape[1]
    rows = hid_ref.shape[0]
    plane = rows // side
    nf = plane // side
    step = plane // 2
    clear_borders(pad_ref, side, plane, nf)
    if first:
        for i in range(side):
            pad_ref[i + 1, nf : nf + plane] = slices[0][i * plane : (i + 1) * plane]
    else:
        def place(k, carry):
            for q, odd, a_ref, b_ref in by_rank(slices, rank):
                top, bottom = halves(odd, a_ref[chunk(k, step), :], b_ref[chunk(k, step), :])
                lanes = pl.ds(pl.multiple_of(128 * q, 128), 128)
                for piece, kk in ((top, k), (bottom, k + side)):
                    at = nf + lax.rem(kk, 2) * step
                    pad_ref[1 + kk // 2, pl.ds(pl.multiple_of(at, 16), step), lanes] = piece.astype(BF)
            return carry

        lax.fori_loop(0, side, place, 0, unroll=True)
    pad_copy = pltpu.make_async_copy(pad_ref, pad_out, sems.at[nz])
    pad_copy.start()
    for copy in fetched:
        copy.wait()
    for t in range(9):
        kn_ref[t] = ktm_ref[:, t * ch : (t + 1) * ch].astype(F32).T.astype(BF)
    join_temporal(lw_ref, lf_ref, ltm_ref)

    def conv(i, total):
        acc = jnp.zeros((plane, hc), F32)
        for t in range(9):
            r, c = t // 3, t % 3
            acc += nn(pad_ref[i + r, c * nf : c * nf + plane, :], kn_ref[t])
        sp_ref[i] = acc
        return total + jnp.sum(acc, axis=0, keepdims=True)

    mean = lax.fori_loop(0, side, conv, jnp.zeros((1, hc), F32), unroll=True) / rows

    def square(i, total):
        cen = sp_ref[i] - mean
        return total + jnp.sum(cen * cen, axis=0, keepdims=True)

    var = lax.fori_loop(0, side, square, jnp.zeros((1, hc), F32), unroll=True) / rows
    rs = lax.rsqrt(var + eps)
    rs_ref[...] = rs
    gain, bias = vec_ref[0:1, :], vec_ref[1:2, :]

    def act(i, carry):
        xhat = (sp_ref[i] - mean) * rs
        xhat_ref[i] = xhat
        v = xhat * gain + bias
        v = v * jax.nn.sigmoid(v)
        sp_ref[i] = v
        hid_ref[chunk(i, plane), :] = v.astype(BF)
        return carry

    lax.fori_loop(0, side, act, 0, unroll=True)
    late = [
        pltpu.make_async_copy(hid_ref, hid_out, sems.at[nz + 1]),
        pltpu.make_async_copy(xhat_ref, xhat_out, sems.at[nz + 2]),
    ]
    for copy in late:
        copy.start()
    low = lax.broadcasted_iota(jnp.int32, (step, 128), 1) < 64

    def temporal(k, carry):
        pieces = []
        for kk in (k, k + side):
            par = lax.rem(kk, 2)
            h = sp_ref[kk // 2, pl.ds(pl.multiple_of(par * step, 8), step), :]
            at = pl.multiple_of(par * (step % nf), 8)
            pieces.append((
                (pltpu.roll(h, 1, 0) * before_ref[pl.ds(at, step), :]).astype(BF),
                h.astype(BF),
                (pltpu.roll(h, step - 1, 0) * after_ref[pl.ds(at, step), :]).astype(BF),
            ))
        part = sum(
            nn(jnp.concatenate([x, y], axis=0), ltm_ref[t * hc : (t + 1) * hc])
            for t, (x, y) in enumerate(zip(*pieces))
        )
        store_packed(rank, mate_ref, keep_ref, part, k, step, low)
        return carry

    lax.fori_loop(0, side, temporal, 0, unroll=True)
    for copy in [pad_copy] + late:
        copy.wait()


def kernel_scratch(w, hc, ch):
    return [
        pltpu.VMEM((hc, 9 * ch), BF),
        pltpu.VMEM((w.shape[0], w.shape[1] - hc, w.shape[2]), BF),
        pltpu.VMEM((3 * hc + w.shape[1] - hc, ch), F32),
        pltpu.VMEM((3 * hc, ch), BF),
    ]


def conv_forward(rank, g, w, vec, before, after, side, pixels, ch, deps=()):
    hc = vec.shape[1]
    plane = pixels // side
    nf = plane // side
    n = len(g)
    shapes = [
        ((side + 2, plane + 2 * nf, ch), BF),
        ((pixels, hc), BF),
        ((side, plane, hc), F32),
    ]
    outs = [jax.ShapeDtypeStruct(*s) for s in shapes] + [
        jax.ShapeDtypeStruct((1, hc), F32),
        jax.ShapeDtypeStruct((4, pixels // 2, 128), BF),
        jax.ShapeDtypeStruct((4, pixels // 2, 128), BF),
    ]
    scratch = [pltpu.VMEM(*s) for s in shapes] + [
        pltpu.VMEM((side, plane, hc), F32),
        *kernel_scratch(w, hc, ch),
        pltpu.VMEM((9, ch, hc), BF),
        pltpu.SemaphoreType.DMA((2 * w.shape[0] + 3,)),
    ]
    flops = 2 * pixels * hc * 12 * ch
    return call(functools.partial(conv_body, side, n == 1), outs, scratch, flops,
                rank, *g, w, vec, before, after,
                deps=deps, far=(n + 1,), far_outs=(0, 1, 2))


def fold(v):
    return v + pltpu.roll(v, 64, 1)


def total_of(refs):
    t = refs[0][...].astype(F32)
    for ref in refs[1:]:
        t += ref[...].astype(F32)
    return t


def pair_sum_body(keep_ref, mate_ref, *out_refs):
    for p, ref in enumerate(out_refs):
        ref[...] = (keep_ref[p].astype(F32) + mate_ref[p].astype(F32)).astype(ref.dtype)


def pair_sum(keep, arrived):
    shape = keep.shape[1:]
    outs = [jax.ShapeDtypeStruct(shape, BF)] * keep.shape[0]
    return call(pair_sum_body, outs, [], keep.size, keep, arrived)


def out_norm_body(n, has_skip, *refs):
    parts, refs = refs[:n], refs[n:]
    if has_skip:
        vec_ref, skip_ref, xhat_ref, rs_ref, pre_ref, res_ref = refs
    else:
        vec_ref, xhat_ref, rs_ref, pre_ref, res_ref = refs
    t = total_of(parts)
    pixels = 2 * t.shape[0]
    mean = fold(jnp.sum(t, axis=0, keepdims=True)) / pixels
    cen = t - mean
    rs = lax.rsqrt(fold(jnp.sum(cen * cen, axis=0, keepdims=True)) / pixels + eps)
    xhat = cen * rs
    pre = xhat * vec_ref[0:1, :] + vec_ref[1:2, :]
    if has_skip:
        pre = pre + skip_ref[...].astype(F32)
    xhat_ref[...] = xhat
    rs_ref[...] = rs
    pre_ref[...] = pre
    res_ref[...] = (pre * jax.nn.sigmoid(pre)).astype(BF)


def out_norm(parts, vec, skip):
    half = parts[0].shape[0]
    outs = [
        jax.ShapeDtypeStruct((half, 128), F32),
        jax.ShapeDtypeStruct((1, 128), F32),
        jax.ShapeDtypeStruct((half, 128), F32),
        jax.ShapeDtypeStruct((half, 128), BF),
    ]
    args = (*parts, vec) + (() if skip is None else (skip,))
    body = functools.partial(out_norm_body, len(parts), skip is not None)
    return call(body, outs, [], half * 128 * 10, *args)


def out_back_body(n, *refs):
    parts, (pre_ref, xhat_ref, rs_ref, vec_ref, dpre_ref, dt_ref, sums_ref) = refs[:n], refs[n:]
    g = total_of(parts)
    pre, xhat = pre_ref[...], xhat_ref[...]
    sig = jax.nn.sigmoid(pre)
    dpre = g * (sig * (1.0 + pre * (1.0 - sig)))
    pixels = 2 * pre.shape[0]
    sb = fold(jnp.sum(dpre, axis=0, keepdims=True))
    sg = fold(jnp.sum(dpre * xhat, axis=0, keepdims=True))
    dpre_ref[...] = dpre.astype(BF)
    scale = vec_ref[0:1, :] * rs_ref[...]
    dt_ref[...] = (scale * (dpre - sb / pixels - xhat * (sg / pixels))).astype(BF)
    sums_ref[0:1, :] = sg
    sums_ref[1:2, :] = sb


def out_back(parts, pre, xhat, rs, vec, deps=()):
    half = pre.shape[0]
    outs = [
        jax.ShapeDtypeStruct((half, 128), BF),
        jax.ShapeDtypeStruct((half, 128), BF),
        jax.ShapeDtypeStruct((2, 128), F32),
    ]
    args = (*parts, pre, xhat, rs, vec)
    return call(functools.partial(out_back_body, len(parts)), outs, [], half * 1280, *args, deps=deps)


def conv_back_body(side, rank_ref, *refs):
    slices, (xhat_in, rs_ref, w_ref, vec_ref, before_ref, after_ref,
             dt_out, ds_out, sums_ref, mate_ref, keep_ref,
             dt_ref, ds_ref, xhat_ref, dy_ref, pad_ref, ktm_ref, lw_ref, lf_ref, ltm_ref, lnt_ref,
             sems) = (refs[:8], refs[8:])
    half = slices[0].shape[0]
    rank = rank_ref[0]
    nz = 2 * w_ref.shape[0]
    rows = 2 * half
    plane = rows // side
    nf = plane // side
    step = plane // 2
    hc = ds_ref.shape[1]
    ch = dt_ref.shape[1]
    fetched = fetch_kernels(w_ref, ktm_ref, lw_ref, sems)
    xhat_copy = pltpu.make_async_copy(xhat_in, xhat_ref, sems.at[nz])
    xhat_copy.start()
    clear_borders(pad_ref, side, plane, nf)

    def place(k, carry):
        for q, odd, a_ref, b_ref in by_rank(slices, rank):
            top, bottom = halves(odd, a_ref[chunk(k, step), :], b_ref[chunk(k, step), :])
            lanes = pl.ds(pl.multiple_of(128 * q, 128), 128)
            dt_ref[chunk(k, step), lanes] = top.astype(BF)
            dt_ref[pl.ds(pl.multiple_of(half + k * step, 16), step), lanes] = bottom.astype(BF)
        return carry

    lax.fori_loop(0, side, place, 0, unroll=True)
    dt_copy = pltpu.make_async_copy(dt_ref, dt_out, sems.at[nz + 1])
    dt_copy.start()
    for copy in fetched + [xhat_copy]:
        copy.wait()
    join_temporal(lw_ref, lf_ref, ltm_ref)
    for t in range(3):
        lnt_ref[t] = ltm_ref[t * hc : (t + 1) * hc].astype(F32).T.astype(BF)
    gain, bias = vec_ref[0:1, :], vec_ref[1:2, :]

    def hidden_grad(i, sums):
        dt = dt_ref[chunk(i, plane), :]
        early = nn(dt, lnt_ref[0]) * before_ref[0:plane, :]
        late = nn(dt, lnt_ref[2]) * after_ref[0:plane, :]
        dh = nn(dt, lnt_ref[1]) + pltpu.roll(early, plane - 1, 0) + pltpu.roll(late, 1, 0)
        xhat = xhat_ref[i]
        v = xhat * gain + bias
        sig = jax.nn.sigmoid(v)
        dy = dh * (sig * (1.0 + v * (1.0 - sig)))
        dy_ref[i] = dy
        return (
            sums[0] + jnp.sum(dy * xhat, axis=0, keepdims=True),
            sums[1] + jnp.sum(dy, axis=0, keepdims=True),
        )

    zero = jnp.zeros((1, hc), F32)
    sg, sb = lax.fori_loop(0, side, hidden_grad, (zero, zero), unroll=True)
    sums_ref[0:1, :] = sg
    sums_ref[1:2, :] = sb
    scale = gain * rs_ref[...]

    def spatial_grad(i, carry):
        ds = (scale * (dy_ref[i] - sb / rows - xhat_ref[i] * (sg / rows))).astype(BF)
        pad_ref[i + 1, nf : nf + plane] = ds
        ds_ref[chunk(i, plane), :] = ds
        return carry

    lax.fori_loop(0, side, spatial_grad, 0, unroll=True)
    ds_copy = pltpu.make_async_copy(ds_ref, ds_out, sems.at[nz + 2])
    ds_copy.start()
    low = lax.broadcasted_iota(jnp.int32, (step, 128), 1) < 64

    def back(k, carry):
        acc = jnp.zeros((2 * step, ch), F32)
        for t in range(9):
            r, c = 2 - t // 3, 2 - t % 3
            pieces = []
            for kk in (k, k + side):
                at = c * nf + lax.rem(kk, 2) * step
                pieces.append(pad_ref[kk // 2 + r, pl.ds(pl.multiple_of(at, 16), step), :])
            acc += nn(jnp.concatenate(pieces, axis=0), ktm_ref[:, t * ch : (t + 1) * ch])
        store_packed(rank, mate_ref, keep_ref, acc, k, step, low)
        return carry

    lax.fori_loop(0, side, back, 0, unroll=True)
    dt_copy.wait()
    ds_copy.wait()


def conv_back(rank, g, xhat, rs, w, vec, before, after, side, deps=()):
    half = g[0].shape[0]
    hc = vec.shape[1]
    ch = len(g) * 64
    pixels = 2 * half
    plane = pixels // side
    nf = plane // side
    outs = [
        jax.ShapeDtypeStruct((pixels, ch), BF),
        jax.ShapeDtypeStruct((pixels, hc), BF),
        jax.ShapeDtypeStruct((2, hc), F32),
        jax.ShapeDtypeStruct((4, half, 128), BF),
        jax.ShapeDtypeStruct((4, half, 128), BF),
    ]
    scratch = [
        pltpu.VMEM((pixels, ch), BF),
        pltpu.VMEM((pixels, hc), BF),
        pltpu.VMEM((side, plane, hc), F32),
        pltpu.VMEM((side, plane, hc), F32),
        pltpu.VMEM((side + 2, plane + 2 * nf, hc), BF),
        *kernel_scratch(w, hc, ch),
        pltpu.VMEM((3, ch, hc), BF),
        pltpu.SemaphoreType.DMA((2 * w.shape[0] + 3,)),
    ]
    flops = 2 * pixels * hc * 12 * ch
    return call(functools.partial(conv_back_body, side), outs, scratch, flops,
                rank, *g, xhat, rs, w, vec, before, after,
                deps=deps, far=(9, 11), far_outs=(0, 1))


def grads_body(side, pad_ref, hid_ref, ds_ref, dt_ref, before_ref, after_ref, mid_ref, out_ref,
               sg_ref, dst_ref, taps_ref, tg_ref, vec_ref):
    ch = pad_ref.shape[2]
    hc = hid_ref.shape[1]
    plane = hid_ref.shape[0] // side
    nf = plane // side
    for i in (0, 1, side + 2, side + 3):
        dst_ref[i] = jnp.zeros(dst_ref.shape[1:], BF)
    for i in range(side):
        at = slice(i * plane, (i + 1) * plane)
        h = hid_ref[at, :].astype(F32)
        taps_ref[i, 0:hc] = (pltpu.roll(h, 1, 0) * before_ref[0:plane, :]).T.astype(BF)
        taps_ref[i, hc : 2 * hc] = h.T.astype(BF)
        taps_ref[i, 2 * hc : 3 * hc] = (pltpu.roll(h, plane - 1, 0) * after_ref[0:plane, :]).T.astype(BF)
        dst_ref[i + 2] = ds_ref[at, :].astype(F32).T.astype(BF)
    tg_ref[0 : 3 * hc, :] = sum(
        nn(taps_ref[i], dt_ref[i * plane : (i + 1) * plane, :]) for i in range(side)
    )
    tg_ref[3 * hc :, :] = jnp.zeros((tg_ref.shape[0] - 3 * hc, ch), F32)
    nz, _, width = sg_ref.shape
    size = 3 * hc // (2 * nz)
    vec_ref[...] = jnp.zeros(vec_ref.shape, F32)
    vec_ref[size : size + 2, 0:hc] = mid_ref[...]
    vec_ref[size + 2 : size + 4, 0:128] = out_ref[...]
    tall = vec_ref.shape[0]
    inside = lax.broadcasted_iota(jnp.int32, (tall, ch), 0) < size
    off = (width // 2) % 128
    for z in range(nz):
        first, second = [
            jnp.where(inside, tg_ref[b * size : b * size + tall, :], vec_ref[...])
            for b in (2 * z, 2 * z + 1)
        ]
        start = width // 2 - off
        sg_ref[z, hc : hc + tall, 0:ch] = first.astype(BF)
        second = pltpu.roll(jnp.concatenate([second, jnp.zeros((tall, 128), F32)], axis=1), off, 1)
        sg_ref[z, hc : hc + tall, start : start + ch + 128] = second.astype(BF)
    for c in range(3):
        acc = sum(
            nn(dst_ref[i : i + 3].reshape(3 * hc, plane), pad_ref[i, c * nf : c * nf + plane, :])
            for i in range(1, side + 1)
        )
        for r in range(3):
            first = (3 * r + c) * ch
            end = first + ch
            at = (2 - r) * hc
            done = 0
            while first < end:
                z = first // width
                last = min(end, (z + 1) * width)
                sg_ref[z, 0:hc, first - z * width : last - z * width] = (
                    acc[at : at + hc, done : done + last - first].astype(BF)
                )
                done += last - first
                first = last


def kernel_grads(pad, hidden, ds, dt, before, after, mid, out, side, shape, deps=()):
    pixels, hc = hidden.shape
    ch = dt.shape[1]
    plane = pixels // side
    outs = [jax.ShapeDtypeStruct(shape, BF)]
    tall = shape[1] - hc
    scratch = [
        pltpu.VMEM((side + 4, hc, plane), BF),
        pltpu.VMEM((side, 3 * hc, plane), BF),
        pltpu.VMEM((3 * hc + tall, ch), F32),
        pltpu.VMEM((tall, ch), F32),
    ]
    flops = 2 * pixels * hc * 12 * ch
    return call(functools.partial(grads_body, side), outs, scratch, flops,
                pad, hidden, ds, dt, before, after, mid, out, deps=deps)[0]


def copy_after_body(v_ref, out_ref):
    out_ref[...] = v_ref[...]


def after_all(v, *deps):
    return call(copy_after_body, [jax.ShapeDtypeStruct(v.shape, v.dtype)], [], v.size, v, deps=deps)[0]


def call(body, outs, scratch, flops, *args, deps=(), far=(), far_outs=()):
    moved = sum(a.size * a.dtype.itemsize for a in args) + sum(
        o.size * o.dtype.itemsize for o in outs
    )
    n = len(deps)

    def spec(a):
        return pl.BlockSpec(memory_space=pltpu.SMEM if a.dtype == jnp.int32 else pltpu.VMEM)

    return pl.pallas_call(
        lambda *refs: body(*refs[n:]),
        out_shape=outs,
        in_specs=[ANY] * n + [ANY if i in far else spec(a) for i, a in enumerate(args)],
        out_specs=[ANY if i in far_outs else spec(o) for i, o in enumerate(outs)],
        scratch_shapes=scratch,
        compiler_params=pltpu.CompilerParams(vmem_limit_bytes=VMEM_CAP),
        cost_estimate=pl.CostEstimate(flops=flops, bytes_accessed=moved, transcendentals=0),
    )(*deps, *args)


def chunk(i, size):
    return pl.ds(pl.multiple_of(i * size, 16), size)


def clear_borders(pad_ref, side, plane, nf):
    zrow = jnp.zeros(pad_ref.shape[1:], BF)
    pad_ref[0] = zrow
    pad_ref[side + 1] = zrow
    zcol = jnp.zeros((nf, pad_ref.shape[2]), BF)
    for i in range(side):
        pad_ref[i + 1, 0:nf] = zcol
        pad_ref[i + 1, nf + plane : 2 * nf + plane] = zcol


def by_rank(slices, rank):
    odd = lax.rem(rank, 2) == 1
    for p in range(len(slices) // 2):
        a, b = slices[2 * p], slices[2 * p + 1]
        yield lax.bitwise_xor(rank // 2, p), odd, a, b


def halves(odd, own, mate):
    low = lax.broadcasted_iota(jnp.int32, own.shape, 1) < 64
    own, mate = own.astype(F32), mate.astype(F32)
    a, b = jnp.where(odd, mate, own), jnp.where(odd, own, mate)
    top = jnp.where(low, a, pltpu.roll(b, 64, 1))
    bottom = jnp.where(low, pltpu.roll(a, 64, 1), b)
    return top, bottom


def store_packed(rank, mate_ref, keep_ref, part, k, step, low):
    rows_now = chunk(k, step)
    odd = lax.rem(rank, 2) == 1
    for q in range(keep_ref.shape[0]):
        x = part[:step, 128 * q : 128 * q + 128]
        y = part[step:, 128 * q : 128 * q + 128]
        even_slice = jnp.where(low, x, pltpu.roll(y, 64, 1))
        odd_slice = jnp.where(low, pltpu.roll(x, 64, 1), y)
        p = lax.bitwise_xor(rank // 2, q)
        keep_ref[p, rows_now, :] = jnp.where(odd, odd_slice, even_slice).astype(BF)
        mate_ref[p, rows_now, :] = jnp.where(odd, even_slice, odd_slice).astype(BF)


def fetch_kernels(w_ref, ktm_ref, lw_ref, sems):
    nz, _, width = w_ref.shape
    hc = ktm_ref.shape[0]
    copies = []
    for z in range(nz):
        copies.append(pltpu.make_async_copy(
            w_ref.at[z, pl.ds(0, hc)], ktm_ref.at[:, pl.ds(z * width, width)], sems.at[2 * z]))
        copies.append(pltpu.make_async_copy(
            w_ref.at[z, pl.ds(hc, lw_ref.shape[1])], lw_ref.at[z], sems.at[2 * z + 1]))
    for copy in copies:
        copy.start()
    return copies


def join_temporal(lw_ref, lf_ref, ltm_ref):
    ch = ltm_ref.shape[1]
    width = lw_ref.shape[2] // 2
    count = 2 * lw_ref.shape[0]
    size = ltm_ref.shape[0] // count
    for z in range(lw_ref.shape[0]):
        first = lw_ref[z, :, 0:ch].astype(F32)
        off = width % 128
        second = lw_ref[z, :, width - off : width - off + ch + 128].astype(F32)
        second = pltpu.roll(second, ch + 128 - off, 1)[:, 0:ch]
        for b, block in ((2 * z, first), (2 * z + 1, second)):
            lf_ref[b * size : b * size + block.shape[0], :] = block
    ltm_ref[...] = lf_ref[0 : ltm_ref.shape[0], :].astype(BF)


def conv_body(side, first, rank_ref, *refs):
    n = 1 if first else 8
    slices = refs[:n]
    (w_ref, vec_ref, before_ref, after_ref,
     pad_out, hid_out, xhat_out, rs_ref, mate_ref, keep_ref,
     pad_ref, hid_ref, xhat_ref, sp_ref, ktm_ref, lw_ref, lf_ref, ltm_ref, kn_ref, sems) = refs[n:]
    rank = rank_ref[0]
    nz = 2 * w_ref.shape[0]
    fetched = fetch_kernels(w_ref, ktm_ref, lw_ref, sems)
    ch, hc = pad_ref.shape[2], hid_ref.shape[1]
    rows = hid_ref.shape[0]
    plane = rows // side
    nf = plane // side
    step = plane // 2
    clear_borders(pad_ref, side, plane, nf)
    if first:
        for i in range(side):
            pad_ref[i + 1, nf : nf + plane] = slices[0][i * plane : (i + 1) * plane]
    else:
        def place(k, carry):
            for q, odd, a_ref, b_ref in by_rank(slices, rank):
                top, bottom = halves(odd, a_ref[chunk(k, step), :], b_ref[chunk(k, step), :])
                lanes = pl.ds(pl.multiple_of(128 * q, 128), 128)
                for piece, kk in ((top, k), (bottom, k + side)):
                    at = nf + lax.rem(kk, 2) * step
                    pad_ref[1 + kk // 2, pl.ds(pl.multiple_of(at, 16), step), lanes] = piece.astype(BF)
            return carry

        lax.fori_loop(0, side, place, 0, unroll=True)
    pad_copy = pltpu.make_async_copy(pad_ref, pad_out, sems.at[nz])
    pad_copy.start()
    for copy in fetched:
        copy.wait()
    for t in range(9):
        kn_ref[t] = ktm_ref[:, t * ch : (t + 1) * ch].astype(F32).T.astype(BF)
    join_temporal(lw_ref, lf_ref, ltm_ref)

    def conv(i, total):
        acc = jnp.zeros((plane, hc), F32)
        for t in range(9):
            r, c = t // 3, t % 3
            acc += nn(pad_ref[i + r, c * nf : c * nf + plane, :], kn_ref[t])
        sp_ref[i] = acc
        return total + jnp.sum(acc, axis=0, keepdims=True)

    mean = lax.fori_loop(0, side, conv, jnp.zeros((1, hc), F32), unroll=True) / rows

    def square(i, total):
        cen = sp_ref[i] - mean
        return total + jnp.sum(cen * cen, axis=0, keepdims=True)

    var = lax.fori_loop(0, side, square, jnp.zeros((1, hc), F32), unroll=True) / rows
    rs = lax.rsqrt(var + eps)
    rs_ref[...] = rs
    gain, bias = vec_ref[0:1, :], vec_ref[1:2, :]

    def act(i, carry):
        xhat = (sp_ref[i] - mean) * rs
        xhat_ref[i] = xhat
        v = xhat * gain + bias
        v = v * jax.nn.sigmoid(v)
        sp_ref[i] = v
        hid_ref[chunk(i, plane), :] = v.astype(BF)
        return carry

    lax.fori_loop(0, side, act, 0, unroll=True)
    late = [
        pltpu.make_async_copy(hid_ref, hid_out, sems.at[nz + 1]),
        pltpu.make_async_copy(xhat_ref, xhat_out, sems.at[nz + 2]),
    ]
    for copy in late:
        copy.start()
    low = lax.broadcasted_iota(jnp.int32, (step, 128), 1) < 64

    def temporal(k, carry):
        pieces = []
        for kk in (k, k + side):
            par = lax.rem(kk, 2)
            h = sp_ref[kk // 2, pl.ds(pl.multiple_of(par * step, 8), step), :]
            at = pl.multiple_of(par * (step % nf), 8)
            pieces.append((
                (pltpu.roll(h, 1, 0) * before_ref[pl.ds(at, step), :]).astype(BF),
                h.astype(BF),
                (pltpu.roll(h, step - 1, 0) * after_ref[pl.ds(at, step), :]).astype(BF),
            ))
        part = sum(
            nn(jnp.concatenate([x, y], axis=0), ltm_ref[t * hc : (t + 1) * hc])
            for t, (x, y) in enumerate(zip(*pieces))
        )
        store_packed(rank, mate_ref, keep_ref, part, k, step, low)
        return carry

    lax.fori_loop(0, side, temporal, 0, unroll=True)
    for copy in [pad_copy] + late:
        copy.wait()


def kernel_scratch(w, hc, ch):
    return [
        pltpu.VMEM((hc, 9 * ch), BF),
        pltpu.VMEM((w.shape[0], w.shape[1] - hc, w.shape[2]), BF),
        pltpu.VMEM((3 * hc + w.shape[1] - hc, ch), F32),
        pltpu.VMEM((3 * hc, ch), BF),
    ]


def conv_forward(rank, g, w, vec, before, after, side, pixels, ch, deps=()):
    hc = vec.shape[1]
    plane = pixels // side
    nf = plane // side
    n = len(g)
    shapes = [
        ((side + 2, plane + 2 * nf, ch), BF),
        ((pixels, hc), BF),
        ((side, plane, hc), F32),
    ]
    outs = [jax.ShapeDtypeStruct(*s) for s in shapes] + [
        jax.ShapeDtypeStruct((1, hc), F32),
        jax.ShapeDtypeStruct((4, pixels // 2, 128), BF),
        jax.ShapeDtypeStruct((4, pixels // 2, 128), BF),
    ]
    scratch = [pltpu.VMEM(*s) for s in shapes] + [
        pltpu.VMEM((side, plane, hc), F32),
        *kernel_scratch(w, hc, ch),
        pltpu.VMEM((9, ch, hc), BF),
        pltpu.SemaphoreType.DMA((2 * w.shape[0] + 3,)),
    ]
    flops = 2 * pixels * hc * 12 * ch
    return call(functools.partial(conv_body, side, n == 1), outs, scratch, flops,
                rank, *g, w, vec, before, after,
                deps=deps, far=(n + 1,), far_outs=(0, 1, 2))


def fold(v):
    return v + pltpu.roll(v, 64, 1)


def total_of(refs):
    t = refs[0][...].astype(F32)
    for ref in refs[1:]:
        t += ref[...].astype(F32)
    return t


def pair_sum_body(keep_ref, mate_ref, *out_refs):
    for p, ref in enumerate(out_refs):
        ref[...] = (keep_ref[p].astype(F32) + mate_ref[p].astype(F32)).astype(ref.dtype)


def pair_sum(keep, arrived):
    shape = keep.shape[1:]
    outs = [jax.ShapeDtypeStruct(shape, BF)] * keep.shape[0]
    return call(pair_sum_body, outs, [], keep.size, keep, arrived)


def out_norm_body(n, has_skip, *refs):
    parts, refs = refs[:n], refs[n:]
    if has_skip:
        vec_ref, skip_ref, xhat_ref, rs_ref, pre_ref, res_ref = refs
    else:
        vec_ref, xhat_ref, rs_ref, pre_ref, res_ref = refs
    t = total_of(parts)
    pixels = 2 * t.shape[0]
    mean = fold(jnp.sum(t, axis=0, keepdims=True)) / pixels
    cen = t - mean
    rs = lax.rsqrt(fold(jnp.sum(cen * cen, axis=0, keepdims=True)) / pixels + eps)
    xhat = cen * rs
    pre = xhat * vec_ref[0:1, :] + vec_ref[1:2, :]
    if has_skip:
        pre = pre + skip_ref[...].astype(F32)
    xhat_ref[...] = xhat
    rs_ref[...] = rs
    pre_ref[...] = pre
    res_ref[...] = (pre * jax.nn.sigmoid(pre)).astype(BF)


def out_norm(parts, vec, skip):
    half = parts[0].shape[0]
    outs = [
        jax.ShapeDtypeStruct((half, 128), F32),
        jax.ShapeDtypeStruct((1, 128), F32),
        jax.ShapeDtypeStruct((half, 128), F32),
        jax.ShapeDtypeStruct((half, 128), BF),
    ]
    args = (*parts, vec) + (() if skip is None else (skip,))
    body = functools.partial(out_norm_body, len(parts), skip is not None)
    return call(body, outs, [], half * 128 * 10, *args)


def out_back_body(n, *refs):
    parts, (pre_ref, xhat_ref, rs_ref, vec_ref, dpre_ref, dt_ref, sums_ref) = refs[:n], refs[n:]
    g = total_of(parts)
    pre, xhat = pre_ref[...], xhat_ref[...]
    sig = jax.nn.sigmoid(pre)
    dpre = g * (sig * (1.0 + pre * (1.0 - sig)))
    pixels = 2 * pre.shape[0]
    sb = fold(jnp.sum(dpre, axis=0, keepdims=True))
    sg = fold(jnp.sum(dpre * xhat, axis=0, keepdims=True))
    dpre_ref[...] = dpre.astype(BF)
    scale = vec_ref[0:1, :] * rs_ref[...]
    dt_ref[...] = (scale * (dpre - sb / pixels - xhat * (sg / pixels))).astype(BF)
    sums_ref[0:1, :] = sg
    sums_ref[1:2, :] = sb


def out_back(parts, pre, xhat, rs, vec, deps=()):
    half = pre.shape[0]
    outs = [
        jax.ShapeDtypeStruct((half, 128), BF),
        jax.ShapeDtypeStruct((half, 128), BF),
        jax.ShapeDtypeStruct((2, 128), F32),
    ]
    args = (*parts, pre, xhat, rs, vec)
    return call(functools.partial(out_back_body, len(parts)), outs, [], half * 1280, *args, deps=deps)


def conv_back_body(side, rank_ref, *refs):
    slices, (xhat_in, rs_ref, w_ref, vec_ref, before_ref, after_ref,
             dt_out, ds_out, sums_ref, mate_ref, keep_ref,
             dt_ref, ds_ref, xhat_ref, dy_ref, pad_ref, ktm_ref, lw_ref, lf_ref, ltm_ref, lnt_ref,
             sems) = (refs[:8], refs[8:])
    half = slices[0].shape[0]
    rank = rank_ref[0]
    nz = 2 * w_ref.shape[0]
    rows = 2 * half
    plane = rows // side
    nf = plane // side
    step = plane // 2
    hc = ds_ref.shape[1]
    ch = dt_ref.shape[1]
    fetched = fetch_kernels(w_ref, ktm_ref, lw_ref, sems)
    xhat_copy = pltpu.make_async_copy(xhat_in, xhat_ref, sems.at[nz])
    xhat_copy.start()
    clear_borders(pad_ref, side, plane, nf)

    def place(k, carry):
        for q, odd, a_ref, b_ref in by_rank(slices, rank):
            top, bottom = halves(odd, a_ref[chunk(k, step), :], b_ref[chunk(k, step), :])
            lanes = pl.ds(pl.multiple_of(128 * q, 128), 128)
            dt_ref[chunk(k, step), lanes] = top.astype(BF)
            dt_ref[pl.ds(pl.multiple_of(half + k * step, 16), step), lanes] = bottom.astype(BF)
        return carry

    lax.fori_loop(0, side, place, 0, unroll=True)
    dt_copy = pltpu.make_async_copy(dt_ref, dt_out, sems.at[nz + 1])
    dt_copy.start()
    for copy in fetched + [xhat_copy]:
        copy.wait()
    join_temporal(lw_ref, lf_ref, ltm_ref)
    for t in range(3):
        lnt_ref[t] = ltm_ref[t * hc : (t + 1) * hc].astype(F32).T.astype(BF)
    gain, bias = vec_ref[0:1, :], vec_ref[1:2, :]

    def hidden_grad(i, sums):
        dt = dt_ref[chunk(i, plane), :]
        early = nn(dt, lnt_ref[0]) * before_ref[0:plane, :]
        late = nn(dt, lnt_ref[2]) * after_ref[0:plane, :]
        dh = nn(dt, lnt_ref[1]) + pltpu.roll(early, plane - 1, 0) + pltpu.roll(late, 1, 0)
        xhat = xhat_ref[i]
        v = xhat * gain + bias
        sig = jax.nn.sigmoid(v)
        dy = dh * (sig * (1.0 + v * (1.0 - sig)))
        dy_ref[i] = dy
        return (
            sums[0] + jnp.sum(dy * xhat, axis=0, keepdims=True),
            sums[1] + jnp.sum(dy, axis=0, keepdims=True),
        )

    zero = jnp.zeros((1, hc), F32)
    sg, sb = lax.fori_loop(0, side, hidden_grad, (zero, zero), unroll=True)
    sums_ref[0:1, :] = sg
    sums_ref[1:2, :] = sb
    scale = gain * rs_ref[...]

    def spatial_grad(i, carry):
        ds = (scale * (dy_ref[i] - sb / rows - xhat_ref[i] * (sg / rows))).astype(BF)
        pad_ref[i + 1, nf : nf + plane] = ds
        ds_ref[chunk(i, plane), :] = ds
        return carry

    lax.fori_loop(0, side, spatial_grad, 0, unroll=True)
    ds_copy = pltpu.make_async_copy(ds_ref, ds_out, sems.at[nz + 2])
    ds_copy.start()
    low = lax.broadcasted_iota(jnp.int32, (step, 128), 1) < 64

    def back(k, carry):
        acc = jnp.zeros((2 * step, ch), F32)
        for t in range(9):
            r, c = 2 - t // 3, 2 - t % 3
            pieces = []
            for kk in (k, k + side):
                at = c * nf + lax.rem(kk, 2) * step
                pieces.append(pad_ref[kk // 2 + r, pl.ds(pl.multiple_of(at, 16), step), :])
            acc += nn(jnp.concatenate(pieces, axis=0), ktm_ref[:, t * ch : (t + 1) * ch])
        store_packed(rank, mate_ref, keep_ref, acc, k, step, low)
        return carry

    lax.fori_loop(0, side, back, 0, unroll=True)
    dt_copy.wait()
    ds_copy.wait()


def conv_back(rank, g, xhat, rs, w, vec, before, after, side, deps=()):
    half = g[0].shape[0]
    hc = vec.shape[1]
    ch = len(g) * 64
    pixels = 2 * half
    plane = pixels // side
    nf = plane // side
    outs = [
        jax.ShapeDtypeStruct((pixels, ch), BF),
        jax.ShapeDtypeStruct((pixels, hc), BF),
        jax.ShapeDtypeStruct((2, hc), F32),
        jax.ShapeDtypeStruct((4, half, 128), BF),
        jax.ShapeDtypeStruct((4, half, 128), BF),
    ]
    scratch = [
        pltpu.VMEM((pixels, ch), BF),
        pltpu.VMEM((pixels, hc), BF),
        pltpu.VMEM((side, plane, hc), F32),
        pltpu.VMEM((side, plane, hc), F32),
        pltpu.VMEM((side + 2, plane + 2 * nf, hc), BF),
        *kernel_scratch(w, hc, ch),
        pltpu.VMEM((3, ch, hc), BF),
        pltpu.SemaphoreType.DMA((2 * w.shape[0] + 3,)),
    ]
    flops = 2 * pixels * hc * 12 * ch
    return call(functools.partial(conv_back_body, side), outs, scratch, flops,
                rank, *g, xhat, rs, w, vec, before, after,
                deps=deps, far=(9, 11), far_outs=(0, 1))


def grads_body(side, pad_ref, hid_ref, ds_ref, dt_ref, before_ref, after_ref, mid_ref, out_ref,
               sg_ref, dst_ref, taps_ref, tg_ref, vec_ref):
    ch = pad_ref.shape[2]
    hc = hid_ref.shape[1]
    plane = hid_ref.shape[0] // side
    nf = plane // side
    for i in (0, 1, side + 2, side + 3):
        dst_ref[i] = jnp.zeros(dst_ref.shape[1:], BF)
    for i in range(side):
        at = slice(i * plane, (i + 1) * plane)
        h = hid_ref[at, :].astype(F32)
        taps_ref[i, 0:hc] = (pltpu.roll(h, 1, 0) * before_ref[0:plane, :]).T.astype(BF)
        taps_ref[i, hc : 2 * hc] = h.T.astype(BF)
        taps_ref[i, 2 * hc : 3 * hc] = (pltpu.roll(h, plane - 1, 0) * after_ref[0:plane, :]).T.astype(BF)
        dst_ref[i + 2] = ds_ref[at, :].astype(F32).T.astype(BF)
    tg_ref[0 : 3 * hc, :] = sum(
        nn(taps_ref[i], dt_ref[i * plane : (i + 1) * plane, :]) for i in range(side)
    )
    tg_ref[3 * hc :, :] = jnp.zeros((tg_ref.shape[0] - 3 * hc, ch), F32)
    nz, _, width = sg_ref.shape
    size = 3 * hc // (2 * nz)
    vec_ref[...] = jnp.zeros(vec_ref.shape, F32)
    vec_ref[size : size + 2, 0:hc] = mid_ref[...]
    vec_ref[size + 2 : size + 4, 0:128] = out_ref[...]
    tall = vec_ref.shape[0]
    inside = lax.broadcasted_iota(jnp.int32, (tall, ch), 0) < size
    off = (width // 2) % 128
    for z in range(nz):
        first, second = [
            jnp.where(inside, tg_ref[b * size : b * size + tall, :], vec_ref[...])
            for b in (2 * z, 2 * z + 1)
        ]
        start = width // 2 - off
        sg_ref[z, hc : hc + tall, 0:ch] = first.astype(BF)
        second = pltpu.roll(jnp.concatenate([second, jnp.zeros((tall, 128), F32)], axis=1), off, 1)
        sg_ref[z, hc : hc + tall, start : start + ch + 128] = second.astype(BF)
    for c in range(3):
        acc = sum(
            nn(dst_ref[i : i + 3].reshape(3 * hc, plane), pad_ref[i, c * nf : c * nf + plane, :])
            for i in range(1, side + 1)
        )
        for r in range(3):
            first = (3 * r + c) * ch
            end = first + ch
            at = (2 - r) * hc
            done = 0
            while first < end:
                z = first // width
                last = min(end, (z + 1) * width)
                sg_ref[z, 0:hc, first - z * width : last - z * width] = (
                    acc[at : at + hc, done : done + last - first].astype(BF)
                )
                done += last - first
                first = last


def kernel_grads(pad, hidden, ds, dt, before, after, mid, out, side, shape, deps=()):
    pixels, hc = hidden.shape
    ch = dt.shape[1]
    plane = pixels // side
    outs = [jax.ShapeDtypeStruct(shape, BF)]
    tall = shape[1] - hc
    scratch = [
        pltpu.VMEM((side + 4, hc, plane), BF),
        pltpu.VMEM((side, 3 * hc, plane), BF),
        pltpu.VMEM((3 * hc + tall, ch), F32),
        pltpu.VMEM((tall, ch), F32),
    ]
    flops = 2 * pixels * hc * 12 * ch
    return call(functools.partial(grads_body, side), outs, scratch, flops,
                pad, hidden, ds, dt, before, after, mid, out, deps=deps)[0]


def copy_after_body(v_ref, out_ref):
    out_ref[...] = v_ref[...]


def after_all(v, *deps):
    return call(copy_after_body, [jax.ShapeDtypeStruct(v.shape, v.dtype)], [], v.size, v, deps=deps)[0]


def hop(v, k):
    n = 1
    for name in EVERY:
        n *= lax.axis_size(name)
    return lax.ppermute(v, EVERY, [(i, i ^ k) for i in range(n)])


def plane_gather(v):
    got = {0: v}
    for k in (6, 2, 4, 1):
        got[k] = hop(v, k)
    for k in (2, 4, 6):
        got[k ^ 1] = hop(got[k], 1)
    return [got[k] for k in range(8)]


def plane_reduce(mate, keep):
    sums = pair_sum(keep, hop(mate, 1))
    arrived = {k: hop(sums[k // 2], k) for k in (6, 2, 4)}
    return [sums[0], arrived[2], arrived[4], arrived[6]]


def on_device(frames, cot, starts, ks, ktm, mg, mb, og, ob):
    nz, n_rank, n_seg = lax.axis_size("z"), 8, 4
    n_dp = nz * 2
    fr, side, ch = frames.shape[0], frames.shape[1], frames.shape[3]
    area = side * side
    hid = ks.shape[2]
    hc, cc = hid // n_rank, ch // n_rank
    q = hc // n_rank
    rank = lax.axis_index(PLANE)
    rank_now = rank.astype(jnp.int32).reshape(1)
    d_index = lax.axis_index(("z", "y"))
    s_index = lax.axis_index(("x", "c"))
    nf = n_dp * fr
    pixels = area * nf
    half = pixels // 2

    to_plane = [(d * n_seg + s, s * n_rank + d) for d in range(n_dp) for s in range(n_seg)]
    from_plane = [(b, a) for a, b in to_plane]
    rows = fr * area
    flag_row = jnp.pad(starts.astype(BF)[None], ((0, 11), (0, ch - fr)))
    moving = jnp.concatenate([frames.reshape(rows, ch), flag_row], axis=0)
    moving = lax.ppermute(moving, EVERY, to_plane)
    cot_moving = lax.ppermute(cot.reshape(rows, ch), EVERY, to_plane)

    perm = (jnp.arange(hid).reshape(n_rank, n_rank, q).transpose(1, 0, 2).reshape(hid)[:, None]
            == jnp.arange(hid)[None, :]).astype(BF)
    kt = lax.dot_general(perm, ks[0].astype(BF), (((1,), (1,)), ((), ())),
                         preferred_element_type=F32).astype(BF)
    kt = kt.reshape(n_rank, hc, ks.shape[1])
    lrows, width = ktm.shape[1] // n_rank, ks.shape[1]
    lt = ktm[0].astype(BF).reshape(-1, n_rank, q, ch).transpose(1, 0, 2, 3).reshape(n_rank, lrows, ch)
    lt = jnp.pad(after_all(lt, moving, cot_moving), ((0, 0), (0, 0), (0, width - ch)))
    extra = jnp.concatenate([v.astype(BF) for v in (mg, mb, og, ob)], axis=1)
    tall = -(-(lrows + 4) // 16) * 16
    extra = jnp.pad(extra, ((0, tall - lrows - 1), (0, width - extra.shape[1])))
    w = jnp.concatenate([kt, lt, jnp.broadcast_to(extra, (n_rank, *extra.shape))], axis=1)
    w = lax.all_to_all(w, PLANE, 0, 0)
    here = w
    high = hc + tall
    w = w.reshape(2, n_seg, high, width).transpose(1, 2, 0, 3).reshape(n_seg, high, 2 * width)
    ws = [lax.all_gather(w[s], "z", axis=0) for s in range(n_seg)]
    mids, outs = [], []
    for s in range(n_seg):
        row = ws[s][:, hc + lrows].reshape(n_dp, width).astype(F32)
        mids.append(jnp.stack([
            lax.dynamic_slice_in_dim(row[:, i * hc : (i + 1) * hc], rank * q, q, axis=1).reshape(hc)
            for i in range(2)]))
        own = lax.dynamic_index_in_dim(row, rank, 0, keepdims=False)
        outs.append(jnp.stack([
            jnp.tile(own[2 * hc + i * cc : 2 * hc + (i + 1) * cc], 2) for i in range(2)]))

    moving = after_all(moving, here)
    gathered = lax.all_to_all(jnp.broadcast_to(moving, (n_rank, *moving.shape)), PLANE, 0, 0)

    def by_pixel(v):
        width = v.shape[2]
        v = v.reshape(n_rank * fr, area, width).transpose(1, 0, 2)
        return v.reshape(pixels, width)

    def packed(v):
        return jnp.concatenate([v[:half], v[half:]], axis=1)

    a0 = by_pixel(gathered[:, :rows])
    flags = gathered[:, rows, :fr].reshape(nf) > 0.5
    slot = jnp.arange(nf) % fr
    before = jnp.where(flags | (slot == 0), 0.0, 1.0)
    after = jnp.where(jnp.roll(flags, -1) | (slot == fr - 1), 0.0, 1.0)
    spread = (side * nf + nf, hc)
    before = jnp.broadcast_to(jnp.tile(before, side + 1)[:, None], spread)
    after = jnp.broadcast_to(jnp.tile(after, side + 1)[:, None], spread)
    skip = packed(lax.dynamic_slice_in_dim(a0, rank * cc, cc, axis=1))

    cot_moving = cot_moving.reshape(rows, n_rank, cc).transpose(1, 0, 2)
    cot_own = packed(by_pixel(lax.all_to_all(after_all(cot_moving, gathered), PLANE, 0, 0)))

    def to_frames(v):
        v = jnp.concatenate([v[:, :cc], v[:, cc:]], axis=0)
        v = v.reshape(area, n_rank, fr, cc).transpose(1, 0, 2, 3).reshape(n_rank, rows, cc)
        v = lax.all_to_all(v, PLANE, 0, 0).transpose(1, 0, 2).reshape(area, fr, ch)
        return lax.ppermute(v, EVERY, from_plane).transpose(1, 0, 2).reshape(frames.shape)

    saved = []
    g = [a0]
    for s in range(n_seg):
        pad, hidden, xm, rm, mate, keep = conv_forward(
            rank_now, g, ws[s], mids[s], before, after, side, pixels, ch,
            deps=(cot_own,) if s == 0 else ())
        parts = plane_reduce(mate, keep)
        xo, ro, pre, res = out_norm(parts, outs[s], skip if s % 2 == 1 else None)
        saved.append((pad, hidden, xm, rm, xo, ro, pre))
        if s % 2 == 1:
            skip = res
        if s < n_seg - 1:
            g = plane_gather(res)
    output = to_frames(res)

    parts = [cot_own]
    skip_grad = None
    grads, raw = [], ()
    for s in reversed(range(n_seg)):
        pad, hidden, xm, rm, xo, ro, pre = saved[s]
        if s == 1:
            parts = parts + [skip_grad]
        dpre, dt, osum = out_back(parts, pre, xo, ro, outs[s], deps=raw + tuple(grads[1:2] if s == 0 else ()))
        if s % 2 == 1:
            skip_grad = dpre
        dtf, ds, msum, mate, keep = conv_back(
            rank_now, plane_gather(dt), xm, rm, ws[s], mids[s], before, after, side)
        if s > 0:
            parts = plane_reduce(mate, keep)
        wait = parts[:1] + (grads[:1] if s == 1 else []) if s > 0 else grads[-1:]
        sg = kernel_grads(pad, hidden, ds, dtf, before, after, msum, osum, side, ws[s].shape, deps=wait)
        raw = (sg,)
        grads.append(lax.psum_scatter(sg, "z", scatter_dimension=0))
        if s == 0:
            parts = plane_reduce(mate, keep)

    da = sum(p.astype(F32) for p in parts) + skip_grad.astype(F32)
    frames_grad = to_frames(da.astype(BF)).astype(F32)

    def by_row(v):
        return v.reshape(high, 2, width).transpose(1, 0, 2)

    grads = grads[::-1]
    g = jnp.stack([by_row(v) for v in grads], axis=1).reshape(n_rank, high, width)
    g = lax.all_to_all(g, PLANE, 0, 0)
    space_grad = lax.dot_general(g[:, :hc].reshape(hid, width), perm, (((0,), (0,)), ((), ())),
                                 preferred_element_type=F32)
    tg = g[:, hc : hc + lrows, :ch].reshape(n_rank, -1, q, ch)
    time_grad = tg.transpose(1, 0, 2, 3).reshape(-1, ch).astype(F32)
    sums = g[:, hc + lrows : hc + lrows + 4].astype(F32)

    def mid_own(v):
        return lax.dynamic_slice_in_dim(v[:, :hc], d_index * q, q, axis=1).reshape(1, hc)

    own = lax.dynamic_index_in_dim(sums, d_index, 0, keepdims=False)
    return (
        output,
        frames_grad,
        space_grad[None],
        time_grad[None],
        mid_own(sums[:, 0]),
        mid_own(sums[:, 1]),
        own[2:3, :cc],
        own[3:4, :cc],
    )


def from_behind(value, axis, steps):
    count = lax.axis_size(axis)
    leading, last = (max(0, -steps), min(count, count - steps))
    return lax.ppermute(value, axis, [(source, source + steps) for source in range(leading, last)])


def space_apply(current, kernel):
    frame_side = current.shape[1]
    padded = jnp.pad(current, ((0, 0), (1, 1), (1, 1), (0, 0)))
    stacked = jnp.concatenate(
        [
            padded[:, row_shift : row_shift + frame_side, col_shift : col_shift + frame_side, :]
            for row_shift in range(3)
            for col_shift in range(3)
        ],
        axis=-1,
    )
    return (
        stacked,
        jnp.einsum("fijc,co->fijo", stacked, kernel, preferred_element_type=jnp.float32),
    )


def space_back(gradient, kernel):
    frame_side = gradient.shape[1]
    channels = kernel.shape[0] // 9
    spread = jnp.einsum("fijo,co->fijc", gradient, kernel, preferred_element_type=jnp.float32)
    total = jnp.zeros((gradient.shape[0], frame_side + 2, frame_side + 2, channels), jnp.float32)
    for tap_index in range(9):
        row_shift = tap_index // 3
        col_shift = tap_index % 3
        piece_now = spread[..., tap_index * channels : (tap_index + 1) * channels]
        total = total + jnp.pad(
            piece_now, ((0, 0), (row_shift, 2 - row_shift), (col_shift, 2 - col_shift), (0, 0))
        )
    return total[:, 1 : frame_side + 1, 1 : frame_side + 1, :]


def time_apply(current, kernel, before_mask, after_mask):
    blanks = jnp.zeros_like(current[:1])
    earlier = jnp.concatenate([blanks, current[:-1]], axis=0) * before_mask[
        :, None, None, None
    ].astype(current.dtype)
    later = jnp.concatenate([current[1:], blanks], axis=0) * after_mask[:, None, None, None].astype(
        current.dtype
    )
    stacked = jnp.concatenate([earlier, current, later], axis=-1)
    return (
        stacked,
        jnp.einsum("fijc,co->fijo", stacked, kernel, preferred_element_type=jnp.float32),
    )


def time_back(gradient, kernel, before_mask, after_mask):
    channels = kernel.shape[0] // 3
    spread = jnp.einsum("fijo,co->fijc", gradient, kernel, preferred_element_type=jnp.float32)
    early_part = spread[..., :channels] * before_mask[:, None, None, None]
    late_part = spread[..., 2 * channels :] * after_mask[:, None, None, None]
    blanks = jnp.zeros_like(early_part[:1])
    moved_early = jnp.concatenate([early_part[1:], blanks], axis=0)
    moved_late = jnp.concatenate([blanks, late_part[:-1]], axis=0)
    return spread[..., channels : 2 * channels] + moved_early + moved_late


def moments(values, pixel_count):
    average = lax.psum(jnp.sum(values, axis=(0, 1, 2)), "dp") / pixel_count
    centered = values - average
    spread = lax.psum(jnp.sum(centered * centered, axis=(0, 1, 2)), "dp") / pixel_count
    return (average, lax.rsqrt(spread + eps))


def reduce_back(gradient, normed):
    return lax.psum(
        (jnp.sum(gradient, axis=(0, 1, 2)), jnp.sum(gradient * normed, axis=(0, 1, 2))), "dp"
    )


def silu_slope(values):
    sigmoid_now = jax.nn.sigmoid(values)
    return sigmoid_now * (1.0 + values * (1.0 - sigmoid_now))


def pick_slot(stack, slot_index):
    return lax.dynamic_index_in_dim(stack, slot_index, 0, keepdims=False)


def store_slot(stack, value, slot_index, usable):
    previous = pick_slot(stack, slot_index)
    return lax.dynamic_update_index_in_dim(stack, jnp.where(usable, value, previous), slot_index, 0)


def on_device_general(
    frames, cotangent, starts, space_kernel, time_kernel, mid_gain, mid_bias, out_gain, out_bias
):
    n_segment = lax.axis_size("segment")
    n_data = lax.axis_size("dp")
    segment_index = lax.axis_index("segment")
    odd_segment = segment_index % 2 == 1
    last_segment = segment_index == n_segment - 1
    first_segment = segment_index == 0
    frame_count = frames.shape[0]
    frame_side = frames.shape[1]
    channels = frames.shape[3]
    hidden_units = mid_gain.shape[1] * n_data
    pixel_count = n_data * frame_count * frame_side * frame_side
    turns = 2 * n_segment - 1
    block_shape = (n_segment,) + frames.shape
    all_frames, all_cot, all_starts = (
        lax.all_gather(frames, "segment", axis=0, tiled=True),
        lax.all_gather(cotangent, "segment", axis=0, tiled=True),
        lax.all_gather(starts.astype(jnp.bfloat16), "segment", axis=0, tiled=True),
    )
    frame_stack = all_frames.reshape(block_shape)
    cot_stack = all_cot.reshape(block_shape)
    clip_flags = all_starts.astype(jnp.float32).reshape(n_segment, frame_count)
    positions = jnp.arange(frame_count)
    before_mask = jnp.where((clip_flags > 0.5) | (positions == 0), 0.0, 1.0)
    following = jnp.concatenate([clip_flags[:, 1:], jnp.ones((n_segment, 1), jnp.float32)], axis=1)
    after_mask = jnp.where(following > 0.5, 0.0, 1.0)
    gathered = (
        lax.all_gather(space_kernel[0].astype(jnp.bfloat16), "dp", axis=0, tiled=True),
        lax.all_gather(time_kernel[0].astype(jnp.bfloat16), "dp", axis=0, tiled=True),
        lax.all_gather(mid_gain[0].astype(jnp.bfloat16), "dp", axis=0, tiled=True),
        lax.all_gather(mid_bias[0].astype(jnp.bfloat16), "dp", axis=0, tiled=True),
        lax.all_gather(out_gain[0].astype(jnp.bfloat16), "dp", axis=0, tiled=True),
        lax.all_gather(out_bias[0].astype(jnp.bfloat16), "dp", axis=0, tiled=True),
    )
    space_low, time_low = (gathered[0], gathered[1])
    mid_gain_now = gathered[2].astype(jnp.float32)
    mid_bias_now = gathered[3].astype(jnp.float32)
    out_gain_now = gathered[4].astype(jnp.float32)
    out_bias_now = gathered[5].astype(jnp.float32)
    incoming = jnp.zeros_like(frames)
    carried = jnp.zeros_like(frames)
    kept_input = jnp.zeros(block_shape, jnp.bfloat16)
    kept_skip = jnp.zeros(block_shape, jnp.bfloat16)
    kept_mid_mean = jnp.zeros((n_segment, hidden_units), jnp.float32)
    kept_mid_scale = jnp.zeros((n_segment, hidden_units), jnp.float32)
    kept_out_mean = jnp.zeros((n_segment, channels), jnp.float32)
    kept_out_scale = jnp.zeros((n_segment, channels), jnp.float32)
    results = jnp.zeros(block_shape, jnp.float32)
    for turn_index in range(turns):
        micro_index = turn_index - segment_index
        usable = (micro_index >= 0) & (micro_index < n_segment)
        slot_index = jnp.clip(micro_index, 0, n_segment - 1)
        current = jnp.where(first_segment, pick_slot(frame_stack, slot_index), incoming)
        skip_input = carried
        _, spatial = space_apply(current, space_low)
        mid_mean, mid_scale = moments(spatial, pixel_count)
        hidden_act = jax.nn.silu(
            (spatial - mid_mean) * mid_scale * mid_gain_now + mid_bias_now
        ).astype(jnp.bfloat16)
        _, temporal = time_apply(
            hidden_act,
            time_low,
            pick_slot(before_mask, slot_index),
            pick_slot(after_mask, slot_index),
        )
        out_mean, out_scale = moments(temporal, pixel_count)
        pre_act = (
            (temporal - out_mean) * out_scale * out_gain_now
            + out_bias_now
            + jnp.where(odd_segment, skip_input.astype(jnp.float32), 0.0)
        )
        result = jax.nn.silu(pre_act).astype(jnp.bfloat16)
        kept_input = store_slot(kept_input, current, slot_index, usable)
        kept_skip = store_slot(kept_skip, skip_input, slot_index, usable)
        kept_mid_mean = store_slot(kept_mid_mean, mid_mean, slot_index, usable)
        kept_mid_scale = store_slot(kept_mid_scale, mid_scale, slot_index, usable)
        kept_out_mean = store_slot(kept_out_mean, out_mean, slot_index, usable)
        kept_out_scale = store_slot(kept_out_scale, out_scale, slot_index, usable)
        results = store_slot(results, result.astype(jnp.float32), slot_index, usable)
        if turn_index < turns - 1:
            incoming, carried = from_behind(
                (result, jnp.where(odd_segment, result, current)), "segment", 1
            )
    gathered = (
        lax.all_gather(space_kernel[0].astype(jnp.bfloat16), "dp", axis=0, tiled=True),
        lax.all_gather(time_kernel[0].astype(jnp.bfloat16), "dp", axis=0, tiled=True),
        lax.all_gather(mid_gain[0].astype(jnp.bfloat16), "dp", axis=0, tiled=True),
        lax.all_gather(mid_bias[0].astype(jnp.bfloat16), "dp", axis=0, tiled=True),
        lax.all_gather(out_gain[0].astype(jnp.bfloat16), "dp", axis=0, tiled=True),
        lax.all_gather(out_bias[0].astype(jnp.bfloat16), "dp", axis=0, tiled=True),
    )
    space_low, time_low = (gathered[0], gathered[1])
    mid_gain_now = gathered[2].astype(jnp.float32)
    mid_bias_now = gathered[3].astype(jnp.float32)
    out_gain_now = gathered[4].astype(jnp.float32)
    out_bias_now = gathered[5].astype(jnp.float32)
    grad_input = jnp.zeros_like(frames)
    grad_skip = jnp.zeros_like(frames)
    space_acc = jnp.zeros(space_low.shape, jnp.float32)
    time_acc = jnp.zeros(time_low.shape, jnp.float32)
    mid_gain_acc = jnp.zeros((hidden_units,), jnp.float32)
    mid_bias_acc = jnp.zeros((hidden_units,), jnp.float32)
    out_gain_acc = jnp.zeros((channels,), jnp.float32)
    out_bias_acc = jnp.zeros((channels,), jnp.float32)
    input_grads = jnp.zeros(block_shape, jnp.float32)
    for turn_index in range(turns):
        micro_index = n_segment - 1 - (turn_index - (n_segment - 1 - segment_index))
        usable = (micro_index >= 0) & (micro_index < n_segment)
        usable_weight = usable.astype(jnp.float32)
        slot_index = jnp.clip(micro_index, 0, n_segment - 1)
        current = pick_slot(kept_input, slot_index)
        skip_input = pick_slot(kept_skip, slot_index)
        before_now = pick_slot(before_mask, slot_index)
        after_now = pick_slot(after_mask, slot_index)
        space_taps, spatial = space_apply(current, space_low)
        mid_normed = (spatial - pick_slot(kept_mid_mean, slot_index)) * pick_slot(
            kept_mid_scale, slot_index
        )
        mid_pre = mid_normed * mid_gain_now + mid_bias_now
        hidden_act = jax.nn.silu(mid_pre).astype(jnp.bfloat16)
        time_taps, temporal = time_apply(hidden_act, time_low, before_now, after_now)
        out_scale = pick_slot(kept_out_scale, slot_index)
        out_normed = (temporal - pick_slot(kept_out_mean, slot_index)) * out_scale
        pre_act = (
            out_normed * out_gain_now
            + out_bias_now
            + jnp.where(odd_segment, skip_input.astype(jnp.float32), 0.0)
        )
        grad_result = jnp.where(
            last_segment,
            pick_slot(cot_stack, slot_index).astype(jnp.float32),
            grad_input.astype(jnp.float32)
            + jnp.where(odd_segment, grad_skip.astype(jnp.float32), 0.0),
        )
        grad_pre = grad_result * silu_slope(pre_act)
        out_bias_sum, out_gain_sum = reduce_back(grad_pre, out_normed)
        grad_temporal = (
            out_gain_now
            * out_scale
            * (grad_pre - out_bias_sum / pixel_count - out_normed * out_gain_sum / pixel_count)
        ).astype(jnp.bfloat16)
        time_acc = time_acc + usable_weight * jnp.einsum(
            "fijc,fijo->co", time_taps, grad_temporal, preferred_element_type=jnp.float32
        )
        grad_hidden = time_back(grad_temporal, time_low, before_now, after_now)
        grad_mid = grad_hidden * silu_slope(mid_pre)
        mid_bias_sum, mid_gain_sum = reduce_back(grad_mid, mid_normed)
        mid_scale = pick_slot(kept_mid_scale, slot_index)
        grad_spatial = (
            mid_gain_now
            * mid_scale
            * (grad_mid - mid_bias_sum / pixel_count - mid_normed * mid_gain_sum / pixel_count)
        ).astype(jnp.bfloat16)
        space_acc = space_acc + usable_weight * jnp.einsum(
            "fijc,fijo->co", space_taps, grad_spatial, preferred_element_type=jnp.float32
        )
        grad_current = space_back(grad_spatial, space_low)
        mid_gain_acc = mid_gain_acc + usable_weight * mid_gain_sum
        mid_bias_acc = mid_bias_acc + usable_weight * mid_bias_sum
        out_gain_acc = out_gain_acc + usable_weight * out_gain_sum
        out_bias_acc = out_bias_acc + usable_weight * out_bias_sum
        input_grads = store_slot(
            input_grads, grad_current + grad_skip.astype(jnp.float32), slot_index, usable
        )
        if turn_index < turns - 1:
            grad_input, grad_skip = from_behind(
                (
                    grad_current.astype(jnp.bfloat16),
                    jnp.where(odd_segment, grad_pre.astype(jnp.bfloat16), grad_skip),
                ),
                "segment",
                -1,
            )
    space_grad, time_grad = (
        lax.psum_scatter(space_acc, "dp", scatter_dimension=0, tiled=True),
        lax.psum_scatter(time_acc, "dp", scatter_dimension=0, tiled=True),
    )
    data_index = lax.axis_index("dp")

    def own_share(full_vector):
        share = full_vector.shape[0] // n_data
        return lax.dynamic_slice_in_dim(full_vector, data_index * share, share)[None]

    flat_shape = (n_segment * frame_count,) + frames.shape[1:]
    arrived_out, arrived_grads = (
        lax.all_to_all(
            results.reshape(flat_shape).astype(jnp.bfloat16),
            "segment",
            split_axis=0,
            concat_axis=0,
            tiled=True,
        ).astype(jnp.float32),
        lax.all_to_all(
            input_grads.reshape(flat_shape).astype(jnp.bfloat16),
            "segment",
            split_axis=0,
            concat_axis=0,
            tiled=True,
        ).astype(jnp.float32),
    )
    output = arrived_out[(n_segment - 1) * frame_count :].astype(jnp.bfloat16)
    frames_grad = arrived_grads[:frame_count]
    return (
        output,
        frames_grad,
        space_grad[None],
        time_grad[None],
        own_share(mid_gain_acc),
        own_share(mid_bias_acc),
        own_share(out_gain_acc),
        own_share(out_bias_acc),
    )


def general(mesh):
    return jax.shard_map(
        on_device_general,
        mesh=mesh,
        in_specs=(
            P(("dp", "segment"), None, None, None),
            P(("dp", "segment"), None, None, None),
            P(("dp", "segment")),
            P("segment", "dp", None),
            P("segment", "dp", None),
            P("segment", "dp"),
            P("segment", "dp"),
            P("segment", "dp"),
            P("segment", "dp"),
        ),
        out_specs=(
            P(("dp", "segment"), None, None, None),
            P(("dp", "segment"), None, None, None),
            P("segment", "dp", None),
            P("segment", "dp", None),
            P("segment", "dp"),
            P("segment", "dp"),
            P("segment", "dp"),
            P("segment", "dp"),
        ),
        check_vma=False,
    )


def solution(mesh):
    if mesh.shape["dp"] != 8 or mesh.shape["segment"] != 4:
        return general(mesh)
    n_dp, n_seg = mesh.shape["dp"], mesh.shape["segment"]
    fine = Mesh(mesh.devices.reshape(n_dp // 2, 2, 2, n_seg // 2), EVERY)
    dp, seg = ("z", "y"), ("x", "c")
    return jax.shard_map(
        on_device,
        mesh=fine,
        in_specs=(
            P(EVERY, None, None, None),
            P(EVERY, None, None, None),
            P(EVERY),
            P(seg, dp, None),
            P(seg, dp, None),
            P(seg, dp),
            P(seg, dp),
            P(seg, dp),
            P(seg, dp),
        ),
        out_specs=(
            P(EVERY, None, None, None),
            P(EVERY, None, None, None),
            P(seg, dp, None),
            P(seg, dp, None),
            P(seg, dp),
            P(seg, dp),
            P(seg, dp),
            P(seg, dp),
        ),
        check_vma=False,
    )
```

```python
import functools

import jax
import jax.numpy as jnp
from jax import lax
from jax.experimental import pallas as pl
from jax.experimental.pallas import tpu as pltpu
from jax.sharding import Mesh, PartitionSpec as P

eps = 1e-05
PLANE = ("y", "x", "c")
EVERY = ("z", "y", "x", "c")
BF = jnp.bfloat16
F32 = jnp.float32


def nt(a, b):
    return lax.dot_general(a, b, (((1,), (1,)), ((), ())), preferred_element_type=F32)


def nn(a, b):
    return lax.dot_general(a, b, (((1,), (0,)), ((), ())), preferred_element_type=F32)


VMEM_CAP = 56 * 1024 * 1024
ANY = pl.BlockSpec(memory_space=pl.ANY)


def call(body, outs, scratch, flops, *args, deps=(), far=(), far_outs=()):
    moved = sum(a.size * a.dtype.itemsize for a in args) + sum(
        o.size * o.dtype.itemsize for o in outs
    )
    n = len(deps)

    def spec(a):
        return pl.BlockSpec(memory_space=pltpu.SMEM if a.dtype == jnp.int32 else pltpu.VMEM)

    return pl.pallas_call(
        lambda *refs: body(*refs[n:]),
        out_shape=outs,
        in_specs=[ANY] * n + [ANY if i in far else spec(a) for i, a in enumerate(args)],
        out_specs=[ANY if i in far_outs else spec(o) for i, o in enumerate(outs)],
        scratch_shapes=scratch,
        compiler_params=pltpu.CompilerParams(vmem_limit_bytes=VMEM_CAP),
        cost_estimate=pl.CostEstimate(flops=flops, bytes_accessed=moved, transcendentals=0),
    )(*deps, *args)


def chunk(i, size):
    return pl.ds(pl.multiple_of(i * size, 16), size)


def clear_borders(pad_ref, side, plane, nf):
    zrow = jnp.zeros(pad_ref.shape[1:], BF)
    pad_ref[0] = zrow
    pad_ref[side + 1] = zrow
    zcol = jnp.zeros((nf, pad_ref.shape[2]), BF)
    for i in range(side):
        pad_ref[i + 1, 0:nf] = zcol
        pad_ref[i + 1, nf + plane : 2 * nf + plane] = zcol


def by_rank(slices, rank):
    odd = lax.rem(rank, 2) == 1
    for p in range(len(slices) // 2):
        a, b = slices[2 * p], slices[2 * p + 1]
        yield lax.bitwise_xor(rank // 2, p), odd, a, b


def halves(odd, own, mate):
    low = lax.broadcasted_iota(jnp.int32, own.shape, 1) < 64
    own, mate = own.astype(F32), mate.astype(F32)
    a, b = jnp.where(odd, mate, own), jnp.where(odd, own, mate)
    top = jnp.where(low, a, pltpu.roll(b, 64, 1))
    bottom = jnp.where(low, pltpu.roll(a, 64, 1), b)
    return top, bottom


def store_packed(rank, mate_ref, keep_ref, part, k, step, low):
    rows_now = chunk(k, step)
    odd = lax.rem(rank, 2) == 1
    for q in range(keep_ref.shape[0]):
        x = part[:step, 128 * q : 128 * q + 128]
        y = part[step:, 128 * q : 128 * q + 128]
        even_slice = jnp.where(low, x, pltpu.roll(y, 64, 1))
        odd_slice = jnp.where(low, pltpu.roll(x, 64, 1), y)
        p = lax.bitwise_xor(rank // 2, q)
        keep_ref[p, rows_now, :] = jnp.where(odd, odd_slice, even_slice).astype(BF)
        mate_ref[p, rows_now, :] = jnp.where(odd, even_slice, odd_slice).astype(BF)


def fetch_kernels(w_ref, ktm_ref, lw_ref, sems):
    nz, _, width = w_ref.shape
    hc = ktm_ref.shape[0]
    copies = []
    for z in range(nz):
        copies.append(pltpu.make_async_copy(
            w_ref.at[z, pl.ds(0, hc)], ktm_ref.at[:, pl.ds(z * width, width)], sems.at[2 * z]))
        copies.append(pltpu.make_async_copy(
            w_ref.at[z, pl.ds(hc, lw_ref.shape[1])], lw_ref.at[z], sems.at[2 * z + 1]))
    for copy in copies:
        copy.start()
    return copies


def join_temporal(lw_ref, lf_ref, ltm_ref):
    ch = ltm_ref.shape[1]
    width = lw_ref.shape[2] // 2
    count = 2 * lw_ref.shape[0]
    size = ltm_ref.shape[0] // count
    for z in range(lw_ref.shape[0]):
        first = lw_ref[z, :, 0:ch].astype(F32)
        off = width % 128
        second = lw_ref[z, :, width - off : width - off + ch + 128].astype(F32)
        second = pltpu.roll(second, ch + 128 - off, 1)[:, 0:ch]
        for b, block in ((2 * z, first), (2 * z + 1, second)):
            lf_ref[b * size : b * size + block.shape[0], :] = block
    ltm_ref[...] = lf_ref[0 : ltm_ref.shape[0], :].astype(BF)


def prepare_body(w_ref, kn_out, l_out, lt_out, ktm_ref, lw_ref, lf_ref, sems):
    hc, ch = ktm_ref.shape[0], l_out.shape[1]
    for copy in fetch_kernels(w_ref, ktm_ref, lw_ref, sems):
        copy.wait()
    for t in range(9):
        kn_out[t] = ktm_ref[:, t * ch : (t + 1) * ch].astype(F32).T.astype(BF)
    join_temporal(lw_ref, lf_ref, l_out)
    for t in range(3):
        lt_out[t] = lf_ref[t * hc : (t + 1) * hc].T.astype(BF)


def prepare(w, hc, ch):
    outs = [
        jax.ShapeDtypeStruct((9, ch, hc), BF),
        jax.ShapeDtypeStruct((3 * hc, ch), BF),
        jax.ShapeDtypeStruct((3, ch, hc), BF),
    ]
    tall = w.shape[1] - hc
    scratch = [
        pltpu.VMEM((hc, 9 * ch), BF),
        pltpu.VMEM((w.shape[0], tall, w.shape[2]), BF),
        pltpu.VMEM((3 * hc + tall, ch), F32),
        pltpu.SemaphoreType.DMA((2 * w.shape[0],)),
    ]
    return call(prepare_body, outs, scratch, 2 * w.size * 512, w, far=(0,))


def conv_body(side, first, rank_ref, *refs):
    n = 1 if first else 8
    slices = refs[:n]
    (kn_in, ltm_ref, vec_ref, before_ref, after_ref,
     pad_out, hid_out, xhat_out, rs_ref, mate_ref, keep_ref,
     pad_ref, hid_ref, xhat_ref, sp_ref, kn_ref, sems) = refs[n:]
    rank = rank_ref[0]
    kn_copy = pltpu.make_async_copy(kn_in, kn_ref, sems.at[0])
    kn_copy.start()
    ch, hc = pad_ref.shape[2], hid_ref.shape[1]
    rows = hid_ref.shape[0]
    plane = rows // side
    nf = plane // side
    step = plane // 2
    clear_borders(pad_ref, side, plane, nf)
    if first:
        for i in range(side):
            pad_ref[i + 1, nf : nf + plane] = slices[0][i * plane : (i + 1) * plane]
    else:
        def place(k, carry):
            for q, odd, a_ref, b_ref in by_rank(slices, rank):
                top, bottom = halves(odd, a_ref[chunk(k, step), :], b_ref[chunk(k, step), :])
                lanes = pl.ds(pl.multiple_of(128 * q, 128), 128)
                for piece, kk in ((top, k), (bottom, k + side)):
                    at = nf + lax.rem(kk, 2) * step
                    pad_ref[1 + kk // 2, pl.ds(pl.multiple_of(at, 16), step), lanes] = piece.astype(BF)
            return carry

        lax.fori_loop(0, side, place, 0, unroll=True)
    pad_copy = pltpu.make_async_copy(pad_ref, pad_out, sems.at[1])
    pad_copy.start()
    kn_copy.wait()

    def conv(i, total):
        acc = jnp.zeros((plane, hc), F32)
        for t in range(9):
            r, c = t // 3, t % 3
            acc += nn(pad_ref[i + r, c * nf : c * nf + plane, :], kn_ref[t])
        sp_ref[i] = acc
        return total + jnp.sum(acc, axis=0, keepdims=True)

    mean = lax.fori_loop(0, side, conv, jnp.zeros((1, hc), F32), unroll=True) / rows

    def square(i, total):
        cen = sp_ref[i] - mean
        return total + jnp.sum(cen * cen, axis=0, keepdims=True)

    var = lax.fori_loop(0, side, square, jnp.zeros((1, hc), F32), unroll=True) / rows
    rs = lax.rsqrt(var + eps)
    rs_ref[...] = rs
    gain, bias = vec_ref[0:1, :], vec_ref[1:2, :]

    def act(i, carry):
        xhat = (sp_ref[i] - mean) * rs
        xhat_ref[i] = xhat
        v = xhat * gain + bias
        v = v * jax.nn.sigmoid(v)
        sp_ref[i] = v
        hid_ref[chunk(i, plane), :] = v.astype(BF)
        return carry

    lax.fori_loop(0, side, act, 0, unroll=True)
    late = [
        pltpu.make_async_copy(hid_ref, hid_out, sems.at[2]),
        pltpu.make_async_copy(xhat_ref, xhat_out, sems.at[3]),
    ]
    for copy in late:
        copy.start()
    low = lax.broadcasted_iota(jnp.int32, (step, 128), 1) < 64

    def temporal(k, carry):
        pieces = []
        for kk in (k, k + side):
            par = lax.rem(kk, 2)
            h = sp_ref[kk // 2, pl.ds(pl.multiple_of(par * step, 8), step), :]
            at = pl.multiple_of(par * (step % nf), 8)
            pieces.append((
                (pltpu.roll(h, 1, 0) * before_ref[pl.ds(at, step), :]).astype(BF),
                h.astype(BF),
                (pltpu.roll(h, step - 1, 0) * after_ref[pl.ds(at, step), :]).astype(BF),
            ))
        part = sum(
            nn(jnp.concatenate([x, y], axis=0), ltm_ref[t * hc : (t + 1) * hc])
            for t, (x, y) in enumerate(zip(*pieces))
        )
        store_packed(rank, mate_ref, keep_ref, part, k, step, low)
        return carry

    lax.fori_loop(0, side, temporal, 0, unroll=True)
    for copy in [pad_copy] + late:
        copy.wait()


def conv_forward(rank, g, kn, lt, vec, before, after, side, pixels, ch, deps=()):
    hc = vec.shape[1]
    plane = pixels // side
    nf = plane // side
    n = len(g)
    shapes = [
        ((side + 2, plane + 2 * nf, ch), BF),
        ((pixels, hc), BF),
        ((side, plane, hc), F32),
    ]
    outs = [jax.ShapeDtypeStruct(*s) for s in shapes] + [
        jax.ShapeDtypeStruct((1, hc), F32),
        jax.ShapeDtypeStruct((4, pixels // 2, 128), BF),
        jax.ShapeDtypeStruct((4, pixels // 2, 128), BF),
    ]
    scratch = [pltpu.VMEM(*s) for s in shapes] + [
        pltpu.VMEM((side, plane, hc), F32),
        pltpu.VMEM((9, ch, hc), BF),
        pltpu.SemaphoreType.DMA((4,)),
    ]
    flops = 2 * pixels * hc * 12 * ch
    return call(functools.partial(conv_body, side, n == 1), outs, scratch, flops,
                rank, *g, kn, lt, vec, before, after,
                deps=deps, far=(n + 1,), far_outs=(0, 1, 2))


def fold(v):
    return v + pltpu.roll(v, 64, 1)


def total_of(refs):
    t = refs[0][...].astype(F32)
    for ref in refs[1:]:
        t += ref[...].astype(F32)
    return t


def pair_sum_body(keep_ref, mate_ref, *out_refs):
    for p, ref in enumerate(out_refs):
        ref[...] = (keep_ref[p].astype(F32) + mate_ref[p].astype(F32)).astype(ref.dtype)


def pair_sum(keep, arrived, deps=()):
    shape = keep.shape[1:]
    outs = [jax.ShapeDtypeStruct(shape, BF)] * keep.shape[0]
    return call(pair_sum_body, outs, [], keep.size, keep, arrived, deps=deps)


def out_norm_body(n, has_skip, *refs):
    parts, refs = refs[:n], refs[n:]
    if has_skip:
        vec_ref, skip_ref, xhat_ref, rs_ref, pre_ref, res_ref = refs
    else:
        vec_ref, xhat_ref, rs_ref, pre_ref, res_ref = refs
    t = total_of(parts)
    pixels = 2 * t.shape[0]
    mean = fold(jnp.sum(t, axis=0, keepdims=True)) / pixels
    cen = t - mean
    rs = lax.rsqrt(fold(jnp.sum(cen * cen, axis=0, keepdims=True)) / pixels + eps)
    xhat = cen * rs
    pre = xhat * vec_ref[0:1, :] + vec_ref[1:2, :]
    if has_skip:
        pre = pre + skip_ref[...].astype(F32)
    xhat_ref[...] = xhat
    rs_ref[...] = rs
    pre_ref[...] = pre
    res_ref[...] = (pre * jax.nn.sigmoid(pre)).astype(BF)


def out_norm(parts, vec, skip):
    half = parts[0].shape[0]
    outs = [
        jax.ShapeDtypeStruct((half, 128), F32),
        jax.ShapeDtypeStruct((1, 128), F32),
        jax.ShapeDtypeStruct((half, 128), F32),
        jax.ShapeDtypeStruct((half, 128), BF),
    ]
    args = (*parts, vec) + (() if skip is None else (skip,))
    body = functools.partial(out_norm_body, len(parts), skip is not None)
    return call(body, outs, [], half * 128 * 10, *args)


def out_back_body(n, *refs):
    parts, (pre_ref, xhat_ref, rs_ref, vec_ref, dpre_ref, dt_ref, sums_ref) = refs[:n], refs[n:]
    g = total_of(parts)
    pre, xhat = pre_ref[...], xhat_ref[...]
    sig = jax.nn.sigmoid(pre)
    dpre = g * (sig * (1.0 + pre * (1.0 - sig)))
    pixels = 2 * pre.shape[0]
    sb = fold(jnp.sum(dpre, axis=0, keepdims=True))
    sg = fold(jnp.sum(dpre * xhat, axis=0, keepdims=True))
    dpre_ref[...] = dpre.astype(BF)
    scale = vec_ref[0:1, :] * rs_ref[...]
    dt_ref[...] = (scale * (dpre - sb / pixels - xhat * (sg / pixels))).astype(BF)
    sums_ref[0:1, :] = sg
    sums_ref[1:2, :] = sb


def out_back(parts, pre, xhat, rs, vec, deps=()):
    half = pre.shape[0]
    outs = [
        jax.ShapeDtypeStruct((half, 128), BF),
        jax.ShapeDtypeStruct((half, 128), BF),
        jax.ShapeDtypeStruct((2, 128), F32),
    ]
    args = (*parts, pre, xhat, rs, vec)
    return call(functools.partial(out_back_body, len(parts)), outs, [], half * 1280, *args, deps=deps)


def conv_back_body(side, rank_ref, *refs):
    slices, (xhat_in, rs_ref, w_ref, lnt_ref, vec_ref, before_ref, after_ref,
             dt_out, ds_out, sums_ref, mate_ref, keep_ref,
             dt_ref, ds_ref, xhat_ref, dy_ref, pad_ref, ktm_ref, sems) = refs[:8], refs[8:]
    half = slices[0].shape[0]
    rank = rank_ref[0]
    nz, _, width = w_ref.shape
    rows = 2 * half
    plane = rows // side
    nf = plane // side
    step = plane // 2
    hc = ds_ref.shape[1]
    ch = dt_ref.shape[1]
    fetched = [
        pltpu.make_async_copy(
            w_ref.at[z, pl.ds(0, hc)], ktm_ref.at[:, pl.ds(z * width, width)], sems.at[z])
        for z in range(nz)
    ]
    xhat_copy = pltpu.make_async_copy(xhat_in, xhat_ref, sems.at[nz])
    for copy in fetched + [xhat_copy]:
        copy.start()
    clear_borders(pad_ref, side, plane, nf)

    def place(k, carry):
        for q, odd, a_ref, b_ref in by_rank(slices, rank):
            top, bottom = halves(odd, a_ref[chunk(k, step), :], b_ref[chunk(k, step), :])
            lanes = pl.ds(pl.multiple_of(128 * q, 128), 128)
            dt_ref[chunk(k, step), lanes] = top.astype(BF)
            dt_ref[pl.ds(pl.multiple_of(half + k * step, 16), step), lanes] = bottom.astype(BF)
        return carry

    lax.fori_loop(0, side, place, 0, unroll=True)
    dt_copy = pltpu.make_async_copy(dt_ref, dt_out, sems.at[nz + 1])
    dt_copy.start()
    xhat_copy.wait()
    gain, bias = vec_ref[0:1, :], vec_ref[1:2, :]

    def hidden_grad(i, sums):
        dt = dt_ref[chunk(i, plane), :]
        early = nn(dt, lnt_ref[0]) * before_ref[0:plane, :]
        late = nn(dt, lnt_ref[2]) * after_ref[0:plane, :]
        dh = nn(dt, lnt_ref[1]) + pltpu.roll(early, plane - 1, 0) + pltpu.roll(late, 1, 0)
        xhat = xhat_ref[i]
        v = xhat * gain + bias
        sig = jax.nn.sigmoid(v)
        dy = dh * (sig * (1.0 + v * (1.0 - sig)))
        dy_ref[i] = dy
        return (
            sums[0] + jnp.sum(dy * xhat, axis=0, keepdims=True),
            sums[1] + jnp.sum(dy, axis=0, keepdims=True),
        )

    zero = jnp.zeros((1, hc), F32)
    sg, sb = lax.fori_loop(0, side, hidden_grad, (zero, zero), unroll=True)
    sums_ref[0:1, :] = sg
    sums_ref[1:2, :] = sb
    scale = gain * rs_ref[...]

    def spatial_grad(i, carry):
        ds = (scale * (dy_ref[i] - sb / rows - xhat_ref[i] * (sg / rows))).astype(BF)
        pad_ref[i + 1, nf : nf + plane] = ds
        ds_ref[chunk(i, plane), :] = ds
        return carry

    lax.fori_loop(0, side, spatial_grad, 0, unroll=True)
    ds_copy = pltpu.make_async_copy(ds_ref, ds_out, sems.at[nz + 2])
    ds_copy.start()
    for copy in fetched:
        copy.wait()
    low = lax.broadcasted_iota(jnp.int32, (step, 128), 1) < 64

    def back(k, carry):
        acc = jnp.zeros((2 * step, ch), F32)
        for t in range(9):
            r, c = 2 - t // 3, 2 - t % 3
            pieces = []
            for kk in (k, k + side):
                at = c * nf + lax.rem(kk, 2) * step
                pieces.append(pad_ref[kk // 2 + r, pl.ds(pl.multiple_of(at, 16), step), :])
            acc += nn(jnp.concatenate(pieces, axis=0), ktm_ref[:, t * ch : (t + 1) * ch])
        store_packed(rank, mate_ref, keep_ref, acc, k, step, low)
        return carry

    lax.fori_loop(0, side, back, 0, unroll=True)
    dt_copy.wait()
    ds_copy.wait()


def conv_back(rank, g, xhat, rs, w, lnt, vec, before, after, side, deps=()):
    half = g[0].shape[0]
    hc = vec.shape[1]
    ch = len(g) * 64
    pixels = 2 * half
    plane = pixels // side
    nf = plane // side
    outs = [
        jax.ShapeDtypeStruct((pixels, ch), BF),
        jax.ShapeDtypeStruct((pixels, hc), BF),
        jax.ShapeDtypeStruct((2, hc), F32),
        jax.ShapeDtypeStruct((4, half, 128), BF),
        jax.ShapeDtypeStruct((4, half, 128), BF),
    ]
    scratch = [
        pltpu.VMEM((pixels, ch), BF),
        pltpu.VMEM((pixels, hc), BF),
        pltpu.VMEM((side, plane, hc), F32),
        pltpu.VMEM((side, plane, hc), F32),
        pltpu.VMEM((side + 2, plane + 2 * nf, hc), BF),
        pltpu.VMEM((hc, 9 * ch), BF),
        pltpu.SemaphoreType.DMA((w.shape[0] + 3,)),
    ]
    flops = 2 * pixels * hc * 12 * ch
    return call(functools.partial(conv_back_body, side), outs, scratch, flops,
                rank, *g, xhat, rs, w, lnt, vec, before, after,
                deps=deps, far=(9, 11), far_outs=(0, 1))


def grads_body(side, pad_ref, hid_ref, ds_ref, dt_ref, before_ref, after_ref, mid_ref, out_ref,
               sg_ref, dst_ref, taps_ref, tg_ref, vec_ref):
    ch = pad_ref.shape[2]
    hc = hid_ref.shape[1]
    plane = hid_ref.shape[0] // side
    nf = plane // side
    for i in (0, 1, side + 2, side + 3):
        dst_ref[i] = jnp.zeros(dst_ref.shape[1:], BF)
    for i in range(side):
        at = slice(i * plane, (i + 1) * plane)
        h = hid_ref[at, :].astype(F32)
        taps_ref[i, 0:hc] = (pltpu.roll(h, 1, 0) * before_ref[0:plane, :]).T.astype(BF)
        taps_ref[i, hc : 2 * hc] = h.T.astype(BF)
        taps_ref[i, 2 * hc : 3 * hc] = (pltpu.roll(h, plane - 1, 0) * after_ref[0:plane, :]).T.astype(BF)
        dst_ref[i + 2] = ds_ref[at, :].astype(F32).T.astype(BF)
    tg_ref[0 : 3 * hc, :] = sum(
        nn(taps_ref[i], dt_ref[i * plane : (i + 1) * plane, :]) for i in range(side)
    )
    tg_ref[3 * hc :, :] = jnp.zeros((tg_ref.shape[0] - 3 * hc, ch), F32)
    nz, _, width = sg_ref.shape
    size = 3 * hc // (2 * nz)
    vec_ref[...] = jnp.zeros(vec_ref.shape, F32)
    vec_ref[size : size + 2, 0:hc] = mid_ref[...]
    vec_ref[size + 2 : size + 4, 0:128] = out_ref[...]
    tall = vec_ref.shape[0]
    inside = lax.broadcasted_iota(jnp.int32, (tall, ch), 0) < size
    off = (width // 2) % 128
    for z in range(nz):
        first, second = [
            jnp.where(inside, tg_ref[b * size : b * size + tall, :], vec_ref[...])
            for b in (2 * z, 2 * z + 1)
        ]
        start = width // 2 - off
        sg_ref[z, hc : hc + tall, 0:ch] = first.astype(BF)
        second = pltpu.roll(jnp.concatenate([second, jnp.zeros((tall, 128), F32)], axis=1), off, 1)
        sg_ref[z, hc : hc + tall, start : start + ch + 128] = second.astype(BF)
    for c in range(3):
        acc = sum(
            nn(dst_ref[i : i + 3].reshape(3 * hc, plane), pad_ref[i, c * nf : c * nf + plane, :])
            for i in range(1, side + 1)
        )
        for r in range(3):
            first = (3 * r + c) * ch
            end = first + ch
            at = (2 - r) * hc
            done = 0
            while first < end:
                z = first // width
                last = min(end, (z + 1) * width)
                sg_ref[z, 0:hc, first - z * width : last - z * width] = (
                    acc[at : at + hc, done : done + last - first].astype(BF)
                )
                done += last - first
                first = last


def kernel_grads(pad, hidden, ds, dt, before, after, mid, out, side, shape, deps=()):
    pixels, hc = hidden.shape
    ch = dt.shape[1]
    plane = pixels // side
    outs = [jax.ShapeDtypeStruct(shape, BF)]
    tall = shape[1] - hc
    scratch = [
        pltpu.VMEM((side + 4, hc, plane), BF),
        pltpu.VMEM((side, 3 * hc, plane), BF),
        pltpu.VMEM((3 * hc + tall, ch), F32),
        pltpu.VMEM((tall, ch), F32),
    ]
    flops = 2 * pixels * hc * 12 * ch
    return call(functools.partial(grads_body, side), outs, scratch, flops,
                pad, hidden, ds, dt, before, after, mid, out, deps=deps)[0]


def copy_after_body(v_ref, out_ref):
    out_ref[...] = v_ref[...]


def after_all(v, *deps):
    return call(copy_after_body, [jax.ShapeDtypeStruct(v.shape, v.dtype)], [], v.size, v, deps=deps)[0]


def call(body, outs, scratch, flops, *args, deps=(), far=(), far_outs=()):
    moved = sum(a.size * a.dtype.itemsize for a in args) + sum(
        o.size * o.dtype.itemsize for o in outs
    )
    n = len(deps)

    def spec(a):
        return pl.BlockSpec(memory_space=pltpu.SMEM if a.dtype == jnp.int32 else pltpu.VMEM)

    return pl.pallas_call(
        lambda *refs: body(*refs[n:]),
        out_shape=outs,
        in_specs=[ANY] * n + [ANY if i in far else spec(a) for i, a in enumerate(args)],
        out_specs=[ANY if i in far_outs else spec(o) for i, o in enumerate(outs)],
        scratch_shapes=scratch,
        compiler_params=pltpu.CompilerParams(vmem_limit_bytes=VMEM_CAP),
        cost_estimate=pl.CostEstimate(flops=flops, bytes_accessed=moved, transcendentals=0),
    )(*deps, *args)


def chunk(i, size):
    return pl.ds(pl.multiple_of(i * size, 16), size)


def clear_borders(pad_ref, side, plane, nf):
    zrow = jnp.zeros(pad_ref.shape[1:], BF)
    pad_ref[0] = zrow
    pad_ref[side + 1] = zrow
    zcol = jnp.zeros((nf, pad_ref.shape[2]), BF)
    for i in range(side):
        pad_ref[i + 1, 0:nf] = zcol
        pad_ref[i + 1, nf + plane : 2 * nf + plane] = zcol


def by_rank(slices, rank):
    odd = lax.rem(rank, 2) == 1
    for p in range(len(slices) // 2):
        a, b = slices[2 * p], slices[2 * p + 1]
        yield lax.bitwise_xor(rank // 2, p), odd, a, b


def halves(odd, own, mate):
    low = lax.broadcasted_iota(jnp.int32, own.shape, 1) < 64
    own, mate = own.astype(F32), mate.astype(F32)
    a, b = jnp.where(odd, mate, own), jnp.where(odd, own, mate)
    top = jnp.where(low, a, pltpu.roll(b, 64, 1))
    bottom = jnp.where(low, pltpu.roll(a, 64, 1), b)
    return top, bottom


def store_packed(rank, mate_ref, keep_ref, part, k, step, low):
    rows_now = chunk(k, step)
    odd = lax.rem(rank, 2) == 1
    for q in range(keep_ref.shape[0]):
        x = part[:step, 128 * q : 128 * q + 128]
        y = part[step:, 128 * q : 128 * q + 128]
        even_slice = jnp.where(low, x, pltpu.roll(y, 64, 1))
        odd_slice = jnp.where(low, pltpu.roll(x, 64, 1), y)
        p = lax.bitwise_xor(rank // 2, q)
        keep_ref[p, rows_now, :] = jnp.where(odd, odd_slice, even_slice).astype(BF)
        mate_ref[p, rows_now, :] = jnp.where(odd, even_slice, odd_slice).astype(BF)


def fetch_kernels(w_ref, ktm_ref, lw_ref, sems):
    nz, _, width = w_ref.shape
    hc = ktm_ref.shape[0]
    copies = []
    for z in range(nz):
        copies.append(pltpu.make_async_copy(
            w_ref.at[z, pl.ds(0, hc)], ktm_ref.at[:, pl.ds(z * width, width)], sems.at[2 * z]))
        copies.append(pltpu.make_async_copy(
            w_ref.at[z, pl.ds(hc, lw_ref.shape[1])], lw_ref.at[z], sems.at[2 * z + 1]))
    for copy in copies:
        copy.start()
    return copies


def join_temporal(lw_ref, lf_ref, ltm_ref):
    ch = ltm_ref.shape[1]
    width = lw_ref.shape[2] // 2
    count = 2 * lw_ref.shape[0]
    size = ltm_ref.shape[0] // count
    for z in range(lw_ref.shape[0]):
        first = lw_ref[z, :, 0:ch].astype(F32)
        off = width % 128
        second = lw_ref[z, :, width - off : width - off + ch + 128].astype(F32)
        second = pltpu.roll(second, ch + 128 - off, 1)[:, 0:ch]
        for b, block in ((2 * z, first), (2 * z + 1, second)):
            lf_ref[b * size : b * size + block.shape[0], :] = block
    ltm_ref[...] = lf_ref[0 : ltm_ref.shape[0], :].astype(BF)


def prepare_body(w_ref, kn_out, l_out, lt_out, ktm_ref, lw_ref, lf_ref, sems):
    hc, ch = ktm_ref.shape[0], l_out.shape[1]
    for copy in fetch_kernels(w_ref, ktm_ref, lw_ref, sems):
        copy.wait()
    for t in range(9):
        kn_out[t] = ktm_ref[:, t * ch : (t + 1) * ch].astype(F32).T.astype(BF)
    join_temporal(lw_ref, lf_ref, l_out)
    for t in range(3):
        lt_out[t] = lf_ref[t * hc : (t + 1) * hc].T.astype(BF)


def prepare(w, hc, ch):
    outs = [
        jax.ShapeDtypeStruct((9, ch, hc), BF),
        jax.ShapeDtypeStruct((3 * hc, ch), BF),
        jax.ShapeDtypeStruct((3, ch, hc), BF),
    ]
    tall = w.shape[1] - hc
    scratch = [
        pltpu.VMEM((hc, 9 * ch), BF),
        pltpu.VMEM((w.shape[0], tall, w.shape[2]), BF),
        pltpu.VMEM((3 * hc + tall, ch), F32),
        pltpu.SemaphoreType.DMA((2 * w.shape[0],)),
    ]
    return call(prepare_body, outs, scratch, 2 * w.size * 512, w, far=(0,))


def conv_body(side, first, rank_ref, *refs):
    n = 1 if first else 8
    slices = refs[:n]
    (kn_in, ltm_ref, vec_ref, before_ref, after_ref,
     pad_out, hid_out, xhat_out, rs_ref, mate_ref, keep_ref,
     pad_ref, hid_ref, xhat_ref, sp_ref, kn_ref, sems) = refs[n:]
    rank = rank_ref[0]
    kn_copy = pltpu.make_async_copy(kn_in, kn_ref, sems.at[0])
    kn_copy.start()
    ch, hc = pad_ref.shape[2], hid_ref.shape[1]
    rows = hid_ref.shape[0]
    plane = rows // side
    nf = plane // side
    step = plane // 2
    clear_borders(pad_ref, side, plane, nf)
    if first:
        for i in range(side):
            pad_ref[i + 1, nf : nf + plane] = slices[0][i * plane : (i + 1) * plane]
    else:
        def place(k, carry):
            for q, odd, a_ref, b_ref in by_rank(slices, rank):
                top, bottom = halves(odd, a_ref[chunk(k, step), :], b_ref[chunk(k, step), :])
                lanes = pl.ds(pl.multiple_of(128 * q, 128), 128)
                for piece, kk in ((top, k), (bottom, k + side)):
                    at = nf + lax.rem(kk, 2) * step
                    pad_ref[1 + kk // 2, pl.ds(pl.multiple_of(at, 16), step), lanes] = piece.astype(BF)
            return carry

        lax.fori_loop(0, side, place, 0, unroll=True)
    pad_copy = pltpu.make_async_copy(pad_ref, pad_out, sems.at[1])
    pad_copy.start()
    kn_copy.wait()

    def conv(i, total):
        acc = jnp.zeros((plane, hc), F32)
        for t in range(9):
            r, c = t // 3, t % 3
            acc += nn(pad_ref[i + r, c * nf : c * nf + plane, :], kn_ref[t])
        sp_ref[i] = acc
        return total + jnp.sum(acc, axis=0, keepdims=True)

    mean = lax.fori_loop(0, side, conv, jnp.zeros((1, hc), F32), unroll=True) / rows

    def square(i, total):
        cen = sp_ref[i] - mean
        return total + jnp.sum(cen * cen, axis=0, keepdims=True)

    var = lax.fori_loop(0, side, square, jnp.zeros((1, hc), F32), unroll=True) / rows
    rs = lax.rsqrt(var + eps)
    rs_ref[...] = rs
    gain, bias = vec_ref[0:1, :], vec_ref[1:2, :]

    def act(i, carry):
        xhat = (sp_ref[i] - mean) * rs
        xhat_ref[i] = xhat
        v = xhat * gain + bias
        v = v * jax.nn.sigmoid(v)
        sp_ref[i] = v
        hid_ref[chunk(i, plane), :] = v.astype(BF)
        return carry

    lax.fori_loop(0, side, act, 0, unroll=True)
    late = [
        pltpu.make_async_copy(hid_ref, hid_out, sems.at[2]),
        pltpu.make_async_copy(xhat_ref, xhat_out, sems.at[3]),
    ]
    for copy in late:
        copy.start()
    low = lax.broadcasted_iota(jnp.int32, (step, 128), 1) < 64

    def temporal(k, carry):
        pieces = []
        for kk in (k, k + side):
            par = lax.rem(kk, 2)
            h = sp_ref[kk // 2, pl.ds(pl.multiple_of(par * step, 8), step), :]
            at = pl.multiple_of(par * (step % nf), 8)
            pieces.append((
                (pltpu.roll(h, 1, 0) * before_ref[pl.ds(at, step), :]).astype(BF),
                h.astype(BF),
                (pltpu.roll(h, step - 1, 0) * after_ref[pl.ds(at, step), :]).astype(BF),
            ))
        part = sum(
            nn(jnp.concatenate([x, y], axis=0), ltm_ref[t * hc : (t + 1) * hc])
            for t, (x, y) in enumerate(zip(*pieces))
        )
        store_packed(rank, mate_ref, keep_ref, part, k, step, low)
        return carry

    lax.fori_loop(0, side, temporal, 0, unroll=True)
    for copy in [pad_copy] + late:
        copy.wait()


def conv_forward(rank, g, kn, lt, vec, before, after, side, pixels, ch, deps=()):
    hc = vec.shape[1]
    plane = pixels // side
    nf = plane // side
    n = len(g)
    shapes = [
        ((side + 2, plane + 2 * nf, ch), BF),
        ((pixels, hc), BF),
        ((side, plane, hc), F32),
    ]
    outs = [jax.ShapeDtypeStruct(*s) for s in shapes] + [
        jax.ShapeDtypeStruct((1, hc), F32),
        jax.ShapeDtypeStruct((4, pixels // 2, 128), BF),
        jax.ShapeDtypeStruct((4, pixels // 2, 128), BF),
    ]
    scratch = [pltpu.VMEM(*s) for s in shapes] + [
        pltpu.VMEM((side, plane, hc), F32),
        pltpu.VMEM((9, ch, hc), BF),
        pltpu.SemaphoreType.DMA((4,)),
    ]
    flops = 2 * pixels * hc * 12 * ch
    return call(functools.partial(conv_body, side, n == 1), outs, scratch, flops,
                rank, *g, kn, lt, vec, before, after,
                deps=deps, far=(n + 1,), far_outs=(0, 1, 2))


def fold(v):
    return v + pltpu.roll(v, 64, 1)


def total_of(refs):
    t = refs[0][...].astype(F32)
    for ref in refs[1:]:
        t += ref[...].astype(F32)
    return t


def pair_sum_body(keep_ref, mate_ref, *out_refs):
    for p, ref in enumerate(out_refs):
        ref[...] = (keep_ref[p].astype(F32) + mate_ref[p].astype(F32)).astype(ref.dtype)


def pair_sum(keep, arrived, deps=()):
    shape = keep.shape[1:]
    outs = [jax.ShapeDtypeStruct(shape, BF)] * keep.shape[0]
    return call(pair_sum_body, outs, [], keep.size, keep, arrived, deps=deps)


def out_norm_body(n, has_skip, *refs):
    parts, refs = refs[:n], refs[n:]
    if has_skip:
        vec_ref, skip_ref, xhat_ref, rs_ref, pre_ref, res_ref = refs
    else:
        vec_ref, xhat_ref, rs_ref, pre_ref, res_ref = refs
    t = total_of(parts)
    pixels = 2 * t.shape[0]
    mean = fold(jnp.sum(t, axis=0, keepdims=True)) / pixels
    cen = t - mean
    rs = lax.rsqrt(fold(jnp.sum(cen * cen, axis=0, keepdims=True)) / pixels + eps)
    xhat = cen * rs
    pre = xhat * vec_ref[0:1, :] + vec_ref[1:2, :]
    if has_skip:
        pre = pre + skip_ref[...].astype(F32)
    xhat_ref[...] = xhat
    rs_ref[...] = rs
    pre_ref[...] = pre
    res_ref[...] = (pre * jax.nn.sigmoid(pre)).astype(BF)


def out_norm(parts, vec, skip):
    half = parts[0].shape[0]
    outs = [
        jax.ShapeDtypeStruct((half, 128), F32),
        jax.ShapeDtypeStruct((1, 128), F32),
        jax.ShapeDtypeStruct((half, 128), F32),
        jax.ShapeDtypeStruct((half, 128), BF),
    ]
    args = (*parts, vec) + (() if skip is None else (skip,))
    body = functools.partial(out_norm_body, len(parts), skip is not None)
    return call(body, outs, [], half * 128 * 10, *args)


def out_back_body(n, *refs):
    parts, (pre_ref, xhat_ref, rs_ref, vec_ref, dpre_ref, dt_ref, sums_ref) = refs[:n], refs[n:]
    g = total_of(parts)
    pre, xhat = pre_ref[...], xhat_ref[...]
    sig = jax.nn.sigmoid(pre)
    dpre = g * (sig * (1.0 + pre * (1.0 - sig)))
    pixels = 2 * pre.shape[0]
    sb = fold(jnp.sum(dpre, axis=0, keepdims=True))
    sg = fold(jnp.sum(dpre * xhat, axis=0, keepdims=True))
    dpre_ref[...] = dpre.astype(BF)
    scale = vec_ref[0:1, :] * rs_ref[...]
    dt_ref[...] = (scale * (dpre - sb / pixels - xhat * (sg / pixels))).astype(BF)
    sums_ref[0:1, :] = sg
    sums_ref[1:2, :] = sb


def out_back(parts, pre, xhat, rs, vec, deps=()):
    half = pre.shape[0]
    outs = [
        jax.ShapeDtypeStruct((half, 128), BF),
        jax.ShapeDtypeStruct((half, 128), BF),
        jax.ShapeDtypeStruct((2, 128), F32),
    ]
    args = (*parts, pre, xhat, rs, vec)
    return call(functools.partial(out_back_body, len(parts)), outs, [], half * 1280, *args, deps=deps)


def conv_back_body(side, rank_ref, *refs):
    slices, (xhat_in, rs_ref, w_ref, lnt_ref, vec_ref, before_ref, after_ref,
             dt_out, ds_out, sums_ref, mate_ref, keep_ref,
             dt_ref, ds_ref, xhat_ref, dy_ref, pad_ref, ktm_ref, sems) = refs[:8], refs[8:]
    half = slices[0].shape[0]
    rank = rank_ref[0]
    nz, _, width = w_ref.shape
    rows = 2 * half
    plane = rows // side
    nf = plane // side
    step = plane // 2
    hc = ds_ref.shape[1]
    ch = dt_ref.shape[1]
    fetched = [
        pltpu.make_async_copy(
            w_ref.at[z, pl.ds(0, hc)], ktm_ref.at[:, pl.ds(z * width, width)], sems.at[z])
        for z in range(nz)
    ]
    xhat_copy = pltpu.make_async_copy(xhat_in, xhat_ref, sems.at[nz])
    for copy in fetched + [xhat_copy]:
        copy.start()
    clear_borders(pad_ref, side, plane, nf)

    def place(k, carry):
        for q, odd, a_ref, b_ref in by_rank(slices, rank):
            top, bottom = halves(odd, a_ref[chunk(k, step), :], b_ref[chunk(k, step), :])
            lanes = pl.ds(pl.multiple_of(128 * q, 128), 128)
            dt_ref[chunk(k, step), lanes] = top.astype(BF)
            dt_ref[pl.ds(pl.multiple_of(half + k * step, 16), step), lanes] = bottom.astype(BF)
        return carry

    lax.fori_loop(0, side, place, 0, unroll=True)
    dt_copy = pltpu.make_async_copy(dt_ref, dt_out, sems.at[nz + 1])
    dt_copy.start()
    xhat_copy.wait()
    gain, bias = vec_ref[0:1, :], vec_ref[1:2, :]

    def hidden_grad(i, sums):
        dt = dt_ref[chunk(i, plane), :]
        early = nn(dt, lnt_ref[0]) * before_ref[0:plane, :]
        late = nn(dt, lnt_ref[2]) * after_ref[0:plane, :]
        dh = nn(dt, lnt_ref[1]) + pltpu.roll(early, plane - 1, 0) + pltpu.roll(late, 1, 0)
        xhat = xhat_ref[i]
        v = xhat * gain + bias
        sig = jax.nn.sigmoid(v)
        dy = dh * (sig * (1.0 + v * (1.0 - sig)))
        dy_ref[i] = dy
        return (
            sums[0] + jnp.sum(dy * xhat, axis=0, keepdims=True),
            sums[1] + jnp.sum(dy, axis=0, keepdims=True),
        )

    zero = jnp.zeros((1, hc), F32)
    sg, sb = lax.fori_loop(0, side, hidden_grad, (zero, zero), unroll=True)
    sums_ref[0:1, :] = sg
    sums_ref[1:2, :] = sb
    scale = gain * rs_ref[...]

    def spatial_grad(i, carry):
        ds = (scale * (dy_ref[i] - sb / rows - xhat_ref[i] * (sg / rows))).astype(BF)
        pad_ref[i + 1, nf : nf + plane] = ds
        ds_ref[chunk(i, plane), :] = ds
        return carry

    lax.fori_loop(0, side, spatial_grad, 0, unroll=True)
    ds_copy = pltpu.make_async_copy(ds_ref, ds_out, sems.at[nz + 2])
    ds_copy.start()
    for copy in fetched:
        copy.wait()
    low = lax.broadcasted_iota(jnp.int32, (step, 128), 1) < 64

    def back(k, carry):
        acc = jnp.zeros((2 * step, ch), F32)
        for t in range(9):
            r, c = 2 - t // 3, 2 - t % 3
            pieces = []
            for kk in (k, k + side):
                at = c * nf + lax.rem(kk, 2) * step
                pieces.append(pad_ref[kk // 2 + r, pl.ds(pl.multiple_of(at, 16), step), :])
            acc += nn(jnp.concatenate(pieces, axis=0), ktm_ref[:, t * ch : (t + 1) * ch])
        store_packed(rank, mate_ref, keep_ref, acc, k, step, low)
        return carry

    lax.fori_loop(0, side, back, 0, unroll=True)
    dt_copy.wait()
    ds_copy.wait()


def conv_back(rank, g, xhat, rs, w, lnt, vec, before, after, side, deps=()):
    half = g[0].shape[0]
    hc = vec.shape[1]
    ch = len(g) * 64
    pixels = 2 * half
    plane = pixels // side
    nf = plane // side
    outs = [
        jax.ShapeDtypeStruct((pixels, ch), BF),
        jax.ShapeDtypeStruct((pixels, hc), BF),
        jax.ShapeDtypeStruct((2, hc), F32),
        jax.ShapeDtypeStruct((4, half, 128), BF),
        jax.ShapeDtypeStruct((4, half, 128), BF),
    ]
    scratch = [
        pltpu.VMEM((pixels, ch), BF),
        pltpu.VMEM((pixels, hc), BF),
        pltpu.VMEM((side, plane, hc), F32),
        pltpu.VMEM((side, plane, hc), F32),
        pltpu.VMEM((side + 2, plane + 2 * nf, hc), BF),
        pltpu.VMEM((hc, 9 * ch), BF),
        pltpu.SemaphoreType.DMA((w.shape[0] + 3,)),
    ]
    flops = 2 * pixels * hc * 12 * ch
    return call(functools.partial(conv_back_body, side), outs, scratch, flops,
                rank, *g, xhat, rs, w, lnt, vec, before, after,
                deps=deps, far=(9, 11), far_outs=(0, 1))


def grads_body(side, pad_ref, hid_ref, ds_ref, dt_ref, before_ref, after_ref, mid_ref, out_ref,
               sg_ref, dst_ref, taps_ref, tg_ref, vec_ref):
    ch = pad_ref.shape[2]
    hc = hid_ref.shape[1]
    plane = hid_ref.shape[0] // side
    nf = plane // side
    for i in (0, 1, side + 2, side + 3):
        dst_ref[i] = jnp.zeros(dst_ref.shape[1:], BF)
    for i in range(side):
        at = slice(i * plane, (i + 1) * plane)
        h = hid_ref[at, :].astype(F32)
        taps_ref[i, 0:hc] = (pltpu.roll(h, 1, 0) * before_ref[0:plane, :]).T.astype(BF)
        taps_ref[i, hc : 2 * hc] = h.T.astype(BF)
        taps_ref[i, 2 * hc : 3 * hc] = (pltpu.roll(h, plane - 1, 0) * after_ref[0:plane, :]).T.astype(BF)
        dst_ref[i + 2] = ds_ref[at, :].astype(F32).T.astype(BF)
    tg_ref[0 : 3 * hc, :] = sum(
        nn(taps_ref[i], dt_ref[i * plane : (i + 1) * plane, :]) for i in range(side)
    )
    tg_ref[3 * hc :, :] = jnp.zeros((tg_ref.shape[0] - 3 * hc, ch), F32)
    nz, _, width = sg_ref.shape
    size = 3 * hc // (2 * nz)
    vec_ref[...] = jnp.zeros(vec_ref.shape, F32)
    vec_ref[size : size + 2, 0:hc] = mid_ref[...]
    vec_ref[size + 2 : size + 4, 0:128] = out_ref[...]
    tall = vec_ref.shape[0]
    inside = lax.broadcasted_iota(jnp.int32, (tall, ch), 0) < size
    off = (width // 2) % 128
    for z in range(nz):
        first, second = [
            jnp.where(inside, tg_ref[b * size : b * size + tall, :], vec_ref[...])
            for b in (2 * z, 2 * z + 1)
        ]
        start = width // 2 - off
        sg_ref[z, hc : hc + tall, 0:ch] = first.astype(BF)
        second = pltpu.roll(jnp.concatenate([second, jnp.zeros((tall, 128), F32)], axis=1), off, 1)
        sg_ref[z, hc : hc + tall, start : start + ch + 128] = second.astype(BF)
    for c in range(3):
        acc = sum(
            nn(dst_ref[i : i + 3].reshape(3 * hc, plane), pad_ref[i, c * nf : c * nf + plane, :])
            for i in range(1, side + 1)
        )
        for r in range(3):
            first = (3 * r + c) * ch
            end = first + ch
            at = (2 - r) * hc
            done = 0
            while first < end:
                z = first // width
                last = min(end, (z + 1) * width)
                sg_ref[z, 0:hc, first - z * width : last - z * width] = (
                    acc[at : at + hc, done : done + last - first].astype(BF)
                )
                done += last - first
                first = last


def kernel_grads(pad, hidden, ds, dt, before, after, mid, out, side, shape, deps=()):
    pixels, hc = hidden.shape
    ch = dt.shape[1]
    plane = pixels // side
    outs = [jax.ShapeDtypeStruct(shape, BF)]
    tall = shape[1] - hc
    scratch = [
        pltpu.VMEM((side + 4, hc, plane), BF),
        pltpu.VMEM((side, 3 * hc, plane), BF),
        pltpu.VMEM((3 * hc + tall, ch), F32),
        pltpu.VMEM((tall, ch), F32),
    ]
    flops = 2 * pixels * hc * 12 * ch
    return call(functools.partial(grads_body, side), outs, scratch, flops,
                pad, hidden, ds, dt, before, after, mid, out, deps=deps)[0]


def copy_after_body(v_ref, out_ref):
    out_ref[...] = v_ref[...]


def after_all(v, *deps):
    return call(copy_after_body, [jax.ShapeDtypeStruct(v.shape, v.dtype)], [], v.size, v, deps=deps)[0]


def hop(v, k):
    n = 1
    for name in EVERY:
        n *= lax.axis_size(name)
    return lax.ppermute(v, EVERY, [(i, i ^ k) for i in range(n)])


def plane_gather(v):
    got = {0: v}
    for k in (6, 2, 4, 1):
        got[k] = hop(v, k)
    for k in (2, 4, 6):
        got[k ^ 1] = hop(got[k], 1)
    return [got[k] for k in range(8)]


def plane_reduce(mate, keep, deps=()):
    sums = pair_sum(keep, hop(mate, 1), deps)
    arrived = {k: hop(sums[k // 2], k) for k in (6, 2, 4)}
    return [sums[0], arrived[2], arrived[4], arrived[6]]


def to_section(v, section, n_seg):
    y = lax.axis_index("y")
    near = lax.dynamic_index_in_dim(v, y, 0, keepdims=False)
    far = lax.dynamic_index_in_dim(v, 1 - y, 0, keepdims=False)
    n = 2 * n_seg * lax.axis_size("z")
    got = []
    for base, block in ((0, near), (n_seg, far)):
        row = []
        for low in range(n_seg):
            k = base + (low ^ section)
            if k == 0:
                row.append(block)
            else:
                pairs = [(i, i ^ k) for i in range(n) if i % n_seg == low]
                row.append(lax.ppermute(block, EVERY, pairs))
        got.append(jnp.stack(row))
    same, other = got
    return jnp.where(y == 0, jnp.concatenate([same, other]), jnp.concatenate([other, same]))

def from_section(blocks, section, n_seg):
    y = lax.axis_index("y")
    blocks = blocks.reshape(2, n_seg, *blocks.shape[1:])
    near = lax.dynamic_index_in_dim(blocks, y, 0, keepdims=False)
    far = lax.dynamic_index_in_dim(blocks, 1 - y, 0, keepdims=False)
    n = 2 * n_seg * lax.axis_size("z")
    got = []
    for base, held in ((0, near), (n_seg, far)):
        total = None
        for low in range(n_seg):
            k = base + (low ^ section)
            if k == 0:
                mine = lax.axis_index(("x", "c")) == section
                piece = jnp.where(mine, held[low], jnp.zeros_like(held[low]))
            else:
                pairs = [(i, i ^ k) for i in range(n) if i % n_seg == section]
                piece = lax.ppermute(held[low], EVERY, pairs)
            total = piece if total is None else total + piece
        got.append(total)
    near, far = got
    return jnp.where(y == 0, jnp.stack([near, far]), jnp.stack([far, near]))


def on_device(frames, cot, starts, ks, ktm, mg, mb, og, ob):
    nz, n_rank, n_seg = lax.axis_size("z"), 8, 4
    n_dp = nz * 2
    fr, side, ch = frames.shape[0], frames.shape[1], frames.shape[3]
    area = side * side
    hid = ks.shape[2]
    hc, cc = hid // n_rank, ch // n_rank
    q = hc // n_rank
    rank = lax.axis_index(PLANE)
    rank_now = rank.astype(jnp.int32).reshape(1)
    d_index = lax.axis_index(("z", "y"))
    s_index = lax.axis_index(("x", "c"))
    nf = n_dp * fr
    pixels = area * nf
    half = pixels // 2

    to_plane = [(d * n_seg + s, s * n_rank + d) for d in range(n_dp) for s in range(n_seg)]
    from_plane = [(b, a) for a, b in to_plane]
    rows = fr * area
    flag_row = jnp.pad(starts.astype(BF)[None], ((0, 11), (0, ch - fr)))
    lead = rows + 12
    moving = jnp.concatenate([frames.reshape(rows, ch), flag_row, cot.reshape(rows, ch)], axis=0)
    moving = lax.ppermute(moving, EVERY, to_plane)

    perm = (jnp.arange(hid).reshape(n_rank, n_rank, q).transpose(1, 0, 2).reshape(hid)[:, None]
            == jnp.arange(hid)[None, :]).astype(BF)
    kt = lax.dot_general(perm, ks[0].astype(BF), (((1,), (1,)), ((), ())),
                         preferred_element_type=F32).astype(BF)
    kt = kt.reshape(n_rank, hc, ks.shape[1])
    lrows, width = ktm.shape[1] // n_rank, ks.shape[1]
    lt = ktm[0].astype(BF).reshape(-1, n_rank, q, ch).transpose(1, 0, 2, 3).reshape(n_rank, lrows, ch)
    lt = jnp.pad(after_all(lt, moving), ((0, 0), (0, 0), (0, width - ch)))
    extra = jnp.concatenate([v.astype(BF) for v in (mg, mb, og, ob)], axis=1)
    tall = -(-(lrows + 4) // 16) * 16
    extra = jnp.pad(extra, ((0, tall - lrows - 1), (0, width - extra.shape[1])))
    w = jnp.concatenate([kt, lt, jnp.broadcast_to(extra, (n_rank, *extra.shape))], axis=1)
    high = hc + tall

    def whole_section(v):
        v = v.transpose(1, 0, 2).reshape(high, 2 * width)
        return lax.all_gather(v, "z", axis=0)

    first = from_section(w, 0, n_seg)
    ws = [whole_section(first)]

    group = 7
    own = moving[lead:].reshape(group, rows // group, n_rank, cc).transpose(2, 1, 0, 3)
    own = own.reshape(n_rank, rows // group, group * cc)
    own = jnp.pad(own, ((0, 0), (0, 4), (0, ch - group * cc)))
    own = jnp.concatenate([jnp.broadcast_to(moving[:lead], (n_rank, lead, ch)), own], axis=1)
    gathered = lax.all_to_all(after_all(own, first), PLANE, 0, 0)
    w = lax.all_to_all(after_all(w, gathered), PLANE, 0, 0)
    w = w.reshape(2, n_seg, high, width)
    ws += [whole_section(w[:, s]) for s in range(1, n_seg)]
    mids, outs = [], []
    for s in range(n_seg):
        row = ws[s][:, hc + lrows].reshape(n_dp, width).astype(F32)
        mids.append(jnp.stack([
            lax.dynamic_slice_in_dim(row[:, i * hc : (i + 1) * hc], rank * q, q, axis=1).reshape(hc)
            for i in range(2)]))
        own = lax.dynamic_index_in_dim(row, rank, 0, keepdims=False)
        outs.append(jnp.stack([
            jnp.tile(own[2 * hc + i * cc : 2 * hc + (i + 1) * cc], 2) for i in range(2)]))

    def by_pixel(v):
        width = v.shape[2]
        v = v.reshape(n_rank * fr, area, width).transpose(1, 0, 2)
        return v.reshape(pixels, width)

    def packed(v):
        return jnp.concatenate([v[:half], v[half:]], axis=1)

    a0 = by_pixel(gathered[:, :rows])
    flags = gathered[:, rows, :fr].reshape(nf) > 0.5
    slot = jnp.arange(nf) % fr
    before = jnp.where(flags | (slot == 0), 0.0, 1.0)
    after = jnp.where(jnp.roll(flags, -1) | (slot == fr - 1), 0.0, 1.0)
    spread = (side * nf + nf, hc)
    before = jnp.broadcast_to(jnp.tile(before, side + 1)[:, None], spread)
    after = jnp.broadcast_to(jnp.tile(after, side + 1)[:, None], spread)
    skip = packed(lax.dynamic_slice_in_dim(a0, rank * cc, cc, axis=1))

    cot_own = gathered[:, lead : lead + rows // group, : group * cc]
    cot_own = cot_own.reshape(n_rank, rows // group, group, cc).transpose(0, 2, 1, 3)
    cot_own = packed(by_pixel(cot_own.reshape(n_rank, rows, cc)))

    def to_frames(*slices):
        n = len(slices)
        v = jnp.stack([jnp.concatenate([v[:, :cc], v[:, cc:]], axis=0) for v in slices])
        v = v.reshape(n, area, n_rank, fr, cc).transpose(2, 0, 1, 3, 4).reshape(n_rank, n * rows, cc)
        v = lax.all_to_all(v, PLANE, 0, 0).transpose(1, 0, 2).reshape(n * rows, ch)
        v = lax.ppermute(v, EVERY, from_plane).reshape(n, area, fr, ch).transpose(0, 2, 1, 3)
        return v.reshape(n, *frames.shape)

    saved = []
    g = [a0]
    for s in range(n_seg):
        kn, lt, lnt = prepare(ws[s], hc, ch)
        pad, hidden, xm, rm, mate, keep = conv_forward(
            rank_now, g, kn, lt, mids[s], before, after, side, pixels, ch)
        parts = plane_reduce(mate, keep)
        xo, ro, pre, res = out_norm(parts, outs[s], skip if s % 2 == 1 else None)
        saved.append((pad, hidden, xm, rm, xo, ro, pre, lnt))
        if s % 2 == 1:
            skip = res
        if s < n_seg - 1:
            g = plane_gather(res)

    parts = [cot_own]
    skip_grad = None
    def by_row(v):
        return v.reshape(high, 2, width).transpose(1, 0, 2)

    grads, raw = [], None
    for s in reversed(range(n_seg)):
        pad, hidden, xm, rm, xo, ro, pre, lnt = saved[s]
        if s == 1:
            parts = parts + [skip_grad]
        deps = () if raw is None else (raw, *grads[len(grads) - 1 :])
        dpre, dt, osum = out_back(parts, pre, xo, ro, outs[s], deps=deps)
        if raw is not None:
            grads.append(lax.psum_scatter(after_all(raw, dt), "z", scatter_dimension=0))
        if s % 2 == 1:
            skip_grad = dpre
        dtf, ds, msum, mate, keep = conv_back(
            rank_now, plane_gather(dt), xm, rm, ws[s], lnt, mids[s], before, after, side)
        if s > 0:
            parts = plane_reduce(mate, keep)
        raw = kernel_grads(pad, hidden, ds, dtf, before, after, msum, osum, side, ws[s].shape,
                           deps=parts[:1] if s > 0 else ())
    last = lax.psum_scatter(raw, "z", scatter_dimension=0)
    early = jnp.stack([jnp.zeros((2, high, width), BF)] + [by_row(v) for v in grads[::-1]], axis=1)
    early = lax.all_to_all(early.reshape(n_rank, high, width), PLANE, 0, 0)
    parts = plane_reduce(mate, keep, deps=(early,))

    da = sum(p.astype(F32) for p in parts) + skip_grad.astype(F32)
    output, frames_grad = to_frames(res, da.astype(BF))
    frames_grad = frames_grad.astype(F32)

    g = jnp.where(s_index == 0, to_section(by_row(last), 0, n_seg), early)
    space_grad = lax.dot_general(g[:, :hc].reshape(hid, width), perm, (((0,), (0,)), ((), ())),
                                 preferred_element_type=F32)
    tg = g[:, hc : hc + lrows, :ch].reshape(n_rank, -1, q, ch)
    time_grad = tg.transpose(1, 0, 2, 3).reshape(-1, ch).astype(F32)
    sums = g[:, hc + lrows : hc + lrows + 4].astype(F32)

    def mid_own(v):
        return lax.dynamic_slice_in_dim(v[:, :hc], d_index * q, q, axis=1).reshape(1, hc)

    own = lax.dynamic_index_in_dim(sums, d_index, 0, keepdims=False)
    return (
        output,
        frames_grad,
        space_grad[None],
        time_grad[None],
        mid_own(sums[:, 0]),
        mid_own(sums[:, 1]),
        own[2:3, :cc],
        own[3:4, :cc],
    )


def from_behind(value, axis, steps):
    count = lax.axis_size(axis)
    leading, last = (max(0, -steps), min(count, count - steps))
    return lax.ppermute(value, axis, [(source, source + steps) for source in range(leading, last)])


def space_apply(current, kernel):
    frame_side = current.shape[1]
    padded = jnp.pad(current, ((0, 0), (1, 1), (1, 1), (0, 0)))
    stacked = jnp.concatenate(
        [
            padded[:, row_shift : row_shift + frame_side, col_shift : col_shift + frame_side, :]
            for row_shift in range(3)
            for col_shift in range(3)
        ],
        axis=-1,
    )
    return (
        stacked,
        jnp.einsum("fijc,co->fijo", stacked, kernel, preferred_element_type=jnp.float32),
    )


def space_back(gradient, kernel):
    frame_side = gradient.shape[1]
    channels = kernel.shape[0] // 9
    spread = jnp.einsum("fijo,co->fijc", gradient, kernel, preferred_element_type=jnp.float32)
    total = jnp.zeros((gradient.shape[0], frame_side + 2, frame_side + 2, channels), jnp.float32)
    for tap_index in range(9):
        row_shift = tap_index // 3
        col_shift = tap_index % 3
        piece_now = spread[..., tap_index * channels : (tap_index + 1) * channels]
        total = total + jnp.pad(
            piece_now, ((0, 0), (row_shift, 2 - row_shift), (col_shift, 2 - col_shift), (0, 0))
        )
    return total[:, 1 : frame_side + 1, 1 : frame_side + 1, :]


def time_apply(current, kernel, before_mask, after_mask):
    blanks = jnp.zeros_like(current[:1])
    earlier = jnp.concatenate([blanks, current[:-1]], axis=0) * before_mask[
        :, None, None, None
    ].astype(current.dtype)
    later = jnp.concatenate([current[1:], blanks], axis=0) * after_mask[:, None, None, None].astype(
        current.dtype
    )
    stacked = jnp.concatenate([earlier, current, later], axis=-1)
    return (
        stacked,
        jnp.einsum("fijc,co->fijo", stacked, kernel, preferred_element_type=jnp.float32),
    )


def time_back(gradient, kernel, before_mask, after_mask):
    channels = kernel.shape[0] // 3
    spread = jnp.einsum("fijo,co->fijc", gradient, kernel, preferred_element_type=jnp.float32)
    early_part = spread[..., :channels] * before_mask[:, None, None, None]
    late_part = spread[..., 2 * channels :] * after_mask[:, None, None, None]
    blanks = jnp.zeros_like(early_part[:1])
    moved_early = jnp.concatenate([early_part[1:], blanks], axis=0)
    moved_late = jnp.concatenate([blanks, late_part[:-1]], axis=0)
    return spread[..., channels : 2 * channels] + moved_early + moved_late


def moments(values, pixel_count):
    average = lax.psum(jnp.sum(values, axis=(0, 1, 2)), "dp") / pixel_count
    centered = values - average
    spread = lax.psum(jnp.sum(centered * centered, axis=(0, 1, 2)), "dp") / pixel_count
    return (average, lax.rsqrt(spread + eps))


def reduce_back(gradient, normed):
    return lax.psum(
        (jnp.sum(gradient, axis=(0, 1, 2)), jnp.sum(gradient * normed, axis=(0, 1, 2))), "dp"
    )


def silu_slope(values):
    sigmoid_now = jax.nn.sigmoid(values)
    return sigmoid_now * (1.0 + values * (1.0 - sigmoid_now))


def pick_slot(stack, slot_index):
    return lax.dynamic_index_in_dim(stack, slot_index, 0, keepdims=False)


def store_slot(stack, value, slot_index, usable):
    previous = pick_slot(stack, slot_index)
    return lax.dynamic_update_index_in_dim(stack, jnp.where(usable, value, previous), slot_index, 0)


def on_device_general(
    frames, cotangent, starts, space_kernel, time_kernel, mid_gain, mid_bias, out_gain, out_bias
):
    n_segment = lax.axis_size("segment")
    n_data = lax.axis_size("dp")
    segment_index = lax.axis_index("segment")
    odd_segment = segment_index % 2 == 1
    last_segment = segment_index == n_segment - 1
    first_segment = segment_index == 0
    frame_count = frames.shape[0]
    frame_side = frames.shape[1]
    channels = frames.shape[3]
    hidden_units = mid_gain.shape[1] * n_data
    pixel_count = n_data * frame_count * frame_side * frame_side
    turns = 2 * n_segment - 1
    block_shape = (n_segment,) + frames.shape
    all_frames, all_cot, all_starts = (
        lax.all_gather(frames, "segment", axis=0, tiled=True),
        lax.all_gather(cotangent, "segment", axis=0, tiled=True),
        lax.all_gather(starts.astype(jnp.bfloat16), "segment", axis=0, tiled=True),
    )
    frame_stack = all_frames.reshape(block_shape)
    cot_stack = all_cot.reshape(block_shape)
    clip_flags = all_starts.astype(jnp.float32).reshape(n_segment, frame_count)
    positions = jnp.arange(frame_count)
    before_mask = jnp.where((clip_flags > 0.5) | (positions == 0), 0.0, 1.0)
    following = jnp.concatenate([clip_flags[:, 1:], jnp.ones((n_segment, 1), jnp.float32)], axis=1)
    after_mask = jnp.where(following > 0.5, 0.0, 1.0)
    gathered = (
        lax.all_gather(space_kernel[0].astype(jnp.bfloat16), "dp", axis=0, tiled=True),
        lax.all_gather(time_kernel[0].astype(jnp.bfloat16), "dp", axis=0, tiled=True),
        lax.all_gather(mid_gain[0].astype(jnp.bfloat16), "dp", axis=0, tiled=True),
        lax.all_gather(mid_bias[0].astype(jnp.bfloat16), "dp", axis=0, tiled=True),
        lax.all_gather(out_gain[0].astype(jnp.bfloat16), "dp", axis=0, tiled=True),
        lax.all_gather(out_bias[0].astype(jnp.bfloat16), "dp", axis=0, tiled=True),
    )
    space_low, time_low = (gathered[0], gathered[1])
    mid_gain_now = gathered[2].astype(jnp.float32)
    mid_bias_now = gathered[3].astype(jnp.float32)
    out_gain_now = gathered[4].astype(jnp.float32)
    out_bias_now = gathered[5].astype(jnp.float32)
    incoming = jnp.zeros_like(frames)
    carried = jnp.zeros_like(frames)
    kept_input = jnp.zeros(block_shape, jnp.bfloat16)
    kept_skip = jnp.zeros(block_shape, jnp.bfloat16)
    kept_mid_mean = jnp.zeros((n_segment, hidden_units), jnp.float32)
    kept_mid_scale = jnp.zeros((n_segment, hidden_units), jnp.float32)
    kept_out_mean = jnp.zeros((n_segment, channels), jnp.float32)
    kept_out_scale = jnp.zeros((n_segment, channels), jnp.float32)
    results = jnp.zeros(block_shape, jnp.float32)
    for turn_index in range(turns):
        micro_index = turn_index - segment_index
        usable = (micro_index >= 0) & (micro_index < n_segment)
        slot_index = jnp.clip(micro_index, 0, n_segment - 1)
        current = jnp.where(first_segment, pick_slot(frame_stack, slot_index), incoming)
        skip_input = carried
        _, spatial = space_apply(current, space_low)
        mid_mean, mid_scale = moments(spatial, pixel_count)
        hidden_act = jax.nn.silu(
            (spatial - mid_mean) * mid_scale * mid_gain_now + mid_bias_now
        ).astype(jnp.bfloat16)
        _, temporal = time_apply(
            hidden_act,
            time_low,
            pick_slot(before_mask, slot_index),
            pick_slot(after_mask, slot_index),
        )
        out_mean, out_scale = moments(temporal, pixel_count)
        pre_act = (
            (temporal - out_mean) * out_scale * out_gain_now
            + out_bias_now
            + jnp.where(odd_segment, skip_input.astype(jnp.float32), 0.0)
        )
        result = jax.nn.silu(pre_act).astype(jnp.bfloat16)
        kept_input = store_slot(kept_input, current, slot_index, usable)
        kept_skip = store_slot(kept_skip, skip_input, slot_index, usable)
        kept_mid_mean = store_slot(kept_mid_mean, mid_mean, slot_index, usable)
        kept_mid_scale = store_slot(kept_mid_scale, mid_scale, slot_index, usable)
        kept_out_mean = store_slot(kept_out_mean, out_mean, slot_index, usable)
        kept_out_scale = store_slot(kept_out_scale, out_scale, slot_index, usable)
        results = store_slot(results, result.astype(jnp.float32), slot_index, usable)
        if turn_index < turns - 1:
            incoming, carried = from_behind(
                (result, jnp.where(odd_segment, result, current)), "segment", 1
            )
    gathered = (
        lax.all_gather(space_kernel[0].astype(jnp.bfloat16), "dp", axis=0, tiled=True),
        lax.all_gather(time_kernel[0].astype(jnp.bfloat16), "dp", axis=0, tiled=True),
        lax.all_gather(mid_gain[0].astype(jnp.bfloat16), "dp", axis=0, tiled=True),
        lax.all_gather(mid_bias[0].astype(jnp.bfloat16), "dp", axis=0, tiled=True),
        lax.all_gather(out_gain[0].astype(jnp.bfloat16), "dp", axis=0, tiled=True),
        lax.all_gather(out_bias[0].astype(jnp.bfloat16), "dp", axis=0, tiled=True),
    )
    space_low, time_low = (gathered[0], gathered[1])
    mid_gain_now = gathered[2].astype(jnp.float32)
    mid_bias_now = gathered[3].astype(jnp.float32)
    out_gain_now = gathered[4].astype(jnp.float32)
    out_bias_now = gathered[5].astype(jnp.float32)
    grad_input = jnp.zeros_like(frames)
    grad_skip = jnp.zeros_like(frames)
    space_acc = jnp.zeros(space_low.shape, jnp.float32)
    time_acc = jnp.zeros(time_low.shape, jnp.float32)
    mid_gain_acc = jnp.zeros((hidden_units,), jnp.float32)
    mid_bias_acc = jnp.zeros((hidden_units,), jnp.float32)
    out_gain_acc = jnp.zeros((channels,), jnp.float32)
    out_bias_acc = jnp.zeros((channels,), jnp.float32)
    input_grads = jnp.zeros(block_shape, jnp.float32)
    for turn_index in range(turns):
        micro_index = n_segment - 1 - (turn_index - (n_segment - 1 - segment_index))
        usable = (micro_index >= 0) & (micro_index < n_segment)
        usable_weight = usable.astype(jnp.float32)
        slot_index = jnp.clip(micro_index, 0, n_segment - 1)
        current = pick_slot(kept_input, slot_index)
        skip_input = pick_slot(kept_skip, slot_index)
        before_now = pick_slot(before_mask, slot_index)
        after_now = pick_slot(after_mask, slot_index)
        space_taps, spatial = space_apply(current, space_low)
        mid_normed = (spatial - pick_slot(kept_mid_mean, slot_index)) * pick_slot(
            kept_mid_scale, slot_index
        )
        mid_pre = mid_normed * mid_gain_now + mid_bias_now
        hidden_act = jax.nn.silu(mid_pre).astype(jnp.bfloat16)
        time_taps, temporal = time_apply(hidden_act, time_low, before_now, after_now)
        out_scale = pick_slot(kept_out_scale, slot_index)
        out_normed = (temporal - pick_slot(kept_out_mean, slot_index)) * out_scale
        pre_act = (
            out_normed * out_gain_now
            + out_bias_now
            + jnp.where(odd_segment, skip_input.astype(jnp.float32), 0.0)
        )
        grad_result = jnp.where(
            last_segment,
            pick_slot(cot_stack, slot_index).astype(jnp.float32),
            grad_input.astype(jnp.float32)
            + jnp.where(odd_segment, grad_skip.astype(jnp.float32), 0.0),
        )
        grad_pre = grad_result * silu_slope(pre_act)
        out_bias_sum, out_gain_sum = reduce_back(grad_pre, out_normed)
        grad_temporal = (
            out_gain_now
            * out_scale
            * (grad_pre - out_bias_sum / pixel_count - out_normed * out_gain_sum / pixel_count)
        ).astype(jnp.bfloat16)
        time_acc = time_acc + usable_weight * jnp.einsum(
            "fijc,fijo->co", time_taps, grad_temporal, preferred_element_type=jnp.float32
        )
        grad_hidden = time_back(grad_temporal, time_low, before_now, after_now)
        grad_mid = grad_hidden * silu_slope(mid_pre)
        mid_bias_sum, mid_gain_sum = reduce_back(grad_mid, mid_normed)
        mid_scale = pick_slot(kept_mid_scale, slot_index)
        grad_spatial = (
            mid_gain_now
            * mid_scale
            * (grad_mid - mid_bias_sum / pixel_count - mid_normed * mid_gain_sum / pixel_count)
        ).astype(jnp.bfloat16)
        space_acc = space_acc + usable_weight * jnp.einsum(
            "fijc,fijo->co", space_taps, grad_spatial, preferred_element_type=jnp.float32
        )
        grad_current = space_back(grad_spatial, space_low)
        mid_gain_acc = mid_gain_acc + usable_weight * mid_gain_sum
        mid_bias_acc = mid_bias_acc + usable_weight * mid_bias_sum
        out_gain_acc = out_gain_acc + usable_weight * out_gain_sum
        out_bias_acc = out_bias_acc + usable_weight * out_bias_sum
        input_grads = store_slot(
            input_grads, grad_current + grad_skip.astype(jnp.float32), slot_index, usable
        )
        if turn_index < turns - 1:
            grad_input, grad_skip = from_behind(
                (
                    grad_current.astype(jnp.bfloat16),
                    jnp.where(odd_segment, grad_pre.astype(jnp.bfloat16), grad_skip),
                ),
                "segment",
                -1,
            )
    space_grad, time_grad = (
        lax.psum_scatter(space_acc, "dp", scatter_dimension=0, tiled=True),
        lax.psum_scatter(time_acc, "dp", scatter_dimension=0, tiled=True),
    )
    data_index = lax.axis_index("dp")

    def own_share(full_vector):
        share = full_vector.shape[0] // n_data
        return lax.dynamic_slice_in_dim(full_vector, data_index * share, share)[None]

    flat_shape = (n_segment * frame_count,) + frames.shape[1:]
    arrived_out, arrived_grads = (
        lax.all_to_all(
            results.reshape(flat_shape).astype(jnp.bfloat16),
            "segment",
            split_axis=0,
            concat_axis=0,
            tiled=True,
        ).astype(jnp.float32),
        lax.all_to_all(
            input_grads.reshape(flat_shape).astype(jnp.bfloat16),
            "segment",
            split_axis=0,
            concat_axis=0,
            tiled=True,
        ).astype(jnp.float32),
    )
    output = arrived_out[(n_segment - 1) * frame_count :].astype(jnp.bfloat16)
    frames_grad = arrived_grads[:frame_count]
    return (
        output,
        frames_grad,
        space_grad[None],
        time_grad[None],
        own_share(mid_gain_acc),
        own_share(mid_bias_acc),
        own_share(out_gain_acc),
        own_share(out_bias_acc),
    )


def general(mesh):
    return jax.shard_map(
        on_device_general,
        mesh=mesh,
        in_specs=(
            P(("dp", "segment"), None, None, None),
            P(("dp", "segment"), None, None, None),
            P(("dp", "segment")),
            P("segment", "dp", None),
            P("segment", "dp", None),
            P("segment", "dp"),
            P("segment", "dp"),
            P("segment", "dp"),
            P("segment", "dp"),
        ),
        out_specs=(
            P(("dp", "segment"), None, None, None),
            P(("dp", "segment"), None, None, None),
            P("segment", "dp", None),
            P("segment", "dp", None),
            P("segment", "dp"),
            P("segment", "dp"),
            P("segment", "dp"),
            P("segment", "dp"),
        ),
        check_vma=False,
    )


def solution(mesh):
    if mesh.shape["dp"] != 8 or mesh.shape["segment"] != 4:
        return general(mesh)
    n_dp, n_seg = mesh.shape["dp"], mesh.shape["segment"]
    fine = Mesh(mesh.devices.reshape(n_dp // 2, 2, 2, n_seg // 2), EVERY)
    dp, seg = ("z", "y"), ("x", "c")
    return jax.shard_map(
        on_device,
        mesh=fine,
        in_specs=(
            P(EVERY, None, None, None),
            P(EVERY, None, None, None),
            P(EVERY),
            P(seg, dp, None),
            P(seg, dp, None),
            P(seg, dp),
            P(seg, dp),
            P(seg, dp),
            P(seg, dp),
        ),
        out_specs=(
            P(EVERY, None, None, None),
            P(EVERY, None, None, None),
            P(seg, dp, None),
            P(seg, dp, None),
            P(seg, dp),
            P(seg, dp),
            P(seg, dp),
            P(seg, dp),
        ),
        check_vma=False,
    )
```

```python
import functools

import jax
import jax.numpy as jnp
from jax import lax
from jax.experimental import pallas as pl
from jax.experimental.pallas import tpu as pltpu
from jax.sharding import Mesh, PartitionSpec as P

eps = 1e-05
PLANE = ("y", "x", "c")
EVERY = ("z", "y", "x", "c")
BF = jnp.bfloat16
F32 = jnp.float32


def nt(a, b):
    return lax.dot_general(a, b, (((1,), (1,)), ((), ())), preferred_element_type=F32)


def nn(a, b):
    return lax.dot_general(a, b, (((1,), (0,)), ((), ())), preferred_element_type=F32)


VMEM_CAP = 56 * 1024 * 1024
ANY = pl.BlockSpec(memory_space=pl.ANY)


def call(body, outs, scratch, flops, *args, deps=(), far=(), far_outs=()):
    moved = sum(a.size * a.dtype.itemsize for a in args) + sum(
        o.size * o.dtype.itemsize for o in outs
    )
    n = len(deps)

    def spec(a):
        return pl.BlockSpec(memory_space=pltpu.SMEM if a.dtype == jnp.int32 else pltpu.VMEM)

    return pl.pallas_call(
        lambda *refs: body(*refs[n:]),
        out_shape=outs,
        in_specs=[ANY] * n + [ANY if i in far else spec(a) for i, a in enumerate(args)],
        out_specs=[ANY if i in far_outs else spec(o) for i, o in enumerate(outs)],
        scratch_shapes=scratch,
        compiler_params=pltpu.CompilerParams(vmem_limit_bytes=VMEM_CAP),
        cost_estimate=pl.CostEstimate(flops=flops, bytes_accessed=moved, transcendentals=0),
    )(*deps, *args)


def chunk(i, size):
    return pl.ds(pl.multiple_of(i * size, 16), size)


def clear_borders(pad_ref, side, plane, nf):
    zrow = jnp.zeros(pad_ref.shape[1:], BF)
    pad_ref[0] = zrow
    pad_ref[side + 1] = zrow
    zcol = jnp.zeros((nf, pad_ref.shape[2]), BF)
    for i in range(side):
        pad_ref[i + 1, 0:nf] = zcol
        pad_ref[i + 1, nf + plane : 2 * nf + plane] = zcol


def by_rank(slices, rank):
    odd = lax.rem(rank, 2) == 1
    for p in range(len(slices) // 2):
        a, b = slices[2 * p], slices[2 * p + 1]
        yield lax.bitwise_xor(rank // 2, p), odd, a, b


def halves(odd, own, mate):
    low = lax.broadcasted_iota(jnp.int32, own.shape, 1) < 64
    own, mate = own.astype(F32), mate.astype(F32)
    a, b = jnp.where(odd, mate, own), jnp.where(odd, own, mate)
    top = jnp.where(low, a, pltpu.roll(b, 64, 1))
    bottom = jnp.where(low, pltpu.roll(a, 64, 1), b)
    return top, bottom


def store_packed(rank, mate_ref, keep_ref, part, k, step, low):
    rows_now = chunk(k, step)
    odd = lax.rem(rank, 2) == 1
    for q in range(keep_ref.shape[0]):
        x = part[:step, 128 * q : 128 * q + 128]
        y = part[step:, 128 * q : 128 * q + 128]
        even_slice = jnp.where(low, x, pltpu.roll(y, 64, 1))
        odd_slice = jnp.where(low, pltpu.roll(x, 64, 1), y)
        p = lax.bitwise_xor(rank // 2, q)
        keep_ref[p, rows_now, :] = jnp.where(odd, odd_slice, even_slice).astype(BF)
        mate_ref[p, rows_now, :] = jnp.where(odd, even_slice, odd_slice).astype(BF)


def fetch_kernels(w_ref, ktm_ref, lw_ref, sems):
    nz, _, width = w_ref.shape
    hc = ktm_ref.shape[0]
    copies = []
    for z in range(nz):
        copies.append(pltpu.make_async_copy(
            w_ref.at[z, pl.ds(0, hc)], ktm_ref.at[:, pl.ds(z * width, width)], sems.at[2 * z]))
        copies.append(pltpu.make_async_copy(
            w_ref.at[z, pl.ds(hc, lw_ref.shape[1])], lw_ref.at[z], sems.at[2 * z + 1]))
    for copy in copies:
        copy.start()
    return copies


def join_temporal(lw_ref, lf_ref, ltm_ref):
    ch = ltm_ref.shape[1]
    width = lw_ref.shape[2] // 2
    count = 2 * lw_ref.shape[0]
    size = ltm_ref.shape[0] // count
    for z in range(lw_ref.shape[0]):
        first = lw_ref[z, :, 0:ch].astype(F32)
        off = width % 128
        second = lw_ref[z, :, width - off : width - off + ch + 128].astype(F32)
        second = pltpu.roll(second, ch + 128 - off, 1)[:, 0:ch]
        for b, block in ((2 * z, first), (2 * z + 1, second)):
            lf_ref[b * size : b * size + block.shape[0], :] = block
    ltm_ref[...] = lf_ref[0 : ltm_ref.shape[0], :].astype(BF)


def prepare_body(w_ref, kn_out, l_out, lt_out, ktm_ref, lw_ref, lf_ref, sems):
    hc, ch = ktm_ref.shape[0], l_out.shape[1]
    for copy in fetch_kernels(w_ref, ktm_ref, lw_ref, sems):
        copy.wait()
    for t in range(9):
        kn_out[t] = ktm_ref[:, t * ch : (t + 1) * ch].astype(F32).T.astype(BF)
    join_temporal(lw_ref, lf_ref, l_out)
    for t in range(3):
        lt_out[t] = lf_ref[t * hc : (t + 1) * hc].T.astype(BF)


def prepare(w, hc, ch):
    outs = [
        jax.ShapeDtypeStruct((9, ch, hc), BF),
        jax.ShapeDtypeStruct((3 * hc, ch), BF),
        jax.ShapeDtypeStruct((3, ch, hc), BF),
    ]
    tall = w.shape[1] - hc
    scratch = [
        pltpu.VMEM((hc, 9 * ch), BF),
        pltpu.VMEM((w.shape[0], tall, w.shape[2]), BF),
        pltpu.VMEM((3 * hc + tall, ch), F32),
        pltpu.SemaphoreType.DMA((2 * w.shape[0],)),
    ]
    return call(prepare_body, outs, scratch, 2 * w.size * 512, w, far=(0,))


def conv_body(side, first, rank_ref, *refs):
    n = 1 if first else 8
    slices = refs[:n]
    (kn_in, ltm_ref, vec_ref, before_ref, after_ref,
     pad_out, hid_out, xhat_out, rs_ref, mate_ref, keep_ref,
     pad_ref, hid_ref, xhat_ref, sp_ref, kn_ref, sems) = refs[n:]
    rank = rank_ref[0]
    kn_copy = pltpu.make_async_copy(kn_in, kn_ref, sems.at[0])
    kn_copy.start()
    ch, hc = pad_ref.shape[2], hid_ref.shape[1]
    rows = hid_ref.shape[0]
    plane = rows // side
    nf = plane // side
    step = plane // 2
    clear_borders(pad_ref, side, plane, nf)
    if first:
        for i in range(side):
            pad_ref[i + 1, nf : nf + plane] = slices[0][i * plane : (i + 1) * plane]
    else:
        def place(k, carry):
            for q, odd, a_ref, b_ref in by_rank(slices, rank):
                top, bottom = halves(odd, a_ref[chunk(k, step), :], b_ref[chunk(k, step), :])
                lanes = pl.ds(pl.multiple_of(128 * q, 128), 128)
                for piece, kk in ((top, k), (bottom, k + side)):
                    at = nf + lax.rem(kk, 2) * step
                    pad_ref[1 + kk // 2, pl.ds(pl.multiple_of(at, 16), step), lanes] = piece.astype(BF)
            return carry

        lax.fori_loop(0, side, place, 0, unroll=True)
    pad_copy = pltpu.make_async_copy(pad_ref, pad_out, sems.at[1])
    pad_copy.start()
    kn_copy.wait()

    def conv(i, total):
        acc = jnp.zeros((plane, hc), F32)
        for t in range(9):
            r, c = t // 3, t % 3
            acc += nn(pad_ref[i + r, c * nf : c * nf + plane, :], kn_ref[t])
        sp_ref[i] = acc
        return total + jnp.sum(acc, axis=0, keepdims=True)

    mean = lax.fori_loop(0, side, conv, jnp.zeros((1, hc), F32), unroll=True) / rows

    def square(i, total):
        cen = sp_ref[i] - mean
        return total + jnp.sum(cen * cen, axis=0, keepdims=True)

    var = lax.fori_loop(0, side, square, jnp.zeros((1, hc), F32), unroll=True) / rows
    rs = lax.rsqrt(var + eps)
    rs_ref[...] = rs
    gain, bias = vec_ref[0:1, :], vec_ref[1:2, :]

    def act(i, carry):
        xhat = (sp_ref[i] - mean) * rs
        xhat_ref[i] = xhat
        v = xhat * gain + bias
        v = v * jax.nn.sigmoid(v)
        sp_ref[i] = v
        hid_ref[chunk(i, plane), :] = v.astype(BF)
        return carry

    lax.fori_loop(0, side, act, 0, unroll=True)
    late = [
        pltpu.make_async_copy(hid_ref, hid_out, sems.at[2]),
        pltpu.make_async_copy(xhat_ref, xhat_out, sems.at[3]),
    ]
    for copy in late:
        copy.start()
    low = lax.broadcasted_iota(jnp.int32, (step, 128), 1) < 64

    def temporal(k, carry):
        pieces = []
        for kk in (k, k + side):
            par = lax.rem(kk, 2)
            h = sp_ref[kk // 2, pl.ds(pl.multiple_of(par * step, 8), step), :]
            at = pl.multiple_of(par * (step % nf), 8)
            pieces.append((
                (pltpu.roll(h, 1, 0) * before_ref[pl.ds(at, step), :]).astype(BF),
                h.astype(BF),
                (pltpu.roll(h, step - 1, 0) * after_ref[pl.ds(at, step), :]).astype(BF),
            ))
        part = sum(
            nn(jnp.concatenate([x, y], axis=0), ltm_ref[t * hc : (t + 1) * hc])
            for t, (x, y) in enumerate(zip(*pieces))
        )
        store_packed(rank, mate_ref, keep_ref, part, k, step, low)
        return carry

    lax.fori_loop(0, side, temporal, 0, unroll=True)
    for copy in [pad_copy] + late:
        copy.wait()


def conv_forward(rank, g, kn, lt, vec, before, after, side, pixels, ch, deps=()):
    hc = vec.shape[1]
    plane = pixels // side
    nf = plane // side
    n = len(g)
    shapes = [
        ((side + 2, plane + 2 * nf, ch), BF),
        ((pixels, hc), BF),
        ((side, plane, hc), F32),
    ]
    outs = [jax.ShapeDtypeStruct(*s) for s in shapes] + [
        jax.ShapeDtypeStruct((1, hc), F32),
        jax.ShapeDtypeStruct((4, pixels // 2, 128), BF),
        jax.ShapeDtypeStruct((4, pixels // 2, 128), BF),
    ]
    scratch = [pltpu.VMEM(*s) for s in shapes] + [
        pltpu.VMEM((side, plane, hc), F32),
        pltpu.VMEM((9, ch, hc), BF),
        pltpu.SemaphoreType.DMA((4,)),
    ]
    flops = 2 * pixels * hc * 12 * ch
    return call(functools.partial(conv_body, side, n == 1), outs, scratch, flops,
                rank, *g, kn, lt, vec, before, after,
                deps=deps, far=(n + 1,), far_outs=(0, 1, 2))


def fold(v):
    return v + pltpu.roll(v, 64, 1)


def total_of(refs):
    t = refs[0][...].astype(F32)
    for ref in refs[1:]:
        t += ref[...].astype(F32)
    return t


def pair_sum_body(keep_ref, mate_ref, *out_refs):
    for p, ref in enumerate(out_refs):
        ref[...] = (keep_ref[p].astype(F32) + mate_ref[p].astype(F32)).astype(ref.dtype)


def pair_sum(keep, arrived, deps=()):
    shape = keep.shape[1:]
    outs = [jax.ShapeDtypeStruct(shape, BF)] * keep.shape[0]
    return call(pair_sum_body, outs, [], keep.size, keep, arrived, deps=deps)


def out_norm_body(n, has_skip, *refs):
    parts, refs = refs[:n], refs[n:]
    if has_skip:
        vec_ref, skip_ref, xhat_ref, rs_ref, pre_ref, res_ref = refs
    else:
        vec_ref, xhat_ref, rs_ref, pre_ref, res_ref = refs
    t = total_of(parts)
    pixels = 2 * t.shape[0]
    mean = fold(jnp.sum(t, axis=0, keepdims=True)) / pixels
    cen = t - mean
    rs = lax.rsqrt(fold(jnp.sum(cen * cen, axis=0, keepdims=True)) / pixels + eps)
    xhat = cen * rs
    pre = xhat * vec_ref[0:1, :] + vec_ref[1:2, :]
    if has_skip:
        pre = pre + skip_ref[...].astype(F32)
    xhat_ref[...] = xhat
    rs_ref[...] = rs
    pre_ref[...] = pre
    res_ref[...] = (pre * jax.nn.sigmoid(pre)).astype(BF)


def out_norm(parts, vec, skip, deps=()):
    half = parts[0].shape[0]
    outs = [
        jax.ShapeDtypeStruct((half, 128), F32),
        jax.ShapeDtypeStruct((1, 128), F32),
        jax.ShapeDtypeStruct((half, 128), F32),
        jax.ShapeDtypeStruct((half, 128), BF),
    ]
    args = (*parts, vec) + (() if skip is None else (skip,))
    body = functools.partial(out_norm_body, len(parts), skip is not None)
    return call(body, outs, [], half * 128 * 10, *args, deps=deps)


def out_back_body(n, *refs):
    parts, (pre_ref, xhat_ref, rs_ref, vec_ref, dpre_ref, dt_ref, sums_ref) = refs[:n], refs[n:]
    g = total_of(parts)
    pre, xhat = pre_ref[...], xhat_ref[...]
    sig = jax.nn.sigmoid(pre)
    dpre = g * (sig * (1.0 + pre * (1.0 - sig)))
    pixels = 2 * pre.shape[0]
    sb = fold(jnp.sum(dpre, axis=0, keepdims=True))
    sg = fold(jnp.sum(dpre * xhat, axis=0, keepdims=True))
    dpre_ref[...] = dpre.astype(BF)
    scale = vec_ref[0:1, :] * rs_ref[...]
    dt_ref[...] = (scale * (dpre - sb / pixels - xhat * (sg / pixels))).astype(BF)
    sums_ref[0:1, :] = sg
    sums_ref[1:2, :] = sb


def out_back(parts, pre, xhat, rs, vec, deps=()):
    half = pre.shape[0]
    outs = [
        jax.ShapeDtypeStruct((half, 128), BF),
        jax.ShapeDtypeStruct((half, 128), BF),
        jax.ShapeDtypeStruct((2, 128), F32),
    ]
    args = (*parts, pre, xhat, rs, vec)
    return call(functools.partial(out_back_body, len(parts)), outs, [], half * 1280, *args, deps=deps)


def conv_back_body(side, rank_ref, *refs):
    slices, (xhat_in, rs_ref, w_ref, lnt_ref, vec_ref, before_ref, after_ref,
             dt_out, ds_out, sums_ref, mate_ref, keep_ref,
             dt_ref, ds_ref, xhat_ref, dy_ref, pad_ref, ktm_ref, sems) = refs[:8], refs[8:]
    half = slices[0].shape[0]
    rank = rank_ref[0]
    nz, _, width = w_ref.shape
    rows = 2 * half
    plane = rows // side
    nf = plane // side
    step = plane // 2
    hc = ds_ref.shape[1]
    ch = dt_ref.shape[1]
    fetched = [
        pltpu.make_async_copy(
            w_ref.at[z, pl.ds(0, hc)], ktm_ref.at[:, pl.ds(z * width, width)], sems.at[z])
        for z in range(nz)
    ]
    xhat_copy = pltpu.make_async_copy(xhat_in, xhat_ref, sems.at[nz])
    for copy in fetched + [xhat_copy]:
        copy.start()
    clear_borders(pad_ref, side, plane, nf)

    def place(k, carry):
        for q, odd, a_ref, b_ref in by_rank(slices, rank):
            top, bottom = halves(odd, a_ref[chunk(k, step), :], b_ref[chunk(k, step), :])
            lanes = pl.ds(pl.multiple_of(128 * q, 128), 128)
            dt_ref[chunk(k, step), lanes] = top.astype(BF)
            dt_ref[pl.ds(pl.multiple_of(half + k * step, 16), step), lanes] = bottom.astype(BF)
        return carry

    lax.fori_loop(0, side, place, 0, unroll=True)
    dt_copy = pltpu.make_async_copy(dt_ref, dt_out, sems.at[nz + 1])
    dt_copy.start()
    xhat_copy.wait()
    gain, bias = vec_ref[0:1, :], vec_ref[1:2, :]

    def hidden_grad(i, sums):
        dt = dt_ref[chunk(i, plane), :]
        early = nn(dt, lnt_ref[0]) * before_ref[0:plane, :]
        late = nn(dt, lnt_ref[2]) * after_ref[0:plane, :]
        dh = nn(dt, lnt_ref[1]) + pltpu.roll(early, plane - 1, 0) + pltpu.roll(late, 1, 0)
        xhat = xhat_ref[i]
        v = xhat * gain + bias
        sig = jax.nn.sigmoid(v)
        dy = dh * (sig * (1.0 + v * (1.0 - sig)))
        dy_ref[i] = dy
        return (
            sums[0] + jnp.sum(dy * xhat, axis=0, keepdims=True),
            sums[1] + jnp.sum(dy, axis=0, keepdims=True),
        )

    zero = jnp.zeros((1, hc), F32)
    sg, sb = lax.fori_loop(0, side, hidden_grad, (zero, zero), unroll=True)
    sums_ref[0:1, :] = sg
    sums_ref[1:2, :] = sb
    scale = gain * rs_ref[...]

    def spatial_grad(i, carry):
        ds = (scale * (dy_ref[i] - sb / rows - xhat_ref[i] * (sg / rows))).astype(BF)
        pad_ref[i + 1, nf : nf + plane] = ds
        ds_ref[chunk(i, plane), :] = ds
        return carry

    lax.fori_loop(0, side, spatial_grad, 0, unroll=True)
    ds_copy = pltpu.make_async_copy(ds_ref, ds_out, sems.at[nz + 2])
    ds_copy.start()
    for copy in fetched:
        copy.wait()
    low = lax.broadcasted_iota(jnp.int32, (step, 128), 1) < 64

    def back(k, carry):
        acc = jnp.zeros((2 * step, ch), F32)
        for t in range(9):
            r, c = 2 - t // 3, 2 - t % 3
            pieces = []
            for kk in (k, k + side):
                at = c * nf + lax.rem(kk, 2) * step
                pieces.append(pad_ref[kk // 2 + r, pl.ds(pl.multiple_of(at, 16), step), :])
            acc += nn(jnp.concatenate(pieces, axis=0), ktm_ref[:, t * ch : (t + 1) * ch])
        store_packed(rank, mate_ref, keep_ref, acc, k, step, low)
        return carry

    lax.fori_loop(0, side, back, 0, unroll=True)
    dt_copy.wait()
    ds_copy.wait()


def conv_back(rank, g, xhat, rs, w, lnt, vec, before, after, side, deps=()):
    half = g[0].shape[0]
    hc = vec.shape[1]
    ch = len(g) * 64
    pixels = 2 * half
    plane = pixels // side
    nf = plane // side
    outs = [
        jax.ShapeDtypeStruct((pixels, ch), BF),
        jax.ShapeDtypeStruct((pixels, hc), BF),
        jax.ShapeDtypeStruct((2, hc), F32),
        jax.ShapeDtypeStruct((4, half, 128), BF),
        jax.ShapeDtypeStruct((4, half, 128), BF),
    ]
    scratch = [
        pltpu.VMEM((pixels, ch), BF),
        pltpu.VMEM((pixels, hc), BF),
        pltpu.VMEM((side, plane, hc), F32),
        pltpu.VMEM((side, plane, hc), F32),
        pltpu.VMEM((side + 2, plane + 2 * nf, hc), BF),
        pltpu.VMEM((hc, 9 * ch), BF),
        pltpu.SemaphoreType.DMA((w.shape[0] + 3,)),
    ]
    flops = 2 * pixels * hc * 12 * ch
    return call(functools.partial(conv_back_body, side), outs, scratch, flops,
                rank, *g, xhat, rs, w, lnt, vec, before, after,
                deps=deps, far=(9, 11), far_outs=(0, 1))


def grads_body(side, pad_ref, hid_ref, ds_ref, dt_ref, before_ref, after_ref, mid_ref, out_ref,
               sg_ref, dst_ref, taps_ref, tg_ref, vec_ref):
    ch = pad_ref.shape[2]
    hc = hid_ref.shape[1]
    plane = hid_ref.shape[0] // side
    nf = plane // side
    for i in (0, 1, side + 2, side + 3):
        dst_ref[i] = jnp.zeros(dst_ref.shape[1:], BF)
    for i in range(side):
        at = slice(i * plane, (i + 1) * plane)
        h = hid_ref[at, :].astype(F32)
        taps_ref[i, 0:hc] = (pltpu.roll(h, 1, 0) * before_ref[0:plane, :]).T.astype(BF)
        taps_ref[i, hc : 2 * hc] = h.T.astype(BF)
        taps_ref[i, 2 * hc : 3 * hc] = (pltpu.roll(h, plane - 1, 0) * after_ref[0:plane, :]).T.astype(BF)
        dst_ref[i + 2] = ds_ref[at, :].astype(F32).T.astype(BF)
    tg_ref[0 : 3 * hc, :] = sum(
        nn(taps_ref[i], dt_ref[i * plane : (i + 1) * plane, :]) for i in range(side)
    )
    tg_ref[3 * hc :, :] = jnp.zeros((tg_ref.shape[0] - 3 * hc, ch), F32)
    nz, _, width = sg_ref.shape
    size = 3 * hc // (2 * nz)
    vec_ref[...] = jnp.zeros(vec_ref.shape, F32)
    vec_ref[size : size + 2, 0:hc] = mid_ref[...]
    vec_ref[size + 2 : size + 4, 0:128] = out_ref[...]
    tall = vec_ref.shape[0]
    inside = lax.broadcasted_iota(jnp.int32, (tall, ch), 0) < size
    off = (width // 2) % 128
    for z in range(nz):
        first, second = [
            jnp.where(inside, tg_ref[b * size : b * size + tall, :], vec_ref[...])
            for b in (2 * z, 2 * z + 1)
        ]
        start = width // 2 - off
        sg_ref[z, hc : hc + tall, 0:ch] = first.astype(BF)
        second = pltpu.roll(jnp.concatenate([second, jnp.zeros((tall, 128), F32)], axis=1), off, 1)
        sg_ref[z, hc : hc + tall, start : start + ch + 128] = second.astype(BF)
    for c in range(3):
        acc = sum(
            nn(dst_ref[i : i + 3].reshape(3 * hc, plane), pad_ref[i, c * nf : c * nf + plane, :])
            for i in range(1, side + 1)
        )
        for r in range(3):
            first = (3 * r + c) * ch
            end = first + ch
            at = (2 - r) * hc
            done = 0
            while first < end:
                z = first // width
                last = min(end, (z + 1) * width)
                sg_ref[z, 0:hc, first - z * width : last - z * width] = (
                    acc[at : at + hc, done : done + last - first].astype(BF)
                )
                done += last - first
                first = last


def kernel_grads(pad, hidden, ds, dt, before, after, mid, out, side, shape, deps=()):
    pixels, hc = hidden.shape
    ch = dt.shape[1]
    plane = pixels // side
    outs = [jax.ShapeDtypeStruct(shape, BF)]
    tall = shape[1] - hc
    scratch = [
        pltpu.VMEM((side + 4, hc, plane), BF),
        pltpu.VMEM((side, 3 * hc, plane), BF),
        pltpu.VMEM((3 * hc + tall, ch), F32),
        pltpu.VMEM((tall, ch), F32),
    ]
    flops = 2 * pixels * hc * 12 * ch
    return call(functools.partial(grads_body, side), outs, scratch, flops,
                pad, hidden, ds, dt, before, after, mid, out, deps=deps)[0]


def copy_after_body(v_ref, out_ref):
    out_ref[...] = v_ref[...]


def after_all(v, *deps):
    return call(copy_after_body, [jax.ShapeDtypeStruct(v.shape, v.dtype)], [], v.size, v, deps=deps)[0]


def pack_kernels_body(kt_ref, lt_ref, vec_ref, out_ref, low_ref):
    ranks, _, width = out_ref.shape
    hc = kt_ref.shape[0] // ranks
    blocks = lt_ref.shape[0] // hc
    q = hc // ranks
    low_ref[...] = jnp.zeros(low_ref.shape, F32)
    for r in range(ranks):
        out_ref[r, 0:hc, :] = kt_ref[r * hc : (r + 1) * hc, :]
        for b in range(blocks):
            low_ref[r, b * q : (b + 1) * q, 0 : lt_ref.shape[1]] = (
                lt_ref[b * hc + r * q : b * hc + (r + 1) * q, :]
            )
        low_ref[r, blocks * q : blocks * q + 1, :] = vec_ref[...]
        out_ref[r, hc:, :] = low_ref[r].astype(BF)


def pack_kernels(kt, lt, vec, ranks, tall, deps):
    width = kt.shape[1]
    outs = [jax.ShapeDtypeStruct((ranks, kt.shape[0] // ranks + tall, width), BF)]
    scratch = [pltpu.VMEM((ranks, tall, width), F32)]
    return call(pack_kernels_body, outs, scratch, kt.size * 8, kt, lt, vec, deps=deps)[0]


def call(body, outs, scratch, flops, *args, deps=(), far=(), far_outs=()):
    moved = sum(a.size * a.dtype.itemsize for a in args) + sum(
        o.size * o.dtype.itemsize for o in outs
    )
    n = len(deps)

    def spec(a):
        return pl.BlockSpec(memory_space=pltpu.SMEM if a.dtype == jnp.int32 else pltpu.VMEM)

    return pl.pallas_call(
        lambda *refs: body(*refs[n:]),
        out_shape=outs,
        in_specs=[ANY] * n + [ANY if i in far else spec(a) for i, a in enumerate(args)],
        out_specs=[ANY if i in far_outs else spec(o) for i, o in enumerate(outs)],
        scratch_shapes=scratch,
        compiler_params=pltpu.CompilerParams(vmem_limit_bytes=VMEM_CAP),
        cost_estimate=pl.CostEstimate(flops=flops, bytes_accessed=moved, transcendentals=0),
    )(*deps, *args)


def chunk(i, size):
    return pl.ds(pl.multiple_of(i * size, 16), size)


def clear_borders(pad_ref, side, plane, nf):
    zrow = jnp.zeros(pad_ref.shape[1:], BF)
    pad_ref[0] = zrow
    pad_ref[side + 1] = zrow
    zcol = jnp.zeros((nf, pad_ref.shape[2]), BF)
    for i in range(side):
        pad_ref[i + 1, 0:nf] = zcol
        pad_ref[i + 1, nf + plane : 2 * nf + plane] = zcol


def by_rank(slices, rank):
    odd = lax.rem(rank, 2) == 1
    for p in range(len(slices) // 2):
        a, b = slices[2 * p], slices[2 * p + 1]
        yield lax.bitwise_xor(rank // 2, p), odd, a, b


def halves(odd, own, mate):
    low = lax.broadcasted_iota(jnp.int32, own.shape, 1) < 64
    own, mate = own.astype(F32), mate.astype(F32)
    a, b = jnp.where(odd, mate, own), jnp.where(odd, own, mate)
    top = jnp.where(low, a, pltpu.roll(b, 64, 1))
    bottom = jnp.where(low, pltpu.roll(a, 64, 1), b)
    return top, bottom


def store_packed(rank, mate_ref, keep_ref, part, k, step, low):
    rows_now = chunk(k, step)
    odd = lax.rem(rank, 2) == 1
    for q in range(keep_ref.shape[0]):
        x = part[:step, 128 * q : 128 * q + 128]
        y = part[step:, 128 * q : 128 * q + 128]
        even_slice = jnp.where(low, x, pltpu.roll(y, 64, 1))
        odd_slice = jnp.where(low, pltpu.roll(x, 64, 1), y)
        p = lax.bitwise_xor(rank // 2, q)
        keep_ref[p, rows_now, :] = jnp.where(odd, odd_slice, even_slice).astype(BF)
        mate_ref[p, rows_now, :] = jnp.where(odd, even_slice, odd_slice).astype(BF)


def fetch_kernels(w_ref, ktm_ref, lw_ref, sems):
    nz, _, width = w_ref.shape
    hc = ktm_ref.shape[0]
    copies = []
    for z in range(nz):
        copies.append(pltpu.make_async_copy(
            w_ref.at[z, pl.ds(0, hc)], ktm_ref.at[:, pl.ds(z * width, width)], sems.at[2 * z]))
        copies.append(pltpu.make_async_copy(
            w_ref.at[z, pl.ds(hc, lw_ref.shape[1])], lw_ref.at[z], sems.at[2 * z + 1]))
    for copy in copies:
        copy.start()
    return copies


def join_temporal(lw_ref, lf_ref, ltm_ref):
    ch = ltm_ref.shape[1]
    width = lw_ref.shape[2] // 2
    count = 2 * lw_ref.shape[0]
    size = ltm_ref.shape[0] // count
    for z in range(lw_ref.shape[0]):
        first = lw_ref[z, :, 0:ch].astype(F32)
        off = width % 128
        second = lw_ref[z, :, width - off : width - off + ch + 128].astype(F32)
        second = pltpu.roll(second, ch + 128 - off, 1)[:, 0:ch]
        for b, block in ((2 * z, first), (2 * z + 1, second)):
            lf_ref[b * size : b * size + block.shape[0], :] = block
    ltm_ref[...] = lf_ref[0 : ltm_ref.shape[0], :].astype(BF)


def prepare_body(w_ref, kn_out, l_out, lt_out, ktm_ref, lw_ref, lf_ref, sems):
    hc, ch = ktm_ref.shape[0], l_out.shape[1]
    for copy in fetch_kernels(w_ref, ktm_ref, lw_ref, sems):
        copy.wait()
    for t in range(9):
        kn_out[t] = ktm_ref[:, t * ch : (t + 1) * ch].astype(F32).T.astype(BF)
    join_temporal(lw_ref, lf_ref, l_out)
    for t in range(3):
        lt_out[t] = lf_ref[t * hc : (t + 1) * hc].T.astype(BF)


def prepare(w, hc, ch):
    outs = [
        jax.ShapeDtypeStruct((9, ch, hc), BF),
        jax.ShapeDtypeStruct((3 * hc, ch), BF),
        jax.ShapeDtypeStruct((3, ch, hc), BF),
    ]
    tall = w.shape[1] - hc
    scratch = [
        pltpu.VMEM((hc, 9 * ch), BF),
        pltpu.VMEM((w.shape[0], tall, w.shape[2]), BF),
        pltpu.VMEM((3 * hc + tall, ch), F32),
        pltpu.SemaphoreType.DMA((2 * w.shape[0],)),
    ]
    return call(prepare_body, outs, scratch, 2 * w.size * 512, w, far=(0,))


def conv_body(side, first, rank_ref, *refs):
    n = 1 if first else 8
    slices = refs[:n]
    (kn_in, ltm_ref, vec_ref, before_ref, after_ref,
     pad_out, hid_out, xhat_out, rs_ref, mate_ref, keep_ref,
     pad_ref, hid_ref, xhat_ref, sp_ref, kn_ref, sems) = refs[n:]
    rank = rank_ref[0]
    kn_copy = pltpu.make_async_copy(kn_in, kn_ref, sems.at[0])
    kn_copy.start()
    ch, hc = pad_ref.shape[2], hid_ref.shape[1]
    rows = hid_ref.shape[0]
    plane = rows // side
    nf = plane // side
    step = plane // 2
    clear_borders(pad_ref, side, plane, nf)
    if first:
        for i in range(side):
            pad_ref[i + 1, nf : nf + plane] = slices[0][i * plane : (i + 1) * plane]
    else:
        def place(k, carry):
            for q, odd, a_ref, b_ref in by_rank(slices, rank):
                top, bottom = halves(odd, a_ref[chunk(k, step), :], b_ref[chunk(k, step), :])
                lanes = pl.ds(pl.multiple_of(128 * q, 128), 128)
                for piece, kk in ((top, k), (bottom, k + side)):
                    at = nf + lax.rem(kk, 2) * step
                    pad_ref[1 + kk // 2, pl.ds(pl.multiple_of(at, 16), step), lanes] = piece.astype(BF)
            return carry

        lax.fori_loop(0, side, place, 0, unroll=True)
    pad_copy = pltpu.make_async_copy(pad_ref, pad_out, sems.at[1])
    pad_copy.start()
    kn_copy.wait()

    def conv(i, total):
        acc = jnp.zeros((plane, hc), F32)
        for t in range(9):
            r, c = t // 3, t % 3
            acc += nn(pad_ref[i + r, c * nf : c * nf + plane, :], kn_ref[t])
        sp_ref[i] = acc
        return total + jnp.sum(acc, axis=0, keepdims=True)

    mean = lax.fori_loop(0, side, conv, jnp.zeros((1, hc), F32), unroll=True) / rows

    def square(i, total):
        cen = sp_ref[i] - mean
        return total + jnp.sum(cen * cen, axis=0, keepdims=True)

    var = lax.fori_loop(0, side, square, jnp.zeros((1, hc), F32), unroll=True) / rows
    rs = lax.rsqrt(var + eps)
    rs_ref[...] = rs
    gain, bias = vec_ref[0:1, :], vec_ref[1:2, :]

    def act(i, carry):
        xhat = (sp_ref[i] - mean) * rs
        xhat_ref[i] = xhat
        v = xhat * gain + bias
        v = v * jax.nn.sigmoid(v)
        sp_ref[i] = v
        hid_ref[chunk(i, plane), :] = v.astype(BF)
        return carry

    lax.fori_loop(0, side, act, 0, unroll=True)
    late = [
        pltpu.make_async_copy(hid_ref, hid_out, sems.at[2]),
        pltpu.make_async_copy(xhat_ref, xhat_out, sems.at[3]),
    ]
    for copy in late:
        copy.start()
    low = lax.broadcasted_iota(jnp.int32, (step, 128), 1) < 64

    def temporal(k, carry):
        pieces = []
        for kk in (k, k + side):
            par = lax.rem(kk, 2)
            h = sp_ref[kk // 2, pl.ds(pl.multiple_of(par * step, 8), step), :]
            at = pl.multiple_of(par * (step % nf), 8)
            pieces.append((
                (pltpu.roll(h, 1, 0) * before_ref[pl.ds(at, step), :]).astype(BF),
                h.astype(BF),
                (pltpu.roll(h, step - 1, 0) * after_ref[pl.ds(at, step), :]).astype(BF),
            ))
        part = sum(
            nn(jnp.concatenate([x, y], axis=0), ltm_ref[t * hc : (t + 1) * hc])
            for t, (x, y) in enumerate(zip(*pieces))
        )
        store_packed(rank, mate_ref, keep_ref, part, k, step, low)
        return carry

    lax.fori_loop(0, side, temporal, 0, unroll=True)
    for copy in [pad_copy] + late:
        copy.wait()


def conv_forward(rank, g, kn, lt, vec, before, after, side, pixels, ch, deps=()):
    hc = vec.shape[1]
    plane = pixels // side
    nf = plane // side
    n = len(g)
    shapes = [
        ((side + 2, plane + 2 * nf, ch), BF),
        ((pixels, hc), BF),
        ((side, plane, hc), F32),
    ]
    outs = [jax.ShapeDtypeStruct(*s) for s in shapes] + [
        jax.ShapeDtypeStruct((1, hc), F32),
        jax.ShapeDtypeStruct((4, pixels // 2, 128), BF),
        jax.ShapeDtypeStruct((4, pixels // 2, 128), BF),
    ]
    scratch = [pltpu.VMEM(*s) for s in shapes] + [
        pltpu.VMEM((side, plane, hc), F32),
        pltpu.VMEM((9, ch, hc), BF),
        pltpu.SemaphoreType.DMA((4,)),
    ]
    flops = 2 * pixels * hc * 12 * ch
    return call(functools.partial(conv_body, side, n == 1), outs, scratch, flops,
                rank, *g, kn, lt, vec, before, after,
                deps=deps, far=(n + 1,), far_outs=(0, 1, 2))


def fold(v):
    return v + pltpu.roll(v, 64, 1)


def total_of(refs):
    t = refs[0][...].astype(F32)
    for ref in refs[1:]:
        t += ref[...].astype(F32)
    return t


def pair_sum_body(keep_ref, mate_ref, *out_refs):
    for p, ref in enumerate(out_refs):
        ref[...] = (keep_ref[p].astype(F32) + mate_ref[p].astype(F32)).astype(ref.dtype)


def pair_sum(keep, arrived, deps=()):
    shape = keep.shape[1:]
    outs = [jax.ShapeDtypeStruct(shape, BF)] * keep.shape[0]
    return call(pair_sum_body, outs, [], keep.size, keep, arrived, deps=deps)


def out_norm_body(n, has_skip, *refs):
    parts, refs = refs[:n], refs[n:]
    if has_skip:
        vec_ref, skip_ref, xhat_ref, rs_ref, pre_ref, res_ref = refs
    else:
        vec_ref, xhat_ref, rs_ref, pre_ref, res_ref = refs
    t = total_of(parts)
    pixels = 2 * t.shape[0]
    mean = fold(jnp.sum(t, axis=0, keepdims=True)) / pixels
    cen = t - mean
    rs = lax.rsqrt(fold(jnp.sum(cen * cen, axis=0, keepdims=True)) / pixels + eps)
    xhat = cen * rs
    pre = xhat * vec_ref[0:1, :] + vec_ref[1:2, :]
    if has_skip:
        pre = pre + skip_ref[...].astype(F32)
    xhat_ref[...] = xhat
    rs_ref[...] = rs
    pre_ref[...] = pre
    res_ref[...] = (pre * jax.nn.sigmoid(pre)).astype(BF)


def out_norm(parts, vec, skip, deps=()):
    half = parts[0].shape[0]
    outs = [
        jax.ShapeDtypeStruct((half, 128), F32),
        jax.ShapeDtypeStruct((1, 128), F32),
        jax.ShapeDtypeStruct((half, 128), F32),
        jax.ShapeDtypeStruct((half, 128), BF),
    ]
    args = (*parts, vec) + (() if skip is None else (skip,))
    body = functools.partial(out_norm_body, len(parts), skip is not None)
    return call(body, outs, [], half * 128 * 10, *args, deps=deps)


def out_back_body(n, *refs):
    parts, (pre_ref, xhat_ref, rs_ref, vec_ref, dpre_ref, dt_ref, sums_ref) = refs[:n], refs[n:]
    g = total_of(parts)
    pre, xhat = pre_ref[...], xhat_ref[...]
    sig = jax.nn.sigmoid(pre)
    dpre = g * (sig * (1.0 + pre * (1.0 - sig)))
    pixels = 2 * pre.shape[0]
    sb = fold(jnp.sum(dpre, axis=0, keepdims=True))
    sg = fold(jnp.sum(dpre * xhat, axis=0, keepdims=True))
    dpre_ref[...] = dpre.astype(BF)
    scale = vec_ref[0:1, :] * rs_ref[...]
    dt_ref[...] = (scale * (dpre - sb / pixels - xhat * (sg / pixels))).astype(BF)
    sums_ref[0:1, :] = sg
    sums_ref[1:2, :] = sb


def out_back(parts, pre, xhat, rs, vec, deps=()):
    half = pre.shape[0]
    outs = [
        jax.ShapeDtypeStruct((half, 128), BF),
        jax.ShapeDtypeStruct((half, 128), BF),
        jax.ShapeDtypeStruct((2, 128), F32),
    ]
    args = (*parts, pre, xhat, rs, vec)
    return call(functools.partial(out_back_body, len(parts)), outs, [], half * 1280, *args, deps=deps)


def conv_back_body(side, rank_ref, *refs):
    slices, (xhat_in, rs_ref, w_ref, lnt_ref, vec_ref, before_ref, after_ref,
             dt_out, ds_out, sums_ref, mate_ref, keep_ref,
             dt_ref, ds_ref, xhat_ref, dy_ref, pad_ref, ktm_ref, sems) = refs[:8], refs[8:]
    half = slices[0].shape[0]
    rank = rank_ref[0]
    nz, _, width = w_ref.shape
    rows = 2 * half
    plane = rows // side
    nf = plane // side
    step = plane // 2
    hc = ds_ref.shape[1]
    ch = dt_ref.shape[1]
    fetched = [
        pltpu.make_async_copy(
            w_ref.at[z, pl.ds(0, hc)], ktm_ref.at[:, pl.ds(z * width, width)], sems.at[z])
        for z in range(nz)
    ]
    xhat_copy = pltpu.make_async_copy(xhat_in, xhat_ref, sems.at[nz])
    for copy in fetched + [xhat_copy]:
        copy.start()
    clear_borders(pad_ref, side, plane, nf)

    def place(k, carry):
        for q, odd, a_ref, b_ref in by_rank(slices, rank):
            top, bottom = halves(odd, a_ref[chunk(k, step), :], b_ref[chunk(k, step), :])
            lanes = pl.ds(pl.multiple_of(128 * q, 128), 128)
            dt_ref[chunk(k, step), lanes] = top.astype(BF)
            dt_ref[pl.ds(pl.multiple_of(half + k * step, 16), step), lanes] = bottom.astype(BF)
        return carry

    lax.fori_loop(0, side, place, 0, unroll=True)
    dt_copy = pltpu.make_async_copy(dt_ref, dt_out, sems.at[nz + 1])
    dt_copy.start()
    xhat_copy.wait()
    gain, bias = vec_ref[0:1, :], vec_ref[1:2, :]

    def hidden_grad(i, sums):
        dt = dt_ref[chunk(i, plane), :]
        early = nn(dt, lnt_ref[0]) * before_ref[0:plane, :]
        late = nn(dt, lnt_ref[2]) * after_ref[0:plane, :]
        dh = nn(dt, lnt_ref[1]) + pltpu.roll(early, plane - 1, 0) + pltpu.roll(late, 1, 0)
        xhat = xhat_ref[i]
        v = xhat * gain + bias
        sig = jax.nn.sigmoid(v)
        dy = dh * (sig * (1.0 + v * (1.0 - sig)))
        dy_ref[i] = dy
        return (
            sums[0] + jnp.sum(dy * xhat, axis=0, keepdims=True),
            sums[1] + jnp.sum(dy, axis=0, keepdims=True),
        )

    zero = jnp.zeros((1, hc), F32)
    sg, sb = lax.fori_loop(0, side, hidden_grad, (zero, zero), unroll=True)
    sums_ref[0:1, :] = sg
    sums_ref[1:2, :] = sb
    scale = gain * rs_ref[...]

    def spatial_grad(i, carry):
        ds = (scale * (dy_ref[i] - sb / rows - xhat_ref[i] * (sg / rows))).astype(BF)
        pad_ref[i + 1, nf : nf + plane] = ds
        ds_ref[chunk(i, plane), :] = ds
        return carry

    lax.fori_loop(0, side, spatial_grad, 0, unroll=True)
    ds_copy = pltpu.make_async_copy(ds_ref, ds_out, sems.at[nz + 2])
    ds_copy.start()
    for copy in fetched:
        copy.wait()
    low = lax.broadcasted_iota(jnp.int32, (step, 128), 1) < 64

    def back(k, carry):
        acc = jnp.zeros((2 * step, ch), F32)
        for t in range(9):
            r, c = 2 - t // 3, 2 - t % 3
            pieces = []
            for kk in (k, k + side):
                at = c * nf + lax.rem(kk, 2) * step
                pieces.append(pad_ref[kk // 2 + r, pl.ds(pl.multiple_of(at, 16), step), :])
            acc += nn(jnp.concatenate(pieces, axis=0), ktm_ref[:, t * ch : (t + 1) * ch])
        store_packed(rank, mate_ref, keep_ref, acc, k, step, low)
        return carry

    lax.fori_loop(0, side, back, 0, unroll=True)
    dt_copy.wait()
    ds_copy.wait()


def conv_back(rank, g, xhat, rs, w, lnt, vec, before, after, side, deps=()):
    half = g[0].shape[0]
    hc = vec.shape[1]
    ch = len(g) * 64
    pixels = 2 * half
    plane = pixels // side
    nf = plane // side
    outs = [
        jax.ShapeDtypeStruct((pixels, ch), BF),
        jax.ShapeDtypeStruct((pixels, hc), BF),
        jax.ShapeDtypeStruct((2, hc), F32),
        jax.ShapeDtypeStruct((4, half, 128), BF),
        jax.ShapeDtypeStruct((4, half, 128), BF),
    ]
    scratch = [
        pltpu.VMEM((pixels, ch), BF),
        pltpu.VMEM((pixels, hc), BF),
        pltpu.VMEM((side, plane, hc), F32),
        pltpu.VMEM((side, plane, hc), F32),
        pltpu.VMEM((side + 2, plane + 2 * nf, hc), BF),
        pltpu.VMEM((hc, 9 * ch), BF),
        pltpu.SemaphoreType.DMA((w.shape[0] + 3,)),
    ]
    flops = 2 * pixels * hc * 12 * ch
    return call(functools.partial(conv_back_body, side), outs, scratch, flops,
                rank, *g, xhat, rs, w, lnt, vec, before, after,
                deps=deps, far=(9, 11), far_outs=(0, 1))


def grads_body(side, pad_ref, hid_ref, ds_ref, dt_ref, before_ref, after_ref, mid_ref, out_ref,
               sg_ref, dst_ref, taps_ref, tg_ref, vec_ref):
    ch = pad_ref.shape[2]
    hc = hid_ref.shape[1]
    plane = hid_ref.shape[0] // side
    nf = plane // side
    for i in (0, 1, side + 2, side + 3):
        dst_ref[i] = jnp.zeros(dst_ref.shape[1:], BF)
    for i in range(side):
        at = slice(i * plane, (i + 1) * plane)
        h = hid_ref[at, :].astype(F32)
        taps_ref[i, 0:hc] = (pltpu.roll(h, 1, 0) * before_ref[0:plane, :]).T.astype(BF)
        taps_ref[i, hc : 2 * hc] = h.T.astype(BF)
        taps_ref[i, 2 * hc : 3 * hc] = (pltpu.roll(h, plane - 1, 0) * after_ref[0:plane, :]).T.astype(BF)
        dst_ref[i + 2] = ds_ref[at, :].astype(F32).T.astype(BF)
    tg_ref[0 : 3 * hc, :] = sum(
        nn(taps_ref[i], dt_ref[i * plane : (i + 1) * plane, :]) for i in range(side)
    )
    tg_ref[3 * hc :, :] = jnp.zeros((tg_ref.shape[0] - 3 * hc, ch), F32)
    nz, _, width = sg_ref.shape
    size = 3 * hc // (2 * nz)
    vec_ref[...] = jnp.zeros(vec_ref.shape, F32)
    vec_ref[size : size + 2, 0:hc] = mid_ref[...]
    vec_ref[size + 2 : size + 4, 0:128] = out_ref[...]
    tall = vec_ref.shape[0]
    inside = lax.broadcasted_iota(jnp.int32, (tall, ch), 0) < size
    off = (width // 2) % 128
    for z in range(nz):
        first, second = [
            jnp.where(inside, tg_ref[b * size : b * size + tall, :], vec_ref[...])
            for b in (2 * z, 2 * z + 1)
        ]
        start = width // 2 - off
        sg_ref[z, hc : hc + tall, 0:ch] = first.astype(BF)
        second = pltpu.roll(jnp.concatenate([second, jnp.zeros((tall, 128), F32)], axis=1), off, 1)
        sg_ref[z, hc : hc + tall, start : start + ch + 128] = second.astype(BF)
    for c in range(3):
        acc = sum(
            nn(dst_ref[i : i + 3].reshape(3 * hc, plane), pad_ref[i, c * nf : c * nf + plane, :])
            for i in range(1, side + 1)
        )
        for r in range(3):
            first = (3 * r + c) * ch
            end = first + ch
            at = (2 - r) * hc
            done = 0
            while first < end:
                z = first // width
                last = min(end, (z + 1) * width)
                sg_ref[z, 0:hc, first - z * width : last - z * width] = (
                    acc[at : at + hc, done : done + last - first].astype(BF)
                )
                done += last - first
                first = last


def kernel_grads(pad, hidden, ds, dt, before, after, mid, out, side, shape, deps=()):
    pixels, hc = hidden.shape
    ch = dt.shape[1]
    plane = pixels // side
    outs = [jax.ShapeDtypeStruct(shape, BF)]
    tall = shape[1] - hc
    scratch = [
        pltpu.VMEM((side + 4, hc, plane), BF),
        pltpu.VMEM((side, 3 * hc, plane), BF),
        pltpu.VMEM((3 * hc + tall, ch), F32),
        pltpu.VMEM((tall, ch), F32),
    ]
    flops = 2 * pixels * hc * 12 * ch
    return call(functools.partial(grads_body, side), outs, scratch, flops,
                pad, hidden, ds, dt, before, after, mid, out, deps=deps)[0]


def copy_after_body(v_ref, out_ref):
    out_ref[...] = v_ref[...]


def after_all(v, *deps):
    return call(copy_after_body, [jax.ShapeDtypeStruct(v.shape, v.dtype)], [], v.size, v, deps=deps)[0]


def pack_kernels_body(kt_ref, lt_ref, vec_ref, out_ref, low_ref):
    ranks, _, width = out_ref.shape
    hc = kt_ref.shape[0] // ranks
    blocks = lt_ref.shape[0] // hc
    q = hc // ranks
    low_ref[...] = jnp.zeros(low_ref.shape, F32)
    for r in range(ranks):
        out_ref[r, 0:hc, :] = kt_ref[r * hc : (r + 1) * hc, :]
        for b in range(blocks):
            low_ref[r, b * q : (b + 1) * q, 0 : lt_ref.shape[1]] = (
                lt_ref[b * hc + r * q : b * hc + (r + 1) * q, :]
            )
        low_ref[r, blocks * q : blocks * q + 1, :] = vec_ref[...]
        out_ref[r, hc:, :] = low_ref[r].astype(BF)


def pack_kernels(kt, lt, vec, ranks, tall, deps):
    width = kt.shape[1]
    outs = [jax.ShapeDtypeStruct((ranks, kt.shape[0] // ranks + tall, width), BF)]
    scratch = [pltpu.VMEM((ranks, tall, width), F32)]
    return call(pack_kernels_body, outs, scratch, kt.size * 8, kt, lt, vec, deps=deps)[0]


def hop(v, k):
    n = 1
    for name in EVERY:
        n *= lax.axis_size(name)
    return lax.ppermute(v, EVERY, [(i, i ^ k) for i in range(n)])


def plane_gather(v):
    got = {0: v}
    for k in (6, 2, 4, 1):
        got[k] = hop(v, k)
    for k in (2, 4, 6):
        got[k ^ 1] = hop(got[k], 1)
    return [got[k] for k in range(8)]


def plane_reduce(mate, keep, deps=()):
    sums = pair_sum(keep, hop(mate, 1), deps)
    arrived = {k: hop(sums[k // 2], k) for k in (6, 2, 4)}
    return [sums[0], arrived[2], arrived[4], arrived[6]]


def to_section(v, section, n_seg):
    y = lax.axis_index("y")
    near = lax.dynamic_index_in_dim(v, y, 0, keepdims=False)
    far = lax.dynamic_index_in_dim(v, 1 - y, 0, keepdims=False)
    n = 2 * n_seg * lax.axis_size("z")
    got = []
    for base, block in ((0, near), (n_seg, far)):
        row = []
        for low in range(n_seg):
            k = base + (low ^ section)
            if k == 0:
                row.append(block)
            else:
                pairs = [(i, i ^ k) for i in range(n) if i % n_seg == low]
                row.append(lax.ppermute(block, EVERY, pairs))
        got.append(jnp.stack(row))
    same, other = got
    return jnp.where(y == 0, jnp.concatenate([same, other]), jnp.concatenate([other, same]))

def on_device(frames, cot, starts, ks, ktm, mg, mb, og, ob):
    nz, n_rank, n_seg = lax.axis_size("z"), 8, 4
    n_dp = nz * 2
    fr, side, ch = frames.shape[0], frames.shape[1], frames.shape[3]
    area = side * side
    hid = ks.shape[2]
    hc, cc = hid // n_rank, ch // n_rank
    q = hc // n_rank
    rank = lax.axis_index(PLANE)
    rank_now = rank.astype(jnp.int32).reshape(1)
    d_index = lax.axis_index(("z", "y"))
    s_index = lax.axis_index(("x", "c"))
    nf = n_dp * fr
    pixels = area * nf
    half = pixels // 2

    to_plane = [(d * n_seg + s, s * n_rank + d) for d in range(n_dp) for s in range(n_seg)]
    from_plane = [(b, a) for a, b in to_plane]
    rows = fr * area
    flag_row = jnp.pad(starts.astype(BF)[None], ((0, 11), (0, ch - fr)))
    lead = rows + 12
    moving = jnp.concatenate([frames.reshape(rows, ch), flag_row, cot.reshape(rows, ch)], axis=0)
    moving = lax.ppermute(moving, EVERY, to_plane)

    perm = (jnp.arange(hid).reshape(n_rank, n_rank, q).transpose(1, 0, 2).reshape(hid)[:, None]
            == jnp.arange(hid)[None, :]).astype(BF)
    kt = lax.dot_general(perm, ks[0].astype(BF), (((1,), (1,)), ((), ())),
                         preferred_element_type=F32).astype(BF)
    lrows, width = ktm.shape[1] // n_rank, ks.shape[1]
    tall = -(-(lrows + 4) // 16) * 16
    extra = jnp.concatenate([mg, mb, og, ob], axis=1)
    extra = jnp.pad(extra, ((0, 0), (0, width - extra.shape[1])))
    w = pack_kernels(kt, ktm[0], extra, n_rank, tall, deps=(moving,))
    w = lax.all_to_all(w, PLANE, 0, 0)
    here = w
    high = hc + tall

    w = w.reshape(2, n_seg, high, width).transpose(1, 2, 0, 3).reshape(n_seg, high, 2 * width)
    ws = [lax.all_gather(w[s], "z", axis=0) for s in range(n_seg)]

    group = 7
    own = moving[lead:].reshape(group, rows // group, n_rank, cc).transpose(2, 1, 0, 3)
    own = own.reshape(n_rank, rows // group, group * cc)
    own = jnp.pad(own, ((0, 0), (0, 4), (0, ch - group * cc)))
    own = jnp.concatenate([jnp.broadcast_to(moving[:lead], (n_rank, lead, ch)), own], axis=1)
    gathered = lax.all_to_all(after_all(own, here), PLANE, 0, 0)
    mids, outs = [], []
    for s in range(n_seg):
        row = ws[s][:, hc + lrows].reshape(n_dp, width).astype(F32)
        mids.append(jnp.stack([
            lax.dynamic_slice_in_dim(row[:, i * hc : (i + 1) * hc], rank * q, q, axis=1).reshape(hc)
            for i in range(2)]))
        own = lax.dynamic_index_in_dim(row, rank, 0, keepdims=False)
        outs.append(jnp.stack([
            jnp.tile(own[2 * hc + i * cc : 2 * hc + (i + 1) * cc], 2) for i in range(2)]))

    def by_pixel(v):
        width = v.shape[2]
        v = v.reshape(n_rank * fr, area, width).transpose(1, 0, 2)
        return v.reshape(pixels, width)

    def packed(v):
        return jnp.concatenate([v[:half], v[half:]], axis=1)

    a0 = by_pixel(gathered[:, :rows])
    flags = gathered[:, rows, :fr].reshape(nf) > 0.5
    slot = jnp.arange(nf) % fr
    before = jnp.where(flags | (slot == 0), 0.0, 1.0)
    after = jnp.where(jnp.roll(flags, -1) | (slot == fr - 1), 0.0, 1.0)
    spread = (side * nf + nf, hc)
    before = jnp.broadcast_to(jnp.tile(before, side + 1)[:, None], spread)
    after = jnp.broadcast_to(jnp.tile(after, side + 1)[:, None], spread)
    skip = packed(lax.dynamic_slice_in_dim(a0, rank * cc, cc, axis=1))

    cot_own = gathered[:, lead : lead + rows // group, : group * cc]
    cot_own = cot_own.reshape(n_rank, rows // group, group, cc).transpose(0, 2, 1, 3)
    cot_own = packed(by_pixel(cot_own.reshape(n_rank, rows, cc)))

    def to_frames(*slices):
        n = len(slices)
        v = jnp.stack([jnp.concatenate([v[:, :cc], v[:, cc:]], axis=0) for v in slices])
        v = v.reshape(n, area, n_rank, fr, cc).transpose(2, 0, 1, 3, 4).reshape(n_rank, n * rows, cc)
        v = lax.all_to_all(v, PLANE, 0, 0).transpose(1, 0, 2).reshape(n * rows, ch)
        v = lax.ppermute(v, EVERY, from_plane).reshape(n, area, fr, ch).transpose(0, 2, 1, 3)
        return v.reshape(n, *frames.shape)

    saved = []
    g = [a0]
    ready = prepare(ws[0], hc, ch)
    for s in range(n_seg):
        kn, lt, lnt = ready
        pad, hidden, xm, rm, mate, keep = conv_forward(
            rank_now, g, kn, lt, mids[s], before, after, side, pixels, ch)
        parts = plane_reduce(mate, keep)
        if s < n_seg - 1:
            ready = prepare(ws[s + 1], hc, ch)
        xo, ro, pre, res = out_norm(parts, outs[s], skip if s % 2 == 1 else None, deps=ready[:1])
        saved.append((pad, hidden, xm, rm, xo, ro, pre, lnt))
        if s % 2 == 1:
            skip = res
        if s < n_seg - 1:
            g = plane_gather(res)

    parts = [cot_own]
    skip_grad = None
    def by_row(v):
        return v.reshape(high, 2, width).transpose(1, 0, 2)

    grads, raw = [], None
    for s in reversed(range(n_seg)):
        pad, hidden, xm, rm, xo, ro, pre, lnt = saved[s]
        if s == 1:
            parts = parts + [skip_grad]
        deps = () if raw is None else (raw, *grads[len(grads) - 1 :])
        dpre, dt, osum = out_back(parts, pre, xo, ro, outs[s], deps=deps)
        if raw is not None:
            grads.append(lax.psum_scatter(after_all(raw, dt), "z", scatter_dimension=0))
        if s % 2 == 1:
            skip_grad = dpre
        dtf, ds, msum, mate, keep = conv_back(
            rank_now, plane_gather(dt), xm, rm, ws[s], lnt, mids[s], before, after, side)
        if s > 0:
            parts = plane_reduce(mate, keep)
        raw = kernel_grads(pad, hidden, ds, dtf, before, after, msum, osum, side, ws[s].shape,
                           deps=parts[:1] if s > 0 else ())
    last = lax.psum_scatter(raw, "z", scatter_dimension=0)
    early = jnp.stack([jnp.zeros((2, high, width), BF)] + [by_row(v) for v in grads[::-1]], axis=1)
    early = lax.all_to_all(early.reshape(n_rank, high, width), PLANE, 0, 0)
    parts = plane_reduce(mate, keep, deps=(raw,))

    da = sum(p.astype(F32) for p in parts) + skip_grad.astype(F32)
    output, frames_grad = to_frames(res, da.astype(BF))
    frames_grad = frames_grad.astype(F32)

    last = to_section(after_all(by_row(last), early, *parts[1:]), 0, n_seg)
    g = jnp.where(s_index == 0, last, early)
    space_grad = lax.dot_general(g[:, :hc].reshape(hid, width), perm, (((0,), (0,)), ((), ())),
                                 preferred_element_type=F32)
    tg = g[:, hc : hc + lrows, :ch].reshape(n_rank, -1, q, ch)
    time_grad = tg.transpose(1, 0, 2, 3).reshape(-1, ch).astype(F32)
    sums = g[:, hc + lrows : hc + lrows + 4].astype(F32)

    def mid_own(v):
        return lax.dynamic_slice_in_dim(v[:, :hc], d_index * q, q, axis=1).reshape(1, hc)

    own = lax.dynamic_index_in_dim(sums, d_index, 0, keepdims=False)
    return (
        output,
        frames_grad,
        space_grad[None],
        time_grad[None],
        mid_own(sums[:, 0]),
        mid_own(sums[:, 1]),
        own[2:3, :cc],
        own[3:4, :cc],
    )


def from_behind(value, axis, steps):
    count = lax.axis_size(axis)
    leading, last = (max(0, -steps), min(count, count - steps))
    return lax.ppermute(value, axis, [(source, source + steps) for source in range(leading, last)])


def space_apply(current, kernel):
    frame_side = current.shape[1]
    padded = jnp.pad(current, ((0, 0), (1, 1), (1, 1), (0, 0)))
    stacked = jnp.concatenate(
        [
            padded[:, row_shift : row_shift + frame_side, col_shift : col_shift + frame_side, :]
            for row_shift in range(3)
            for col_shift in range(3)
        ],
        axis=-1,
    )
    return (
        stacked,
        jnp.einsum("fijc,co->fijo", stacked, kernel, preferred_element_type=jnp.float32),
    )


def space_back(gradient, kernel):
    frame_side = gradient.shape[1]
    channels = kernel.shape[0] // 9
    spread = jnp.einsum("fijo,co->fijc", gradient, kernel, preferred_element_type=jnp.float32)
    total = jnp.zeros((gradient.shape[0], frame_side + 2, frame_side + 2, channels), jnp.float32)
    for tap_index in range(9):
        row_shift = tap_index // 3
        col_shift = tap_index % 3
        piece_now = spread[..., tap_index * channels : (tap_index + 1) * channels]
        total = total + jnp.pad(
            piece_now, ((0, 0), (row_shift, 2 - row_shift), (col_shift, 2 - col_shift), (0, 0))
        )
    return total[:, 1 : frame_side + 1, 1 : frame_side + 1, :]


def time_apply(current, kernel, before_mask, after_mask):
    blanks = jnp.zeros_like(current[:1])
    earlier = jnp.concatenate([blanks, current[:-1]], axis=0) * before_mask[
        :, None, None, None
    ].astype(current.dtype)
    later = jnp.concatenate([current[1:], blanks], axis=0) * after_mask[:, None, None, None].astype(
        current.dtype
    )
    stacked = jnp.concatenate([earlier, current, later], axis=-1)
    return (
        stacked,
        jnp.einsum("fijc,co->fijo", stacked, kernel, preferred_element_type=jnp.float32),
    )


def time_back(gradient, kernel, before_mask, after_mask):
    channels = kernel.shape[0] // 3
    spread = jnp.einsum("fijo,co->fijc", gradient, kernel, preferred_element_type=jnp.float32)
    early_part = spread[..., :channels] * before_mask[:, None, None, None]
    late_part = spread[..., 2 * channels :] * after_mask[:, None, None, None]
    blanks = jnp.zeros_like(early_part[:1])
    moved_early = jnp.concatenate([early_part[1:], blanks], axis=0)
    moved_late = jnp.concatenate([blanks, late_part[:-1]], axis=0)
    return spread[..., channels : 2 * channels] + moved_early + moved_late


def moments(values, pixel_count):
    average = lax.psum(jnp.sum(values, axis=(0, 1, 2)), "dp") / pixel_count
    centered = values - average
    spread = lax.psum(jnp.sum(centered * centered, axis=(0, 1, 2)), "dp") / pixel_count
    return (average, lax.rsqrt(spread + eps))


def reduce_back(gradient, normed):
    return lax.psum(
        (jnp.sum(gradient, axis=(0, 1, 2)), jnp.sum(gradient * normed, axis=(0, 1, 2))), "dp"
    )


def silu_slope(values):
    sigmoid_now = jax.nn.sigmoid(values)
    return sigmoid_now * (1.0 + values * (1.0 - sigmoid_now))


def pick_slot(stack, slot_index):
    return lax.dynamic_index_in_dim(stack, slot_index, 0, keepdims=False)


def store_slot(stack, value, slot_index, usable):
    previous = pick_slot(stack, slot_index)
    return lax.dynamic_update_index_in_dim(stack, jnp.where(usable, value, previous), slot_index, 0)


def on_device_general(
    frames, cotangent, starts, space_kernel, time_kernel, mid_gain, mid_bias, out_gain, out_bias
):
    n_segment = lax.axis_size("segment")
    n_data = lax.axis_size("dp")
    segment_index = lax.axis_index("segment")
    odd_segment = segment_index % 2 == 1
    last_segment = segment_index == n_segment - 1
    first_segment = segment_index == 0
    frame_count = frames.shape[0]
    frame_side = frames.shape[1]
    channels = frames.shape[3]
    hidden_units = mid_gain.shape[1] * n_data
    pixel_count = n_data * frame_count * frame_side * frame_side
    turns = 2 * n_segment - 1
    block_shape = (n_segment,) + frames.shape
    all_frames, all_cot, all_starts = (
        lax.all_gather(frames, "segment", axis=0, tiled=True),
        lax.all_gather(cotangent, "segment", axis=0, tiled=True),
        lax.all_gather(starts.astype(jnp.bfloat16), "segment", axis=0, tiled=True),
    )
    frame_stack = all_frames.reshape(block_shape)
    cot_stack = all_cot.reshape(block_shape)
    clip_flags = all_starts.astype(jnp.float32).reshape(n_segment, frame_count)
    positions = jnp.arange(frame_count)
    before_mask = jnp.where((clip_flags > 0.5) | (positions == 0), 0.0, 1.0)
    following = jnp.concatenate([clip_flags[:, 1:], jnp.ones((n_segment, 1), jnp.float32)], axis=1)
    after_mask = jnp.where(following > 0.5, 0.0, 1.0)
    gathered = (
        lax.all_gather(space_kernel[0].astype(jnp.bfloat16), "dp", axis=0, tiled=True),
        lax.all_gather(time_kernel[0].astype(jnp.bfloat16), "dp", axis=0, tiled=True),
        lax.all_gather(mid_gain[0].astype(jnp.bfloat16), "dp", axis=0, tiled=True),
        lax.all_gather(mid_bias[0].astype(jnp.bfloat16), "dp", axis=0, tiled=True),
        lax.all_gather(out_gain[0].astype(jnp.bfloat16), "dp", axis=0, tiled=True),
        lax.all_gather(out_bias[0].astype(jnp.bfloat16), "dp", axis=0, tiled=True),
    )
    space_low, time_low = (gathered[0], gathered[1])
    mid_gain_now = gathered[2].astype(jnp.float32)
    mid_bias_now = gathered[3].astype(jnp.float32)
    out_gain_now = gathered[4].astype(jnp.float32)
    out_bias_now = gathered[5].astype(jnp.float32)
    incoming = jnp.zeros_like(frames)
    carried = jnp.zeros_like(frames)
    kept_input = jnp.zeros(block_shape, jnp.bfloat16)
    kept_skip = jnp.zeros(block_shape, jnp.bfloat16)
    kept_mid_mean = jnp.zeros((n_segment, hidden_units), jnp.float32)
    kept_mid_scale = jnp.zeros((n_segment, hidden_units), jnp.float32)
    kept_out_mean = jnp.zeros((n_segment, channels), jnp.float32)
    kept_out_scale = jnp.zeros((n_segment, channels), jnp.float32)
    results = jnp.zeros(block_shape, jnp.float32)
    for turn_index in range(turns):
        micro_index = turn_index - segment_index
        usable = (micro_index >= 0) & (micro_index < n_segment)
        slot_index = jnp.clip(micro_index, 0, n_segment - 1)
        current = jnp.where(first_segment, pick_slot(frame_stack, slot_index), incoming)
        skip_input = carried
        _, spatial = space_apply(current, space_low)
        mid_mean, mid_scale = moments(spatial, pixel_count)
        hidden_act = jax.nn.silu(
            (spatial - mid_mean) * mid_scale * mid_gain_now + mid_bias_now
        ).astype(jnp.bfloat16)
        _, temporal = time_apply(
            hidden_act,
            time_low,
            pick_slot(before_mask, slot_index),
            pick_slot(after_mask, slot_index),
        )
        out_mean, out_scale = moments(temporal, pixel_count)
        pre_act = (
            (temporal - out_mean) * out_scale * out_gain_now
            + out_bias_now
            + jnp.where(odd_segment, skip_input.astype(jnp.float32), 0.0)
        )
        result = jax.nn.silu(pre_act).astype(jnp.bfloat16)
        kept_input = store_slot(kept_input, current, slot_index, usable)
        kept_skip = store_slot(kept_skip, skip_input, slot_index, usable)
        kept_mid_mean = store_slot(kept_mid_mean, mid_mean, slot_index, usable)
        kept_mid_scale = store_slot(kept_mid_scale, mid_scale, slot_index, usable)
        kept_out_mean = store_slot(kept_out_mean, out_mean, slot_index, usable)
        kept_out_scale = store_slot(kept_out_scale, out_scale, slot_index, usable)
        results = store_slot(results, result.astype(jnp.float32), slot_index, usable)
        if turn_index < turns - 1:
            incoming, carried = from_behind(
                (result, jnp.where(odd_segment, result, current)), "segment", 1
            )
    gathered = (
        lax.all_gather(space_kernel[0].astype(jnp.bfloat16), "dp", axis=0, tiled=True),
        lax.all_gather(time_kernel[0].astype(jnp.bfloat16), "dp", axis=0, tiled=True),
        lax.all_gather(mid_gain[0].astype(jnp.bfloat16), "dp", axis=0, tiled=True),
        lax.all_gather(mid_bias[0].astype(jnp.bfloat16), "dp", axis=0, tiled=True),
        lax.all_gather(out_gain[0].astype(jnp.bfloat16), "dp", axis=0, tiled=True),
        lax.all_gather(out_bias[0].astype(jnp.bfloat16), "dp", axis=0, tiled=True),
    )
    space_low, time_low = (gathered[0], gathered[1])
    mid_gain_now = gathered[2].astype(jnp.float32)
    mid_bias_now = gathered[3].astype(jnp.float32)
    out_gain_now = gathered[4].astype(jnp.float32)
    out_bias_now = gathered[5].astype(jnp.float32)
    grad_input = jnp.zeros_like(frames)
    grad_skip = jnp.zeros_like(frames)
    space_acc = jnp.zeros(space_low.shape, jnp.float32)
    time_acc = jnp.zeros(time_low.shape, jnp.float32)
    mid_gain_acc = jnp.zeros((hidden_units,), jnp.float32)
    mid_bias_acc = jnp.zeros((hidden_units,), jnp.float32)
    out_gain_acc = jnp.zeros((channels,), jnp.float32)
    out_bias_acc = jnp.zeros((channels,), jnp.float32)
    input_grads = jnp.zeros(block_shape, jnp.float32)
    for turn_index in range(turns):
        micro_index = n_segment - 1 - (turn_index - (n_segment - 1 - segment_index))
        usable = (micro_index >= 0) & (micro_index < n_segment)
        usable_weight = usable.astype(jnp.float32)
        slot_index = jnp.clip(micro_index, 0, n_segment - 1)
        current = pick_slot(kept_input, slot_index)
        skip_input = pick_slot(kept_skip, slot_index)
        before_now = pick_slot(before_mask, slot_index)
        after_now = pick_slot(after_mask, slot_index)
        space_taps, spatial = space_apply(current, space_low)
        mid_normed = (spatial - pick_slot(kept_mid_mean, slot_index)) * pick_slot(
            kept_mid_scale, slot_index
        )
        mid_pre = mid_normed * mid_gain_now + mid_bias_now
        hidden_act = jax.nn.silu(mid_pre).astype(jnp.bfloat16)
        time_taps, temporal = time_apply(hidden_act, time_low, before_now, after_now)
        out_scale = pick_slot(kept_out_scale, slot_index)
        out_normed = (temporal - pick_slot(kept_out_mean, slot_index)) * out_scale
        pre_act = (
            out_normed * out_gain_now
            + out_bias_now
            + jnp.where(odd_segment, skip_input.astype(jnp.float32), 0.0)
        )
        grad_result = jnp.where(
            last_segment,
            pick_slot(cot_stack, slot_index).astype(jnp.float32),
            grad_input.astype(jnp.float32)
            + jnp.where(odd_segment, grad_skip.astype(jnp.float32), 0.0),
        )
        grad_pre = grad_result * silu_slope(pre_act)
        out_bias_sum, out_gain_sum = reduce_back(grad_pre, out_normed)
        grad_temporal = (
            out_gain_now
            * out_scale
            * (grad_pre - out_bias_sum / pixel_count - out_normed * out_gain_sum / pixel_count)
        ).astype(jnp.bfloat16)
        time_acc = time_acc + usable_weight * jnp.einsum(
            "fijc,fijo->co", time_taps, grad_temporal, preferred_element_type=jnp.float32
        )
        grad_hidden = time_back(grad_temporal, time_low, before_now, after_now)
        grad_mid = grad_hidden * silu_slope(mid_pre)
        mid_bias_sum, mid_gain_sum = reduce_back(grad_mid, mid_normed)
        mid_scale = pick_slot(kept_mid_scale, slot_index)
        grad_spatial = (
            mid_gain_now
            * mid_scale
            * (grad_mid - mid_bias_sum / pixel_count - mid_normed * mid_gain_sum / pixel_count)
        ).astype(jnp.bfloat16)
        space_acc = space_acc + usable_weight * jnp.einsum(
            "fijc,fijo->co", space_taps, grad_spatial, preferred_element_type=jnp.float32
        )
        grad_current = space_back(grad_spatial, space_low)
        mid_gain_acc = mid_gain_acc + usable_weight * mid_gain_sum
        mid_bias_acc = mid_bias_acc + usable_weight * mid_bias_sum
        out_gain_acc = out_gain_acc + usable_weight * out_gain_sum
        out_bias_acc = out_bias_acc + usable_weight * out_bias_sum
        input_grads = store_slot(
            input_grads, grad_current + grad_skip.astype(jnp.float32), slot_index, usable
        )
        if turn_index < turns - 1:
            grad_input, grad_skip = from_behind(
                (
                    grad_current.astype(jnp.bfloat16),
                    jnp.where(odd_segment, grad_pre.astype(jnp.bfloat16), grad_skip),
                ),
                "segment",
                -1,
            )
    space_grad, time_grad = (
        lax.psum_scatter(space_acc, "dp", scatter_dimension=0, tiled=True),
        lax.psum_scatter(time_acc, "dp", scatter_dimension=0, tiled=True),
    )
    data_index = lax.axis_index("dp")

    def own_share(full_vector):
        share = full_vector.shape[0] // n_data
        return lax.dynamic_slice_in_dim(full_vector, data_index * share, share)[None]

    flat_shape = (n_segment * frame_count,) + frames.shape[1:]
    arrived_out, arrived_grads = (
        lax.all_to_all(
            results.reshape(flat_shape).astype(jnp.bfloat16),
            "segment",
            split_axis=0,
            concat_axis=0,
            tiled=True,
        ).astype(jnp.float32),
        lax.all_to_all(
            input_grads.reshape(flat_shape).astype(jnp.bfloat16),
            "segment",
            split_axis=0,
            concat_axis=0,
            tiled=True,
        ).astype(jnp.float32),
    )
    output = arrived_out[(n_segment - 1) * frame_count :].astype(jnp.bfloat16)
    frames_grad = arrived_grads[:frame_count]
    return (
        output,
        frames_grad,
        space_grad[None],
        time_grad[None],
        own_share(mid_gain_acc),
        own_share(mid_bias_acc),
        own_share(out_gain_acc),
        own_share(out_bias_acc),
    )


def general(mesh):
    return jax.shard_map(
        on_device_general,
        mesh=mesh,
        in_specs=(
            P(("dp", "segment"), None, None, None),
            P(("dp", "segment"), None, None, None),
            P(("dp", "segment")),
            P("segment", "dp", None),
            P("segment", "dp", None),
            P("segment", "dp"),
            P("segment", "dp"),
            P("segment", "dp"),
            P("segment", "dp"),
        ),
        out_specs=(
            P(("dp", "segment"), None, None, None),
            P(("dp", "segment"), None, None, None),
            P("segment", "dp", None),
            P("segment", "dp", None),
            P("segment", "dp"),
            P("segment", "dp"),
            P("segment", "dp"),
            P("segment", "dp"),
        ),
        check_vma=False,
    )


def solution(mesh):
    if mesh.shape["dp"] != 8 or mesh.shape["segment"] != 4:
        return general(mesh)
    n_dp, n_seg = mesh.shape["dp"], mesh.shape["segment"]
    fine = Mesh(mesh.devices.reshape(n_dp // 2, 2, 2, n_seg // 2), EVERY)
    dp, seg = ("z", "y"), ("x", "c")
    return jax.shard_map(
        on_device,
        mesh=fine,
        in_specs=(
            P(EVERY, None, None, None),
            P(EVERY, None, None, None),
            P(EVERY),
            P(seg, dp, None),
            P(seg, dp, None),
            P(seg, dp),
            P(seg, dp),
            P(seg, dp),
            P(seg, dp),
        ),
        out_specs=(
            P(EVERY, None, None, None),
            P(EVERY, None, None, None),
            P(seg, dp, None),
            P(seg, dp, None),
            P(seg, dp),
            P(seg, dp),
            P(seg, dp),
            P(seg, dp),
        ),
        check_vma=False,
    )
```

```python
import functools

import jax
import jax.numpy as jnp
from jax import lax
from jax.experimental import pallas as pl
from jax.experimental.pallas import tpu as pltpu
from jax.sharding import Mesh, PartitionSpec as P

eps = 1e-05
PLANE = ("y", "x", "c")
EVERY = ("z", "y", "x", "c")
BF = jnp.bfloat16
F32 = jnp.float32


def nt(a, b):
    return lax.dot_general(a, b, (((1,), (1,)), ((), ())), preferred_element_type=F32)


def nn(a, b):
    return lax.dot_general(a, b, (((1,), (0,)), ((), ())), preferred_element_type=F32)


VMEM_CAP = 56 * 1024 * 1024
ANY = pl.BlockSpec(memory_space=pl.ANY)


def call(body, outs, scratch, flops, *args, deps=(), far=(), far_outs=()):
    moved = sum(a.size * a.dtype.itemsize for a in args) + sum(
        o.size * o.dtype.itemsize for o in outs
    )
    n = len(deps)

    def spec(a):
        return pl.BlockSpec(memory_space=pltpu.SMEM if a.dtype == jnp.int32 else pltpu.VMEM)

    return pl.pallas_call(
        lambda *refs: body(*refs[n:]),
        out_shape=outs,
        in_specs=[ANY] * n + [ANY if i in far else spec(a) for i, a in enumerate(args)],
        out_specs=[ANY if i in far_outs else spec(o) for i, o in enumerate(outs)],
        scratch_shapes=scratch,
        compiler_params=pltpu.CompilerParams(vmem_limit_bytes=VMEM_CAP),
        cost_estimate=pl.CostEstimate(flops=flops, bytes_accessed=moved, transcendentals=0),
    )(*deps, *args)


def chunk(i, size):
    return pl.ds(pl.multiple_of(i * size, 16), size)


def clear_borders(pad_ref, side, plane, nf):
    zrow = jnp.zeros(pad_ref.shape[1:], BF)
    pad_ref[0] = zrow
    pad_ref[side + 1] = zrow
    zcol = jnp.zeros((nf, pad_ref.shape[2]), BF)
    for i in range(side):
        pad_ref[i + 1, 0:nf] = zcol
        pad_ref[i + 1, nf + plane : 2 * nf + plane] = zcol


def by_rank(slices, rank):
    odd = lax.rem(rank, 2) == 1
    for p in range(len(slices) // 2):
        a, b = slices[2 * p], slices[2 * p + 1]
        yield lax.bitwise_xor(rank // 2, p), odd, a, b


def halves(odd, own, mate):
    low = lax.broadcasted_iota(jnp.int32, own.shape, 1) < 64
    own, mate = own.astype(F32), mate.astype(F32)
    a, b = jnp.where(odd, mate, own), jnp.where(odd, own, mate)
    top = jnp.where(low, a, pltpu.roll(b, 64, 1))
    bottom = jnp.where(low, pltpu.roll(a, 64, 1), b)
    return top, bottom


def store_packed(rank, mate_ref, keep_ref, part, k, step, low):
    rows_now = chunk(k, step)
    odd = lax.rem(rank, 2) == 1
    for q in range(keep_ref.shape[0]):
        x = part[:step, 128 * q : 128 * q + 128]
        y = part[step:, 128 * q : 128 * q + 128]
        even_slice = jnp.where(low, x, pltpu.roll(y, 64, 1))
        odd_slice = jnp.where(low, pltpu.roll(x, 64, 1), y)
        p = lax.bitwise_xor(rank // 2, q)
        keep_ref[p, rows_now, :] = jnp.where(odd, odd_slice, even_slice).astype(BF)
        mate_ref[p, rows_now, :] = jnp.where(odd, even_slice, odd_slice).astype(BF)


def fetch_kernels(w_ref, ktm_ref, lw_ref, sems):
    nz, _, width = w_ref.shape
    hc = ktm_ref.shape[0]
    copies = []
    for z in range(nz):
        copies.append(pltpu.make_async_copy(
            w_ref.at[z, pl.ds(0, hc)], ktm_ref.at[:, pl.ds(z * width, width)], sems.at[2 * z]))
        copies.append(pltpu.make_async_copy(
            w_ref.at[z, pl.ds(hc, lw_ref.shape[1])], lw_ref.at[z], sems.at[2 * z + 1]))
    for copy in copies:
        copy.start()
    return copies


def join_temporal(lw_ref, lf_ref, ltm_ref):
    ch = ltm_ref.shape[1]
    width = lw_ref.shape[2] // 2
    count = 2 * lw_ref.shape[0]
    size = ltm_ref.shape[0] // count
    for z in range(lw_ref.shape[0]):
        first = lw_ref[z, :, 0:ch].astype(F32)
        off = width % 128
        second = lw_ref[z, :, width - off : width - off + ch + 128].astype(F32)
        second = pltpu.roll(second, ch + 128 - off, 1)[:, 0:ch]
        for b, block in ((2 * z, first), (2 * z + 1, second)):
            lf_ref[b * size : b * size + block.shape[0], :] = block
    ltm_ref[...] = lf_ref[0 : ltm_ref.shape[0], :].astype(BF)


def prepare_body(w_ref, kn_out, l_out, lt_out, ktm_ref, lw_ref, lf_ref, sems):
    hc, ch = ktm_ref.shape[0], l_out.shape[1]
    for copy in fetch_kernels(w_ref, ktm_ref, lw_ref, sems):
        copy.wait()
    for t in range(9):
        kn_out[t] = ktm_ref[:, t * ch : (t + 1) * ch].astype(F32).T.astype(BF)
    join_temporal(lw_ref, lf_ref, l_out)
    for t in range(3):
        lt_out[t] = lf_ref[t * hc : (t + 1) * hc].T.astype(BF)


def prepare(w, hc, ch, deps=()):
    outs = [
        jax.ShapeDtypeStruct((9, ch, hc), BF),
        jax.ShapeDtypeStruct((3 * hc, ch), BF),
        jax.ShapeDtypeStruct((3, ch, hc), BF),
    ]
    tall = w.shape[1] - hc
    scratch = [
        pltpu.VMEM((hc, 9 * ch), BF),
        pltpu.VMEM((w.shape[0], tall, w.shape[2]), BF),
        pltpu.VMEM((3 * hc + tall, ch), F32),
        pltpu.SemaphoreType.DMA((2 * w.shape[0],)),
    ]
    return call(prepare_body, outs, scratch, 2 * w.size * 512, w, deps=deps, far=(0,))


def conv_body(side, first, rank_ref, *refs):
    n = 1 if first else 8
    slices = refs[:n]
    (kn_in, ltm_ref, vec_ref, before_ref, after_ref,
     pad_out, hid_out, xhat_out, rs_ref, mate_ref, keep_ref,
     pad_ref, hid_ref, xhat_ref, sp_ref, kn_ref, sems) = refs[n:]
    rank = rank_ref[0]
    kn_copy = pltpu.make_async_copy(kn_in, kn_ref, sems.at[0])
    kn_copy.start()
    ch, hc = pad_ref.shape[2], hid_ref.shape[1]
    rows = hid_ref.shape[0]
    plane = rows // side
    nf = plane // side
    step = plane // 2
    clear_borders(pad_ref, side, plane, nf)
    if first:
        for i in range(side):
            pad_ref[i + 1, nf : nf + plane] = slices[0][i * plane : (i + 1) * plane]
    else:
        def place(k, carry):
            for q, odd, a_ref, b_ref in by_rank(slices, rank):
                top, bottom = halves(odd, a_ref[chunk(k, step), :], b_ref[chunk(k, step), :])
                lanes = pl.ds(pl.multiple_of(128 * q, 128), 128)
                for piece, kk in ((top, k), (bottom, k + side)):
                    at = nf + lax.rem(kk, 2) * step
                    pad_ref[1 + kk // 2, pl.ds(pl.multiple_of(at, 16), step), lanes] = piece.astype(BF)
            return carry

        lax.fori_loop(0, side, place, 0, unroll=True)
    pad_copy = pltpu.make_async_copy(pad_ref, pad_out, sems.at[1])
    pad_copy.start()
    kn_copy.wait()

    def conv(i, total):
        acc = jnp.zeros((plane, hc), F32)
        for t in range(9):
            r, c = t // 3, t % 3
            acc += nn(pad_ref[i + r, c * nf : c * nf + plane, :], kn_ref[t])
        sp_ref[i] = acc
        return total + jnp.sum(acc, axis=0, keepdims=True)

    mean = lax.fori_loop(0, side, conv, jnp.zeros((1, hc), F32), unroll=True) / rows

    def square(i, total):
        cen = sp_ref[i] - mean
        return total + jnp.sum(cen * cen, axis=0, keepdims=True)

    var = lax.fori_loop(0, side, square, jnp.zeros((1, hc), F32), unroll=True) / rows
    rs = lax.rsqrt(var + eps)
    rs_ref[...] = rs
    gain, bias = vec_ref[0:1, :], vec_ref[1:2, :]

    def act(i, carry):
        xhat = (sp_ref[i] - mean) * rs
        xhat_ref[i] = xhat
        v = xhat * gain + bias
        v = v * jax.nn.sigmoid(v)
        sp_ref[i] = v
        hid_ref[chunk(i, plane), :] = v.astype(BF)
        return carry

    lax.fori_loop(0, side, act, 0, unroll=True)
    late = [
        pltpu.make_async_copy(hid_ref, hid_out, sems.at[2]),
        pltpu.make_async_copy(xhat_ref, xhat_out, sems.at[3]),
    ]
    for copy in late:
        copy.start()
    low = lax.broadcasted_iota(jnp.int32, (step, 128), 1) < 64

    def temporal(k, carry):
        pieces = []
        for kk in (k, k + side):
            par = lax.rem(kk, 2)
            h = sp_ref[kk // 2, pl.ds(pl.multiple_of(par * step, 8), step), :]
            at = pl.multiple_of(par * (step % nf), 8)
            pieces.append((
                (pltpu.roll(h, 1, 0) * before_ref[pl.ds(at, step), :]).astype(BF),
                h.astype(BF),
                (pltpu.roll(h, step - 1, 0) * after_ref[pl.ds(at, step), :]).astype(BF),
            ))
        part = sum(
            nn(jnp.concatenate([x, y], axis=0), ltm_ref[t * hc : (t + 1) * hc])
            for t, (x, y) in enumerate(zip(*pieces))
        )
        store_packed(rank, mate_ref, keep_ref, part, k, step, low)
        return carry

    lax.fori_loop(0, side, temporal, 0, unroll=True)
    for copy in [pad_copy] + late:
        copy.wait()


def conv_forward(rank, g, kn, lt, vec, before, after, side, pixels, ch, deps=()):
    hc = vec.shape[1]
    plane = pixels // side
    nf = plane // side
    n = len(g)
    shapes = [
        ((side + 2, plane + 2 * nf, ch), BF),
        ((pixels, hc), BF),
        ((side, plane, hc), F32),
    ]
    outs = [jax.ShapeDtypeStruct(*s) for s in shapes] + [
        jax.ShapeDtypeStruct((1, hc), F32),
        jax.ShapeDtypeStruct((4, pixels // 2, 128), BF),
        jax.ShapeDtypeStruct((4, pixels // 2, 128), BF),
    ]
    scratch = [pltpu.VMEM(*s) for s in shapes] + [
        pltpu.VMEM((side, plane, hc), F32),
        pltpu.VMEM((9, ch, hc), BF),
        pltpu.SemaphoreType.DMA((4,)),
    ]
    flops = 2 * pixels * hc * 12 * ch
    return call(functools.partial(conv_body, side, n == 1), outs, scratch, flops,
                rank, *g, kn, lt, vec, before, after,
                deps=deps, far=(n + 1,), far_outs=(0, 1, 2))


def fold(v):
    return v + pltpu.roll(v, 64, 1)


def total_of(refs):
    t = refs[0][...].astype(F32)
    for ref in refs[1:]:
        t += ref[...].astype(F32)
    return t


def pair_sum_body(keep_ref, mate_ref, *out_refs):
    for p, ref in enumerate(out_refs):
        ref[...] = (keep_ref[p].astype(F32) + mate_ref[p].astype(F32)).astype(ref.dtype)


def pair_sum(keep, arrived, deps=()):
    shape = keep.shape[1:]
    outs = [jax.ShapeDtypeStruct(shape, BF)] * keep.shape[0]
    return call(pair_sum_body, outs, [], keep.size, keep, arrived, deps=deps)


def out_norm_body(n, has_skip, *refs):
    parts, refs = refs[:n], refs[n:]
    if has_skip:
        vec_ref, skip_ref, xhat_ref, rs_ref, pre_ref, res_ref = refs
    else:
        vec_ref, xhat_ref, rs_ref, pre_ref, res_ref = refs
    t = total_of(parts)
    pixels = 2 * t.shape[0]
    mean = fold(jnp.sum(t, axis=0, keepdims=True)) / pixels
    cen = t - mean
    rs = lax.rsqrt(fold(jnp.sum(cen * cen, axis=0, keepdims=True)) / pixels + eps)
    xhat = cen * rs
    pre = xhat * vec_ref[0:1, :] + vec_ref[1:2, :]
    if has_skip:
        pre = pre + skip_ref[...].astype(F32)
    xhat_ref[...] = xhat
    rs_ref[...] = rs
    pre_ref[...] = pre
    res_ref[...] = (pre * jax.nn.sigmoid(pre)).astype(BF)


def out_norm(parts, vec, skip, deps=()):
    half = parts[0].shape[0]
    outs = [
        jax.ShapeDtypeStruct((half, 128), F32),
        jax.ShapeDtypeStruct((1, 128), F32),
        jax.ShapeDtypeStruct((half, 128), F32),
        jax.ShapeDtypeStruct((half, 128), BF),
    ]
    args = (*parts, vec) + (() if skip is None else (skip,))
    body = functools.partial(out_norm_body, len(parts), skip is not None)
    return call(body, outs, [], half * 128 * 10, *args, deps=deps)


def out_back_body(n, *refs):
    parts, (pre_ref, xhat_ref, rs_ref, vec_ref, dpre_ref, dt_ref, sums_ref) = refs[:n], refs[n:]
    g = total_of(parts)
    pre, xhat = pre_ref[...], xhat_ref[...]
    sig = jax.nn.sigmoid(pre)
    dpre = g * (sig * (1.0 + pre * (1.0 - sig)))
    pixels = 2 * pre.shape[0]
    sb = fold(jnp.sum(dpre, axis=0, keepdims=True))
    sg = fold(jnp.sum(dpre * xhat, axis=0, keepdims=True))
    dpre_ref[...] = dpre.astype(BF)
    scale = vec_ref[0:1, :] * rs_ref[...]
    dt_ref[...] = (scale * (dpre - sb / pixels - xhat * (sg / pixels))).astype(BF)
    sums_ref[0:1, :] = sg
    sums_ref[1:2, :] = sb


def out_back(parts, pre, xhat, rs, vec, deps=()):
    half = pre.shape[0]
    outs = [
        jax.ShapeDtypeStruct((half, 128), BF),
        jax.ShapeDtypeStruct((half, 128), BF),
        jax.ShapeDtypeStruct((2, 128), F32),
    ]
    args = (*parts, pre, xhat, rs, vec)
    return call(functools.partial(out_back_body, len(parts)), outs, [], half * 1280, *args, deps=deps)


def conv_back_body(side, rank_ref, *refs):
    slices, (xhat_in, rs_ref, w_ref, lnt_ref, vec_ref, before_ref, after_ref,
             dt_out, ds_out, sums_ref, mate_ref, keep_ref,
             dt_ref, ds_ref, xhat_ref, dy_ref, pad_ref, ktm_ref, sems) = refs[:8], refs[8:]
    half = slices[0].shape[0]
    rank = rank_ref[0]
    nz, _, width = w_ref.shape
    rows = 2 * half
    plane = rows // side
    nf = plane // side
    step = plane // 2
    hc = ds_ref.shape[1]
    ch = dt_ref.shape[1]
    fetched = [
        pltpu.make_async_copy(
            w_ref.at[z, pl.ds(0, hc)], ktm_ref.at[:, pl.ds(z * width, width)], sems.at[z])
        for z in range(nz)
    ]
    xhat_copy = pltpu.make_async_copy(xhat_in, xhat_ref, sems.at[nz])
    for copy in fetched + [xhat_copy]:
        copy.start()
    clear_borders(pad_ref, side, plane, nf)

    def place(k, carry):
        for q, odd, a_ref, b_ref in by_rank(slices, rank):
            top, bottom = halves(odd, a_ref[chunk(k, step), :], b_ref[chunk(k, step), :])
            lanes = pl.ds(pl.multiple_of(128 * q, 128), 128)
            dt_ref[chunk(k, step), lanes] = top.astype(BF)
            dt_ref[pl.ds(pl.multiple_of(half + k * step, 16), step), lanes] = bottom.astype(BF)
        return carry

    lax.fori_loop(0, side, place, 0, unroll=True)
    dt_copy = pltpu.make_async_copy(dt_ref, dt_out, sems.at[nz + 1])
    dt_copy.start()
    xhat_copy.wait()
    gain, bias = vec_ref[0:1, :], vec_ref[1:2, :]

    def hidden_grad(i, sums):
        dt = dt_ref[chunk(i, plane), :]
        early = nn(dt, lnt_ref[0]) * before_ref[0:plane, :]
        late = nn(dt, lnt_ref[2]) * after_ref[0:plane, :]
        dh = nn(dt, lnt_ref[1]) + pltpu.roll(early, plane - 1, 0) + pltpu.roll(late, 1, 0)
        xhat = xhat_ref[i]
        v = xhat * gain + bias
        sig = jax.nn.sigmoid(v)
        dy = dh * (sig * (1.0 + v * (1.0 - sig)))
        dy_ref[i] = dy
        return (
            sums[0] + jnp.sum(dy * xhat, axis=0, keepdims=True),
            sums[1] + jnp.sum(dy, axis=0, keepdims=True),
        )

    zero = jnp.zeros((1, hc), F32)
    sg, sb = lax.fori_loop(0, side, hidden_grad, (zero, zero), unroll=True)
    sums_ref[0:1, :] = sg
    sums_ref[1:2, :] = sb
    scale = gain * rs_ref[...]

    def spatial_grad(i, carry):
        ds = (scale * (dy_ref[i] - sb / rows - xhat_ref[i] * (sg / rows))).astype(BF)
        pad_ref[i + 1, nf : nf + plane] = ds
        ds_ref[chunk(i, plane), :] = ds
        return carry

    lax.fori_loop(0, side, spatial_grad, 0, unroll=True)
    ds_copy = pltpu.make_async_copy(ds_ref, ds_out, sems.at[nz + 2])
    ds_copy.start()
    for copy in fetched:
        copy.wait()
    low = lax.broadcasted_iota(jnp.int32, (step, 128), 1) < 64

    def back(k, carry):
        acc = jnp.zeros((2 * step, ch), F32)
        for t in range(9):
            r, c = 2 - t // 3, 2 - t % 3
            pieces = []
            for kk in (k, k + side):
                at = c * nf + lax.rem(kk, 2) * step
                pieces.append(pad_ref[kk // 2 + r, pl.ds(pl.multiple_of(at, 16), step), :])
            acc += nn(jnp.concatenate(pieces, axis=0), ktm_ref[:, t * ch : (t + 1) * ch])
        store_packed(rank, mate_ref, keep_ref, acc, k, step, low)
        return carry

    lax.fori_loop(0, side, back, 0, unroll=True)
    dt_copy.wait()
    ds_copy.wait()


def conv_back(rank, g, xhat, rs, w, lnt, vec, before, after, side, deps=()):
    half = g[0].shape[0]
    hc = vec.shape[1]
    ch = len(g) * 64
    pixels = 2 * half
    plane = pixels // side
    nf = plane // side
    outs = [
        jax.ShapeDtypeStruct((pixels, ch), BF),
        jax.ShapeDtypeStruct((pixels, hc), BF),
        jax.ShapeDtypeStruct((2, hc), F32),
        jax.ShapeDtypeStruct((4, half, 128), BF),
        jax.ShapeDtypeStruct((4, half, 128), BF),
    ]
    scratch = [
        pltpu.VMEM((pixels, ch), BF),
        pltpu.VMEM((pixels, hc), BF),
        pltpu.VMEM((side, plane, hc), F32),
        pltpu.VMEM((side, plane, hc), F32),
        pltpu.VMEM((side + 2, plane + 2 * nf, hc), BF),
        pltpu.VMEM((hc, 9 * ch), BF),
        pltpu.SemaphoreType.DMA((w.shape[0] + 3,)),
    ]
    flops = 2 * pixels * hc * 12 * ch
    return call(functools.partial(conv_back_body, side), outs, scratch, flops,
                rank, *g, xhat, rs, w, lnt, vec, before, after,
                deps=deps, far=(9, 11), far_outs=(0, 1))


def grads_body(side, pad_ref, hid_ref, ds_ref, dt_ref, before_ref, after_ref, mid_ref, out_ref,
               sg_ref, dst_ref, taps_ref, tg_ref, vec_ref):
    ch = pad_ref.shape[2]
    hc = hid_ref.shape[1]
    plane = hid_ref.shape[0] // side
    nf = plane // side
    for i in (0, 1, side + 2, side + 3):
        dst_ref[i] = jnp.zeros(dst_ref.shape[1:], BF)
    for i in range(side):
        at = slice(i * plane, (i + 1) * plane)
        h = hid_ref[at, :].astype(F32)
        taps_ref[i, 0:hc] = (pltpu.roll(h, 1, 0) * before_ref[0:plane, :]).T.astype(BF)
        taps_ref[i, hc : 2 * hc] = h.T.astype(BF)
        taps_ref[i, 2 * hc : 3 * hc] = (pltpu.roll(h, plane - 1, 0) * after_ref[0:plane, :]).T.astype(BF)
        dst_ref[i + 2] = ds_ref[at, :].astype(F32).T.astype(BF)
    tg_ref[0 : 3 * hc, :] = sum(
        nn(taps_ref[i], dt_ref[i * plane : (i + 1) * plane, :]) for i in range(side)
    )
    tg_ref[3 * hc :, :] = jnp.zeros((tg_ref.shape[0] - 3 * hc, ch), F32)
    nz, _, width = sg_ref.shape
    size = 3 * hc // (2 * nz)
    vec_ref[...] = jnp.zeros(vec_ref.shape, F32)
    vec_ref[size : size + 2, 0:hc] = mid_ref[...]
    vec_ref[size + 2 : size + 4, 0:128] = out_ref[...]
    tall = vec_ref.shape[0]
    inside = lax.broadcasted_iota(jnp.int32, (tall, ch), 0) < size
    off = (width // 2) % 128
    for z in range(nz):
        first, second = [
            jnp.where(inside, tg_ref[b * size : b * size + tall, :], vec_ref[...])
            for b in (2 * z, 2 * z + 1)
        ]
        start = width // 2 - off
        sg_ref[z, hc : hc + tall, 0:ch] = first.astype(BF)
        second = pltpu.roll(jnp.concatenate([second, jnp.zeros((tall, 128), F32)], axis=1), off, 1)
        sg_ref[z, hc : hc + tall, start : start + ch + 128] = second.astype(BF)
    for c in range(3):
        acc = sum(
            nn(dst_ref[i : i + 3].reshape(3 * hc, plane), pad_ref[i, c * nf : c * nf + plane, :])
            for i in range(1, side + 1)
        )
        for r in range(3):
            first = (3 * r + c) * ch
            end = first + ch
            at = (2 - r) * hc
            done = 0
            while first < end:
                z = first // width
                last = min(end, (z + 1) * width)
                sg_ref[z, 0:hc, first - z * width : last - z * width] = (
                    acc[at : at + hc, done : done + last - first].astype(BF)
                )
                done += last - first
                first = last


def kernel_grads(pad, hidden, ds, dt, before, after, mid, out, side, shape, deps=()):
    pixels, hc = hidden.shape
    ch = dt.shape[1]
    plane = pixels // side
    outs = [jax.ShapeDtypeStruct(shape, BF)]
    tall = shape[1] - hc
    scratch = [
        pltpu.VMEM((side + 4, hc, plane), BF),
        pltpu.VMEM((side, 3 * hc, plane), BF),
        pltpu.VMEM((3 * hc + tall, ch), F32),
        pltpu.VMEM((tall, ch), F32),
    ]
    flops = 2 * pixels * hc * 12 * ch
    return call(functools.partial(grads_body, side), outs, scratch, flops,
                pad, hidden, ds, dt, before, after, mid, out, deps=deps)[0]


def copy_after_body(v_ref, out_ref):
    out_ref[...] = v_ref[...]


def after_all(v, *deps):
    return call(copy_after_body, [jax.ShapeDtypeStruct(v.shape, v.dtype)], [], v.size, v, deps=deps)[0]


def pack_kernels_body(kt_ref, lt_ref, vec_ref, out_ref, low_ref):
    ranks, _, width = out_ref.shape
    hc = kt_ref.shape[0] // ranks
    blocks = lt_ref.shape[0] // hc
    q = hc // ranks
    low_ref[...] = jnp.zeros(low_ref.shape, F32)
    for r in range(ranks):
        out_ref[r, 0:hc, :] = kt_ref[r * hc : (r + 1) * hc, :]
        for b in range(blocks):
            low_ref[r, b * q : (b + 1) * q, 0 : lt_ref.shape[1]] = (
                lt_ref[b * hc + r * q : b * hc + (r + 1) * q, :]
            )
        low_ref[r, blocks * q : blocks * q + 1, :] = vec_ref[...]
        out_ref[r, hc:, :] = low_ref[r].astype(BF)


def pack_kernels(kt, lt, vec, ranks, tall, deps):
    width = kt.shape[1]
    outs = [jax.ShapeDtypeStruct((ranks, kt.shape[0] // ranks + tall, width), BF)]
    scratch = [pltpu.VMEM((ranks, tall, width), F32)]
    return call(pack_kernels_body, outs, scratch, kt.size * 8, kt, lt, vec, deps=deps)[0]


def call(body, outs, scratch, flops, *args, deps=(), far=(), far_outs=()):
    moved = sum(a.size * a.dtype.itemsize for a in args) + sum(
        o.size * o.dtype.itemsize for o in outs
    )
    n = len(deps)

    def spec(a):
        return pl.BlockSpec(memory_space=pltpu.SMEM if a.dtype == jnp.int32 else pltpu.VMEM)

    return pl.pallas_call(
        lambda *refs: body(*refs[n:]),
        out_shape=outs,
        in_specs=[ANY] * n + [ANY if i in far else spec(a) for i, a in enumerate(args)],
        out_specs=[ANY if i in far_outs else spec(o) for i, o in enumerate(outs)],
        scratch_shapes=scratch,
        compiler_params=pltpu.CompilerParams(vmem_limit_bytes=VMEM_CAP),
        cost_estimate=pl.CostEstimate(flops=flops, bytes_accessed=moved, transcendentals=0),
    )(*deps, *args)


def chunk(i, size):
    return pl.ds(pl.multiple_of(i * size, 16), size)


def clear_borders(pad_ref, side, plane, nf):
    zrow = jnp.zeros(pad_ref.shape[1:], BF)
    pad_ref[0] = zrow
    pad_ref[side + 1] = zrow
    zcol = jnp.zeros((nf, pad_ref.shape[2]), BF)
    for i in range(side):
        pad_ref[i + 1, 0:nf] = zcol
        pad_ref[i + 1, nf + plane : 2 * nf + plane] = zcol


def by_rank(slices, rank):
    odd = lax.rem(rank, 2) == 1
    for p in range(len(slices) // 2):
        a, b = slices[2 * p], slices[2 * p + 1]
        yield lax.bitwise_xor(rank // 2, p), odd, a, b


def halves(odd, own, mate):
    low = lax.broadcasted_iota(jnp.int32, own.shape, 1) < 64
    own, mate = own.astype(F32), mate.astype(F32)
    a, b = jnp.where(odd, mate, own), jnp.where(odd, own, mate)
    top = jnp.where(low, a, pltpu.roll(b, 64, 1))
    bottom = jnp.where(low, pltpu.roll(a, 64, 1), b)
    return top, bottom


def store_packed(rank, mate_ref, keep_ref, part, k, step, low):
    rows_now = chunk(k, step)
    odd = lax.rem(rank, 2) == 1
    for q in range(keep_ref.shape[0]):
        x = part[:step, 128 * q : 128 * q + 128]
        y = part[step:, 128 * q : 128 * q + 128]
        even_slice = jnp.where(low, x, pltpu.roll(y, 64, 1))
        odd_slice = jnp.where(low, pltpu.roll(x, 64, 1), y)
        p = lax.bitwise_xor(rank // 2, q)
        keep_ref[p, rows_now, :] = jnp.where(odd, odd_slice, even_slice).astype(BF)
        mate_ref[p, rows_now, :] = jnp.where(odd, even_slice, odd_slice).astype(BF)


def fetch_kernels(w_ref, ktm_ref, lw_ref, sems):
    nz, _, width = w_ref.shape
    hc = ktm_ref.shape[0]
    copies = []
    for z in range(nz):
        copies.append(pltpu.make_async_copy(
            w_ref.at[z, pl.ds(0, hc)], ktm_ref.at[:, pl.ds(z * width, width)], sems.at[2 * z]))
        copies.append(pltpu.make_async_copy(
            w_ref.at[z, pl.ds(hc, lw_ref.shape[1])], lw_ref.at[z], sems.at[2 * z + 1]))
    for copy in copies:
        copy.start()
    return copies


def join_temporal(lw_ref, lf_ref, ltm_ref):
    ch = ltm_ref.shape[1]
    width = lw_ref.shape[2] // 2
    count = 2 * lw_ref.shape[0]
    size = ltm_ref.shape[0] // count
    for z in range(lw_ref.shape[0]):
        first = lw_ref[z, :, 0:ch].astype(F32)
        off = width % 128
        second = lw_ref[z, :, width - off : width - off + ch + 128].astype(F32)
        second = pltpu.roll(second, ch + 128 - off, 1)[:, 0:ch]
        for b, block in ((2 * z, first), (2 * z + 1, second)):
            lf_ref[b * size : b * size + block.shape[0], :] = block
    ltm_ref[...] = lf_ref[0 : ltm_ref.shape[0], :].astype(BF)


def prepare_body(w_ref, kn_out, l_out, lt_out, ktm_ref, lw_ref, lf_ref, sems):
    hc, ch = ktm_ref.shape[0], l_out.shape[1]
    for copy in fetch_kernels(w_ref, ktm_ref, lw_ref, sems):
        copy.wait()
    for t in range(9):
        kn_out[t] = ktm_ref[:, t * ch : (t + 1) * ch].astype(F32).T.astype(BF)
    join_temporal(lw_ref, lf_ref, l_out)
    for t in range(3):
        lt_out[t] = lf_ref[t * hc : (t + 1) * hc].T.astype(BF)


def prepare(w, hc, ch, deps=()):
    outs = [
        jax.ShapeDtypeStruct((9, ch, hc), BF),
        jax.ShapeDtypeStruct((3 * hc, ch), BF),
        jax.ShapeDtypeStruct((3, ch, hc), BF),
    ]
    tall = w.shape[1] - hc
    scratch = [
        pltpu.VMEM((hc, 9 * ch), BF),
        pltpu.VMEM((w.shape[0], tall, w.shape[2]), BF),
        pltpu.VMEM((3 * hc + tall, ch), F32),
        pltpu.SemaphoreType.DMA((2 * w.shape[0],)),
    ]
    return call(prepare_body, outs, scratch, 2 * w.size * 512, w, deps=deps, far=(0,))


def conv_body(side, first, rank_ref, *refs):
    n = 1 if first else 8
    slices = refs[:n]
    (kn_in, ltm_ref, vec_ref, before_ref, after_ref,
     pad_out, hid_out, xhat_out, rs_ref, mate_ref, keep_ref,
     pad_ref, hid_ref, xhat_ref, sp_ref, kn_ref, sems) = refs[n:]
    rank = rank_ref[0]
    kn_copy = pltpu.make_async_copy(kn_in, kn_ref, sems.at[0])
    kn_copy.start()
    ch, hc = pad_ref.shape[2], hid_ref.shape[1]
    rows = hid_ref.shape[0]
    plane = rows // side
    nf = plane // side
    step = plane // 2
    clear_borders(pad_ref, side, plane, nf)
    if first:
        for i in range(side):
            pad_ref[i + 1, nf : nf + plane] = slices[0][i * plane : (i + 1) * plane]
    else:
        def place(k, carry):
            for q, odd, a_ref, b_ref in by_rank(slices, rank):
                top, bottom = halves(odd, a_ref[chunk(k, step), :], b_ref[chunk(k, step), :])
                lanes = pl.ds(pl.multiple_of(128 * q, 128), 128)
                for piece, kk in ((top, k), (bottom, k + side)):
                    at = nf + lax.rem(kk, 2) * step
                    pad_ref[1 + kk // 2, pl.ds(pl.multiple_of(at, 16), step), lanes] = piece.astype(BF)
            return carry

        lax.fori_loop(0, side, place, 0, unroll=True)
    pad_copy = pltpu.make_async_copy(pad_ref, pad_out, sems.at[1])
    pad_copy.start()
    kn_copy.wait()

    def conv(i, total):
        acc = jnp.zeros((plane, hc), F32)
        for t in range(9):
            r, c = t // 3, t % 3
            acc += nn(pad_ref[i + r, c * nf : c * nf + plane, :], kn_ref[t])
        sp_ref[i] = acc
        return total + jnp.sum(acc, axis=0, keepdims=True)

    mean = lax.fori_loop(0, side, conv, jnp.zeros((1, hc), F32), unroll=True) / rows

    def square(i, total):
        cen = sp_ref[i] - mean
        return total + jnp.sum(cen * cen, axis=0, keepdims=True)

    var = lax.fori_loop(0, side, square, jnp.zeros((1, hc), F32), unroll=True) / rows
    rs = lax.rsqrt(var + eps)
    rs_ref[...] = rs
    gain, bias = vec_ref[0:1, :], vec_ref[1:2, :]

    def act(i, carry):
        xhat = (sp_ref[i] - mean) * rs
        xhat_ref[i] = xhat
        v = xhat * gain + bias
        v = v * jax.nn.sigmoid(v)
        sp_ref[i] = v
        hid_ref[chunk(i, plane), :] = v.astype(BF)
        return carry

    lax.fori_loop(0, side, act, 0, unroll=True)
    late = [
        pltpu.make_async_copy(hid_ref, hid_out, sems.at[2]),
        pltpu.make_async_copy(xhat_ref, xhat_out, sems.at[3]),
    ]
    for copy in late:
        copy.start()
    low = lax.broadcasted_iota(jnp.int32, (step, 128), 1) < 64

    def temporal(k, carry):
        pieces = []
        for kk in (k, k + side):
            par = lax.rem(kk, 2)
            h = sp_ref[kk // 2, pl.ds(pl.multiple_of(par * step, 8), step), :]
            at = pl.multiple_of(par * (step % nf), 8)
            pieces.append((
                (pltpu.roll(h, 1, 0) * before_ref[pl.ds(at, step), :]).astype(BF),
                h.astype(BF),
                (pltpu.roll(h, step - 1, 0) * after_ref[pl.ds(at, step), :]).astype(BF),
            ))
        part = sum(
            nn(jnp.concatenate([x, y], axis=0), ltm_ref[t * hc : (t + 1) * hc])
            for t, (x, y) in enumerate(zip(*pieces))
        )
        store_packed(rank, mate_ref, keep_ref, part, k, step, low)
        return carry

    lax.fori_loop(0, side, temporal, 0, unroll=True)
    for copy in [pad_copy] + late:
        copy.wait()


def conv_forward(rank, g, kn, lt, vec, before, after, side, pixels, ch, deps=()):
    hc = vec.shape[1]
    plane = pixels // side
    nf = plane // side
    n = len(g)
    shapes = [
        ((side + 2, plane + 2 * nf, ch), BF),
        ((pixels, hc), BF),
        ((side, plane, hc), F32),
    ]
    outs = [jax.ShapeDtypeStruct(*s) for s in shapes] + [
        jax.ShapeDtypeStruct((1, hc), F32),
        jax.ShapeDtypeStruct((4, pixels // 2, 128), BF),
        jax.ShapeDtypeStruct((4, pixels // 2, 128), BF),
    ]
    scratch = [pltpu.VMEM(*s) for s in shapes] + [
        pltpu.VMEM((side, plane, hc), F32),
        pltpu.VMEM((9, ch, hc), BF),
        pltpu.SemaphoreType.DMA((4,)),
    ]
    flops = 2 * pixels * hc * 12 * ch
    return call(functools.partial(conv_body, side, n == 1), outs, scratch, flops,
                rank, *g, kn, lt, vec, before, after,
                deps=deps, far=(n + 1,), far_outs=(0, 1, 2))


def fold(v):
    return v + pltpu.roll(v, 64, 1)


def total_of(refs):
    t = refs[0][...].astype(F32)
    for ref in refs[1:]:
        t += ref[...].astype(F32)
    return t


def pair_sum_body(keep_ref, mate_ref, *out_refs):
    for p, ref in enumerate(out_refs):
        ref[...] = (keep_ref[p].astype(F32) + mate_ref[p].astype(F32)).astype(ref.dtype)


def pair_sum(keep, arrived, deps=()):
    shape = keep.shape[1:]
    outs = [jax.ShapeDtypeStruct(shape, BF)] * keep.shape[0]
    return call(pair_sum_body, outs, [], keep.size, keep, arrived, deps=deps)


def out_norm_body(n, has_skip, *refs):
    parts, refs = refs[:n], refs[n:]
    if has_skip:
        vec_ref, skip_ref, xhat_ref, rs_ref, pre_ref, res_ref = refs
    else:
        vec_ref, xhat_ref, rs_ref, pre_ref, res_ref = refs
    t = total_of(parts)
    pixels = 2 * t.shape[0]
    mean = fold(jnp.sum(t, axis=0, keepdims=True)) / pixels
    cen = t - mean
    rs = lax.rsqrt(fold(jnp.sum(cen * cen, axis=0, keepdims=True)) / pixels + eps)
    xhat = cen * rs
    pre = xhat * vec_ref[0:1, :] + vec_ref[1:2, :]
    if has_skip:
        pre = pre + skip_ref[...].astype(F32)
    xhat_ref[...] = xhat
    rs_ref[...] = rs
    pre_ref[...] = pre
    res_ref[...] = (pre * jax.nn.sigmoid(pre)).astype(BF)


def out_norm(parts, vec, skip, deps=()):
    half = parts[0].shape[0]
    outs = [
        jax.ShapeDtypeStruct((half, 128), F32),
        jax.ShapeDtypeStruct((1, 128), F32),
        jax.ShapeDtypeStruct((half, 128), F32),
        jax.ShapeDtypeStruct((half, 128), BF),
    ]
    args = (*parts, vec) + (() if skip is None else (skip,))
    body = functools.partial(out_norm_body, len(parts), skip is not None)
    return call(body, outs, [], half * 128 * 10, *args, deps=deps)


def out_back_body(n, *refs):
    parts, (pre_ref, xhat_ref, rs_ref, vec_ref, dpre_ref, dt_ref, sums_ref) = refs[:n], refs[n:]
    g = total_of(parts)
    pre, xhat = pre_ref[...], xhat_ref[...]
    sig = jax.nn.sigmoid(pre)
    dpre = g * (sig * (1.0 + pre * (1.0 - sig)))
    pixels = 2 * pre.shape[0]
    sb = fold(jnp.sum(dpre, axis=0, keepdims=True))
    sg = fold(jnp.sum(dpre * xhat, axis=0, keepdims=True))
    dpre_ref[...] = dpre.astype(BF)
    scale = vec_ref[0:1, :] * rs_ref[...]
    dt_ref[...] = (scale * (dpre - sb / pixels - xhat * (sg / pixels))).astype(BF)
    sums_ref[0:1, :] = sg
    sums_ref[1:2, :] = sb


def out_back(parts, pre, xhat, rs, vec, deps=()):
    half = pre.shape[0]
    outs = [
        jax.ShapeDtypeStruct((half, 128), BF),
        jax.ShapeDtypeStruct((half, 128), BF),
        jax.ShapeDtypeStruct((2, 128), F32),
    ]
    args = (*parts, pre, xhat, rs, vec)
    return call(functools.partial(out_back_body, len(parts)), outs, [], half * 1280, *args, deps=deps)


def conv_back_body(side, rank_ref, *refs):
    slices, (xhat_in, rs_ref, w_ref, lnt_ref, vec_ref, before_ref, after_ref,
             dt_out, ds_out, sums_ref, mate_ref, keep_ref,
             dt_ref, ds_ref, xhat_ref, dy_ref, pad_ref, ktm_ref, sems) = refs[:8], refs[8:]
    half = slices[0].shape[0]
    rank = rank_ref[0]
    nz, _, width = w_ref.shape
    rows = 2 * half
    plane = rows // side
    nf = plane // side
    step = plane // 2
    hc = ds_ref.shape[1]
    ch = dt_ref.shape[1]
    fetched = [
        pltpu.make_async_copy(
            w_ref.at[z, pl.ds(0, hc)], ktm_ref.at[:, pl.ds(z * width, width)], sems.at[z])
        for z in range(nz)
    ]
    xhat_copy = pltpu.make_async_copy(xhat_in, xhat_ref, sems.at[nz])
    for copy in fetched + [xhat_copy]:
        copy.start()
    clear_borders(pad_ref, side, plane, nf)

    def place(k, carry):
        for q, odd, a_ref, b_ref in by_rank(slices, rank):
            top, bottom = halves(odd, a_ref[chunk(k, step), :], b_ref[chunk(k, step), :])
            lanes = pl.ds(pl.multiple_of(128 * q, 128), 128)
            dt_ref[chunk(k, step), lanes] = top.astype(BF)
            dt_ref[pl.ds(pl.multiple_of(half + k * step, 16), step), lanes] = bottom.astype(BF)
        return carry

    lax.fori_loop(0, side, place, 0, unroll=True)
    dt_copy = pltpu.make_async_copy(dt_ref, dt_out, sems.at[nz + 1])
    dt_copy.start()
    xhat_copy.wait()
    gain, bias = vec_ref[0:1, :], vec_ref[1:2, :]

    def hidden_grad(i, sums):
        dt = dt_ref[chunk(i, plane), :]
        early = nn(dt, lnt_ref[0]) * before_ref[0:plane, :]
        late = nn(dt, lnt_ref[2]) * after_ref[0:plane, :]
        dh = nn(dt, lnt_ref[1]) + pltpu.roll(early, plane - 1, 0) + pltpu.roll(late, 1, 0)
        xhat = xhat_ref[i]
        v = xhat * gain + bias
        sig = jax.nn.sigmoid(v)
        dy = dh * (sig * (1.0 + v * (1.0 - sig)))
        dy_ref[i] = dy
        return (
            sums[0] + jnp.sum(dy * xhat, axis=0, keepdims=True),
            sums[1] + jnp.sum(dy, axis=0, keepdims=True),
        )

    zero = jnp.zeros((1, hc), F32)
    sg, sb = lax.fori_loop(0, side, hidden_grad, (zero, zero), unroll=True)
    sums_ref[0:1, :] = sg
    sums_ref[1:2, :] = sb
    scale = gain * rs_ref[...]

    def spatial_grad(i, carry):
        ds = (scale * (dy_ref[i] - sb / rows - xhat_ref[i] * (sg / rows))).astype(BF)
        pad_ref[i + 1, nf : nf + plane] = ds
        ds_ref[chunk(i, plane), :] = ds
        return carry

    lax.fori_loop(0, side, spatial_grad, 0, unroll=True)
    ds_copy = pltpu.make_async_copy(ds_ref, ds_out, sems.at[nz + 2])
    ds_copy.start()
    for copy in fetched:
        copy.wait()
    low = lax.broadcasted_iota(jnp.int32, (step, 128), 1) < 64

    def back(k, carry):
        acc = jnp.zeros((2 * step, ch), F32)
        for t in range(9):
            r, c = 2 - t // 3, 2 - t % 3
            pieces = []
            for kk in (k, k + side):
                at = c * nf + lax.rem(kk, 2) * step
                pieces.append(pad_ref[kk // 2 + r, pl.ds(pl.multiple_of(at, 16), step), :])
            acc += nn(jnp.concatenate(pieces, axis=0), ktm_ref[:, t * ch : (t + 1) * ch])
        store_packed(rank, mate_ref, keep_ref, acc, k, step, low)
        return carry

    lax.fori_loop(0, side, back, 0, unroll=True)
    dt_copy.wait()
    ds_copy.wait()


def conv_back(rank, g, xhat, rs, w, lnt, vec, before, after, side, deps=()):
    half = g[0].shape[0]
    hc = vec.shape[1]
    ch = len(g) * 64
    pixels = 2 * half
    plane = pixels // side
    nf = plane // side
    outs = [
        jax.ShapeDtypeStruct((pixels, ch), BF),
        jax.ShapeDtypeStruct((pixels, hc), BF),
        jax.ShapeDtypeStruct((2, hc), F32),
        jax.ShapeDtypeStruct((4, half, 128), BF),
        jax.ShapeDtypeStruct((4, half, 128), BF),
    ]
    scratch = [
        pltpu.VMEM((pixels, ch), BF),
        pltpu.VMEM((pixels, hc), BF),
        pltpu.VMEM((side, plane, hc), F32),
        pltpu.VMEM((side, plane, hc), F32),
        pltpu.VMEM((side + 2, plane + 2 * nf, hc), BF),
        pltpu.VMEM((hc, 9 * ch), BF),
        pltpu.SemaphoreType.DMA((w.shape[0] + 3,)),
    ]
    flops = 2 * pixels * hc * 12 * ch
    return call(functools.partial(conv_back_body, side), outs, scratch, flops,
                rank, *g, xhat, rs, w, lnt, vec, before, after,
                deps=deps, far=(9, 11), far_outs=(0, 1))


def grads_body(side, pad_ref, hid_ref, ds_ref, dt_ref, before_ref, after_ref, mid_ref, out_ref,
               sg_ref, dst_ref, taps_ref, tg_ref, vec_ref):
    ch = pad_ref.shape[2]
    hc = hid_ref.shape[1]
    plane = hid_ref.shape[0] // side
    nf = plane // side
    for i in (0, 1, side + 2, side + 3):
        dst_ref[i] = jnp.zeros(dst_ref.shape[1:], BF)
    for i in range(side):
        at = slice(i * plane, (i + 1) * plane)
        h = hid_ref[at, :].astype(F32)
        taps_ref[i, 0:hc] = (pltpu.roll(h, 1, 0) * before_ref[0:plane, :]).T.astype(BF)
        taps_ref[i, hc : 2 * hc] = h.T.astype(BF)
        taps_ref[i, 2 * hc : 3 * hc] = (pltpu.roll(h, plane - 1, 0) * after_ref[0:plane, :]).T.astype(BF)
        dst_ref[i + 2] = ds_ref[at, :].astype(F32).T.astype(BF)
    tg_ref[0 : 3 * hc, :] = sum(
        nn(taps_ref[i], dt_ref[i * plane : (i + 1) * plane, :]) for i in range(side)
    )
    tg_ref[3 * hc :, :] = jnp.zeros((tg_ref.shape[0] - 3 * hc, ch), F32)
    nz, _, width = sg_ref.shape
    size = 3 * hc // (2 * nz)
    vec_ref[...] = jnp.zeros(vec_ref.shape, F32)
    vec_ref[size : size + 2, 0:hc] = mid_ref[...]
    vec_ref[size + 2 : size + 4, 0:128] = out_ref[...]
    tall = vec_ref.shape[0]
    inside = lax.broadcasted_iota(jnp.int32, (tall, ch), 0) < size
    off = (width // 2) % 128
    for z in range(nz):
        first, second = [
            jnp.where(inside, tg_ref[b * size : b * size + tall, :], vec_ref[...])
            for b in (2 * z, 2 * z + 1)
        ]
        start = width // 2 - off
        sg_ref[z, hc : hc + tall, 0:ch] = first.astype(BF)
        second = pltpu.roll(jnp.concatenate([second, jnp.zeros((tall, 128), F32)], axis=1), off, 1)
        sg_ref[z, hc : hc + tall, start : start + ch + 128] = second.astype(BF)
    for c in range(3):
        acc = sum(
            nn(dst_ref[i : i + 3].reshape(3 * hc, plane), pad_ref[i, c * nf : c * nf + plane, :])
            for i in range(1, side + 1)
        )
        for r in range(3):
            first = (3 * r + c) * ch
            end = first + ch
            at = (2 - r) * hc
            done = 0
            while first < end:
                z = first // width
                last = min(end, (z + 1) * width)
                sg_ref[z, 0:hc, first - z * width : last - z * width] = (
                    acc[at : at + hc, done : done + last - first].astype(BF)
                )
                done += last - first
                first = last


def kernel_grads(pad, hidden, ds, dt, before, after, mid, out, side, shape, deps=()):
    pixels, hc = hidden.shape
    ch = dt.shape[1]
    plane = pixels // side
    outs = [jax.ShapeDtypeStruct(shape, BF)]
    tall = shape[1] - hc
    scratch = [
        pltpu.VMEM((side + 4, hc, plane), BF),
        pltpu.VMEM((side, 3 * hc, plane), BF),
        pltpu.VMEM((3 * hc + tall, ch), F32),
        pltpu.VMEM((tall, ch), F32),
    ]
    flops = 2 * pixels * hc * 12 * ch
    return call(functools.partial(grads_body, side), outs, scratch, flops,
                pad, hidden, ds, dt, before, after, mid, out, deps=deps)[0]


def copy_after_body(v_ref, out_ref):
    out_ref[...] = v_ref[...]


def after_all(v, *deps):
    return call(copy_after_body, [jax.ShapeDtypeStruct(v.shape, v.dtype)], [], v.size, v, deps=deps)[0]


def pack_kernels_body(kt_ref, lt_ref, vec_ref, out_ref, low_ref):
    ranks, _, width = out_ref.shape
    hc = kt_ref.shape[0] // ranks
    blocks = lt_ref.shape[0] // hc
    q = hc // ranks
    low_ref[...] = jnp.zeros(low_ref.shape, F32)
    for r in range(ranks):
        out_ref[r, 0:hc, :] = kt_ref[r * hc : (r + 1) * hc, :]
        for b in range(blocks):
            low_ref[r, b * q : (b + 1) * q, 0 : lt_ref.shape[1]] = (
                lt_ref[b * hc + r * q : b * hc + (r + 1) * q, :]
            )
        low_ref[r, blocks * q : blocks * q + 1, :] = vec_ref[...]
        out_ref[r, hc:, :] = low_ref[r].astype(BF)


def pack_kernels(kt, lt, vec, ranks, tall, deps):
    width = kt.shape[1]
    outs = [jax.ShapeDtypeStruct((ranks, kt.shape[0] // ranks + tall, width), BF)]
    scratch = [pltpu.VMEM((ranks, tall, width), F32)]
    return call(pack_kernels_body, outs, scratch, kt.size * 8, kt, lt, vec, deps=deps)[0]


def hop(v, k):
    n = 1
    for name in EVERY:
        n *= lax.axis_size(name)
    return lax.ppermute(v, EVERY, [(i, i ^ k) for i in range(n)])


def plane_gather(v, aside=()):
    got = {0: v}
    for k in (6, 2, 4):
        got[k] = hop(v, k)
    got[1] = hop(after_all(v, *aside) if aside else v, 1)
    for k in (2, 4, 6):
        got[k ^ 1] = hop(got[k], 1)
    return [got[k] for k in range(8)]


def plane_reduce(mate, keep, deps=()):
    sums = pair_sum(keep, hop(mate, 1), deps)
    arrived = {k: hop(sums[k // 2], k) for k in (6, 2, 4)}
    return [sums[0], arrived[2], arrived[4], arrived[6]]


def on_device(frames, cot, starts, ks, ktm, mg, mb, og, ob):
    nz, n_rank, n_seg = lax.axis_size("z"), 8, 4
    n_dp = nz * 2
    fr, side, ch = frames.shape[0], frames.shape[1], frames.shape[3]
    area = side * side
    hid = ks.shape[2]
    hc, cc = hid // n_rank, ch // n_rank
    q = hc // n_rank
    rank = lax.axis_index(PLANE)
    rank_now = rank.astype(jnp.int32).reshape(1)
    d_index = lax.axis_index(("z", "y"))
    nf = n_dp * fr
    pixels = area * nf
    half = pixels // 2

    to_plane = [(d * n_seg + s, s * n_rank + d) for d in range(n_dp) for s in range(n_seg)]
    from_plane = [(b, a) for a, b in to_plane]
    rows = fr * area
    flag_row = jnp.pad(starts.astype(BF)[None], ((0, 11), (0, ch - fr)))
    moving = jnp.concatenate([frames.reshape(rows, ch), flag_row], axis=0)
    moving = lax.ppermute(moving, EVERY, to_plane)

    perm = (jnp.arange(hid).reshape(n_rank, n_rank, q).transpose(1, 0, 2).reshape(hid)[:, None]
            == jnp.arange(hid)[None, :]).astype(BF)
    kt = lax.dot_general(perm, ks[0].astype(BF), (((1,), (1,)), ((), ())),
                         preferred_element_type=F32).astype(BF)
    lrows, width = ktm.shape[1] // n_rank, ks.shape[1]
    tall = -(-(lrows + 4) // 16) * 16
    extra = jnp.concatenate([mg, mb, og, ob], axis=1)
    extra = jnp.pad(extra, ((0, 0), (0, width - extra.shape[1])))
    w = pack_kernels(kt, ktm[0], extra, n_rank, tall, deps=(moving,))
    w = lax.all_to_all(w, PLANE, 0, 0)
    here = w
    high = hc + tall

    w = w.reshape(2, n_seg, high, width).transpose(1, 2, 0, 3).reshape(n_seg, high, 2 * width)
    ws = [lax.all_gather(w[s], "z", axis=0) for s in range(n_seg)]

    moving = after_all(moving, here)
    gathered = lax.all_to_all(jnp.broadcast_to(moving, (n_rank, *moving.shape)), PLANE, 0, 0)
    mids, outs = [], []
    for s in range(n_seg):
        row = ws[s][:, hc + lrows].reshape(n_dp, width).astype(F32)
        mids.append(jnp.stack([
            lax.dynamic_slice_in_dim(row[:, i * hc : (i + 1) * hc], rank * q, q, axis=1).reshape(hc)
            for i in range(2)]))
        own = lax.dynamic_index_in_dim(row, rank, 0, keepdims=False)
        outs.append(jnp.stack([
            jnp.tile(own[2 * hc + i * cc : 2 * hc + (i + 1) * cc], 2) for i in range(2)]))

    def by_pixel(v):
        width = v.shape[2]
        v = v.reshape(n_rank * fr, area, width).transpose(1, 0, 2)
        return v.reshape(pixels, width)

    def packed(v):
        return jnp.concatenate([v[:half], v[half:]], axis=1)

    a0 = by_pixel(gathered[:, :rows])
    flags = gathered[:, rows, :fr].reshape(nf) > 0.5
    slot = jnp.arange(nf) % fr
    before = jnp.where(flags | (slot == 0), 0.0, 1.0)
    after = jnp.where(jnp.roll(flags, -1) | (slot == fr - 1), 0.0, 1.0)
    spread = (side * nf + nf, hc)
    before = jnp.broadcast_to(jnp.tile(before, side + 1)[:, None], spread)
    after = jnp.broadcast_to(jnp.tile(after, side + 1)[:, None], spread)
    skip = packed(lax.dynamic_slice_in_dim(a0, rank * cc, cc, axis=1))

    def to_frames(*slices):
        n = len(slices)
        v = jnp.stack([jnp.concatenate([v[:, :cc], v[:, cc:]], axis=0) for v in slices])
        v = v.reshape(n, area, n_rank, fr, cc).transpose(2, 0, 1, 3, 4).reshape(n_rank, n * rows, cc)
        v = lax.all_to_all(v, PLANE, 0, 0).transpose(1, 0, 2).reshape(n * rows, ch)
        v = lax.ppermute(v, EVERY, from_plane).reshape(n, area, fr, ch).transpose(0, 2, 1, 3)
        return v.reshape(n, *frames.shape)

    saved = []
    g = [a0]
    ready = prepare(ws[0], hc, ch)
    for s in range(n_seg):
        kn, lt, lnt = ready
        pad, hidden, xm, rm, mate, keep = conv_forward(
            rank_now, g, kn, lt, mids[s], before, after, side, pixels, ch)
        parts = plane_reduce(mate, keep)
        deps = ()
        if s == n_seg - 1:
            cot_own = lax.ppermute(after_all(cot.reshape(rows, ch), kn), EVERY, to_plane)
            cot_own = cot_own.reshape(rows, n_rank, cc).transpose(1, 0, 2)
            cot_own = packed(by_pixel(lax.all_to_all(cot_own, PLANE, 0, 0)))
            deps = (cot_own,)
        xo, ro, pre, res = out_norm(parts, outs[s], skip if s % 2 == 1 else None, deps=deps)
        saved.append((pad, hidden, xm, rm, xo, ro, pre, lnt))
        if s % 2 == 1:
            skip = res
        if s < n_seg - 1:
            ready = prepare(ws[s + 1], hc, ch, deps=(res,))
            g = plane_gather(res, ready[:1])

    parts = [cot_own]
    skip_grad = None

    def by_row(v):
        return v.reshape(high, 2, width).transpose(1, 0, 2)

    grads, raw = [], None
    for s in reversed(range(n_seg)):
        pad, hidden, xm, rm, xo, ro, pre, lnt = saved[s]
        if s == 1:
            parts = parts + [skip_grad]
        deps = () if raw is None else (raw, *grads[len(grads) - 1 :])
        dpre, dt, osum = out_back(parts, pre, xo, ro, outs[s], deps=deps)
        if raw is not None:
            grads.append(lax.psum_scatter(after_all(raw, dt), "z", scatter_dimension=0))
        if s % 2 == 1:
            skip_grad = dpre
        dtf, ds, msum, mate, keep = conv_back(
            rank_now, plane_gather(dt), xm, rm, ws[s], lnt, mids[s], before, after, side)
        if s > 0:
            parts = plane_reduce(mate, keep)
        raw = kernel_grads(pad, hidden, ds, dtf, before, after, msum, osum, side, ws[s].shape,
                           deps=parts[:1] if s > 0 else ())
    last = lax.psum_scatter(raw, "z", scatter_dimension=0)
    parts = plane_reduce(mate, keep, deps=(raw,))

    da = sum(p.astype(F32) for p in parts) + skip_grad.astype(F32)
    output, frames_grad = to_frames(res, da.astype(BF))
    frames_grad = frames_grad.astype(F32)

    grads = [by_row(v) for v in grads[::-1]]
    g = jnp.stack([by_row(last)] + grads, axis=1).reshape(n_rank, high, width)
    g = lax.all_to_all(g, PLANE, 0, 0)
    space_grad = lax.dot_general(g[:, :hc].reshape(hid, width), perm, (((0,), (0,)), ((), ())),
                                 preferred_element_type=F32)
    tg = g[:, hc : hc + lrows, :ch].reshape(n_rank, -1, q, ch)
    time_grad = tg.transpose(1, 0, 2, 3).reshape(-1, ch).astype(F32)
    sums = g[:, hc + lrows : hc + lrows + 4].astype(F32)

    def mid_own(v):
        return lax.dynamic_slice_in_dim(v[:, :hc], d_index * q, q, axis=1).reshape(1, hc)

    own = lax.dynamic_index_in_dim(sums, d_index, 0, keepdims=False)
    return (
        output,
        frames_grad,
        space_grad[None],
        time_grad[None],
        mid_own(sums[:, 0]),
        mid_own(sums[:, 1]),
        own[2:3, :cc],
        own[3:4, :cc],
    )


def from_behind(value, axis, steps):
    count = lax.axis_size(axis)
    leading, last = (max(0, -steps), min(count, count - steps))
    return lax.ppermute(value, axis, [(source, source + steps) for source in range(leading, last)])


def space_apply(current, kernel):
    frame_side = current.shape[1]
    padded = jnp.pad(current, ((0, 0), (1, 1), (1, 1), (0, 0)))
    stacked = jnp.concatenate(
        [
            padded[:, row_shift : row_shift + frame_side, col_shift : col_shift + frame_side, :]
            for row_shift in range(3)
            for col_shift in range(3)
        ],
        axis=-1,
    )
    return (
        stacked,
        jnp.einsum("fijc,co->fijo", stacked, kernel, preferred_element_type=jnp.float32),
    )


def space_back(gradient, kernel):
    frame_side = gradient.shape[1]
    channels = kernel.shape[0] // 9
    spread = jnp.einsum("fijo,co->fijc", gradient, kernel, preferred_element_type=jnp.float32)
    total = jnp.zeros((gradient.shape[0], frame_side + 2, frame_side + 2, channels), jnp.float32)
    for tap_index in range(9):
        row_shift = tap_index // 3
        col_shift = tap_index % 3
        piece_now = spread[..., tap_index * channels : (tap_index + 1) * channels]
        total = total + jnp.pad(
            piece_now, ((0, 0), (row_shift, 2 - row_shift), (col_shift, 2 - col_shift), (0, 0))
        )
    return total[:, 1 : frame_side + 1, 1 : frame_side + 1, :]


def time_apply(current, kernel, before_mask, after_mask):
    blanks = jnp.zeros_like(current[:1])
    earlier = jnp.concatenate([blanks, current[:-1]], axis=0) * before_mask[
        :, None, None, None
    ].astype(current.dtype)
    later = jnp.concatenate([current[1:], blanks], axis=0) * after_mask[:, None, None, None].astype(
        current.dtype
    )
    stacked = jnp.concatenate([earlier, current, later], axis=-1)
    return (
        stacked,
        jnp.einsum("fijc,co->fijo", stacked, kernel, preferred_element_type=jnp.float32),
    )


def time_back(gradient, kernel, before_mask, after_mask):
    channels = kernel.shape[0] // 3
    spread = jnp.einsum("fijo,co->fijc", gradient, kernel, preferred_element_type=jnp.float32)
    early_part = spread[..., :channels] * before_mask[:, None, None, None]
    late_part = spread[..., 2 * channels :] * after_mask[:, None, None, None]
    blanks = jnp.zeros_like(early_part[:1])
    moved_early = jnp.concatenate([early_part[1:], blanks], axis=0)
    moved_late = jnp.concatenate([blanks, late_part[:-1]], axis=0)
    return spread[..., channels : 2 * channels] + moved_early + moved_late


def moments(values, pixel_count):
    average = lax.psum(jnp.sum(values, axis=(0, 1, 2)), "dp") / pixel_count
    centered = values - average
    spread = lax.psum(jnp.sum(centered * centered, axis=(0, 1, 2)), "dp") / pixel_count
    return (average, lax.rsqrt(spread + eps))


def reduce_back(gradient, normed):
    return lax.psum(
        (jnp.sum(gradient, axis=(0, 1, 2)), jnp.sum(gradient * normed, axis=(0, 1, 2))), "dp"
    )


def silu_slope(values):
    sigmoid_now = jax.nn.sigmoid(values)
    return sigmoid_now * (1.0 + values * (1.0 - sigmoid_now))


def pick_slot(stack, slot_index):
    return lax.dynamic_index_in_dim(stack, slot_index, 0, keepdims=False)


def store_slot(stack, value, slot_index, usable):
    previous = pick_slot(stack, slot_index)
    return lax.dynamic_update_index_in_dim(stack, jnp.where(usable, value, previous), slot_index, 0)


def on_device_general(
    frames, cotangent, starts, space_kernel, time_kernel, mid_gain, mid_bias, out_gain, out_bias
):
    n_segment = lax.axis_size("segment")
    n_data = lax.axis_size("dp")
    segment_index = lax.axis_index("segment")
    odd_segment = segment_index % 2 == 1
    last_segment = segment_index == n_segment - 1
    first_segment = segment_index == 0
    frame_count = frames.shape[0]
    frame_side = frames.shape[1]
    channels = frames.shape[3]
    hidden_units = mid_gain.shape[1] * n_data
    pixel_count = n_data * frame_count * frame_side * frame_side
    turns = 2 * n_segment - 1
    block_shape = (n_segment,) + frames.shape
    all_frames, all_cot, all_starts = (
        lax.all_gather(frames, "segment", axis=0, tiled=True),
        lax.all_gather(cotangent, "segment", axis=0, tiled=True),
        lax.all_gather(starts.astype(jnp.bfloat16), "segment", axis=0, tiled=True),
    )
    frame_stack = all_frames.reshape(block_shape)
    cot_stack = all_cot.reshape(block_shape)
    clip_flags = all_starts.astype(jnp.float32).reshape(n_segment, frame_count)
    positions = jnp.arange(frame_count)
    before_mask = jnp.where((clip_flags > 0.5) | (positions == 0), 0.0, 1.0)
    following = jnp.concatenate([clip_flags[:, 1:], jnp.ones((n_segment, 1), jnp.float32)], axis=1)
    after_mask = jnp.where(following > 0.5, 0.0, 1.0)
    gathered = (
        lax.all_gather(space_kernel[0].astype(jnp.bfloat16), "dp", axis=0, tiled=True),
        lax.all_gather(time_kernel[0].astype(jnp.bfloat16), "dp", axis=0, tiled=True),
        lax.all_gather(mid_gain[0].astype(jnp.bfloat16), "dp", axis=0, tiled=True),
        lax.all_gather(mid_bias[0].astype(jnp.bfloat16), "dp", axis=0, tiled=True),
        lax.all_gather(out_gain[0].astype(jnp.bfloat16), "dp", axis=0, tiled=True),
        lax.all_gather(out_bias[0].astype(jnp.bfloat16), "dp", axis=0, tiled=True),
    )
    space_low, time_low = (gathered[0], gathered[1])
    mid_gain_now = gathered[2].astype(jnp.float32)
    mid_bias_now = gathered[3].astype(jnp.float32)
    out_gain_now = gathered[4].astype(jnp.float32)
    out_bias_now = gathered[5].astype(jnp.float32)
    incoming = jnp.zeros_like(frames)
    carried = jnp.zeros_like(frames)
    kept_input = jnp.zeros(block_shape, jnp.bfloat16)
    kept_skip = jnp.zeros(block_shape, jnp.bfloat16)
    kept_mid_mean = jnp.zeros((n_segment, hidden_units), jnp.float32)
    kept_mid_scale = jnp.zeros((n_segment, hidden_units), jnp.float32)
    kept_out_mean = jnp.zeros((n_segment, channels), jnp.float32)
    kept_out_scale = jnp.zeros((n_segment, channels), jnp.float32)
    results = jnp.zeros(block_shape, jnp.float32)
    for turn_index in range(turns):
        micro_index = turn_index - segment_index
        usable = (micro_index >= 0) & (micro_index < n_segment)
        slot_index = jnp.clip(micro_index, 0, n_segment - 1)
        current = jnp.where(first_segment, pick_slot(frame_stack, slot_index), incoming)
        skip_input = carried
        _, spatial = space_apply(current, space_low)
        mid_mean, mid_scale = moments(spatial, pixel_count)
        hidden_act = jax.nn.silu(
            (spatial - mid_mean) * mid_scale * mid_gain_now + mid_bias_now
        ).astype(jnp.bfloat16)
        _, temporal = time_apply(
            hidden_act,
            time_low,
            pick_slot(before_mask, slot_index),
            pick_slot(after_mask, slot_index),
        )
        out_mean, out_scale = moments(temporal, pixel_count)
        pre_act = (
            (temporal - out_mean) * out_scale * out_gain_now
            + out_bias_now
            + jnp.where(odd_segment, skip_input.astype(jnp.float32), 0.0)
        )
        result = jax.nn.silu(pre_act).astype(jnp.bfloat16)
        kept_input = store_slot(kept_input, current, slot_index, usable)
        kept_skip = store_slot(kept_skip, skip_input, slot_index, usable)
        kept_mid_mean = store_slot(kept_mid_mean, mid_mean, slot_index, usable)
        kept_mid_scale = store_slot(kept_mid_scale, mid_scale, slot_index, usable)
        kept_out_mean = store_slot(kept_out_mean, out_mean, slot_index, usable)
        kept_out_scale = store_slot(kept_out_scale, out_scale, slot_index, usable)
        results = store_slot(results, result.astype(jnp.float32), slot_index, usable)
        if turn_index < turns - 1:
            incoming, carried = from_behind(
                (result, jnp.where(odd_segment, result, current)), "segment", 1
            )
    gathered = (
        lax.all_gather(space_kernel[0].astype(jnp.bfloat16), "dp", axis=0, tiled=True),
        lax.all_gather(time_kernel[0].astype(jnp.bfloat16), "dp", axis=0, tiled=True),
        lax.all_gather(mid_gain[0].astype(jnp.bfloat16), "dp", axis=0, tiled=True),
        lax.all_gather(mid_bias[0].astype(jnp.bfloat16), "dp", axis=0, tiled=True),
        lax.all_gather(out_gain[0].astype(jnp.bfloat16), "dp", axis=0, tiled=True),
        lax.all_gather(out_bias[0].astype(jnp.bfloat16), "dp", axis=0, tiled=True),
    )
    space_low, time_low = (gathered[0], gathered[1])
    mid_gain_now = gathered[2].astype(jnp.float32)
    mid_bias_now = gathered[3].astype(jnp.float32)
    out_gain_now = gathered[4].astype(jnp.float32)
    out_bias_now = gathered[5].astype(jnp.float32)
    grad_input = jnp.zeros_like(frames)
    grad_skip = jnp.zeros_like(frames)
    space_acc = jnp.zeros(space_low.shape, jnp.float32)
    time_acc = jnp.zeros(time_low.shape, jnp.float32)
    mid_gain_acc = jnp.zeros((hidden_units,), jnp.float32)
    mid_bias_acc = jnp.zeros((hidden_units,), jnp.float32)
    out_gain_acc = jnp.zeros((channels,), jnp.float32)
    out_bias_acc = jnp.zeros((channels,), jnp.float32)
    input_grads = jnp.zeros(block_shape, jnp.float32)
    for turn_index in range(turns):
        micro_index = n_segment - 1 - (turn_index - (n_segment - 1 - segment_index))
        usable = (micro_index >= 0) & (micro_index < n_segment)
        usable_weight = usable.astype(jnp.float32)
        slot_index = jnp.clip(micro_index, 0, n_segment - 1)
        current = pick_slot(kept_input, slot_index)
        skip_input = pick_slot(kept_skip, slot_index)
        before_now = pick_slot(before_mask, slot_index)
        after_now = pick_slot(after_mask, slot_index)
        space_taps, spatial = space_apply(current, space_low)
        mid_normed = (spatial - pick_slot(kept_mid_mean, slot_index)) * pick_slot(
            kept_mid_scale, slot_index
        )
        mid_pre = mid_normed * mid_gain_now + mid_bias_now
        hidden_act = jax.nn.silu(mid_pre).astype(jnp.bfloat16)
        time_taps, temporal = time_apply(hidden_act, time_low, before_now, after_now)
        out_scale = pick_slot(kept_out_scale, slot_index)
        out_normed = (temporal - pick_slot(kept_out_mean, slot_index)) * out_scale
        pre_act = (
            out_normed * out_gain_now
            + out_bias_now
            + jnp.where(odd_segment, skip_input.astype(jnp.float32), 0.0)
        )
        grad_result = jnp.where(
            last_segment,
            pick_slot(cot_stack, slot_index).astype(jnp.float32),
            grad_input.astype(jnp.float32)
            + jnp.where(odd_segment, grad_skip.astype(jnp.float32), 0.0),
        )
        grad_pre = grad_result * silu_slope(pre_act)
        out_bias_sum, out_gain_sum = reduce_back(grad_pre, out_normed)
        grad_temporal = (
            out_gain_now
            * out_scale
            * (grad_pre - out_bias_sum / pixel_count - out_normed * out_gain_sum / pixel_count)
        ).astype(jnp.bfloat16)
        time_acc = time_acc + usable_weight * jnp.einsum(
            "fijc,fijo->co", time_taps, grad_temporal, preferred_element_type=jnp.float32
        )
        grad_hidden = time_back(grad_temporal, time_low, before_now, after_now)
        grad_mid = grad_hidden * silu_slope(mid_pre)
        mid_bias_sum, mid_gain_sum = reduce_back(grad_mid, mid_normed)
        mid_scale = pick_slot(kept_mid_scale, slot_index)
        grad_spatial = (
            mid_gain_now
            * mid_scale
            * (grad_mid - mid_bias_sum / pixel_count - mid_normed * mid_gain_sum / pixel_count)
        ).astype(jnp.bfloat16)
        space_acc = space_acc + usable_weight * jnp.einsum(
            "fijc,fijo->co", space_taps, grad_spatial, preferred_element_type=jnp.float32
        )
        grad_current = space_back(grad_spatial, space_low)
        mid_gain_acc = mid_gain_acc + usable_weight * mid_gain_sum
        mid_bias_acc = mid_bias_acc + usable_weight * mid_bias_sum
        out_gain_acc = out_gain_acc + usable_weight * out_gain_sum
        out_bias_acc = out_bias_acc + usable_weight * out_bias_sum
        input_grads = store_slot(
            input_grads, grad_current + grad_skip.astype(jnp.float32), slot_index, usable
        )
        if turn_index < turns - 1:
            grad_input, grad_skip = from_behind(
                (
                    grad_current.astype(jnp.bfloat16),
                    jnp.where(odd_segment, grad_pre.astype(jnp.bfloat16), grad_skip),
                ),
                "segment",
                -1,
            )
    space_grad, time_grad = (
        lax.psum_scatter(space_acc, "dp", scatter_dimension=0, tiled=True),
        lax.psum_scatter(time_acc, "dp", scatter_dimension=0, tiled=True),
    )
    data_index = lax.axis_index("dp")

    def own_share(full_vector):
        share = full_vector.shape[0] // n_data
        return lax.dynamic_slice_in_dim(full_vector, data_index * share, share)[None]

    flat_shape = (n_segment * frame_count,) + frames.shape[1:]
    arrived_out, arrived_grads = (
        lax.all_to_all(
            results.reshape(flat_shape).astype(jnp.bfloat16),
            "segment",
            split_axis=0,
            concat_axis=0,
            tiled=True,
        ).astype(jnp.float32),
        lax.all_to_all(
            input_grads.reshape(flat_shape).astype(jnp.bfloat16),
            "segment",
            split_axis=0,
            concat_axis=0,
            tiled=True,
        ).astype(jnp.float32),
    )
    output = arrived_out[(n_segment - 1) * frame_count :].astype(jnp.bfloat16)
    frames_grad = arrived_grads[:frame_count]
    return (
        output,
        frames_grad,
        space_grad[None],
        time_grad[None],
        own_share(mid_gain_acc),
        own_share(mid_bias_acc),
        own_share(out_gain_acc),
        own_share(out_bias_acc),
    )


def general(mesh):
    return jax.shard_map(
        on_device_general,
        mesh=mesh,
        in_specs=(
            P(("dp", "segment"), None, None, None),
            P(("dp", "segment"), None, None, None),
            P(("dp", "segment")),
            P("segment", "dp", None),
            P("segment", "dp", None),
            P("segment", "dp"),
            P("segment", "dp"),
            P("segment", "dp"),
            P("segment", "dp"),
        ),
        out_specs=(
            P(("dp", "segment"), None, None, None),
            P(("dp", "segment"), None, None, None),
            P("segment", "dp", None),
            P("segment", "dp", None),
            P("segment", "dp"),
            P("segment", "dp"),
            P("segment", "dp"),
            P("segment", "dp"),
        ),
        check_vma=False,
    )


def solution(mesh):
    if mesh.shape["dp"] != 8 or mesh.shape["segment"] != 4:
        return general(mesh)
    n_dp, n_seg = mesh.shape["dp"], mesh.shape["segment"]
    fine = Mesh(mesh.devices.reshape(n_dp // 2, 2, 2, n_seg // 2), EVERY)
    dp, seg = ("z", "y"), ("x", "c")
    return jax.shard_map(
        on_device,
        mesh=fine,
        in_specs=(
            P(EVERY, None, None, None),
            P(EVERY, None, None, None),
            P(EVERY),
            P(seg, dp, None),
            P(seg, dp, None),
            P(seg, dp),
            P(seg, dp),
            P(seg, dp),
            P(seg, dp),
        ),
        out_specs=(
            P(EVERY, None, None, None),
            P(EVERY, None, None, None),
            P(seg, dp, None),
            P(seg, dp, None),
            P(seg, dp),
            P(seg, dp),
            P(seg, dp),
            P(seg, dp),
        ),
        check_vma=False,
    )
```

```python
import functools

import jax
import jax.numpy as jnp
from jax import lax
from jax.experimental import pallas as pl
from jax.experimental.pallas import tpu as pltpu
from jax.sharding import Mesh, PartitionSpec as P

eps = 1e-05
PLANE = ("y", "x", "c")
EVERY = ("z", "y", "x", "c")
BF = jnp.bfloat16
F32 = jnp.float32


def nt(a, b):
    return lax.dot_general(a, b, (((1,), (1,)), ((), ())), preferred_element_type=F32)


def nn(a, b):
    return lax.dot_general(a, b, (((1,), (0,)), ((), ())), preferred_element_type=F32)


VMEM_CAP = 56 * 1024 * 1024
ANY = pl.BlockSpec(memory_space=pl.ANY)


def call(body, outs, scratch, flops, *args, deps=(), far=(), far_outs=()):
    moved = sum(a.size * a.dtype.itemsize for a in args) + sum(
        o.size * o.dtype.itemsize for o in outs
    )
    n = len(deps)

    def spec(a):
        return pl.BlockSpec(memory_space=pltpu.SMEM if a.dtype == jnp.int32 else pltpu.VMEM)

    return pl.pallas_call(
        lambda *refs: body(*refs[n:]),
        out_shape=outs,
        in_specs=[ANY] * n + [ANY if i in far else spec(a) for i, a in enumerate(args)],
        out_specs=[ANY if i in far_outs else spec(o) for i, o in enumerate(outs)],
        scratch_shapes=scratch,
        compiler_params=pltpu.CompilerParams(vmem_limit_bytes=VMEM_CAP),
        cost_estimate=pl.CostEstimate(flops=flops, bytes_accessed=moved, transcendentals=0),
    )(*deps, *args)


def chunk(i, size):
    return pl.ds(pl.multiple_of(i * size, 16), size)


def clear_borders(pad_ref, side, plane, nf):
    zrow = jnp.zeros(pad_ref.shape[1:], BF)
    pad_ref[0] = zrow
    pad_ref[side + 1] = zrow
    zcol = jnp.zeros((nf, pad_ref.shape[2]), BF)
    for i in range(side):
        pad_ref[i + 1, 0:nf] = zcol
        pad_ref[i + 1, nf + plane : 2 * nf + plane] = zcol


def by_rank(slices, rank):
    odd = lax.rem(rank, 2) == 1
    for p in range(len(slices) // 2):
        a, b = slices[2 * p], slices[2 * p + 1]
        yield lax.bitwise_xor(rank // 2, p), odd, a, b


def halves(odd, own, mate):
    low = lax.broadcasted_iota(jnp.int32, own.shape, 1) < 64
    own, mate = own.astype(F32), mate.astype(F32)
    a, b = jnp.where(odd, mate, own), jnp.where(odd, own, mate)
    top = jnp.where(low, a, pltpu.roll(b, 64, 1))
    bottom = jnp.where(low, pltpu.roll(a, 64, 1), b)
    return top, bottom


def store_packed(rank, mate_ref, keep_ref, part, k, step, low):
    rows_now = chunk(k, step)
    odd = lax.rem(rank, 2) == 1
    for q in range(keep_ref.shape[0]):
        x = part[:step, 128 * q : 128 * q + 128]
        y = part[step:, 128 * q : 128 * q + 128]
        even_slice = jnp.where(low, x, pltpu.roll(y, 64, 1))
        odd_slice = jnp.where(low, pltpu.roll(x, 64, 1), y)
        p = lax.bitwise_xor(rank // 2, q)
        keep_ref[p, rows_now, :] = jnp.where(odd, odd_slice, even_slice).astype(BF)
        mate_ref[p, rows_now, :] = jnp.where(odd, even_slice, odd_slice).astype(BF)


def fetch_kernels(w_ref, ktm_ref, lw_ref, sems):
    nz, _, width = w_ref.shape
    hc = ktm_ref.shape[0]
    copies = []
    for z in range(nz):
        copies.append(pltpu.make_async_copy(
            w_ref.at[z, pl.ds(0, hc)], ktm_ref.at[:, pl.ds(z * width, width)], sems.at[2 * z]))
        copies.append(pltpu.make_async_copy(
            w_ref.at[z, pl.ds(hc, lw_ref.shape[1])], lw_ref.at[z], sems.at[2 * z + 1]))
    for copy in copies:
        copy.start()
    return copies


def join_temporal(lw_ref, lf_ref, ltm_ref):
    ch = ltm_ref.shape[1]
    width = lw_ref.shape[2] // 2
    count = 2 * lw_ref.shape[0]
    size = ltm_ref.shape[0] // count
    for z in range(lw_ref.shape[0]):
        first = lw_ref[z, :, 0:ch].astype(F32)
        off = width % 128
        second = lw_ref[z, :, width - off : width - off + ch + 128].astype(F32)
        second = pltpu.roll(second, ch + 128 - off, 1)[:, 0:ch]
        for b, block in ((2 * z, first), (2 * z + 1, second)):
            lf_ref[b * size : b * size + block.shape[0], :] = block
    ltm_ref[...] = lf_ref[0 : ltm_ref.shape[0], :].astype(BF)


def prepare_body(w_ref, kn_out, l_out, lt_out, rows_out, ktm_ref, lw_ref, lf_ref, sems):
    hc, ch = ktm_ref.shape[0], l_out.shape[1]
    for copy in fetch_kernels(w_ref, ktm_ref, lw_ref, sems):
        copy.wait()
    for t in range(9):
        kn_out[t] = ktm_ref[:, t * ch : (t + 1) * ch].astype(F32).T.astype(BF)
    join_temporal(lw_ref, lf_ref, l_out)
    rows_out[...] = lw_ref[:, lw_ref.shape[1] - rows_out.shape[1] :, :]
    for t in range(3):
        lt_out[t] = lf_ref[t * hc : (t + 1) * hc].T.astype(BF)


def prepare(w, hc, ch, deps=()):
    outs = [
        jax.ShapeDtypeStruct((9, ch, hc), BF),
        jax.ShapeDtypeStruct((3 * hc, ch), BF),
        jax.ShapeDtypeStruct((3, ch, hc), BF),
        jax.ShapeDtypeStruct((w.shape[0], 16, w.shape[2]), BF),
    ]
    tall = w.shape[1] - hc
    scratch = [
        pltpu.VMEM((hc, 9 * ch), BF),
        pltpu.VMEM((w.shape[0], tall, w.shape[2]), BF),
        pltpu.VMEM((3 * hc + tall, ch), F32),
        pltpu.SemaphoreType.DMA((2 * w.shape[0],)),
    ]
    return call(prepare_body, outs, scratch, 2 * w.size * 512, w, deps=deps, far=(0,))


def conv_body(side, first, rank_ref, *refs):
    n = 1 if first else 8
    slices = refs[:n]
    (kn_in, ltm_ref, vec_ref, before_ref, after_ref,
     pad_out, hid_out, xhat_out, rs_ref, mate_ref, keep_ref,
     pad_ref, hid_ref, xhat_ref, sp_ref, kn_ref, sems) = refs[n:]
    rank = rank_ref[0]
    kn_copy = pltpu.make_async_copy(kn_in, kn_ref, sems.at[0])
    kn_copy.start()
    ch, hc = pad_ref.shape[2], hid_ref.shape[1]
    rows = hid_ref.shape[0]
    plane = rows // side
    nf = plane // side
    step = plane // 2
    clear_borders(pad_ref, side, plane, nf)
    if first:
        for i in range(side):
            pad_ref[i + 1, nf : nf + plane] = slices[0][i * plane : (i + 1) * plane]
    else:
        def place(k, carry):
            for q, odd, a_ref, b_ref in by_rank(slices, rank):
                top, bottom = halves(odd, a_ref[chunk(k, step), :], b_ref[chunk(k, step), :])
                lanes = pl.ds(pl.multiple_of(128 * q, 128), 128)
                for piece, kk in ((top, k), (bottom, k + side)):
                    at = nf + lax.rem(kk, 2) * step
                    pad_ref[1 + kk // 2, pl.ds(pl.multiple_of(at, 16), step), lanes] = piece.astype(BF)
            return carry

        lax.fori_loop(0, side, place, 0, unroll=True)
    pad_copy = pltpu.make_async_copy(pad_ref, pad_out, sems.at[1])
    pad_copy.start()
    kn_copy.wait()

    def conv(i, total):
        acc = jnp.zeros((plane, hc), F32)
        for t in range(9):
            r, c = t // 3, t % 3
            acc += nn(pad_ref[i + r, c * nf : c * nf + plane, :], kn_ref[t])
        sp_ref[i] = acc
        return total + jnp.sum(acc, axis=0, keepdims=True)

    mean = lax.fori_loop(0, side, conv, jnp.zeros((1, hc), F32), unroll=True) / rows

    def square(i, total):
        cen = sp_ref[i] - mean
        return total + jnp.sum(cen * cen, axis=0, keepdims=True)

    var = lax.fori_loop(0, side, square, jnp.zeros((1, hc), F32), unroll=True) / rows
    rs = lax.rsqrt(var + eps)
    rs_ref[...] = rs
    gain, bias = vec_ref[0:1, :], vec_ref[1:2, :]

    def act(i, carry):
        xhat = (sp_ref[i] - mean) * rs
        xhat_ref[i] = xhat
        v = xhat * gain + bias
        v = v * jax.nn.sigmoid(v)
        sp_ref[i] = v
        hid_ref[chunk(i, plane), :] = v.astype(BF)
        return carry

    lax.fori_loop(0, side, act, 0, unroll=True)
    late = [
        pltpu.make_async_copy(hid_ref, hid_out, sems.at[2]),
        pltpu.make_async_copy(xhat_ref, xhat_out, sems.at[3]),
    ]
    for copy in late:
        copy.start()
    low = lax.broadcasted_iota(jnp.int32, (step, 128), 1) < 64

    def temporal(k, carry):
        pieces = []
        for kk in (k, k + side):
            par = lax.rem(kk, 2)
            h = sp_ref[kk // 2, pl.ds(pl.multiple_of(par * step, 8), step), :]
            at = pl.multiple_of(par * (step % nf), 8)
            pieces.append((
                (pltpu.roll(h, 1, 0) * before_ref[pl.ds(at, step), :]).astype(BF),
                h.astype(BF),
                (pltpu.roll(h, step - 1, 0) * after_ref[pl.ds(at, step), :]).astype(BF),
            ))
        part = sum(
            nn(jnp.concatenate([x, y], axis=0), ltm_ref[t * hc : (t + 1) * hc])
            for t, (x, y) in enumerate(zip(*pieces))
        )
        store_packed(rank, mate_ref, keep_ref, part, k, step, low)
        return carry

    lax.fori_loop(0, side, temporal, 0, unroll=True)
    for copy in [pad_copy] + late:
        copy.wait()


def conv_forward(rank, g, kn, lt, vec, before, after, side, pixels, ch, deps=()):
    hc = vec.shape[1]
    plane = pixels // side
    nf = plane // side
    n = len(g)
    shapes = [
        ((side + 2, plane + 2 * nf, ch), BF),
        ((pixels, hc), BF),
        ((side, plane, hc), F32),
    ]
    outs = [jax.ShapeDtypeStruct(*s) for s in shapes] + [
        jax.ShapeDtypeStruct((1, hc), F32),
        jax.ShapeDtypeStruct((4, pixels // 2, 128), BF),
        jax.ShapeDtypeStruct((4, pixels // 2, 128), BF),
    ]
    scratch = [pltpu.VMEM(*s) for s in shapes] + [
        pltpu.VMEM((side, plane, hc), F32),
        pltpu.VMEM((9, ch, hc), BF),
        pltpu.SemaphoreType.DMA((4,)),
    ]
    flops = 2 * pixels * hc * 12 * ch
    return call(functools.partial(conv_body, side, n == 1), outs, scratch, flops,
                rank, *g, kn, lt, vec, before, after,
                deps=deps, far=(n + 1,), far_outs=(0, 1, 2))


def fold(v):
    return v + pltpu.roll(v, 64, 1)


def total_of(refs):
    t = refs[0][...].astype(F32)
    for ref in refs[1:]:
        t += ref[...].astype(F32)
    return t


def pair_sum_body(keep_ref, mate_ref, *out_refs):
    for p, ref in enumerate(out_refs):
        ref[...] = (keep_ref[p].astype(F32) + mate_ref[p].astype(F32)).astype(ref.dtype)


def pair_sum(keep, arrived, deps=()):
    shape = keep.shape[1:]
    outs = [jax.ShapeDtypeStruct(shape, BF)] * keep.shape[0]
    return call(pair_sum_body, outs, [], keep.size, keep, arrived, deps=deps)


def out_norm_body(n, has_skip, *refs):
    parts, refs = refs[:n], refs[n:]
    if has_skip:
        vec_ref, skip_ref, xhat_ref, rs_ref, pre_ref, res_ref = refs
    else:
        vec_ref, xhat_ref, rs_ref, pre_ref, res_ref = refs
    t = total_of(parts)
    pixels = 2 * t.shape[0]
    mean = fold(jnp.sum(t, axis=0, keepdims=True)) / pixels
    cen = t - mean
    rs = lax.rsqrt(fold(jnp.sum(cen * cen, axis=0, keepdims=True)) / pixels + eps)
    xhat = cen * rs
    pre = xhat * vec_ref[0:1, :] + vec_ref[1:2, :]
    if has_skip:
        pre = pre + skip_ref[...].astype(F32)
    xhat_ref[...] = xhat
    rs_ref[...] = rs
    pre_ref[...] = pre
    res_ref[...] = (pre * jax.nn.sigmoid(pre)).astype(BF)


def out_norm(parts, vec, skip, deps=()):
    half = parts[0].shape[0]
    outs = [
        jax.ShapeDtypeStruct((half, 128), F32),
        jax.ShapeDtypeStruct((1, 128), F32),
        jax.ShapeDtypeStruct((half, 128), F32),
        jax.ShapeDtypeStruct((half, 128), BF),
    ]
    args = (*parts, vec) + (() if skip is None else (skip,))
    body = functools.partial(out_norm_body, len(parts), skip is not None)
    return call(body, outs, [], half * 128 * 10, *args, deps=deps)


def out_back_body(n, *refs):
    parts, (pre_ref, xhat_ref, rs_ref, vec_ref, dpre_ref, dt_ref, sums_ref) = refs[:n], refs[n:]
    g = total_of(parts)
    pre, xhat = pre_ref[...], xhat_ref[...]
    sig = jax.nn.sigmoid(pre)
    dpre = g * (sig * (1.0 + pre * (1.0 - sig)))
    pixels = 2 * pre.shape[0]
    sb = fold(jnp.sum(dpre, axis=0, keepdims=True))
    sg = fold(jnp.sum(dpre * xhat, axis=0, keepdims=True))
    dpre_ref[...] = dpre.astype(BF)
    scale = vec_ref[0:1, :] * rs_ref[...]
    dt_ref[...] = (scale * (dpre - sb / pixels - xhat * (sg / pixels))).astype(BF)
    sums_ref[0:1, :] = sg
    sums_ref[1:2, :] = sb


def out_back(parts, pre, xhat, rs, vec, deps=()):
    half = pre.shape[0]
    outs = [
        jax.ShapeDtypeStruct((half, 128), BF),
        jax.ShapeDtypeStruct((half, 128), BF),
        jax.ShapeDtypeStruct((2, 128), F32),
    ]
    args = (*parts, pre, xhat, rs, vec)
    return call(functools.partial(out_back_body, len(parts)), outs, [], half * 1280, *args, deps=deps)


def conv_back_body(side, rank_ref, *refs):
    slices, (xhat_in, rs_ref, w_ref, lnt_ref, vec_ref, before_ref, after_ref,
             dt_out, ds_out, sums_ref, mate_ref, keep_ref,
             dt_ref, ds_ref, xhat_ref, dy_ref, pad_ref, ktm_ref, sems) = refs[:8], refs[8:]
    half = slices[0].shape[0]
    rank = rank_ref[0]
    nz, _, width = w_ref.shape
    rows = 2 * half
    plane = rows // side
    nf = plane // side
    step = plane // 2
    hc = ds_ref.shape[1]
    ch = dt_ref.shape[1]
    fetched = [
        pltpu.make_async_copy(
            w_ref.at[z, pl.ds(0, hc)], ktm_ref.at[:, pl.ds(z * width, width)], sems.at[z])
        for z in range(nz)
    ]
    xhat_copy = pltpu.make_async_copy(xhat_in, xhat_ref, sems.at[nz])
    for copy in fetched + [xhat_copy]:
        copy.start()
    clear_borders(pad_ref, side, plane, nf)

    def place(k, carry):
        for q, odd, a_ref, b_ref in by_rank(slices, rank):
            top, bottom = halves(odd, a_ref[chunk(k, step), :], b_ref[chunk(k, step), :])
            lanes = pl.ds(pl.multiple_of(128 * q, 128), 128)
            dt_ref[chunk(k, step), lanes] = top.astype(BF)
            dt_ref[pl.ds(pl.multiple_of(half + k * step, 16), step), lanes] = bottom.astype(BF)
        return carry

    lax.fori_loop(0, side, place, 0, unroll=True)
    dt_copy = pltpu.make_async_copy(dt_ref, dt_out, sems.at[nz + 1])
    dt_copy.start()
    xhat_copy.wait()
    gain, bias = vec_ref[0:1, :], vec_ref[1:2, :]

    def hidden_grad(i, sums):
        dt = dt_ref[chunk(i, plane), :]
        early = nn(dt, lnt_ref[0]) * before_ref[0:plane, :]
        late = nn(dt, lnt_ref[2]) * after_ref[0:plane, :]
        dh = nn(dt, lnt_ref[1]) + pltpu.roll(early, plane - 1, 0) + pltpu.roll(late, 1, 0)
        xhat = xhat_ref[i]
        v = xhat * gain + bias
        sig = jax.nn.sigmoid(v)
        dy = dh * (sig * (1.0 + v * (1.0 - sig)))
        dy_ref[i] = dy
        return (
            sums[0] + jnp.sum(dy * xhat, axis=0, keepdims=True),
            sums[1] + jnp.sum(dy, axis=0, keepdims=True),
        )

    zero = jnp.zeros((1, hc), F32)
    sg, sb = lax.fori_loop(0, side, hidden_grad, (zero, zero), unroll=True)
    sums_ref[0:1, :] = sg
    sums_ref[1:2, :] = sb
    scale = gain * rs_ref[...]

    def spatial_grad(i, carry):
        ds = (scale * (dy_ref[i] - sb / rows - xhat_ref[i] * (sg / rows))).astype(BF)
        pad_ref[i + 1, nf : nf + plane] = ds
        ds_ref[chunk(i, plane), :] = ds
        return carry

    lax.fori_loop(0, side, spatial_grad, 0, unroll=True)
    ds_copy = pltpu.make_async_copy(ds_ref, ds_out, sems.at[nz + 2])
    ds_copy.start()
    for copy in fetched:
        copy.wait()
    low = lax.broadcasted_iota(jnp.int32, (step, 128), 1) < 64

    def back(k, carry):
        acc = jnp.zeros((2 * step, ch), F32)
        for t in range(9):
            r, c = 2 - t // 3, 2 - t % 3
            pieces = []
            for kk in (k, k + side):
                at = c * nf + lax.rem(kk, 2) * step
                pieces.append(pad_ref[kk // 2 + r, pl.ds(pl.multiple_of(at, 16), step), :])
            acc += nn(jnp.concatenate(pieces, axis=0), ktm_ref[:, t * ch : (t + 1) * ch])
        store_packed(rank, mate_ref, keep_ref, acc, k, step, low)
        return carry

    lax.fori_loop(0, side, back, 0, unroll=True)
    dt_copy.wait()
    ds_copy.wait()


def conv_back(rank, g, xhat, rs, w, lnt, vec, before, after, side, deps=()):
    half = g[0].shape[0]
    hc = vec.shape[1]
    ch = len(g) * 64
    pixels = 2 * half
    plane = pixels // side
    nf = plane // side
    outs = [
        jax.ShapeDtypeStruct((pixels, ch), BF),
        jax.ShapeDtypeStruct((pixels, hc), BF),
        jax.ShapeDtypeStruct((2, hc), F32),
        jax.ShapeDtypeStruct((4, half, 128), BF),
        jax.ShapeDtypeStruct((4, half, 128), BF),
    ]
    scratch = [
        pltpu.VMEM((pixels, ch), BF),
        pltpu.VMEM((pixels, hc), BF),
        pltpu.VMEM((side, plane, hc), F32),
        pltpu.VMEM((side, plane, hc), F32),
        pltpu.VMEM((side + 2, plane + 2 * nf, hc), BF),
        pltpu.VMEM((hc, 9 * ch), BF),
        pltpu.SemaphoreType.DMA((w.shape[0] + 3,)),
    ]
    flops = 2 * pixels * hc * 12 * ch
    return call(functools.partial(conv_back_body, side), outs, scratch, flops,
                rank, *g, xhat, rs, w, lnt, vec, before, after,
                deps=deps, far=(9, 11), far_outs=(0, 1))


def grads_body(side, pad_ref, hid_ref, ds_ref, dt_ref, before_ref, after_ref, mid_ref, out_ref,
               sg_ref, dst_ref, taps_ref, tg_ref, vec_ref):
    ch = pad_ref.shape[2]
    hc = hid_ref.shape[1]
    plane = hid_ref.shape[0] // side
    nf = plane // side
    for i in (0, 1, side + 2, side + 3):
        dst_ref[i] = jnp.zeros(dst_ref.shape[1:], BF)
    for i in range(side):
        at = slice(i * plane, (i + 1) * plane)
        h = hid_ref[at, :].astype(F32)
        taps_ref[i, 0:hc] = (pltpu.roll(h, 1, 0) * before_ref[0:plane, :]).T.astype(BF)
        taps_ref[i, hc : 2 * hc] = h.T.astype(BF)
        taps_ref[i, 2 * hc : 3 * hc] = (pltpu.roll(h, plane - 1, 0) * after_ref[0:plane, :]).T.astype(BF)
        dst_ref[i + 2] = ds_ref[at, :].astype(F32).T.astype(BF)
    tg_ref[0 : 3 * hc, :] = sum(
        nn(taps_ref[i], dt_ref[i * plane : (i + 1) * plane, :]) for i in range(side)
    )
    tg_ref[3 * hc :, :] = jnp.zeros((tg_ref.shape[0] - 3 * hc, ch), F32)
    nz, _, width = sg_ref.shape
    size = 3 * hc // (2 * nz)
    vec_ref[...] = jnp.zeros(vec_ref.shape, F32)
    vec_ref[size : size + 2, 0:hc] = mid_ref[...]
    vec_ref[size + 2 : size + 4, 0:128] = out_ref[...]
    tall = vec_ref.shape[0]
    inside = lax.broadcasted_iota(jnp.int32, (tall, ch), 0) < size
    off = (width // 2) % 128
    for z in range(nz):
        first, second = [
            jnp.where(inside, tg_ref[b * size : b * size + tall, :], vec_ref[...])
            for b in (2 * z, 2 * z + 1)
        ]
        start = width // 2 - off
        sg_ref[z, hc : hc + tall, 0:ch] = first.astype(BF)
        second = pltpu.roll(jnp.concatenate([second, jnp.zeros((tall, 128), F32)], axis=1), off, 1)
        sg_ref[z, hc : hc + tall, start : start + ch + 128] = second.astype(BF)
    for c in range(3):
        acc = sum(
            nn(dst_ref[i : i + 3].reshape(3 * hc, plane), pad_ref[i, c * nf : c * nf + plane, :])
            for i in range(1, side + 1)
        )
        for r in range(3):
            first = (3 * r + c) * ch
            end = first + ch
            at = (2 - r) * hc
            done = 0
            while first < end:
                z = first // width
                last = min(end, (z + 1) * width)
                sg_ref[z, 0:hc, first - z * width : last - z * width] = (
                    acc[at : at + hc, done : done + last - first].astype(BF)
                )
                done += last - first
                first = last


def kernel_grads(pad, hidden, ds, dt, before, after, mid, out, side, shape, deps=()):
    pixels, hc = hidden.shape
    ch = dt.shape[1]
    plane = pixels // side
    outs = [jax.ShapeDtypeStruct(shape, BF)]
    tall = shape[1] - hc
    scratch = [
        pltpu.VMEM((side + 4, hc, plane), BF),
        pltpu.VMEM((side, 3 * hc, plane), BF),
        pltpu.VMEM((3 * hc + tall, ch), F32),
        pltpu.VMEM((tall, ch), F32),
    ]
    flops = 2 * pixels * hc * 12 * ch
    return call(functools.partial(grads_body, side), outs, scratch, flops,
                pad, hidden, ds, dt, before, after, mid, out, deps=deps)[0]


def copy_after_body(v_ref, out_ref):
    out_ref[...] = v_ref[...]


def after_all(v, *deps):
    return call(copy_after_body, [jax.ShapeDtypeStruct(v.shape, v.dtype)], [], v.size, v, deps=deps)[0]


def pack_kernels_body(kt_ref, lt_ref, vec_ref, out_ref, low_ref):
    ranks, _, width = out_ref.shape
    hc = kt_ref.shape[0] // ranks
    blocks = lt_ref.shape[0] // hc
    q = hc // ranks
    low_ref[...] = jnp.zeros(low_ref.shape, F32)
    for r in range(ranks):
        out_ref[r, 0:hc, :] = kt_ref[r * hc : (r + 1) * hc, :]
        for b in range(blocks):
            low_ref[r, b * q : (b + 1) * q, 0 : lt_ref.shape[1]] = (
                lt_ref[b * hc + r * q : b * hc + (r + 1) * q, :]
            )
        low_ref[r, blocks * q : blocks * q + 1, :] = vec_ref[...]
        out_ref[r, hc:, :] = low_ref[r].astype(BF)


def pack_kernels(kt, lt, vec, ranks, tall, deps):
    width = kt.shape[1]
    outs = [jax.ShapeDtypeStruct((ranks, kt.shape[0] // ranks + tall, width), BF)]
    scratch = [pltpu.VMEM((ranks, tall, width), F32)]
    return call(pack_kernels_body, outs, scratch, kt.size * 8, kt, lt, vec, deps=deps)[0]


def two_blocks(v_ref, width):
    off = width % 128
    second = v_ref[:, width - off : 2 * width].astype(F32)
    return v_ref[:, 0:width], pltpu.roll(second, width, 1)[:, 0:width].astype(BF)


def stack_sections_body(count, *refs):
    out_ref, sections = refs[-1], refs[:-1]
    out_ref[...] = jnp.zeros(out_ref.shape, BF)
    for s, ref in enumerate(sections):
        first, second = two_blocks(ref, out_ref.shape[2])
        out_ref[count - len(sections) + s] = first
        out_ref[2 * count - len(sections) + s] = second


def stack_sections(sections, count, deps):
    high, width = sections[0].shape
    outs = [jax.ShapeDtypeStruct((2 * count, high, width // 2), BF)]
    return call(functools.partial(stack_sections_body, count), outs, [], high * width * 8, *sections,
                deps=deps)[0]


def near_far_body(y_ref, v_ref, near_ref, far_ref):
    first, second = two_blocks(v_ref, near_ref.shape[1])
    here = y_ref[0] == 0
    near_ref[...] = jnp.where(here, first, second)
    far_ref[...] = jnp.where(here, second, first)


def near_far(y, v, deps):
    high, width = v.shape
    outs = [jax.ShapeDtypeStruct((high, width // 2), BF)] * 2
    return call(near_far_body, outs, [], high * width * 4, y, v, deps=deps)


def call(body, outs, scratch, flops, *args, deps=(), far=(), far_outs=()):
    moved = sum(a.size * a.dtype.itemsize for a in args) + sum(
        o.size * o.dtype.itemsize for o in outs
    )
    n = len(deps)

    def spec(a):
        return pl.BlockSpec(memory_space=pltpu.SMEM if a.dtype == jnp.int32 else pltpu.VMEM)

    return pl.pallas_call(
        lambda *refs: body(*refs[n:]),
        out_shape=outs,
        in_specs=[ANY] * n + [ANY if i in far else spec(a) for i, a in enumerate(args)],
        out_specs=[ANY if i in far_outs else spec(o) for i, o in enumerate(outs)],
        scratch_shapes=scratch,
        compiler_params=pltpu.CompilerParams(vmem_limit_bytes=VMEM_CAP),
        cost_estimate=pl.CostEstimate(flops=flops, bytes_accessed=moved, transcendentals=0),
    )(*deps, *args)


def chunk(i, size):
    return pl.ds(pl.multiple_of(i * size, 16), size)


def clear_borders(pad_ref, side, plane, nf):
    zrow = jnp.zeros(pad_ref.shape[1:], BF)
    pad_ref[0] = zrow
    pad_ref[side + 1] = zrow
    zcol = jnp.zeros((nf, pad_ref.shape[2]), BF)
    for i in range(side):
        pad_ref[i + 1, 0:nf] = zcol
        pad_ref[i + 1, nf + plane : 2 * nf + plane] = zcol


def by_rank(slices, rank):
    odd = lax.rem(rank, 2) == 1
    for p in range(len(slices) // 2):
        a, b = slices[2 * p], slices[2 * p + 1]
        yield lax.bitwise_xor(rank // 2, p), odd, a, b


def halves(odd, own, mate):
    low = lax.broadcasted_iota(jnp.int32, own.shape, 1) < 64
    own, mate = own.astype(F32), mate.astype(F32)
    a, b = jnp.where(odd, mate, own), jnp.where(odd, own, mate)
    top = jnp.where(low, a, pltpu.roll(b, 64, 1))
    bottom = jnp.where(low, pltpu.roll(a, 64, 1), b)
    return top, bottom


def store_packed(rank, mate_ref, keep_ref, part, k, step, low):
    rows_now = chunk(k, step)
    odd = lax.rem(rank, 2) == 1
    for q in range(keep_ref.shape[0]):
        x = part[:step, 128 * q : 128 * q + 128]
        y = part[step:, 128 * q : 128 * q + 128]
        even_slice = jnp.where(low, x, pltpu.roll(y, 64, 1))
        odd_slice = jnp.where(low, pltpu.roll(x, 64, 1), y)
        p = lax.bitwise_xor(rank // 2, q)
        keep_ref[p, rows_now, :] = jnp.where(odd, odd_slice, even_slice).astype(BF)
        mate_ref[p, rows_now, :] = jnp.where(odd, even_slice, odd_slice).astype(BF)


def fetch_kernels(w_ref, ktm_ref, lw_ref, sems):
    nz, _, width = w_ref.shape
    hc = ktm_ref.shape[0]
    copies = []
    for z in range(nz):
        copies.append(pltpu.make_async_copy(
            w_ref.at[z, pl.ds(0, hc)], ktm_ref.at[:, pl.ds(z * width, width)], sems.at[2 * z]))
        copies.append(pltpu.make_async_copy(
            w_ref.at[z, pl.ds(hc, lw_ref.shape[1])], lw_ref.at[z], sems.at[2 * z + 1]))
    for copy in copies:
        copy.start()
    return copies


def join_temporal(lw_ref, lf_ref, ltm_ref):
    ch = ltm_ref.shape[1]
    width = lw_ref.shape[2] // 2
    count = 2 * lw_ref.shape[0]
    size = ltm_ref.shape[0] // count
    for z in range(lw_ref.shape[0]):
        first = lw_ref[z, :, 0:ch].astype(F32)
        off = width % 128
        second = lw_ref[z, :, width - off : width - off + ch + 128].astype(F32)
        second = pltpu.roll(second, ch + 128 - off, 1)[:, 0:ch]
        for b, block in ((2 * z, first), (2 * z + 1, second)):
            lf_ref[b * size : b * size + block.shape[0], :] = block
    ltm_ref[...] = lf_ref[0 : ltm_ref.shape[0], :].astype(BF)


def prepare_body(w_ref, kn_out, l_out, lt_out, rows_out, ktm_ref, lw_ref, lf_ref, sems):
    hc, ch = ktm_ref.shape[0], l_out.shape[1]
    for copy in fetch_kernels(w_ref, ktm_ref, lw_ref, sems):
        copy.wait()
    for t in range(9):
        kn_out[t] = ktm_ref[:, t * ch : (t + 1) * ch].astype(F32).T.astype(BF)
    join_temporal(lw_ref, lf_ref, l_out)
    rows_out[...] = lw_ref[:, lw_ref.shape[1] - rows_out.shape[1] :, :]
    for t in range(3):
        lt_out[t] = lf_ref[t * hc : (t + 1) * hc].T.astype(BF)


def prepare(w, hc, ch, deps=()):
    outs = [
        jax.ShapeDtypeStruct((9, ch, hc), BF),
        jax.ShapeDtypeStruct((3 * hc, ch), BF),
        jax.ShapeDtypeStruct((3, ch, hc), BF),
        jax.ShapeDtypeStruct((w.shape[0], 16, w.shape[2]), BF),
    ]
    tall = w.shape[1] - hc
    scratch = [
        pltpu.VMEM((hc, 9 * ch), BF),
        pltpu.VMEM((w.shape[0], tall, w.shape[2]), BF),
        pltpu.VMEM((3 * hc + tall, ch), F32),
        pltpu.SemaphoreType.DMA((2 * w.shape[0],)),
    ]
    return call(prepare_body, outs, scratch, 2 * w.size * 512, w, deps=deps, far=(0,))


def conv_body(side, first, rank_ref, *refs):
    n = 1 if first else 8
    slices = refs[:n]
    (kn_in, ltm_ref, vec_ref, before_ref, after_ref,
     pad_out, hid_out, xhat_out, rs_ref, mate_ref, keep_ref,
     pad_ref, hid_ref, xhat_ref, sp_ref, kn_ref, sems) = refs[n:]
    rank = rank_ref[0]
    kn_copy = pltpu.make_async_copy(kn_in, kn_ref, sems.at[0])
    kn_copy.start()
    ch, hc = pad_ref.shape[2], hid_ref.shape[1]
    rows = hid_ref.shape[0]
    plane = rows // side
    nf = plane // side
    step = plane // 2
    clear_borders(pad_ref, side, plane, nf)
    if first:
        for i in range(side):
            pad_ref[i + 1, nf : nf + plane] = slices[0][i * plane : (i + 1) * plane]
    else:
        def place(k, carry):
            for q, odd, a_ref, b_ref in by_rank(slices, rank):
                top, bottom = halves(odd, a_ref[chunk(k, step), :], b_ref[chunk(k, step), :])
                lanes = pl.ds(pl.multiple_of(128 * q, 128), 128)
                for piece, kk in ((top, k), (bottom, k + side)):
                    at = nf + lax.rem(kk, 2) * step
                    pad_ref[1 + kk // 2, pl.ds(pl.multiple_of(at, 16), step), lanes] = piece.astype(BF)
            return carry

        lax.fori_loop(0, side, place, 0, unroll=True)
    pad_copy = pltpu.make_async_copy(pad_ref, pad_out, sems.at[1])
    pad_copy.start()
    kn_copy.wait()

    def conv(i, total):
        acc = jnp.zeros((plane, hc), F32)
        for t in range(9):
            r, c = t // 3, t % 3
            acc += nn(pad_ref[i + r, c * nf : c * nf + plane, :], kn_ref[t])
        sp_ref[i] = acc
        return total + jnp.sum(acc, axis=0, keepdims=True)

    mean = lax.fori_loop(0, side, conv, jnp.zeros((1, hc), F32), unroll=True) / rows

    def square(i, total):
        cen = sp_ref[i] - mean
        return total + jnp.sum(cen * cen, axis=0, keepdims=True)

    var = lax.fori_loop(0, side, square, jnp.zeros((1, hc), F32), unroll=True) / rows
    rs = lax.rsqrt(var + eps)
    rs_ref[...] = rs
    gain, bias = vec_ref[0:1, :], vec_ref[1:2, :]

    def act(i, carry):
        xhat = (sp_ref[i] - mean) * rs
        xhat_ref[i] = xhat
        v = xhat * gain + bias
        v = v * jax.nn.sigmoid(v)
        sp_ref[i] = v
        hid_ref[chunk(i, plane), :] = v.astype(BF)
        return carry

    lax.fori_loop(0, side, act, 0, unroll=True)
    late = [
        pltpu.make_async_copy(hid_ref, hid_out, sems.at[2]),
        pltpu.make_async_copy(xhat_ref, xhat_out, sems.at[3]),
    ]
    for copy in late:
        copy.start()
    low = lax.broadcasted_iota(jnp.int32, (step, 128), 1) < 64

    def temporal(k, carry):
        pieces = []
        for kk in (k, k + side):
            par = lax.rem(kk, 2)
            h = sp_ref[kk // 2, pl.ds(pl.multiple_of(par * step, 8), step), :]
            at = pl.multiple_of(par * (step % nf), 8)
            pieces.append((
                (pltpu.roll(h, 1, 0) * before_ref[pl.ds(at, step), :]).astype(BF),
                h.astype(BF),
                (pltpu.roll(h, step - 1, 0) * after_ref[pl.ds(at, step), :]).astype(BF),
            ))
        part = sum(
            nn(jnp.concatenate([x, y], axis=0), ltm_ref[t * hc : (t + 1) * hc])
            for t, (x, y) in enumerate(zip(*pieces))
        )
        store_packed(rank, mate_ref, keep_ref, part, k, step, low)
        return carry

    lax.fori_loop(0, side, temporal, 0, unroll=True)
    for copy in [pad_copy] + late:
        copy.wait()


def conv_forward(rank, g, kn, lt, vec, before, after, side, pixels, ch, deps=()):
    hc = vec.shape[1]
    plane = pixels // side
    nf = plane // side
    n = len(g)
    shapes = [
        ((side + 2, plane + 2 * nf, ch), BF),
        ((pixels, hc), BF),
        ((side, plane, hc), F32),
    ]
    outs = [jax.ShapeDtypeStruct(*s) for s in shapes] + [
        jax.ShapeDtypeStruct((1, hc), F32),
        jax.ShapeDtypeStruct((4, pixels // 2, 128), BF),
        jax.ShapeDtypeStruct((4, pixels // 2, 128), BF),
    ]
    scratch = [pltpu.VMEM(*s) for s in shapes] + [
        pltpu.VMEM((side, plane, hc), F32),
        pltpu.VMEM((9, ch, hc), BF),
        pltpu.SemaphoreType.DMA((4,)),
    ]
    flops = 2 * pixels * hc * 12 * ch
    return call(functools.partial(conv_body, side, n == 1), outs, scratch, flops,
                rank, *g, kn, lt, vec, before, after,
                deps=deps, far=(n + 1,), far_outs=(0, 1, 2))


def fold(v):
    return v + pltpu.roll(v, 64, 1)


def total_of(refs):
    t = refs[0][...].astype(F32)
    for ref in refs[1:]:
        t += ref[...].astype(F32)
    return t


def pair_sum_body(keep_ref, mate_ref, *out_refs):
    for p, ref in enumerate(out_refs):
        ref[...] = (keep_ref[p].astype(F32) + mate_ref[p].astype(F32)).astype(ref.dtype)


def pair_sum(keep, arrived, deps=()):
    shape = keep.shape[1:]
    outs = [jax.ShapeDtypeStruct(shape, BF)] * keep.shape[0]
    return call(pair_sum_body, outs, [], keep.size, keep, arrived, deps=deps)


def out_norm_body(n, has_skip, *refs):
    parts, refs = refs[:n], refs[n:]
    if has_skip:
        vec_ref, skip_ref, xhat_ref, rs_ref, pre_ref, res_ref = refs
    else:
        vec_ref, xhat_ref, rs_ref, pre_ref, res_ref = refs
    t = total_of(parts)
    pixels = 2 * t.shape[0]
    mean = fold(jnp.sum(t, axis=0, keepdims=True)) / pixels
    cen = t - mean
    rs = lax.rsqrt(fold(jnp.sum(cen * cen, axis=0, keepdims=True)) / pixels + eps)
    xhat = cen * rs
    pre = xhat * vec_ref[0:1, :] + vec_ref[1:2, :]
    if has_skip:
        pre = pre + skip_ref[...].astype(F32)
    xhat_ref[...] = xhat
    rs_ref[...] = rs
    pre_ref[...] = pre
    res_ref[...] = (pre * jax.nn.sigmoid(pre)).astype(BF)


def out_norm(parts, vec, skip, deps=()):
    half = parts[0].shape[0]
    outs = [
        jax.ShapeDtypeStruct((half, 128), F32),
        jax.ShapeDtypeStruct((1, 128), F32),
        jax.ShapeDtypeStruct((half, 128), F32),
        jax.ShapeDtypeStruct((half, 128), BF),
    ]
    args = (*parts, vec) + (() if skip is None else (skip,))
    body = functools.partial(out_norm_body, len(parts), skip is not None)
    return call(body, outs, [], half * 128 * 10, *args, deps=deps)


def out_back_body(n, *refs):
    parts, (pre_ref, xhat_ref, rs_ref, vec_ref, dpre_ref, dt_ref, sums_ref) = refs[:n], refs[n:]
    g = total_of(parts)
    pre, xhat = pre_ref[...], xhat_ref[...]
    sig = jax.nn.sigmoid(pre)
    dpre = g * (sig * (1.0 + pre * (1.0 - sig)))
    pixels = 2 * pre.shape[0]
    sb = fold(jnp.sum(dpre, axis=0, keepdims=True))
    sg = fold(jnp.sum(dpre * xhat, axis=0, keepdims=True))
    dpre_ref[...] = dpre.astype(BF)
    scale = vec_ref[0:1, :] * rs_ref[...]
    dt_ref[...] = (scale * (dpre - sb / pixels - xhat * (sg / pixels))).astype(BF)
    sums_ref[0:1, :] = sg
    sums_ref[1:2, :] = sb


def out_back(parts, pre, xhat, rs, vec, deps=()):
    half = pre.shape[0]
    outs = [
        jax.ShapeDtypeStruct((half, 128), BF),
        jax.ShapeDtypeStruct((half, 128), BF),
        jax.ShapeDtypeStruct((2, 128), F32),
    ]
    args = (*parts, pre, xhat, rs, vec)
    return call(functools.partial(out_back_body, len(parts)), outs, [], half * 1280, *args, deps=deps)


def conv_back_body(side, rank_ref, *refs):
    slices, (xhat_in, rs_ref, w_ref, lnt_ref, vec_ref, before_ref, after_ref,
             dt_out, ds_out, sums_ref, mate_ref, keep_ref,
             dt_ref, ds_ref, xhat_ref, dy_ref, pad_ref, ktm_ref, sems) = refs[:8], refs[8:]
    half = slices[0].shape[0]
    rank = rank_ref[0]
    nz, _, width = w_ref.shape
    rows = 2 * half
    plane = rows // side
    nf = plane // side
    step = plane // 2
    hc = ds_ref.shape[1]
    ch = dt_ref.shape[1]
    fetched = [
        pltpu.make_async_copy(
            w_ref.at[z, pl.ds(0, hc)], ktm_ref.at[:, pl.ds(z * width, width)], sems.at[z])
        for z in range(nz)
    ]
    xhat_copy = pltpu.make_async_copy(xhat_in, xhat_ref, sems.at[nz])
    for copy in fetched + [xhat_copy]:
        copy.start()
    clear_borders(pad_ref, side, plane, nf)

    def place(k, carry):
        for q, odd, a_ref, b_ref in by_rank(slices, rank):
            top, bottom = halves(odd, a_ref[chunk(k, step), :], b_ref[chunk(k, step), :])
            lanes = pl.ds(pl.multiple_of(128 * q, 128), 128)
            dt_ref[chunk(k, step), lanes] = top.astype(BF)
            dt_ref[pl.ds(pl.multiple_of(half + k * step, 16), step), lanes] = bottom.astype(BF)
        return carry

    lax.fori_loop(0, side, place, 0, unroll=True)
    dt_copy = pltpu.make_async_copy(dt_ref, dt_out, sems.at[nz + 1])
    dt_copy.start()
    xhat_copy.wait()
    gain, bias = vec_ref[0:1, :], vec_ref[1:2, :]

    def hidden_grad(i, sums):
        dt = dt_ref[chunk(i, plane), :]
        early = nn(dt, lnt_ref[0]) * before_ref[0:plane, :]
        late = nn(dt, lnt_ref[2]) * after_ref[0:plane, :]
        dh = nn(dt, lnt_ref[1]) + pltpu.roll(early, plane - 1, 0) + pltpu.roll(late, 1, 0)
        xhat = xhat_ref[i]
        v = xhat * gain + bias
        sig = jax.nn.sigmoid(v)
        dy = dh * (sig * (1.0 + v * (1.0 - sig)))
        dy_ref[i] = dy
        return (
            sums[0] + jnp.sum(dy * xhat, axis=0, keepdims=True),
            sums[1] + jnp.sum(dy, axis=0, keepdims=True),
        )

    zero = jnp.zeros((1, hc), F32)
    sg, sb = lax.fori_loop(0, side, hidden_grad, (zero, zero), unroll=True)
    sums_ref[0:1, :] = sg
    sums_ref[1:2, :] = sb
    scale = gain * rs_ref[...]

    def spatial_grad(i, carry):
        ds = (scale * (dy_ref[i] - sb / rows - xhat_ref[i] * (sg / rows))).astype(BF)
        pad_ref[i + 1, nf : nf + plane] = ds
        ds_ref[chunk(i, plane), :] = ds
        return carry

    lax.fori_loop(0, side, spatial_grad, 0, unroll=True)
    ds_copy = pltpu.make_async_copy(ds_ref, ds_out, sems.at[nz + 2])
    ds_copy.start()
    for copy in fetched:
        copy.wait()
    low = lax.broadcasted_iota(jnp.int32, (step, 128), 1) < 64

    def back(k, carry):
        acc = jnp.zeros((2 * step, ch), F32)
        for t in range(9):
            r, c = 2 - t // 3, 2 - t % 3
            pieces = []
            for kk in (k, k + side):
                at = c * nf + lax.rem(kk, 2) * step
                pieces.append(pad_ref[kk // 2 + r, pl.ds(pl.multiple_of(at, 16), step), :])
            acc += nn(jnp.concatenate(pieces, axis=0), ktm_ref[:, t * ch : (t + 1) * ch])
        store_packed(rank, mate_ref, keep_ref, acc, k, step, low)
        return carry

    lax.fori_loop(0, side, back, 0, unroll=True)
    dt_copy.wait()
    ds_copy.wait()


def conv_back(rank, g, xhat, rs, w, lnt, vec, before, after, side, deps=()):
    half = g[0].shape[0]
    hc = vec.shape[1]
    ch = len(g) * 64
    pixels = 2 * half
    plane = pixels // side
    nf = plane // side
    outs = [
        jax.ShapeDtypeStruct((pixels, ch), BF),
        jax.ShapeDtypeStruct((pixels, hc), BF),
        jax.ShapeDtypeStruct((2, hc), F32),
        jax.ShapeDtypeStruct((4, half, 128), BF),
        jax.ShapeDtypeStruct((4, half, 128), BF),
    ]
    scratch = [
        pltpu.VMEM((pixels, ch), BF),
        pltpu.VMEM((pixels, hc), BF),
        pltpu.VMEM((side, plane, hc), F32),
        pltpu.VMEM((side, plane, hc), F32),
        pltpu.VMEM((side + 2, plane + 2 * nf, hc), BF),
        pltpu.VMEM((hc, 9 * ch), BF),
        pltpu.SemaphoreType.DMA((w.shape[0] + 3,)),
    ]
    flops = 2 * pixels * hc * 12 * ch
    return call(functools.partial(conv_back_body, side), outs, scratch, flops,
                rank, *g, xhat, rs, w, lnt, vec, before, after,
                deps=deps, far=(9, 11), far_outs=(0, 1))


def grads_body(side, pad_ref, hid_ref, ds_ref, dt_ref, before_ref, after_ref, mid_ref, out_ref,
               sg_ref, dst_ref, taps_ref, tg_ref, vec_ref):
    ch = pad_ref.shape[2]
    hc = hid_ref.shape[1]
    plane = hid_ref.shape[0] // side
    nf = plane // side
    for i in (0, 1, side + 2, side + 3):
        dst_ref[i] = jnp.zeros(dst_ref.shape[1:], BF)
    for i in range(side):
        at = slice(i * plane, (i + 1) * plane)
        h = hid_ref[at, :].astype(F32)
        taps_ref[i, 0:hc] = (pltpu.roll(h, 1, 0) * before_ref[0:plane, :]).T.astype(BF)
        taps_ref[i, hc : 2 * hc] = h.T.astype(BF)
        taps_ref[i, 2 * hc : 3 * hc] = (pltpu.roll(h, plane - 1, 0) * after_ref[0:plane, :]).T.astype(BF)
        dst_ref[i + 2] = ds_ref[at, :].astype(F32).T.astype(BF)
    tg_ref[0 : 3 * hc, :] = sum(
        nn(taps_ref[i], dt_ref[i * plane : (i + 1) * plane, :]) for i in range(side)
    )
    tg_ref[3 * hc :, :] = jnp.zeros((tg_ref.shape[0] - 3 * hc, ch), F32)
    nz, _, width = sg_ref.shape
    size = 3 * hc // (2 * nz)
    vec_ref[...] = jnp.zeros(vec_ref.shape, F32)
    vec_ref[size : size + 2, 0:hc] = mid_ref[...]
    vec_ref[size + 2 : size + 4, 0:128] = out_ref[...]
    tall = vec_ref.shape[0]
    inside = lax.broadcasted_iota(jnp.int32, (tall, ch), 0) < size
    off = (width // 2) % 128
    for z in range(nz):
        first, second = [
            jnp.where(inside, tg_ref[b * size : b * size + tall, :], vec_ref[...])
            for b in (2 * z, 2 * z + 1)
        ]
        start = width // 2 - off
        sg_ref[z, hc : hc + tall, 0:ch] = first.astype(BF)
        second = pltpu.roll(jnp.concatenate([second, jnp.zeros((tall, 128), F32)], axis=1), off, 1)
        sg_ref[z, hc : hc + tall, start : start + ch + 128] = second.astype(BF)
    for c in range(3):
        acc = sum(
            nn(dst_ref[i : i + 3].reshape(3 * hc, plane), pad_ref[i, c * nf : c * nf + plane, :])
            for i in range(1, side + 1)
        )
        for r in range(3):
            first = (3 * r + c) * ch
            end = first + ch
            at = (2 - r) * hc
            done = 0
            while first < end:
                z = first // width
                last = min(end, (z + 1) * width)
                sg_ref[z, 0:hc, first - z * width : last - z * width] = (
                    acc[at : at + hc, done : done + last - first].astype(BF)
                )
                done += last - first
                first = last


def kernel_grads(pad, hidden, ds, dt, before, after, mid, out, side, shape, deps=()):
    pixels, hc = hidden.shape
    ch = dt.shape[1]
    plane = pixels // side
    outs = [jax.ShapeDtypeStruct(shape, BF)]
    tall = shape[1] - hc
    scratch = [
        pltpu.VMEM((side + 4, hc, plane), BF),
        pltpu.VMEM((side, 3 * hc, plane), BF),
        pltpu.VMEM((3 * hc + tall, ch), F32),
        pltpu.VMEM((tall, ch), F32),
    ]
    flops = 2 * pixels * hc * 12 * ch
    return call(functools.partial(grads_body, side), outs, scratch, flops,
                pad, hidden, ds, dt, before, after, mid, out, deps=deps)[0]


def copy_after_body(v_ref, out_ref):
    out_ref[...] = v_ref[...]


def after_all(v, *deps):
    return call(copy_after_body, [jax.ShapeDtypeStruct(v.shape, v.dtype)], [], v.size, v, deps=deps)[0]


def pack_kernels_body(kt_ref, lt_ref, vec_ref, out_ref, low_ref):
    ranks, _, width = out_ref.shape
    hc = kt_ref.shape[0] // ranks
    blocks = lt_ref.shape[0] // hc
    q = hc // ranks
    low_ref[...] = jnp.zeros(low_ref.shape, F32)
    for r in range(ranks):
        out_ref[r, 0:hc, :] = kt_ref[r * hc : (r + 1) * hc, :]
        for b in range(blocks):
            low_ref[r, b * q : (b + 1) * q, 0 : lt_ref.shape[1]] = (
                lt_ref[b * hc + r * q : b * hc + (r + 1) * q, :]
            )
        low_ref[r, blocks * q : blocks * q + 1, :] = vec_ref[...]
        out_ref[r, hc:, :] = low_ref[r].astype(BF)


def pack_kernels(kt, lt, vec, ranks, tall, deps):
    width = kt.shape[1]
    outs = [jax.ShapeDtypeStruct((ranks, kt.shape[0] // ranks + tall, width), BF)]
    scratch = [pltpu.VMEM((ranks, tall, width), F32)]
    return call(pack_kernels_body, outs, scratch, kt.size * 8, kt, lt, vec, deps=deps)[0]


def two_blocks(v_ref, width):
    off = width % 128
    second = v_ref[:, width - off : 2 * width].astype(F32)
    return v_ref[:, 0:width], pltpu.roll(second, width, 1)[:, 0:width].astype(BF)


def stack_sections_body(count, *refs):
    out_ref, sections = refs[-1], refs[:-1]
    out_ref[...] = jnp.zeros(out_ref.shape, BF)
    for s, ref in enumerate(sections):
        first, second = two_blocks(ref, out_ref.shape[2])
        out_ref[count - len(sections) + s] = first
        out_ref[2 * count - len(sections) + s] = second


def stack_sections(sections, count, deps):
    high, width = sections[0].shape
    outs = [jax.ShapeDtypeStruct((2 * count, high, width // 2), BF)]
    return call(functools.partial(stack_sections_body, count), outs, [], high * width * 8, *sections,
                deps=deps)[0]


def near_far_body(y_ref, v_ref, near_ref, far_ref):
    first, second = two_blocks(v_ref, near_ref.shape[1])
    here = y_ref[0] == 0
    near_ref[...] = jnp.where(here, first, second)
    far_ref[...] = jnp.where(here, second, first)


def near_far(y, v, deps):
    high, width = v.shape
    outs = [jax.ShapeDtypeStruct((high, width // 2), BF)] * 2
    return call(near_far_body, outs, [], high * width * 4, y, v, deps=deps)


def hop(v, k):
    n = 1
    for name in EVERY:
        n *= lax.axis_size(name)
    return lax.ppermute(v, EVERY, [(i, i ^ k) for i in range(n)])


def plane_gather(v, aside=()):
    got = {0: v}
    for k in (6, 2, 4):
        got[k] = hop(v, k)
    got[1] = hop(after_all(v, *aside) if aside else v, 1)
    for k in (2, 4, 6):
        got[k ^ 1] = hop(got[k], 1)
    return [got[k] for k in range(8)]


def plane_reduce(mate, keep, deps=()):
    sums = pair_sum(keep, hop(mate, 1), deps)
    arrived = {k: hop(sums[k // 2], k) for k in (6, 2, 4)}
    return [sums[0], arrived[2], arrived[4], arrived[6]]


def to_section(near, far, section, n_seg):
    n = 2 * n_seg * lax.axis_size("z")
    got = []
    for base, block in ((0, near), (n_seg, far)):
        row = []
        for low in range(n_seg):
            k = base + (low ^ section)
            if k == 0:
                row.append(block)
            else:
                pairs = [(i, i ^ k) for i in range(n) if i % n_seg == low]
                row.append(lax.ppermute(block, EVERY, pairs))
        got.append(jnp.stack(row))
    same, other = got
    first = lax.axis_index("y") == 0
    return jnp.where(first, jnp.concatenate([same, other]), jnp.concatenate([other, same]))


def on_device(frames, cot, starts, ks, ktm, mg, mb, og, ob):
    nz, n_rank, n_seg = lax.axis_size("z"), 8, 4
    n_dp = nz * 2
    fr, side, ch = frames.shape[0], frames.shape[1], frames.shape[3]
    area = side * side
    hid = ks.shape[2]
    hc, cc = hid // n_rank, ch // n_rank
    q = hc // n_rank
    rank = lax.axis_index(PLANE)
    rank_now = rank.astype(jnp.int32).reshape(1)
    d_index = lax.axis_index(("z", "y"))
    nf = n_dp * fr
    pixels = area * nf
    half = pixels // 2

    to_plane = [(d * n_seg + s, s * n_rank + d) for d in range(n_dp) for s in range(n_seg)]
    from_plane = [(b, a) for a, b in to_plane]
    rows = fr * area
    flag_row = jnp.pad(starts.astype(BF)[None], ((0, 11), (0, ch - fr)))
    moving = jnp.concatenate([frames.reshape(rows, ch), flag_row], axis=0)
    moving = lax.ppermute(moving, EVERY, to_plane)

    perm = (jnp.arange(hid).reshape(n_rank, n_rank, q).transpose(1, 0, 2).reshape(hid)[:, None]
            == jnp.arange(hid)[None, :]).astype(BF)
    kt = lax.dot_general(perm, ks[0].astype(BF), (((1,), (1,)), ((), ())),
                         preferred_element_type=F32).astype(BF)
    lrows, width = ktm.shape[1] // n_rank, ks.shape[1]
    tall = -(-(lrows + 4) // 16) * 16
    extra = jnp.concatenate([mg, mb, og, ob], axis=1)
    extra = jnp.pad(extra, ((0, 0), (0, width - extra.shape[1])))
    w = pack_kernels(kt, ktm[0], extra, n_rank, tall, deps=(moving,))
    w = lax.all_to_all(w, PLANE, 0, 0)
    here = w
    high = hc + tall

    w = w.reshape(2, n_seg, high, width).transpose(1, 2, 0, 3).reshape(n_seg, high, 2 * width)
    ws = [lax.all_gather(w[s], "z", axis=0) for s in range(n_seg)]

    moving = after_all(moving, here)
    gathered = lax.all_to_all(jnp.broadcast_to(moving, (n_rank, *moving.shape)), PLANE, 0, 0)

    def norm_rows(rows_now):
        row = rows_now[:, (lrows - tall) % 16].reshape(n_dp, width).astype(F32)
        mid = jnp.stack([
            lax.dynamic_slice_in_dim(row[:, i * hc : (i + 1) * hc], rank * q, q, axis=1).reshape(hc)
            for i in range(2)])
        own = lax.dynamic_index_in_dim(row, rank, 0, keepdims=False)
        out = jnp.stack([
            jnp.tile(own[2 * hc + i * cc : 2 * hc + (i + 1) * cc], 2) for i in range(2)])
        return mid, out

    moving = after_all(moving, here)
    gathered = lax.all_to_all(jnp.broadcast_to(moving, (n_rank, *moving.shape)), PLANE, 0, 0)
    mids, outs = [], []
    for s in range(n_seg):
        row = ws[s][:, hc + lrows].reshape(n_dp, width).astype(F32)
        mids.append(jnp.stack([
            lax.dynamic_slice_in_dim(row[:, i * hc : (i + 1) * hc], rank * q, q, axis=1).reshape(hc)
            for i in range(2)]))
        own = lax.dynamic_index_in_dim(row, rank, 0, keepdims=False)
        outs.append(jnp.stack([
            jnp.tile(own[2 * hc + i * cc : 2 * hc + (i + 1) * cc], 2) for i in range(2)]))

    def by_pixel(v):
        width = v.shape[2]
        v = v.reshape(n_rank * fr, area, width).transpose(1, 0, 2)
        return v.reshape(pixels, width)

    def packed(v):
        return jnp.concatenate([v[:half], v[half:]], axis=1)

    a0 = by_pixel(gathered[:, :rows])
    flags = gathered[:, rows, :fr].reshape(nf) > 0.5
    slot = jnp.arange(nf) % fr
    before = jnp.where(flags | (slot == 0), 0.0, 1.0)
    after = jnp.where(jnp.roll(flags, -1) | (slot == fr - 1), 0.0, 1.0)
    spread = (side * nf + nf, hc)
    before = jnp.broadcast_to(jnp.tile(before, side + 1)[:, None], spread)
    after = jnp.broadcast_to(jnp.tile(after, side + 1)[:, None], spread)
    skip = packed(lax.dynamic_slice_in_dim(a0, rank * cc, cc, axis=1))

    def across(*slices):
        n = len(slices)
        v = jnp.stack([jnp.concatenate([v[:, :cc], v[:, cc:]], axis=0) for v in slices])
        v = v.reshape(n, area, n_rank, fr, cc).transpose(2, 0, 1, 3, 4).reshape(n_rank, n * rows, cc)
        return lax.all_to_all(v, PLANE, 0, 0)

    def home(v, after):
        n = v.shape[1] // rows
        v = v.transpose(1, 0, 2).reshape(n * rows, ch)
        v = after_all(lax.ppermute(v, EVERY, from_plane), after)
        v = v.reshape(n, area, fr, ch).transpose(0, 2, 1, 3)
        return v.reshape(n, *frames.shape)

    saved = []
    g = [a0]
    ready = prepare(ws[0], hc, ch)
    for s in range(n_seg):
        kn, lt, lnt, rows_now = ready
        mid, out = norm_rows(rows_now)
        pad, hidden, xm, rm, mate, keep = conv_forward(
            rank_now, g, kn, lt, mid, before, after, side, pixels, ch)
        parts = plane_reduce(mate, keep)
        deps = ()
        if s == 0:
            cot_moving = lax.ppermute(after_all(cot.reshape(rows, ch), kn), EVERY, to_plane)
            cot_moving = cot_moving.reshape(rows, n_rank, cc).transpose(1, 0, 2)
        if s == n_seg - 1:
            cot_own = lax.all_to_all(after_all(cot_moving, parts[0]), PLANE, 0, 0)
            deps = (cot_own,)
        xo, ro, pre, res = out_norm(parts, out, skip if s % 2 == 1 else None, deps=deps)
        saved.append((pad, hidden, xm, rm, xo, ro, pre, lnt, mid, out))
        if s % 2 == 1:
            skip = res
        if s < n_seg - 1:
            ready = prepare(ws[s + 1], hc, ch, deps=(res, cot_moving) if s == 1 else (res,))
            g = plane_gather(res, ready[:1])
    cot_own = packed(by_pixel(cot_own))

    parts = [cot_own]
    skip_grad = None

    grads, raw = [], None
    for s in reversed(range(n_seg)):
        pad, hidden, xm, rm, xo, ro, pre, lnt, mid, out = saved[s]
        if s == 1:
            parts = parts + [skip_grad]
        deps = () if raw is None else (raw, *grads[len(grads) - 1 :])
        dpre, dt, osum = out_back(parts, pre, xo, ro, out, deps=deps)
        if raw is not None:
            grads.append(lax.psum_scatter(after_all(raw, dt), "z", scatter_dimension=0))
        if s % 2 == 1:
            skip_grad = dpre
        dtf, ds, msum, mate, keep = conv_back(
            rank_now, plane_gather(dt), xm, rm, ws[s], lnt, mid, before, after, side)
        if s > 0:
            parts = plane_reduce(mate, keep)
        raw = kernel_grads(pad, hidden, ds, dtf, before, after, msum, osum, side, ws[s].shape,
                           deps=parts[:1] if s > 0 else ())
    last = lax.psum_scatter(raw, "z", scatter_dimension=0)
    parts = plane_reduce(mate, keep, deps=(raw,))

    da = sum(p.astype(F32) for p in parts) + skip_grad.astype(F32)
    exchanged = across(res, da.astype(BF))

    early = lax.all_to_all(stack_sections(grads[::-1], n_seg, (exchanged,)), PLANE, 0, 0)
    output, frames_grad = home(exchanged, early)
    frames_grad = frames_grad.astype(F32)
    y = lax.axis_index("y").astype(jnp.int32).reshape(1)
    last = to_section(*near_far(y, last, (early,)), 0, n_seg)
    g = jnp.where(lax.axis_index(("x", "c")) == 0, last, early)
    space_grad = lax.dot_general(g[:, :hc].reshape(hid, width), perm, (((0,), (0,)), ((), ())),
                                 preferred_element_type=F32)
    tg = g[:, hc : hc + lrows, :ch].reshape(n_rank, -1, q, ch)
    time_grad = tg.transpose(1, 0, 2, 3).reshape(-1, ch).astype(F32)
    sums = g[:, hc + lrows : hc + lrows + 4].astype(F32)

    def mid_own(v):
        return lax.dynamic_slice_in_dim(v[:, :hc], d_index * q, q, axis=1).reshape(1, hc)

    own = lax.dynamic_index_in_dim(sums, d_index, 0, keepdims=False)
    return (
        output,
        frames_grad,
        space_grad[None],
        time_grad[None],
        mid_own(sums[:, 0]),
        mid_own(sums[:, 1]),
        own[2:3, :cc],
        own[3:4, :cc],
    )


def from_behind(value, axis, steps):
    count = lax.axis_size(axis)
    leading, last = (max(0, -steps), min(count, count - steps))
    return lax.ppermute(value, axis, [(source, source + steps) for source in range(leading, last)])


def space_apply(current, kernel):
    frame_side = current.shape[1]
    padded = jnp.pad(current, ((0, 0), (1, 1), (1, 1), (0, 0)))
    stacked = jnp.concatenate(
        [
            padded[:, row_shift : row_shift + frame_side, col_shift : col_shift + frame_side, :]
            for row_shift in range(3)
            for col_shift in range(3)
        ],
        axis=-1,
    )
    return (
        stacked,
        jnp.einsum("fijc,co->fijo", stacked, kernel, preferred_element_type=jnp.float32),
    )


def space_back(gradient, kernel):
    frame_side = gradient.shape[1]
    channels = kernel.shape[0] // 9
    spread = jnp.einsum("fijo,co->fijc", gradient, kernel, preferred_element_type=jnp.float32)
    total = jnp.zeros((gradient.shape[0], frame_side + 2, frame_side + 2, channels), jnp.float32)
    for tap_index in range(9):
        row_shift = tap_index // 3
        col_shift = tap_index % 3
        piece_now = spread[..., tap_index * channels : (tap_index + 1) * channels]
        total = total + jnp.pad(
            piece_now, ((0, 0), (row_shift, 2 - row_shift), (col_shift, 2 - col_shift), (0, 0))
        )
    return total[:, 1 : frame_side + 1, 1 : frame_side + 1, :]


def time_apply(current, kernel, before_mask, after_mask):
    blanks = jnp.zeros_like(current[:1])
    earlier = jnp.concatenate([blanks, current[:-1]], axis=0) * before_mask[
        :, None, None, None
    ].astype(current.dtype)
    later = jnp.concatenate([current[1:], blanks], axis=0) * after_mask[:, None, None, None].astype(
        current.dtype
    )
    stacked = jnp.concatenate([earlier, current, later], axis=-1)
    return (
        stacked,
        jnp.einsum("fijc,co->fijo", stacked, kernel, preferred_element_type=jnp.float32),
    )


def time_back(gradient, kernel, before_mask, after_mask):
    channels = kernel.shape[0] // 3
    spread = jnp.einsum("fijo,co->fijc", gradient, kernel, preferred_element_type=jnp.float32)
    early_part = spread[..., :channels] * before_mask[:, None, None, None]
    late_part = spread[..., 2 * channels :] * after_mask[:, None, None, None]
    blanks = jnp.zeros_like(early_part[:1])
    moved_early = jnp.concatenate([early_part[1:], blanks], axis=0)
    moved_late = jnp.concatenate([blanks, late_part[:-1]], axis=0)
    return spread[..., channels : 2 * channels] + moved_early + moved_late


def moments(values, pixel_count):
    average = lax.psum(jnp.sum(values, axis=(0, 1, 2)), "dp") / pixel_count
    centered = values - average
    spread = lax.psum(jnp.sum(centered * centered, axis=(0, 1, 2)), "dp") / pixel_count
    return (average, lax.rsqrt(spread + eps))


def reduce_back(gradient, normed):
    return lax.psum(
        (jnp.sum(gradient, axis=(0, 1, 2)), jnp.sum(gradient * normed, axis=(0, 1, 2))), "dp"
    )


def silu_slope(values):
    sigmoid_now = jax.nn.sigmoid(values)
    return sigmoid_now * (1.0 + values * (1.0 - sigmoid_now))


def pick_slot(stack, slot_index):
    return lax.dynamic_index_in_dim(stack, slot_index, 0, keepdims=False)


def store_slot(stack, value, slot_index, usable):
    previous = pick_slot(stack, slot_index)
    return lax.dynamic_update_index_in_dim(stack, jnp.where(usable, value, previous), slot_index, 0)


def on_device_general(
    frames, cotangent, starts, space_kernel, time_kernel, mid_gain, mid_bias, out_gain, out_bias
):
    n_segment = lax.axis_size("segment")
    n_data = lax.axis_size("dp")
    segment_index = lax.axis_index("segment")
    odd_segment = segment_index % 2 == 1
    last_segment = segment_index == n_segment - 1
    first_segment = segment_index == 0
    frame_count = frames.shape[0]
    frame_side = frames.shape[1]
    channels = frames.shape[3]
    hidden_units = mid_gain.shape[1] * n_data
    pixel_count = n_data * frame_count * frame_side * frame_side
    turns = 2 * n_segment - 1
    block_shape = (n_segment,) + frames.shape
    all_frames, all_cot, all_starts = (
        lax.all_gather(frames, "segment", axis=0, tiled=True),
        lax.all_gather(cotangent, "segment", axis=0, tiled=True),
        lax.all_gather(starts.astype(jnp.bfloat16), "segment", axis=0, tiled=True),
    )
    frame_stack = all_frames.reshape(block_shape)
    cot_stack = all_cot.reshape(block_shape)
    clip_flags = all_starts.astype(jnp.float32).reshape(n_segment, frame_count)
    positions = jnp.arange(frame_count)
    before_mask = jnp.where((clip_flags > 0.5) | (positions == 0), 0.0, 1.0)
    following = jnp.concatenate([clip_flags[:, 1:], jnp.ones((n_segment, 1), jnp.float32)], axis=1)
    after_mask = jnp.where(following > 0.5, 0.0, 1.0)
    gathered = (
        lax.all_gather(space_kernel[0].astype(jnp.bfloat16), "dp", axis=0, tiled=True),
        lax.all_gather(time_kernel[0].astype(jnp.bfloat16), "dp", axis=0, tiled=True),
        lax.all_gather(mid_gain[0].astype(jnp.bfloat16), "dp", axis=0, tiled=True),
        lax.all_gather(mid_bias[0].astype(jnp.bfloat16), "dp", axis=0, tiled=True),
        lax.all_gather(out_gain[0].astype(jnp.bfloat16), "dp", axis=0, tiled=True),
        lax.all_gather(out_bias[0].astype(jnp.bfloat16), "dp", axis=0, tiled=True),
    )
    space_low, time_low = (gathered[0], gathered[1])
    mid_gain_now = gathered[2].astype(jnp.float32)
    mid_bias_now = gathered[3].astype(jnp.float32)
    out_gain_now = gathered[4].astype(jnp.float32)
    out_bias_now = gathered[5].astype(jnp.float32)
    incoming = jnp.zeros_like(frames)
    carried = jnp.zeros_like(frames)
    kept_input = jnp.zeros(block_shape, jnp.bfloat16)
    kept_skip = jnp.zeros(block_shape, jnp.bfloat16)
    kept_mid_mean = jnp.zeros((n_segment, hidden_units), jnp.float32)
    kept_mid_scale = jnp.zeros((n_segment, hidden_units), jnp.float32)
    kept_out_mean = jnp.zeros((n_segment, channels), jnp.float32)
    kept_out_scale = jnp.zeros((n_segment, channels), jnp.float32)
    results = jnp.zeros(block_shape, jnp.float32)
    for turn_index in range(turns):
        micro_index = turn_index - segment_index
        usable = (micro_index >= 0) & (micro_index < n_segment)
        slot_index = jnp.clip(micro_index, 0, n_segment - 1)
        current = jnp.where(first_segment, pick_slot(frame_stack, slot_index), incoming)
        skip_input = carried
        _, spatial = space_apply(current, space_low)
        mid_mean, mid_scale = moments(spatial, pixel_count)
        hidden_act = jax.nn.silu(
            (spatial - mid_mean) * mid_scale * mid_gain_now + mid_bias_now
        ).astype(jnp.bfloat16)
        _, temporal = time_apply(
            hidden_act,
            time_low,
            pick_slot(before_mask, slot_index),
            pick_slot(after_mask, slot_index),
        )
        out_mean, out_scale = moments(temporal, pixel_count)
        pre_act = (
            (temporal - out_mean) * out_scale * out_gain_now
            + out_bias_now
            + jnp.where(odd_segment, skip_input.astype(jnp.float32), 0.0)
        )
        result = jax.nn.silu(pre_act).astype(jnp.bfloat16)
        kept_input = store_slot(kept_input, current, slot_index, usable)
        kept_skip = store_slot(kept_skip, skip_input, slot_index, usable)
        kept_mid_mean = store_slot(kept_mid_mean, mid_mean, slot_index, usable)
        kept_mid_scale = store_slot(kept_mid_scale, mid_scale, slot_index, usable)
        kept_out_mean = store_slot(kept_out_mean, out_mean, slot_index, usable)
        kept_out_scale = store_slot(kept_out_scale, out_scale, slot_index, usable)
        results = store_slot(results, result.astype(jnp.float32), slot_index, usable)
        if turn_index < turns - 1:
            incoming, carried = from_behind(
                (result, jnp.where(odd_segment, result, current)), "segment", 1
            )
    gathered = (
        lax.all_gather(space_kernel[0].astype(jnp.bfloat16), "dp", axis=0, tiled=True),
        lax.all_gather(time_kernel[0].astype(jnp.bfloat16), "dp", axis=0, tiled=True),
        lax.all_gather(mid_gain[0].astype(jnp.bfloat16), "dp", axis=0, tiled=True),
        lax.all_gather(mid_bias[0].astype(jnp.bfloat16), "dp", axis=0, tiled=True),
        lax.all_gather(out_gain[0].astype(jnp.bfloat16), "dp", axis=0, tiled=True),
        lax.all_gather(out_bias[0].astype(jnp.bfloat16), "dp", axis=0, tiled=True),
    )
    space_low, time_low = (gathered[0], gathered[1])
    mid_gain_now = gathered[2].astype(jnp.float32)
    mid_bias_now = gathered[3].astype(jnp.float32)
    out_gain_now = gathered[4].astype(jnp.float32)
    out_bias_now = gathered[5].astype(jnp.float32)
    grad_input = jnp.zeros_like(frames)
    grad_skip = jnp.zeros_like(frames)
    space_acc = jnp.zeros(space_low.shape, jnp.float32)
    time_acc = jnp.zeros(time_low.shape, jnp.float32)
    mid_gain_acc = jnp.zeros((hidden_units,), jnp.float32)
    mid_bias_acc = jnp.zeros((hidden_units,), jnp.float32)
    out_gain_acc = jnp.zeros((channels,), jnp.float32)
    out_bias_acc = jnp.zeros((channels,), jnp.float32)
    input_grads = jnp.zeros(block_shape, jnp.float32)
    for turn_index in range(turns):
        micro_index = n_segment - 1 - (turn_index - (n_segment - 1 - segment_index))
        usable = (micro_index >= 0) & (micro_index < n_segment)
        usable_weight = usable.astype(jnp.float32)
        slot_index = jnp.clip(micro_index, 0, n_segment - 1)
        current = pick_slot(kept_input, slot_index)
        skip_input = pick_slot(kept_skip, slot_index)
        before_now = pick_slot(before_mask, slot_index)
        after_now = pick_slot(after_mask, slot_index)
        space_taps, spatial = space_apply(current, space_low)
        mid_normed = (spatial - pick_slot(kept_mid_mean, slot_index)) * pick_slot(
            kept_mid_scale, slot_index
        )
        mid_pre = mid_normed * mid_gain_now + mid_bias_now
        hidden_act = jax.nn.silu(mid_pre).astype(jnp.bfloat16)
        time_taps, temporal = time_apply(hidden_act, time_low, before_now, after_now)
        out_scale = pick_slot(kept_out_scale, slot_index)
        out_normed = (temporal - pick_slot(kept_out_mean, slot_index)) * out_scale
        pre_act = (
            out_normed * out_gain_now
            + out_bias_now
            + jnp.where(odd_segment, skip_input.astype(jnp.float32), 0.0)
        )
        grad_result = jnp.where(
            last_segment,
            pick_slot(cot_stack, slot_index).astype(jnp.float32),
            grad_input.astype(jnp.float32)
            + jnp.where(odd_segment, grad_skip.astype(jnp.float32), 0.0),
        )
        grad_pre = grad_result * silu_slope(pre_act)
        out_bias_sum, out_gain_sum = reduce_back(grad_pre, out_normed)
        grad_temporal = (
            out_gain_now
            * out_scale
            * (grad_pre - out_bias_sum / pixel_count - out_normed * out_gain_sum / pixel_count)
        ).astype(jnp.bfloat16)
        time_acc = time_acc + usable_weight * jnp.einsum(
            "fijc,fijo->co", time_taps, grad_temporal, preferred_element_type=jnp.float32
        )
        grad_hidden = time_back(grad_temporal, time_low, before_now, after_now)
        grad_mid = grad_hidden * silu_slope(mid_pre)
        mid_bias_sum, mid_gain_sum = reduce_back(grad_mid, mid_normed)
        mid_scale = pick_slot(kept_mid_scale, slot_index)
        grad_spatial = (
            mid_gain_now
            * mid_scale
            * (grad_mid - mid_bias_sum / pixel_count - mid_normed * mid_gain_sum / pixel_count)
        ).astype(jnp.bfloat16)
        space_acc = space_acc + usable_weight * jnp.einsum(
            "fijc,fijo->co", space_taps, grad_spatial, preferred_element_type=jnp.float32
        )
        grad_current = space_back(grad_spatial, space_low)
        mid_gain_acc = mid_gain_acc + usable_weight * mid_gain_sum
        mid_bias_acc = mid_bias_acc + usable_weight * mid_bias_sum
        out_gain_acc = out_gain_acc + usable_weight * out_gain_sum
        out_bias_acc = out_bias_acc + usable_weight * out_bias_sum
        input_grads = store_slot(
            input_grads, grad_current + grad_skip.astype(jnp.float32), slot_index, usable
        )
        if turn_index < turns - 1:
            grad_input, grad_skip = from_behind(
                (
                    grad_current.astype(jnp.bfloat16),
                    jnp.where(odd_segment, grad_pre.astype(jnp.bfloat16), grad_skip),
                ),
                "segment",
                -1,
            )
    space_grad, time_grad = (
        lax.psum_scatter(space_acc, "dp", scatter_dimension=0, tiled=True),
        lax.psum_scatter(time_acc, "dp", scatter_dimension=0, tiled=True),
    )
    data_index = lax.axis_index("dp")

    def own_share(full_vector):
        share = full_vector.shape[0] // n_data
        return lax.dynamic_slice_in_dim(full_vector, data_index * share, share)[None]

    flat_shape = (n_segment * frame_count,) + frames.shape[1:]
    arrived_out, arrived_grads = (
        lax.all_to_all(
            results.reshape(flat_shape).astype(jnp.bfloat16),
            "segment",
            split_axis=0,
            concat_axis=0,
            tiled=True,
        ).astype(jnp.float32),
        lax.all_to_all(
            input_grads.reshape(flat_shape).astype(jnp.bfloat16),
            "segment",
            split_axis=0,
            concat_axis=0,
            tiled=True,
        ).astype(jnp.float32),
    )
    output = arrived_out[(n_segment - 1) * frame_count :].astype(jnp.bfloat16)
    frames_grad = arrived_grads[:frame_count]
    return (
        output,
        frames_grad,
        space_grad[None],
        time_grad[None],
        own_share(mid_gain_acc),
        own_share(mid_bias_acc),
        own_share(out_gain_acc),
        own_share(out_bias_acc),
    )


def general(mesh):
    return jax.shard_map(
        on_device_general,
        mesh=mesh,
        in_specs=(
            P(("dp", "segment"), None, None, None),
            P(("dp", "segment"), None, None, None),
            P(("dp", "segment")),
            P("segment", "dp", None),
            P("segment", "dp", None),
            P("segment", "dp"),
            P("segment", "dp"),
            P("segment", "dp"),
            P("segment", "dp"),
        ),
        out_specs=(
            P(("dp", "segment"), None, None, None),
            P(("dp", "segment"), None, None, None),
            P("segment", "dp", None),
            P("segment", "dp", None),
            P("segment", "dp"),
            P("segment", "dp"),
            P("segment", "dp"),
            P("segment", "dp"),
        ),
        check_vma=False,
    )


def solution(mesh):
    if mesh.shape["dp"] != 8 or mesh.shape["segment"] != 4:
        return general(mesh)
    n_dp, n_seg = mesh.shape["dp"], mesh.shape["segment"]
    fine = Mesh(mesh.devices.reshape(n_dp // 2, 2, 2, n_seg // 2), EVERY)
    dp, seg = ("z", "y"), ("x", "c")
    return jax.shard_map(
        on_device,
        mesh=fine,
        in_specs=(
            P(EVERY, None, None, None),
            P(EVERY, None, None, None),
            P(EVERY),
            P(seg, dp, None),
            P(seg, dp, None),
            P(seg, dp),
            P(seg, dp),
            P(seg, dp),
            P(seg, dp),
        ),
        out_specs=(
            P(EVERY, None, None, None),
            P(EVERY, None, None, None),
            P(seg, dp, None),
            P(seg, dp, None),
            P(seg, dp),
            P(seg, dp),
            P(seg, dp),
            P(seg, dp),
        ),
        check_vma=False,
    )
```

```python
import functools

import jax
import jax.numpy as jnp
from jax import lax
from jax.experimental import pallas as pl
from jax.experimental.pallas import tpu as pltpu
from jax.sharding import Mesh, PartitionSpec as P

eps = 1e-05
PLANE = ("y", "x", "c")
EVERY = ("z", "y", "x", "c")
BF = jnp.bfloat16
F32 = jnp.float32


def nt(a, b):
    return lax.dot_general(a, b, (((1,), (1,)), ((), ())), preferred_element_type=F32)


def nn(a, b):
    return lax.dot_general(a, b, (((1,), (0,)), ((), ())), preferred_element_type=F32)


VMEM_CAP = 56 * 1024 * 1024
ANY = pl.BlockSpec(memory_space=pl.ANY)


def call(body, outs, scratch, flops, *args, deps=(), far=(), far_outs=()):
    moved = sum(a.size * a.dtype.itemsize for a in args) + sum(
        o.size * o.dtype.itemsize for o in outs
    )
    n = len(deps)

    def spec(a):
        return pl.BlockSpec(memory_space=pltpu.SMEM if a.dtype == jnp.int32 else pltpu.VMEM)

    return pl.pallas_call(
        lambda *refs: body(*refs[n:]),
        out_shape=outs,
        in_specs=[ANY] * n + [ANY if i in far else spec(a) for i, a in enumerate(args)],
        out_specs=[ANY if i in far_outs else spec(o) for i, o in enumerate(outs)],
        scratch_shapes=scratch,
        compiler_params=pltpu.CompilerParams(vmem_limit_bytes=VMEM_CAP),
        cost_estimate=pl.CostEstimate(flops=flops, bytes_accessed=moved, transcendentals=0),
    )(*deps, *args)


def chunk(i, size):
    return pl.ds(pl.multiple_of(i * size, 16), size)


def clear_borders(pad_ref, side, plane, nf):
    zrow = jnp.zeros(pad_ref.shape[1:], BF)
    pad_ref[0] = zrow
    pad_ref[side + 1] = zrow
    zcol = jnp.zeros((nf, pad_ref.shape[2]), BF)
    for i in range(side):
        pad_ref[i + 1, 0:nf] = zcol
        pad_ref[i + 1, nf + plane : 2 * nf + plane] = zcol


def by_rank(slices, rank):
    odd = lax.rem(rank, 2) == 1
    for p in range(len(slices) // 2):
        a, b = slices[2 * p], slices[2 * p + 1]
        yield lax.bitwise_xor(rank // 2, p), odd, a, b


def halves(odd, own, mate):
    low = lax.broadcasted_iota(jnp.int32, own.shape, 1) < 64
    own, mate = own.astype(F32), mate.astype(F32)
    a, b = jnp.where(odd, mate, own), jnp.where(odd, own, mate)
    top = jnp.where(low, a, pltpu.roll(b, 64, 1))
    bottom = jnp.where(low, pltpu.roll(a, 64, 1), b)
    return top, bottom


def store_packed(rank, mate_ref, keep_ref, part, k, step, low):
    rows_now = chunk(k, step)
    odd = lax.rem(rank, 2) == 1
    for q in range(keep_ref.shape[0]):
        x = part[:step, 128 * q : 128 * q + 128]
        y = part[step:, 128 * q : 128 * q + 128]
        even_slice = jnp.where(low, x, pltpu.roll(y, 64, 1))
        odd_slice = jnp.where(low, pltpu.roll(x, 64, 1), y)
        p = lax.bitwise_xor(rank // 2, q)
        keep_ref[p, rows_now, :] = jnp.where(odd, odd_slice, even_slice).astype(BF)
        mate_ref[p, rows_now, :] = jnp.where(odd, even_slice, odd_slice).astype(BF)


def fetch_kernels(w_ref, ktm_ref, lw_ref, sems):
    nz, _, width = w_ref.shape
    hc = ktm_ref.shape[0]
    copies = []
    for z in range(nz):
        copies.append(pltpu.make_async_copy(
            w_ref.at[z, pl.ds(0, hc)], ktm_ref.at[:, pl.ds(z * width, width)], sems.at[2 * z]))
        copies.append(pltpu.make_async_copy(
            w_ref.at[z, pl.ds(hc, lw_ref.shape[1])], lw_ref.at[z], sems.at[2 * z + 1]))
    for copy in copies:
        copy.start()
    return copies


def join_temporal(lw_ref, lf_ref, ltm_ref):
    ch = ltm_ref.shape[1]
    width = lw_ref.shape[2] // 2
    count = 2 * lw_ref.shape[0]
    size = ltm_ref.shape[0] // count
    for z in range(lw_ref.shape[0]):
        first = lw_ref[z, :, 0:ch].astype(F32)
        off = width % 128
        second = lw_ref[z, :, width - off : width - off + ch + 128].astype(F32)
        second = pltpu.roll(second, ch + 128 - off, 1)[:, 0:ch]
        for b, block in ((2 * z, first), (2 * z + 1, second)):
            lf_ref[b * size : b * size + block.shape[0], :] = block
    ltm_ref[...] = lf_ref[0 : ltm_ref.shape[0], :].astype(BF)


def prepare_body(w_ref, kn_out, l_out, lt_out, rows_out, ktm_ref, lw_ref, lf_ref, sems):
    hc, ch = ktm_ref.shape[0], l_out.shape[1]
    for copy in fetch_kernels(w_ref, ktm_ref, lw_ref, sems):
        copy.wait()
    for t in range(9):
        kn_out[t] = ktm_ref[:, t * ch : (t + 1) * ch].astype(F32).T.astype(BF)
    join_temporal(lw_ref, lf_ref, l_out)
    rows_out[...] = lw_ref[:, lw_ref.shape[1] - rows_out.shape[1] :, :]
    for t in range(3):
        lt_out[t] = lf_ref[t * hc : (t + 1) * hc].T.astype(BF)


def prepare(w, hc, ch, deps=()):
    outs = [
        jax.ShapeDtypeStruct((9, ch, hc), BF),
        jax.ShapeDtypeStruct((3 * hc, ch), BF),
        jax.ShapeDtypeStruct((3, ch, hc), BF),
        jax.ShapeDtypeStruct((w.shape[0], 16, w.shape[2]), BF),
    ]
    tall = w.shape[1] - hc
    scratch = [
        pltpu.VMEM((hc, 9 * ch), BF),
        pltpu.VMEM((w.shape[0], tall, w.shape[2]), BF),
        pltpu.VMEM((3 * hc + tall, ch), F32),
        pltpu.SemaphoreType.DMA((2 * w.shape[0],)),
    ]
    return call(prepare_body, outs, scratch, 2 * w.size * 512, w, deps=deps, far=(0,))


def conv_body(side, first, rank_ref, *refs):
    n = 1 if first else 8
    slices = refs[:n]
    (kn_in, ltm_ref, vec_ref, before_ref, after_ref,
     pad_out, hid_out, xhat_out, rs_ref, mate_ref, keep_ref,
     pad_ref, hid_ref, xhat_ref, sp_ref, kn_ref, sems) = refs[n:]
    rank = rank_ref[0]
    kn_copy = pltpu.make_async_copy(kn_in, kn_ref, sems.at[0])
    kn_copy.start()
    ch, hc = pad_ref.shape[2], hid_ref.shape[1]
    rows = hid_ref.shape[0]
    plane = rows // side
    nf = plane // side
    step = plane // 2
    clear_borders(pad_ref, side, plane, nf)
    if first:
        for i in range(side):
            pad_ref[i + 1, nf : nf + plane] = slices[0][i * plane : (i + 1) * plane]
    else:
        def place(k, carry):
            for q, odd, a_ref, b_ref in by_rank(slices, rank):
                top, bottom = halves(odd, a_ref[chunk(k, step), :], b_ref[chunk(k, step), :])
                lanes = pl.ds(pl.multiple_of(128 * q, 128), 128)
                for piece, kk in ((top, k), (bottom, k + side)):
                    at = nf + lax.rem(kk, 2) * step
                    pad_ref[1 + kk // 2, pl.ds(pl.multiple_of(at, 16), step), lanes] = piece.astype(BF)
            return carry

        lax.fori_loop(0, side, place, 0, unroll=True)
    pad_copy = pltpu.make_async_copy(pad_ref, pad_out, sems.at[1])
    pad_copy.start()
    kn_copy.wait()

    def conv(i, total):
        acc = jnp.zeros((plane, hc), F32)
        for t in range(9):
            r, c = t // 3, t % 3
            acc += nn(pad_ref[i + r, c * nf : c * nf + plane, :], kn_ref[t])
        sp_ref[i] = acc
        return total + jnp.sum(acc, axis=0, keepdims=True)

    mean = lax.fori_loop(0, side, conv, jnp.zeros((1, hc), F32), unroll=True) / rows

    def square(i, total):
        cen = sp_ref[i] - mean
        return total + jnp.sum(cen * cen, axis=0, keepdims=True)

    var = lax.fori_loop(0, side, square, jnp.zeros((1, hc), F32), unroll=True) / rows
    rs = lax.rsqrt(var + eps)
    rs_ref[...] = rs
    gain, bias = vec_ref[0:1, :], vec_ref[1:2, :]

    def act(i, carry):
        xhat = (sp_ref[i] - mean) * rs
        xhat_ref[i] = xhat
        v = xhat * gain + bias
        v = v * jax.nn.sigmoid(v)
        sp_ref[i] = v
        hid_ref[chunk(i, plane), :] = v.astype(BF)
        return carry

    lax.fori_loop(0, side, act, 0, unroll=True)
    late = [
        pltpu.make_async_copy(hid_ref, hid_out, sems.at[2]),
        pltpu.make_async_copy(xhat_ref, xhat_out, sems.at[3]),
    ]
    for copy in late:
        copy.start()
    low = lax.broadcasted_iota(jnp.int32, (step, 128), 1) < 64

    def temporal(k, carry):
        pieces = []
        for kk in (k, k + side):
            par = lax.rem(kk, 2)
            h = sp_ref[kk // 2, pl.ds(pl.multiple_of(par * step, 8), step), :]
            at = pl.multiple_of(par * (step % nf), 8)
            pieces.append((
                (pltpu.roll(h, 1, 0) * before_ref[pl.ds(at, step), :]).astype(BF),
                h.astype(BF),
                (pltpu.roll(h, step - 1, 0) * after_ref[pl.ds(at, step), :]).astype(BF),
            ))
        part = sum(
            nn(jnp.concatenate([x, y], axis=0), ltm_ref[t * hc : (t + 1) * hc])
            for t, (x, y) in enumerate(zip(*pieces))
        )
        store_packed(rank, mate_ref, keep_ref, part, k, step, low)
        return carry

    lax.fori_loop(0, side, temporal, 0, unroll=True)
    for copy in [pad_copy] + late:
        copy.wait()


def conv_forward(rank, g, kn, lt, vec, before, after, side, pixels, ch, deps=()):
    hc = vec.shape[1]
    plane = pixels // side
    nf = plane // side
    n = len(g)
    shapes = [
        ((side + 2, plane + 2 * nf, ch), BF),
        ((pixels, hc), BF),
        ((side, plane, hc), F32),
    ]
    outs = [jax.ShapeDtypeStruct(*s) for s in shapes] + [
        jax.ShapeDtypeStruct((1, hc), F32),
        jax.ShapeDtypeStruct((4, pixels // 2, 128), BF),
        jax.ShapeDtypeStruct((4, pixels // 2, 128), BF),
    ]
    scratch = [pltpu.VMEM(*s) for s in shapes] + [
        pltpu.VMEM((side, plane, hc), F32),
        pltpu.VMEM((9, ch, hc), BF),
        pltpu.SemaphoreType.DMA((4,)),
    ]
    flops = 2 * pixels * hc * 12 * ch
    return call(functools.partial(conv_body, side, n == 1), outs, scratch, flops,
                rank, *g, kn, lt, vec, before, after,
                deps=deps, far=(n + 1,), far_outs=(0, 1, 2))


def fold(v):
    return v + pltpu.roll(v, 64, 1)


def total_of(refs):
    t = refs[0][...].astype(F32)
    for ref in refs[1:]:
        t += ref[...].astype(F32)
    return t


def pair_sum_body(keep_ref, mate_ref, *out_refs):
    for p, ref in enumerate(out_refs):
        ref[...] = (keep_ref[p].astype(F32) + mate_ref[p].astype(F32)).astype(ref.dtype)


def pair_sum(keep, arrived, deps=()):
    shape = keep.shape[1:]
    outs = [jax.ShapeDtypeStruct(shape, BF)] * keep.shape[0]
    return call(pair_sum_body, outs, [], keep.size, keep, arrived, deps=deps)


def out_norm_body(n, has_skip, *refs):
    parts, refs = refs[:n], refs[n:]
    if has_skip:
        vec_ref, skip_ref, xhat_ref, rs_ref, pre_ref, res_ref = refs
    else:
        vec_ref, xhat_ref, rs_ref, pre_ref, res_ref = refs
    t = total_of(parts)
    pixels = 2 * t.shape[0]
    mean = fold(jnp.sum(t, axis=0, keepdims=True)) / pixels
    cen = t - mean
    rs = lax.rsqrt(fold(jnp.sum(cen * cen, axis=0, keepdims=True)) / pixels + eps)
    xhat = cen * rs
    pre = xhat * vec_ref[0:1, :] + vec_ref[1:2, :]
    if has_skip:
        pre = pre + skip_ref[...].astype(F32)
    xhat_ref[...] = xhat
    rs_ref[...] = rs
    pre_ref[...] = pre
    res_ref[...] = (pre * jax.nn.sigmoid(pre)).astype(BF)


def out_norm(parts, vec, skip, deps=()):
    half = parts[0].shape[0]
    outs = [
        jax.ShapeDtypeStruct((half, 128), F32),
        jax.ShapeDtypeStruct((1, 128), F32),
        jax.ShapeDtypeStruct((half, 128), F32),
        jax.ShapeDtypeStruct((half, 128), BF),
    ]
    args = (*parts, vec) + (() if skip is None else (skip,))
    body = functools.partial(out_norm_body, len(parts), skip is not None)
    return call(body, outs, [], half * 128 * 10, *args, deps=deps)


def out_back_body(n, *refs):
    parts, (pre_ref, xhat_ref, rs_ref, vec_ref, dpre_ref, dt_ref, sums_ref) = refs[:n], refs[n:]
    g = total_of(parts)
    pre, xhat = pre_ref[...], xhat_ref[...]
    sig = jax.nn.sigmoid(pre)
    dpre = g * (sig * (1.0 + pre * (1.0 - sig)))
    pixels = 2 * pre.shape[0]
    sb = fold(jnp.sum(dpre, axis=0, keepdims=True))
    sg = fold(jnp.sum(dpre * xhat, axis=0, keepdims=True))
    dpre_ref[...] = dpre.astype(BF)
    scale = vec_ref[0:1, :] * rs_ref[...]
    dt_ref[...] = (scale * (dpre - sb / pixels - xhat * (sg / pixels))).astype(BF)
    sums_ref[0:1, :] = sg
    sums_ref[1:2, :] = sb


def out_back(parts, pre, xhat, rs, vec, deps=()):
    half = pre.shape[0]
    outs = [
        jax.ShapeDtypeStruct((half, 128), BF),
        jax.ShapeDtypeStruct((half, 128), BF),
        jax.ShapeDtypeStruct((2, 128), F32),
    ]
    args = (*parts, pre, xhat, rs, vec)
    return call(functools.partial(out_back_body, len(parts)), outs, [], half * 1280, *args, deps=deps)


def conv_back_body(side, rank_ref, *refs):
    slices, (xhat_in, rs_ref, w_ref, lnt_ref, vec_ref, before_ref, after_ref,
             dt_out, ds_out, sums_ref, mate_ref, keep_ref,
             dt_ref, ds_ref, xhat_ref, dy_ref, pad_ref, ktm_ref, sems) = refs[:8], refs[8:]
    half = slices[0].shape[0]
    rank = rank_ref[0]
    nz, _, width = w_ref.shape
    rows = 2 * half
    plane = rows // side
    nf = plane // side
    step = plane // 2
    hc = ds_ref.shape[1]
    ch = dt_ref.shape[1]
    fetched = [
        pltpu.make_async_copy(
            w_ref.at[z, pl.ds(0, hc)], ktm_ref.at[:, pl.ds(z * width, width)], sems.at[z])
        for z in range(nz)
    ]
    xhat_copy = pltpu.make_async_copy(xhat_in, xhat_ref, sems.at[nz])
    for copy in fetched + [xhat_copy]:
        copy.start()
    clear_borders(pad_ref, side, plane, nf)

    def place(k, carry):
        for q, odd, a_ref, b_ref in by_rank(slices, rank):
            top, bottom = halves(odd, a_ref[chunk(k, step), :], b_ref[chunk(k, step), :])
            lanes = pl.ds(pl.multiple_of(128 * q, 128), 128)
            dt_ref[chunk(k, step), lanes] = top.astype(BF)
            dt_ref[pl.ds(pl.multiple_of(half + k * step, 16), step), lanes] = bottom.astype(BF)
        return carry

    lax.fori_loop(0, side, place, 0, unroll=True)
    dt_copy = pltpu.make_async_copy(dt_ref, dt_out, sems.at[nz + 1])
    dt_copy.start()
    xhat_copy.wait()
    gain, bias = vec_ref[0:1, :], vec_ref[1:2, :]

    def hidden_grad(i, sums):
        dt = dt_ref[chunk(i, plane), :]
        early = nn(dt, lnt_ref[0]) * before_ref[0:plane, :]
        late = nn(dt, lnt_ref[2]) * after_ref[0:plane, :]
        dh = nn(dt, lnt_ref[1]) + pltpu.roll(early, plane - 1, 0) + pltpu.roll(late, 1, 0)
        xhat = xhat_ref[i]
        v = xhat * gain + bias
        sig = jax.nn.sigmoid(v)
        dy = dh * (sig * (1.0 + v * (1.0 - sig)))
        dy_ref[i] = dy
        return (
            sums[0] + jnp.sum(dy * xhat, axis=0, keepdims=True),
            sums[1] + jnp.sum(dy, axis=0, keepdims=True),
        )

    zero = jnp.zeros((1, hc), F32)
    sg, sb = lax.fori_loop(0, side, hidden_grad, (zero, zero), unroll=True)
    sums_ref[0:1, :] = sg
    sums_ref[1:2, :] = sb
    scale = gain * rs_ref[...]

    def spatial_grad(i, carry):
        ds = (scale * (dy_ref[i] - sb / rows - xhat_ref[i] * (sg / rows))).astype(BF)
        pad_ref[i + 1, nf : nf + plane] = ds
        ds_ref[chunk(i, plane), :] = ds
        return carry

    lax.fori_loop(0, side, spatial_grad, 0, unroll=True)
    ds_copy = pltpu.make_async_copy(ds_ref, ds_out, sems.at[nz + 2])
    ds_copy.start()
    for copy in fetched:
        copy.wait()
    low = lax.broadcasted_iota(jnp.int32, (step, 128), 1) < 64

    def back(k, carry):
        acc = jnp.zeros((2 * step, ch), F32)
        for t in range(9):
            r, c = 2 - t // 3, 2 - t % 3
            pieces = []
            for kk in (k, k + side):
                at = c * nf + lax.rem(kk, 2) * step
                pieces.append(pad_ref[kk // 2 + r, pl.ds(pl.multiple_of(at, 16), step), :])
            acc += nn(jnp.concatenate(pieces, axis=0), ktm_ref[:, t * ch : (t + 1) * ch])
        store_packed(rank, mate_ref, keep_ref, acc, k, step, low)
        return carry

    lax.fori_loop(0, side, back, 0, unroll=True)
    dt_copy.wait()
    ds_copy.wait()


def conv_back(rank, g, xhat, rs, w, lnt, vec, before, after, side, deps=()):
    half = g[0].shape[0]
    hc = vec.shape[1]
    ch = len(g) * 64
    pixels = 2 * half
    plane = pixels // side
    nf = plane // side
    outs = [
        jax.ShapeDtypeStruct((pixels, ch), BF),
        jax.ShapeDtypeStruct((pixels, hc), BF),
        jax.ShapeDtypeStruct((2, hc), F32),
        jax.ShapeDtypeStruct((4, half, 128), BF),
        jax.ShapeDtypeStruct((4, half, 128), BF),
    ]
    scratch = [
        pltpu.VMEM((pixels, ch), BF),
        pltpu.VMEM((pixels, hc), BF),
        pltpu.VMEM((side, plane, hc), F32),
        pltpu.VMEM((side, plane, hc), F32),
        pltpu.VMEM((side + 2, plane + 2 * nf, hc), BF),
        pltpu.VMEM((hc, 9 * ch), BF),
        pltpu.SemaphoreType.DMA((w.shape[0] + 3,)),
    ]
    flops = 2 * pixels * hc * 12 * ch
    return call(functools.partial(conv_back_body, side), outs, scratch, flops,
                rank, *g, xhat, rs, w, lnt, vec, before, after,
                deps=deps, far=(9, 11), far_outs=(0, 1))


def grads_body(side, pad_ref, hid_ref, ds_ref, dt_ref, before_ref, after_ref, mid_ref, out_ref,
               sg_ref, dst_ref, taps_ref, tg_ref, vec_ref):
    ch = pad_ref.shape[2]
    hc = hid_ref.shape[1]
    plane = hid_ref.shape[0] // side
    nf = plane // side
    for i in (0, 1, side + 2, side + 3):
        dst_ref[i] = jnp.zeros(dst_ref.shape[1:], BF)
    for i in range(side):
        at = slice(i * plane, (i + 1) * plane)
        h = hid_ref[at, :].astype(F32)
        taps_ref[i, 0:hc] = (pltpu.roll(h, 1, 0) * before_ref[0:plane, :]).T.astype(BF)
        taps_ref[i, hc : 2 * hc] = h.T.astype(BF)
        taps_ref[i, 2 * hc : 3 * hc] = (pltpu.roll(h, plane - 1, 0) * after_ref[0:plane, :]).T.astype(BF)
        dst_ref[i + 2] = ds_ref[at, :].astype(F32).T.astype(BF)
    tg_ref[0 : 3 * hc, :] = sum(
        nn(taps_ref[i], dt_ref[i * plane : (i + 1) * plane, :]) for i in range(side)
    )
    tg_ref[3 * hc :, :] = jnp.zeros((tg_ref.shape[0] - 3 * hc, ch), F32)
    nz, _, width = sg_ref.shape
    size = 3 * hc // (2 * nz)
    vec_ref[...] = jnp.zeros(vec_ref.shape, F32)
    vec_ref[size : size + 2, 0:hc] = mid_ref[...]
    vec_ref[size + 2 : size + 4, 0:128] = out_ref[...]
    tall = vec_ref.shape[0]
    inside = lax.broadcasted_iota(jnp.int32, (tall, ch), 0) < size
    off = (width // 2) % 128
    for z in range(nz):
        first, second = [
            jnp.where(inside, tg_ref[b * size : b * size + tall, :], vec_ref[...])
            for b in (2 * z, 2 * z + 1)
        ]
        start = width // 2 - off
        sg_ref[z, hc : hc + tall, 0:ch] = first.astype(BF)
        second = pltpu.roll(jnp.concatenate([second, jnp.zeros((tall, 128), F32)], axis=1), off, 1)
        sg_ref[z, hc : hc + tall, start : start + ch + 128] = second.astype(BF)
    for c in range(3):
        acc = sum(
            nn(dst_ref[i : i + 3].reshape(3 * hc, plane), pad_ref[i, c * nf : c * nf + plane, :])
            for i in range(1, side + 1)
        )
        for r in range(3):
            first = (3 * r + c) * ch
            end = first + ch
            at = (2 - r) * hc
            done = 0
            while first < end:
                z = first // width
                last = min(end, (z + 1) * width)
                sg_ref[z, 0:hc, first - z * width : last - z * width] = (
                    acc[at : at + hc, done : done + last - first].astype(BF)
                )
                done += last - first
                first = last


def kernel_grads(pad, hidden, ds, dt, before, after, mid, out, side, shape, deps=()):
    pixels, hc = hidden.shape
    ch = dt.shape[1]
    plane = pixels // side
    outs = [jax.ShapeDtypeStruct(shape, BF)]
    tall = shape[1] - hc
    scratch = [
        pltpu.VMEM((side + 4, hc, plane), BF),
        pltpu.VMEM((side, 3 * hc, plane), BF),
        pltpu.VMEM((3 * hc + tall, ch), F32),
        pltpu.VMEM((tall, ch), F32),
    ]
    flops = 2 * pixels * hc * 12 * ch
    return call(functools.partial(grads_body, side), outs, scratch, flops,
                pad, hidden, ds, dt, before, after, mid, out, deps=deps)[0]


def copy_after_body(v_ref, out_ref):
    out_ref[...] = v_ref[...]


def after_all(v, *deps):
    return call(copy_after_body, [jax.ShapeDtypeStruct(v.shape, v.dtype)], [], v.size, v, deps=deps)[0]


def pack_kernels_body(kt_ref, lt_ref, vec_ref, out_ref, low_ref):
    ranks, _, width = out_ref.shape
    hc = kt_ref.shape[0] // ranks
    blocks = lt_ref.shape[0] // hc
    q = hc // ranks
    low_ref[...] = jnp.zeros(low_ref.shape, F32)
    for r in range(ranks):
        out_ref[r, 0:hc, :] = kt_ref[r * hc : (r + 1) * hc, :]
        for b in range(blocks):
            low_ref[r, b * q : (b + 1) * q, 0 : lt_ref.shape[1]] = (
                lt_ref[b * hc + r * q : b * hc + (r + 1) * q, :]
            )
        low_ref[r, blocks * q : blocks * q + 1, :] = vec_ref[...]
        out_ref[r, hc:, :] = low_ref[r].astype(BF)


def pack_kernels(kt, lt, vec, ranks, tall, deps):
    width = kt.shape[1]
    outs = [jax.ShapeDtypeStruct((ranks, kt.shape[0] // ranks + tall, width), BF)]
    scratch = [pltpu.VMEM((ranks, tall, width), F32)]
    return call(pack_kernels_body, outs, scratch, kt.size * 8, kt, lt, vec, deps=deps)[0]


def call(body, outs, scratch, flops, *args, deps=(), far=(), far_outs=()):
    moved = sum(a.size * a.dtype.itemsize for a in args) + sum(
        o.size * o.dtype.itemsize for o in outs
    )
    n = len(deps)

    def spec(a):
        return pl.BlockSpec(memory_space=pltpu.SMEM if a.dtype == jnp.int32 else pltpu.VMEM)

    return pl.pallas_call(
        lambda *refs: body(*refs[n:]),
        out_shape=outs,
        in_specs=[ANY] * n + [ANY if i in far else spec(a) for i, a in enumerate(args)],
        out_specs=[ANY if i in far_outs else spec(o) for i, o in enumerate(outs)],
        scratch_shapes=scratch,
        compiler_params=pltpu.CompilerParams(vmem_limit_bytes=VMEM_CAP),
        cost_estimate=pl.CostEstimate(flops=flops, bytes_accessed=moved, transcendentals=0),
    )(*deps, *args)


def chunk(i, size):
    return pl.ds(pl.multiple_of(i * size, 16), size)


def clear_borders(pad_ref, side, plane, nf):
    zrow = jnp.zeros(pad_ref.shape[1:], BF)
    pad_ref[0] = zrow
    pad_ref[side + 1] = zrow
    zcol = jnp.zeros((nf, pad_ref.shape[2]), BF)
    for i in range(side):
        pad_ref[i + 1, 0:nf] = zcol
        pad_ref[i + 1, nf + plane : 2 * nf + plane] = zcol


def by_rank(slices, rank):
    odd = lax.rem(rank, 2) == 1
    for p in range(len(slices) // 2):
        a, b = slices[2 * p], slices[2 * p + 1]
        yield lax.bitwise_xor(rank // 2, p), odd, a, b


def halves(odd, own, mate):
    low = lax.broadcasted_iota(jnp.int32, own.shape, 1) < 64
    own, mate = own.astype(F32), mate.astype(F32)
    a, b = jnp.where(odd, mate, own), jnp.where(odd, own, mate)
    top = jnp.where(low, a, pltpu.roll(b, 64, 1))
    bottom = jnp.where(low, pltpu.roll(a, 64, 1), b)
    return top, bottom


def store_packed(rank, mate_ref, keep_ref, part, k, step, low):
    rows_now = chunk(k, step)
    odd = lax.rem(rank, 2) == 1
    for q in range(keep_ref.shape[0]):
        x = part[:step, 128 * q : 128 * q + 128]
        y = part[step:, 128 * q : 128 * q + 128]
        even_slice = jnp.where(low, x, pltpu.roll(y, 64, 1))
        odd_slice = jnp.where(low, pltpu.roll(x, 64, 1), y)
        p = lax.bitwise_xor(rank // 2, q)
        keep_ref[p, rows_now, :] = jnp.where(odd, odd_slice, even_slice).astype(BF)
        mate_ref[p, rows_now, :] = jnp.where(odd, even_slice, odd_slice).astype(BF)


def fetch_kernels(w_ref, ktm_ref, lw_ref, sems):
    nz, _, width = w_ref.shape
    hc = ktm_ref.shape[0]
    copies = []
    for z in range(nz):
        copies.append(pltpu.make_async_copy(
            w_ref.at[z, pl.ds(0, hc)], ktm_ref.at[:, pl.ds(z * width, width)], sems.at[2 * z]))
        copies.append(pltpu.make_async_copy(
            w_ref.at[z, pl.ds(hc, lw_ref.shape[1])], lw_ref.at[z], sems.at[2 * z + 1]))
    for copy in copies:
        copy.start()
    return copies


def join_temporal(lw_ref, lf_ref, ltm_ref):
    ch = ltm_ref.shape[1]
    width = lw_ref.shape[2] // 2
    count = 2 * lw_ref.shape[0]
    size = ltm_ref.shape[0] // count
    for z in range(lw_ref.shape[0]):
        first = lw_ref[z, :, 0:ch].astype(F32)
        off = width % 128
        second = lw_ref[z, :, width - off : width - off + ch + 128].astype(F32)
        second = pltpu.roll(second, ch + 128 - off, 1)[:, 0:ch]
        for b, block in ((2 * z, first), (2 * z + 1, second)):
            lf_ref[b * size : b * size + block.shape[0], :] = block
    ltm_ref[...] = lf_ref[0 : ltm_ref.shape[0], :].astype(BF)


def prepare_body(w_ref, kn_out, l_out, lt_out, rows_out, ktm_ref, lw_ref, lf_ref, sems):
    hc, ch = ktm_ref.shape[0], l_out.shape[1]
    for copy in fetch_kernels(w_ref, ktm_ref, lw_ref, sems):
        copy.wait()
    for t in range(9):
        kn_out[t] = ktm_ref[:, t * ch : (t + 1) * ch].astype(F32).T.astype(BF)
    join_temporal(lw_ref, lf_ref, l_out)
    rows_out[...] = lw_ref[:, lw_ref.shape[1] - rows_out.shape[1] :, :]
    for t in range(3):
        lt_out[t] = lf_ref[t * hc : (t + 1) * hc].T.astype(BF)


def prepare(w, hc, ch, deps=()):
    outs = [
        jax.ShapeDtypeStruct((9, ch, hc), BF),
        jax.ShapeDtypeStruct((3 * hc, ch), BF),
        jax.ShapeDtypeStruct((3, ch, hc), BF),
        jax.ShapeDtypeStruct((w.shape[0], 16, w.shape[2]), BF),
    ]
    tall = w.shape[1] - hc
    scratch = [
        pltpu.VMEM((hc, 9 * ch), BF),
        pltpu.VMEM((w.shape[0], tall, w.shape[2]), BF),
        pltpu.VMEM((3 * hc + tall, ch), F32),
        pltpu.SemaphoreType.DMA((2 * w.shape[0],)),
    ]
    return call(prepare_body, outs, scratch, 2 * w.size * 512, w, deps=deps, far=(0,))


def conv_body(side, first, rank_ref, *refs):
    n = 1 if first else 8
    slices = refs[:n]
    (kn_in, ltm_ref, vec_ref, before_ref, after_ref,
     pad_out, hid_out, xhat_out, rs_ref, mate_ref, keep_ref,
     pad_ref, hid_ref, xhat_ref, sp_ref, kn_ref, sems) = refs[n:]
    rank = rank_ref[0]
    kn_copy = pltpu.make_async_copy(kn_in, kn_ref, sems.at[0])
    kn_copy.start()
    ch, hc = pad_ref.shape[2], hid_ref.shape[1]
    rows = hid_ref.shape[0]
    plane = rows // side
    nf = plane // side
    step = plane // 2
    clear_borders(pad_ref, side, plane, nf)
    if first:
        for i in range(side):
            pad_ref[i + 1, nf : nf + plane] = slices[0][i * plane : (i + 1) * plane]
    else:
        def place(k, carry):
            for q, odd, a_ref, b_ref in by_rank(slices, rank):
                top, bottom = halves(odd, a_ref[chunk(k, step), :], b_ref[chunk(k, step), :])
                lanes = pl.ds(pl.multiple_of(128 * q, 128), 128)
                for piece, kk in ((top, k), (bottom, k + side)):
                    at = nf + lax.rem(kk, 2) * step
                    pad_ref[1 + kk // 2, pl.ds(pl.multiple_of(at, 16), step), lanes] = piece.astype(BF)
            return carry

        lax.fori_loop(0, side, place, 0, unroll=True)
    pad_copy = pltpu.make_async_copy(pad_ref, pad_out, sems.at[1])
    pad_copy.start()
    kn_copy.wait()

    def conv(i, total):
        acc = jnp.zeros((plane, hc), F32)
        for t in range(9):
            r, c = t // 3, t % 3
            acc += nn(pad_ref[i + r, c * nf : c * nf + plane, :], kn_ref[t])
        sp_ref[i] = acc
        return total + jnp.sum(acc, axis=0, keepdims=True)

    mean = lax.fori_loop(0, side, conv, jnp.zeros((1, hc), F32), unroll=True) / rows

    def square(i, total):
        cen = sp_ref[i] - mean
        return total + jnp.sum(cen * cen, axis=0, keepdims=True)

    var = lax.fori_loop(0, side, square, jnp.zeros((1, hc), F32), unroll=True) / rows
    rs = lax.rsqrt(var + eps)
    rs_ref[...] = rs
    gain, bias = vec_ref[0:1, :], vec_ref[1:2, :]

    def act(i, carry):
        xhat = (sp_ref[i] - mean) * rs
        xhat_ref[i] = xhat
        v = xhat * gain + bias
        v = v * jax.nn.sigmoid(v)
        sp_ref[i] = v
        hid_ref[chunk(i, plane), :] = v.astype(BF)
        return carry

    lax.fori_loop(0, side, act, 0, unroll=True)
    late = [
        pltpu.make_async_copy(hid_ref, hid_out, sems.at[2]),
        pltpu.make_async_copy(xhat_ref, xhat_out, sems.at[3]),
    ]
    for copy in late:
        copy.start()
    low = lax.broadcasted_iota(jnp.int32, (step, 128), 1) < 64

    def temporal(k, carry):
        pieces = []
        for kk in (k, k + side):
            par = lax.rem(kk, 2)
            h = sp_ref[kk // 2, pl.ds(pl.multiple_of(par * step, 8), step), :]
            at = pl.multiple_of(par * (step % nf), 8)
            pieces.append((
                (pltpu.roll(h, 1, 0) * before_ref[pl.ds(at, step), :]).astype(BF),
                h.astype(BF),
                (pltpu.roll(h, step - 1, 0) * after_ref[pl.ds(at, step), :]).astype(BF),
            ))
        part = sum(
            nn(jnp.concatenate([x, y], axis=0), ltm_ref[t * hc : (t + 1) * hc])
            for t, (x, y) in enumerate(zip(*pieces))
        )
        store_packed(rank, mate_ref, keep_ref, part, k, step, low)
        return carry

    lax.fori_loop(0, side, temporal, 0, unroll=True)
    for copy in [pad_copy] + late:
        copy.wait()


def conv_forward(rank, g, kn, lt, vec, before, after, side, pixels, ch, deps=()):
    hc = vec.shape[1]
    plane = pixels // side
    nf = plane // side
    n = len(g)
    shapes = [
        ((side + 2, plane + 2 * nf, ch), BF),
        ((pixels, hc), BF),
        ((side, plane, hc), F32),
    ]
    outs = [jax.ShapeDtypeStruct(*s) for s in shapes] + [
        jax.ShapeDtypeStruct((1, hc), F32),
        jax.ShapeDtypeStruct((4, pixels // 2, 128), BF),
        jax.ShapeDtypeStruct((4, pixels // 2, 128), BF),
    ]
    scratch = [pltpu.VMEM(*s) for s in shapes] + [
        pltpu.VMEM((side, plane, hc), F32),
        pltpu.VMEM((9, ch, hc), BF),
        pltpu.SemaphoreType.DMA((4,)),
    ]
    flops = 2 * pixels * hc * 12 * ch
    return call(functools.partial(conv_body, side, n == 1), outs, scratch, flops,
                rank, *g, kn, lt, vec, before, after,
                deps=deps, far=(n + 1,), far_outs=(0, 1, 2))


def fold(v):
    return v + pltpu.roll(v, 64, 1)


def total_of(refs):
    t = refs[0][...].astype(F32)
    for ref in refs[1:]:
        t += ref[...].astype(F32)
    return t


def pair_sum_body(keep_ref, mate_ref, *out_refs):
    for p, ref in enumerate(out_refs):
        ref[...] = (keep_ref[p].astype(F32) + mate_ref[p].astype(F32)).astype(ref.dtype)


def pair_sum(keep, arrived, deps=()):
    shape = keep.shape[1:]
    outs = [jax.ShapeDtypeStruct(shape, BF)] * keep.shape[0]
    return call(pair_sum_body, outs, [], keep.size, keep, arrived, deps=deps)


def out_norm_body(n, has_skip, *refs):
    parts, refs = refs[:n], refs[n:]
    if has_skip:
        vec_ref, skip_ref, xhat_ref, rs_ref, pre_ref, res_ref = refs
    else:
        vec_ref, xhat_ref, rs_ref, pre_ref, res_ref = refs
    t = total_of(parts)
    pixels = 2 * t.shape[0]
    mean = fold(jnp.sum(t, axis=0, keepdims=True)) / pixels
    cen = t - mean
    rs = lax.rsqrt(fold(jnp.sum(cen * cen, axis=0, keepdims=True)) / pixels + eps)
    xhat = cen * rs
    pre = xhat * vec_ref[0:1, :] + vec_ref[1:2, :]
    if has_skip:
        pre = pre + skip_ref[...].astype(F32)
    xhat_ref[...] = xhat
    rs_ref[...] = rs
    pre_ref[...] = pre
    res_ref[...] = (pre * jax.nn.sigmoid(pre)).astype(BF)


def out_norm(parts, vec, skip, deps=()):
    half = parts[0].shape[0]
    outs = [
        jax.ShapeDtypeStruct((half, 128), F32),
        jax.ShapeDtypeStruct((1, 128), F32),
        jax.ShapeDtypeStruct((half, 128), F32),
        jax.ShapeDtypeStruct((half, 128), BF),
    ]
    args = (*parts, vec) + (() if skip is None else (skip,))
    body = functools.partial(out_norm_body, len(parts), skip is not None)
    return call(body, outs, [], half * 128 * 10, *args, deps=deps)


def out_back_body(n, *refs):
    parts, (pre_ref, xhat_ref, rs_ref, vec_ref, dpre_ref, dt_ref, sums_ref) = refs[:n], refs[n:]
    g = total_of(parts)
    pre, xhat = pre_ref[...], xhat_ref[...]
    sig = jax.nn.sigmoid(pre)
    dpre = g * (sig * (1.0 + pre * (1.0 - sig)))
    pixels = 2 * pre.shape[0]
    sb = fold(jnp.sum(dpre, axis=0, keepdims=True))
    sg = fold(jnp.sum(dpre * xhat, axis=0, keepdims=True))
    dpre_ref[...] = dpre.astype(BF)
    scale = vec_ref[0:1, :] * rs_ref[...]
    dt_ref[...] = (scale * (dpre - sb / pixels - xhat * (sg / pixels))).astype(BF)
    sums_ref[0:1, :] = sg
    sums_ref[1:2, :] = sb


def out_back(parts, pre, xhat, rs, vec, deps=()):
    half = pre.shape[0]
    outs = [
        jax.ShapeDtypeStruct((half, 128), BF),
        jax.ShapeDtypeStruct((half, 128), BF),
        jax.ShapeDtypeStruct((2, 128), F32),
    ]
    args = (*parts, pre, xhat, rs, vec)
    return call(functools.partial(out_back_body, len(parts)), outs, [], half * 1280, *args, deps=deps)


def conv_back_body(side, rank_ref, *refs):
    slices, (xhat_in, rs_ref, w_ref, lnt_ref, vec_ref, before_ref, after_ref,
             dt_out, ds_out, sums_ref, mate_ref, keep_ref,
             dt_ref, ds_ref, xhat_ref, dy_ref, pad_ref, ktm_ref, sems) = refs[:8], refs[8:]
    half = slices[0].shape[0]
    rank = rank_ref[0]
    nz, _, width = w_ref.shape
    rows = 2 * half
    plane = rows // side
    nf = plane // side
    step = plane // 2
    hc = ds_ref.shape[1]
    ch = dt_ref.shape[1]
    fetched = [
        pltpu.make_async_copy(
            w_ref.at[z, pl.ds(0, hc)], ktm_ref.at[:, pl.ds(z * width, width)], sems.at[z])
        for z in range(nz)
    ]
    xhat_copy = pltpu.make_async_copy(xhat_in, xhat_ref, sems.at[nz])
    for copy in fetched + [xhat_copy]:
        copy.start()
    clear_borders(pad_ref, side, plane, nf)

    def place(k, carry):
        for q, odd, a_ref, b_ref in by_rank(slices, rank):
            top, bottom = halves(odd, a_ref[chunk(k, step), :], b_ref[chunk(k, step), :])
            lanes = pl.ds(pl.multiple_of(128 * q, 128), 128)
            dt_ref[chunk(k, step), lanes] = top.astype(BF)
            dt_ref[pl.ds(pl.multiple_of(half + k * step, 16), step), lanes] = bottom.astype(BF)
        return carry

    lax.fori_loop(0, side, place, 0, unroll=True)
    dt_copy = pltpu.make_async_copy(dt_ref, dt_out, sems.at[nz + 1])
    dt_copy.start()
    xhat_copy.wait()
    gain, bias = vec_ref[0:1, :], vec_ref[1:2, :]

    def hidden_grad(i, sums):
        dt = dt_ref[chunk(i, plane), :]
        early = nn(dt, lnt_ref[0]) * before_ref[0:plane, :]
        late = nn(dt, lnt_ref[2]) * after_ref[0:plane, :]
        dh = nn(dt, lnt_ref[1]) + pltpu.roll(early, plane - 1, 0) + pltpu.roll(late, 1, 0)
        xhat = xhat_ref[i]
        v = xhat * gain + bias
        sig = jax.nn.sigmoid(v)
        dy = dh * (sig * (1.0 + v * (1.0 - sig)))
        dy_ref[i] = dy
        return (
            sums[0] + jnp.sum(dy * xhat, axis=0, keepdims=True),
            sums[1] + jnp.sum(dy, axis=0, keepdims=True),
        )

    zero = jnp.zeros((1, hc), F32)
    sg, sb = lax.fori_loop(0, side, hidden_grad, (zero, zero), unroll=True)
    sums_ref[0:1, :] = sg
    sums_ref[1:2, :] = sb
    scale = gain * rs_ref[...]

    def spatial_grad(i, carry):
        ds = (scale * (dy_ref[i] - sb / rows - xhat_ref[i] * (sg / rows))).astype(BF)
        pad_ref[i + 1, nf : nf + plane] = ds
        ds_ref[chunk(i, plane), :] = ds
        return carry

    lax.fori_loop(0, side, spatial_grad, 0, unroll=True)
    ds_copy = pltpu.make_async_copy(ds_ref, ds_out, sems.at[nz + 2])
    ds_copy.start()
    for copy in fetched:
        copy.wait()
    low = lax.broadcasted_iota(jnp.int32, (step, 128), 1) < 64

    def back(k, carry):
        acc = jnp.zeros((2 * step, ch), F32)
        for t in range(9):
            r, c = 2 - t // 3, 2 - t % 3
            pieces = []
            for kk in (k, k + side):
                at = c * nf + lax.rem(kk, 2) * step
                pieces.append(pad_ref[kk // 2 + r, pl.ds(pl.multiple_of(at, 16), step), :])
            acc += nn(jnp.concatenate(pieces, axis=0), ktm_ref[:, t * ch : (t + 1) * ch])
        store_packed(rank, mate_ref, keep_ref, acc, k, step, low)
        return carry

    lax.fori_loop(0, side, back, 0, unroll=True)
    dt_copy.wait()
    ds_copy.wait()


def conv_back(rank, g, xhat, rs, w, lnt, vec, before, after, side, deps=()):
    half = g[0].shape[0]
    hc = vec.shape[1]
    ch = len(g) * 64
    pixels = 2 * half
    plane = pixels // side
    nf = plane // side
    outs = [
        jax.ShapeDtypeStruct((pixels, ch), BF),
        jax.ShapeDtypeStruct((pixels, hc), BF),
        jax.ShapeDtypeStruct((2, hc), F32),
        jax.ShapeDtypeStruct((4, half, 128), BF),
        jax.ShapeDtypeStruct((4, half, 128), BF),
    ]
    scratch = [
        pltpu.VMEM((pixels, ch), BF),
        pltpu.VMEM((pixels, hc), BF),
        pltpu.VMEM((side, plane, hc), F32),
        pltpu.VMEM((side, plane, hc), F32),
        pltpu.VMEM((side + 2, plane + 2 * nf, hc), BF),
        pltpu.VMEM((hc, 9 * ch), BF),
        pltpu.SemaphoreType.DMA((w.shape[0] + 3,)),
    ]
    flops = 2 * pixels * hc * 12 * ch
    return call(functools.partial(conv_back_body, side), outs, scratch, flops,
                rank, *g, xhat, rs, w, lnt, vec, before, after,
                deps=deps, far=(9, 11), far_outs=(0, 1))


def grads_body(side, pad_ref, hid_ref, ds_ref, dt_ref, before_ref, after_ref, mid_ref, out_ref,
               sg_ref, dst_ref, taps_ref, tg_ref, vec_ref):
    ch = pad_ref.shape[2]
    hc = hid_ref.shape[1]
    plane = hid_ref.shape[0] // side
    nf = plane // side
    for i in (0, 1, side + 2, side + 3):
        dst_ref[i] = jnp.zeros(dst_ref.shape[1:], BF)
    for i in range(side):
        at = slice(i * plane, (i + 1) * plane)
        h = hid_ref[at, :].astype(F32)
        taps_ref[i, 0:hc] = (pltpu.roll(h, 1, 0) * before_ref[0:plane, :]).T.astype(BF)
        taps_ref[i, hc : 2 * hc] = h.T.astype(BF)
        taps_ref[i, 2 * hc : 3 * hc] = (pltpu.roll(h, plane - 1, 0) * after_ref[0:plane, :]).T.astype(BF)
        dst_ref[i + 2] = ds_ref[at, :].astype(F32).T.astype(BF)
    tg_ref[0 : 3 * hc, :] = sum(
        nn(taps_ref[i], dt_ref[i * plane : (i + 1) * plane, :]) for i in range(side)
    )
    tg_ref[3 * hc :, :] = jnp.zeros((tg_ref.shape[0] - 3 * hc, ch), F32)
    nz, _, width = sg_ref.shape
    size = 3 * hc // (2 * nz)
    vec_ref[...] = jnp.zeros(vec_ref.shape, F32)
    vec_ref[size : size + 2, 0:hc] = mid_ref[...]
    vec_ref[size + 2 : size + 4, 0:128] = out_ref[...]
    tall = vec_ref.shape[0]
    inside = lax.broadcasted_iota(jnp.int32, (tall, ch), 0) < size
    off = (width // 2) % 128
    for z in range(nz):
        first, second = [
            jnp.where(inside, tg_ref[b * size : b * size + tall, :], vec_ref[...])
            for b in (2 * z, 2 * z + 1)
        ]
        start = width // 2 - off
        sg_ref[z, hc : hc + tall, 0:ch] = first.astype(BF)
        second = pltpu.roll(jnp.concatenate([second, jnp.zeros((tall, 128), F32)], axis=1), off, 1)
        sg_ref[z, hc : hc + tall, start : start + ch + 128] = second.astype(BF)
    for c in range(3):
        acc = sum(
            nn(dst_ref[i : i + 3].reshape(3 * hc, plane), pad_ref[i, c * nf : c * nf + plane, :])
            for i in range(1, side + 1)
        )
        for r in range(3):
            first = (3 * r + c) * ch
            end = first + ch
            at = (2 - r) * hc
            done = 0
            while first < end:
                z = first // width
                last = min(end, (z + 1) * width)
                sg_ref[z, 0:hc, first - z * width : last - z * width] = (
                    acc[at : at + hc, done : done + last - first].astype(BF)
                )
                done += last - first
                first = last


def kernel_grads(pad, hidden, ds, dt, before, after, mid, out, side, shape, deps=()):
    pixels, hc = hidden.shape
    ch = dt.shape[1]
    plane = pixels // side
    outs = [jax.ShapeDtypeStruct(shape, BF)]
    tall = shape[1] - hc
    scratch = [
        pltpu.VMEM((side + 4, hc, plane), BF),
        pltpu.VMEM((side, 3 * hc, plane), BF),
        pltpu.VMEM((3 * hc + tall, ch), F32),
        pltpu.VMEM((tall, ch), F32),
    ]
    flops = 2 * pixels * hc * 12 * ch
    return call(functools.partial(grads_body, side), outs, scratch, flops,
                pad, hidden, ds, dt, before, after, mid, out, deps=deps)[0]


def copy_after_body(v_ref, out_ref):
    out_ref[...] = v_ref[...]


def after_all(v, *deps):
    return call(copy_after_body, [jax.ShapeDtypeStruct(v.shape, v.dtype)], [], v.size, v, deps=deps)[0]


def pack_kernels_body(kt_ref, lt_ref, vec_ref, out_ref, low_ref):
    ranks, _, width = out_ref.shape
    hc = kt_ref.shape[0] // ranks
    blocks = lt_ref.shape[0] // hc
    q = hc // ranks
    low_ref[...] = jnp.zeros(low_ref.shape, F32)
    for r in range(ranks):
        out_ref[r, 0:hc, :] = kt_ref[r * hc : (r + 1) * hc, :]
        for b in range(blocks):
            low_ref[r, b * q : (b + 1) * q, 0 : lt_ref.shape[1]] = (
                lt_ref[b * hc + r * q : b * hc + (r + 1) * q, :]
            )
        low_ref[r, blocks * q : blocks * q + 1, :] = vec_ref[...]
        out_ref[r, hc:, :] = low_ref[r].astype(BF)


def pack_kernels(kt, lt, vec, ranks, tall, deps):
    width = kt.shape[1]
    outs = [jax.ShapeDtypeStruct((ranks, kt.shape[0] // ranks + tall, width), BF)]
    scratch = [pltpu.VMEM((ranks, tall, width), F32)]
    return call(pack_kernels_body, outs, scratch, kt.size * 8, kt, lt, vec, deps=deps)[0]


def hop(v, k):
    n = 1
    for name in EVERY:
        n *= lax.axis_size(name)
    return lax.ppermute(v, EVERY, [(i, i ^ k) for i in range(n)])


def plane_gather(v, aside=()):
    got = {0: v}
    for k in (6, 2, 4):
        got[k] = hop(v, k)
    got[1] = hop(after_all(v, *aside) if aside else v, 1)
    for k in (2, 4, 6):
        got[k ^ 1] = hop(got[k], 1)
    return [got[k] for k in range(8)]


def plane_reduce(mate, keep, deps=()):
    sums = pair_sum(keep, hop(mate, 1), deps)
    arrived = {k: hop(sums[k // 2], k) for k in (6, 2, 4)}
    return [sums[0], arrived[2], arrived[4], arrived[6]]


def on_device(frames, cot, starts, ks, ktm, mg, mb, og, ob):
    nz, n_rank, n_seg = lax.axis_size("z"), 8, 4
    n_dp = nz * 2
    fr, side, ch = frames.shape[0], frames.shape[1], frames.shape[3]
    area = side * side
    hid = ks.shape[2]
    hc, cc = hid // n_rank, ch // n_rank
    q = hc // n_rank
    rank = lax.axis_index(PLANE)
    rank_now = rank.astype(jnp.int32).reshape(1)
    d_index = lax.axis_index(("z", "y"))
    nf = n_dp * fr
    pixels = area * nf
    half = pixels // 2

    to_plane = [(d * n_seg + s, s * n_rank + d) for d in range(n_dp) for s in range(n_seg)]
    from_plane = [(b, a) for a, b in to_plane]
    rows = fr * area
    flag_row = jnp.pad(starts.astype(BF)[None], ((0, 11), (0, ch - fr)))
    moving = jnp.concatenate([frames.reshape(rows, ch), flag_row], axis=0)
    moving = lax.ppermute(moving, EVERY, to_plane)

    perm = (jnp.arange(hid).reshape(n_rank, n_rank, q).transpose(1, 0, 2).reshape(hid)[:, None]
            == jnp.arange(hid)[None, :]).astype(BF)
    kt = lax.dot_general(perm, ks[0].astype(BF), (((1,), (1,)), ((), ())),
                         preferred_element_type=F32).astype(BF)
    lrows, width = ktm.shape[1] // n_rank, ks.shape[1]
    tall = -(-(lrows + 4) // 16) * 16
    extra = jnp.concatenate([mg, mb, og, ob], axis=1)
    extra = jnp.pad(extra, ((0, 0), (0, width - extra.shape[1])))
    w = pack_kernels(kt, ktm[0], extra, n_rank, tall, deps=(moving,))
    w = lax.all_to_all(w, PLANE, 0, 0)
    here = w
    high = hc + tall

    w = w.reshape(2, n_seg, high, width).transpose(1, 2, 0, 3).reshape(n_seg, high, 2 * width)
    ws = [lax.all_gather(w[s], "z", axis=0) for s in range(n_seg)]

    moving = after_all(moving, here)
    gathered = lax.all_to_all(jnp.broadcast_to(moving, (n_rank, *moving.shape)), PLANE, 0, 0)

    def norm_rows(rows_now):
        row = rows_now[:, (lrows - tall) % 16].reshape(n_dp, width).astype(F32)
        mid = jnp.stack([
            lax.dynamic_slice_in_dim(row[:, i * hc : (i + 1) * hc], rank * q, q, axis=1).reshape(hc)
            for i in range(2)])
        own = lax.dynamic_index_in_dim(row, rank, 0, keepdims=False)
        out = jnp.stack([
            jnp.tile(own[2 * hc + i * cc : 2 * hc + (i + 1) * cc], 2) for i in range(2)])
        return mid, out

    moving = after_all(moving, here)
    gathered = lax.all_to_all(jnp.broadcast_to(moving, (n_rank, *moving.shape)), PLANE, 0, 0)
    mids, outs = [], []
    for s in range(n_seg):
        row = ws[s][:, hc + lrows].reshape(n_dp, width).astype(F32)
        mids.append(jnp.stack([
            lax.dynamic_slice_in_dim(row[:, i * hc : (i + 1) * hc], rank * q, q, axis=1).reshape(hc)
            for i in range(2)]))
        own = lax.dynamic_index_in_dim(row, rank, 0, keepdims=False)
        outs.append(jnp.stack([
            jnp.tile(own[2 * hc + i * cc : 2 * hc + (i + 1) * cc], 2) for i in range(2)]))

    def by_pixel(v):
        width = v.shape[2]
        v = v.reshape(n_rank * fr, area, width).transpose(1, 0, 2)
        return v.reshape(pixels, width)

    def packed(v):
        return jnp.concatenate([v[:half], v[half:]], axis=1)

    a0 = by_pixel(gathered[:, :rows])
    flags = gathered[:, rows, :fr].reshape(nf) > 0.5
    slot = jnp.arange(nf) % fr
    before = jnp.where(flags | (slot == 0), 0.0, 1.0)
    after = jnp.where(jnp.roll(flags, -1) | (slot == fr - 1), 0.0, 1.0)
    spread = (side * nf + nf, hc)
    before = jnp.broadcast_to(jnp.tile(before, side + 1)[:, None], spread)
    after = jnp.broadcast_to(jnp.tile(after, side + 1)[:, None], spread)
    skip = packed(lax.dynamic_slice_in_dim(a0, rank * cc, cc, axis=1))

    def across(*slices):
        n = len(slices)
        v = jnp.stack([jnp.concatenate([v[:, :cc], v[:, cc:]], axis=0) for v in slices])
        v = v.reshape(n, area, n_rank, fr, cc).transpose(2, 0, 1, 3, 4).reshape(n_rank, n * rows, cc)
        return lax.all_to_all(v, PLANE, 0, 0)

    def home(v):
        n = v.shape[1] // rows
        v = v.transpose(1, 0, 2).reshape(n * rows, ch)
        v = lax.ppermute(v, EVERY, from_plane).reshape(n, area, fr, ch).transpose(0, 2, 1, 3)
        return v.reshape(n, *frames.shape)

    saved = []
    g = [a0]
    ready = prepare(ws[0], hc, ch)
    for s in range(n_seg):
        kn, lt, lnt, rows_now = ready
        mid, out = norm_rows(rows_now)
        deps = ()
        if s == n_seg - 1:
            cot_moving = after_all(cot.reshape(rows, ch), kn)
            deps = (cot_moving,)
            cot_moving = lax.ppermute(cot_moving, EVERY, to_plane)
            cot_moving = cot_moving.reshape(rows, n_rank, cc).transpose(1, 0, 2)
        pad, hidden, xm, rm, mate, keep = conv_forward(
            rank_now, g, kn, lt, mid, before, after, side, pixels, ch, deps=deps)
        parts = plane_reduce(mate, keep)
        deps = ()
        if s == n_seg - 1:
            cot_own = lax.all_to_all(after_all(cot_moving, parts[0]), PLANE, 0, 0)
            deps = (cot_own,)
        xo, ro, pre, res = out_norm(parts, out, skip if s % 2 == 1 else None, deps=deps)
        saved.append((pad, hidden, xm, rm, xo, ro, pre, lnt, mid, out))
        if s % 2 == 1:
            skip = res
        if s < n_seg - 1:
            ready = prepare(ws[s + 1], hc, ch, deps=(res,))
            g = plane_gather(res, ready[:1])
    cot_own = packed(by_pixel(cot_own))

    parts = [cot_own]
    skip_grad = None

    grads, raw = [], None
    for s in reversed(range(n_seg)):
        pad, hidden, xm, rm, xo, ro, pre, lnt, mid, out = saved[s]
        if s == 1:
            parts = parts + [skip_grad]
        deps = () if raw is None else (raw, *grads[len(grads) - 1 :])
        dpre, dt, osum = out_back(parts, pre, xo, ro, out, deps=deps)
        if raw is not None:
            grads.append(lax.psum_scatter(after_all(raw, dt), "z", scatter_dimension=0))
        if s % 2 == 1:
            skip_grad = dpre
        dtf, ds, msum, mate, keep = conv_back(
            rank_now, plane_gather(dt), xm, rm, ws[s], lnt, mid, before, after, side)
        if s > 0:
            parts = plane_reduce(mate, keep)
        raw = kernel_grads(pad, hidden, ds, dtf, before, after, msum, osum, side, ws[s].shape,
                           deps=parts[:1] if s > 0 else ())
    last = lax.psum_scatter(raw, "z", scatter_dimension=0)
    parts = plane_reduce(mate, keep, deps=(raw,))

    da = sum(p.astype(F32) for p in parts) + skip_grad.astype(F32)
    home_now = home(across(res, da.astype(BF)))
    output, frames_grad = home_now[0], home_now[1].astype(F32)

    def by_row(v):
        return v.reshape(high, 2, width).transpose(1, 0, 2)

    last = after_all(last, home_now)
    g = jnp.stack([by_row(v) for v in [last] + grads[::-1]], axis=1).reshape(n_rank, high, width)
    g = lax.all_to_all(g, PLANE, 0, 0)
    space_grad = lax.dot_general(g[:, :hc].reshape(hid, width), perm, (((0,), (0,)), ((), ())),
                                 preferred_element_type=F32)
    tg = g[:, hc : hc + lrows, :ch].reshape(n_rank, -1, q, ch)
    time_grad = tg.transpose(1, 0, 2, 3).reshape(-1, ch).astype(F32)
    sums = g[:, hc + lrows : hc + lrows + 4].astype(F32)

    def mid_own(v):
        return lax.dynamic_slice_in_dim(v[:, :hc], d_index * q, q, axis=1).reshape(1, hc)

    own = lax.dynamic_index_in_dim(sums, d_index, 0, keepdims=False)
    return (
        output,
        frames_grad,
        space_grad[None],
        time_grad[None],
        mid_own(sums[:, 0]),
        mid_own(sums[:, 1]),
        own[2:3, :cc],
        own[3:4, :cc],
    )


def from_behind(value, axis, steps):
    count = lax.axis_size(axis)
    leading, last = (max(0, -steps), min(count, count - steps))
    return lax.ppermute(value, axis, [(source, source + steps) for source in range(leading, last)])


def space_apply(current, kernel):
    frame_side = current.shape[1]
    padded = jnp.pad(current, ((0, 0), (1, 1), (1, 1), (0, 0)))
    stacked = jnp.concatenate(
        [
            padded[:, row_shift : row_shift + frame_side, col_shift : col_shift + frame_side, :]
            for row_shift in range(3)
            for col_shift in range(3)
        ],
        axis=-1,
    )
    return (
        stacked,
        jnp.einsum("fijc,co->fijo", stacked, kernel, preferred_element_type=jnp.float32),
    )


def space_back(gradient, kernel):
    frame_side = gradient.shape[1]
    channels = kernel.shape[0] // 9
    spread = jnp.einsum("fijo,co->fijc", gradient, kernel, preferred_element_type=jnp.float32)
    total = jnp.zeros((gradient.shape[0], frame_side + 2, frame_side + 2, channels), jnp.float32)
    for tap_index in range(9):
        row_shift = tap_index // 3
        col_shift = tap_index % 3
        piece_now = spread[..., tap_index * channels : (tap_index + 1) * channels]
        total = total + jnp.pad(
            piece_now, ((0, 0), (row_shift, 2 - row_shift), (col_shift, 2 - col_shift), (0, 0))
        )
    return total[:, 1 : frame_side + 1, 1 : frame_side + 1, :]


def time_apply(current, kernel, before_mask, after_mask):
    blanks = jnp.zeros_like(current[:1])
    earlier = jnp.concatenate([blanks, current[:-1]], axis=0) * before_mask[
        :, None, None, None
    ].astype(current.dtype)
    later = jnp.concatenate([current[1:], blanks], axis=0) * after_mask[:, None, None, None].astype(
        current.dtype
    )
    stacked = jnp.concatenate([earlier, current, later], axis=-1)
    return (
        stacked,
        jnp.einsum("fijc,co->fijo", stacked, kernel, preferred_element_type=jnp.float32),
    )


def time_back(gradient, kernel, before_mask, after_mask):
    channels = kernel.shape[0] // 3
    spread = jnp.einsum("fijo,co->fijc", gradient, kernel, preferred_element_type=jnp.float32)
    early_part = spread[..., :channels] * before_mask[:, None, None, None]
    late_part = spread[..., 2 * channels :] * after_mask[:, None, None, None]
    blanks = jnp.zeros_like(early_part[:1])
    moved_early = jnp.concatenate([early_part[1:], blanks], axis=0)
    moved_late = jnp.concatenate([blanks, late_part[:-1]], axis=0)
    return spread[..., channels : 2 * channels] + moved_early + moved_late


def moments(values, pixel_count):
    average = lax.psum(jnp.sum(values, axis=(0, 1, 2)), "dp") / pixel_count
    centered = values - average
    spread = lax.psum(jnp.sum(centered * centered, axis=(0, 1, 2)), "dp") / pixel_count
    return (average, lax.rsqrt(spread + eps))


def reduce_back(gradient, normed):
    return lax.psum(
        (jnp.sum(gradient, axis=(0, 1, 2)), jnp.sum(gradient * normed, axis=(0, 1, 2))), "dp"
    )


def silu_slope(values):
    sigmoid_now = jax.nn.sigmoid(values)
    return sigmoid_now * (1.0 + values * (1.0 - sigmoid_now))


def pick_slot(stack, slot_index):
    return lax.dynamic_index_in_dim(stack, slot_index, 0, keepdims=False)


def store_slot(stack, value, slot_index, usable):
    previous = pick_slot(stack, slot_index)
    return lax.dynamic_update_index_in_dim(stack, jnp.where(usable, value, previous), slot_index, 0)


def on_device_general(
    frames, cotangent, starts, space_kernel, time_kernel, mid_gain, mid_bias, out_gain, out_bias
):
    n_segment = lax.axis_size("segment")
    n_data = lax.axis_size("dp")
    segment_index = lax.axis_index("segment")
    odd_segment = segment_index % 2 == 1
    last_segment = segment_index == n_segment - 1
    first_segment = segment_index == 0
    frame_count = frames.shape[0]
    frame_side = frames.shape[1]
    channels = frames.shape[3]
    hidden_units = mid_gain.shape[1] * n_data
    pixel_count = n_data * frame_count * frame_side * frame_side
    turns = 2 * n_segment - 1
    block_shape = (n_segment,) + frames.shape
    all_frames, all_cot, all_starts = (
        lax.all_gather(frames, "segment", axis=0, tiled=True),
        lax.all_gather(cotangent, "segment", axis=0, tiled=True),
        lax.all_gather(starts.astype(jnp.bfloat16), "segment", axis=0, tiled=True),
    )
    frame_stack = all_frames.reshape(block_shape)
    cot_stack = all_cot.reshape(block_shape)
    clip_flags = all_starts.astype(jnp.float32).reshape(n_segment, frame_count)
    positions = jnp.arange(frame_count)
    before_mask = jnp.where((clip_flags > 0.5) | (positions == 0), 0.0, 1.0)
    following = jnp.concatenate([clip_flags[:, 1:], jnp.ones((n_segment, 1), jnp.float32)], axis=1)
    after_mask = jnp.where(following > 0.5, 0.0, 1.0)
    gathered = (
        lax.all_gather(space_kernel[0].astype(jnp.bfloat16), "dp", axis=0, tiled=True),
        lax.all_gather(time_kernel[0].astype(jnp.bfloat16), "dp", axis=0, tiled=True),
        lax.all_gather(mid_gain[0].astype(jnp.bfloat16), "dp", axis=0, tiled=True),
        lax.all_gather(mid_bias[0].astype(jnp.bfloat16), "dp", axis=0, tiled=True),
        lax.all_gather(out_gain[0].astype(jnp.bfloat16), "dp", axis=0, tiled=True),
        lax.all_gather(out_bias[0].astype(jnp.bfloat16), "dp", axis=0, tiled=True),
    )
    space_low, time_low = (gathered[0], gathered[1])
    mid_gain_now = gathered[2].astype(jnp.float32)
    mid_bias_now = gathered[3].astype(jnp.float32)
    out_gain_now = gathered[4].astype(jnp.float32)
    out_bias_now = gathered[5].astype(jnp.float32)
    incoming = jnp.zeros_like(frames)
    carried = jnp.zeros_like(frames)
    kept_input = jnp.zeros(block_shape, jnp.bfloat16)
    kept_skip = jnp.zeros(block_shape, jnp.bfloat16)
    kept_mid_mean = jnp.zeros((n_segment, hidden_units), jnp.float32)
    kept_mid_scale = jnp.zeros((n_segment, hidden_units), jnp.float32)
    kept_out_mean = jnp.zeros((n_segment, channels), jnp.float32)
    kept_out_scale = jnp.zeros((n_segment, channels), jnp.float32)
    results = jnp.zeros(block_shape, jnp.float32)
    for turn_index in range(turns):
        micro_index = turn_index - segment_index
        usable = (micro_index >= 0) & (micro_index < n_segment)
        slot_index = jnp.clip(micro_index, 0, n_segment - 1)
        current = jnp.where(first_segment, pick_slot(frame_stack, slot_index), incoming)
        skip_input = carried
        _, spatial = space_apply(current, space_low)
        mid_mean, mid_scale = moments(spatial, pixel_count)
        hidden_act = jax.nn.silu(
            (spatial - mid_mean) * mid_scale * mid_gain_now + mid_bias_now
        ).astype(jnp.bfloat16)
        _, temporal = time_apply(
            hidden_act,
            time_low,
            pick_slot(before_mask, slot_index),
            pick_slot(after_mask, slot_index),
        )
        out_mean, out_scale = moments(temporal, pixel_count)
        pre_act = (
            (temporal - out_mean) * out_scale * out_gain_now
            + out_bias_now
            + jnp.where(odd_segment, skip_input.astype(jnp.float32), 0.0)
        )
        result = jax.nn.silu(pre_act).astype(jnp.bfloat16)
        kept_input = store_slot(kept_input, current, slot_index, usable)
        kept_skip = store_slot(kept_skip, skip_input, slot_index, usable)
        kept_mid_mean = store_slot(kept_mid_mean, mid_mean, slot_index, usable)
        kept_mid_scale = store_slot(kept_mid_scale, mid_scale, slot_index, usable)
        kept_out_mean = store_slot(kept_out_mean, out_mean, slot_index, usable)
        kept_out_scale = store_slot(kept_out_scale, out_scale, slot_index, usable)
        results = store_slot(results, result.astype(jnp.float32), slot_index, usable)
        if turn_index < turns - 1:
            incoming, carried = from_behind(
                (result, jnp.where(odd_segment, result, current)), "segment", 1
            )
    gathered = (
        lax.all_gather(space_kernel[0].astype(jnp.bfloat16), "dp", axis=0, tiled=True),
        lax.all_gather(time_kernel[0].astype(jnp.bfloat16), "dp", axis=0, tiled=True),
        lax.all_gather(mid_gain[0].astype(jnp.bfloat16), "dp", axis=0, tiled=True),
        lax.all_gather(mid_bias[0].astype(jnp.bfloat16), "dp", axis=0, tiled=True),
        lax.all_gather(out_gain[0].astype(jnp.bfloat16), "dp", axis=0, tiled=True),
        lax.all_gather(out_bias[0].astype(jnp.bfloat16), "dp", axis=0, tiled=True),
    )
    space_low, time_low = (gathered[0], gathered[1])
    mid_gain_now = gathered[2].astype(jnp.float32)
    mid_bias_now = gathered[3].astype(jnp.float32)
    out_gain_now = gathered[4].astype(jnp.float32)
    out_bias_now = gathered[5].astype(jnp.float32)
    grad_input = jnp.zeros_like(frames)
    grad_skip = jnp.zeros_like(frames)
    space_acc = jnp.zeros(space_low.shape, jnp.float32)
    time_acc = jnp.zeros(time_low.shape, jnp.float32)
    mid_gain_acc = jnp.zeros((hidden_units,), jnp.float32)
    mid_bias_acc = jnp.zeros((hidden_units,), jnp.float32)
    out_gain_acc = jnp.zeros((channels,), jnp.float32)
    out_bias_acc = jnp.zeros((channels,), jnp.float32)
    input_grads = jnp.zeros(block_shape, jnp.float32)
    for turn_index in range(turns):
        micro_index = n_segment - 1 - (turn_index - (n_segment - 1 - segment_index))
        usable = (micro_index >= 0) & (micro_index < n_segment)
        usable_weight = usable.astype(jnp.float32)
        slot_index = jnp.clip(micro_index, 0, n_segment - 1)
        current = pick_slot(kept_input, slot_index)
        skip_input = pick_slot(kept_skip, slot_index)
        before_now = pick_slot(before_mask, slot_index)
        after_now = pick_slot(after_mask, slot_index)
        space_taps, spatial = space_apply(current, space_low)
        mid_normed = (spatial - pick_slot(kept_mid_mean, slot_index)) * pick_slot(
            kept_mid_scale, slot_index
        )
        mid_pre = mid_normed * mid_gain_now + mid_bias_now
        hidden_act = jax.nn.silu(mid_pre).astype(jnp.bfloat16)
        time_taps, temporal = time_apply(hidden_act, time_low, before_now, after_now)
        out_scale = pick_slot(kept_out_scale, slot_index)
        out_normed = (temporal - pick_slot(kept_out_mean, slot_index)) * out_scale
        pre_act = (
            out_normed * out_gain_now
            + out_bias_now
            + jnp.where(odd_segment, skip_input.astype(jnp.float32), 0.0)
        )
        grad_result = jnp.where(
            last_segment,
            pick_slot(cot_stack, slot_index).astype(jnp.float32),
            grad_input.astype(jnp.float32)
            + jnp.where(odd_segment, grad_skip.astype(jnp.float32), 0.0),
        )
        grad_pre = grad_result * silu_slope(pre_act)
        out_bias_sum, out_gain_sum = reduce_back(grad_pre, out_normed)
        grad_temporal = (
            out_gain_now
            * out_scale
            * (grad_pre - out_bias_sum / pixel_count - out_normed * out_gain_sum / pixel_count)
        ).astype(jnp.bfloat16)
        time_acc = time_acc + usable_weight * jnp.einsum(
            "fijc,fijo->co", time_taps, grad_temporal, preferred_element_type=jnp.float32
        )
        grad_hidden = time_back(grad_temporal, time_low, before_now, after_now)
        grad_mid = grad_hidden * silu_slope(mid_pre)
        mid_bias_sum, mid_gain_sum = reduce_back(grad_mid, mid_normed)
        mid_scale = pick_slot(kept_mid_scale, slot_index)
        grad_spatial = (
            mid_gain_now
            * mid_scale
            * (grad_mid - mid_bias_sum / pixel_count - mid_normed * mid_gain_sum / pixel_count)
        ).astype(jnp.bfloat16)
        space_acc = space_acc + usable_weight * jnp.einsum(
            "fijc,fijo->co", space_taps, grad_spatial, preferred_element_type=jnp.float32
        )
        grad_current = space_back(grad_spatial, space_low)
        mid_gain_acc = mid_gain_acc + usable_weight * mid_gain_sum
        mid_bias_acc = mid_bias_acc + usable_weight * mid_bias_sum
        out_gain_acc = out_gain_acc + usable_weight * out_gain_sum
        out_bias_acc = out_bias_acc + usable_weight * out_bias_sum
        input_grads = store_slot(
            input_grads, grad_current + grad_skip.astype(jnp.float32), slot_index, usable
        )
        if turn_index < turns - 1:
            grad_input, grad_skip = from_behind(
                (
                    grad_current.astype(jnp.bfloat16),
                    jnp.where(odd_segment, grad_pre.astype(jnp.bfloat16), grad_skip),
                ),
                "segment",
                -1,
            )
    space_grad, time_grad = (
        lax.psum_scatter(space_acc, "dp", scatter_dimension=0, tiled=True),
        lax.psum_scatter(time_acc, "dp", scatter_dimension=0, tiled=True),
    )
    data_index = lax.axis_index("dp")

    def own_share(full_vector):
        share = full_vector.shape[0] // n_data
        return lax.dynamic_slice_in_dim(full_vector, data_index * share, share)[None]

    flat_shape = (n_segment * frame_count,) + frames.shape[1:]
    arrived_out, arrived_grads = (
        lax.all_to_all(
            results.reshape(flat_shape).astype(jnp.bfloat16),
            "segment",
            split_axis=0,
            concat_axis=0,
            tiled=True,
        ).astype(jnp.float32),
        lax.all_to_all(
            input_grads.reshape(flat_shape).astype(jnp.bfloat16),
            "segment",
            split_axis=0,
            concat_axis=0,
            tiled=True,
        ).astype(jnp.float32),
    )
    output = arrived_out[(n_segment - 1) * frame_count :].astype(jnp.bfloat16)
    frames_grad = arrived_grads[:frame_count]
    return (
        output,
        frames_grad,
        space_grad[None],
        time_grad[None],
        own_share(mid_gain_acc),
        own_share(mid_bias_acc),
        own_share(out_gain_acc),
        own_share(out_bias_acc),
    )


def general(mesh):
    return jax.shard_map(
        on_device_general,
        mesh=mesh,
        in_specs=(
            P(("dp", "segment"), None, None, None),
            P(("dp", "segment"), None, None, None),
            P(("dp", "segment")),
            P("segment", "dp", None),
            P("segment", "dp", None),
            P("segment", "dp"),
            P("segment", "dp"),
            P("segment", "dp"),
            P("segment", "dp"),
        ),
        out_specs=(
            P(("dp", "segment"), None, None, None),
            P(("dp", "segment"), None, None, None),
            P("segment", "dp", None),
            P("segment", "dp", None),
            P("segment", "dp"),
            P("segment", "dp"),
            P("segment", "dp"),
            P("segment", "dp"),
        ),
        check_vma=False,
    )


def solution(mesh):
    if mesh.shape["dp"] != 8 or mesh.shape["segment"] != 4:
        return general(mesh)
    n_dp, n_seg = mesh.shape["dp"], mesh.shape["segment"]
    fine = Mesh(mesh.devices.reshape(n_dp // 2, 2, 2, n_seg // 2), EVERY)
    dp, seg = ("z", "y"), ("x", "c")
    return jax.shard_map(
        on_device,
        mesh=fine,
        in_specs=(
            P(EVERY, None, None, None),
            P(EVERY, None, None, None),
            P(EVERY),
            P(seg, dp, None),
            P(seg, dp, None),
            P(seg, dp),
            P(seg, dp),
            P(seg, dp),
            P(seg, dp),
        ),
        out_specs=(
            P(EVERY, None, None, None),
            P(EVERY, None, None, None),
            P(seg, dp, None),
            P(seg, dp, None),
            P(seg, dp),
            P(seg, dp),
            P(seg, dp),
            P(seg, dp),
        ),
        check_vma=False,
    )
```

```python
import functools

import jax
import jax.numpy as jnp
from jax import lax
from jax.experimental import pallas as pl
from jax.experimental.pallas import tpu as pltpu
from jax.sharding import Mesh, PartitionSpec as P

eps = 1e-05
PLANE = ("y", "x", "c")
EVERY = ("z", "y", "x", "c")
BF = jnp.bfloat16
F32 = jnp.float32


def nt(a, b):
    return lax.dot_general(a, b, (((1,), (1,)), ((), ())), preferred_element_type=F32)


def nn(a, b):
    return lax.dot_general(a, b, (((1,), (0,)), ((), ())), preferred_element_type=F32)


VMEM_CAP = 56 * 1024 * 1024
ANY = pl.BlockSpec(memory_space=pl.ANY)


def call(body, outs, scratch, flops, *args, deps=(), far=(), far_outs=()):
    moved = sum(a.size * a.dtype.itemsize for a in args) + sum(
        o.size * o.dtype.itemsize for o in outs
    )
    n = len(deps)

    def spec(a):
        return pl.BlockSpec(memory_space=pltpu.SMEM if a.dtype == jnp.int32 else pltpu.VMEM)

    return pl.pallas_call(
        lambda *refs: body(*refs[n:]),
        out_shape=outs,
        in_specs=[ANY] * n + [ANY if i in far else spec(a) for i, a in enumerate(args)],
        out_specs=[ANY if i in far_outs else spec(o) for i, o in enumerate(outs)],
        scratch_shapes=scratch,
        compiler_params=pltpu.CompilerParams(vmem_limit_bytes=VMEM_CAP),
        cost_estimate=pl.CostEstimate(flops=flops, bytes_accessed=moved, transcendentals=0),
    )(*deps, *args)


def chunk(i, size):
    return pl.ds(pl.multiple_of(i * size, 16), size)


def clear_borders(pad_ref, side, plane, nf):
    zrow = jnp.zeros(pad_ref.shape[1:], BF)
    pad_ref[0] = zrow
    pad_ref[side + 1] = zrow
    zcol = jnp.zeros((nf, pad_ref.shape[2]), BF)
    for i in range(side):
        pad_ref[i + 1, 0:nf] = zcol
        pad_ref[i + 1, nf + plane : 2 * nf + plane] = zcol


def by_rank(slices, rank):
    odd = lax.rem(rank, 2) == 1
    for p in range(len(slices) // 2):
        a, b = slices[2 * p], slices[2 * p + 1]
        yield lax.bitwise_xor(rank // 2, p), odd, a, b


def halves(odd, own, mate):
    low = lax.broadcasted_iota(jnp.int32, own.shape, 1) < 64
    own, mate = own.astype(F32), mate.astype(F32)
    a, b = jnp.where(odd, mate, own), jnp.where(odd, own, mate)
    top = jnp.where(low, a, pltpu.roll(b, 64, 1))
    bottom = jnp.where(low, pltpu.roll(a, 64, 1), b)
    return top, bottom


def store_packed(rank, mate_ref, keep_ref, part, k, step, low):
    rows_now = chunk(k, step)
    odd = lax.rem(rank, 2) == 1
    for q in range(keep_ref.shape[0]):
        x = part[:step, 128 * q : 128 * q + 128]
        y = part[step:, 128 * q : 128 * q + 128]
        even_slice = jnp.where(low, x, pltpu.roll(y, 64, 1))
        odd_slice = jnp.where(low, pltpu.roll(x, 64, 1), y)
        p = lax.bitwise_xor(rank // 2, q)
        keep_ref[p, rows_now, :] = jnp.where(odd, odd_slice, even_slice).astype(BF)
        mate_ref[p, rows_now, :] = jnp.where(odd, even_slice, odd_slice).astype(BF)


def fetch_kernels(w_ref, ktm_ref, lw_ref, sems):
    nz, _, width = w_ref.shape
    hc = ktm_ref.shape[0]
    copies = []
    for z in range(nz):
        copies.append(pltpu.make_async_copy(
            w_ref.at[z, pl.ds(0, hc)], ktm_ref.at[:, pl.ds(z * width, width)], sems.at[2 * z]))
        copies.append(pltpu.make_async_copy(
            w_ref.at[z, pl.ds(hc, lw_ref.shape[1])], lw_ref.at[z], sems.at[2 * z + 1]))
    for copy in copies:
        copy.start()
    return copies


def join_temporal(lw_ref, lf_ref, ltm_ref):
    ch = ltm_ref.shape[1]
    width = lw_ref.shape[2] // 2
    count = 2 * lw_ref.shape[0]
    size = ltm_ref.shape[0] // count
    for z in range(lw_ref.shape[0]):
        first = lw_ref[z, :, 0:ch].astype(F32)
        off = width % 128
        second = lw_ref[z, :, width - off : width - off + ch + 128].astype(F32)
        second = pltpu.roll(second, ch + 128 - off, 1)[:, 0:ch]
        for b, block in ((2 * z, first), (2 * z + 1, second)):
            lf_ref[b * size : b * size + block.shape[0], :] = block
    ltm_ref[...] = lf_ref[0 : ltm_ref.shape[0], :].astype(BF)


def chunk_copies(k, step, sems, *pairs):
    rows = chunk(k, step)
    return [
        pltpu.make_async_copy(here.at[:, rows], there.at[:, rows], sems.at[i, k])
        for i, (here, there) in enumerate(pairs)
    ]


def prepare_body(w_ref, kn_out, l_out, lt_out, rows_out, ktm_ref, lw_ref, lf_ref, sems):
    hc, ch = ktm_ref.shape[0], l_out.shape[1]
    for copy in fetch_kernels(w_ref, ktm_ref, lw_ref, sems):
        copy.wait()
    for t in range(9):
        kn_out[t] = ktm_ref[:, t * ch : (t + 1) * ch].astype(F32).T.astype(BF)
    join_temporal(lw_ref, lf_ref, l_out)
    rows_out[...] = lw_ref[:, lw_ref.shape[1] - rows_out.shape[1] :, :]
    for t in range(3):
        lt_out[t] = lf_ref[t * hc : (t + 1) * hc].T.astype(BF)


def prepare(w, hc, ch, deps=()):
    outs = [
        jax.ShapeDtypeStruct((9, ch, hc), BF),
        jax.ShapeDtypeStruct((3 * hc, ch), BF),
        jax.ShapeDtypeStruct((3, ch, hc), BF),
        jax.ShapeDtypeStruct((w.shape[0], 16, w.shape[2]), BF),
    ]
    tall = w.shape[1] - hc
    scratch = [
        pltpu.VMEM((hc, 9 * ch), BF),
        pltpu.VMEM((w.shape[0], tall, w.shape[2]), BF),
        pltpu.VMEM((3 * hc + tall, ch), F32),
        pltpu.SemaphoreType.DMA((2 * w.shape[0],)),
    ]
    return call(prepare_body, outs, scratch, 2 * w.size * 512, w, deps=deps, far=(0,))


def conv_body(side, first, rank_ref, *refs):
    n = 1 if first else 8
    slices = refs[:n]
    (kn_in, ltm_ref, vec_ref, before_ref, after_ref,
     pad_out, hid_out, xhat_out, rs_ref, mate_out, keep_out,
     pad_ref, hid_ref, xhat_ref, mate_ref, keep_ref, sp_ref, kn_ref, sems, leave) = refs[n:]
    rank = rank_ref[0]
    kn_copy = pltpu.make_async_copy(kn_in, kn_ref, sems.at[0])
    kn_copy.start()
    ch, hc = pad_ref.shape[2], hid_ref.shape[1]
    rows = hid_ref.shape[0]
    plane = rows // side
    nf = plane // side
    step = plane // 2
    clear_borders(pad_ref, side, plane, nf)
    if first:
        for i in range(side):
            pad_ref[i + 1, nf : nf + plane] = slices[0][i * plane : (i + 1) * plane]
    else:
        def place(k, carry):
            for q, odd, a_ref, b_ref in by_rank(slices, rank):
                top, bottom = halves(odd, a_ref[chunk(k, step), :], b_ref[chunk(k, step), :])
                lanes = pl.ds(pl.multiple_of(128 * q, 128), 128)
                for piece, kk in ((top, k), (bottom, k + side)):
                    at = nf + lax.rem(kk, 2) * step
                    pad_ref[1 + kk // 2, pl.ds(pl.multiple_of(at, 16), step), lanes] = piece.astype(BF)
            return carry

        lax.fori_loop(0, side, place, 0, unroll=True)
    pad_copy = pltpu.make_async_copy(pad_ref, pad_out, sems.at[1])
    pad_copy.start()
    kn_copy.wait()

    def conv(i, total):
        acc = jnp.zeros((plane, hc), F32)
        for t in range(9):
            r, c = t // 3, t % 3
            acc += nn(pad_ref[i + r, c * nf : c * nf + plane, :], kn_ref[t])
        sp_ref[i] = acc
        return total + jnp.sum(acc, axis=0, keepdims=True)

    mean = lax.fori_loop(0, side, conv, jnp.zeros((1, hc), F32), unroll=True) / rows

    def square(i, total):
        cen = sp_ref[i] - mean
        return total + jnp.sum(cen * cen, axis=0, keepdims=True)

    var = lax.fori_loop(0, side, square, jnp.zeros((1, hc), F32), unroll=True) / rows
    rs = lax.rsqrt(var + eps)
    rs_ref[...] = rs
    gain, bias = vec_ref[0:1, :], vec_ref[1:2, :]

    def act(i, carry):
        xhat = (sp_ref[i] - mean) * rs
        xhat_ref[i] = xhat
        v = xhat * gain + bias
        v = v * jax.nn.sigmoid(v)
        sp_ref[i] = v
        hid_ref[chunk(i, plane), :] = v.astype(BF)
        return carry

    lax.fori_loop(0, side, act, 0, unroll=True)
    late = [
        pltpu.make_async_copy(hid_ref, hid_out, sems.at[2]),
        pltpu.make_async_copy(xhat_ref, xhat_out, sems.at[3]),
    ]
    for copy in late:
        copy.start()
    low = lax.broadcasted_iota(jnp.int32, (step, 128), 1) < 64

    def temporal(k, carry):
        pieces = []
        for kk in (k, k + side):
            par = lax.rem(kk, 2)
            h = sp_ref[kk // 2, pl.ds(pl.multiple_of(par * step, 8), step), :]
            at = pl.multiple_of(par * (step % nf), 8)
            pieces.append((
                (pltpu.roll(h, 1, 0) * before_ref[pl.ds(at, step), :]).astype(BF),
                h.astype(BF),
                (pltpu.roll(h, step - 1, 0) * after_ref[pl.ds(at, step), :]).astype(BF),
            ))
        part = sum(
            nn(jnp.concatenate([x, y], axis=0), ltm_ref[t * hc : (t + 1) * hc])
            for t, (x, y) in enumerate(zip(*pieces))
        )
        store_packed(rank, mate_ref, keep_ref, part, k, step, low)
        for copy in chunk_copies(k, step, leave, (mate_ref, mate_out), (keep_ref, keep_out)):
            copy.start()
        return carry

    lax.fori_loop(0, side, temporal, 0, unroll=True)
    for k in range(side):
        late += chunk_copies(k, step, leave, (mate_ref, mate_out), (keep_ref, keep_out))
    for copy in [pad_copy] + late:
        copy.wait()


def conv_forward(rank, g, kn, lt, vec, before, after, side, pixels, ch, deps=()):
    hc = vec.shape[1]
    plane = pixels // side
    nf = plane // side
    n = len(g)
    shapes = [
        ((side + 2, plane + 2 * nf, ch), BF),
        ((pixels, hc), BF),
        ((side, plane, hc), F32),
        ((4, pixels // 2, 128), BF),
        ((4, pixels // 2, 128), BF),
    ]
    outs = [jax.ShapeDtypeStruct(*s) for s in shapes]
    outs.insert(3, jax.ShapeDtypeStruct((1, hc), F32))
    scratch = [pltpu.VMEM(*s) for s in shapes] + [
        pltpu.VMEM((side, plane, hc), F32),
        pltpu.VMEM((9, ch, hc), BF),
        pltpu.SemaphoreType.DMA((4,)),
        pltpu.SemaphoreType.DMA((2, side)),
    ]
    flops = 2 * pixels * hc * 12 * ch
    return call(functools.partial(conv_body, side, n == 1), outs, scratch, flops,
                rank, *g, kn, lt, vec, before, after,
                deps=deps, far=(n + 1,), far_outs=(0, 1, 2, 4, 5))


def fold(v):
    return v + pltpu.roll(v, 64, 1)


def total_of(refs):
    t = refs[0][...].astype(F32)
    for ref in refs[1:]:
        t += ref[...].astype(F32)
    return t


def pair_sum_body(keep_ref, mate_ref, *out_refs):
    for p, ref in enumerate(out_refs):
        ref[...] = (keep_ref[p].astype(F32) + mate_ref[p].astype(F32)).astype(ref.dtype)


def pair_sum(keep, arrived, deps=()):
    shape = keep.shape[1:]
    outs = [jax.ShapeDtypeStruct(shape, BF)] * keep.shape[0]
    return call(pair_sum_body, outs, [], keep.size, keep, arrived, deps=deps)


def out_norm_body(n, has_skip, *refs):
    parts, refs = refs[:n], refs[n:]
    if has_skip:
        vec_ref, skip_ref, xhat_ref, rs_ref, pre_ref, res_ref = refs
    else:
        vec_ref, xhat_ref, rs_ref, pre_ref, res_ref = refs
    t = total_of(parts)
    pixels = 2 * t.shape[0]
    mean = fold(jnp.sum(t, axis=0, keepdims=True)) / pixels
    cen = t - mean
    rs = lax.rsqrt(fold(jnp.sum(cen * cen, axis=0, keepdims=True)) / pixels + eps)
    xhat = cen * rs
    pre = xhat * vec_ref[0:1, :] + vec_ref[1:2, :]
    if has_skip:
        pre = pre + skip_ref[...].astype(F32)
    xhat_ref[...] = xhat
    rs_ref[...] = rs
    pre_ref[...] = pre
    res_ref[...] = (pre * jax.nn.sigmoid(pre)).astype(BF)


def out_norm(parts, vec, skip, deps=()):
    half = parts[0].shape[0]
    outs = [
        jax.ShapeDtypeStruct((half, 128), F32),
        jax.ShapeDtypeStruct((1, 128), F32),
        jax.ShapeDtypeStruct((half, 128), F32),
        jax.ShapeDtypeStruct((half, 128), BF),
    ]
    args = (*parts, vec) + (() if skip is None else (skip,))
    body = functools.partial(out_norm_body, len(parts), skip is not None)
    return call(body, outs, [], half * 128 * 10, *args, deps=deps)


def out_back_body(n, *refs):
    parts, (pre_ref, xhat_ref, rs_ref, vec_ref, dpre_ref, dt_ref, sums_ref) = refs[:n], refs[n:]
    g = total_of(parts)
    pre, xhat = pre_ref[...], xhat_ref[...]
    sig = jax.nn.sigmoid(pre)
    dpre = g * (sig * (1.0 + pre * (1.0 - sig)))
    pixels = 2 * pre.shape[0]
    sb = fold(jnp.sum(dpre, axis=0, keepdims=True))
    sg = fold(jnp.sum(dpre * xhat, axis=0, keepdims=True))
    dpre_ref[...] = dpre.astype(BF)
    scale = vec_ref[0:1, :] * rs_ref[...]
    dt_ref[...] = (scale * (dpre - sb / pixels - xhat * (sg / pixels))).astype(BF)
    sums_ref[0:1, :] = sg
    sums_ref[1:2, :] = sb


def out_back(parts, pre, xhat, rs, vec, deps=()):
    half = pre.shape[0]
    outs = [
        jax.ShapeDtypeStruct((half, 128), BF),
        jax.ShapeDtypeStruct((half, 128), BF),
        jax.ShapeDtypeStruct((2, 128), F32),
    ]
    args = (*parts, pre, xhat, rs, vec)
    return call(functools.partial(out_back_body, len(parts)), outs, [], half * 1280, *args, deps=deps)


def conv_back_body(side, rank_ref, *refs):
    slices, (xhat_in, rs_ref, w_ref, lnt_ref, vec_ref, before_ref, after_ref,
             dt_out, ds_out, sums_ref, mate_out, keep_out,
             dt_ref, ds_ref, mate_ref, keep_ref, xhat_ref, dy_ref, pad_ref, ktm_ref, sems,
             leave) = refs[:8], refs[8:]
    half = slices[0].shape[0]
    rank = rank_ref[0]
    nz, _, width = w_ref.shape
    rows = 2 * half
    plane = rows // side
    nf = plane // side
    step = plane // 2
    hc = ds_ref.shape[1]
    ch = dt_ref.shape[1]
    fetched = [
        pltpu.make_async_copy(
            w_ref.at[z, pl.ds(0, hc)], ktm_ref.at[:, pl.ds(z * width, width)], sems.at[z])
        for z in range(nz)
    ]
    xhat_copy = pltpu.make_async_copy(xhat_in, xhat_ref, sems.at[nz])
    for copy in fetched + [xhat_copy]:
        copy.start()
    clear_borders(pad_ref, side, plane, nf)

    def place(k, carry):
        for q, odd, a_ref, b_ref in by_rank(slices, rank):
            top, bottom = halves(odd, a_ref[chunk(k, step), :], b_ref[chunk(k, step), :])
            lanes = pl.ds(pl.multiple_of(128 * q, 128), 128)
            dt_ref[chunk(k, step), lanes] = top.astype(BF)
            dt_ref[pl.ds(pl.multiple_of(half + k * step, 16), step), lanes] = bottom.astype(BF)
        return carry

    lax.fori_loop(0, side, place, 0, unroll=True)
    dt_copy = pltpu.make_async_copy(dt_ref, dt_out, sems.at[nz + 1])
    dt_copy.start()
    xhat_copy.wait()
    gain, bias = vec_ref[0:1, :], vec_ref[1:2, :]

    def hidden_grad(i, sums):
        dt = dt_ref[chunk(i, plane), :]
        early = nn(dt, lnt_ref[0]) * before_ref[0:plane, :]
        late = nn(dt, lnt_ref[2]) * after_ref[0:plane, :]
        dh = nn(dt, lnt_ref[1]) + pltpu.roll(early, plane - 1, 0) + pltpu.roll(late, 1, 0)
        xhat = xhat_ref[i]
        v = xhat * gain + bias
        sig = jax.nn.sigmoid(v)
        dy = dh * (sig * (1.0 + v * (1.0 - sig)))
        dy_ref[i] = dy
        return (
            sums[0] + jnp.sum(dy * xhat, axis=0, keepdims=True),
            sums[1] + jnp.sum(dy, axis=0, keepdims=True),
        )

    zero = jnp.zeros((1, hc), F32)
    sg, sb = lax.fori_loop(0, side, hidden_grad, (zero, zero), unroll=True)
    sums_ref[0:1, :] = sg
    sums_ref[1:2, :] = sb
    scale = gain * rs_ref[...]

    def spatial_grad(i, carry):
        ds = (scale * (dy_ref[i] - sb / rows - xhat_ref[i] * (sg / rows))).astype(BF)
        pad_ref[i + 1, nf : nf + plane] = ds
        ds_ref[chunk(i, plane), :] = ds
        return carry

    lax.fori_loop(0, side, spatial_grad, 0, unroll=True)
    ds_copy = pltpu.make_async_copy(ds_ref, ds_out, sems.at[nz + 2])
    ds_copy.start()
    for copy in fetched:
        copy.wait()
    low = lax.broadcasted_iota(jnp.int32, (step, 128), 1) < 64

    def back(k, carry):
        acc = jnp.zeros((2 * step, ch), F32)
        for t in range(9):
            r, c = 2 - t // 3, 2 - t % 3
            pieces = []
            for kk in (k, k + side):
                at = c * nf + lax.rem(kk, 2) * step
                pieces.append(pad_ref[kk // 2 + r, pl.ds(pl.multiple_of(at, 16), step), :])
            acc += nn(jnp.concatenate(pieces, axis=0), ktm_ref[:, t * ch : (t + 1) * ch])
        store_packed(rank, mate_ref, keep_ref, acc, k, step, low)
        for copy in chunk_copies(k, step, leave, (mate_ref, mate_out), (keep_ref, keep_out)):
            copy.start()
        return carry

    lax.fori_loop(0, side, back, 0, unroll=True)
    late = [dt_copy, ds_copy]
    for k in range(side):
        late += chunk_copies(k, step, leave, (mate_ref, mate_out), (keep_ref, keep_out))
    for copy in late:
        copy.wait()


def conv_back(rank, g, xhat, rs, w, lnt, vec, before, after, side, deps=()):
    half = g[0].shape[0]
    hc = vec.shape[1]
    ch = len(g) * 64
    pixels = 2 * half
    plane = pixels // side
    nf = plane // side
    outs = [
        jax.ShapeDtypeStruct((pixels, ch), BF),
        jax.ShapeDtypeStruct((pixels, hc), BF),
        jax.ShapeDtypeStruct((2, hc), F32),
        jax.ShapeDtypeStruct((4, half, 128), BF),
        jax.ShapeDtypeStruct((4, half, 128), BF),
    ]
    scratch = [
        pltpu.VMEM((pixels, ch), BF),
        pltpu.VMEM((pixels, hc), BF),
        pltpu.VMEM((4, half, 128), BF),
        pltpu.VMEM((4, half, 128), BF),
        pltpu.VMEM((side, plane, hc), F32),
        pltpu.VMEM((side, plane, hc), F32),
        pltpu.VMEM((side + 2, plane + 2 * nf, hc), BF),
        pltpu.VMEM((hc, 9 * ch), BF),
        pltpu.SemaphoreType.DMA((w.shape[0] + 3,)),
        pltpu.SemaphoreType.DMA((2, side)),
    ]
    flops = 2 * pixels * hc * 12 * ch
    return call(functools.partial(conv_back_body, side), outs, scratch, flops,
                rank, *g, xhat, rs, w, lnt, vec, before, after,
                deps=deps, far=(9, 11), far_outs=(0, 1, 3, 4))


def grads_body(side, pad_ref, hid_ref, ds_ref, dt_ref, before_ref, after_ref, mid_ref, out_ref,
               sg_ref, dst_ref, taps_ref, tg_ref, vec_ref):
    ch = pad_ref.shape[2]
    hc = hid_ref.shape[1]
    plane = hid_ref.shape[0] // side
    nf = plane // side
    for i in (0, 1, side + 2, side + 3):
        dst_ref[i] = jnp.zeros(dst_ref.shape[1:], BF)
    for i in range(side):
        at = slice(i * plane, (i + 1) * plane)
        h = hid_ref[at, :].astype(F32)
        taps_ref[i, 0:hc] = (pltpu.roll(h, 1, 0) * before_ref[0:plane, :]).T.astype(BF)
        taps_ref[i, hc : 2 * hc] = h.T.astype(BF)
        taps_ref[i, 2 * hc : 3 * hc] = (pltpu.roll(h, plane - 1, 0) * after_ref[0:plane, :]).T.astype(BF)
        dst_ref[i + 2] = ds_ref[at, :].astype(F32).T.astype(BF)
    tg_ref[0 : 3 * hc, :] = sum(
        nn(taps_ref[i], dt_ref[i * plane : (i + 1) * plane, :]) for i in range(side)
    )
    tg_ref[3 * hc :, :] = jnp.zeros((tg_ref.shape[0] - 3 * hc, ch), F32)
    nz, _, width = sg_ref.shape
    size = 3 * hc // (2 * nz)
    vec_ref[...] = jnp.zeros(vec_ref.shape, F32)
    vec_ref[size : size + 2, 0:hc] = mid_ref[...]
    vec_ref[size + 2 : size + 4, 0:128] = out_ref[...]
    tall = vec_ref.shape[0]
    inside = lax.broadcasted_iota(jnp.int32, (tall, ch), 0) < size
    off = (width // 2) % 128
    for z in range(nz):
        first, second = [
            jnp.where(inside, tg_ref[b * size : b * size + tall, :], vec_ref[...])
            for b in (2 * z, 2 * z + 1)
        ]
        start = width // 2 - off
        sg_ref[z, hc : hc + tall, 0:ch] = first.astype(BF)
        second = pltpu.roll(jnp.concatenate([second, jnp.zeros((tall, 128), F32)], axis=1), off, 1)
        sg_ref[z, hc : hc + tall, start : start + ch + 128] = second.astype(BF)
    for c in range(3):
        acc = sum(
            nn(dst_ref[i : i + 3].reshape(3 * hc, plane), pad_ref[i, c * nf : c * nf + plane, :])
            for i in range(1, side + 1)
        )
        for r in range(3):
            first = (3 * r + c) * ch
            end = first + ch
            at = (2 - r) * hc
            done = 0
            while first < end:
                z = first // width
                last = min(end, (z + 1) * width)
                sg_ref[z, 0:hc, first - z * width : last - z * width] = (
                    acc[at : at + hc, done : done + last - first].astype(BF)
                )
                done += last - first
                first = last


def kernel_grads(pad, hidden, ds, dt, before, after, mid, out, side, shape, deps=()):
    pixels, hc = hidden.shape
    ch = dt.shape[1]
    plane = pixels // side
    outs = [jax.ShapeDtypeStruct(shape, BF)]
    tall = shape[1] - hc
    scratch = [
        pltpu.VMEM((side + 4, hc, plane), BF),
        pltpu.VMEM((side, 3 * hc, plane), BF),
        pltpu.VMEM((3 * hc + tall, ch), F32),
        pltpu.VMEM((tall, ch), F32),
    ]
    flops = 2 * pixels * hc * 12 * ch
    return call(functools.partial(grads_body, side), outs, scratch, flops,
                pad, hidden, ds, dt, before, after, mid, out, deps=deps)[0]


def copy_after_body(v_ref, out_ref):
    out_ref[...] = v_ref[...]


def after_all(v, *deps):
    return call(copy_after_body, [jax.ShapeDtypeStruct(v.shape, v.dtype)], [], v.size, v, deps=deps)[0]


def pack_kernels_body(kt_ref, lt_ref, vec_ref, out_ref, low_ref):
    ranks, _, width = out_ref.shape
    hc = kt_ref.shape[0] // ranks
    blocks = lt_ref.shape[0] // hc
    q = hc // ranks
    low_ref[...] = jnp.zeros(low_ref.shape, F32)
    for r in range(ranks):
        out_ref[r, 0:hc, :] = kt_ref[r * hc : (r + 1) * hc, :]
        for b in range(blocks):
            low_ref[r, b * q : (b + 1) * q, 0 : lt_ref.shape[1]] = (
                lt_ref[b * hc + r * q : b * hc + (r + 1) * q, :]
            )
        low_ref[r, blocks * q : blocks * q + 1, :] = vec_ref[...]
        out_ref[r, hc:, :] = low_ref[r].astype(BF)


def pack_kernels(kt, lt, vec, ranks, tall, deps):
    width = kt.shape[1]
    outs = [jax.ShapeDtypeStruct((ranks, kt.shape[0] // ranks + tall, width), BF)]
    scratch = [pltpu.VMEM((ranks, tall, width), F32)]
    return call(pack_kernels_body, outs, scratch, kt.size * 8, kt, lt, vec, deps=deps)[0]


def call(body, outs, scratch, flops, *args, deps=(), far=(), far_outs=()):
    moved = sum(a.size * a.dtype.itemsize for a in args) + sum(
        o.size * o.dtype.itemsize for o in outs
    )
    n = len(deps)

    def spec(a):
        return pl.BlockSpec(memory_space=pltpu.SMEM if a.dtype == jnp.int32 else pltpu.VMEM)

    return pl.pallas_call(
        lambda *refs: body(*refs[n:]),
        out_shape=outs,
        in_specs=[ANY] * n + [ANY if i in far else spec(a) for i, a in enumerate(args)],
        out_specs=[ANY if i in far_outs else spec(o) for i, o in enumerate(outs)],
        scratch_shapes=scratch,
        compiler_params=pltpu.CompilerParams(vmem_limit_bytes=VMEM_CAP),
        cost_estimate=pl.CostEstimate(flops=flops, bytes_accessed=moved, transcendentals=0),
    )(*deps, *args)


def chunk(i, size):
    return pl.ds(pl.multiple_of(i * size, 16), size)


def clear_borders(pad_ref, side, plane, nf):
    zrow = jnp.zeros(pad_ref.shape[1:], BF)
    pad_ref[0] = zrow
    pad_ref[side + 1] = zrow
    zcol = jnp.zeros((nf, pad_ref.shape[2]), BF)
    for i in range(side):
        pad_ref[i + 1, 0:nf] = zcol
        pad_ref[i + 1, nf + plane : 2 * nf + plane] = zcol


def by_rank(slices, rank):
    odd = lax.rem(rank, 2) == 1
    for p in range(len(slices) // 2):
        a, b = slices[2 * p], slices[2 * p + 1]
        yield lax.bitwise_xor(rank // 2, p), odd, a, b


def halves(odd, own, mate):
    low = lax.broadcasted_iota(jnp.int32, own.shape, 1) < 64
    own, mate = own.astype(F32), mate.astype(F32)
    a, b = jnp.where(odd, mate, own), jnp.where(odd, own, mate)
    top = jnp.where(low, a, pltpu.roll(b, 64, 1))
    bottom = jnp.where(low, pltpu.roll(a, 64, 1), b)
    return top, bottom


def store_packed(rank, mate_ref, keep_ref, part, k, step, low):
    rows_now = chunk(k, step)
    odd = lax.rem(rank, 2) == 1
    for q in range(keep_ref.shape[0]):
        x = part[:step, 128 * q : 128 * q + 128]
        y = part[step:, 128 * q : 128 * q + 128]
        even_slice = jnp.where(low, x, pltpu.roll(y, 64, 1))
        odd_slice = jnp.where(low, pltpu.roll(x, 64, 1), y)
        p = lax.bitwise_xor(rank // 2, q)
        keep_ref[p, rows_now, :] = jnp.where(odd, odd_slice, even_slice).astype(BF)
        mate_ref[p, rows_now, :] = jnp.where(odd, even_slice, odd_slice).astype(BF)


def fetch_kernels(w_ref, ktm_ref, lw_ref, sems):
    nz, _, width = w_ref.shape
    hc = ktm_ref.shape[0]
    copies = []
    for z in range(nz):
        copies.append(pltpu.make_async_copy(
            w_ref.at[z, pl.ds(0, hc)], ktm_ref.at[:, pl.ds(z * width, width)], sems.at[2 * z]))
        copies.append(pltpu.make_async_copy(
            w_ref.at[z, pl.ds(hc, lw_ref.shape[1])], lw_ref.at[z], sems.at[2 * z + 1]))
    for copy in copies:
        copy.start()
    return copies


def join_temporal(lw_ref, lf_ref, ltm_ref):
    ch = ltm_ref.shape[1]
    width = lw_ref.shape[2] // 2
    count = 2 * lw_ref.shape[0]
    size = ltm_ref.shape[0] // count
    for z in range(lw_ref.shape[0]):
        first = lw_ref[z, :, 0:ch].astype(F32)
        off = width % 128
        second = lw_ref[z, :, width - off : width - off + ch + 128].astype(F32)
        second = pltpu.roll(second, ch + 128 - off, 1)[:, 0:ch]
        for b, block in ((2 * z, first), (2 * z + 1, second)):
            lf_ref[b * size : b * size + block.shape[0], :] = block
    ltm_ref[...] = lf_ref[0 : ltm_ref.shape[0], :].astype(BF)


def chunk_copies(k, step, sems, *pairs):
    rows = chunk(k, step)
    return [
        pltpu.make_async_copy(here.at[:, rows], there.at[:, rows], sems.at[i, k])
        for i, (here, there) in enumerate(pairs)
    ]


def prepare_body(w_ref, kn_out, l_out, lt_out, rows_out, ktm_ref, lw_ref, lf_ref, sems):
    hc, ch = ktm_ref.shape[0], l_out.shape[1]
    for copy in fetch_kernels(w_ref, ktm_ref, lw_ref, sems):
        copy.wait()
    for t in range(9):
        kn_out[t] = ktm_ref[:, t * ch : (t + 1) * ch].astype(F32).T.astype(BF)
    join_temporal(lw_ref, lf_ref, l_out)
    rows_out[...] = lw_ref[:, lw_ref.shape[1] - rows_out.shape[1] :, :]
    for t in range(3):
        lt_out[t] = lf_ref[t * hc : (t + 1) * hc].T.astype(BF)


def prepare(w, hc, ch, deps=()):
    outs = [
        jax.ShapeDtypeStruct((9, ch, hc), BF),
        jax.ShapeDtypeStruct((3 * hc, ch), BF),
        jax.ShapeDtypeStruct((3, ch, hc), BF),
        jax.ShapeDtypeStruct((w.shape[0], 16, w.shape[2]), BF),
    ]
    tall = w.shape[1] - hc
    scratch = [
        pltpu.VMEM((hc, 9 * ch), BF),
        pltpu.VMEM((w.shape[0], tall, w.shape[2]), BF),
        pltpu.VMEM((3 * hc + tall, ch), F32),
        pltpu.SemaphoreType.DMA((2 * w.shape[0],)),
    ]
    return call(prepare_body, outs, scratch, 2 * w.size * 512, w, deps=deps, far=(0,))


def conv_body(side, first, rank_ref, *refs):
    n = 1 if first else 8
    slices = refs[:n]
    (kn_in, ltm_ref, vec_ref, before_ref, after_ref,
     pad_out, hid_out, xhat_out, rs_ref, mate_out, keep_out,
     pad_ref, hid_ref, xhat_ref, mate_ref, keep_ref, sp_ref, kn_ref, sems, leave) = refs[n:]
    rank = rank_ref[0]
    kn_copy = pltpu.make_async_copy(kn_in, kn_ref, sems.at[0])
    kn_copy.start()
    ch, hc = pad_ref.shape[2], hid_ref.shape[1]
    rows = hid_ref.shape[0]
    plane = rows // side
    nf = plane // side
    step = plane // 2
    clear_borders(pad_ref, side, plane, nf)
    if first:
        for i in range(side):
            pad_ref[i + 1, nf : nf + plane] = slices[0][i * plane : (i + 1) * plane]
    else:
        def place(k, carry):
            for q, odd, a_ref, b_ref in by_rank(slices, rank):
                top, bottom = halves(odd, a_ref[chunk(k, step), :], b_ref[chunk(k, step), :])
                lanes = pl.ds(pl.multiple_of(128 * q, 128), 128)
                for piece, kk in ((top, k), (bottom, k + side)):
                    at = nf + lax.rem(kk, 2) * step
                    pad_ref[1 + kk // 2, pl.ds(pl.multiple_of(at, 16), step), lanes] = piece.astype(BF)
            return carry

        lax.fori_loop(0, side, place, 0, unroll=True)
    pad_copy = pltpu.make_async_copy(pad_ref, pad_out, sems.at[1])
    pad_copy.start()
    kn_copy.wait()

    def conv(i, total):
        acc = jnp.zeros((plane, hc), F32)
        for t in range(9):
            r, c = t // 3, t % 3
            acc += nn(pad_ref[i + r, c * nf : c * nf + plane, :], kn_ref[t])
        sp_ref[i] = acc
        return total + jnp.sum(acc, axis=0, keepdims=True)

    mean = lax.fori_loop(0, side, conv, jnp.zeros((1, hc), F32), unroll=True) / rows

    def square(i, total):
        cen = sp_ref[i] - mean
        return total + jnp.sum(cen * cen, axis=0, keepdims=True)

    var = lax.fori_loop(0, side, square, jnp.zeros((1, hc), F32), unroll=True) / rows
    rs = lax.rsqrt(var + eps)
    rs_ref[...] = rs
    gain, bias = vec_ref[0:1, :], vec_ref[1:2, :]

    def act(i, carry):
        xhat = (sp_ref[i] - mean) * rs
        xhat_ref[i] = xhat
        v = xhat * gain + bias
        v = v * jax.nn.sigmoid(v)
        sp_ref[i] = v
        hid_ref[chunk(i, plane), :] = v.astype(BF)
        return carry

    lax.fori_loop(0, side, act, 0, unroll=True)
    late = [
        pltpu.make_async_copy(hid_ref, hid_out, sems.at[2]),
        pltpu.make_async_copy(xhat_ref, xhat_out, sems.at[3]),
    ]
    for copy in late:
        copy.start()
    low = lax.broadcasted_iota(jnp.int32, (step, 128), 1) < 64

    def temporal(k, carry):
        pieces = []
        for kk in (k, k + side):
            par = lax.rem(kk, 2)
            h = sp_ref[kk // 2, pl.ds(pl.multiple_of(par * step, 8), step), :]
            at = pl.multiple_of(par * (step % nf), 8)
            pieces.append((
                (pltpu.roll(h, 1, 0) * before_ref[pl.ds(at, step), :]).astype(BF),
                h.astype(BF),
                (pltpu.roll(h, step - 1, 0) * after_ref[pl.ds(at, step), :]).astype(BF),
            ))
        part = sum(
            nn(jnp.concatenate([x, y], axis=0), ltm_ref[t * hc : (t + 1) * hc])
            for t, (x, y) in enumerate(zip(*pieces))
        )
        store_packed(rank, mate_ref, keep_ref, part, k, step, low)
        for copy in chunk_copies(k, step, leave, (mate_ref, mate_out), (keep_ref, keep_out)):
            copy.start()
        return carry

    lax.fori_loop(0, side, temporal, 0, unroll=True)
    for k in range(side):
        late += chunk_copies(k, step, leave, (mate_ref, mate_out), (keep_ref, keep_out))
    for copy in [pad_copy] + late:
        copy.wait()


def conv_forward(rank, g, kn, lt, vec, before, after, side, pixels, ch, deps=()):
    hc = vec.shape[1]
    plane = pixels // side
    nf = plane // side
    n = len(g)
    shapes = [
        ((side + 2, plane + 2 * nf, ch), BF),
        ((pixels, hc), BF),
        ((side, plane, hc), F32),
        ((4, pixels // 2, 128), BF),
        ((4, pixels // 2, 128), BF),
    ]
    outs = [jax.ShapeDtypeStruct(*s) for s in shapes]
    outs.insert(3, jax.ShapeDtypeStruct((1, hc), F32))
    scratch = [pltpu.VMEM(*s) for s in shapes] + [
        pltpu.VMEM((side, plane, hc), F32),
        pltpu.VMEM((9, ch, hc), BF),
        pltpu.SemaphoreType.DMA((4,)),
        pltpu.SemaphoreType.DMA((2, side)),
    ]
    flops = 2 * pixels * hc * 12 * ch
    return call(functools.partial(conv_body, side, n == 1), outs, scratch, flops,
                rank, *g, kn, lt, vec, before, after,
                deps=deps, far=(n + 1,), far_outs=(0, 1, 2, 4, 5))


def fold(v):
    return v + pltpu.roll(v, 64, 1)


def total_of(refs):
    t = refs[0][...].astype(F32)
    for ref in refs[1:]:
        t += ref[...].astype(F32)
    return t


def pair_sum_body(keep_ref, mate_ref, *out_refs):
    for p, ref in enumerate(out_refs):
        ref[...] = (keep_ref[p].astype(F32) + mate_ref[p].astype(F32)).astype(ref.dtype)


def pair_sum(keep, arrived, deps=()):
    shape = keep.shape[1:]
    outs = [jax.ShapeDtypeStruct(shape, BF)] * keep.shape[0]
    return call(pair_sum_body, outs, [], keep.size, keep, arrived, deps=deps)


def out_norm_body(n, has_skip, *refs):
    parts, refs = refs[:n], refs[n:]
    if has_skip:
        vec_ref, skip_ref, xhat_ref, rs_ref, pre_ref, res_ref = refs
    else:
        vec_ref, xhat_ref, rs_ref, pre_ref, res_ref = refs
    t = total_of(parts)
    pixels = 2 * t.shape[0]
    mean = fold(jnp.sum(t, axis=0, keepdims=True)) / pixels
    cen = t - mean
    rs = lax.rsqrt(fold(jnp.sum(cen * cen, axis=0, keepdims=True)) / pixels + eps)
    xhat = cen * rs
    pre = xhat * vec_ref[0:1, :] + vec_ref[1:2, :]
    if has_skip:
        pre = pre + skip_ref[...].astype(F32)
    xhat_ref[...] = xhat
    rs_ref[...] = rs
    pre_ref[...] = pre
    res_ref[...] = (pre * jax.nn.sigmoid(pre)).astype(BF)


def out_norm(parts, vec, skip, deps=()):
    half = parts[0].shape[0]
    outs = [
        jax.ShapeDtypeStruct((half, 128), F32),
        jax.ShapeDtypeStruct((1, 128), F32),
        jax.ShapeDtypeStruct((half, 128), F32),
        jax.ShapeDtypeStruct((half, 128), BF),
    ]
    args = (*parts, vec) + (() if skip is None else (skip,))
    body = functools.partial(out_norm_body, len(parts), skip is not None)
    return call(body, outs, [], half * 128 * 10, *args, deps=deps)


def out_back_body(n, *refs):
    parts, (pre_ref, xhat_ref, rs_ref, vec_ref, dpre_ref, dt_ref, sums_ref) = refs[:n], refs[n:]
    g = total_of(parts)
    pre, xhat = pre_ref[...], xhat_ref[...]
    sig = jax.nn.sigmoid(pre)
    dpre = g * (sig * (1.0 + pre * (1.0 - sig)))
    pixels = 2 * pre.shape[0]
    sb = fold(jnp.sum(dpre, axis=0, keepdims=True))
    sg = fold(jnp.sum(dpre * xhat, axis=0, keepdims=True))
    dpre_ref[...] = dpre.astype(BF)
    scale = vec_ref[0:1, :] * rs_ref[...]
    dt_ref[...] = (scale * (dpre - sb / pixels - xhat * (sg / pixels))).astype(BF)
    sums_ref[0:1, :] = sg
    sums_ref[1:2, :] = sb


def out_back(parts, pre, xhat, rs, vec, deps=()):
    half = pre.shape[0]
    outs = [
        jax.ShapeDtypeStruct((half, 128), BF),
        jax.ShapeDtypeStruct((half, 128), BF),
        jax.ShapeDtypeStruct((2, 128), F32),
    ]
    args = (*parts, pre, xhat, rs, vec)
    return call(functools.partial(out_back_body, len(parts)), outs, [], half * 1280, *args, deps=deps)


def conv_back_body(side, rank_ref, *refs):
    slices, (xhat_in, rs_ref, w_ref, lnt_ref, vec_ref, before_ref, after_ref,
             dt_out, ds_out, sums_ref, mate_out, keep_out,
             dt_ref, ds_ref, mate_ref, keep_ref, xhat_ref, dy_ref, pad_ref, ktm_ref, sems,
             leave) = refs[:8], refs[8:]
    half = slices[0].shape[0]
    rank = rank_ref[0]
    nz, _, width = w_ref.shape
    rows = 2 * half
    plane = rows // side
    nf = plane // side
    step = plane // 2
    hc = ds_ref.shape[1]
    ch = dt_ref.shape[1]
    fetched = [
        pltpu.make_async_copy(
            w_ref.at[z, pl.ds(0, hc)], ktm_ref.at[:, pl.ds(z * width, width)], sems.at[z])
        for z in range(nz)
    ]
    xhat_copy = pltpu.make_async_copy(xhat_in, xhat_ref, sems.at[nz])
    for copy in fetched + [xhat_copy]:
        copy.start()
    clear_borders(pad_ref, side, plane, nf)

    def place(k, carry):
        for q, odd, a_ref, b_ref in by_rank(slices, rank):
            top, bottom = halves(odd, a_ref[chunk(k, step), :], b_ref[chunk(k, step), :])
            lanes = pl.ds(pl.multiple_of(128 * q, 128), 128)
            dt_ref[chunk(k, step), lanes] = top.astype(BF)
            dt_ref[pl.ds(pl.multiple_of(half + k * step, 16), step), lanes] = bottom.astype(BF)
        return carry

    lax.fori_loop(0, side, place, 0, unroll=True)
    dt_copy = pltpu.make_async_copy(dt_ref, dt_out, sems.at[nz + 1])
    dt_copy.start()
    xhat_copy.wait()
    gain, bias = vec_ref[0:1, :], vec_ref[1:2, :]

    def hidden_grad(i, sums):
        dt = dt_ref[chunk(i, plane), :]
        early = nn(dt, lnt_ref[0]) * before_ref[0:plane, :]
        late = nn(dt, lnt_ref[2]) * after_ref[0:plane, :]
        dh = nn(dt, lnt_ref[1]) + pltpu.roll(early, plane - 1, 0) + pltpu.roll(late, 1, 0)
        xhat = xhat_ref[i]
        v = xhat * gain + bias
        sig = jax.nn.sigmoid(v)
        dy = dh * (sig * (1.0 + v * (1.0 - sig)))
        dy_ref[i] = dy
        return (
            sums[0] + jnp.sum(dy * xhat, axis=0, keepdims=True),
            sums[1] + jnp.sum(dy, axis=0, keepdims=True),
        )

    zero = jnp.zeros((1, hc), F32)
    sg, sb = lax.fori_loop(0, side, hidden_grad, (zero, zero), unroll=True)
    sums_ref[0:1, :] = sg
    sums_ref[1:2, :] = sb
    scale = gain * rs_ref[...]

    def spatial_grad(i, carry):
        ds = (scale * (dy_ref[i] - sb / rows - xhat_ref[i] * (sg / rows))).astype(BF)
        pad_ref[i + 1, nf : nf + plane] = ds
        ds_ref[chunk(i, plane), :] = ds
        return carry

    lax.fori_loop(0, side, spatial_grad, 0, unroll=True)
    ds_copy = pltpu.make_async_copy(ds_ref, ds_out, sems.at[nz + 2])
    ds_copy.start()
    for copy in fetched:
        copy.wait()
    low = lax.broadcasted_iota(jnp.int32, (step, 128), 1) < 64

    def back(k, carry):
        acc = jnp.zeros((2 * step, ch), F32)
        for t in range(9):
            r, c = 2 - t // 3, 2 - t % 3
            pieces = []
            for kk in (k, k + side):
                at = c * nf + lax.rem(kk, 2) * step
                pieces.append(pad_ref[kk // 2 + r, pl.ds(pl.multiple_of(at, 16), step), :])
            acc += nn(jnp.concatenate(pieces, axis=0), ktm_ref[:, t * ch : (t + 1) * ch])
        store_packed(rank, mate_ref, keep_ref, acc, k, step, low)
        for copy in chunk_copies(k, step, leave, (mate_ref, mate_out), (keep_ref, keep_out)):
            copy.start()
        return carry

    lax.fori_loop(0, side, back, 0, unroll=True)
    late = [dt_copy, ds_copy]
    for k in range(side):
        late += chunk_copies(k, step, leave, (mate_ref, mate_out), (keep_ref, keep_out))
    for copy in late:
        copy.wait()


def conv_back(rank, g, xhat, rs, w, lnt, vec, before, after, side, deps=()):
    half = g[0].shape[0]
    hc = vec.shape[1]
    ch = len(g) * 64
    pixels = 2 * half
    plane = pixels // side
    nf = plane // side
    outs = [
        jax.ShapeDtypeStruct((pixels, ch), BF),
        jax.ShapeDtypeStruct((pixels, hc), BF),
        jax.ShapeDtypeStruct((2, hc), F32),
        jax.ShapeDtypeStruct((4, half, 128), BF),
        jax.ShapeDtypeStruct((4, half, 128), BF),
    ]
    scratch = [
        pltpu.VMEM((pixels, ch), BF),
        pltpu.VMEM((pixels, hc), BF),
        pltpu.VMEM((4, half, 128), BF),
        pltpu.VMEM((4, half, 128), BF),
        pltpu.VMEM((side, plane, hc), F32),
        pltpu.VMEM((side, plane, hc), F32),
        pltpu.VMEM((side + 2, plane + 2 * nf, hc), BF),
        pltpu.VMEM((hc, 9 * ch), BF),
        pltpu.SemaphoreType.DMA((w.shape[0] + 3,)),
        pltpu.SemaphoreType.DMA((2, side)),
    ]
    flops = 2 * pixels * hc * 12 * ch
    return call(functools.partial(conv_back_body, side), outs, scratch, flops,
                rank, *g, xhat, rs, w, lnt, vec, before, after,
                deps=deps, far=(9, 11), far_outs=(0, 1, 3, 4))


def grads_body(side, pad_ref, hid_ref, ds_ref, dt_ref, before_ref, after_ref, mid_ref, out_ref,
               sg_ref, dst_ref, taps_ref, tg_ref, vec_ref):
    ch = pad_ref.shape[2]
    hc = hid_ref.shape[1]
    plane = hid_ref.shape[0] // side
    nf = plane // side
    for i in (0, 1, side + 2, side + 3):
        dst_ref[i] = jnp.zeros(dst_ref.shape[1:], BF)
    for i in range(side):
        at = slice(i * plane, (i + 1) * plane)
        h = hid_ref[at, :].astype(F32)
        taps_ref[i, 0:hc] = (pltpu.roll(h, 1, 0) * before_ref[0:plane, :]).T.astype(BF)
        taps_ref[i, hc : 2 * hc] = h.T.astype(BF)
        taps_ref[i, 2 * hc : 3 * hc] = (pltpu.roll(h, plane - 1, 0) * after_ref[0:plane, :]).T.astype(BF)
        dst_ref[i + 2] = ds_ref[at, :].astype(F32).T.astype(BF)
    tg_ref[0 : 3 * hc, :] = sum(
        nn(taps_ref[i], dt_ref[i * plane : (i + 1) * plane, :]) for i in range(side)
    )
    tg_ref[3 * hc :, :] = jnp.zeros((tg_ref.shape[0] - 3 * hc, ch), F32)
    nz, _, width = sg_ref.shape
    size = 3 * hc // (2 * nz)
    vec_ref[...] = jnp.zeros(vec_ref.shape, F32)
    vec_ref[size : size + 2, 0:hc] = mid_ref[...]
    vec_ref[size + 2 : size + 4, 0:128] = out_ref[...]
    tall = vec_ref.shape[0]
    inside = lax.broadcasted_iota(jnp.int32, (tall, ch), 0) < size
    off = (width // 2) % 128
    for z in range(nz):
        first, second = [
            jnp.where(inside, tg_ref[b * size : b * size + tall, :], vec_ref[...])
            for b in (2 * z, 2 * z + 1)
        ]
        start = width // 2 - off
        sg_ref[z, hc : hc + tall, 0:ch] = first.astype(BF)
        second = pltpu.roll(jnp.concatenate([second, jnp.zeros((tall, 128), F32)], axis=1), off, 1)
        sg_ref[z, hc : hc + tall, start : start + ch + 128] = second.astype(BF)
    for c in range(3):
        acc = sum(
            nn(dst_ref[i : i + 3].reshape(3 * hc, plane), pad_ref[i, c * nf : c * nf + plane, :])
            for i in range(1, side + 1)
        )
        for r in range(3):
            first = (3 * r + c) * ch
            end = first + ch
            at = (2 - r) * hc
            done = 0
            while first < end:
                z = first // width
                last = min(end, (z + 1) * width)
                sg_ref[z, 0:hc, first - z * width : last - z * width] = (
                    acc[at : at + hc, done : done + last - first].astype(BF)
                )
                done += last - first
                first = last


def kernel_grads(pad, hidden, ds, dt, before, after, mid, out, side, shape, deps=()):
    pixels, hc = hidden.shape
    ch = dt.shape[1]
    plane = pixels // side
    outs = [jax.ShapeDtypeStruct(shape, BF)]
    tall = shape[1] - hc
    scratch = [
        pltpu.VMEM((side + 4, hc, plane), BF),
        pltpu.VMEM((side, 3 * hc, plane), BF),
        pltpu.VMEM((3 * hc + tall, ch), F32),
        pltpu.VMEM((tall, ch), F32),
    ]
    flops = 2 * pixels * hc * 12 * ch
    return call(functools.partial(grads_body, side), outs, scratch, flops,
                pad, hidden, ds, dt, before, after, mid, out, deps=deps)[0]


def copy_after_body(v_ref, out_ref):
    out_ref[...] = v_ref[...]


def after_all(v, *deps):
    return call(copy_after_body, [jax.ShapeDtypeStruct(v.shape, v.dtype)], [], v.size, v, deps=deps)[0]


def pack_kernels_body(kt_ref, lt_ref, vec_ref, out_ref, low_ref):
    ranks, _, width = out_ref.shape
    hc = kt_ref.shape[0] // ranks
    blocks = lt_ref.shape[0] // hc
    q = hc // ranks
    low_ref[...] = jnp.zeros(low_ref.shape, F32)
    for r in range(ranks):
        out_ref[r, 0:hc, :] = kt_ref[r * hc : (r + 1) * hc, :]
        for b in range(blocks):
            low_ref[r, b * q : (b + 1) * q, 0 : lt_ref.shape[1]] = (
                lt_ref[b * hc + r * q : b * hc + (r + 1) * q, :]
            )
        low_ref[r, blocks * q : blocks * q + 1, :] = vec_ref[...]
        out_ref[r, hc:, :] = low_ref[r].astype(BF)


def pack_kernels(kt, lt, vec, ranks, tall, deps):
    width = kt.shape[1]
    outs = [jax.ShapeDtypeStruct((ranks, kt.shape[0] // ranks + tall, width), BF)]
    scratch = [pltpu.VMEM((ranks, tall, width), F32)]
    return call(pack_kernels_body, outs, scratch, kt.size * 8, kt, lt, vec, deps=deps)[0]


def hop(v, k):
    n = 1
    for name in EVERY:
        n *= lax.axis_size(name)
    return lax.ppermute(v, EVERY, [(i, i ^ k) for i in range(n)])


def plane_gather(v, aside=()):
    got = {0: v}
    for k in (6, 2, 4):
        got[k] = hop(v, k)
    got[1] = hop(after_all(v, *aside) if aside else v, 1)
    for k in (2, 4, 6):
        got[k ^ 1] = hop(got[k], 1)
    return [got[k] for k in range(8)]


def plane_reduce(mate, keep, deps=()):
    sums = pair_sum(keep, hop(mate, 1), deps)
    arrived = {k: hop(sums[k // 2], k) for k in (6, 2, 4)}
    return [sums[0], arrived[2], arrived[4], arrived[6]]


def on_device(frames, cot, starts, ks, ktm, mg, mb, og, ob):
    nz, n_rank, n_seg = lax.axis_size("z"), 8, 4
    n_dp = nz * 2
    fr, side, ch = frames.shape[0], frames.shape[1], frames.shape[3]
    area = side * side
    hid = ks.shape[2]
    hc, cc = hid // n_rank, ch // n_rank
    q = hc // n_rank
    rank = lax.axis_index(PLANE)
    rank_now = rank.astype(jnp.int32).reshape(1)
    d_index = lax.axis_index(("z", "y"))
    nf = n_dp * fr
    pixels = area * nf
    half = pixels // 2

    to_plane = [(d * n_seg + s, s * n_rank + d) for d in range(n_dp) for s in range(n_seg)]
    from_plane = [(b, a) for a, b in to_plane]
    rows = fr * area
    flag_row = jnp.pad(starts.astype(BF)[None], ((0, 11), (0, ch - fr)))
    moving = jnp.concatenate([frames.reshape(rows, ch), flag_row], axis=0)
    moving = lax.ppermute(moving, EVERY, to_plane)

    perm = (jnp.arange(hid).reshape(n_rank, n_rank, q).transpose(1, 0, 2).reshape(hid)[:, None]
            == jnp.arange(hid)[None, :]).astype(BF)
    kt = lax.dot_general(perm, ks[0].astype(BF), (((1,), (1,)), ((), ())),
                         preferred_element_type=F32).astype(BF)
    lrows, width = ktm.shape[1] // n_rank, ks.shape[1]
    tall = -(-(lrows + 4) // 16) * 16
    extra = jnp.concatenate([mg, mb, og, ob], axis=1)
    extra = jnp.pad(extra, ((0, 0), (0, width - extra.shape[1])))
    w = pack_kernels(kt, ktm[0], extra, n_rank, tall, deps=(moving,))
    w = lax.all_to_all(w, PLANE, 0, 0)
    here = w
    high = hc + tall

    w = w.reshape(2, n_seg, high, width).transpose(1, 2, 0, 3).reshape(n_seg, high, 2 * width)
    ws = [lax.all_gather(w[s], "z", axis=0) for s in range(n_seg)]

    moving = after_all(moving, here)
    gathered = lax.all_to_all(jnp.broadcast_to(moving, (n_rank, *moving.shape)), PLANE, 0, 0)

    def norm_rows(rows_now):
        row = rows_now[:, (lrows - tall) % 16].reshape(n_dp, width).astype(F32)
        mid = jnp.stack([
            lax.dynamic_slice_in_dim(row[:, i * hc : (i + 1) * hc], rank * q, q, axis=1).reshape(hc)
            for i in range(2)])
        own = lax.dynamic_index_in_dim(row, rank, 0, keepdims=False)
        out = jnp.stack([
            jnp.tile(own[2 * hc + i * cc : 2 * hc + (i + 1) * cc], 2) for i in range(2)])
        return mid, out

    moving = after_all(moving, here)
    gathered = lax.all_to_all(jnp.broadcast_to(moving, (n_rank, *moving.shape)), PLANE, 0, 0)
    mids, outs = [], []
    for s in range(n_seg):
        row = ws[s][:, hc + lrows].reshape(n_dp, width).astype(F32)
        mids.append(jnp.stack([
            lax.dynamic_slice_in_dim(row[:, i * hc : (i + 1) * hc], rank * q, q, axis=1).reshape(hc)
            for i in range(2)]))
        own = lax.dynamic_index_in_dim(row, rank, 0, keepdims=False)
        outs.append(jnp.stack([
            jnp.tile(own[2 * hc + i * cc : 2 * hc + (i + 1) * cc], 2) for i in range(2)]))

    def by_pixel(v):
        width = v.shape[2]
        v = v.reshape(n_rank * fr, area, width).transpose(1, 0, 2)
        return v.reshape(pixels, width)

    def packed(v):
        return jnp.concatenate([v[:half], v[half:]], axis=1)

    a0 = by_pixel(gathered[:, :rows])
    flags = gathered[:, rows, :fr].reshape(nf) > 0.5
    slot = jnp.arange(nf) % fr
    before = jnp.where(flags | (slot == 0), 0.0, 1.0)
    after = jnp.where(jnp.roll(flags, -1) | (slot == fr - 1), 0.0, 1.0)
    spread = (side * nf + nf, hc)
    before = jnp.broadcast_to(jnp.tile(before, side + 1)[:, None], spread)
    after = jnp.broadcast_to(jnp.tile(after, side + 1)[:, None], spread)
    skip = packed(lax.dynamic_slice_in_dim(a0, rank * cc, cc, axis=1))

    def by_frames(v):
        v = jnp.concatenate([v[:, :cc], v[:, cc:]], axis=0)
        return v.reshape(area, n_rank, fr, cc).transpose(1, 0, 2, 3).reshape(n_rank, rows, cc)

    def home(v):
        v = v.transpose(1, 0, 2).reshape(rows, ch)
        return lax.ppermute(v, EVERY, from_plane)

    def as_frames(v):
        return v.reshape(area, fr, ch).transpose(1, 0, 2).reshape(frames.shape)

    saved = []
    g = [a0]
    ready = prepare(ws[0], hc, ch)
    for s in range(n_seg):
        kn, lt, lnt, rows_now = ready
        mid, out = norm_rows(rows_now)
        pad, hidden, xm, rm, mate, keep = conv_forward(
            rank_now, g, kn, lt, mid, before, after, side, pixels, ch)
        parts = plane_reduce(mate, keep)
        deps = ()
        if s == n_seg - 2:
            cot_moving = after_all(cot.reshape(rows, ch), mate)
            deps = (cot_moving,)
            cot_moving = lax.ppermute(cot_moving, EVERY, to_plane)
            cot_moving = cot_moving.reshape(rows, n_rank, cc).transpose(1, 0, 2)
        if s == n_seg - 1:
            cot_own = lax.all_to_all(after_all(cot_moving, parts[0]), PLANE, 0, 0)
            deps = (cot_own,)
        xo, ro, pre, res = out_norm(parts, out, skip if s % 2 == 1 else None, deps=deps)
        saved.append((pad, hidden, xm, rm, xo, ro, pre, lnt, mid, out))
        if s % 2 == 1:
            skip = res
        if s < n_seg - 1:
            ready = prepare(ws[s + 1], hc, ch, deps=(res,))
            g = plane_gather(res, ready[:1])
    cot_own = packed(by_pixel(cot_own))

    parts = [cot_own]
    skip_grad = None

    grads, raw = [], None
    for s in reversed(range(n_seg)):
        pad, hidden, xm, rm, xo, ro, pre, lnt, mid, out = saved[s]
        if s == 1:
            parts = parts + [skip_grad]
        deps = () if raw is None else (raw, *grads[len(grads) - 1 :])
        dpre, dt, osum = out_back(parts, pre, xo, ro, out, deps=deps)
        if raw is not None:
            grads.append(lax.psum_scatter(after_all(raw, dt), "z", scatter_dimension=0))
        if s % 2 == 1:
            skip_grad = dpre
        deps = ()
        if s == n_seg - 1:
            output = lax.all_to_all(after_all(by_frames(res), dt), PLANE, 0, 0)
            deps = (output,)
            output = home(output)
        dtf, ds, msum, mate, keep = conv_back(
            rank_now, plane_gather(dt), xm, rm, ws[s], lnt, mid, before, after, side, deps=deps)
        if s > 0:
            parts = plane_reduce(mate, keep)
        raw = kernel_grads(pad, hidden, ds, dtf, before, after, msum, osum, side, ws[s].shape,
                           deps=parts[:1] + ([output] if s == n_seg - 2 else []) if s > 0 else ())
    last = lax.psum_scatter(raw, "z", scatter_dimension=0)
    parts = plane_reduce(mate, keep, deps=(raw,))

    da = sum(p.astype(F32) for p in parts) + skip_grad.astype(F32)
    home_now = home(lax.all_to_all(by_frames(da.astype(BF)), PLANE, 0, 0))
    output, frames_grad = as_frames(output), as_frames(home_now).astype(F32)

    def by_row(v):
        return v.reshape(high, 2, width).transpose(1, 0, 2)

    last = after_all(last, home_now)
    g = jnp.stack([by_row(v) for v in [last] + grads[::-1]], axis=1).reshape(n_rank, high, width)
    g = lax.all_to_all(g, PLANE, 0, 0)
    space_grad = lax.dot_general(g[:, :hc].reshape(hid, width), perm, (((0,), (0,)), ((), ())),
                                 preferred_element_type=F32)
    tg = g[:, hc : hc + lrows, :ch].reshape(n_rank, -1, q, ch)
    time_grad = tg.transpose(1, 0, 2, 3).reshape(-1, ch).astype(F32)
    sums = g[:, hc + lrows : hc + lrows + 4].astype(F32)

    def mid_own(v):
        return lax.dynamic_slice_in_dim(v[:, :hc], d_index * q, q, axis=1).reshape(1, hc)

    own = lax.dynamic_index_in_dim(sums, d_index, 0, keepdims=False)
    return (
        output,
        frames_grad,
        space_grad[None],
        time_grad[None],
        mid_own(sums[:, 0]),
        mid_own(sums[:, 1]),
        own[2:3, :cc],
        own[3:4, :cc],
    )


def from_behind(value, axis, steps):
    count = lax.axis_size(axis)
    leading, last = (max(0, -steps), min(count, count - steps))
    return lax.ppermute(value, axis, [(source, source + steps) for source in range(leading, last)])


def space_apply(current, kernel):
    frame_side = current.shape[1]
    padded = jnp.pad(current, ((0, 0), (1, 1), (1, 1), (0, 0)))
    stacked = jnp.concatenate(
        [
            padded[:, row_shift : row_shift + frame_side, col_shift : col_shift + frame_side, :]
            for row_shift in range(3)
            for col_shift in range(3)
        ],
        axis=-1,
    )
    return (
        stacked,
        jnp.einsum("fijc,co->fijo", stacked, kernel, preferred_element_type=jnp.float32),
    )


def space_back(gradient, kernel):
    frame_side = gradient.shape[1]
    channels = kernel.shape[0] // 9
    spread = jnp.einsum("fijo,co->fijc", gradient, kernel, preferred_element_type=jnp.float32)
    total = jnp.zeros((gradient.shape[0], frame_side + 2, frame_side + 2, channels), jnp.float32)
    for tap_index in range(9):
        row_shift = tap_index // 3
        col_shift = tap_index % 3
        piece_now = spread[..., tap_index * channels : (tap_index + 1) * channels]
        total = total + jnp.pad(
            piece_now, ((0, 0), (row_shift, 2 - row_shift), (col_shift, 2 - col_shift), (0, 0))
        )
    return total[:, 1 : frame_side + 1, 1 : frame_side + 1, :]


def time_apply(current, kernel, before_mask, after_mask):
    blanks = jnp.zeros_like(current[:1])
    earlier = jnp.concatenate([blanks, current[:-1]], axis=0) * before_mask[
        :, None, None, None
    ].astype(current.dtype)
    later = jnp.concatenate([current[1:], blanks], axis=0) * after_mask[:, None, None, None].astype(
        current.dtype
    )
    stacked = jnp.concatenate([earlier, current, later], axis=-1)
    return (
        stacked,
        jnp.einsum("fijc,co->fijo", stacked, kernel, preferred_element_type=jnp.float32),
    )


def time_back(gradient, kernel, before_mask, after_mask):
    channels = kernel.shape[0] // 3
    spread = jnp.einsum("fijo,co->fijc", gradient, kernel, preferred_element_type=jnp.float32)
    early_part = spread[..., :channels] * before_mask[:, None, None, None]
    late_part = spread[..., 2 * channels :] * after_mask[:, None, None, None]
    blanks = jnp.zeros_like(early_part[:1])
    moved_early = jnp.concatenate([early_part[1:], blanks], axis=0)
    moved_late = jnp.concatenate([blanks, late_part[:-1]], axis=0)
    return spread[..., channels : 2 * channels] + moved_early + moved_late


def moments(values, pixel_count):
    average = lax.psum(jnp.sum(values, axis=(0, 1, 2)), "dp") / pixel_count
    centered = values - average
    spread = lax.psum(jnp.sum(centered * centered, axis=(0, 1, 2)), "dp") / pixel_count
    return (average, lax.rsqrt(spread + eps))


def reduce_back(gradient, normed):
    return lax.psum(
        (jnp.sum(gradient, axis=(0, 1, 2)), jnp.sum(gradient * normed, axis=(0, 1, 2))), "dp"
    )


def silu_slope(values):
    sigmoid_now = jax.nn.sigmoid(values)
    return sigmoid_now * (1.0 + values * (1.0 - sigmoid_now))


def pick_slot(stack, slot_index):
    return lax.dynamic_index_in_dim(stack, slot_index, 0, keepdims=False)


def store_slot(stack, value, slot_index, usable):
    previous = pick_slot(stack, slot_index)
    return lax.dynamic_update_index_in_dim(stack, jnp.where(usable, value, previous), slot_index, 0)


def on_device_general(
    frames, cotangent, starts, space_kernel, time_kernel, mid_gain, mid_bias, out_gain, out_bias
):
    n_segment = lax.axis_size("segment")
    n_data = lax.axis_size("dp")
    segment_index = lax.axis_index("segment")
    odd_segment = segment_index % 2 == 1
    last_segment = segment_index == n_segment - 1
    first_segment = segment_index == 0
    frame_count = frames.shape[0]
    frame_side = frames.shape[1]
    channels = frames.shape[3]
    hidden_units = mid_gain.shape[1] * n_data
    pixel_count = n_data * frame_count * frame_side * frame_side
    turns = 2 * n_segment - 1
    block_shape = (n_segment,) + frames.shape
    all_frames, all_cot, all_starts = (
        lax.all_gather(frames, "segment", axis=0, tiled=True),
        lax.all_gather(cotangent, "segment", axis=0, tiled=True),
        lax.all_gather(starts.astype(jnp.bfloat16), "segment", axis=0, tiled=True),
    )
    frame_stack = all_frames.reshape(block_shape)
    cot_stack = all_cot.reshape(block_shape)
    clip_flags = all_starts.astype(jnp.float32).reshape(n_segment, frame_count)
    positions = jnp.arange(frame_count)
    before_mask = jnp.where((clip_flags > 0.5) | (positions == 0), 0.0, 1.0)
    following = jnp.concatenate([clip_flags[:, 1:], jnp.ones((n_segment, 1), jnp.float32)], axis=1)
    after_mask = jnp.where(following > 0.5, 0.0, 1.0)
    gathered = (
        lax.all_gather(space_kernel[0].astype(jnp.bfloat16), "dp", axis=0, tiled=True),
        lax.all_gather(time_kernel[0].astype(jnp.bfloat16), "dp", axis=0, tiled=True),
        lax.all_gather(mid_gain[0].astype(jnp.bfloat16), "dp", axis=0, tiled=True),
        lax.all_gather(mid_bias[0].astype(jnp.bfloat16), "dp", axis=0, tiled=True),
        lax.all_gather(out_gain[0].astype(jnp.bfloat16), "dp", axis=0, tiled=True),
        lax.all_gather(out_bias[0].astype(jnp.bfloat16), "dp", axis=0, tiled=True),
    )
    space_low, time_low = (gathered[0], gathered[1])
    mid_gain_now = gathered[2].astype(jnp.float32)
    mid_bias_now = gathered[3].astype(jnp.float32)
    out_gain_now = gathered[4].astype(jnp.float32)
    out_bias_now = gathered[5].astype(jnp.float32)
    incoming = jnp.zeros_like(frames)
    carried = jnp.zeros_like(frames)
    kept_input = jnp.zeros(block_shape, jnp.bfloat16)
    kept_skip = jnp.zeros(block_shape, jnp.bfloat16)
    kept_mid_mean = jnp.zeros((n_segment, hidden_units), jnp.float32)
    kept_mid_scale = jnp.zeros((n_segment, hidden_units), jnp.float32)
    kept_out_mean = jnp.zeros((n_segment, channels), jnp.float32)
    kept_out_scale = jnp.zeros((n_segment, channels), jnp.float32)
    results = jnp.zeros(block_shape, jnp.float32)
    for turn_index in range(turns):
        micro_index = turn_index - segment_index
        usable = (micro_index >= 0) & (micro_index < n_segment)
        slot_index = jnp.clip(micro_index, 0, n_segment - 1)
        current = jnp.where(first_segment, pick_slot(frame_stack, slot_index), incoming)
        skip_input = carried
        _, spatial = space_apply(current, space_low)
        mid_mean, mid_scale = moments(spatial, pixel_count)
        hidden_act = jax.nn.silu(
            (spatial - mid_mean) * mid_scale * mid_gain_now + mid_bias_now
        ).astype(jnp.bfloat16)
        _, temporal = time_apply(
            hidden_act,
            time_low,
            pick_slot(before_mask, slot_index),
            pick_slot(after_mask, slot_index),
        )
        out_mean, out_scale = moments(temporal, pixel_count)
        pre_act = (
            (temporal - out_mean) * out_scale * out_gain_now
            + out_bias_now
            + jnp.where(odd_segment, skip_input.astype(jnp.float32), 0.0)
        )
        result = jax.nn.silu(pre_act).astype(jnp.bfloat16)
        kept_input = store_slot(kept_input, current, slot_index, usable)
        kept_skip = store_slot(kept_skip, skip_input, slot_index, usable)
        kept_mid_mean = store_slot(kept_mid_mean, mid_mean, slot_index, usable)
        kept_mid_scale = store_slot(kept_mid_scale, mid_scale, slot_index, usable)
        kept_out_mean = store_slot(kept_out_mean, out_mean, slot_index, usable)
        kept_out_scale = store_slot(kept_out_scale, out_scale, slot_index, usable)
        results = store_slot(results, result.astype(jnp.float32), slot_index, usable)
        if turn_index < turns - 1:
            incoming, carried = from_behind(
                (result, jnp.where(odd_segment, result, current)), "segment", 1
            )
    gathered = (
        lax.all_gather(space_kernel[0].astype(jnp.bfloat16), "dp", axis=0, tiled=True),
        lax.all_gather(time_kernel[0].astype(jnp.bfloat16), "dp", axis=0, tiled=True),
        lax.all_gather(mid_gain[0].astype(jnp.bfloat16), "dp", axis=0, tiled=True),
        lax.all_gather(mid_bias[0].astype(jnp.bfloat16), "dp", axis=0, tiled=True),
        lax.all_gather(out_gain[0].astype(jnp.bfloat16), "dp", axis=0, tiled=True),
        lax.all_gather(out_bias[0].astype(jnp.bfloat16), "dp", axis=0, tiled=True),
    )
    space_low, time_low = (gathered[0], gathered[1])
    mid_gain_now = gathered[2].astype(jnp.float32)
    mid_bias_now = gathered[3].astype(jnp.float32)
    out_gain_now = gathered[4].astype(jnp.float32)
    out_bias_now = gathered[5].astype(jnp.float32)
    grad_input = jnp.zeros_like(frames)
    grad_skip = jnp.zeros_like(frames)
    space_acc = jnp.zeros(space_low.shape, jnp.float32)
    time_acc = jnp.zeros(time_low.shape, jnp.float32)
    mid_gain_acc = jnp.zeros((hidden_units,), jnp.float32)
    mid_bias_acc = jnp.zeros((hidden_units,), jnp.float32)
    out_gain_acc = jnp.zeros((channels,), jnp.float32)
    out_bias_acc = jnp.zeros((channels,), jnp.float32)
    input_grads = jnp.zeros(block_shape, jnp.float32)
    for turn_index in range(turns):
        micro_index = n_segment - 1 - (turn_index - (n_segment - 1 - segment_index))
        usable = (micro_index >= 0) & (micro_index < n_segment)
        usable_weight = usable.astype(jnp.float32)
        slot_index = jnp.clip(micro_index, 0, n_segment - 1)
        current = pick_slot(kept_input, slot_index)
        skip_input = pick_slot(kept_skip, slot_index)
        before_now = pick_slot(before_mask, slot_index)
        after_now = pick_slot(after_mask, slot_index)
        space_taps, spatial = space_apply(current, space_low)
        mid_normed = (spatial - pick_slot(kept_mid_mean, slot_index)) * pick_slot(
            kept_mid_scale, slot_index
        )
        mid_pre = mid_normed * mid_gain_now + mid_bias_now
        hidden_act = jax.nn.silu(mid_pre).astype(jnp.bfloat16)
        time_taps, temporal = time_apply(hidden_act, time_low, before_now, after_now)
        out_scale = pick_slot(kept_out_scale, slot_index)
        out_normed = (temporal - pick_slot(kept_out_mean, slot_index)) * out_scale
        pre_act = (
            out_normed * out_gain_now
            + out_bias_now
            + jnp.where(odd_segment, skip_input.astype(jnp.float32), 0.0)
        )
        grad_result = jnp.where(
            last_segment,
            pick_slot(cot_stack, slot_index).astype(jnp.float32),
            grad_input.astype(jnp.float32)
            + jnp.where(odd_segment, grad_skip.astype(jnp.float32), 0.0),
        )
        grad_pre = grad_result * silu_slope(pre_act)
        out_bias_sum, out_gain_sum = reduce_back(grad_pre, out_normed)
        grad_temporal = (
            out_gain_now
            * out_scale
            * (grad_pre - out_bias_sum / pixel_count - out_normed * out_gain_sum / pixel_count)
        ).astype(jnp.bfloat16)
        time_acc = time_acc + usable_weight * jnp.einsum(
            "fijc,fijo->co", time_taps, grad_temporal, preferred_element_type=jnp.float32
        )
        grad_hidden = time_back(grad_temporal, time_low, before_now, after_now)
        grad_mid = grad_hidden * silu_slope(mid_pre)
        mid_bias_sum, mid_gain_sum = reduce_back(grad_mid, mid_normed)
        mid_scale = pick_slot(kept_mid_scale, slot_index)
        grad_spatial = (
            mid_gain_now
            * mid_scale
            * (grad_mid - mid_bias_sum / pixel_count - mid_normed * mid_gain_sum / pixel_count)
        ).astype(jnp.bfloat16)
        space_acc = space_acc + usable_weight * jnp.einsum(
            "fijc,fijo->co", space_taps, grad_spatial, preferred_element_type=jnp.float32
        )
        grad_current = space_back(grad_spatial, space_low)
        mid_gain_acc = mid_gain_acc + usable_weight * mid_gain_sum
        mid_bias_acc = mid_bias_acc + usable_weight * mid_bias_sum
        out_gain_acc = out_gain_acc + usable_weight * out_gain_sum
        out_bias_acc = out_bias_acc + usable_weight * out_bias_sum
        input_grads = store_slot(
            input_grads, grad_current + grad_skip.astype(jnp.float32), slot_index, usable
        )
        if turn_index < turns - 1:
            grad_input, grad_skip = from_behind(
                (
                    grad_current.astype(jnp.bfloat16),
                    jnp.where(odd_segment, grad_pre.astype(jnp.bfloat16), grad_skip),
                ),
                "segment",
                -1,
            )
    space_grad, time_grad = (
        lax.psum_scatter(space_acc, "dp", scatter_dimension=0, tiled=True),
        lax.psum_scatter(time_acc, "dp", scatter_dimension=0, tiled=True),
    )
    data_index = lax.axis_index("dp")

    def own_share(full_vector):
        share = full_vector.shape[0] // n_data
        return lax.dynamic_slice_in_dim(full_vector, data_index * share, share)[None]

    flat_shape = (n_segment * frame_count,) + frames.shape[1:]
    arrived_out, arrived_grads = (
        lax.all_to_all(
            results.reshape(flat_shape).astype(jnp.bfloat16),
            "segment",
            split_axis=0,
            concat_axis=0,
            tiled=True,
        ).astype(jnp.float32),
        lax.all_to_all(
            input_grads.reshape(flat_shape).astype(jnp.bfloat16),
            "segment",
            split_axis=0,
            concat_axis=0,
            tiled=True,
        ).astype(jnp.float32),
    )
    output = arrived_out[(n_segment - 1) * frame_count :].astype(jnp.bfloat16)
    frames_grad = arrived_grads[:frame_count]
    return (
        output,
        frames_grad,
        space_grad[None],
        time_grad[None],
        own_share(mid_gain_acc),
        own_share(mid_bias_acc),
        own_share(out_gain_acc),
        own_share(out_bias_acc),
    )


def general(mesh):
    return jax.shard_map(
        on_device_general,
        mesh=mesh,
        in_specs=(
            P(("dp", "segment"), None, None, None),
            P(("dp", "segment"), None, None, None),
            P(("dp", "segment")),
            P("segment", "dp", None),
            P("segment", "dp", None),
            P("segment", "dp"),
            P("segment", "dp"),
            P("segment", "dp"),
            P("segment", "dp"),
        ),
        out_specs=(
            P(("dp", "segment"), None, None, None),
            P(("dp", "segment"), None, None, None),
            P("segment", "dp", None),
            P("segment", "dp", None),
            P("segment", "dp"),
            P("segment", "dp"),
            P("segment", "dp"),
            P("segment", "dp"),
        ),
        check_vma=False,
    )


def solution(mesh):
    if mesh.shape["dp"] != 8 or mesh.shape["segment"] != 4:
        return general(mesh)
    n_dp, n_seg = mesh.shape["dp"], mesh.shape["segment"]
    fine = Mesh(mesh.devices.reshape(n_dp // 2, 2, 2, n_seg // 2), EVERY)
    dp, seg = ("z", "y"), ("x", "c")
    return jax.shard_map(
        on_device,
        mesh=fine,
        in_specs=(
            P(EVERY, None, None, None),
            P(EVERY, None, None, None),
            P(EVERY),
            P(seg, dp, None),
            P(seg, dp, None),
            P(seg, dp),
            P(seg, dp),
            P(seg, dp),
            P(seg, dp),
        ),
        out_specs=(
            P(EVERY, None, None, None),
            P(EVERY, None, None, None),
            P(seg, dp, None),
            P(seg, dp, None),
            P(seg, dp),
            P(seg, dp),
            P(seg, dp),
            P(seg, dp),
        ),
        check_vma=False,
    )
```

```python
import functools

import jax
import jax.numpy as jnp
from jax import lax
from jax.experimental import pallas as pl
from jax.experimental.pallas import tpu as pltpu
from jax.sharding import Mesh, PartitionSpec as P

eps = 1e-05
PLANE = ("y", "x", "c")
EVERY = ("z", "y", "x", "c")
BF = jnp.bfloat16
F32 = jnp.float32


def nt(a, b):
    return lax.dot_general(a, b, (((1,), (1,)), ((), ())), preferred_element_type=F32)


def nn(a, b):
    return lax.dot_general(a, b, (((1,), (0,)), ((), ())), preferred_element_type=F32)


VMEM_CAP = 56 * 1024 * 1024
ANY = pl.BlockSpec(memory_space=pl.ANY)


def call(body, outs, scratch, flops, *args, deps=(), far=(), far_outs=()):
    moved = sum(a.size * a.dtype.itemsize for a in args) + sum(
        o.size * o.dtype.itemsize for o in outs
    )
    n = len(deps)

    def spec(a):
        return pl.BlockSpec(memory_space=pltpu.SMEM if a.dtype == jnp.int32 else pltpu.VMEM)

    return pl.pallas_call(
        lambda *refs: body(*refs[n:]),
        out_shape=outs,
        in_specs=[ANY] * n + [ANY if i in far else spec(a) for i, a in enumerate(args)],
        out_specs=[ANY if i in far_outs else spec(o) for i, o in enumerate(outs)],
        scratch_shapes=scratch,
        compiler_params=pltpu.CompilerParams(vmem_limit_bytes=VMEM_CAP),
        cost_estimate=pl.CostEstimate(flops=flops, bytes_accessed=moved, transcendentals=0),
    )(*deps, *args)


def chunk(i, size):
    return pl.ds(pl.multiple_of(i * size, 16), size)


def clear_borders(pad_ref, side, plane, nf):
    zrow = jnp.zeros(pad_ref.shape[1:], BF)
    pad_ref[0] = zrow
    pad_ref[side + 1] = zrow
    zcol = jnp.zeros((nf, pad_ref.shape[2]), BF)
    for i in range(side):
        pad_ref[i + 1, 0:nf] = zcol
        pad_ref[i + 1, nf + plane : 2 * nf + plane] = zcol


def by_rank(slices, rank):
    odd = lax.rem(rank, 2) == 1
    for p in range(len(slices) // 2):
        a, b = slices[2 * p], slices[2 * p + 1]
        yield lax.bitwise_xor(rank // 2, p), odd, a, b


def halves(odd, own, mate):
    low = lax.broadcasted_iota(jnp.int32, own.shape, 1) < 64
    own, mate = own.astype(F32), mate.astype(F32)
    a, b = jnp.where(odd, mate, own), jnp.where(odd, own, mate)
    top = jnp.where(low, a, pltpu.roll(b, 64, 1))
    bottom = jnp.where(low, pltpu.roll(a, 64, 1), b)
    return top, bottom


def store_packed(rank, mate_ref, keep_ref, part, k, step, low):
    rows_now = chunk(k, step)
    odd = lax.rem(rank, 2) == 1
    for q in range(keep_ref.shape[0]):
        x = part[:step, 128 * q : 128 * q + 128]
        y = part[step:, 128 * q : 128 * q + 128]
        even_slice = jnp.where(low, x, pltpu.roll(y, 64, 1))
        odd_slice = jnp.where(low, pltpu.roll(x, 64, 1), y)
        p = lax.bitwise_xor(rank // 2, q)
        keep_ref[p, rows_now, :] = jnp.where(odd, odd_slice, even_slice).astype(BF)
        mate_ref[p, rows_now, :] = jnp.where(odd, even_slice, odd_slice).astype(BF)


def fetch_kernels(w_ref, ktm_ref, lw_ref, sems):
    nz, _, width = w_ref.shape
    hc = ktm_ref.shape[0]
    copies = []
    for z in range(nz):
        copies.append(pltpu.make_async_copy(
            w_ref.at[z, pl.ds(0, hc)], ktm_ref.at[:, pl.ds(z * width, width)], sems.at[2 * z]))
        copies.append(pltpu.make_async_copy(
            w_ref.at[z, pl.ds(hc, lw_ref.shape[1])], lw_ref.at[z], sems.at[2 * z + 1]))
    for copy in copies:
        copy.start()
    return copies


def join_temporal(lw_ref, lf_ref, ltm_ref):
    ch = ltm_ref.shape[1]
    width = lw_ref.shape[2] // 2
    count = 2 * lw_ref.shape[0]
    size = ltm_ref.shape[0] // count
    for z in range(lw_ref.shape[0]):
        first = lw_ref[z, :, 0:ch].astype(F32)
        off = width % 128
        second = lw_ref[z, :, width - off : width - off + ch + 128].astype(F32)
        second = pltpu.roll(second, ch + 128 - off, 1)[:, 0:ch]
        for b, block in ((2 * z, first), (2 * z + 1, second)):
            lf_ref[b * size : b * size + block.shape[0], :] = block
    ltm_ref[...] = lf_ref[0 : ltm_ref.shape[0], :].astype(BF)


def prepare_body(w_ref, kn_out, l_out, lt_out, rows_out, ktm_ref, lw_ref, lf_ref, sems):
    hc, ch = ktm_ref.shape[0], l_out.shape[1]
    for copy in fetch_kernels(w_ref, ktm_ref, lw_ref, sems):
        copy.wait()
    for t in range(9):
        kn_out[t] = ktm_ref[:, t * ch : (t + 1) * ch].astype(F32).T.astype(BF)
    join_temporal(lw_ref, lf_ref, l_out)
    rows_out[...] = lw_ref[:, lw_ref.shape[1] - rows_out.shape[1] :, :]
    for t in range(3):
        lt_out[t] = lf_ref[t * hc : (t + 1) * hc].T.astype(BF)


def prepare(w, hc, ch, deps=()):
    outs = [
        jax.ShapeDtypeStruct((9, ch, hc), BF),
        jax.ShapeDtypeStruct((3 * hc, ch), BF),
        jax.ShapeDtypeStruct((3, ch, hc), BF),
        jax.ShapeDtypeStruct((w.shape[0], 16, w.shape[2]), BF),
    ]
    tall = w.shape[1] - hc
    scratch = [
        pltpu.VMEM((hc, 9 * ch), BF),
        pltpu.VMEM((w.shape[0], tall, w.shape[2]), BF),
        pltpu.VMEM((3 * hc + tall, ch), F32),
        pltpu.SemaphoreType.DMA((2 * w.shape[0],)),
    ]
    return call(prepare_body, outs, scratch, 2 * w.size * 512, w, deps=deps, far=(0,))


def conv_body(side, first, rank_ref, *refs):
    n = 1 if first else 8
    slices = refs[:n]
    (kn_in, ltm_ref, vec_ref, before_ref, after_ref,
     pad_out, hid_out, xhat_out, rs_ref, mate_ref, keep_ref,
     pad_ref, hid_ref, xhat_ref, sp_ref, kn_ref, sems) = refs[n:]
    rank = rank_ref[0]
    kn_copy = pltpu.make_async_copy(kn_in, kn_ref, sems.at[0])
    kn_copy.start()
    ch, hc = pad_ref.shape[2], hid_ref.shape[1]
    rows = hid_ref.shape[0]
    plane = rows // side
    nf = plane // side
    step = plane // 2
    clear_borders(pad_ref, side, plane, nf)
    if first:
        for i in range(side):
            pad_ref[i + 1, nf : nf + plane] = slices[0][i * plane : (i + 1) * plane]
    else:
        def place(k, carry):
            for q, odd, a_ref, b_ref in by_rank(slices, rank):
                top, bottom = halves(odd, a_ref[chunk(k, step), :], b_ref[chunk(k, step), :])
                lanes = pl.ds(pl.multiple_of(128 * q, 128), 128)
                for piece, kk in ((top, k), (bottom, k + side)):
                    at = nf + lax.rem(kk, 2) * step
                    pad_ref[1 + kk // 2, pl.ds(pl.multiple_of(at, 16), step), lanes] = piece.astype(BF)
            return carry

        lax.fori_loop(0, side, place, 0, unroll=True)
    pad_copy = pltpu.make_async_copy(pad_ref, pad_out, sems.at[1])
    pad_copy.start()
    kn_copy.wait()

    def conv(i, total):
        acc = jnp.zeros((plane, hc), F32)
        for t in range(9):
            r, c = t // 3, t % 3
            acc += nn(pad_ref[i + r, c * nf : c * nf + plane, :], kn_ref[t])
        sp_ref[i] = acc
        return total + jnp.sum(acc, axis=0, keepdims=True)

    mean = lax.fori_loop(0, side, conv, jnp.zeros((1, hc), F32), unroll=True) / rows

    def square(i, total):
        cen = sp_ref[i] - mean
        return total + jnp.sum(cen * cen, axis=0, keepdims=True)

    var = lax.fori_loop(0, side, square, jnp.zeros((1, hc), F32), unroll=True) / rows
    rs = lax.rsqrt(var + eps)
    rs_ref[...] = rs
    gain, bias = vec_ref[0:1, :], vec_ref[1:2, :]

    def act(i, carry):
        xhat = (sp_ref[i] - mean) * rs
        xhat_ref[i] = xhat
        v = xhat * gain + bias
        v = v * jax.nn.sigmoid(v)
        sp_ref[i] = v
        hid_ref[chunk(i, plane), :] = v.astype(BF)
        return carry

    lax.fori_loop(0, side, act, 0, unroll=True)
    late = [
        pltpu.make_async_copy(hid_ref, hid_out, sems.at[2]),
        pltpu.make_async_copy(xhat_ref, xhat_out, sems.at[3]),
    ]
    for copy in late:
        copy.start()
    low = lax.broadcasted_iota(jnp.int32, (step, 128), 1) < 64

    def temporal(k, carry):
        pieces = []
        for kk in (k, k + side):
            par = lax.rem(kk, 2)
            h = sp_ref[kk // 2, pl.ds(pl.multiple_of(par * step, 8), step), :]
            at = pl.multiple_of(par * (step % nf), 8)
            pieces.append((
                (pltpu.roll(h, 1, 0) * before_ref[pl.ds(at, step), :]).astype(BF),
                h.astype(BF),
                (pltpu.roll(h, step - 1, 0) * after_ref[pl.ds(at, step), :]).astype(BF),
            ))
        part = sum(
            nn(jnp.concatenate([x, y], axis=0), ltm_ref[t * hc : (t + 1) * hc])
            for t, (x, y) in enumerate(zip(*pieces))
        )
        store_packed(rank, mate_ref, keep_ref, part, k, step, low)
        return carry

    lax.fori_loop(0, side, temporal, 0, unroll=True)
    for copy in [pad_copy] + late:
        copy.wait()


def conv_forward(rank, g, kn, lt, vec, before, after, side, pixels, ch, deps=()):
    hc = vec.shape[1]
    plane = pixels // side
    nf = plane // side
    n = len(g)
    shapes = [
        ((side + 2, plane + 2 * nf, ch), BF),
        ((pixels, hc), BF),
        ((side, plane, hc), F32),
    ]
    outs = [jax.ShapeDtypeStruct(*s) for s in shapes] + [
        jax.ShapeDtypeStruct((1, hc), F32),
        jax.ShapeDtypeStruct((4, pixels // 2, 128), BF),
        jax.ShapeDtypeStruct((4, pixels // 2, 128), BF),
    ]
    scratch = [pltpu.VMEM(*s) for s in shapes] + [
        pltpu.VMEM((side, plane, hc), F32),
        pltpu.VMEM((9, ch, hc), BF),
        pltpu.SemaphoreType.DMA((4,)),
    ]
    flops = 2 * pixels * hc * 12 * ch
    return call(functools.partial(conv_body, side, n == 1), outs, scratch, flops,
                rank, *g, kn, lt, vec, before, after,
                deps=deps, far=(n + 1,), far_outs=(0, 1, 2))


def fold(v):
    return v + pltpu.roll(v, 64, 1)


def total_of(refs):
    t = refs[0][...].astype(F32)
    for ref in refs[1:]:
        t += ref[...].astype(F32)
    return t


def pair_sum_body(keep_ref, mate_ref, *out_refs):
    for p, ref in enumerate(out_refs):
        ref[...] = (keep_ref[p].astype(F32) + mate_ref[p].astype(F32)).astype(ref.dtype)


def pair_sum(keep, arrived, deps=()):
    shape = keep.shape[1:]
    outs = [jax.ShapeDtypeStruct(shape, BF)] * keep.shape[0]
    return call(pair_sum_body, outs, [], keep.size, keep, arrived, deps=deps)


def out_norm_body(n, has_skip, *refs):
    parts, refs = refs[:n], refs[n:]
    if has_skip:
        vec_ref, skip_ref, xhat_ref, rs_ref, pre_ref, res_ref = refs
    else:
        vec_ref, xhat_ref, rs_ref, pre_ref, res_ref = refs
    t = total_of(parts)
    pixels = 2 * t.shape[0]
    mean = fold(jnp.sum(t, axis=0, keepdims=True)) / pixels
    cen = t - mean
    rs = lax.rsqrt(fold(jnp.sum(cen * cen, axis=0, keepdims=True)) / pixels + eps)
    xhat = cen * rs
    pre = xhat * vec_ref[0:1, :] + vec_ref[1:2, :]
    if has_skip:
        pre = pre + skip_ref[...].astype(F32)
    xhat_ref[...] = xhat
    rs_ref[...] = rs
    pre_ref[...] = pre
    res_ref[...] = (pre * jax.nn.sigmoid(pre)).astype(BF)


def out_norm(parts, vec, skip, deps=()):
    half = parts[0].shape[0]
    outs = [
        jax.ShapeDtypeStruct((half, 128), F32),
        jax.ShapeDtypeStruct((1, 128), F32),
        jax.ShapeDtypeStruct((half, 128), F32),
        jax.ShapeDtypeStruct((half, 128), BF),
    ]
    args = (*parts, vec) + (() if skip is None else (skip,))
    body = functools.partial(out_norm_body, len(parts), skip is not None)
    return call(body, outs, [], half * 128 * 10, *args, deps=deps)


def out_back_body(n, *refs):
    parts, (pre_ref, xhat_ref, rs_ref, vec_ref, dpre_ref, dt_ref, sums_ref) = refs[:n], refs[n:]
    g = total_of(parts)
    pre, xhat = pre_ref[...], xhat_ref[...]
    sig = jax.nn.sigmoid(pre)
    dpre = g * (sig * (1.0 + pre * (1.0 - sig)))
    pixels = 2 * pre.shape[0]
    sb = fold(jnp.sum(dpre, axis=0, keepdims=True))
    sg = fold(jnp.sum(dpre * xhat, axis=0, keepdims=True))
    dpre_ref[...] = dpre.astype(BF)
    scale = vec_ref[0:1, :] * rs_ref[...]
    dt_ref[...] = (scale * (dpre - sb / pixels - xhat * (sg / pixels))).astype(BF)
    sums_ref[0:1, :] = sg
    sums_ref[1:2, :] = sb


def out_back(parts, pre, xhat, rs, vec, deps=()):
    half = pre.shape[0]
    outs = [
        jax.ShapeDtypeStruct((half, 128), BF),
        jax.ShapeDtypeStruct((half, 128), BF),
        jax.ShapeDtypeStruct((2, 128), F32),
    ]
    args = (*parts, pre, xhat, rs, vec)
    return call(functools.partial(out_back_body, len(parts)), outs, [], half * 1280, *args, deps=deps)


def conv_back_body(side, rank_ref, *refs):
    slices, (xhat_in, rs_ref, w_ref, lnt_ref, vec_ref, before_ref, after_ref,
             dt_out, ds_out, sums_ref, mate_ref, keep_ref,
             dt_ref, ds_ref, xhat_ref, dy_ref, pad_ref, ktm_ref, sems) = refs[:8], refs[8:]
    half = slices[0].shape[0]
    rank = rank_ref[0]
    nz, _, width = w_ref.shape
    rows = 2 * half
    plane = rows // side
    nf = plane // side
    step = plane // 2
    hc = ds_ref.shape[1]
    ch = dt_ref.shape[1]
    fetched = [
        pltpu.make_async_copy(
            w_ref.at[z, pl.ds(0, hc)], ktm_ref.at[:, pl.ds(z * width, width)], sems.at[z])
        for z in range(nz)
    ]
    xhat_copy = pltpu.make_async_copy(xhat_in, xhat_ref, sems.at[nz])
    for copy in fetched + [xhat_copy]:
        copy.start()
    clear_borders(pad_ref, side, plane, nf)

    def place(k, carry):
        for q, odd, a_ref, b_ref in by_rank(slices, rank):
            top, bottom = halves(odd, a_ref[chunk(k, step), :], b_ref[chunk(k, step), :])
            lanes = pl.ds(pl.multiple_of(128 * q, 128), 128)
            dt_ref[chunk(k, step), lanes] = top.astype(BF)
            dt_ref[pl.ds(pl.multiple_of(half + k * step, 16), step), lanes] = bottom.astype(BF)
        return carry

    lax.fori_loop(0, side, place, 0, unroll=True)
    dt_copy = pltpu.make_async_copy(dt_ref, dt_out, sems.at[nz + 1])
    dt_copy.start()
    xhat_copy.wait()
    gain, bias = vec_ref[0:1, :], vec_ref[1:2, :]

    def hidden_grad(i, sums):
        dt = dt_ref[chunk(i, plane), :]
        early = nn(dt, lnt_ref[0]) * before_ref[0:plane, :]
        late = nn(dt, lnt_ref[2]) * after_ref[0:plane, :]
        dh = nn(dt, lnt_ref[1]) + pltpu.roll(early, plane - 1, 0) + pltpu.roll(late, 1, 0)
        xhat = xhat_ref[i]
        v = xhat * gain + bias
        sig = jax.nn.sigmoid(v)
        dy = dh * (sig * (1.0 + v * (1.0 - sig)))
        dy_ref[i] = dy
        return (
            sums[0] + jnp.sum(dy * xhat, axis=0, keepdims=True),
            sums[1] + jnp.sum(dy, axis=0, keepdims=True),
        )

    zero = jnp.zeros((1, hc), F32)
    sg, sb = lax.fori_loop(0, side, hidden_grad, (zero, zero), unroll=True)
    sums_ref[0:1, :] = sg
    sums_ref[1:2, :] = sb
    scale = gain * rs_ref[...]

    def spatial_grad(i, carry):
        ds = (scale * (dy_ref[i] - sb / rows - xhat_ref[i] * (sg / rows))).astype(BF)
        pad_ref[i + 1, nf : nf + plane] = ds
        ds_ref[chunk(i, plane), :] = ds
        return carry

    lax.fori_loop(0, side, spatial_grad, 0, unroll=True)
    ds_copy = pltpu.make_async_copy(ds_ref, ds_out, sems.at[nz + 2])
    ds_copy.start()
    for copy in fetched:
        copy.wait()
    low = lax.broadcasted_iota(jnp.int32, (step, 128), 1) < 64

    def back(k, carry):
        acc = jnp.zeros((2 * step, ch), F32)
        for t in range(9):
            r, c = 2 - t // 3, 2 - t % 3
            pieces = []
            for kk in (k, k + side):
                at = c * nf + lax.rem(kk, 2) * step
                pieces.append(pad_ref[kk // 2 + r, pl.ds(pl.multiple_of(at, 16), step), :])
            acc += nn(jnp.concatenate(pieces, axis=0), ktm_ref[:, t * ch : (t + 1) * ch])
        store_packed(rank, mate_ref, keep_ref, acc, k, step, low)
        return carry

    lax.fori_loop(0, side, back, 0, unroll=True)
    dt_copy.wait()
    ds_copy.wait()


def conv_back(rank, g, xhat, rs, w, lnt, vec, before, after, side, deps=()):
    half = g[0].shape[0]
    hc = vec.shape[1]
    ch = len(g) * 64
    pixels = 2 * half
    plane = pixels // side
    nf = plane // side
    outs = [
        jax.ShapeDtypeStruct((pixels, ch), BF),
        jax.ShapeDtypeStruct((pixels, hc), BF),
        jax.ShapeDtypeStruct((2, hc), F32),
        jax.ShapeDtypeStruct((4, half, 128), BF),
        jax.ShapeDtypeStruct((4, half, 128), BF),
    ]
    scratch = [
        pltpu.VMEM((pixels, ch), BF),
        pltpu.VMEM((pixels, hc), BF),
        pltpu.VMEM((side, plane, hc), F32),
        pltpu.VMEM((side, plane, hc), F32),
        pltpu.VMEM((side + 2, plane + 2 * nf, hc), BF),
        pltpu.VMEM((hc, 9 * ch), BF),
        pltpu.SemaphoreType.DMA((w.shape[0] + 3,)),
    ]
    flops = 2 * pixels * hc * 12 * ch
    return call(functools.partial(conv_back_body, side), outs, scratch, flops,
                rank, *g, xhat, rs, w, lnt, vec, before, after,
                deps=deps, far=(9, 11), far_outs=(0, 1))


def grads_body(side, pad_ref, hid_ref, ds_ref, dt_ref, before_ref, after_ref, mid_ref, out_ref,
               sg_ref, dst_ref, taps_ref, tg_ref, vec_ref):
    ch = pad_ref.shape[2]
    hc = hid_ref.shape[1]
    plane = hid_ref.shape[0] // side
    nf = plane // side
    for i in (0, 1, side + 2, side + 3):
        dst_ref[i] = jnp.zeros(dst_ref.shape[1:], BF)
    for i in range(side):
        at = slice(i * plane, (i + 1) * plane)
        h = hid_ref[at, :].astype(F32)
        taps_ref[i, 0:hc] = (pltpu.roll(h, 1, 0) * before_ref[0:plane, :]).T.astype(BF)
        taps_ref[i, hc : 2 * hc] = h.T.astype(BF)
        taps_ref[i, 2 * hc : 3 * hc] = (pltpu.roll(h, plane - 1, 0) * after_ref[0:plane, :]).T.astype(BF)
        dst_ref[i + 2] = ds_ref[at, :].astype(F32).T.astype(BF)
    tg_ref[0 : 3 * hc, :] = sum(
        nn(taps_ref[i], dt_ref[i * plane : (i + 1) * plane, :]) for i in range(side)
    )
    tg_ref[3 * hc :, :] = jnp.zeros((tg_ref.shape[0] - 3 * hc, ch), F32)
    nz, _, width = sg_ref.shape
    size = 3 * hc // (2 * nz)
    vec_ref[...] = jnp.zeros(vec_ref.shape, F32)
    vec_ref[size : size + 2, 0:hc] = mid_ref[...]
    vec_ref[size + 2 : size + 4, 0:128] = out_ref[...]
    tall = vec_ref.shape[0]
    inside = lax.broadcasted_iota(jnp.int32, (tall, ch), 0) < size
    off = (width // 2) % 128
    for z in range(nz):
        first, second = [
            jnp.where(inside, tg_ref[b * size : b * size + tall, :], vec_ref[...])
            for b in (2 * z, 2 * z + 1)
        ]
        start = width // 2 - off
        sg_ref[z, hc : hc + tall, 0:ch] = first.astype(BF)
        second = pltpu.roll(jnp.concatenate([second, jnp.zeros((tall, 128), F32)], axis=1), off, 1)
        sg_ref[z, hc : hc + tall, start : start + ch + 128] = second.astype(BF)
    for c in range(3):
        acc = sum(
            nn(dst_ref[i : i + 3].reshape(3 * hc, plane), pad_ref[i, c * nf : c * nf + plane, :])
            for i in range(1, side + 1)
        )
        for r in range(3):
            first = (3 * r + c) * ch
            end = first + ch
            at = (2 - r) * hc
            done = 0
            while first < end:
                z = first // width
                last = min(end, (z + 1) * width)
                sg_ref[z, 0:hc, first - z * width : last - z * width] = (
                    acc[at : at + hc, done : done + last - first].astype(BF)
                )
                done += last - first
                first = last


def kernel_grads(pad, hidden, ds, dt, before, after, mid, out, side, shape, deps=()):
    pixels, hc = hidden.shape
    ch = dt.shape[1]
    plane = pixels // side
    outs = [jax.ShapeDtypeStruct(shape, BF)]
    tall = shape[1] - hc
    scratch = [
        pltpu.VMEM((side + 4, hc, plane), BF),
        pltpu.VMEM((side, 3 * hc, plane), BF),
        pltpu.VMEM((3 * hc + tall, ch), F32),
        pltpu.VMEM((tall, ch), F32),
    ]
    flops = 2 * pixels * hc * 12 * ch
    return call(functools.partial(grads_body, side), outs, scratch, flops,
                pad, hidden, ds, dt, before, after, mid, out, deps=deps)[0]


def copy_after_body(v_ref, out_ref):
    out_ref[...] = v_ref[...]


def after_all(v, *deps):
    return call(copy_after_body, [jax.ShapeDtypeStruct(v.shape, v.dtype)], [], v.size, v, deps=deps)[0]


def pack_kernels_body(kt_ref, lt_ref, vec_ref, out_ref, low_ref):
    ranks, _, width = out_ref.shape
    hc = kt_ref.shape[0] // ranks
    blocks = lt_ref.shape[0] // hc
    q = hc // ranks
    low_ref[...] = jnp.zeros(low_ref.shape, F32)
    for r in range(ranks):
        out_ref[r, 0:hc, :] = kt_ref[r * hc : (r + 1) * hc, :]
        for b in range(blocks):
            low_ref[r, b * q : (b + 1) * q, 0 : lt_ref.shape[1]] = (
                lt_ref[b * hc + r * q : b * hc + (r + 1) * q, :]
            )
        low_ref[r, blocks * q : blocks * q + 1, :] = vec_ref[...]
        out_ref[r, hc:, :] = low_ref[r].astype(BF)


def pack_kernels(kt, lt, vec, ranks, tall, deps):
    width = kt.shape[1]
    outs = [jax.ShapeDtypeStruct((ranks, kt.shape[0] // ranks + tall, width), BF)]
    scratch = [pltpu.VMEM((ranks, tall, width), F32)]
    return call(pack_kernels_body, outs, scratch, kt.size * 8, kt, lt, vec, deps=deps)[0]


def call(body, outs, scratch, flops, *args, deps=(), far=(), far_outs=()):
    moved = sum(a.size * a.dtype.itemsize for a in args) + sum(
        o.size * o.dtype.itemsize for o in outs
    )
    n = len(deps)

    def spec(a):
        return pl.BlockSpec(memory_space=pltpu.SMEM if a.dtype == jnp.int32 else pltpu.VMEM)

    return pl.pallas_call(
        lambda *refs: body(*refs[n:]),
        out_shape=outs,
        in_specs=[ANY] * n + [ANY if i in far else spec(a) for i, a in enumerate(args)],
        out_specs=[ANY if i in far_outs else spec(o) for i, o in enumerate(outs)],
        scratch_shapes=scratch,
        compiler_params=pltpu.CompilerParams(vmem_limit_bytes=VMEM_CAP),
        cost_estimate=pl.CostEstimate(flops=flops, bytes_accessed=moved, transcendentals=0),
    )(*deps, *args)


def chunk(i, size):
    return pl.ds(pl.multiple_of(i * size, 16), size)


def clear_borders(pad_ref, side, plane, nf):
    zrow = jnp.zeros(pad_ref.shape[1:], BF)
    pad_ref[0] = zrow
    pad_ref[side + 1] = zrow
    zcol = jnp.zeros((nf, pad_ref.shape[2]), BF)
    for i in range(side):
        pad_ref[i + 1, 0:nf] = zcol
        pad_ref[i + 1, nf + plane : 2 * nf + plane] = zcol


def by_rank(slices, rank):
    odd = lax.rem(rank, 2) == 1
    for p in range(len(slices) // 2):
        a, b = slices[2 * p], slices[2 * p + 1]
        yield lax.bitwise_xor(rank // 2, p), odd, a, b


def halves(odd, own, mate):
    low = lax.broadcasted_iota(jnp.int32, own.shape, 1) < 64
    own, mate = own.astype(F32), mate.astype(F32)
    a, b = jnp.where(odd, mate, own), jnp.where(odd, own, mate)
    top = jnp.where(low, a, pltpu.roll(b, 64, 1))
    bottom = jnp.where(low, pltpu.roll(a, 64, 1), b)
    return top, bottom


def store_packed(rank, mate_ref, keep_ref, part, k, step, low):
    rows_now = chunk(k, step)
    odd = lax.rem(rank, 2) == 1
    for q in range(keep_ref.shape[0]):
        x = part[:step, 128 * q : 128 * q + 128]
        y = part[step:, 128 * q : 128 * q + 128]
        even_slice = jnp.where(low, x, pltpu.roll(y, 64, 1))
        odd_slice = jnp.where(low, pltpu.roll(x, 64, 1), y)
        p = lax.bitwise_xor(rank // 2, q)
        keep_ref[p, rows_now, :] = jnp.where(odd, odd_slice, even_slice).astype(BF)
        mate_ref[p, rows_now, :] = jnp.where(odd, even_slice, odd_slice).astype(BF)


def fetch_kernels(w_ref, ktm_ref, lw_ref, sems):
    nz, _, width = w_ref.shape
    hc = ktm_ref.shape[0]
    copies = []
    for z in range(nz):
        copies.append(pltpu.make_async_copy(
            w_ref.at[z, pl.ds(0, hc)], ktm_ref.at[:, pl.ds(z * width, width)], sems.at[2 * z]))
        copies.append(pltpu.make_async_copy(
            w_ref.at[z, pl.ds(hc, lw_ref.shape[1])], lw_ref.at[z], sems.at[2 * z + 1]))
    for copy in copies:
        copy.start()
    return copies


def join_temporal(lw_ref, lf_ref, ltm_ref):
    ch = ltm_ref.shape[1]
    width = lw_ref.shape[2] // 2
    count = 2 * lw_ref.shape[0]
    size = ltm_ref.shape[0] // count
    for z in range(lw_ref.shape[0]):
        first = lw_ref[z, :, 0:ch].astype(F32)
        off = width % 128
        second = lw_ref[z, :, width - off : width - off + ch + 128].astype(F32)
        second = pltpu.roll(second, ch + 128 - off, 1)[:, 0:ch]
        for b, block in ((2 * z, first), (2 * z + 1, second)):
            lf_ref[b * size : b * size + block.shape[0], :] = block
    ltm_ref[...] = lf_ref[0 : ltm_ref.shape[0], :].astype(BF)


def prepare_body(w_ref, kn_out, l_out, lt_out, rows_out, ktm_ref, lw_ref, lf_ref, sems):
    hc, ch = ktm_ref.shape[0], l_out.shape[1]
    for copy in fetch_kernels(w_ref, ktm_ref, lw_ref, sems):
        copy.wait()
    for t in range(9):
        kn_out[t] = ktm_ref[:, t * ch : (t + 1) * ch].astype(F32).T.astype(BF)
    join_temporal(lw_ref, lf_ref, l_out)
    rows_out[...] = lw_ref[:, lw_ref.shape[1] - rows_out.shape[1] :, :]
    for t in range(3):
        lt_out[t] = lf_ref[t * hc : (t + 1) * hc].T.astype(BF)


def prepare(w, hc, ch, deps=()):
    outs = [
        jax.ShapeDtypeStruct((9, ch, hc), BF),
        jax.ShapeDtypeStruct((3 * hc, ch), BF),
        jax.ShapeDtypeStruct((3, ch, hc), BF),
        jax.ShapeDtypeStruct((w.shape[0], 16, w.shape[2]), BF),
    ]
    tall = w.shape[1] - hc
    scratch = [
        pltpu.VMEM((hc, 9 * ch), BF),
        pltpu.VMEM((w.shape[0], tall, w.shape[2]), BF),
        pltpu.VMEM((3 * hc + tall, ch), F32),
        pltpu.SemaphoreType.DMA((2 * w.shape[0],)),
    ]
    return call(prepare_body, outs, scratch, 2 * w.size * 512, w, deps=deps, far=(0,))


def conv_body(side, first, rank_ref, *refs):
    n = 1 if first else 8
    slices = refs[:n]
    (kn_in, ltm_ref, vec_ref, before_ref, after_ref,
     pad_out, hid_out, xhat_out, rs_ref, mate_ref, keep_ref,
     pad_ref, hid_ref, xhat_ref, sp_ref, kn_ref, sems) = refs[n:]
    rank = rank_ref[0]
    kn_copy = pltpu.make_async_copy(kn_in, kn_ref, sems.at[0])
    kn_copy.start()
    ch, hc = pad_ref.shape[2], hid_ref.shape[1]
    rows = hid_ref.shape[0]
    plane = rows // side
    nf = plane // side
    step = plane // 2
    clear_borders(pad_ref, side, plane, nf)
    if first:
        for i in range(side):
            pad_ref[i + 1, nf : nf + plane] = slices[0][i * plane : (i + 1) * plane]
    else:
        def place(k, carry):
            for q, odd, a_ref, b_ref in by_rank(slices, rank):
                top, bottom = halves(odd, a_ref[chunk(k, step), :], b_ref[chunk(k, step), :])
                lanes = pl.ds(pl.multiple_of(128 * q, 128), 128)
                for piece, kk in ((top, k), (bottom, k + side)):
                    at = nf + lax.rem(kk, 2) * step
                    pad_ref[1 + kk // 2, pl.ds(pl.multiple_of(at, 16), step), lanes] = piece.astype(BF)
            return carry

        lax.fori_loop(0, side, place, 0, unroll=True)
    pad_copy = pltpu.make_async_copy(pad_ref, pad_out, sems.at[1])
    pad_copy.start()
    kn_copy.wait()

    def conv(i, total):
        acc = jnp.zeros((plane, hc), F32)
        for t in range(9):
            r, c = t // 3, t % 3
            acc += nn(pad_ref[i + r, c * nf : c * nf + plane, :], kn_ref[t])
        sp_ref[i] = acc
        return total + jnp.sum(acc, axis=0, keepdims=True)

    mean = lax.fori_loop(0, side, conv, jnp.zeros((1, hc), F32), unroll=True) / rows

    def square(i, total):
        cen = sp_ref[i] - mean
        return total + jnp.sum(cen * cen, axis=0, keepdims=True)

    var = lax.fori_loop(0, side, square, jnp.zeros((1, hc), F32), unroll=True) / rows
    rs = lax.rsqrt(var + eps)
    rs_ref[...] = rs
    gain, bias = vec_ref[0:1, :], vec_ref[1:2, :]

    def act(i, carry):
        xhat = (sp_ref[i] - mean) * rs
        xhat_ref[i] = xhat
        v = xhat * gain + bias
        v = v * jax.nn.sigmoid(v)
        sp_ref[i] = v
        hid_ref[chunk(i, plane), :] = v.astype(BF)
        return carry

    lax.fori_loop(0, side, act, 0, unroll=True)
    late = [
        pltpu.make_async_copy(hid_ref, hid_out, sems.at[2]),
        pltpu.make_async_copy(xhat_ref, xhat_out, sems.at[3]),
    ]
    for copy in late:
        copy.start()
    low = lax.broadcasted_iota(jnp.int32, (step, 128), 1) < 64

    def temporal(k, carry):
        pieces = []
        for kk in (k, k + side):
            par = lax.rem(kk, 2)
            h = sp_ref[kk // 2, pl.ds(pl.multiple_of(par * step, 8), step), :]
            at = pl.multiple_of(par * (step % nf), 8)
            pieces.append((
                (pltpu.roll(h, 1, 0) * before_ref[pl.ds(at, step), :]).astype(BF),
                h.astype(BF),
                (pltpu.roll(h, step - 1, 0) * after_ref[pl.ds(at, step), :]).astype(BF),
            ))
        part = sum(
            nn(jnp.concatenate([x, y], axis=0), ltm_ref[t * hc : (t + 1) * hc])
            for t, (x, y) in enumerate(zip(*pieces))
        )
        store_packed(rank, mate_ref, keep_ref, part, k, step, low)
        return carry

    lax.fori_loop(0, side, temporal, 0, unroll=True)
    for copy in [pad_copy] + late:
        copy.wait()


def conv_forward(rank, g, kn, lt, vec, before, after, side, pixels, ch, deps=()):
    hc = vec.shape[1]
    plane = pixels // side
    nf = plane // side
    n = len(g)
    shapes = [
        ((side + 2, plane + 2 * nf, ch), BF),
        ((pixels, hc), BF),
        ((side, plane, hc), F32),
    ]
    outs = [jax.ShapeDtypeStruct(*s) for s in shapes] + [
        jax.ShapeDtypeStruct((1, hc), F32),
        jax.ShapeDtypeStruct((4, pixels // 2, 128), BF),
        jax.ShapeDtypeStruct((4, pixels // 2, 128), BF),
    ]
    scratch = [pltpu.VMEM(*s) for s in shapes] + [
        pltpu.VMEM((side, plane, hc), F32),
        pltpu.VMEM((9, ch, hc), BF),
        pltpu.SemaphoreType.DMA((4,)),
    ]
    flops = 2 * pixels * hc * 12 * ch
    return call(functools.partial(conv_body, side, n == 1), outs, scratch, flops,
                rank, *g, kn, lt, vec, before, after,
                deps=deps, far=(n + 1,), far_outs=(0, 1, 2))


def fold(v):
    return v + pltpu.roll(v, 64, 1)


def total_of(refs):
    t = refs[0][...].astype(F32)
    for ref in refs[1:]:
        t += ref[...].astype(F32)
    return t


def pair_sum_body(keep_ref, mate_ref, *out_refs):
    for p, ref in enumerate(out_refs):
        ref[...] = (keep_ref[p].astype(F32) + mate_ref[p].astype(F32)).astype(ref.dtype)


def pair_sum(keep, arrived, deps=()):
    shape = keep.shape[1:]
    outs = [jax.ShapeDtypeStruct(shape, BF)] * keep.shape[0]
    return call(pair_sum_body, outs, [], keep.size, keep, arrived, deps=deps)


def out_norm_body(n, has_skip, *refs):
    parts, refs = refs[:n], refs[n:]
    if has_skip:
        vec_ref, skip_ref, xhat_ref, rs_ref, pre_ref, res_ref = refs
    else:
        vec_ref, xhat_ref, rs_ref, pre_ref, res_ref = refs
    t = total_of(parts)
    pixels = 2 * t.shape[0]
    mean = fold(jnp.sum(t, axis=0, keepdims=True)) / pixels
    cen = t - mean
    rs = lax.rsqrt(fold(jnp.sum(cen * cen, axis=0, keepdims=True)) / pixels + eps)
    xhat = cen * rs
    pre = xhat * vec_ref[0:1, :] + vec_ref[1:2, :]
    if has_skip:
        pre = pre + skip_ref[...].astype(F32)
    xhat_ref[...] = xhat
    rs_ref[...] = rs
    pre_ref[...] = pre
    res_ref[...] = (pre * jax.nn.sigmoid(pre)).astype(BF)


def out_norm(parts, vec, skip, deps=()):
    half = parts[0].shape[0]
    outs = [
        jax.ShapeDtypeStruct((half, 128), F32),
        jax.ShapeDtypeStruct((1, 128), F32),
        jax.ShapeDtypeStruct((half, 128), F32),
        jax.ShapeDtypeStruct((half, 128), BF),
    ]
    args = (*parts, vec) + (() if skip is None else (skip,))
    body = functools.partial(out_norm_body, len(parts), skip is not None)
    return call(body, outs, [], half * 128 * 10, *args, deps=deps)


def out_back_body(n, *refs):
    parts, (pre_ref, xhat_ref, rs_ref, vec_ref, dpre_ref, dt_ref, sums_ref) = refs[:n], refs[n:]
    g = total_of(parts)
    pre, xhat = pre_ref[...], xhat_ref[...]
    sig = jax.nn.sigmoid(pre)
    dpre = g * (sig * (1.0 + pre * (1.0 - sig)))
    pixels = 2 * pre.shape[0]
    sb = fold(jnp.sum(dpre, axis=0, keepdims=True))
    sg = fold(jnp.sum(dpre * xhat, axis=0, keepdims=True))
    dpre_ref[...] = dpre.astype(BF)
    scale = vec_ref[0:1, :] * rs_ref[...]
    dt_ref[...] = (scale * (dpre - sb / pixels - xhat * (sg / pixels))).astype(BF)
    sums_ref[0:1, :] = sg
    sums_ref[1:2, :] = sb


def out_back(parts, pre, xhat, rs, vec, deps=()):
    half = pre.shape[0]
    outs = [
        jax.ShapeDtypeStruct((half, 128), BF),
        jax.ShapeDtypeStruct((half, 128), BF),
        jax.ShapeDtypeStruct((2, 128), F32),
    ]
    args = (*parts, pre, xhat, rs, vec)
    return call(functools.partial(out_back_body, len(parts)), outs, [], half * 1280, *args, deps=deps)


def conv_back_body(side, rank_ref, *refs):
    slices, (xhat_in, rs_ref, w_ref, lnt_ref, vec_ref, before_ref, after_ref,
             dt_out, ds_out, sums_ref, mate_ref, keep_ref,
             dt_ref, ds_ref, xhat_ref, dy_ref, pad_ref, ktm_ref, sems) = refs[:8], refs[8:]
    half = slices[0].shape[0]
    rank = rank_ref[0]
    nz, _, width = w_ref.shape
    rows = 2 * half
    plane = rows // side
    nf = plane // side
    step = plane // 2
    hc = ds_ref.shape[1]
    ch = dt_ref.shape[1]
    fetched = [
        pltpu.make_async_copy(
            w_ref.at[z, pl.ds(0, hc)], ktm_ref.at[:, pl.ds(z * width, width)], sems.at[z])
        for z in range(nz)
    ]
    xhat_copy = pltpu.make_async_copy(xhat_in, xhat_ref, sems.at[nz])
    for copy in fetched + [xhat_copy]:
        copy.start()
    clear_borders(pad_ref, side, plane, nf)

    def place(k, carry):
        for q, odd, a_ref, b_ref in by_rank(slices, rank):
            top, bottom = halves(odd, a_ref[chunk(k, step), :], b_ref[chunk(k, step), :])
            lanes = pl.ds(pl.multiple_of(128 * q, 128), 128)
            dt_ref[chunk(k, step), lanes] = top.astype(BF)
            dt_ref[pl.ds(pl.multiple_of(half + k * step, 16), step), lanes] = bottom.astype(BF)
        return carry

    lax.fori_loop(0, side, place, 0, unroll=True)
    dt_copy = pltpu.make_async_copy(dt_ref, dt_out, sems.at[nz + 1])
    dt_copy.start()
    xhat_copy.wait()
    gain, bias = vec_ref[0:1, :], vec_ref[1:2, :]

    def hidden_grad(i, sums):
        dt = dt_ref[chunk(i, plane), :]
        early = nn(dt, lnt_ref[0]) * before_ref[0:plane, :]
        late = nn(dt, lnt_ref[2]) * after_ref[0:plane, :]
        dh = nn(dt, lnt_ref[1]) + pltpu.roll(early, plane - 1, 0) + pltpu.roll(late, 1, 0)
        xhat = xhat_ref[i]
        v = xhat * gain + bias
        sig = jax.nn.sigmoid(v)
        dy = dh * (sig * (1.0 + v * (1.0 - sig)))
        dy_ref[i] = dy
        return (
            sums[0] + jnp.sum(dy * xhat, axis=0, keepdims=True),
            sums[1] + jnp.sum(dy, axis=0, keepdims=True),
        )

    zero = jnp.zeros((1, hc), F32)
    sg, sb = lax.fori_loop(0, side, hidden_grad, (zero, zero), unroll=True)
    sums_ref[0:1, :] = sg
    sums_ref[1:2, :] = sb
    scale = gain * rs_ref[...]

    def spatial_grad(i, carry):
        ds = (scale * (dy_ref[i] - sb / rows - xhat_ref[i] * (sg / rows))).astype(BF)
        pad_ref[i + 1, nf : nf + plane] = ds
        ds_ref[chunk(i, plane), :] = ds
        return carry

    lax.fori_loop(0, side, spatial_grad, 0, unroll=True)
    ds_copy = pltpu.make_async_copy(ds_ref, ds_out, sems.at[nz + 2])
    ds_copy.start()
    for copy in fetched:
        copy.wait()
    low = lax.broadcasted_iota(jnp.int32, (step, 128), 1) < 64

    def back(k, carry):
        acc = jnp.zeros((2 * step, ch), F32)
        for t in range(9):
            r, c = 2 - t // 3, 2 - t % 3
            pieces = []
            for kk in (k, k + side):
                at = c * nf + lax.rem(kk, 2) * step
                pieces.append(pad_ref[kk // 2 + r, pl.ds(pl.multiple_of(at, 16), step), :])
            acc += nn(jnp.concatenate(pieces, axis=0), ktm_ref[:, t * ch : (t + 1) * ch])
        store_packed(rank, mate_ref, keep_ref, acc, k, step, low)
        return carry

    lax.fori_loop(0, side, back, 0, unroll=True)
    dt_copy.wait()
    ds_copy.wait()


def conv_back(rank, g, xhat, rs, w, lnt, vec, before, after, side, deps=()):
    half = g[0].shape[0]
    hc = vec.shape[1]
    ch = len(g) * 64
    pixels = 2 * half
    plane = pixels // side
    nf = plane // side
    outs = [
        jax.ShapeDtypeStruct((pixels, ch), BF),
        jax.ShapeDtypeStruct((pixels, hc), BF),
        jax.ShapeDtypeStruct((2, hc), F32),
        jax.ShapeDtypeStruct((4, half, 128), BF),
        jax.ShapeDtypeStruct((4, half, 128), BF),
    ]
    scratch = [
        pltpu.VMEM((pixels, ch), BF),
        pltpu.VMEM((pixels, hc), BF),
        pltpu.VMEM((side, plane, hc), F32),
        pltpu.VMEM((side, plane, hc), F32),
        pltpu.VMEM((side + 2, plane + 2 * nf, hc), BF),
        pltpu.VMEM((hc, 9 * ch), BF),
        pltpu.SemaphoreType.DMA((w.shape[0] + 3,)),
    ]
    flops = 2 * pixels * hc * 12 * ch
    return call(functools.partial(conv_back_body, side), outs, scratch, flops,
                rank, *g, xhat, rs, w, lnt, vec, before, after,
                deps=deps, far=(9, 11), far_outs=(0, 1))


def grads_body(side, pad_ref, hid_ref, ds_ref, dt_ref, before_ref, after_ref, mid_ref, out_ref,
               sg_ref, dst_ref, taps_ref, tg_ref, vec_ref):
    ch = pad_ref.shape[2]
    hc = hid_ref.shape[1]
    plane = hid_ref.shape[0] // side
    nf = plane // side
    for i in (0, 1, side + 2, side + 3):
        dst_ref[i] = jnp.zeros(dst_ref.shape[1:], BF)
    for i in range(side):
        at = slice(i * plane, (i + 1) * plane)
        h = hid_ref[at, :].astype(F32)
        taps_ref[i, 0:hc] = (pltpu.roll(h, 1, 0) * before_ref[0:plane, :]).T.astype(BF)
        taps_ref[i, hc : 2 * hc] = h.T.astype(BF)
        taps_ref[i, 2 * hc : 3 * hc] = (pltpu.roll(h, plane - 1, 0) * after_ref[0:plane, :]).T.astype(BF)
        dst_ref[i + 2] = ds_ref[at, :].astype(F32).T.astype(BF)
    tg_ref[0 : 3 * hc, :] = sum(
        nn(taps_ref[i], dt_ref[i * plane : (i + 1) * plane, :]) for i in range(side)
    )
    tg_ref[3 * hc :, :] = jnp.zeros((tg_ref.shape[0] - 3 * hc, ch), F32)
    nz, _, width = sg_ref.shape
    size = 3 * hc // (2 * nz)
    vec_ref[...] = jnp.zeros(vec_ref.shape, F32)
    vec_ref[size : size + 2, 0:hc] = mid_ref[...]
    vec_ref[size + 2 : size + 4, 0:128] = out_ref[...]
    tall = vec_ref.shape[0]
    inside = lax.broadcasted_iota(jnp.int32, (tall, ch), 0) < size
    off = (width // 2) % 128
    for z in range(nz):
        first, second = [
            jnp.where(inside, tg_ref[b * size : b * size + tall, :], vec_ref[...])
            for b in (2 * z, 2 * z + 1)
        ]
        start = width // 2 - off
        sg_ref[z, hc : hc + tall, 0:ch] = first.astype(BF)
        second = pltpu.roll(jnp.concatenate([second, jnp.zeros((tall, 128), F32)], axis=1), off, 1)
        sg_ref[z, hc : hc + tall, start : start + ch + 128] = second.astype(BF)
    for c in range(3):
        acc = sum(
            nn(dst_ref[i : i + 3].reshape(3 * hc, plane), pad_ref[i, c * nf : c * nf + plane, :])
            for i in range(1, side + 1)
        )
        for r in range(3):
            first = (3 * r + c) * ch
            end = first + ch
            at = (2 - r) * hc
            done = 0
            while first < end:
                z = first // width
                last = min(end, (z + 1) * width)
                sg_ref[z, 0:hc, first - z * width : last - z * width] = (
                    acc[at : at + hc, done : done + last - first].astype(BF)
                )
                done += last - first
                first = last


def kernel_grads(pad, hidden, ds, dt, before, after, mid, out, side, shape, deps=()):
    pixels, hc = hidden.shape
    ch = dt.shape[1]
    plane = pixels // side
    outs = [jax.ShapeDtypeStruct(shape, BF)]
    tall = shape[1] - hc
    scratch = [
        pltpu.VMEM((side + 4, hc, plane), BF),
        pltpu.VMEM((side, 3 * hc, plane), BF),
        pltpu.VMEM((3 * hc + tall, ch), F32),
        pltpu.VMEM((tall, ch), F32),
    ]
    flops = 2 * pixels * hc * 12 * ch
    return call(functools.partial(grads_body, side), outs, scratch, flops,
                pad, hidden, ds, dt, before, after, mid, out, deps=deps)[0]


def copy_after_body(v_ref, out_ref):
    out_ref[...] = v_ref[...]


def after_all(v, *deps):
    return call(copy_after_body, [jax.ShapeDtypeStruct(v.shape, v.dtype)], [], v.size, v, deps=deps)[0]


def pack_kernels_body(kt_ref, lt_ref, vec_ref, out_ref, low_ref):
    ranks, _, width = out_ref.shape
    hc = kt_ref.shape[0] // ranks
    blocks = lt_ref.shape[0] // hc
    q = hc // ranks
    low_ref[...] = jnp.zeros(low_ref.shape, F32)
    for r in range(ranks):
        out_ref[r, 0:hc, :] = kt_ref[r * hc : (r + 1) * hc, :]
        for b in range(blocks):
            low_ref[r, b * q : (b + 1) * q, 0 : lt_ref.shape[1]] = (
                lt_ref[b * hc + r * q : b * hc + (r + 1) * q, :]
            )
        low_ref[r, blocks * q : blocks * q + 1, :] = vec_ref[...]
        out_ref[r, hc:, :] = low_ref[r].astype(BF)


def pack_kernels(kt, lt, vec, ranks, tall, deps):
    width = kt.shape[1]
    outs = [jax.ShapeDtypeStruct((ranks, kt.shape[0] // ranks + tall, width), BF)]
    scratch = [pltpu.VMEM((ranks, tall, width), F32)]
    return call(pack_kernels_body, outs, scratch, kt.size * 8, kt, lt, vec, deps=deps)[0]


def hop(v, k):
    n = 1
    for name in EVERY:
        n *= lax.axis_size(name)
    return lax.ppermute(v, EVERY, [(i, i ^ k) for i in range(n)])


def plane_gather(v, aside=()):
    got = {0: v}
    for k in (6, 2, 4):
        got[k] = hop(v, k)
    got[1] = hop(after_all(v, *aside) if aside else v, 1)
    for k in (2, 4, 6):
        got[k ^ 1] = hop(got[k], 1)
    return [got[k] for k in range(8)]


def plane_reduce(mate, keep, deps=()):
    sums = pair_sum(keep, hop(mate, 1), deps)
    arrived = {k: hop(sums[k // 2], k) for k in (6, 2, 4)}
    return [sums[0], arrived[2], arrived[4], arrived[6]]


def on_device(frames, cot, starts, ks, ktm, mg, mb, og, ob):
    nz, n_rank, n_seg = lax.axis_size("z"), 8, 4
    n_dp = nz * 2
    fr, side, ch = frames.shape[0], frames.shape[1], frames.shape[3]
    area = side * side
    hid = ks.shape[2]
    hc, cc = hid // n_rank, ch // n_rank
    q = hc // n_rank
    rank = lax.axis_index(PLANE)
    rank_now = rank.astype(jnp.int32).reshape(1)
    d_index = lax.axis_index(("z", "y"))
    nf = n_dp * fr
    pixels = area * nf
    half = pixels // 2

    to_plane = [(d * n_seg + s, s * n_rank + d) for d in range(n_dp) for s in range(n_seg)]
    from_plane = [(b, a) for a, b in to_plane]
    rows = fr * area
    flag_row = jnp.pad(starts.astype(BF)[None], ((0, 11), (0, ch - fr)))
    moving = jnp.concatenate([frames.reshape(rows, ch), flag_row], axis=0)
    moving = lax.ppermute(moving, EVERY, to_plane)

    perm = (jnp.arange(hid).reshape(n_rank, n_rank, q).transpose(1, 0, 2).reshape(hid)[:, None]
            == jnp.arange(hid)[None, :]).astype(BF)
    kt = lax.dot_general(perm, ks[0].astype(BF), (((1,), (1,)), ((), ())),
                         preferred_element_type=F32).astype(BF)
    lrows, width = ktm.shape[1] // n_rank, ks.shape[1]
    tall = -(-(lrows + 4) // 16) * 16
    extra = jnp.concatenate([mg, mb, og, ob], axis=1)
    extra = jnp.pad(extra, ((0, 0), (0, width - extra.shape[1])))
    w = pack_kernels(kt, ktm[0], extra, n_rank, tall, deps=(moving,))
    w = lax.all_to_all(w, PLANE, 0, 0)
    here = w
    high = hc + tall

    w = w.reshape(2, n_seg, high, width).transpose(1, 2, 0, 3).reshape(n_seg, high, 2 * width)
    ws = [lax.all_gather(w[s], "z", axis=0) for s in range(n_seg)]

    moving = after_all(moving, here)
    gathered = lax.all_to_all(jnp.broadcast_to(moving, (n_rank, *moving.shape)), PLANE, 0, 0)

    def norm_rows(rows_now):
        row = rows_now[:, (lrows - tall) % 16].reshape(n_dp, width).astype(F32)
        mid = jnp.stack([
            lax.dynamic_slice_in_dim(row[:, i * hc : (i + 1) * hc], rank * q, q, axis=1).reshape(hc)
            for i in range(2)])
        own = lax.dynamic_index_in_dim(row, rank, 0, keepdims=False)
        out = jnp.stack([
            jnp.tile(own[2 * hc + i * cc : 2 * hc + (i + 1) * cc], 2) for i in range(2)])
        return mid, out

    moving = after_all(moving, here)
    gathered = lax.all_to_all(jnp.broadcast_to(moving, (n_rank, *moving.shape)), PLANE, 0, 0)
    mids, outs = [], []
    for s in range(n_seg):
        row = ws[s][:, hc + lrows].reshape(n_dp, width).astype(F32)
        mids.append(jnp.stack([
            lax.dynamic_slice_in_dim(row[:, i * hc : (i + 1) * hc], rank * q, q, axis=1).reshape(hc)
            for i in range(2)]))
        own = lax.dynamic_index_in_dim(row, rank, 0, keepdims=False)
        outs.append(jnp.stack([
            jnp.tile(own[2 * hc + i * cc : 2 * hc + (i + 1) * cc], 2) for i in range(2)]))

    def by_pixel(v):
        width = v.shape[2]
        v = v.reshape(n_rank * fr, area, width).transpose(1, 0, 2)
        return v.reshape(pixels, width)

    def packed(v):
        return jnp.concatenate([v[:half], v[half:]], axis=1)

    a0 = by_pixel(gathered[:, :rows])
    flags = gathered[:, rows, :fr].reshape(nf) > 0.5
    slot = jnp.arange(nf) % fr
    before = jnp.where(flags | (slot == 0), 0.0, 1.0)
    after = jnp.where(jnp.roll(flags, -1) | (slot == fr - 1), 0.0, 1.0)
    spread = (side * nf + nf, hc)
    before = jnp.broadcast_to(jnp.tile(before, side + 1)[:, None], spread)
    after = jnp.broadcast_to(jnp.tile(after, side + 1)[:, None], spread)
    skip = packed(lax.dynamic_slice_in_dim(a0, rank * cc, cc, axis=1))

    def by_frames(v):
        v = jnp.concatenate([v[:, :cc], v[:, cc:]], axis=0)
        return v.reshape(area, n_rank, fr, cc).transpose(1, 0, 2, 3).reshape(n_rank, rows, cc)

    def home(v):
        v = v.transpose(1, 0, 2).reshape(rows, ch)
        return lax.ppermute(v, EVERY, from_plane)

    def as_frames(v):
        return v.reshape(area, fr, ch).transpose(1, 0, 2).reshape(frames.shape)

    saved = []
    g = [a0]
    ready = prepare(ws[0], hc, ch)
    for s in range(n_seg):
        kn, lt, lnt, rows_now = ready
        mid, out = norm_rows(rows_now)
        pad, hidden, xm, rm, mate, keep = conv_forward(
            rank_now, g, kn, lt, mid, before, after, side, pixels, ch)
        if s == n_seg - 1:
            cot_own = lax.all_to_all(after_all(cot_moving, mate), PLANE, 0, 0)
            parts = plane_reduce(mate, keep, deps=(cot_own,))
        else:
            parts = plane_reduce(mate, keep)
        deps = ()
        if s == n_seg - 2:
            cot_moving = after_all(cot.reshape(rows, ch), mate)
            deps = (cot_moving,)
            cot_moving = lax.ppermute(cot_moving, EVERY, to_plane)
            cot_moving = cot_moving.reshape(rows, n_rank, cc).transpose(1, 0, 2)
            cot_moving = jnp.pad(cot_moving, ((0, 0), (0, 12), (0, 0)))
        xo, ro, pre, res = out_norm(parts, out, skip if s % 2 == 1 else None, deps=deps)
        saved.append((pad, hidden, xm, rm, xo, ro, pre, lnt, mid, out))
        if s % 2 == 1:
            skip = res
        if s < n_seg - 1:
            ready = prepare(ws[s + 1], hc, ch, deps=(res,))
            g = plane_gather(res, ready[:1])
    cot_own = packed(by_pixel(cot_own[:, :rows]))

    parts = [cot_own]
    skip_grad = None

    grads, raw = [], None
    for s in reversed(range(n_seg)):
        pad, hidden, xm, rm, xo, ro, pre, lnt, mid, out = saved[s]
        if s == 1:
            parts = parts + [skip_grad]
        deps = () if raw is None else (raw, *grads[len(grads) - 1 :])
        dpre, dt, osum = out_back(parts, pre, xo, ro, out, deps=deps)
        if raw is not None:
            grads.append(lax.psum_scatter(after_all(raw, dt), "z", scatter_dimension=0))
        if s % 2 == 1:
            skip_grad = dpre
        dtf, ds, msum, mate, keep = conv_back(
            rank_now, plane_gather(dt), xm, rm, ws[s], lnt, mid, before, after, side)
        deps = ()
        if s == n_seg - 1:
            output = lax.all_to_all(after_all(by_frames(res), mate), PLANE, 0, 0)
            deps = (output,)
            output = home(output)
        parts = plane_reduce(mate, keep, deps=deps)
        raw = kernel_grads(pad, hidden, ds, dtf, before, after, msum, osum, side, ws[s].shape,
                           deps=parts[:1] + ([output] if s == n_seg - 2 else []))
    last = lax.psum_scatter(raw, "z", scatter_dimension=0)

    da = sum(p.astype(F32) for p in parts) + skip_grad.astype(F32)
    home_now = home(lax.all_to_all(by_frames(da.astype(BF)), PLANE, 0, 0))
    output, frames_grad = as_frames(output), as_frames(home_now).astype(F32)

    def by_row(v):
        return v.reshape(high, 2, width).transpose(1, 0, 2)

    last = after_all(last, home_now)
    g = jnp.stack([by_row(v) for v in [last] + grads[::-1]], axis=1).reshape(n_rank, high, width)
    g = lax.all_to_all(g, PLANE, 0, 0)
    space_grad = lax.dot_general(g[:, :hc].reshape(hid, width), perm, (((0,), (0,)), ((), ())),
                                 preferred_element_type=F32)
    tg = g[:, hc : hc + lrows, :ch].reshape(n_rank, -1, q, ch)
    time_grad = tg.transpose(1, 0, 2, 3).reshape(-1, ch).astype(F32)
    sums = g[:, hc + lrows : hc + lrows + 4].astype(F32)

    def mid_own(v):
        return lax.dynamic_slice_in_dim(v[:, :hc], d_index * q, q, axis=1).reshape(1, hc)

    own = lax.dynamic_index_in_dim(sums, d_index, 0, keepdims=False)
    return (
        output,
        frames_grad,
        space_grad[None],
        time_grad[None],
        mid_own(sums[:, 0]),
        mid_own(sums[:, 1]),
        own[2:3, :cc],
        own[3:4, :cc],
    )


def from_behind(value, axis, steps):
    count = lax.axis_size(axis)
    leading, last = (max(0, -steps), min(count, count - steps))
    return lax.ppermute(value, axis, [(source, source + steps) for source in range(leading, last)])


def space_apply(current, kernel):
    frame_side = current.shape[1]
    padded = jnp.pad(current, ((0, 0), (1, 1), (1, 1), (0, 0)))
    stacked = jnp.concatenate(
        [
            padded[:, row_shift : row_shift + frame_side, col_shift : col_shift + frame_side, :]
            for row_shift in range(3)
            for col_shift in range(3)
        ],
        axis=-1,
    )
    return (
        stacked,
        jnp.einsum("fijc,co->fijo", stacked, kernel, preferred_element_type=jnp.float32),
    )


def space_back(gradient, kernel):
    frame_side = gradient.shape[1]
    channels = kernel.shape[0] // 9
    spread = jnp.einsum("fijo,co->fijc", gradient, kernel, preferred_element_type=jnp.float32)
    total = jnp.zeros((gradient.shape[0], frame_side + 2, frame_side + 2, channels), jnp.float32)
    for tap_index in range(9):
        row_shift = tap_index // 3
        col_shift = tap_index % 3
        piece_now = spread[..., tap_index * channels : (tap_index + 1) * channels]
        total = total + jnp.pad(
            piece_now, ((0, 0), (row_shift, 2 - row_shift), (col_shift, 2 - col_shift), (0, 0))
        )
    return total[:, 1 : frame_side + 1, 1 : frame_side + 1, :]


def time_apply(current, kernel, before_mask, after_mask):
    blanks = jnp.zeros_like(current[:1])
    earlier = jnp.concatenate([blanks, current[:-1]], axis=0) * before_mask[
        :, None, None, None
    ].astype(current.dtype)
    later = jnp.concatenate([current[1:], blanks], axis=0) * after_mask[:, None, None, None].astype(
        current.dtype
    )
    stacked = jnp.concatenate([earlier, current, later], axis=-1)
    return (
        stacked,
        jnp.einsum("fijc,co->fijo", stacked, kernel, preferred_element_type=jnp.float32),
    )


def time_back(gradient, kernel, before_mask, after_mask):
    channels = kernel.shape[0] // 3
    spread = jnp.einsum("fijo,co->fijc", gradient, kernel, preferred_element_type=jnp.float32)
    early_part = spread[..., :channels] * before_mask[:, None, None, None]
    late_part = spread[..., 2 * channels :] * after_mask[:, None, None, None]
    blanks = jnp.zeros_like(early_part[:1])
    moved_early = jnp.concatenate([early_part[1:], blanks], axis=0)
    moved_late = jnp.concatenate([blanks, late_part[:-1]], axis=0)
    return spread[..., channels : 2 * channels] + moved_early + moved_late


def moments(values, pixel_count):
    average = lax.psum(jnp.sum(values, axis=(0, 1, 2)), "dp") / pixel_count
    centered = values - average
    spread = lax.psum(jnp.sum(centered * centered, axis=(0, 1, 2)), "dp") / pixel_count
    return (average, lax.rsqrt(spread + eps))


def reduce_back(gradient, normed):
    return lax.psum(
        (jnp.sum(gradient, axis=(0, 1, 2)), jnp.sum(gradient * normed, axis=(0, 1, 2))), "dp"
    )


def silu_slope(values):
    sigmoid_now = jax.nn.sigmoid(values)
    return sigmoid_now * (1.0 + values * (1.0 - sigmoid_now))


def pick_slot(stack, slot_index):
    return lax.dynamic_index_in_dim(stack, slot_index, 0, keepdims=False)


def store_slot(stack, value, slot_index, usable):
    previous = pick_slot(stack, slot_index)
    return lax.dynamic_update_index_in_dim(stack, jnp.where(usable, value, previous), slot_index, 0)


def on_device_general(
    frames, cotangent, starts, space_kernel, time_kernel, mid_gain, mid_bias, out_gain, out_bias
):
    n_segment = lax.axis_size("segment")
    n_data = lax.axis_size("dp")
    segment_index = lax.axis_index("segment")
    odd_segment = segment_index % 2 == 1
    last_segment = segment_index == n_segment - 1
    first_segment = segment_index == 0
    frame_count = frames.shape[0]
    frame_side = frames.shape[1]
    channels = frames.shape[3]
    hidden_units = mid_gain.shape[1] * n_data
    pixel_count = n_data * frame_count * frame_side * frame_side
    turns = 2 * n_segment - 1
    block_shape = (n_segment,) + frames.shape
    all_frames, all_cot, all_starts = (
        lax.all_gather(frames, "segment", axis=0, tiled=True),
        lax.all_gather(cotangent, "segment", axis=0, tiled=True),
        lax.all_gather(starts.astype(jnp.bfloat16), "segment", axis=0, tiled=True),
    )
    frame_stack = all_frames.reshape(block_shape)
    cot_stack = all_cot.reshape(block_shape)
    clip_flags = all_starts.astype(jnp.float32).reshape(n_segment, frame_count)
    positions = jnp.arange(frame_count)
    before_mask = jnp.where((clip_flags > 0.5) | (positions == 0), 0.0, 1.0)
    following = jnp.concatenate([clip_flags[:, 1:], jnp.ones((n_segment, 1), jnp.float32)], axis=1)
    after_mask = jnp.where(following > 0.5, 0.0, 1.0)
    gathered = (
        lax.all_gather(space_kernel[0].astype(jnp.bfloat16), "dp", axis=0, tiled=True),
        lax.all_gather(time_kernel[0].astype(jnp.bfloat16), "dp", axis=0, tiled=True),
        lax.all_gather(mid_gain[0].astype(jnp.bfloat16), "dp", axis=0, tiled=True),
        lax.all_gather(mid_bias[0].astype(jnp.bfloat16), "dp", axis=0, tiled=True),
        lax.all_gather(out_gain[0].astype(jnp.bfloat16), "dp", axis=0, tiled=True),
        lax.all_gather(out_bias[0].astype(jnp.bfloat16), "dp", axis=0, tiled=True),
    )
    space_low, time_low = (gathered[0], gathered[1])
    mid_gain_now = gathered[2].astype(jnp.float32)
    mid_bias_now = gathered[3].astype(jnp.float32)
    out_gain_now = gathered[4].astype(jnp.float32)
    out_bias_now = gathered[5].astype(jnp.float32)
    incoming = jnp.zeros_like(frames)
    carried = jnp.zeros_like(frames)
    kept_input = jnp.zeros(block_shape, jnp.bfloat16)
    kept_skip = jnp.zeros(block_shape, jnp.bfloat16)
    kept_mid_mean = jnp.zeros((n_segment, hidden_units), jnp.float32)
    kept_mid_scale = jnp.zeros((n_segment, hidden_units), jnp.float32)
    kept_out_mean = jnp.zeros((n_segment, channels), jnp.float32)
    kept_out_scale = jnp.zeros((n_segment, channels), jnp.float32)
    results = jnp.zeros(block_shape, jnp.float32)
    for turn_index in range(turns):
        micro_index = turn_index - segment_index
        usable = (micro_index >= 0) & (micro_index < n_segment)
        slot_index = jnp.clip(micro_index, 0, n_segment - 1)
        current = jnp.where(first_segment, pick_slot(frame_stack, slot_index), incoming)
        skip_input = carried
        _, spatial = space_apply(current, space_low)
        mid_mean, mid_scale = moments(spatial, pixel_count)
        hidden_act = jax.nn.silu(
            (spatial - mid_mean) * mid_scale * mid_gain_now + mid_bias_now
        ).astype(jnp.bfloat16)
        _, temporal = time_apply(
            hidden_act,
            time_low,
            pick_slot(before_mask, slot_index),
            pick_slot(after_mask, slot_index),
        )
        out_mean, out_scale = moments(temporal, pixel_count)
        pre_act = (
            (temporal - out_mean) * out_scale * out_gain_now
            + out_bias_now
            + jnp.where(odd_segment, skip_input.astype(jnp.float32), 0.0)
        )
        result = jax.nn.silu(pre_act).astype(jnp.bfloat16)
        kept_input = store_slot(kept_input, current, slot_index, usable)
        kept_skip = store_slot(kept_skip, skip_input, slot_index, usable)
        kept_mid_mean = store_slot(kept_mid_mean, mid_mean, slot_index, usable)
        kept_mid_scale = store_slot(kept_mid_scale, mid_scale, slot_index, usable)
        kept_out_mean = store_slot(kept_out_mean, out_mean, slot_index, usable)
        kept_out_scale = store_slot(kept_out_scale, out_scale, slot_index, usable)
        results = store_slot(results, result.astype(jnp.float32), slot_index, usable)
        if turn_index < turns - 1:
            incoming, carried = from_behind(
                (result, jnp.where(odd_segment, result, current)), "segment", 1
            )
    gathered = (
        lax.all_gather(space_kernel[0].astype(jnp.bfloat16), "dp", axis=0, tiled=True),
        lax.all_gather(time_kernel[0].astype(jnp.bfloat16), "dp", axis=0, tiled=True),
        lax.all_gather(mid_gain[0].astype(jnp.bfloat16), "dp", axis=0, tiled=True),
        lax.all_gather(mid_bias[0].astype(jnp.bfloat16), "dp", axis=0, tiled=True),
        lax.all_gather(out_gain[0].astype(jnp.bfloat16), "dp", axis=0, tiled=True),
        lax.all_gather(out_bias[0].astype(jnp.bfloat16), "dp", axis=0, tiled=True),
    )
    space_low, time_low = (gathered[0], gathered[1])
    mid_gain_now = gathered[2].astype(jnp.float32)
    mid_bias_now = gathered[3].astype(jnp.float32)
    out_gain_now = gathered[4].astype(jnp.float32)
    out_bias_now = gathered[5].astype(jnp.float32)
    grad_input = jnp.zeros_like(frames)
    grad_skip = jnp.zeros_like(frames)
    space_acc = jnp.zeros(space_low.shape, jnp.float32)
    time_acc = jnp.zeros(time_low.shape, jnp.float32)
    mid_gain_acc = jnp.zeros((hidden_units,), jnp.float32)
    mid_bias_acc = jnp.zeros((hidden_units,), jnp.float32)
    out_gain_acc = jnp.zeros((channels,), jnp.float32)
    out_bias_acc = jnp.zeros((channels,), jnp.float32)
    input_grads = jnp.zeros(block_shape, jnp.float32)
    for turn_index in range(turns):
        micro_index = n_segment - 1 - (turn_index - (n_segment - 1 - segment_index))
        usable = (micro_index >= 0) & (micro_index < n_segment)
        usable_weight = usable.astype(jnp.float32)
        slot_index = jnp.clip(micro_index, 0, n_segment - 1)
        current = pick_slot(kept_input, slot_index)
        skip_input = pick_slot(kept_skip, slot_index)
        before_now = pick_slot(before_mask, slot_index)
        after_now = pick_slot(after_mask, slot_index)
        space_taps, spatial = space_apply(current, space_low)
        mid_normed = (spatial - pick_slot(kept_mid_mean, slot_index)) * pick_slot(
            kept_mid_scale, slot_index
        )
        mid_pre = mid_normed * mid_gain_now + mid_bias_now
        hidden_act = jax.nn.silu(mid_pre).astype(jnp.bfloat16)
        time_taps, temporal = time_apply(hidden_act, time_low, before_now, after_now)
        out_scale = pick_slot(kept_out_scale, slot_index)
        out_normed = (temporal - pick_slot(kept_out_mean, slot_index)) * out_scale
        pre_act = (
            out_normed * out_gain_now
            + out_bias_now
            + jnp.where(odd_segment, skip_input.astype(jnp.float32), 0.0)
        )
        grad_result = jnp.where(
            last_segment,
            pick_slot(cot_stack, slot_index).astype(jnp.float32),
            grad_input.astype(jnp.float32)
            + jnp.where(odd_segment, grad_skip.astype(jnp.float32), 0.0),
        )
        grad_pre = grad_result * silu_slope(pre_act)
        out_bias_sum, out_gain_sum = reduce_back(grad_pre, out_normed)
        grad_temporal = (
            out_gain_now
            * out_scale
            * (grad_pre - out_bias_sum / pixel_count - out_normed * out_gain_sum / pixel_count)
        ).astype(jnp.bfloat16)
        time_acc = time_acc + usable_weight * jnp.einsum(
            "fijc,fijo->co", time_taps, grad_temporal, preferred_element_type=jnp.float32
        )
        grad_hidden = time_back(grad_temporal, time_low, before_now, after_now)
        grad_mid = grad_hidden * silu_slope(mid_pre)
        mid_bias_sum, mid_gain_sum = reduce_back(grad_mid, mid_normed)
        mid_scale = pick_slot(kept_mid_scale, slot_index)
        grad_spatial = (
            mid_gain_now
            * mid_scale
            * (grad_mid - mid_bias_sum / pixel_count - mid_normed * mid_gain_sum / pixel_count)
        ).astype(jnp.bfloat16)
        space_acc = space_acc + usable_weight * jnp.einsum(
            "fijc,fijo->co", space_taps, grad_spatial, preferred_element_type=jnp.float32
        )
        grad_current = space_back(grad_spatial, space_low)
        mid_gain_acc = mid_gain_acc + usable_weight * mid_gain_sum
        mid_bias_acc = mid_bias_acc + usable_weight * mid_bias_sum
        out_gain_acc = out_gain_acc + usable_weight * out_gain_sum
        out_bias_acc = out_bias_acc + usable_weight * out_bias_sum
        input_grads = store_slot(
            input_grads, grad_current + grad_skip.astype(jnp.float32), slot_index, usable
        )
        if turn_index < turns - 1:
            grad_input, grad_skip = from_behind(
                (
                    grad_current.astype(jnp.bfloat16),
                    jnp.where(odd_segment, grad_pre.astype(jnp.bfloat16), grad_skip),
                ),
                "segment",
                -1,
            )
    space_grad, time_grad = (
        lax.psum_scatter(space_acc, "dp", scatter_dimension=0, tiled=True),
        lax.psum_scatter(time_acc, "dp", scatter_dimension=0, tiled=True),
    )
    data_index = lax.axis_index("dp")

    def own_share(full_vector):
        share = full_vector.shape[0] // n_data
        return lax.dynamic_slice_in_dim(full_vector, data_index * share, share)[None]

    flat_shape = (n_segment * frame_count,) + frames.shape[1:]
    arrived_out, arrived_grads = (
        lax.all_to_all(
            results.reshape(flat_shape).astype(jnp.bfloat16),
            "segment",
            split_axis=0,
            concat_axis=0,
            tiled=True,
        ).astype(jnp.float32),
        lax.all_to_all(
            input_grads.reshape(flat_shape).astype(jnp.bfloat16),
            "segment",
            split_axis=0,
            concat_axis=0,
            tiled=True,
        ).astype(jnp.float32),
    )
    output = arrived_out[(n_segment - 1) * frame_count :].astype(jnp.bfloat16)
    frames_grad = arrived_grads[:frame_count]
    return (
        output,
        frames_grad,
        space_grad[None],
        time_grad[None],
        own_share(mid_gain_acc),
        own_share(mid_bias_acc),
        own_share(out_gain_acc),
        own_share(out_bias_acc),
    )


def general(mesh):
    return jax.shard_map(
        on_device_general,
        mesh=mesh,
        in_specs=(
            P(("dp", "segment"), None, None, None),
            P(("dp", "segment"), None, None, None),
            P(("dp", "segment")),
            P("segment", "dp", None),
            P("segment", "dp", None),
            P("segment", "dp"),
            P("segment", "dp"),
            P("segment", "dp"),
            P("segment", "dp"),
        ),
        out_specs=(
            P(("dp", "segment"), None, None, None),
            P(("dp", "segment"), None, None, None),
            P("segment", "dp", None),
            P("segment", "dp", None),
            P("segment", "dp"),
            P("segment", "dp"),
            P("segment", "dp"),
            P("segment", "dp"),
        ),
        check_vma=False,
    )


def solution(mesh):
    if mesh.shape["dp"] != 8 or mesh.shape["segment"] != 4:
        return general(mesh)
    n_dp, n_seg = mesh.shape["dp"], mesh.shape["segment"]
    fine = Mesh(mesh.devices.reshape(n_dp // 2, 2, 2, n_seg // 2), EVERY)
    dp, seg = ("z", "y"), ("x", "c")
    return jax.shard_map(
        on_device,
        mesh=fine,
        in_specs=(
            P(EVERY, None, None, None),
            P(EVERY, None, None, None),
            P(EVERY),
            P(seg, dp, None),
            P(seg, dp, None),
            P(seg, dp),
            P(seg, dp),
            P(seg, dp),
            P(seg, dp),
        ),
        out_specs=(
            P(EVERY, None, None, None),
            P(EVERY, None, None, None),
            P(seg, dp, None),
            P(seg, dp, None),
            P(seg, dp),
            P(seg, dp),
            P(seg, dp),
            P(seg, dp),
        ),
        check_vma=False,
    )
```

```python
import functools

import jax
import jax.numpy as jnp
from jax import lax
from jax.experimental import pallas as pl
from jax.experimental.pallas import tpu as pltpu
from jax.sharding import Mesh, PartitionSpec as P

eps = 1e-05
PLANE = ("y", "x", "c")
EVERY = ("z", "y", "x", "c")
BF = jnp.bfloat16
F32 = jnp.float32


def nt(a, b):
    return lax.dot_general(a, b, (((1,), (1,)), ((), ())), preferred_element_type=F32)


def nn(a, b):
    return lax.dot_general(a, b, (((1,), (0,)), ((), ())), preferred_element_type=F32)


VMEM_CAP = 56 * 1024 * 1024
ANY = pl.BlockSpec(memory_space=pl.ANY)


def call(body, outs, scratch, flops, *args, deps=(), far=(), far_outs=()):
    moved = sum(a.size * a.dtype.itemsize for a in args) + sum(
        o.size * o.dtype.itemsize for o in outs
    )
    n = len(deps)

    def spec(a):
        return pl.BlockSpec(memory_space=pltpu.SMEM if a.dtype == jnp.int32 else pltpu.VMEM)

    return pl.pallas_call(
        lambda *refs: body(*refs[n:]),
        out_shape=outs,
        in_specs=[ANY] * n + [ANY if i in far else spec(a) for i, a in enumerate(args)],
        out_specs=[ANY if i in far_outs else spec(o) for i, o in enumerate(outs)],
        scratch_shapes=scratch,
        compiler_params=pltpu.CompilerParams(vmem_limit_bytes=VMEM_CAP),
        cost_estimate=pl.CostEstimate(flops=flops, bytes_accessed=moved, transcendentals=0),
    )(*deps, *args)


def chunk(i, size):
    return pl.ds(pl.multiple_of(i * size, 16), size)


def clear_borders(pad_ref, side, plane, nf):
    zrow = jnp.zeros(pad_ref.shape[1:], BF)
    pad_ref[0] = zrow
    pad_ref[side + 1] = zrow
    zcol = jnp.zeros((nf, pad_ref.shape[2]), BF)
    for i in range(side):
        pad_ref[i + 1, 0:nf] = zcol
        pad_ref[i + 1, nf + plane : 2 * nf + plane] = zcol


def by_rank(slices, rank):
    odd = lax.rem(rank, 2) == 1
    for p in range(len(slices) // 2):
        a, b = slices[2 * p], slices[2 * p + 1]
        yield lax.bitwise_xor(rank // 2, p), odd, a, b


def halves(odd, own, mate):
    low = lax.broadcasted_iota(jnp.int32, own.shape, 1) < 64
    own, mate = own.astype(F32), mate.astype(F32)
    a, b = jnp.where(odd, mate, own), jnp.where(odd, own, mate)
    top = jnp.where(low, a, pltpu.roll(b, 64, 1))
    bottom = jnp.where(low, pltpu.roll(a, 64, 1), b)
    return top, bottom


def store_packed(rank, mate_ref, keep_ref, part, k, step, low):
    rows_now = chunk(k, step)
    odd = lax.rem(rank, 2) == 1
    for q in range(keep_ref.shape[0]):
        x = part[:step, 128 * q : 128 * q + 128]
        y = part[step:, 128 * q : 128 * q + 128]
        even_slice = jnp.where(low, x, pltpu.roll(y, 64, 1))
        odd_slice = jnp.where(low, pltpu.roll(x, 64, 1), y)
        p = lax.bitwise_xor(rank // 2, q)
        keep_ref[p, rows_now, :] = jnp.where(odd, odd_slice, even_slice).astype(BF)
        mate_ref[p, rows_now, :] = jnp.where(odd, even_slice, odd_slice).astype(BF)


def fetch_kernels(w_ref, ktm_ref, lw_ref, sems):
    nz, _, width = w_ref.shape
    hc = ktm_ref.shape[0]
    copies = []
    for z in range(nz):
        copies.append(pltpu.make_async_copy(
            w_ref.at[z, pl.ds(0, hc)], ktm_ref.at[:, pl.ds(z * width, width)], sems.at[2 * z]))
        copies.append(pltpu.make_async_copy(
            w_ref.at[z, pl.ds(hc, lw_ref.shape[1])], lw_ref.at[z], sems.at[2 * z + 1]))
    for copy in copies:
        copy.start()
    return copies


def join_temporal(lw_ref, lf_ref, ltm_ref):
    ch = ltm_ref.shape[1]
    width = lw_ref.shape[2] // 2
    count = 2 * lw_ref.shape[0]
    size = ltm_ref.shape[0] // count
    for z in range(lw_ref.shape[0]):
        first = lw_ref[z, :, 0:ch].astype(F32)
        off = width % 128
        second = lw_ref[z, :, width - off : width - off + ch + 128].astype(F32)
        second = pltpu.roll(second, ch + 128 - off, 1)[:, 0:ch]
        for b, block in ((2 * z, first), (2 * z + 1, second)):
            lf_ref[b * size : b * size + block.shape[0], :] = block
    ltm_ref[...] = lf_ref[0 : ltm_ref.shape[0], :].astype(BF)


def prepare_body(w_ref, kn_out, l_out, lt_out, rows_out, ktm_ref, lw_ref, lf_ref, sems):
    hc, ch = ktm_ref.shape[0], l_out.shape[1]
    for copy in fetch_kernels(w_ref, ktm_ref, lw_ref, sems):
        copy.wait()
    for t in range(9):
        kn_out[t] = ktm_ref[:, t * ch : (t + 1) * ch].astype(F32).T.astype(BF)
    join_temporal(lw_ref, lf_ref, l_out)
    rows_out[...] = lw_ref[:, lw_ref.shape[1] - rows_out.shape[1] :, :]
    for t in range(3):
        lt_out[t] = lf_ref[t * hc : (t + 1) * hc].T.astype(BF)


def prepare(w, hc, ch, deps=()):
    outs = [
        jax.ShapeDtypeStruct((9, ch, hc), BF),
        jax.ShapeDtypeStruct((3 * hc, ch), BF),
        jax.ShapeDtypeStruct((3, ch, hc), BF),
        jax.ShapeDtypeStruct((w.shape[0], 16, w.shape[2]), BF),
    ]
    tall = w.shape[1] - hc
    scratch = [
        pltpu.VMEM((hc, 9 * ch), BF),
        pltpu.VMEM((w.shape[0], tall, w.shape[2]), BF),
        pltpu.VMEM((3 * hc + tall, ch), F32),
        pltpu.SemaphoreType.DMA((2 * w.shape[0],)),
    ]
    return call(prepare_body, outs, scratch, 2 * w.size * 512, w, deps=deps, far=(0,))


def conv_body(side, first, rank_ref, *refs):
    n = 1 if first else 8
    slices = refs[:n]
    (kn_in, ltm_ref, vec_ref, before_ref, after_ref,
     pad_out, hid_out, xhat_out, rs_ref, mate_ref, keep_ref,
     pad_ref, hid_ref, xhat_ref, sp_ref, kn_ref, sems) = refs[n:]
    rank = rank_ref[0]
    kn_copy = pltpu.make_async_copy(kn_in, kn_ref, sems.at[0])
    kn_copy.start()
    ch, hc = pad_ref.shape[2], hid_ref.shape[1]
    rows = hid_ref.shape[0]
    plane = rows // side
    nf = plane // side
    step = plane // 2
    clear_borders(pad_ref, side, plane, nf)
    if first:
        for i in range(side):
            pad_ref[i + 1, nf : nf + plane] = slices[0][i * plane : (i + 1) * plane]
    else:
        def place(k, carry):
            for q, odd, a_ref, b_ref in by_rank(slices, rank):
                top, bottom = halves(odd, a_ref[chunk(k, step), :], b_ref[chunk(k, step), :])
                lanes = pl.ds(pl.multiple_of(128 * q, 128), 128)
                for piece, kk in ((top, k), (bottom, k + side)):
                    at = nf + lax.rem(kk, 2) * step
                    pad_ref[1 + kk // 2, pl.ds(pl.multiple_of(at, 16), step), lanes] = piece.astype(BF)
            return carry

        lax.fori_loop(0, side, place, 0, unroll=True)
    pad_copy = pltpu.make_async_copy(pad_ref, pad_out, sems.at[1])
    pad_copy.start()
    kn_copy.wait()

    def conv(i, total):
        acc = jnp.zeros((plane, hc), F32)
        for t in range(9):
            r, c = t // 3, t % 3
            acc += nn(pad_ref[i + r, c * nf : c * nf + plane, :], kn_ref[t])
        sp_ref[i] = acc
        return total + jnp.sum(acc, axis=0, keepdims=True)

    mean = lax.fori_loop(0, side, conv, jnp.zeros((1, hc), F32), unroll=True) / rows

    def square(i, total):
        cen = sp_ref[i] - mean
        return total + jnp.sum(cen * cen, axis=0, keepdims=True)

    var = lax.fori_loop(0, side, square, jnp.zeros((1, hc), F32), unroll=True) / rows
    rs = lax.rsqrt(var + eps)
    rs_ref[...] = rs
    gain, bias = vec_ref[0:1, :], vec_ref[1:2, :]

    def act(i, carry):
        xhat = (sp_ref[i] - mean) * rs
        xhat_ref[i] = xhat
        v = xhat * gain + bias
        v = v * jax.nn.sigmoid(v)
        sp_ref[i] = v
        hid_ref[chunk(i, plane), :] = v.astype(BF)
        return carry

    lax.fori_loop(0, side, act, 0, unroll=True)
    late = [
        pltpu.make_async_copy(hid_ref, hid_out, sems.at[2]),
        pltpu.make_async_copy(xhat_ref, xhat_out, sems.at[3]),
    ]
    for copy in late:
        copy.start()
    low = lax.broadcasted_iota(jnp.int32, (step, 128), 1) < 64

    def temporal(k, carry):
        pieces = []
        for kk in (k, k + side):
            par = lax.rem(kk, 2)
            h = sp_ref[kk // 2, pl.ds(pl.multiple_of(par * step, 8), step), :]
            at = pl.multiple_of(par * (step % nf), 8)
            pieces.append((
                (pltpu.roll(h, 1, 0) * before_ref[pl.ds(at, step), :]).astype(BF),
                h.astype(BF),
                (pltpu.roll(h, step - 1, 0) * after_ref[pl.ds(at, step), :]).astype(BF),
            ))
        part = sum(
            nn(jnp.concatenate([x, y], axis=0), ltm_ref[t * hc : (t + 1) * hc])
            for t, (x, y) in enumerate(zip(*pieces))
        )
        store_packed(rank, mate_ref, keep_ref, part, k, step, low)
        return carry

    lax.fori_loop(0, side, temporal, 0, unroll=True)
    for copy in [pad_copy] + late:
        copy.wait()


def conv_forward(rank, g, kn, lt, vec, before, after, side, pixels, ch, deps=()):
    hc = vec.shape[1]
    plane = pixels // side
    nf = plane // side
    n = len(g)
    shapes = [
        ((side + 2, plane + 2 * nf, ch), BF),
        ((pixels, hc), BF),
        ((side, plane, hc), F32),
    ]
    outs = [jax.ShapeDtypeStruct(*s) for s in shapes] + [
        jax.ShapeDtypeStruct((1, hc), F32),
        jax.ShapeDtypeStruct((4, pixels // 2, 128), BF),
        jax.ShapeDtypeStruct((4, pixels // 2, 128), BF),
    ]
    scratch = [pltpu.VMEM(*s) for s in shapes] + [
        pltpu.VMEM((side, plane, hc), F32),
        pltpu.VMEM((9, ch, hc), BF),
        pltpu.SemaphoreType.DMA((4,)),
    ]
    flops = 2 * pixels * hc * 12 * ch
    return call(functools.partial(conv_body, side, n == 1), outs, scratch, flops,
                rank, *g, kn, lt, vec, before, after,
                deps=deps, far=(n + 1,), far_outs=(0, 1, 2))


def fold(v):
    return v + pltpu.roll(v, 64, 1)


def total_of(refs):
    t = refs[0][...].astype(F32)
    for ref in refs[1:]:
        t += ref[...].astype(F32)
    return t


def pair_sum_body(keep_ref, mate_ref, *out_refs):
    for p, ref in enumerate(out_refs):
        ref[...] = (keep_ref[p].astype(F32) + mate_ref[p].astype(F32)).astype(ref.dtype)


def pair_sum(keep, arrived, deps=()):
    shape = keep.shape[1:]
    outs = [jax.ShapeDtypeStruct(shape, BF)] * keep.shape[0]
    return call(pair_sum_body, outs, [], keep.size, keep, arrived, deps=deps)


def out_norm_body(n, has_skip, *refs):
    parts, refs = refs[:n], refs[n:]
    if has_skip:
        vec_ref, skip_ref, xhat_ref, rs_ref, pre_ref, res_ref = refs
    else:
        vec_ref, xhat_ref, rs_ref, pre_ref, res_ref = refs
    t = total_of(parts)
    pixels = 2 * t.shape[0]
    mean = fold(jnp.sum(t, axis=0, keepdims=True)) / pixels
    cen = t - mean
    rs = lax.rsqrt(fold(jnp.sum(cen * cen, axis=0, keepdims=True)) / pixels + eps)
    xhat = cen * rs
    pre = xhat * vec_ref[0:1, :] + vec_ref[1:2, :]
    if has_skip:
        pre = pre + skip_ref[...].astype(F32)
    xhat_ref[...] = xhat
    rs_ref[...] = rs
    pre_ref[...] = pre
    res_ref[...] = (pre * jax.nn.sigmoid(pre)).astype(BF)


def out_norm(parts, vec, skip, deps=()):
    half = parts[0].shape[0]
    outs = [
        jax.ShapeDtypeStruct((half, 128), F32),
        jax.ShapeDtypeStruct((1, 128), F32),
        jax.ShapeDtypeStruct((half, 128), F32),
        jax.ShapeDtypeStruct((half, 128), BF),
    ]
    args = (*parts, vec) + (() if skip is None else (skip,))
    body = functools.partial(out_norm_body, len(parts), skip is not None)
    return call(body, outs, [], half * 128 * 10, *args, deps=deps)


def out_back_body(n, *refs):
    parts, (pre_ref, xhat_ref, rs_ref, vec_ref, dpre_ref, dt_ref, sums_ref) = refs[:n], refs[n:]
    g = total_of(parts)
    pre, xhat = pre_ref[...], xhat_ref[...]
    sig = jax.nn.sigmoid(pre)
    dpre = g * (sig * (1.0 + pre * (1.0 - sig)))
    pixels = 2 * pre.shape[0]
    sb = fold(jnp.sum(dpre, axis=0, keepdims=True))
    sg = fold(jnp.sum(dpre * xhat, axis=0, keepdims=True))
    dpre_ref[...] = dpre.astype(BF)
    scale = vec_ref[0:1, :] * rs_ref[...]
    dt_ref[...] = (scale * (dpre - sb / pixels - xhat * (sg / pixels))).astype(BF)
    sums_ref[0:1, :] = sg
    sums_ref[1:2, :] = sb


def out_back(parts, pre, xhat, rs, vec, deps=()):
    half = pre.shape[0]
    outs = [
        jax.ShapeDtypeStruct((half, 128), BF),
        jax.ShapeDtypeStruct((half, 128), BF),
        jax.ShapeDtypeStruct((2, 128), F32),
    ]
    args = (*parts, pre, xhat, rs, vec)
    return call(functools.partial(out_back_body, len(parts)), outs, [], half * 1280, *args, deps=deps)


def conv_back_body(side, rank_ref, *refs):
    slices, (xhat_in, rs_ref, w_ref, lnt_ref, vec_ref, before_ref, after_ref,
             dt_out, ds_out, sums_ref, mate_ref, keep_ref,
             dt_ref, ds_ref, xhat_ref, dy_ref, pad_ref, ktm_ref, sems) = refs[:8], refs[8:]
    half = slices[0].shape[0]
    rank = rank_ref[0]
    nz, _, width = w_ref.shape
    rows = 2 * half
    plane = rows // side
    nf = plane // side
    step = plane // 2
    hc = ds_ref.shape[1]
    ch = dt_ref.shape[1]
    fetched = [
        pltpu.make_async_copy(
            w_ref.at[z, pl.ds(0, hc)], ktm_ref.at[:, pl.ds(z * width, width)], sems.at[z])
        for z in range(nz)
    ]
    xhat_copy = pltpu.make_async_copy(xhat_in, xhat_ref, sems.at[nz])
    for copy in fetched + [xhat_copy]:
        copy.start()
    clear_borders(pad_ref, side, plane, nf)

    def place(k, carry):
        for q, odd, a_ref, b_ref in by_rank(slices, rank):
            top, bottom = halves(odd, a_ref[chunk(k, step), :], b_ref[chunk(k, step), :])
            lanes = pl.ds(pl.multiple_of(128 * q, 128), 128)
            dt_ref[chunk(k, step), lanes] = top.astype(BF)
            dt_ref[pl.ds(pl.multiple_of(half + k * step, 16), step), lanes] = bottom.astype(BF)
        return carry

    lax.fori_loop(0, side, place, 0, unroll=True)
    dt_copy = pltpu.make_async_copy(dt_ref, dt_out, sems.at[nz + 1])
    dt_copy.start()
    xhat_copy.wait()
    gain, bias = vec_ref[0:1, :], vec_ref[1:2, :]

    def hidden_grad(i, sums):
        dt = dt_ref[chunk(i, plane), :]
        early = nn(dt, lnt_ref[0]) * before_ref[0:plane, :]
        late = nn(dt, lnt_ref[2]) * after_ref[0:plane, :]
        dh = nn(dt, lnt_ref[1]) + pltpu.roll(early, plane - 1, 0) + pltpu.roll(late, 1, 0)
        xhat = xhat_ref[i]
        v = xhat * gain + bias
        sig = jax.nn.sigmoid(v)
        dy = dh * (sig * (1.0 + v * (1.0 - sig)))
        dy_ref[i] = dy
        return (
            sums[0] + jnp.sum(dy * xhat, axis=0, keepdims=True),
            sums[1] + jnp.sum(dy, axis=0, keepdims=True),
        )

    zero = jnp.zeros((1, hc), F32)
    sg, sb = lax.fori_loop(0, side, hidden_grad, (zero, zero), unroll=True)
    sums_ref[0:1, :] = sg
    sums_ref[1:2, :] = sb
    scale = gain * rs_ref[...]

    def spatial_grad(i, carry):
        ds = (scale * (dy_ref[i] - sb / rows - xhat_ref[i] * (sg / rows))).astype(BF)
        pad_ref[i + 1, nf : nf + plane] = ds
        ds_ref[chunk(i, plane), :] = ds
        return carry

    lax.fori_loop(0, side, spatial_grad, 0, unroll=True)
    ds_copy = pltpu.make_async_copy(ds_ref, ds_out, sems.at[nz + 2])
    ds_copy.start()
    for copy in fetched:
        copy.wait()
    low = lax.broadcasted_iota(jnp.int32, (step, 128), 1) < 64

    def back(k, carry):
        acc = jnp.zeros((2 * step, ch), F32)
        for t in range(9):
            r, c = 2 - t // 3, 2 - t % 3
            pieces = []
            for kk in (k, k + side):
                at = c * nf + lax.rem(kk, 2) * step
                pieces.append(pad_ref[kk // 2 + r, pl.ds(pl.multiple_of(at, 16), step), :])
            acc += nn(jnp.concatenate(pieces, axis=0), ktm_ref[:, t * ch : (t + 1) * ch])
        store_packed(rank, mate_ref, keep_ref, acc, k, step, low)
        return carry

    lax.fori_loop(0, side, back, 0, unroll=True)
    dt_copy.wait()
    ds_copy.wait()


def conv_back(rank, g, xhat, rs, w, lnt, vec, before, after, side, deps=()):
    half = g[0].shape[0]
    hc = vec.shape[1]
    ch = len(g) * 64
    pixels = 2 * half
    plane = pixels // side
    nf = plane // side
    outs = [
        jax.ShapeDtypeStruct((pixels, ch), BF),
        jax.ShapeDtypeStruct((pixels, hc), BF),
        jax.ShapeDtypeStruct((2, hc), F32),
        jax.ShapeDtypeStruct((4, half, 128), BF),
        jax.ShapeDtypeStruct((4, half, 128), BF),
    ]
    scratch = [
        pltpu.VMEM((pixels, ch), BF),
        pltpu.VMEM((pixels, hc), BF),
        pltpu.VMEM((side, plane, hc), F32),
        pltpu.VMEM((side, plane, hc), F32),
        pltpu.VMEM((side + 2, plane + 2 * nf, hc), BF),
        pltpu.VMEM((hc, 9 * ch), BF),
        pltpu.SemaphoreType.DMA((w.shape[0] + 3,)),
    ]
    flops = 2 * pixels * hc * 12 * ch
    return call(functools.partial(conv_back_body, side), outs, scratch, flops,
                rank, *g, xhat, rs, w, lnt, vec, before, after,
                deps=deps, far=(9, 11), far_outs=(0, 1))


def grads_body(side, pad_ref, hid_ref, ds_ref, dt_ref, before_ref, after_ref, mid_ref, out_ref,
               sg_ref, dst_ref, taps_ref, tg_ref, vec_ref):
    ch = pad_ref.shape[2]
    hc = hid_ref.shape[1]
    plane = hid_ref.shape[0] // side
    nf = plane // side
    for i in (0, 1, side + 2, side + 3):
        dst_ref[i] = jnp.zeros(dst_ref.shape[1:], BF)
    for i in range(side):
        at = slice(i * plane, (i + 1) * plane)
        h = hid_ref[at, :].astype(F32)
        taps_ref[i, 0:hc] = (pltpu.roll(h, 1, 0) * before_ref[0:plane, :]).T.astype(BF)
        taps_ref[i, hc : 2 * hc] = h.T.astype(BF)
        taps_ref[i, 2 * hc : 3 * hc] = (pltpu.roll(h, plane - 1, 0) * after_ref[0:plane, :]).T.astype(BF)
        dst_ref[i + 2] = ds_ref[at, :].astype(F32).T.astype(BF)
    tg_ref[0 : 3 * hc, :] = sum(
        nn(taps_ref[i], dt_ref[i * plane : (i + 1) * plane, :]) for i in range(side)
    )
    tg_ref[3 * hc :, :] = jnp.zeros((tg_ref.shape[0] - 3 * hc, ch), F32)
    nz, _, width = sg_ref.shape
    size = 3 * hc // (2 * nz)
    vec_ref[...] = jnp.zeros(vec_ref.shape, F32)
    vec_ref[size : size + 2, 0:hc] = mid_ref[...]
    vec_ref[size + 2 : size + 4, 0:128] = out_ref[...]
    tall = vec_ref.shape[0]
    inside = lax.broadcasted_iota(jnp.int32, (tall, ch), 0) < size
    off = (width // 2) % 128
    for z in range(nz):
        first, second = [
            jnp.where(inside, tg_ref[b * size : b * size + tall, :], vec_ref[...])
            for b in (2 * z, 2 * z + 1)
        ]
        start = width // 2 - off
        sg_ref[z, hc : hc + tall, 0:ch] = first.astype(BF)
        second = pltpu.roll(jnp.concatenate([second, jnp.zeros((tall, 128), F32)], axis=1), off, 1)
        sg_ref[z, hc : hc + tall, start : start + ch + 128] = second.astype(BF)
    for c in range(3):
        acc = sum(
            nn(dst_ref[i : i + 3].reshape(3 * hc, plane), pad_ref[i, c * nf : c * nf + plane, :])
            for i in range(1, side + 1)
        )
        for r in range(3):
            first = (3 * r + c) * ch
            end = first + ch
            at = (2 - r) * hc
            done = 0
            while first < end:
                z = first // width
                last = min(end, (z + 1) * width)
                sg_ref[z, 0:hc, first - z * width : last - z * width] = (
                    acc[at : at + hc, done : done + last - first].astype(BF)
                )
                done += last - first
                first = last


def kernel_grads(pad, hidden, ds, dt, before, after, mid, out, side, shape, deps=()):
    pixels, hc = hidden.shape
    ch = dt.shape[1]
    plane = pixels // side
    outs = [jax.ShapeDtypeStruct(shape, BF)]
    tall = shape[1] - hc
    scratch = [
        pltpu.VMEM((side + 4, hc, plane), BF),
        pltpu.VMEM((side, 3 * hc, plane), BF),
        pltpu.VMEM((3 * hc + tall, ch), F32),
        pltpu.VMEM((tall, ch), F32),
    ]
    flops = 2 * pixels * hc * 12 * ch
    return call(functools.partial(grads_body, side), outs, scratch, flops,
                pad, hidden, ds, dt, before, after, mid, out, deps=deps)[0]


def copy_after_body(v_ref, out_ref):
    out_ref[...] = v_ref[...]


def after_all(v, *deps):
    return call(copy_after_body, [jax.ShapeDtypeStruct(v.shape, v.dtype)], [], v.size, v, deps=deps)[0]


def pack_kernels_body(kt_ref, lt_ref, vec_ref, out_ref, low_ref):
    ranks, _, width = out_ref.shape
    hc = kt_ref.shape[0] // ranks
    blocks = lt_ref.shape[0] // hc
    q = hc // ranks
    low_ref[...] = jnp.zeros(low_ref.shape, F32)
    for r in range(ranks):
        out_ref[r, 0:hc, :] = kt_ref[r * hc : (r + 1) * hc, :]
        for b in range(blocks):
            low_ref[r, b * q : (b + 1) * q, 0 : lt_ref.shape[1]] = (
                lt_ref[b * hc + r * q : b * hc + (r + 1) * q, :]
            )
        low_ref[r, blocks * q : blocks * q + 1, :] = vec_ref[...]
        out_ref[r, hc:, :] = low_ref[r].astype(BF)


def pack_kernels(kt, lt, vec, ranks, tall, deps):
    width = kt.shape[1]
    outs = [jax.ShapeDtypeStruct((ranks, kt.shape[0] // ranks + tall, width), BF)]
    scratch = [pltpu.VMEM((ranks, tall, width), F32)]
    return call(pack_kernels_body, outs, scratch, kt.size * 8, kt, lt, vec, deps=deps)[0]


def call(body, outs, scratch, flops, *args, deps=(), far=(), far_outs=()):
    moved = sum(a.size * a.dtype.itemsize for a in args) + sum(
        o.size * o.dtype.itemsize for o in outs
    )
    n = len(deps)

    def spec(a):
        return pl.BlockSpec(memory_space=pltpu.SMEM if a.dtype == jnp.int32 else pltpu.VMEM)

    return pl.pallas_call(
        lambda *refs: body(*refs[n:]),
        out_shape=outs,
        in_specs=[ANY] * n + [ANY if i in far else spec(a) for i, a in enumerate(args)],
        out_specs=[ANY if i in far_outs else spec(o) for i, o in enumerate(outs)],
        scratch_shapes=scratch,
        compiler_params=pltpu.CompilerParams(vmem_limit_bytes=VMEM_CAP),
        cost_estimate=pl.CostEstimate(flops=flops, bytes_accessed=moved, transcendentals=0),
    )(*deps, *args)


def chunk(i, size):
    return pl.ds(pl.multiple_of(i * size, 16), size)


def clear_borders(pad_ref, side, plane, nf):
    zrow = jnp.zeros(pad_ref.shape[1:], BF)
    pad_ref[0] = zrow
    pad_ref[side + 1] = zrow
    zcol = jnp.zeros((nf, pad_ref.shape[2]), BF)
    for i in range(side):
        pad_ref[i + 1, 0:nf] = zcol
        pad_ref[i + 1, nf + plane : 2 * nf + plane] = zcol


def by_rank(slices, rank):
    odd = lax.rem(rank, 2) == 1
    for p in range(len(slices) // 2):
        a, b = slices[2 * p], slices[2 * p + 1]
        yield lax.bitwise_xor(rank // 2, p), odd, a, b


def halves(odd, own, mate):
    low = lax.broadcasted_iota(jnp.int32, own.shape, 1) < 64
    own, mate = own.astype(F32), mate.astype(F32)
    a, b = jnp.where(odd, mate, own), jnp.where(odd, own, mate)
    top = jnp.where(low, a, pltpu.roll(b, 64, 1))
    bottom = jnp.where(low, pltpu.roll(a, 64, 1), b)
    return top, bottom


def store_packed(rank, mate_ref, keep_ref, part, k, step, low):
    rows_now = chunk(k, step)
    odd = lax.rem(rank, 2) == 1
    for q in range(keep_ref.shape[0]):
        x = part[:step, 128 * q : 128 * q + 128]
        y = part[step:, 128 * q : 128 * q + 128]
        even_slice = jnp.where(low, x, pltpu.roll(y, 64, 1))
        odd_slice = jnp.where(low, pltpu.roll(x, 64, 1), y)
        p = lax.bitwise_xor(rank // 2, q)
        keep_ref[p, rows_now, :] = jnp.where(odd, odd_slice, even_slice).astype(BF)
        mate_ref[p, rows_now, :] = jnp.where(odd, even_slice, odd_slice).astype(BF)


def fetch_kernels(w_ref, ktm_ref, lw_ref, sems):
    nz, _, width = w_ref.shape
    hc = ktm_ref.shape[0]
    copies = []
    for z in range(nz):
        copies.append(pltpu.make_async_copy(
            w_ref.at[z, pl.ds(0, hc)], ktm_ref.at[:, pl.ds(z * width, width)], sems.at[2 * z]))
        copies.append(pltpu.make_async_copy(
            w_ref.at[z, pl.ds(hc, lw_ref.shape[1])], lw_ref.at[z], sems.at[2 * z + 1]))
    for copy in copies:
        copy.start()
    return copies


def join_temporal(lw_ref, lf_ref, ltm_ref):
    ch = ltm_ref.shape[1]
    width = lw_ref.shape[2] // 2
    count = 2 * lw_ref.shape[0]
    size = ltm_ref.shape[0] // count
    for z in range(lw_ref.shape[0]):
        first = lw_ref[z, :, 0:ch].astype(F32)
        off = width % 128
        second = lw_ref[z, :, width - off : width - off + ch + 128].astype(F32)
        second = pltpu.roll(second, ch + 128 - off, 1)[:, 0:ch]
        for b, block in ((2 * z, first), (2 * z + 1, second)):
            lf_ref[b * size : b * size + block.shape[0], :] = block
    ltm_ref[...] = lf_ref[0 : ltm_ref.shape[0], :].astype(BF)


def prepare_body(w_ref, kn_out, l_out, lt_out, rows_out, ktm_ref, lw_ref, lf_ref, sems):
    hc, ch = ktm_ref.shape[0], l_out.shape[1]
    for copy in fetch_kernels(w_ref, ktm_ref, lw_ref, sems):
        copy.wait()
    for t in range(9):
        kn_out[t] = ktm_ref[:, t * ch : (t + 1) * ch].astype(F32).T.astype(BF)
    join_temporal(lw_ref, lf_ref, l_out)
    rows_out[...] = lw_ref[:, lw_ref.shape[1] - rows_out.shape[1] :, :]
    for t in range(3):
        lt_out[t] = lf_ref[t * hc : (t + 1) * hc].T.astype(BF)


def prepare(w, hc, ch, deps=()):
    outs = [
        jax.ShapeDtypeStruct((9, ch, hc), BF),
        jax.ShapeDtypeStruct((3 * hc, ch), BF),
        jax.ShapeDtypeStruct((3, ch, hc), BF),
        jax.ShapeDtypeStruct((w.shape[0], 16, w.shape[2]), BF),
    ]
    tall = w.shape[1] - hc
    scratch = [
        pltpu.VMEM((hc, 9 * ch), BF),
        pltpu.VMEM((w.shape[0], tall, w.shape[2]), BF),
        pltpu.VMEM((3 * hc + tall, ch), F32),
        pltpu.SemaphoreType.DMA((2 * w.shape[0],)),
    ]
    return call(prepare_body, outs, scratch, 2 * w.size * 512, w, deps=deps, far=(0,))


def conv_body(side, first, rank_ref, *refs):
    n = 1 if first else 8
    slices = refs[:n]
    (kn_in, ltm_ref, vec_ref, before_ref, after_ref,
     pad_out, hid_out, xhat_out, rs_ref, mate_ref, keep_ref,
     pad_ref, hid_ref, xhat_ref, sp_ref, kn_ref, sems) = refs[n:]
    rank = rank_ref[0]
    kn_copy = pltpu.make_async_copy(kn_in, kn_ref, sems.at[0])
    kn_copy.start()
    ch, hc = pad_ref.shape[2], hid_ref.shape[1]
    rows = hid_ref.shape[0]
    plane = rows // side
    nf = plane // side
    step = plane // 2
    clear_borders(pad_ref, side, plane, nf)
    if first:
        for i in range(side):
            pad_ref[i + 1, nf : nf + plane] = slices[0][i * plane : (i + 1) * plane]
    else:
        def place(k, carry):
            for q, odd, a_ref, b_ref in by_rank(slices, rank):
                top, bottom = halves(odd, a_ref[chunk(k, step), :], b_ref[chunk(k, step), :])
                lanes = pl.ds(pl.multiple_of(128 * q, 128), 128)
                for piece, kk in ((top, k), (bottom, k + side)):
                    at = nf + lax.rem(kk, 2) * step
                    pad_ref[1 + kk // 2, pl.ds(pl.multiple_of(at, 16), step), lanes] = piece.astype(BF)
            return carry

        lax.fori_loop(0, side, place, 0, unroll=True)
    pad_copy = pltpu.make_async_copy(pad_ref, pad_out, sems.at[1])
    pad_copy.start()
    kn_copy.wait()

    def conv(i, total):
        acc = jnp.zeros((plane, hc), F32)
        for t in range(9):
            r, c = t // 3, t % 3
            acc += nn(pad_ref[i + r, c * nf : c * nf + plane, :], kn_ref[t])
        sp_ref[i] = acc
        return total + jnp.sum(acc, axis=0, keepdims=True)

    mean = lax.fori_loop(0, side, conv, jnp.zeros((1, hc), F32), unroll=True) / rows

    def square(i, total):
        cen = sp_ref[i] - mean
        return total + jnp.sum(cen * cen, axis=0, keepdims=True)

    var = lax.fori_loop(0, side, square, jnp.zeros((1, hc), F32), unroll=True) / rows
    rs = lax.rsqrt(var + eps)
    rs_ref[...] = rs
    gain, bias = vec_ref[0:1, :], vec_ref[1:2, :]

    def act(i, carry):
        xhat = (sp_ref[i] - mean) * rs
        xhat_ref[i] = xhat
        v = xhat * gain + bias
        v = v * jax.nn.sigmoid(v)
        sp_ref[i] = v
        hid_ref[chunk(i, plane), :] = v.astype(BF)
        return carry

    lax.fori_loop(0, side, act, 0, unroll=True)
    late = [
        pltpu.make_async_copy(hid_ref, hid_out, sems.at[2]),
        pltpu.make_async_copy(xhat_ref, xhat_out, sems.at[3]),
    ]
    for copy in late:
        copy.start()
    low = lax.broadcasted_iota(jnp.int32, (step, 128), 1) < 64

    def temporal(k, carry):
        pieces = []
        for kk in (k, k + side):
            par = lax.rem(kk, 2)
            h = sp_ref[kk // 2, pl.ds(pl.multiple_of(par * step, 8), step), :]
            at = pl.multiple_of(par * (step % nf), 8)
            pieces.append((
                (pltpu.roll(h, 1, 0) * before_ref[pl.ds(at, step), :]).astype(BF),
                h.astype(BF),
                (pltpu.roll(h, step - 1, 0) * after_ref[pl.ds(at, step), :]).astype(BF),
            ))
        part = sum(
            nn(jnp.concatenate([x, y], axis=0), ltm_ref[t * hc : (t + 1) * hc])
            for t, (x, y) in enumerate(zip(*pieces))
        )
        store_packed(rank, mate_ref, keep_ref, part, k, step, low)
        return carry

    lax.fori_loop(0, side, temporal, 0, unroll=True)
    for copy in [pad_copy] + late:
        copy.wait()


def conv_forward(rank, g, kn, lt, vec, before, after, side, pixels, ch, deps=()):
    hc = vec.shape[1]
    plane = pixels // side
    nf = plane // side
    n = len(g)
    shapes = [
        ((side + 2, plane + 2 * nf, ch), BF),
        ((pixels, hc), BF),
        ((side, plane, hc), F32),
    ]
    outs = [jax.ShapeDtypeStruct(*s) for s in shapes] + [
        jax.ShapeDtypeStruct((1, hc), F32),
        jax.ShapeDtypeStruct((4, pixels // 2, 128), BF),
        jax.ShapeDtypeStruct((4, pixels // 2, 128), BF),
    ]
    scratch = [pltpu.VMEM(*s) for s in shapes] + [
        pltpu.VMEM((side, plane, hc), F32),
        pltpu.VMEM((9, ch, hc), BF),
        pltpu.SemaphoreType.DMA((4,)),
    ]
    flops = 2 * pixels * hc * 12 * ch
    return call(functools.partial(conv_body, side, n == 1), outs, scratch, flops,
                rank, *g, kn, lt, vec, before, after,
                deps=deps, far=(n + 1,), far_outs=(0, 1, 2))


def fold(v):
    return v + pltpu.roll(v, 64, 1)


def total_of(refs):
    t = refs[0][...].astype(F32)
    for ref in refs[1:]:
        t += ref[...].astype(F32)
    return t


def pair_sum_body(keep_ref, mate_ref, *out_refs):
    for p, ref in enumerate(out_refs):
        ref[...] = (keep_ref[p].astype(F32) + mate_ref[p].astype(F32)).astype(ref.dtype)


def pair_sum(keep, arrived, deps=()):
    shape = keep.shape[1:]
    outs = [jax.ShapeDtypeStruct(shape, BF)] * keep.shape[0]
    return call(pair_sum_body, outs, [], keep.size, keep, arrived, deps=deps)


def out_norm_body(n, has_skip, *refs):
    parts, refs = refs[:n], refs[n:]
    if has_skip:
        vec_ref, skip_ref, xhat_ref, rs_ref, pre_ref, res_ref = refs
    else:
        vec_ref, xhat_ref, rs_ref, pre_ref, res_ref = refs
    t = total_of(parts)
    pixels = 2 * t.shape[0]
    mean = fold(jnp.sum(t, axis=0, keepdims=True)) / pixels
    cen = t - mean
    rs = lax.rsqrt(fold(jnp.sum(cen * cen, axis=0, keepdims=True)) / pixels + eps)
    xhat = cen * rs
    pre = xhat * vec_ref[0:1, :] + vec_ref[1:2, :]
    if has_skip:
        pre = pre + skip_ref[...].astype(F32)
    xhat_ref[...] = xhat
    rs_ref[...] = rs
    pre_ref[...] = pre
    res_ref[...] = (pre * jax.nn.sigmoid(pre)).astype(BF)


def out_norm(parts, vec, skip, deps=()):
    half = parts[0].shape[0]
    outs = [
        jax.ShapeDtypeStruct((half, 128), F32),
        jax.ShapeDtypeStruct((1, 128), F32),
        jax.ShapeDtypeStruct((half, 128), F32),
        jax.ShapeDtypeStruct((half, 128), BF),
    ]
    args = (*parts, vec) + (() if skip is None else (skip,))
    body = functools.partial(out_norm_body, len(parts), skip is not None)
    return call(body, outs, [], half * 128 * 10, *args, deps=deps)


def out_back_body(n, *refs):
    parts, (pre_ref, xhat_ref, rs_ref, vec_ref, dpre_ref, dt_ref, sums_ref) = refs[:n], refs[n:]
    g = total_of(parts)
    pre, xhat = pre_ref[...], xhat_ref[...]
    sig = jax.nn.sigmoid(pre)
    dpre = g * (sig * (1.0 + pre * (1.0 - sig)))
    pixels = 2 * pre.shape[0]
    sb = fold(jnp.sum(dpre, axis=0, keepdims=True))
    sg = fold(jnp.sum(dpre * xhat, axis=0, keepdims=True))
    dpre_ref[...] = dpre.astype(BF)
    scale = vec_ref[0:1, :] * rs_ref[...]
    dt_ref[...] = (scale * (dpre - sb / pixels - xhat * (sg / pixels))).astype(BF)
    sums_ref[0:1, :] = sg
    sums_ref[1:2, :] = sb


def out_back(parts, pre, xhat, rs, vec, deps=()):
    half = pre.shape[0]
    outs = [
        jax.ShapeDtypeStruct((half, 128), BF),
        jax.ShapeDtypeStruct((half, 128), BF),
        jax.ShapeDtypeStruct((2, 128), F32),
    ]
    args = (*parts, pre, xhat, rs, vec)
    return call(functools.partial(out_back_body, len(parts)), outs, [], half * 1280, *args, deps=deps)


def conv_back_body(side, rank_ref, *refs):
    slices, (xhat_in, rs_ref, w_ref, lnt_ref, vec_ref, before_ref, after_ref,
             dt_out, ds_out, sums_ref, mate_ref, keep_ref,
             dt_ref, ds_ref, xhat_ref, dy_ref, pad_ref, ktm_ref, sems) = refs[:8], refs[8:]
    half = slices[0].shape[0]
    rank = rank_ref[0]
    nz, _, width = w_ref.shape
    rows = 2 * half
    plane = rows // side
    nf = plane // side
    step = plane // 2
    hc = ds_ref.shape[1]
    ch = dt_ref.shape[1]
    fetched = [
        pltpu.make_async_copy(
            w_ref.at[z, pl.ds(0, hc)], ktm_ref.at[:, pl.ds(z * width, width)], sems.at[z])
        for z in range(nz)
    ]
    xhat_copy = pltpu.make_async_copy(xhat_in, xhat_ref, sems.at[nz])
    for copy in fetched + [xhat_copy]:
        copy.start()
    clear_borders(pad_ref, side, plane, nf)

    def place(k, carry):
        for q, odd, a_ref, b_ref in by_rank(slices, rank):
            top, bottom = halves(odd, a_ref[chunk(k, step), :], b_ref[chunk(k, step), :])
            lanes = pl.ds(pl.multiple_of(128 * q, 128), 128)
            dt_ref[chunk(k, step), lanes] = top.astype(BF)
            dt_ref[pl.ds(pl.multiple_of(half + k * step, 16), step), lanes] = bottom.astype(BF)
        return carry

    lax.fori_loop(0, side, place, 0, unroll=True)
    dt_copy = pltpu.make_async_copy(dt_ref, dt_out, sems.at[nz + 1])
    dt_copy.start()
    xhat_copy.wait()
    gain, bias = vec_ref[0:1, :], vec_ref[1:2, :]

    def hidden_grad(i, sums):
        dt = dt_ref[chunk(i, plane), :]
        early = nn(dt, lnt_ref[0]) * before_ref[0:plane, :]
        late = nn(dt, lnt_ref[2]) * after_ref[0:plane, :]
        dh = nn(dt, lnt_ref[1]) + pltpu.roll(early, plane - 1, 0) + pltpu.roll(late, 1, 0)
        xhat = xhat_ref[i]
        v = xhat * gain + bias
        sig = jax.nn.sigmoid(v)
        dy = dh * (sig * (1.0 + v * (1.0 - sig)))
        dy_ref[i] = dy
        return (
            sums[0] + jnp.sum(dy * xhat, axis=0, keepdims=True),
            sums[1] + jnp.sum(dy, axis=0, keepdims=True),
        )

    zero = jnp.zeros((1, hc), F32)
    sg, sb = lax.fori_loop(0, side, hidden_grad, (zero, zero), unroll=True)
    sums_ref[0:1, :] = sg
    sums_ref[1:2, :] = sb
    scale = gain * rs_ref[...]

    def spatial_grad(i, carry):
        ds = (scale * (dy_ref[i] - sb / rows - xhat_ref[i] * (sg / rows))).astype(BF)
        pad_ref[i + 1, nf : nf + plane] = ds
        ds_ref[chunk(i, plane), :] = ds
        return carry

    lax.fori_loop(0, side, spatial_grad, 0, unroll=True)
    ds_copy = pltpu.make_async_copy(ds_ref, ds_out, sems.at[nz + 2])
    ds_copy.start()
    for copy in fetched:
        copy.wait()
    low = lax.broadcasted_iota(jnp.int32, (step, 128), 1) < 64

    def back(k, carry):
        acc = jnp.zeros((2 * step, ch), F32)
        for t in range(9):
            r, c = 2 - t // 3, 2 - t % 3
            pieces = []
            for kk in (k, k + side):
                at = c * nf + lax.rem(kk, 2) * step
                pieces.append(pad_ref[kk // 2 + r, pl.ds(pl.multiple_of(at, 16), step), :])
            acc += nn(jnp.concatenate(pieces, axis=0), ktm_ref[:, t * ch : (t + 1) * ch])
        store_packed(rank, mate_ref, keep_ref, acc, k, step, low)
        return carry

    lax.fori_loop(0, side, back, 0, unroll=True)
    dt_copy.wait()
    ds_copy.wait()


def conv_back(rank, g, xhat, rs, w, lnt, vec, before, after, side, deps=()):
    half = g[0].shape[0]
    hc = vec.shape[1]
    ch = len(g) * 64
    pixels = 2 * half
    plane = pixels // side
    nf = plane // side
    outs = [
        jax.ShapeDtypeStruct((pixels, ch), BF),
        jax.ShapeDtypeStruct((pixels, hc), BF),
        jax.ShapeDtypeStruct((2, hc), F32),
        jax.ShapeDtypeStruct((4, half, 128), BF),
        jax.ShapeDtypeStruct((4, half, 128), BF),
    ]
    scratch = [
        pltpu.VMEM((pixels, ch), BF),
        pltpu.VMEM((pixels, hc), BF),
        pltpu.VMEM((side, plane, hc), F32),
        pltpu.VMEM((side, plane, hc), F32),
        pltpu.VMEM((side + 2, plane + 2 * nf, hc), BF),
        pltpu.VMEM((hc, 9 * ch), BF),
        pltpu.SemaphoreType.DMA((w.shape[0] + 3,)),
    ]
    flops = 2 * pixels * hc * 12 * ch
    return call(functools.partial(conv_back_body, side), outs, scratch, flops,
                rank, *g, xhat, rs, w, lnt, vec, before, after,
                deps=deps, far=(9, 11), far_outs=(0, 1))


def grads_body(side, pad_ref, hid_ref, ds_ref, dt_ref, before_ref, after_ref, mid_ref, out_ref,
               sg_ref, dst_ref, taps_ref, tg_ref, vec_ref):
    ch = pad_ref.shape[2]
    hc = hid_ref.shape[1]
    plane = hid_ref.shape[0] // side
    nf = plane // side
    for i in (0, 1, side + 2, side + 3):
        dst_ref[i] = jnp.zeros(dst_ref.shape[1:], BF)
    for i in range(side):
        at = slice(i * plane, (i + 1) * plane)
        h = hid_ref[at, :].astype(F32)
        taps_ref[i, 0:hc] = (pltpu.roll(h, 1, 0) * before_ref[0:plane, :]).T.astype(BF)
        taps_ref[i, hc : 2 * hc] = h.T.astype(BF)
        taps_ref[i, 2 * hc : 3 * hc] = (pltpu.roll(h, plane - 1, 0) * after_ref[0:plane, :]).T.astype(BF)
        dst_ref[i + 2] = ds_ref[at, :].astype(F32).T.astype(BF)
    tg_ref[0 : 3 * hc, :] = sum(
        nn(taps_ref[i], dt_ref[i * plane : (i + 1) * plane, :]) for i in range(side)
    )
    tg_ref[3 * hc :, :] = jnp.zeros((tg_ref.shape[0] - 3 * hc, ch), F32)
    nz, _, width = sg_ref.shape
    size = 3 * hc // (2 * nz)
    vec_ref[...] = jnp.zeros(vec_ref.shape, F32)
    vec_ref[size : size + 2, 0:hc] = mid_ref[...]
    vec_ref[size + 2 : size + 4, 0:128] = out_ref[...]
    tall = vec_ref.shape[0]
    inside = lax.broadcasted_iota(jnp.int32, (tall, ch), 0) < size
    off = (width // 2) % 128
    for z in range(nz):
        first, second = [
            jnp.where(inside, tg_ref[b * size : b * size + tall, :], vec_ref[...])
            for b in (2 * z, 2 * z + 1)
        ]
        start = width // 2 - off
        sg_ref[z, hc : hc + tall, 0:ch] = first.astype(BF)
        second = pltpu.roll(jnp.concatenate([second, jnp.zeros((tall, 128), F32)], axis=1), off, 1)
        sg_ref[z, hc : hc + tall, start : start + ch + 128] = second.astype(BF)
    for c in range(3):
        acc = sum(
            nn(dst_ref[i : i + 3].reshape(3 * hc, plane), pad_ref[i, c * nf : c * nf + plane, :])
            for i in range(1, side + 1)
        )
        for r in range(3):
            first = (3 * r + c) * ch
            end = first + ch
            at = (2 - r) * hc
            done = 0
            while first < end:
                z = first // width
                last = min(end, (z + 1) * width)
                sg_ref[z, 0:hc, first - z * width : last - z * width] = (
                    acc[at : at + hc, done : done + last - first].astype(BF)
                )
                done += last - first
                first = last


def kernel_grads(pad, hidden, ds, dt, before, after, mid, out, side, shape, deps=()):
    pixels, hc = hidden.shape
    ch = dt.shape[1]
    plane = pixels // side
    outs = [jax.ShapeDtypeStruct(shape, BF)]
    tall = shape[1] - hc
    scratch = [
        pltpu.VMEM((side + 4, hc, plane), BF),
        pltpu.VMEM((side, 3 * hc, plane), BF),
        pltpu.VMEM((3 * hc + tall, ch), F32),
        pltpu.VMEM((tall, ch), F32),
    ]
    flops = 2 * pixels * hc * 12 * ch
    return call(functools.partial(grads_body, side), outs, scratch, flops,
                pad, hidden, ds, dt, before, after, mid, out, deps=deps)[0]


def copy_after_body(v_ref, out_ref):
    out_ref[...] = v_ref[...]


def after_all(v, *deps):
    return call(copy_after_body, [jax.ShapeDtypeStruct(v.shape, v.dtype)], [], v.size, v, deps=deps)[0]


def pack_kernels_body(kt_ref, lt_ref, vec_ref, out_ref, low_ref):
    ranks, _, width = out_ref.shape
    hc = kt_ref.shape[0] // ranks
    blocks = lt_ref.shape[0] // hc
    q = hc // ranks
    low_ref[...] = jnp.zeros(low_ref.shape, F32)
    for r in range(ranks):
        out_ref[r, 0:hc, :] = kt_ref[r * hc : (r + 1) * hc, :]
        for b in range(blocks):
            low_ref[r, b * q : (b + 1) * q, 0 : lt_ref.shape[1]] = (
                lt_ref[b * hc + r * q : b * hc + (r + 1) * q, :]
            )
        low_ref[r, blocks * q : blocks * q + 1, :] = vec_ref[...]
        out_ref[r, hc:, :] = low_ref[r].astype(BF)


def pack_kernels(kt, lt, vec, ranks, tall, deps):
    width = kt.shape[1]
    outs = [jax.ShapeDtypeStruct((ranks, kt.shape[0] // ranks + tall, width), BF)]
    scratch = [pltpu.VMEM((ranks, tall, width), F32)]
    return call(pack_kernels_body, outs, scratch, kt.size * 8, kt, lt, vec, deps=deps)[0]


def hop(v, k):
    n = 1
    for name in EVERY:
        n *= lax.axis_size(name)
    return lax.ppermute(v, EVERY, [(i, i ^ k) for i in range(n)])


def plane_gather(v, aside=()):
    got = {0: v}
    for k in (6, 2, 4):
        got[k] = hop(v, k)
    got[1] = hop(after_all(v, *aside) if aside else v, 1)
    for k in (2, 4, 6):
        got[k ^ 1] = hop(got[k], 1)
    return [got[k] for k in range(8)]


def plane_reduce(mate, keep, deps=()):
    sums = pair_sum(keep, hop(mate, 1), deps)
    arrived = {k: hop(sums[k // 2], k) for k in (6, 2, 4)}
    return [sums[0], arrived[2], arrived[4], arrived[6]]


def on_device(frames, cot, starts, ks, ktm, mg, mb, og, ob):
    nz, n_rank, n_seg = lax.axis_size("z"), 8, 4
    n_dp = nz * 2
    fr, side, ch = frames.shape[0], frames.shape[1], frames.shape[3]
    area = side * side
    hid = ks.shape[2]
    hc, cc = hid // n_rank, ch // n_rank
    q = hc // n_rank
    rank = lax.axis_index(PLANE)
    rank_now = rank.astype(jnp.int32).reshape(1)
    d_index = lax.axis_index(("z", "y"))
    nf = n_dp * fr
    pixels = area * nf
    half = pixels // 2

    def keeper(d, s):
        v = (d // 2) ^ s
        return (d % 2) * 4 + (v % 2) * 2 + v // 2

    to_plane = [
        (d * n_seg + s, s * n_rank + keeper(d, s)) for d in range(n_dp) for s in range(n_seg)
    ]
    from_plane = [(b, a) for a, b in to_plane]
    rows = fr * area
    flag_row = jnp.pad(starts.astype(BF)[None], ((0, 11), (0, ch - fr)))
    lead = rows + 12
    moving = jnp.concatenate([frames.reshape(rows, ch), flag_row, cot.reshape(rows, ch)], axis=0)
    moving = lax.ppermute(moving, EVERY, to_plane)

    perm = (jnp.arange(hid).reshape(n_rank, n_rank, q).transpose(1, 0, 2).reshape(hid)[:, None]
            == jnp.arange(hid)[None, :]).astype(BF)
    kt = lax.dot_general(perm, ks[0].astype(BF), (((1,), (1,)), ((), ())),
                         preferred_element_type=F32).astype(BF)
    lrows, width = ktm.shape[1] // n_rank, ks.shape[1]
    tall = -(-(lrows + 4) // 16) * 16
    extra = jnp.concatenate([mg, mb, og, ob], axis=1)
    extra = jnp.pad(extra, ((0, 0), (0, width - extra.shape[1])))
    w = pack_kernels(kt, ktm[0], extra, n_rank, tall, deps=(moving,))
    w = lax.all_to_all(w, PLANE, 0, 0)
    here = w
    high = hc + tall

    w = w.reshape(2, n_seg, high, width).transpose(1, 2, 0, 3).reshape(n_seg, high, 2 * width)
    ws = [lax.all_gather(w[s], "z", axis=0) for s in range(n_seg)]

    group = 7
    own = moving[lead:].reshape(group, rows // group, n_rank, cc).transpose(2, 1, 0, 3)
    own = own.reshape(n_rank, rows // group, group * cc)
    own = jnp.pad(own, ((0, 0), (0, 4), (0, ch - group * cc)))
    own = jnp.concatenate([jnp.broadcast_to(moving[:lead], (n_rank, lead, ch)), own], axis=1)
    gathered = lax.all_to_all(after_all(own, here), PLANE, 0, 0)


    def norm_rows(rows_now):
        row = rows_now[:, (lrows - tall) % 16].reshape(n_dp, width).astype(F32)
        mid = jnp.stack([
            lax.dynamic_slice_in_dim(row[:, i * hc : (i + 1) * hc], rank * q, q, axis=1).reshape(hc)
            for i in range(2)])
        own = lax.dynamic_index_in_dim(row, rank, 0, keepdims=False)
        out = jnp.stack([
            jnp.tile(own[2 * hc + i * cc : 2 * hc + (i + 1) * cc], 2) for i in range(2)])
        return mid, out

    def by_pixel(v):
        width = v.shape[2]
        v = v.reshape(n_rank * fr, area, width).transpose(1, 0, 2)
        return v.reshape(pixels, width)

    def packed(v):
        return jnp.concatenate([v[:half], v[half:]], axis=1)

    a0 = by_pixel(gathered[:, :rows])
    flags = gathered[:, rows, :fr].reshape(nf) > 0.5
    slot = jnp.arange(nf) % fr
    before = jnp.where(flags | (slot == 0), 0.0, 1.0)
    after = jnp.where(jnp.roll(flags, -1) | (slot == fr - 1), 0.0, 1.0)
    spread = (side * nf + nf, hc)
    before = jnp.broadcast_to(jnp.tile(before, side + 1)[:, None], spread)
    after = jnp.broadcast_to(jnp.tile(after, side + 1)[:, None], spread)
    skip = packed(lax.dynamic_slice_in_dim(a0, rank * cc, cc, axis=1))

    def across(*slices):
        n = len(slices)
        v = jnp.stack([jnp.concatenate([v[:, :cc], v[:, cc:]], axis=0) for v in slices])
        v = v.reshape(n, area, n_rank, fr, cc).transpose(2, 0, 1, 3, 4).reshape(n_rank, n * rows, cc)
        return lax.all_to_all(v, PLANE, 0, 0)

    def home(v):
        n = v.shape[1] // rows
        v = v.transpose(1, 0, 2).reshape(n * rows, ch)
        v = lax.ppermute(v, EVERY, from_plane).reshape(n, area, fr, ch).transpose(0, 2, 1, 3)
        return v.reshape(n, *frames.shape)

    saved = []
    g = [a0]
    ready = prepare(ws[0], hc, ch)
    for s in range(n_seg):
        kn, lt, lnt, rows_now = ready
        mid, out = norm_rows(rows_now)
        pad, hidden, xm, rm, mate, keep = conv_forward(
            rank_now, g, kn, lt, mid, before, after, side, pixels, ch)
        parts = plane_reduce(mate, keep)
        xo, ro, pre, res = out_norm(parts, out, skip if s % 2 == 1 else None)
        saved.append((pad, hidden, xm, rm, xo, ro, pre, lnt, mid, out))
        if s % 2 == 1:
            skip = res
        if s < n_seg - 1:
            ready = prepare(ws[s + 1], hc, ch, deps=(res,))
            g = plane_gather(res, ready[:1])
    cot_own = gathered[:, lead : lead + rows // group, : group * cc]
    cot_own = cot_own.reshape(n_rank, rows // group, group, cc).transpose(0, 2, 1, 3)
    cot_own = packed(by_pixel(cot_own.reshape(n_rank, rows, cc)))

    parts = [cot_own]
    skip_grad = None

    grads, raw = [], None
    for s in reversed(range(n_seg)):
        pad, hidden, xm, rm, xo, ro, pre, lnt, mid, out = saved[s]
        if s == 1:
            parts = parts + [skip_grad]
        deps = () if raw is None else (raw, *grads[len(grads) - 1 :])
        dpre, dt, osum = out_back(parts, pre, xo, ro, out, deps=deps)
        if raw is not None:
            grads.append(lax.psum_scatter(after_all(raw, dt), "z", scatter_dimension=0))
        if s % 2 == 1:
            skip_grad = dpre
        dtf, ds, msum, mate, keep = conv_back(
            rank_now, plane_gather(dt), xm, rm, ws[s], lnt, mid, before, after, side)
        if s > 0:
            parts = plane_reduce(mate, keep)
        raw = kernel_grads(pad, hidden, ds, dtf, before, after, msum, osum, side, ws[s].shape,
                           deps=parts[:1] if s > 0 else ())
    last = lax.psum_scatter(raw, "z", scatter_dimension=0)
    parts = plane_reduce(mate, keep, deps=(raw,))

    da = sum(p.astype(F32) for p in parts) + skip_grad.astype(F32)
    home_now = home(across(res, da.astype(BF)))
    output, frames_grad = home_now[0], home_now[1].astype(F32)

    def by_row(v):
        return v.reshape(high, 2, width).transpose(1, 0, 2)

    g = jnp.stack([by_row(v) for v in [last] + grads[::-1]], axis=1).reshape(n_rank, high, width)
    g = lax.all_to_all(g, PLANE, 0, 0)
    space_grad = lax.dot_general(g[:, :hc].reshape(hid, width), perm, (((0,), (0,)), ((), ())),
                                 preferred_element_type=F32)
    tg = g[:, hc : hc + lrows, :ch].reshape(n_rank, -1, q, ch)
    time_grad = tg.transpose(1, 0, 2, 3).reshape(-1, ch).astype(F32)
    sums = g[:, hc + lrows : hc + lrows + 4].astype(F32)

    def mid_own(v):
        return lax.dynamic_slice_in_dim(v[:, :hc], d_index * q, q, axis=1).reshape(1, hc)

    own = lax.dynamic_index_in_dim(sums, d_index, 0, keepdims=False)
    return (
        output,
        frames_grad,
        space_grad[None],
        time_grad[None],
        mid_own(sums[:, 0]),
        mid_own(sums[:, 1]),
        own[2:3, :cc],
        own[3:4, :cc],
    )


def from_behind(value, axis, steps):
    count = lax.axis_size(axis)
    leading, last = (max(0, -steps), min(count, count - steps))
    return lax.ppermute(value, axis, [(source, source + steps) for source in range(leading, last)])


def space_apply(current, kernel):
    frame_side = current.shape[1]
    padded = jnp.pad(current, ((0, 0), (1, 1), (1, 1), (0, 0)))
    stacked = jnp.concatenate(
        [
            padded[:, row_shift : row_shift + frame_side, col_shift : col_shift + frame_side, :]
            for row_shift in range(3)
            for col_shift in range(3)
        ],
        axis=-1,
    )
    return (
        stacked,
        jnp.einsum("fijc,co->fijo", stacked, kernel, preferred_element_type=jnp.float32),
    )


def space_back(gradient, kernel):
    frame_side = gradient.shape[1]
    channels = kernel.shape[0] // 9
    spread = jnp.einsum("fijo,co->fijc", gradient, kernel, preferred_element_type=jnp.float32)
    total = jnp.zeros((gradient.shape[0], frame_side + 2, frame_side + 2, channels), jnp.float32)
    for tap_index in range(9):
        row_shift = tap_index // 3
        col_shift = tap_index % 3
        piece_now = spread[..., tap_index * channels : (tap_index + 1) * channels]
        total = total + jnp.pad(
            piece_now, ((0, 0), (row_shift, 2 - row_shift), (col_shift, 2 - col_shift), (0, 0))
        )
    return total[:, 1 : frame_side + 1, 1 : frame_side + 1, :]


def time_apply(current, kernel, before_mask, after_mask):
    blanks = jnp.zeros_like(current[:1])
    earlier = jnp.concatenate([blanks, current[:-1]], axis=0) * before_mask[
        :, None, None, None
    ].astype(current.dtype)
    later = jnp.concatenate([current[1:], blanks], axis=0) * after_mask[:, None, None, None].astype(
        current.dtype
    )
    stacked = jnp.concatenate([earlier, current, later], axis=-1)
    return (
        stacked,
        jnp.einsum("fijc,co->fijo", stacked, kernel, preferred_element_type=jnp.float32),
    )


def time_back(gradient, kernel, before_mask, after_mask):
    channels = kernel.shape[0] // 3
    spread = jnp.einsum("fijo,co->fijc", gradient, kernel, preferred_element_type=jnp.float32)
    early_part = spread[..., :channels] * before_mask[:, None, None, None]
    late_part = spread[..., 2 * channels :] * after_mask[:, None, None, None]
    blanks = jnp.zeros_like(early_part[:1])
    moved_early = jnp.concatenate([early_part[1:], blanks], axis=0)
    moved_late = jnp.concatenate([blanks, late_part[:-1]], axis=0)
    return spread[..., channels : 2 * channels] + moved_early + moved_late


def moments(values, pixel_count):
    average = lax.psum(jnp.sum(values, axis=(0, 1, 2)), "dp") / pixel_count
    centered = values - average
    spread = lax.psum(jnp.sum(centered * centered, axis=(0, 1, 2)), "dp") / pixel_count
    return (average, lax.rsqrt(spread + eps))


def reduce_back(gradient, normed):
    return lax.psum(
        (jnp.sum(gradient, axis=(0, 1, 2)), jnp.sum(gradient * normed, axis=(0, 1, 2))), "dp"
    )


def silu_slope(values):
    sigmoid_now = jax.nn.sigmoid(values)
    return sigmoid_now * (1.0 + values * (1.0 - sigmoid_now))


def pick_slot(stack, slot_index):
    return lax.dynamic_index_in_dim(stack, slot_index, 0, keepdims=False)


def store_slot(stack, value, slot_index, usable):
    previous = pick_slot(stack, slot_index)
    return lax.dynamic_update_index_in_dim(stack, jnp.where(usable, value, previous), slot_index, 0)


def on_device_general(
    frames, cotangent, starts, space_kernel, time_kernel, mid_gain, mid_bias, out_gain, out_bias
):
    n_segment = lax.axis_size("segment")
    n_data = lax.axis_size("dp")
    segment_index = lax.axis_index("segment")
    odd_segment = segment_index % 2 == 1
    last_segment = segment_index == n_segment - 1
    first_segment = segment_index == 0
    frame_count = frames.shape[0]
    frame_side = frames.shape[1]
    channels = frames.shape[3]
    hidden_units = mid_gain.shape[1] * n_data
    pixel_count = n_data * frame_count * frame_side * frame_side
    turns = 2 * n_segment - 1
    block_shape = (n_segment,) + frames.shape
    all_frames, all_cot, all_starts = (
        lax.all_gather(frames, "segment", axis=0, tiled=True),
        lax.all_gather(cotangent, "segment", axis=0, tiled=True),
        lax.all_gather(starts.astype(jnp.bfloat16), "segment", axis=0, tiled=True),
    )
    frame_stack = all_frames.reshape(block_shape)
    cot_stack = all_cot.reshape(block_shape)
    clip_flags = all_starts.astype(jnp.float32).reshape(n_segment, frame_count)
    positions = jnp.arange(frame_count)
    before_mask = jnp.where((clip_flags > 0.5) | (positions == 0), 0.0, 1.0)
    following = jnp.concatenate([clip_flags[:, 1:], jnp.ones((n_segment, 1), jnp.float32)], axis=1)
    after_mask = jnp.where(following > 0.5, 0.0, 1.0)
    gathered = (
        lax.all_gather(space_kernel[0].astype(jnp.bfloat16), "dp", axis=0, tiled=True),
        lax.all_gather(time_kernel[0].astype(jnp.bfloat16), "dp", axis=0, tiled=True),
        lax.all_gather(mid_gain[0].astype(jnp.bfloat16), "dp", axis=0, tiled=True),
        lax.all_gather(mid_bias[0].astype(jnp.bfloat16), "dp", axis=0, tiled=True),
        lax.all_gather(out_gain[0].astype(jnp.bfloat16), "dp", axis=0, tiled=True),
        lax.all_gather(out_bias[0].astype(jnp.bfloat16), "dp", axis=0, tiled=True),
    )
    space_low, time_low = (gathered[0], gathered[1])
    mid_gain_now = gathered[2].astype(jnp.float32)
    mid_bias_now = gathered[3].astype(jnp.float32)
    out_gain_now = gathered[4].astype(jnp.float32)
    out_bias_now = gathered[5].astype(jnp.float32)
    incoming = jnp.zeros_like(frames)
    carried = jnp.zeros_like(frames)
    kept_input = jnp.zeros(block_shape, jnp.bfloat16)
    kept_skip = jnp.zeros(block_shape, jnp.bfloat16)
    kept_mid_mean = jnp.zeros((n_segment, hidden_units), jnp.float32)
    kept_mid_scale = jnp.zeros((n_segment, hidden_units), jnp.float32)
    kept_out_mean = jnp.zeros((n_segment, channels), jnp.float32)
    kept_out_scale = jnp.zeros((n_segment, channels), jnp.float32)
    results = jnp.zeros(block_shape, jnp.float32)
    for turn_index in range(turns):
        micro_index = turn_index - segment_index
        usable = (micro_index >= 0) & (micro_index < n_segment)
        slot_index = jnp.clip(micro_index, 0, n_segment - 1)
        current = jnp.where(first_segment, pick_slot(frame_stack, slot_index), incoming)
        skip_input = carried
        _, spatial = space_apply(current, space_low)
        mid_mean, mid_scale = moments(spatial, pixel_count)
        hidden_act = jax.nn.silu(
            (spatial - mid_mean) * mid_scale * mid_gain_now + mid_bias_now
        ).astype(jnp.bfloat16)
        _, temporal = time_apply(
            hidden_act,
            time_low,
            pick_slot(before_mask, slot_index),
            pick_slot(after_mask, slot_index),
        )
        out_mean, out_scale = moments(temporal, pixel_count)
        pre_act = (
            (temporal - out_mean) * out_scale * out_gain_now
            + out_bias_now
            + jnp.where(odd_segment, skip_input.astype(jnp.float32), 0.0)
        )
        result = jax.nn.silu(pre_act).astype(jnp.bfloat16)
        kept_input = store_slot(kept_input, current, slot_index, usable)
        kept_skip = store_slot(kept_skip, skip_input, slot_index, usable)
        kept_mid_mean = store_slot(kept_mid_mean, mid_mean, slot_index, usable)
        kept_mid_scale = store_slot(kept_mid_scale, mid_scale, slot_index, usable)
        kept_out_mean = store_slot(kept_out_mean, out_mean, slot_index, usable)
        kept_out_scale = store_slot(kept_out_scale, out_scale, slot_index, usable)
        results = store_slot(results, result.astype(jnp.float32), slot_index, usable)
        if turn_index < turns - 1:
            incoming, carried = from_behind(
                (result, jnp.where(odd_segment, result, current)), "segment", 1
            )
    gathered = (
        lax.all_gather(space_kernel[0].astype(jnp.bfloat16), "dp", axis=0, tiled=True),
        lax.all_gather(time_kernel[0].astype(jnp.bfloat16), "dp", axis=0, tiled=True),
        lax.all_gather(mid_gain[0].astype(jnp.bfloat16), "dp", axis=0, tiled=True),
        lax.all_gather(mid_bias[0].astype(jnp.bfloat16), "dp", axis=0, tiled=True),
        lax.all_gather(out_gain[0].astype(jnp.bfloat16), "dp", axis=0, tiled=True),
        lax.all_gather(out_bias[0].astype(jnp.bfloat16), "dp", axis=0, tiled=True),
    )
    space_low, time_low = (gathered[0], gathered[1])
    mid_gain_now = gathered[2].astype(jnp.float32)
    mid_bias_now = gathered[3].astype(jnp.float32)
    out_gain_now = gathered[4].astype(jnp.float32)
    out_bias_now = gathered[5].astype(jnp.float32)
    grad_input = jnp.zeros_like(frames)
    grad_skip = jnp.zeros_like(frames)
    space_acc = jnp.zeros(space_low.shape, jnp.float32)
    time_acc = jnp.zeros(time_low.shape, jnp.float32)
    mid_gain_acc = jnp.zeros((hidden_units,), jnp.float32)
    mid_bias_acc = jnp.zeros((hidden_units,), jnp.float32)
    out_gain_acc = jnp.zeros((channels,), jnp.float32)
    out_bias_acc = jnp.zeros((channels,), jnp.float32)
    input_grads = jnp.zeros(block_shape, jnp.float32)
    for turn_index in range(turns):
        micro_index = n_segment - 1 - (turn_index - (n_segment - 1 - segment_index))
        usable = (micro_index >= 0) & (micro_index < n_segment)
        usable_weight = usable.astype(jnp.float32)
        slot_index = jnp.clip(micro_index, 0, n_segment - 1)
        current = pick_slot(kept_input, slot_index)
        skip_input = pick_slot(kept_skip, slot_index)
        before_now = pick_slot(before_mask, slot_index)
        after_now = pick_slot(after_mask, slot_index)
        space_taps, spatial = space_apply(current, space_low)
        mid_normed = (spatial - pick_slot(kept_mid_mean, slot_index)) * pick_slot(
            kept_mid_scale, slot_index
        )
        mid_pre = mid_normed * mid_gain_now + mid_bias_now
        hidden_act = jax.nn.silu(mid_pre).astype(jnp.bfloat16)
        time_taps, temporal = time_apply(hidden_act, time_low, before_now, after_now)
        out_scale = pick_slot(kept_out_scale, slot_index)
        out_normed = (temporal - pick_slot(kept_out_mean, slot_index)) * out_scale
        pre_act = (
            out_normed * out_gain_now
            + out_bias_now
            + jnp.where(odd_segment, skip_input.astype(jnp.float32), 0.0)
        )
        grad_result = jnp.where(
            last_segment,
            pick_slot(cot_stack, slot_index).astype(jnp.float32),
            grad_input.astype(jnp.float32)
            + jnp.where(odd_segment, grad_skip.astype(jnp.float32), 0.0),
        )
        grad_pre = grad_result * silu_slope(pre_act)
        out_bias_sum, out_gain_sum = reduce_back(grad_pre, out_normed)
        grad_temporal = (
            out_gain_now
            * out_scale
            * (grad_pre - out_bias_sum / pixel_count - out_normed * out_gain_sum / pixel_count)
        ).astype(jnp.bfloat16)
        time_acc = time_acc + usable_weight * jnp.einsum(
            "fijc,fijo->co", time_taps, grad_temporal, preferred_element_type=jnp.float32
        )
        grad_hidden = time_back(grad_temporal, time_low, before_now, after_now)
        grad_mid = grad_hidden * silu_slope(mid_pre)
        mid_bias_sum, mid_gain_sum = reduce_back(grad_mid, mid_normed)
        mid_scale = pick_slot(kept_mid_scale, slot_index)
        grad_spatial = (
            mid_gain_now
            * mid_scale
            * (grad_mid - mid_bias_sum / pixel_count - mid_normed * mid_gain_sum / pixel_count)
        ).astype(jnp.bfloat16)
        space_acc = space_acc + usable_weight * jnp.einsum(
            "fijc,fijo->co", space_taps, grad_spatial, preferred_element_type=jnp.float32
        )
        grad_current = space_back(grad_spatial, space_low)
        mid_gain_acc = mid_gain_acc + usable_weight * mid_gain_sum
        mid_bias_acc = mid_bias_acc + usable_weight * mid_bias_sum
        out_gain_acc = out_gain_acc + usable_weight * out_gain_sum
        out_bias_acc = out_bias_acc + usable_weight * out_bias_sum
        input_grads = store_slot(
            input_grads, grad_current + grad_skip.astype(jnp.float32), slot_index, usable
        )
        if turn_index < turns - 1:
            grad_input, grad_skip = from_behind(
                (
                    grad_current.astype(jnp.bfloat16),
                    jnp.where(odd_segment, grad_pre.astype(jnp.bfloat16), grad_skip),
                ),
                "segment",
                -1,
            )
    space_grad, time_grad = (
        lax.psum_scatter(space_acc, "dp", scatter_dimension=0, tiled=True),
        lax.psum_scatter(time_acc, "dp", scatter_dimension=0, tiled=True),
    )
    data_index = lax.axis_index("dp")

    def own_share(full_vector):
        share = full_vector.shape[0] // n_data
        return lax.dynamic_slice_in_dim(full_vector, data_index * share, share)[None]

    flat_shape = (n_segment * frame_count,) + frames.shape[1:]
    arrived_out, arrived_grads = (
        lax.all_to_all(
            results.reshape(flat_shape).astype(jnp.bfloat16),
            "segment",
            split_axis=0,
            concat_axis=0,
            tiled=True,
        ).astype(jnp.float32),
        lax.all_to_all(
            input_grads.reshape(flat_shape).astype(jnp.bfloat16),
            "segment",
            split_axis=0,
            concat_axis=0,
            tiled=True,
        ).astype(jnp.float32),
    )
    output = arrived_out[(n_segment - 1) * frame_count :].astype(jnp.bfloat16)
    frames_grad = arrived_grads[:frame_count]
    return (
        output,
        frames_grad,
        space_grad[None],
        time_grad[None],
        own_share(mid_gain_acc),
        own_share(mid_bias_acc),
        own_share(out_gain_acc),
        own_share(out_bias_acc),
    )


def general(mesh):
    return jax.shard_map(
        on_device_general,
        mesh=mesh,
        in_specs=(
            P(("dp", "segment"), None, None, None),
            P(("dp", "segment"), None, None, None),
            P(("dp", "segment")),
            P("segment", "dp", None),
            P("segment", "dp", None),
            P("segment", "dp"),
            P("segment", "dp"),
            P("segment", "dp"),
            P("segment", "dp"),
        ),
        out_specs=(
            P(("dp", "segment"), None, None, None),
            P(("dp", "segment"), None, None, None),
            P("segment", "dp", None),
            P("segment", "dp", None),
            P("segment", "dp"),
            P("segment", "dp"),
            P("segment", "dp"),
            P("segment", "dp"),
        ),
        check_vma=False,
    )


def solution(mesh):
    if mesh.shape["dp"] != 8 or mesh.shape["segment"] != 4:
        return general(mesh)
    n_dp, n_seg = mesh.shape["dp"], mesh.shape["segment"]
    fine = Mesh(mesh.devices.reshape(n_dp // 2, 2, 2, n_seg // 2), EVERY)
    dp, seg = ("z", "y"), ("x", "c")
    return jax.shard_map(
        on_device,
        mesh=fine,
        in_specs=(
            P(EVERY, None, None, None),
            P(EVERY, None, None, None),
            P(EVERY),
            P(seg, dp, None),
            P(seg, dp, None),
            P(seg, dp),
            P(seg, dp),
            P(seg, dp),
            P(seg, dp),
        ),
        out_specs=(
            P(EVERY, None, None, None),
            P(EVERY, None, None, None),
            P(seg, dp, None),
            P(seg, dp, None),
            P(seg, dp),
            P(seg, dp),
            P(seg, dp),
            P(seg, dp),
        ),
        check_vma=False,
    )
```

```python
import functools

import jax
import jax.numpy as jnp
from jax import lax
from jax.experimental import pallas as pl
from jax.experimental.pallas import tpu as pltpu
from jax.sharding import Mesh, PartitionSpec as P

eps = 1e-05
PLANE = ("y", "x", "c")
EVERY = ("z", "y", "x", "c")
BF = jnp.bfloat16
F32 = jnp.float32


def nt(a, b):
    return lax.dot_general(a, b, (((1,), (1,)), ((), ())), preferred_element_type=F32)


def nn(a, b):
    return lax.dot_general(a, b, (((1,), (0,)), ((), ())), preferred_element_type=F32)


VMEM_CAP = 56 * 1024 * 1024
ANY = pl.BlockSpec(memory_space=pl.ANY)


def call(body, outs, scratch, flops, *args, deps=(), far=(), far_outs=()):
    moved = sum(a.size * a.dtype.itemsize for a in args) + sum(
        o.size * o.dtype.itemsize for o in outs
    )
    n = len(deps)

    def spec(a):
        return pl.BlockSpec(memory_space=pltpu.SMEM if a.dtype == jnp.int32 else pltpu.VMEM)

    return pl.pallas_call(
        lambda *refs: body(*refs[n:]),
        out_shape=outs,
        in_specs=[ANY] * n + [ANY if i in far else spec(a) for i, a in enumerate(args)],
        out_specs=[ANY if i in far_outs else spec(o) for i, o in enumerate(outs)],
        scratch_shapes=scratch,
        compiler_params=pltpu.CompilerParams(vmem_limit_bytes=VMEM_CAP),
        cost_estimate=pl.CostEstimate(flops=flops, bytes_accessed=moved, transcendentals=0),
    )(*deps, *args)


def chunk(i, size):
    return pl.ds(pl.multiple_of(i * size, 16), size)


def clear_borders(pad_ref, side, plane, nf):
    zrow = jnp.zeros(pad_ref.shape[1:], BF)
    pad_ref[0] = zrow
    pad_ref[side + 1] = zrow
    zcol = jnp.zeros((nf, pad_ref.shape[2]), BF)
    for i in range(side):
        pad_ref[i + 1, 0:nf] = zcol
        pad_ref[i + 1, nf + plane : 2 * nf + plane] = zcol


def by_rank(slices, rank):
    odd = lax.rem(rank, 2) == 1
    for p in range(len(slices) // 2):
        a, b = slices[2 * p], slices[2 * p + 1]
        yield lax.bitwise_xor(rank // 2, p), odd, a, b


def halves(odd, own, mate):
    a, b = jnp.where(odd, mate, own), jnp.where(odd, own, mate)
    top = jnp.concatenate([a[:, :64], b[:, :64]], axis=1)
    bottom = jnp.concatenate([a[:, 64:], b[:, 64:]], axis=1)
    return top, bottom


def store_packed(rank, mate_ref, keep_ref, part, k, step, low):
    rows_now = chunk(k, step)
    odd = lax.rem(rank, 2) == 1
    part = part.astype(BF)
    for q in range(keep_ref.shape[0]):
        x = part[:step, 128 * q : 128 * q + 128]
        y = part[step:, 128 * q : 128 * q + 128]
        even_slice = jnp.concatenate([x[:, :64], y[:, :64]], axis=1)
        odd_slice = jnp.concatenate([x[:, 64:], y[:, 64:]], axis=1)
        p = lax.bitwise_xor(rank // 2, q)
        keep_ref[p, rows_now, :] = jnp.where(odd, odd_slice, even_slice)
        mate_ref[p, rows_now, :] = jnp.where(odd, even_slice, odd_slice)


def fetch_kernels(w_ref, ktm_ref, lw_ref, sems):
    nz, _, width = w_ref.shape
    hc = ktm_ref.shape[0]
    copies = []
    for z in range(nz):
        copies.append(pltpu.make_async_copy(
            w_ref.at[z, pl.ds(0, hc)], ktm_ref.at[:, pl.ds(z * width, width)], sems.at[2 * z]))
        copies.append(pltpu.make_async_copy(
            w_ref.at[z, pl.ds(hc, lw_ref.shape[1])], lw_ref.at[z], sems.at[2 * z + 1]))
    for copy in copies:
        copy.start()
    return copies


def join_temporal(lw_ref, lf_ref, ltm_ref):
    ch = ltm_ref.shape[1]
    width = lw_ref.shape[2] // 2
    count = 2 * lw_ref.shape[0]
    size = ltm_ref.shape[0] // count
    for z in range(lw_ref.shape[0]):
        first = lw_ref[z, :, 0:ch].astype(F32)
        off = width % 128
        second = lw_ref[z, :, width - off : width - off + ch + 128].astype(F32)
        second = pltpu.roll(second, ch + 128 - off, 1)[:, 0:ch]
        for b, block in ((2 * z, first), (2 * z + 1, second)):
            lf_ref[b * size : b * size + block.shape[0], :] = block
    ltm_ref[...] = lf_ref[0 : ltm_ref.shape[0], :].astype(BF)


def prepare_body(w_ref, kn_out, l_out, lt_out, rows_out, ktm_ref, lw_ref, lf_ref, sems):
    hc, ch = ktm_ref.shape[0], l_out.shape[1]
    for copy in fetch_kernels(w_ref, ktm_ref, lw_ref, sems):
        copy.wait()
    for t in range(9):
        kn_out[t] = ktm_ref[:, t * ch : (t + 1) * ch].astype(F32).T.astype(BF)
    join_temporal(lw_ref, lf_ref, l_out)
    rows_out[...] = lw_ref[:, lw_ref.shape[1] - rows_out.shape[1] :, :]
    for t in range(3):
        lt_out[t] = lf_ref[t * hc : (t + 1) * hc].T.astype(BF)


def prepare(w, hc, ch, deps=()):
    outs = [
        jax.ShapeDtypeStruct((9, ch, hc), BF),
        jax.ShapeDtypeStruct((3 * hc, ch), BF),
        jax.ShapeDtypeStruct((3, ch, hc), BF),
        jax.ShapeDtypeStruct((w.shape[0], 16, w.shape[2]), BF),
    ]
    tall = w.shape[1] - hc
    scratch = [
        pltpu.VMEM((hc, 9 * ch), BF),
        pltpu.VMEM((w.shape[0], tall, w.shape[2]), BF),
        pltpu.VMEM((3 * hc + tall, ch), F32),
        pltpu.SemaphoreType.DMA((2 * w.shape[0],)),
    ]
    return call(prepare_body, outs, scratch, 2 * w.size * 512, w, deps=deps, far=(0,))


def conv_body(side, first, rank_ref, *refs):
    n = 1 if first else 8
    slices = refs[:n]
    (kn_in, ltm_ref, vec_ref, before_ref, after_ref,
     pad_out, hid_out, xhat_out, rs_ref, mate_ref, keep_ref,
     pad_ref, hid_ref, xhat_ref, sp_ref, kn_ref, sems) = refs[n:]
    rank = rank_ref[0]
    kn_copy = pltpu.make_async_copy(kn_in, kn_ref, sems.at[0])
    kn_copy.start()
    ch, hc = pad_ref.shape[2], hid_ref.shape[1]
    rows = hid_ref.shape[0]
    plane = rows // side
    nf = plane // side
    step = plane // 2
    clear_borders(pad_ref, side, plane, nf)
    if first:
        for i in range(side):
            pad_ref[i + 1, nf : nf + plane] = slices[0][i * plane : (i + 1) * plane]
    else:
        def place(k, carry):
            for q, odd, a_ref, b_ref in by_rank(slices, rank):
                top, bottom = halves(odd, a_ref[chunk(k, step), :], b_ref[chunk(k, step), :])
                lanes = pl.ds(pl.multiple_of(128 * q, 128), 128)
                for piece, kk in ((top, k), (bottom, k + side)):
                    at = nf + lax.rem(kk, 2) * step
                    pad_ref[1 + kk // 2, pl.ds(pl.multiple_of(at, 16), step), lanes] = piece
            return carry

        lax.fori_loop(0, side, place, 0, unroll=True)
    pad_copy = pltpu.make_async_copy(pad_ref, pad_out, sems.at[1])
    pad_copy.start()
    kn_copy.wait()

    def conv(i, total):
        acc = jnp.zeros((plane, hc), F32)
        for t in range(9):
            r, c = t // 3, t % 3
            acc += nn(pad_ref[i + r, c * nf : c * nf + plane, :], kn_ref[t])
        sp_ref[i] = acc
        return total + jnp.sum(acc, axis=0, keepdims=True)

    mean = lax.fori_loop(0, side, conv, jnp.zeros((1, hc), F32), unroll=True) / rows

    def square(i, total):
        cen = sp_ref[i] - mean
        return total + jnp.sum(cen * cen, axis=0, keepdims=True)

    var = lax.fori_loop(0, side, square, jnp.zeros((1, hc), F32), unroll=True) / rows
    rs = lax.rsqrt(var + eps)
    rs_ref[...] = rs
    gain, bias = vec_ref[0:1, :], vec_ref[1:2, :]

    def act(i, carry):
        xhat = (sp_ref[i] - mean) * rs
        xhat_ref[i] = xhat
        v = xhat * gain + bias
        v = v * jax.nn.sigmoid(v)
        sp_ref[i] = v
        hid_ref[chunk(i, plane), :] = v.astype(BF)
        return carry

    lax.fori_loop(0, side, act, 0, unroll=True)
    late = [
        pltpu.make_async_copy(hid_ref, hid_out, sems.at[2]),
        pltpu.make_async_copy(xhat_ref, xhat_out, sems.at[3]),
    ]
    for copy in late:
        copy.start()
    low = lax.broadcasted_iota(jnp.int32, (step, 128), 1) < 64

    def temporal(k, carry):
        pieces = []
        for kk in (k, k + side):
            par = lax.rem(kk, 2)
            h = sp_ref[kk // 2, pl.ds(pl.multiple_of(par * step, 8), step), :]
            at = pl.multiple_of(par * (step % nf), 8)
            pieces.append((
                (pltpu.roll(h, 1, 0) * before_ref[pl.ds(at, step), :]).astype(BF),
                h.astype(BF),
                (pltpu.roll(h, step - 1, 0) * after_ref[pl.ds(at, step), :]).astype(BF),
            ))
        part = sum(
            nn(jnp.concatenate([x, y], axis=0), ltm_ref[t * hc : (t + 1) * hc])
            for t, (x, y) in enumerate(zip(*pieces))
        )
        store_packed(rank, mate_ref, keep_ref, part, k, step, low)
        return carry

    lax.fori_loop(0, side, temporal, 0, unroll=True)
    for copy in [pad_copy] + late:
        copy.wait()


def conv_forward(rank, g, kn, lt, vec, before, after, side, pixels, ch, deps=()):
    hc = vec.shape[1]
    plane = pixels // side
    nf = plane // side
    n = len(g)
    shapes = [
        ((side + 2, plane + 2 * nf, ch), BF),
        ((pixels, hc), BF),
        ((side, plane, hc), F32),
    ]
    outs = [jax.ShapeDtypeStruct(*s) for s in shapes] + [
        jax.ShapeDtypeStruct((1, hc), F32),
        jax.ShapeDtypeStruct((4, pixels // 2, 128), BF),
        jax.ShapeDtypeStruct((4, pixels // 2, 128), BF),
    ]
    scratch = [pltpu.VMEM(*s) for s in shapes] + [
        pltpu.VMEM((side, plane, hc), F32),
        pltpu.VMEM((9, ch, hc), BF),
        pltpu.SemaphoreType.DMA((4,)),
    ]
    flops = 2 * pixels * hc * 12 * ch
    return call(functools.partial(conv_body, side, n == 1), outs, scratch, flops,
                rank, *g, kn, lt, vec, before, after,
                deps=deps, far=(n + 1,), far_outs=(0, 1, 2))


def fold(v):
    return v + pltpu.roll(v, 64, 1)


def total_of(refs):
    t = refs[0][...].astype(F32)
    for ref in refs[1:]:
        t += ref[...].astype(F32)
    return t


def pair_sum_body(keep_ref, mate_ref, *out_refs):
    for p, ref in enumerate(out_refs):
        ref[...] = (keep_ref[p].astype(F32) + mate_ref[p].astype(F32)).astype(ref.dtype)


def pair_sum(keep, arrived, deps=()):
    shape = keep.shape[1:]
    outs = [jax.ShapeDtypeStruct(shape, BF)] * keep.shape[0]
    return call(pair_sum_body, outs, [], keep.size, keep, arrived, deps=deps)


def out_norm_body(n, has_skip, *refs):
    parts, refs = refs[:n], refs[n:]
    if has_skip:
        vec_ref, skip_ref, xhat_ref, rs_ref, pre_ref, res_ref = refs
    else:
        vec_ref, xhat_ref, rs_ref, pre_ref, res_ref = refs
    t = total_of(parts)
    pixels = 2 * t.shape[0]
    mean = fold(jnp.sum(t, axis=0, keepdims=True)) / pixels
    cen = t - mean
    rs = lax.rsqrt(fold(jnp.sum(cen * cen, axis=0, keepdims=True)) / pixels + eps)
    xhat = cen * rs
    pre = xhat * vec_ref[0:1, :] + vec_ref[1:2, :]
    if has_skip:
        pre = pre + skip_ref[...].astype(F32)
    xhat_ref[...] = xhat
    rs_ref[...] = rs
    pre_ref[...] = pre
    res_ref[...] = (pre * jax.nn.sigmoid(pre)).astype(BF)


def out_norm(parts, vec, skip, deps=()):
    half = parts[0].shape[0]
    outs = [
        jax.ShapeDtypeStruct((half, 128), F32),
        jax.ShapeDtypeStruct((1, 128), F32),
        jax.ShapeDtypeStruct((half, 128), F32),
        jax.ShapeDtypeStruct((half, 128), BF),
    ]
    args = (*parts, vec) + (() if skip is None else (skip,))
    body = functools.partial(out_norm_body, len(parts), skip is not None)
    return call(body, outs, [], half * 128 * 10, *args, deps=deps)


def out_back_body(n, *refs):
    parts, (pre_ref, xhat_ref, rs_ref, vec_ref, dpre_ref, dt_ref, sums_ref) = refs[:n], refs[n:]
    g = total_of(parts)
    pre, xhat = pre_ref[...], xhat_ref[...]
    sig = jax.nn.sigmoid(pre)
    dpre = g * (sig * (1.0 + pre * (1.0 - sig)))
    pixels = 2 * pre.shape[0]
    sb = fold(jnp.sum(dpre, axis=0, keepdims=True))
    sg = fold(jnp.sum(dpre * xhat, axis=0, keepdims=True))
    dpre_ref[...] = dpre.astype(BF)
    scale = vec_ref[0:1, :] * rs_ref[...]
    dt_ref[...] = (scale * (dpre - sb / pixels - xhat * (sg / pixels))).astype(BF)
    sums_ref[0:1, :] = sg
    sums_ref[1:2, :] = sb


def out_back(parts, pre, xhat, rs, vec, deps=()):
    half = pre.shape[0]
    outs = [
        jax.ShapeDtypeStruct((half, 128), BF),
        jax.ShapeDtypeStruct((half, 128), BF),
        jax.ShapeDtypeStruct((2, 128), F32),
    ]
    args = (*parts, pre, xhat, rs, vec)
    return call(functools.partial(out_back_body, len(parts)), outs, [], half * 1280, *args, deps=deps)


def conv_back_body(side, rank_ref, *refs):
    slices, (xhat_in, rs_ref, w_ref, lnt_ref, vec_ref, before_ref, after_ref,
             dt_out, ds_out, sums_ref, mate_ref, keep_ref,
             dt_ref, ds_ref, xhat_ref, dy_ref, pad_ref, ktm_ref, sems) = refs[:8], refs[8:]
    half = slices[0].shape[0]
    rank = rank_ref[0]
    nz, _, width = w_ref.shape
    rows = 2 * half
    plane = rows // side
    nf = plane // side
    step = plane // 2
    hc = ds_ref.shape[1]
    ch = dt_ref.shape[1]
    fetched = [
        pltpu.make_async_copy(
            w_ref.at[z, pl.ds(0, hc)], ktm_ref.at[:, pl.ds(z * width, width)], sems.at[z])
        for z in range(nz)
    ]
    xhat_copy = pltpu.make_async_copy(xhat_in, xhat_ref, sems.at[nz])
    for copy in fetched + [xhat_copy]:
        copy.start()
    clear_borders(pad_ref, side, plane, nf)

    def place(k, carry):
        for q, odd, a_ref, b_ref in by_rank(slices, rank):
            top, bottom = halves(odd, a_ref[chunk(k, step), :], b_ref[chunk(k, step), :])
            lanes = pl.ds(pl.multiple_of(128 * q, 128), 128)
            dt_ref[chunk(k, step), lanes] = top
            dt_ref[pl.ds(pl.multiple_of(half + k * step, 16), step), lanes] = bottom
        return carry

    lax.fori_loop(0, side, place, 0, unroll=True)
    dt_copy = pltpu.make_async_copy(dt_ref, dt_out, sems.at[nz + 1])
    dt_copy.start()
    xhat_copy.wait()
    gain, bias = vec_ref[0:1, :], vec_ref[1:2, :]

    def hidden_grad(i, sums):
        dt = dt_ref[chunk(i, plane), :]
        early = nn(dt, lnt_ref[0]) * before_ref[0:plane, :]
        late = nn(dt, lnt_ref[2]) * after_ref[0:plane, :]
        dh = nn(dt, lnt_ref[1]) + pltpu.roll(early, plane - 1, 0) + pltpu.roll(late, 1, 0)
        xhat = xhat_ref[i]
        v = xhat * gain + bias
        sig = jax.nn.sigmoid(v)
        dy = dh * (sig * (1.0 + v * (1.0 - sig)))
        dy_ref[i] = dy
        return (
            sums[0] + jnp.sum(dy * xhat, axis=0, keepdims=True),
            sums[1] + jnp.sum(dy, axis=0, keepdims=True),
        )

    zero = jnp.zeros((1, hc), F32)
    sg, sb = lax.fori_loop(0, side, hidden_grad, (zero, zero), unroll=True)
    sums_ref[0:1, :] = sg
    sums_ref[1:2, :] = sb
    scale = gain * rs_ref[...]

    def spatial_grad(i, carry):
        ds = (scale * (dy_ref[i] - sb / rows - xhat_ref[i] * (sg / rows))).astype(BF)
        pad_ref[i + 1, nf : nf + plane] = ds
        ds_ref[chunk(i, plane), :] = ds
        return carry

    lax.fori_loop(0, side, spatial_grad, 0, unroll=True)
    ds_copy = pltpu.make_async_copy(ds_ref, ds_out, sems.at[nz + 2])
    ds_copy.start()
    for copy in fetched:
        copy.wait()
    low = lax.broadcasted_iota(jnp.int32, (step, 128), 1) < 64

    def back(k, carry):
        acc = jnp.zeros((2 * step, ch), F32)
        for t in range(9):
            r, c = 2 - t // 3, 2 - t % 3
            pieces = []
            for kk in (k, k + side):
                at = c * nf + lax.rem(kk, 2) * step
                pieces.append(pad_ref[kk // 2 + r, pl.ds(pl.multiple_of(at, 16), step), :])
            acc += nn(jnp.concatenate(pieces, axis=0), ktm_ref[:, t * ch : (t + 1) * ch])
        store_packed(rank, mate_ref, keep_ref, acc, k, step, low)
        return carry

    lax.fori_loop(0, side, back, 0, unroll=True)
    dt_copy.wait()
    ds_copy.wait()


def conv_back(rank, g, xhat, rs, w, lnt, vec, before, after, side, deps=()):
    half = g[0].shape[0]
    hc = vec.shape[1]
    ch = len(g) * 64
    pixels = 2 * half
    plane = pixels // side
    nf = plane // side
    outs = [
        jax.ShapeDtypeStruct((pixels, ch), BF),
        jax.ShapeDtypeStruct((pixels, hc), BF),
        jax.ShapeDtypeStruct((2, hc), F32),
        jax.ShapeDtypeStruct((4, half, 128), BF),
        jax.ShapeDtypeStruct((4, half, 128), BF),
    ]
    scratch = [
        pltpu.VMEM((pixels, ch), BF),
        pltpu.VMEM((pixels, hc), BF),
        pltpu.VMEM((side, plane, hc), F32),
        pltpu.VMEM((side, plane, hc), F32),
        pltpu.VMEM((side + 2, plane + 2 * nf, hc), BF),
        pltpu.VMEM((hc, 9 * ch), BF),
        pltpu.SemaphoreType.DMA((w.shape[0] + 3,)),
    ]
    flops = 2 * pixels * hc * 12 * ch
    return call(functools.partial(conv_back_body, side), outs, scratch, flops,
                rank, *g, xhat, rs, w, lnt, vec, before, after,
                deps=deps, far=(9, 11), far_outs=(0, 1))


def grads_body(side, pad_ref, hid_ref, ds_ref, dt_ref, before_ref, after_ref, mid_ref, out_ref,
               sg_ref, dst_ref, taps_ref, tg_ref, vec_ref):
    ch = pad_ref.shape[2]
    hc = hid_ref.shape[1]
    plane = hid_ref.shape[0] // side
    nf = plane // side
    for i in (0, 1, side + 2, side + 3):
        dst_ref[i] = jnp.zeros(dst_ref.shape[1:], BF)
    for i in range(side):
        at = slice(i * plane, (i + 1) * plane)
        h = hid_ref[at, :].astype(F32)
        taps_ref[i, 0:hc] = (pltpu.roll(h, 1, 0) * before_ref[0:plane, :]).T.astype(BF)
        taps_ref[i, hc : 2 * hc] = h.T.astype(BF)
        taps_ref[i, 2 * hc : 3 * hc] = (pltpu.roll(h, plane - 1, 0) * after_ref[0:plane, :]).T.astype(BF)
        dst_ref[i + 2] = ds_ref[at, :].astype(F32).T.astype(BF)
    tg_ref[0 : 3 * hc, :] = sum(
        nn(taps_ref[i], dt_ref[i * plane : (i + 1) * plane, :]) for i in range(side)
    )
    tg_ref[3 * hc :, :] = jnp.zeros((tg_ref.shape[0] - 3 * hc, ch), F32)
    nz, _, width = sg_ref.shape
    size = 3 * hc // (2 * nz)
    vec_ref[...] = jnp.zeros(vec_ref.shape, F32)
    vec_ref[size : size + 2, 0:hc] = mid_ref[...]
    vec_ref[size + 2 : size + 4, 0:128] = out_ref[...]
    tall = vec_ref.shape[0]
    inside = lax.broadcasted_iota(jnp.int32, (tall, ch), 0) < size
    off = (width // 2) % 128
    for z in range(nz):
        first, second = [
            jnp.where(inside, tg_ref[b * size : b * size + tall, :], vec_ref[...])
            for b in (2 * z, 2 * z + 1)
        ]
        start = width // 2 - off
        sg_ref[z, hc : hc + tall, 0:ch] = first.astype(BF)
        second = pltpu.roll(jnp.concatenate([second, jnp.zeros((tall, 128), F32)], axis=1), off, 1)
        sg_ref[z, hc : hc + tall, start : start + ch + 128] = second.astype(BF)
    for c in range(3):
        acc = sum(
            nn(dst_ref[i : i + 3].reshape(3 * hc, plane), pad_ref[i, c * nf : c * nf + plane, :])
            for i in range(1, side + 1)
        )
        for r in range(3):
            first = (3 * r + c) * ch
            end = first + ch
            at = (2 - r) * hc
            done = 0
            while first < end:
                z = first // width
                last = min(end, (z + 1) * width)
                sg_ref[z, 0:hc, first - z * width : last - z * width] = (
                    acc[at : at + hc, done : done + last - first].astype(BF)
                )
                done += last - first
                first = last


def kernel_grads(pad, hidden, ds, dt, before, after, mid, out, side, shape, deps=()):
    pixels, hc = hidden.shape
    ch = dt.shape[1]
    plane = pixels // side
    outs = [jax.ShapeDtypeStruct(shape, BF)]
    tall = shape[1] - hc
    scratch = [
        pltpu.VMEM((side + 4, hc, plane), BF),
        pltpu.VMEM((side, 3 * hc, plane), BF),
        pltpu.VMEM((3 * hc + tall, ch), F32),
        pltpu.VMEM((tall, ch), F32),
    ]
    flops = 2 * pixels * hc * 12 * ch
    return call(functools.partial(grads_body, side), outs, scratch, flops,
                pad, hidden, ds, dt, before, after, mid, out, deps=deps)[0]


def copy_after_body(v_ref, out_ref):
    out_ref[...] = v_ref[...]


def after_all(v, *deps):
    return call(copy_after_body, [jax.ShapeDtypeStruct(v.shape, v.dtype)], [], v.size, v, deps=deps)[0]


def pack_kernels_body(kt_ref, lt_ref, vec_ref, out_ref, low_ref):
    ranks, _, width = out_ref.shape
    hc = kt_ref.shape[0] // ranks
    blocks = lt_ref.shape[0] // hc
    q = hc // ranks
    low_ref[...] = jnp.zeros(low_ref.shape, F32)
    for r in range(ranks):
        out_ref[r, 0:hc, :] = kt_ref[r * hc : (r + 1) * hc, :]
        for b in range(blocks):
            low_ref[r, b * q : (b + 1) * q, 0 : lt_ref.shape[1]] = (
                lt_ref[b * hc + r * q : b * hc + (r + 1) * q, :]
            )
        low_ref[r, blocks * q : blocks * q + 1, :] = vec_ref[...]
        out_ref[r, hc:, :] = low_ref[r].astype(BF)


def pack_kernels(kt, lt, vec, ranks, tall, deps):
    width = kt.shape[1]
    outs = [jax.ShapeDtypeStruct((ranks, kt.shape[0] // ranks + tall, width), BF)]
    scratch = [pltpu.VMEM((ranks, tall, width), F32)]
    return call(pack_kernels_body, outs, scratch, kt.size * 8, kt, lt, vec, deps=deps)[0]


def call(body, outs, scratch, flops, *args, deps=(), far=(), far_outs=()):
    moved = sum(a.size * a.dtype.itemsize for a in args) + sum(
        o.size * o.dtype.itemsize for o in outs
    )
    n = len(deps)

    def spec(a):
        return pl.BlockSpec(memory_space=pltpu.SMEM if a.dtype == jnp.int32 else pltpu.VMEM)

    return pl.pallas_call(
        lambda *refs: body(*refs[n:]),
        out_shape=outs,
        in_specs=[ANY] * n + [ANY if i in far else spec(a) for i, a in enumerate(args)],
        out_specs=[ANY if i in far_outs else spec(o) for i, o in enumerate(outs)],
        scratch_shapes=scratch,
        compiler_params=pltpu.CompilerParams(vmem_limit_bytes=VMEM_CAP),
        cost_estimate=pl.CostEstimate(flops=flops, bytes_accessed=moved, transcendentals=0),
    )(*deps, *args)


def chunk(i, size):
    return pl.ds(pl.multiple_of(i * size, 16), size)


def clear_borders(pad_ref, side, plane, nf):
    zrow = jnp.zeros(pad_ref.shape[1:], BF)
    pad_ref[0] = zrow
    pad_ref[side + 1] = zrow
    zcol = jnp.zeros((nf, pad_ref.shape[2]), BF)
    for i in range(side):
        pad_ref[i + 1, 0:nf] = zcol
        pad_ref[i + 1, nf + plane : 2 * nf + plane] = zcol


def by_rank(slices, rank):
    odd = lax.rem(rank, 2) == 1
    for p in range(len(slices) // 2):
        a, b = slices[2 * p], slices[2 * p + 1]
        yield lax.bitwise_xor(rank // 2, p), odd, a, b


def halves(odd, own, mate):
    a, b = jnp.where(odd, mate, own), jnp.where(odd, own, mate)
    top = jnp.concatenate([a[:, :64], b[:, :64]], axis=1)
    bottom = jnp.concatenate([a[:, 64:], b[:, 64:]], axis=1)
    return top, bottom


def store_packed(rank, mate_ref, keep_ref, part, k, step, low):
    rows_now = chunk(k, step)
    odd = lax.rem(rank, 2) == 1
    part = part.astype(BF)
    for q in range(keep_ref.shape[0]):
        x = part[:step, 128 * q : 128 * q + 128]
        y = part[step:, 128 * q : 128 * q + 128]
        even_slice = jnp.concatenate([x[:, :64], y[:, :64]], axis=1)
        odd_slice = jnp.concatenate([x[:, 64:], y[:, 64:]], axis=1)
        p = lax.bitwise_xor(rank // 2, q)
        keep_ref[p, rows_now, :] = jnp.where(odd, odd_slice, even_slice)
        mate_ref[p, rows_now, :] = jnp.where(odd, even_slice, odd_slice)


def fetch_kernels(w_ref, ktm_ref, lw_ref, sems):
    nz, _, width = w_ref.shape
    hc = ktm_ref.shape[0]
    copies = []
    for z in range(nz):
        copies.append(pltpu.make_async_copy(
            w_ref.at[z, pl.ds(0, hc)], ktm_ref.at[:, pl.ds(z * width, width)], sems.at[2 * z]))
        copies.append(pltpu.make_async_copy(
            w_ref.at[z, pl.ds(hc, lw_ref.shape[1])], lw_ref.at[z], sems.at[2 * z + 1]))
    for copy in copies:
        copy.start()
    return copies


def join_temporal(lw_ref, lf_ref, ltm_ref):
    ch = ltm_ref.shape[1]
    width = lw_ref.shape[2] // 2
    count = 2 * lw_ref.shape[0]
    size = ltm_ref.shape[0] // count
    for z in range(lw_ref.shape[0]):
        first = lw_ref[z, :, 0:ch].astype(F32)
        off = width % 128
        second = lw_ref[z, :, width - off : width - off + ch + 128].astype(F32)
        second = pltpu.roll(second, ch + 128 - off, 1)[:, 0:ch]
        for b, block in ((2 * z, first), (2 * z + 1, second)):
            lf_ref[b * size : b * size + block.shape[0], :] = block
    ltm_ref[...] = lf_ref[0 : ltm_ref.shape[0], :].astype(BF)


def prepare_body(w_ref, kn_out, l_out, lt_out, rows_out, ktm_ref, lw_ref, lf_ref, sems):
    hc, ch = ktm_ref.shape[0], l_out.shape[1]
    for copy in fetch_kernels(w_ref, ktm_ref, lw_ref, sems):
        copy.wait()
    for t in range(9):
        kn_out[t] = ktm_ref[:, t * ch : (t + 1) * ch].astype(F32).T.astype(BF)
    join_temporal(lw_ref, lf_ref, l_out)
    rows_out[...] = lw_ref[:, lw_ref.shape[1] - rows_out.shape[1] :, :]
    for t in range(3):
        lt_out[t] = lf_ref[t * hc : (t + 1) * hc].T.astype(BF)


def prepare(w, hc, ch, deps=()):
    outs = [
        jax.ShapeDtypeStruct((9, ch, hc), BF),
        jax.ShapeDtypeStruct((3 * hc, ch), BF),
        jax.ShapeDtypeStruct((3, ch, hc), BF),
        jax.ShapeDtypeStruct((w.shape[0], 16, w.shape[2]), BF),
    ]
    tall = w.shape[1] - hc
    scratch = [
        pltpu.VMEM((hc, 9 * ch), BF),
        pltpu.VMEM((w.shape[0], tall, w.shape[2]), BF),
        pltpu.VMEM((3 * hc + tall, ch), F32),
        pltpu.SemaphoreType.DMA((2 * w.shape[0],)),
    ]
    return call(prepare_body, outs, scratch, 2 * w.size * 512, w, deps=deps, far=(0,))


def conv_body(side, first, rank_ref, *refs):
    n = 1 if first else 8
    slices = refs[:n]
    (kn_in, ltm_ref, vec_ref, before_ref, after_ref,
     pad_out, hid_out, xhat_out, rs_ref, mate_ref, keep_ref,
     pad_ref, hid_ref, xhat_ref, sp_ref, kn_ref, sems) = refs[n:]
    rank = rank_ref[0]
    kn_copy = pltpu.make_async_copy(kn_in, kn_ref, sems.at[0])
    kn_copy.start()
    ch, hc = pad_ref.shape[2], hid_ref.shape[1]
    rows = hid_ref.shape[0]
    plane = rows // side
    nf = plane // side
    step = plane // 2
    clear_borders(pad_ref, side, plane, nf)
    if first:
        for i in range(side):
            pad_ref[i + 1, nf : nf + plane] = slices[0][i * plane : (i + 1) * plane]
    else:
        def place(k, carry):
            for q, odd, a_ref, b_ref in by_rank(slices, rank):
                top, bottom = halves(odd, a_ref[chunk(k, step), :], b_ref[chunk(k, step), :])
                lanes = pl.ds(pl.multiple_of(128 * q, 128), 128)
                for piece, kk in ((top, k), (bottom, k + side)):
                    at = nf + lax.rem(kk, 2) * step
                    pad_ref[1 + kk // 2, pl.ds(pl.multiple_of(at, 16), step), lanes] = piece
            return carry

        lax.fori_loop(0, side, place, 0, unroll=True)
    pad_copy = pltpu.make_async_copy(pad_ref, pad_out, sems.at[1])
    pad_copy.start()
    kn_copy.wait()

    def conv(i, total):
        acc = jnp.zeros((plane, hc), F32)
        for t in range(9):
            r, c = t // 3, t % 3
            acc += nn(pad_ref[i + r, c * nf : c * nf + plane, :], kn_ref[t])
        sp_ref[i] = acc
        return total + jnp.sum(acc, axis=0, keepdims=True)

    mean = lax.fori_loop(0, side, conv, jnp.zeros((1, hc), F32), unroll=True) / rows

    def square(i, total):
        cen = sp_ref[i] - mean
        return total + jnp.sum(cen * cen, axis=0, keepdims=True)

    var = lax.fori_loop(0, side, square, jnp.zeros((1, hc), F32), unroll=True) / rows
    rs = lax.rsqrt(var + eps)
    rs_ref[...] = rs
    gain, bias = vec_ref[0:1, :], vec_ref[1:2, :]

    def act(i, carry):
        xhat = (sp_ref[i] - mean) * rs
        xhat_ref[i] = xhat
        v = xhat * gain + bias
        v = v * jax.nn.sigmoid(v)
        sp_ref[i] = v
        hid_ref[chunk(i, plane), :] = v.astype(BF)
        return carry

    lax.fori_loop(0, side, act, 0, unroll=True)
    late = [
        pltpu.make_async_copy(hid_ref, hid_out, sems.at[2]),
        pltpu.make_async_copy(xhat_ref, xhat_out, sems.at[3]),
    ]
    for copy in late:
        copy.start()
    low = lax.broadcasted_iota(jnp.int32, (step, 128), 1) < 64

    def temporal(k, carry):
        pieces = []
        for kk in (k, k + side):
            par = lax.rem(kk, 2)
            h = sp_ref[kk // 2, pl.ds(pl.multiple_of(par * step, 8), step), :]
            at = pl.multiple_of(par * (step % nf), 8)
            pieces.append((
                (pltpu.roll(h, 1, 0) * before_ref[pl.ds(at, step), :]).astype(BF),
                h.astype(BF),
                (pltpu.roll(h, step - 1, 0) * after_ref[pl.ds(at, step), :]).astype(BF),
            ))
        part = sum(
            nn(jnp.concatenate([x, y], axis=0), ltm_ref[t * hc : (t + 1) * hc])
            for t, (x, y) in enumerate(zip(*pieces))
        )
        store_packed(rank, mate_ref, keep_ref, part, k, step, low)
        return carry

    lax.fori_loop(0, side, temporal, 0, unroll=True)
    for copy in [pad_copy] + late:
        copy.wait()


def conv_forward(rank, g, kn, lt, vec, before, after, side, pixels, ch, deps=()):
    hc = vec.shape[1]
    plane = pixels // side
    nf = plane // side
    n = len(g)
    shapes = [
        ((side + 2, plane + 2 * nf, ch), BF),
        ((pixels, hc), BF),
        ((side, plane, hc), F32),
    ]
    outs = [jax.ShapeDtypeStruct(*s) for s in shapes] + [
        jax.ShapeDtypeStruct((1, hc), F32),
        jax.ShapeDtypeStruct((4, pixels // 2, 128), BF),
        jax.ShapeDtypeStruct((4, pixels // 2, 128), BF),
    ]
    scratch = [pltpu.VMEM(*s) for s in shapes] + [
        pltpu.VMEM((side, plane, hc), F32),
        pltpu.VMEM((9, ch, hc), BF),
        pltpu.SemaphoreType.DMA((4,)),
    ]
    flops = 2 * pixels * hc * 12 * ch
    return call(functools.partial(conv_body, side, n == 1), outs, scratch, flops,
                rank, *g, kn, lt, vec, before, after,
                deps=deps, far=(n + 1,), far_outs=(0, 1, 2))


def fold(v):
    return v + pltpu.roll(v, 64, 1)


def total_of(refs):
    t = refs[0][...].astype(F32)
    for ref in refs[1:]:
        t += ref[...].astype(F32)
    return t


def pair_sum_body(keep_ref, mate_ref, *out_refs):
    for p, ref in enumerate(out_refs):
        ref[...] = (keep_ref[p].astype(F32) + mate_ref[p].astype(F32)).astype(ref.dtype)


def pair_sum(keep, arrived, deps=()):
    shape = keep.shape[1:]
    outs = [jax.ShapeDtypeStruct(shape, BF)] * keep.shape[0]
    return call(pair_sum_body, outs, [], keep.size, keep, arrived, deps=deps)


def out_norm_body(n, has_skip, *refs):
    parts, refs = refs[:n], refs[n:]
    if has_skip:
        vec_ref, skip_ref, xhat_ref, rs_ref, pre_ref, res_ref = refs
    else:
        vec_ref, xhat_ref, rs_ref, pre_ref, res_ref = refs
    t = total_of(parts)
    pixels = 2 * t.shape[0]
    mean = fold(jnp.sum(t, axis=0, keepdims=True)) / pixels
    cen = t - mean
    rs = lax.rsqrt(fold(jnp.sum(cen * cen, axis=0, keepdims=True)) / pixels + eps)
    xhat = cen * rs
    pre = xhat * vec_ref[0:1, :] + vec_ref[1:2, :]
    if has_skip:
        pre = pre + skip_ref[...].astype(F32)
    xhat_ref[...] = xhat
    rs_ref[...] = rs
    pre_ref[...] = pre
    res_ref[...] = (pre * jax.nn.sigmoid(pre)).astype(BF)


def out_norm(parts, vec, skip, deps=()):
    half = parts[0].shape[0]
    outs = [
        jax.ShapeDtypeStruct((half, 128), F32),
        jax.ShapeDtypeStruct((1, 128), F32),
        jax.ShapeDtypeStruct((half, 128), F32),
        jax.ShapeDtypeStruct((half, 128), BF),
    ]
    args = (*parts, vec) + (() if skip is None else (skip,))
    body = functools.partial(out_norm_body, len(parts), skip is not None)
    return call(body, outs, [], half * 128 * 10, *args, deps=deps)


def out_back_body(n, *refs):
    parts, (pre_ref, xhat_ref, rs_ref, vec_ref, dpre_ref, dt_ref, sums_ref) = refs[:n], refs[n:]
    g = total_of(parts)
    pre, xhat = pre_ref[...], xhat_ref[...]
    sig = jax.nn.sigmoid(pre)
    dpre = g * (sig * (1.0 + pre * (1.0 - sig)))
    pixels = 2 * pre.shape[0]
    sb = fold(jnp.sum(dpre, axis=0, keepdims=True))
    sg = fold(jnp.sum(dpre * xhat, axis=0, keepdims=True))
    dpre_ref[...] = dpre.astype(BF)
    scale = vec_ref[0:1, :] * rs_ref[...]
    dt_ref[...] = (scale * (dpre - sb / pixels - xhat * (sg / pixels))).astype(BF)
    sums_ref[0:1, :] = sg
    sums_ref[1:2, :] = sb


def out_back(parts, pre, xhat, rs, vec, deps=()):
    half = pre.shape[0]
    outs = [
        jax.ShapeDtypeStruct((half, 128), BF),
        jax.ShapeDtypeStruct((half, 128), BF),
        jax.ShapeDtypeStruct((2, 128), F32),
    ]
    args = (*parts, pre, xhat, rs, vec)
    return call(functools.partial(out_back_body, len(parts)), outs, [], half * 1280, *args, deps=deps)


def conv_back_body(side, rank_ref, *refs):
    slices, (xhat_in, rs_ref, w_ref, lnt_ref, vec_ref, before_ref, after_ref,
             dt_out, ds_out, sums_ref, mate_ref, keep_ref,
             dt_ref, ds_ref, xhat_ref, dy_ref, pad_ref, ktm_ref, sems) = refs[:8], refs[8:]
    half = slices[0].shape[0]
    rank = rank_ref[0]
    nz, _, width = w_ref.shape
    rows = 2 * half
    plane = rows // side
    nf = plane // side
    step = plane // 2
    hc = ds_ref.shape[1]
    ch = dt_ref.shape[1]
    fetched = [
        pltpu.make_async_copy(
            w_ref.at[z, pl.ds(0, hc)], ktm_ref.at[:, pl.ds(z * width, width)], sems.at[z])
        for z in range(nz)
    ]
    xhat_copy = pltpu.make_async_copy(xhat_in, xhat_ref, sems.at[nz])
    for copy in fetched + [xhat_copy]:
        copy.start()
    clear_borders(pad_ref, side, plane, nf)

    def place(k, carry):
        for q, odd, a_ref, b_ref in by_rank(slices, rank):
            top, bottom = halves(odd, a_ref[chunk(k, step), :], b_ref[chunk(k, step), :])
            lanes = pl.ds(pl.multiple_of(128 * q, 128), 128)
            dt_ref[chunk(k, step), lanes] = top
            dt_ref[pl.ds(pl.multiple_of(half + k * step, 16), step), lanes] = bottom
        return carry

    lax.fori_loop(0, side, place, 0, unroll=True)
    dt_copy = pltpu.make_async_copy(dt_ref, dt_out, sems.at[nz + 1])
    dt_copy.start()
    xhat_copy.wait()
    gain, bias = vec_ref[0:1, :], vec_ref[1:2, :]

    def hidden_grad(i, sums):
        dt = dt_ref[chunk(i, plane), :]
        early = nn(dt, lnt_ref[0]) * before_ref[0:plane, :]
        late = nn(dt, lnt_ref[2]) * after_ref[0:plane, :]
        dh = nn(dt, lnt_ref[1]) + pltpu.roll(early, plane - 1, 0) + pltpu.roll(late, 1, 0)
        xhat = xhat_ref[i]
        v = xhat * gain + bias
        sig = jax.nn.sigmoid(v)
        dy = dh * (sig * (1.0 + v * (1.0 - sig)))
        dy_ref[i] = dy
        return (
            sums[0] + jnp.sum(dy * xhat, axis=0, keepdims=True),
            sums[1] + jnp.sum(dy, axis=0, keepdims=True),
        )

    zero = jnp.zeros((1, hc), F32)
    sg, sb = lax.fori_loop(0, side, hidden_grad, (zero, zero), unroll=True)
    sums_ref[0:1, :] = sg
    sums_ref[1:2, :] = sb
    scale = gain * rs_ref[...]

    def spatial_grad(i, carry):
        ds = (scale * (dy_ref[i] - sb / rows - xhat_ref[i] * (sg / rows))).astype(BF)
        pad_ref[i + 1, nf : nf + plane] = ds
        ds_ref[chunk(i, plane), :] = ds
        return carry

    lax.fori_loop(0, side, spatial_grad, 0, unroll=True)
    ds_copy = pltpu.make_async_copy(ds_ref, ds_out, sems.at[nz + 2])
    ds_copy.start()
    for copy in fetched:
        copy.wait()
    low = lax.broadcasted_iota(jnp.int32, (step, 128), 1) < 64

    def back(k, carry):
        acc = jnp.zeros((2 * step, ch), F32)
        for t in range(9):
            r, c = 2 - t // 3, 2 - t % 3
            pieces = []
            for kk in (k, k + side):
                at = c * nf + lax.rem(kk, 2) * step
                pieces.append(pad_ref[kk // 2 + r, pl.ds(pl.multiple_of(at, 16), step), :])
            acc += nn(jnp.concatenate(pieces, axis=0), ktm_ref[:, t * ch : (t + 1) * ch])
        store_packed(rank, mate_ref, keep_ref, acc, k, step, low)
        return carry

    lax.fori_loop(0, side, back, 0, unroll=True)
    dt_copy.wait()
    ds_copy.wait()


def conv_back(rank, g, xhat, rs, w, lnt, vec, before, after, side, deps=()):
    half = g[0].shape[0]
    hc = vec.shape[1]
    ch = len(g) * 64
    pixels = 2 * half
    plane = pixels // side
    nf = plane // side
    outs = [
        jax.ShapeDtypeStruct((pixels, ch), BF),
        jax.ShapeDtypeStruct((pixels, hc), BF),
        jax.ShapeDtypeStruct((2, hc), F32),
        jax.ShapeDtypeStruct((4, half, 128), BF),
        jax.ShapeDtypeStruct((4, half, 128), BF),
    ]
    scratch = [
        pltpu.VMEM((pixels, ch), BF),
        pltpu.VMEM((pixels, hc), BF),
        pltpu.VMEM((side, plane, hc), F32),
        pltpu.VMEM((side, plane, hc), F32),
        pltpu.VMEM((side + 2, plane + 2 * nf, hc), BF),
        pltpu.VMEM((hc, 9 * ch), BF),
        pltpu.SemaphoreType.DMA((w.shape[0] + 3,)),
    ]
    flops = 2 * pixels * hc * 12 * ch
    return call(functools.partial(conv_back_body, side), outs, scratch, flops,
                rank, *g, xhat, rs, w, lnt, vec, before, after,
                deps=deps, far=(9, 11), far_outs=(0, 1))


def grads_body(side, pad_ref, hid_ref, ds_ref, dt_ref, before_ref, after_ref, mid_ref, out_ref,
               sg_ref, dst_ref, taps_ref, tg_ref, vec_ref):
    ch = pad_ref.shape[2]
    hc = hid_ref.shape[1]
    plane = hid_ref.shape[0] // side
    nf = plane // side
    for i in (0, 1, side + 2, side + 3):
        dst_ref[i] = jnp.zeros(dst_ref.shape[1:], BF)
    for i in range(side):
        at = slice(i * plane, (i + 1) * plane)
        h = hid_ref[at, :].astype(F32)
        taps_ref[i, 0:hc] = (pltpu.roll(h, 1, 0) * before_ref[0:plane, :]).T.astype(BF)
        taps_ref[i, hc : 2 * hc] = h.T.astype(BF)
        taps_ref[i, 2 * hc : 3 * hc] = (pltpu.roll(h, plane - 1, 0) * after_ref[0:plane, :]).T.astype(BF)
        dst_ref[i + 2] = ds_ref[at, :].astype(F32).T.astype(BF)
    tg_ref[0 : 3 * hc, :] = sum(
        nn(taps_ref[i], dt_ref[i * plane : (i + 1) * plane, :]) for i in range(side)
    )
    tg_ref[3 * hc :, :] = jnp.zeros((tg_ref.shape[0] - 3 * hc, ch), F32)
    nz, _, width = sg_ref.shape
    size = 3 * hc // (2 * nz)
    vec_ref[...] = jnp.zeros(vec_ref.shape, F32)
    vec_ref[size : size + 2, 0:hc] = mid_ref[...]
    vec_ref[size + 2 : size + 4, 0:128] = out_ref[...]
    tall = vec_ref.shape[0]
    inside = lax.broadcasted_iota(jnp.int32, (tall, ch), 0) < size
    off = (width // 2) % 128
    for z in range(nz):
        first, second = [
            jnp.where(inside, tg_ref[b * size : b * size + tall, :], vec_ref[...])
            for b in (2 * z, 2 * z + 1)
        ]
        start = width // 2 - off
        sg_ref[z, hc : hc + tall, 0:ch] = first.astype(BF)
        second = pltpu.roll(jnp.concatenate([second, jnp.zeros((tall, 128), F32)], axis=1), off, 1)
        sg_ref[z, hc : hc + tall, start : start + ch + 128] = second.astype(BF)
    for c in range(3):
        acc = sum(
            nn(dst_ref[i : i + 3].reshape(3 * hc, plane), pad_ref[i, c * nf : c * nf + plane, :])
            for i in range(1, side + 1)
        )
        for r in range(3):
            first = (3 * r + c) * ch
            end = first + ch
            at = (2 - r) * hc
            done = 0
            while first < end:
                z = first // width
                last = min(end, (z + 1) * width)
                sg_ref[z, 0:hc, first - z * width : last - z * width] = (
                    acc[at : at + hc, done : done + last - first].astype(BF)
                )
                done += last - first
                first = last


def kernel_grads(pad, hidden, ds, dt, before, after, mid, out, side, shape, deps=()):
    pixels, hc = hidden.shape
    ch = dt.shape[1]
    plane = pixels // side
    outs = [jax.ShapeDtypeStruct(shape, BF)]
    tall = shape[1] - hc
    scratch = [
        pltpu.VMEM((side + 4, hc, plane), BF),
        pltpu.VMEM((side, 3 * hc, plane), BF),
        pltpu.VMEM((3 * hc + tall, ch), F32),
        pltpu.VMEM((tall, ch), F32),
    ]
    flops = 2 * pixels * hc * 12 * ch
    return call(functools.partial(grads_body, side), outs, scratch, flops,
                pad, hidden, ds, dt, before, after, mid, out, deps=deps)[0]


def copy_after_body(v_ref, out_ref):
    out_ref[...] = v_ref[...]


def after_all(v, *deps):
    return call(copy_after_body, [jax.ShapeDtypeStruct(v.shape, v.dtype)], [], v.size, v, deps=deps)[0]


def pack_kernels_body(kt_ref, lt_ref, vec_ref, out_ref, low_ref):
    ranks, _, width = out_ref.shape
    hc = kt_ref.shape[0] // ranks
    blocks = lt_ref.shape[0] // hc
    q = hc // ranks
    low_ref[...] = jnp.zeros(low_ref.shape, F32)
    for r in range(ranks):
        out_ref[r, 0:hc, :] = kt_ref[r * hc : (r + 1) * hc, :]
        for b in range(blocks):
            low_ref[r, b * q : (b + 1) * q, 0 : lt_ref.shape[1]] = (
                lt_ref[b * hc + r * q : b * hc + (r + 1) * q, :]
            )
        low_ref[r, blocks * q : blocks * q + 1, :] = vec_ref[...]
        out_ref[r, hc:, :] = low_ref[r].astype(BF)


def pack_kernels(kt, lt, vec, ranks, tall, deps):
    width = kt.shape[1]
    outs = [jax.ShapeDtypeStruct((ranks, kt.shape[0] // ranks + tall, width), BF)]
    scratch = [pltpu.VMEM((ranks, tall, width), F32)]
    return call(pack_kernels_body, outs, scratch, kt.size * 8, kt, lt, vec, deps=deps)[0]


def hop(v, k):
    n = 1
    for name in EVERY:
        n *= lax.axis_size(name)
    return lax.ppermute(v, EVERY, [(i, i ^ k) for i in range(n)])


def plane_gather(v, aside=()):
    got = {0: v}
    for k in (6, 2, 4):
        got[k] = hop(v, k)
    got[1] = hop(after_all(v, *aside) if aside else v, 1)
    for k in (2, 4, 6):
        got[k ^ 1] = hop(got[k], 1)
    return [got[k] for k in range(8)]


def plane_reduce(mate, keep, deps=()):
    sums = pair_sum(keep, hop(mate, 1), deps)
    arrived = {k: hop(sums[k // 2], k) for k in (6, 2, 4)}
    return [sums[0], arrived[2], arrived[4], arrived[6]]


def on_device(frames, cot, starts, ks, ktm, mg, mb, og, ob):
    nz, n_rank, n_seg = lax.axis_size("z"), 8, 4
    n_dp = nz * 2
    fr, side, ch = frames.shape[0], frames.shape[1], frames.shape[3]
    area = side * side
    hid = ks.shape[2]
    hc, cc = hid // n_rank, ch // n_rank
    q = hc // n_rank
    rank = lax.axis_index(PLANE)
    rank_now = rank.astype(jnp.int32).reshape(1)
    d_index = lax.axis_index(("z", "y"))
    nf = n_dp * fr
    pixels = area * nf
    half = pixels // 2

    def keeper(d, s):
        v = (d // 2) ^ s
        return (d % 2) * 4 + (v % 2) * 2 + v // 2

    to_plane = [
        (d * n_seg + s, s * n_rank + keeper(d, s)) for d in range(n_dp) for s in range(n_seg)
    ]
    from_plane = [(b, a) for a, b in to_plane]
    rows = fr * area
    flag_row = jnp.pad(starts.astype(BF)[None], ((0, 11), (0, ch - fr)))
    lead = rows + 12
    moving = jnp.concatenate([frames.reshape(rows, ch), flag_row, cot.reshape(rows, ch)], axis=0)
    moving = lax.ppermute(moving, EVERY, to_plane)

    perm = (jnp.arange(hid).reshape(n_rank, n_rank, q).transpose(1, 0, 2).reshape(hid)[:, None]
            == jnp.arange(hid)[None, :]).astype(BF)
    kt = lax.dot_general(perm, ks[0].astype(BF), (((1,), (1,)), ((), ())),
                         preferred_element_type=F32).astype(BF)
    lrows, width = ktm.shape[1] // n_rank, ks.shape[1]
    tall = -(-(lrows + 4) // 16) * 16
    extra = jnp.concatenate([mg, mb, og, ob], axis=1)
    extra = jnp.pad(extra, ((0, 0), (0, width - extra.shape[1])))
    w = pack_kernels(kt, ktm[0], extra, n_rank, tall, deps=(moving,))
    w = lax.all_to_all(w, PLANE, 0, 0)
    here = w
    high = hc + tall

    w = w.reshape(2, n_seg, high, width).transpose(1, 2, 0, 3).reshape(n_seg, high, 2 * width)
    ws = [lax.all_gather(w[s], "z", axis=0) for s in range(n_seg)]

    group = 7
    own = moving[lead:].reshape(group, rows // group, n_rank, cc).transpose(2, 1, 0, 3)
    own = own.reshape(n_rank, rows // group, group * cc)
    own = jnp.pad(own, ((0, 0), (0, 4), (0, ch - group * cc)))
    own = jnp.concatenate([jnp.broadcast_to(moving[:lead], (n_rank, lead, ch)), own], axis=1)
    gathered = lax.all_to_all(after_all(own, here), PLANE, 0, 0)


    def norm_rows(rows_now):
        row = rows_now[:, (lrows - tall) % 16].reshape(n_dp, width).astype(F32)
        mid = jnp.stack([
            lax.dynamic_slice_in_dim(row[:, i * hc : (i + 1) * hc], rank * q, q, axis=1).reshape(hc)
            for i in range(2)])
        own = lax.dynamic_index_in_dim(row, rank, 0, keepdims=False)
        out = jnp.stack([
            jnp.tile(own[2 * hc + i * cc : 2 * hc + (i + 1) * cc], 2) for i in range(2)])
        return mid, out

    def by_pixel(v):
        width = v.shape[2]
        v = v.reshape(n_rank * fr, area, width).transpose(1, 0, 2)
        return v.reshape(pixels, width)

    def packed(v):
        return jnp.concatenate([v[:half], v[half:]], axis=1)

    a0 = by_pixel(gathered[:, :rows])
    flags = gathered[:, rows, :fr].reshape(nf) > 0.5
    slot = jnp.arange(nf) % fr
    before = jnp.where(flags | (slot == 0), 0.0, 1.0)
    after = jnp.where(jnp.roll(flags, -1) | (slot == fr - 1), 0.0, 1.0)
    spread = (side * nf + nf, hc)
    before = jnp.broadcast_to(jnp.tile(before, side + 1)[:, None], spread)
    after = jnp.broadcast_to(jnp.tile(after, side + 1)[:, None], spread)
    skip = packed(lax.dynamic_slice_in_dim(a0, rank * cc, cc, axis=1))

    def across(*slices):
        n = len(slices)
        v = jnp.stack([jnp.concatenate([v[:, :cc], v[:, cc:]], axis=0) for v in slices])
        v = v.reshape(n, area, n_rank, fr, cc).transpose(2, 0, 1, 3, 4).reshape(n_rank, n * rows, cc)
        return lax.all_to_all(v, PLANE, 0, 0)

    def home(v):
        n = v.shape[1] // rows
        v = v.transpose(1, 0, 2).reshape(n * rows, ch)
        v = lax.ppermute(v, EVERY, from_plane).reshape(n, area, fr, ch).transpose(0, 2, 1, 3)
        return v.reshape(n, *frames.shape)

    saved = []
    g = [a0]
    ready = prepare(ws[0], hc, ch)
    for s in range(n_seg):
        kn, lt, lnt, rows_now = ready
        mid, out = norm_rows(rows_now)
        pad, hidden, xm, rm, mate, keep = conv_forward(
            rank_now, g, kn, lt, mid, before, after, side, pixels, ch)
        parts = plane_reduce(mate, keep)
        xo, ro, pre, res = out_norm(parts, out, skip if s % 2 == 1 else None)
        saved.append((pad, hidden, xm, rm, xo, ro, pre, lnt, mid, out))
        if s % 2 == 1:
            skip = res
        if s < n_seg - 1:
            ready = prepare(ws[s + 1], hc, ch, deps=(res,))
            g = plane_gather(res, ready[:1])
    cot_own = gathered[:, lead : lead + rows // group, : group * cc]
    cot_own = cot_own.reshape(n_rank, rows // group, group, cc).transpose(0, 2, 1, 3)
    cot_own = packed(by_pixel(cot_own.reshape(n_rank, rows, cc)))

    parts = [cot_own]
    skip_grad = None

    grads, raw = [], None
    for s in reversed(range(n_seg)):
        pad, hidden, xm, rm, xo, ro, pre, lnt, mid, out = saved[s]
        if s == 1:
            parts = parts + [skip_grad]
        deps = () if raw is None else (raw, *grads[len(grads) - 1 :])
        dpre, dt, osum = out_back(parts, pre, xo, ro, out, deps=deps)
        slices = plane_gather(dt)
        if raw is not None:
            begun = dt if s == 0 else slices[6]
            grads.append(lax.psum_scatter(after_all(raw, begun), "z", scatter_dimension=0))
        if s % 2 == 1:
            skip_grad = dpre
        dtf, ds, msum, mate, keep = conv_back(
            rank_now, slices, xm, rm, ws[s], lnt, mid, before, after, side)
        if s > 0:
            parts = plane_reduce(mate, keep)
        raw = kernel_grads(pad, hidden, ds, dtf, before, after, msum, osum, side, ws[s].shape,
                           deps=parts[:1] if s > 0 else ())
    last = lax.psum_scatter(raw, "z", scatter_dimension=0)
    parts = plane_reduce(mate, keep, deps=(raw,))

    da = sum(p.astype(F32) for p in parts) + skip_grad.astype(F32)
    home_now = home(across(res, da.astype(BF)))
    output, frames_grad = home_now[0], home_now[1].astype(F32)

    def by_row(v):
        return v.reshape(high, 2, width).transpose(1, 0, 2)

    g = jnp.stack([by_row(v) for v in [last] + grads[::-1]], axis=1).reshape(n_rank, high, width)
    g = lax.all_to_all(g, PLANE, 0, 0)
    space_grad = lax.dot_general(g[:, :hc].reshape(hid, width), perm, (((0,), (0,)), ((), ())),
                                 preferred_element_type=F32)
    tg = g[:, hc : hc + lrows, :ch].reshape(n_rank, -1, q, ch)
    time_grad = tg.transpose(1, 0, 2, 3).reshape(-1, ch).astype(F32)
    sums = g[:, hc + lrows : hc + lrows + 4].astype(F32)

    def mid_own(v):
        return lax.dynamic_slice_in_dim(v[:, :hc], d_index * q, q, axis=1).reshape(1, hc)

    own = lax.dynamic_index_in_dim(sums, d_index, 0, keepdims=False)
    return (
        output,
        frames_grad,
        space_grad[None],
        time_grad[None],
        mid_own(sums[:, 0]),
        mid_own(sums[:, 1]),
        own[2:3, :cc],
        own[3:4, :cc],
    )


def from_behind(value, axis, steps):
    count = lax.axis_size(axis)
    leading, last = (max(0, -steps), min(count, count - steps))
    return lax.ppermute(value, axis, [(source, source + steps) for source in range(leading, last)])


def space_apply(current, kernel):
    frame_side = current.shape[1]
    padded = jnp.pad(current, ((0, 0), (1, 1), (1, 1), (0, 0)))
    stacked = jnp.concatenate(
        [
            padded[:, row_shift : row_shift + frame_side, col_shift : col_shift + frame_side, :]
            for row_shift in range(3)
            for col_shift in range(3)
        ],
        axis=-1,
    )
    return (
        stacked,
        jnp.einsum("fijc,co->fijo", stacked, kernel, preferred_element_type=jnp.float32),
    )


def space_back(gradient, kernel):
    frame_side = gradient.shape[1]
    channels = kernel.shape[0] // 9
    spread = jnp.einsum("fijo,co->fijc", gradient, kernel, preferred_element_type=jnp.float32)
    total = jnp.zeros((gradient.shape[0], frame_side + 2, frame_side + 2, channels), jnp.float32)
    for tap_index in range(9):
        row_shift = tap_index // 3
        col_shift = tap_index % 3
        piece_now = spread[..., tap_index * channels : (tap_index + 1) * channels]
        total = total + jnp.pad(
            piece_now, ((0, 0), (row_shift, 2 - row_shift), (col_shift, 2 - col_shift), (0, 0))
        )
    return total[:, 1 : frame_side + 1, 1 : frame_side + 1, :]


def time_apply(current, kernel, before_mask, after_mask):
    blanks = jnp.zeros_like(current[:1])
    earlier = jnp.concatenate([blanks, current[:-1]], axis=0) * before_mask[
        :, None, None, None
    ].astype(current.dtype)
    later = jnp.concatenate([current[1:], blanks], axis=0) * after_mask[:, None, None, None].astype(
        current.dtype
    )
    stacked = jnp.concatenate([earlier, current, later], axis=-1)
    return (
        stacked,
        jnp.einsum("fijc,co->fijo", stacked, kernel, preferred_element_type=jnp.float32),
    )


def time_back(gradient, kernel, before_mask, after_mask):
    channels = kernel.shape[0] // 3
    spread = jnp.einsum("fijo,co->fijc", gradient, kernel, preferred_element_type=jnp.float32)
    early_part = spread[..., :channels] * before_mask[:, None, None, None]
    late_part = spread[..., 2 * channels :] * after_mask[:, None, None, None]
    blanks = jnp.zeros_like(early_part[:1])
    moved_early = jnp.concatenate([early_part[1:], blanks], axis=0)
    moved_late = jnp.concatenate([blanks, late_part[:-1]], axis=0)
    return spread[..., channels : 2 * channels] + moved_early + moved_late


def moments(values, pixel_count):
    average = lax.psum(jnp.sum(values, axis=(0, 1, 2)), "dp") / pixel_count
    centered = values - average
    spread = lax.psum(jnp.sum(centered * centered, axis=(0, 1, 2)), "dp") / pixel_count
    return (average, lax.rsqrt(spread + eps))


def reduce_back(gradient, normed):
    return lax.psum(
        (jnp.sum(gradient, axis=(0, 1, 2)), jnp.sum(gradient * normed, axis=(0, 1, 2))), "dp"
    )


def silu_slope(values):
    sigmoid_now = jax.nn.sigmoid(values)
    return sigmoid_now * (1.0 + values * (1.0 - sigmoid_now))


def pick_slot(stack, slot_index):
    return lax.dynamic_index_in_dim(stack, slot_index, 0, keepdims=False)


def store_slot(stack, value, slot_index, usable):
    previous = pick_slot(stack, slot_index)
    return lax.dynamic_update_index_in_dim(stack, jnp.where(usable, value, previous), slot_index, 0)


def on_device_general(
    frames, cotangent, starts, space_kernel, time_kernel, mid_gain, mid_bias, out_gain, out_bias
):
    n_segment = lax.axis_size("segment")
    n_data = lax.axis_size("dp")
    segment_index = lax.axis_index("segment")
    odd_segment = segment_index % 2 == 1
    last_segment = segment_index == n_segment - 1
    first_segment = segment_index == 0
    frame_count = frames.shape[0]
    frame_side = frames.shape[1]
    channels = frames.shape[3]
    hidden_units = mid_gain.shape[1] * n_data
    pixel_count = n_data * frame_count * frame_side * frame_side
    turns = 2 * n_segment - 1
    block_shape = (n_segment,) + frames.shape
    all_frames, all_cot, all_starts = (
        lax.all_gather(frames, "segment", axis=0, tiled=True),
        lax.all_gather(cotangent, "segment", axis=0, tiled=True),
        lax.all_gather(starts.astype(jnp.bfloat16), "segment", axis=0, tiled=True),
    )
    frame_stack = all_frames.reshape(block_shape)
    cot_stack = all_cot.reshape(block_shape)
    clip_flags = all_starts.astype(jnp.float32).reshape(n_segment, frame_count)
    positions = jnp.arange(frame_count)
    before_mask = jnp.where((clip_flags > 0.5) | (positions == 0), 0.0, 1.0)
    following = jnp.concatenate([clip_flags[:, 1:], jnp.ones((n_segment, 1), jnp.float32)], axis=1)
    after_mask = jnp.where(following > 0.5, 0.0, 1.0)
    gathered = (
        lax.all_gather(space_kernel[0].astype(jnp.bfloat16), "dp", axis=0, tiled=True),
        lax.all_gather(time_kernel[0].astype(jnp.bfloat16), "dp", axis=0, tiled=True),
        lax.all_gather(mid_gain[0].astype(jnp.bfloat16), "dp", axis=0, tiled=True),
        lax.all_gather(mid_bias[0].astype(jnp.bfloat16), "dp", axis=0, tiled=True),
        lax.all_gather(out_gain[0].astype(jnp.bfloat16), "dp", axis=0, tiled=True),
        lax.all_gather(out_bias[0].astype(jnp.bfloat16), "dp", axis=0, tiled=True),
    )
    space_low, time_low = (gathered[0], gathered[1])
    mid_gain_now = gathered[2].astype(jnp.float32)
    mid_bias_now = gathered[3].astype(jnp.float32)
    out_gain_now = gathered[4].astype(jnp.float32)
    out_bias_now = gathered[5].astype(jnp.float32)
    incoming = jnp.zeros_like(frames)
    carried = jnp.zeros_like(frames)
    kept_input = jnp.zeros(block_shape, jnp.bfloat16)
    kept_skip = jnp.zeros(block_shape, jnp.bfloat16)
    kept_mid_mean = jnp.zeros((n_segment, hidden_units), jnp.float32)
    kept_mid_scale = jnp.zeros((n_segment, hidden_units), jnp.float32)
    kept_out_mean = jnp.zeros((n_segment, channels), jnp.float32)
    kept_out_scale = jnp.zeros((n_segment, channels), jnp.float32)
    results = jnp.zeros(block_shape, jnp.float32)
    for turn_index in range(turns):
        micro_index = turn_index - segment_index
        usable = (micro_index >= 0) & (micro_index < n_segment)
        slot_index = jnp.clip(micro_index, 0, n_segment - 1)
        current = jnp.where(first_segment, pick_slot(frame_stack, slot_index), incoming)
        skip_input = carried
        _, spatial = space_apply(current, space_low)
        mid_mean, mid_scale = moments(spatial, pixel_count)
        hidden_act = jax.nn.silu(
            (spatial - mid_mean) * mid_scale * mid_gain_now + mid_bias_now
        ).astype(jnp.bfloat16)
        _, temporal = time_apply(
            hidden_act,
            time_low,
            pick_slot(before_mask, slot_index),
            pick_slot(after_mask, slot_index),
        )
        out_mean, out_scale = moments(temporal, pixel_count)
        pre_act = (
            (temporal - out_mean) * out_scale * out_gain_now
            + out_bias_now
            + jnp.where(odd_segment, skip_input.astype(jnp.float32), 0.0)
        )
        result = jax.nn.silu(pre_act).astype(jnp.bfloat16)
        kept_input = store_slot(kept_input, current, slot_index, usable)
        kept_skip = store_slot(kept_skip, skip_input, slot_index, usable)
        kept_mid_mean = store_slot(kept_mid_mean, mid_mean, slot_index, usable)
        kept_mid_scale = store_slot(kept_mid_scale, mid_scale, slot_index, usable)
        kept_out_mean = store_slot(kept_out_mean, out_mean, slot_index, usable)
        kept_out_scale = store_slot(kept_out_scale, out_scale, slot_index, usable)
        results = store_slot(results, result.astype(jnp.float32), slot_index, usable)
        if turn_index < turns - 1:
            incoming, carried = from_behind(
                (result, jnp.where(odd_segment, result, current)), "segment", 1
            )
    gathered = (
        lax.all_gather(space_kernel[0].astype(jnp.bfloat16), "dp", axis=0, tiled=True),
        lax.all_gather(time_kernel[0].astype(jnp.bfloat16), "dp", axis=0, tiled=True),
        lax.all_gather(mid_gain[0].astype(jnp.bfloat16), "dp", axis=0, tiled=True),
        lax.all_gather(mid_bias[0].astype(jnp.bfloat16), "dp", axis=0, tiled=True),
        lax.all_gather(out_gain[0].astype(jnp.bfloat16), "dp", axis=0, tiled=True),
        lax.all_gather(out_bias[0].astype(jnp.bfloat16), "dp", axis=0, tiled=True),
    )
    space_low, time_low = (gathered[0], gathered[1])
    mid_gain_now = gathered[2].astype(jnp.float32)
    mid_bias_now = gathered[3].astype(jnp.float32)
    out_gain_now = gathered[4].astype(jnp.float32)
    out_bias_now = gathered[5].astype(jnp.float32)
    grad_input = jnp.zeros_like(frames)
    grad_skip = jnp.zeros_like(frames)
    space_acc = jnp.zeros(space_low.shape, jnp.float32)
    time_acc = jnp.zeros(time_low.shape, jnp.float32)
    mid_gain_acc = jnp.zeros((hidden_units,), jnp.float32)
    mid_bias_acc = jnp.zeros((hidden_units,), jnp.float32)
    out_gain_acc = jnp.zeros((channels,), jnp.float32)
    out_bias_acc = jnp.zeros((channels,), jnp.float32)
    input_grads = jnp.zeros(block_shape, jnp.float32)
    for turn_index in range(turns):
        micro_index = n_segment - 1 - (turn_index - (n_segment - 1 - segment_index))
        usable = (micro_index >= 0) & (micro_index < n_segment)
        usable_weight = usable.astype(jnp.float32)
        slot_index = jnp.clip(micro_index, 0, n_segment - 1)
        current = pick_slot(kept_input, slot_index)
        skip_input = pick_slot(kept_skip, slot_index)
        before_now = pick_slot(before_mask, slot_index)
        after_now = pick_slot(after_mask, slot_index)
        space_taps, spatial = space_apply(current, space_low)
        mid_normed = (spatial - pick_slot(kept_mid_mean, slot_index)) * pick_slot(
            kept_mid_scale, slot_index
        )
        mid_pre = mid_normed * mid_gain_now + mid_bias_now
        hidden_act = jax.nn.silu(mid_pre).astype(jnp.bfloat16)
        time_taps, temporal = time_apply(hidden_act, time_low, before_now, after_now)
        out_scale = pick_slot(kept_out_scale, slot_index)
        out_normed = (temporal - pick_slot(kept_out_mean, slot_index)) * out_scale
        pre_act = (
            out_normed * out_gain_now
            + out_bias_now
            + jnp.where(odd_segment, skip_input.astype(jnp.float32), 0.0)
        )
        grad_result = jnp.where(
            last_segment,
            pick_slot(cot_stack, slot_index).astype(jnp.float32),
            grad_input.astype(jnp.float32)
            + jnp.where(odd_segment, grad_skip.astype(jnp.float32), 0.0),
        )
        grad_pre = grad_result * silu_slope(pre_act)
        out_bias_sum, out_gain_sum = reduce_back(grad_pre, out_normed)
        grad_temporal = (
            out_gain_now
            * out_scale
            * (grad_pre - out_bias_sum / pixel_count - out_normed * out_gain_sum / pixel_count)
        ).astype(jnp.bfloat16)
        time_acc = time_acc + usable_weight * jnp.einsum(
            "fijc,fijo->co", time_taps, grad_temporal, preferred_element_type=jnp.float32
        )
        grad_hidden = time_back(grad_temporal, time_low, before_now, after_now)
        grad_mid = grad_hidden * silu_slope(mid_pre)
        mid_bias_sum, mid_gain_sum = reduce_back(grad_mid, mid_normed)
        mid_scale = pick_slot(kept_mid_scale, slot_index)
        grad_spatial = (
            mid_gain_now
            * mid_scale
            * (grad_mid - mid_bias_sum / pixel_count - mid_normed * mid_gain_sum / pixel_count)
        ).astype(jnp.bfloat16)
        space_acc = space_acc + usable_weight * jnp.einsum(
            "fijc,fijo->co", space_taps, grad_spatial, preferred_element_type=jnp.float32
        )
        grad_current = space_back(grad_spatial, space_low)
        mid_gain_acc = mid_gain_acc + usable_weight * mid_gain_sum
        mid_bias_acc = mid_bias_acc + usable_weight * mid_bias_sum
        out_gain_acc = out_gain_acc + usable_weight * out_gain_sum
        out_bias_acc = out_bias_acc + usable_weight * out_bias_sum
        input_grads = store_slot(
            input_grads, grad_current + grad_skip.astype(jnp.float32), slot_index, usable
        )
        if turn_index < turns - 1:
            grad_input, grad_skip = from_behind(
                (
                    grad_current.astype(jnp.bfloat16),
                    jnp.where(odd_segment, grad_pre.astype(jnp.bfloat16), grad_skip),
                ),
                "segment",
                -1,
            )
    space_grad, time_grad = (
        lax.psum_scatter(space_acc, "dp", scatter_dimension=0, tiled=True),
        lax.psum_scatter(time_acc, "dp", scatter_dimension=0, tiled=True),
    )
    data_index = lax.axis_index("dp")

    def own_share(full_vector):
        share = full_vector.shape[0] // n_data
        return lax.dynamic_slice_in_dim(full_vector, data_index * share, share)[None]

    flat_shape = (n_segment * frame_count,) + frames.shape[1:]
    arrived_out, arrived_grads = (
        lax.all_to_all(
            results.reshape(flat_shape).astype(jnp.bfloat16),
            "segment",
            split_axis=0,
            concat_axis=0,
            tiled=True,
        ).astype(jnp.float32),
        lax.all_to_all(
            input_grads.reshape(flat_shape).astype(jnp.bfloat16),
            "segment",
            split_axis=0,
            concat_axis=0,
            tiled=True,
        ).astype(jnp.float32),
    )
    output = arrived_out[(n_segment - 1) * frame_count :].astype(jnp.bfloat16)
    frames_grad = arrived_grads[:frame_count]
    return (
        output,
        frames_grad,
        space_grad[None],
        time_grad[None],
        own_share(mid_gain_acc),
        own_share(mid_bias_acc),
        own_share(out_gain_acc),
        own_share(out_bias_acc),
    )


def general(mesh):
    return jax.shard_map(
        on_device_general,
        mesh=mesh,
        in_specs=(
            P(("dp", "segment"), None, None, None),
            P(("dp", "segment"), None, None, None),
            P(("dp", "segment")),
            P("segment", "dp", None),
            P("segment", "dp", None),
            P("segment", "dp"),
            P("segment", "dp"),
            P("segment", "dp"),
            P("segment", "dp"),
        ),
        out_specs=(
            P(("dp", "segment"), None, None, None),
            P(("dp", "segment"), None, None, None),
            P("segment", "dp", None),
            P("segment", "dp", None),
            P("segment", "dp"),
            P("segment", "dp"),
            P("segment", "dp"),
            P("segment", "dp"),
        ),
        check_vma=False,
    )


def solution(mesh):
    if mesh.shape["dp"] != 8 or mesh.shape["segment"] != 4:
        return general(mesh)
    n_dp, n_seg = mesh.shape["dp"], mesh.shape["segment"]
    fine = Mesh(mesh.devices.reshape(n_dp // 2, 2, 2, n_seg // 2), EVERY)
    dp, seg = ("z", "y"), ("x", "c")
    return jax.shard_map(
        on_device,
        mesh=fine,
        in_specs=(
            P(EVERY, None, None, None),
            P(EVERY, None, None, None),
            P(EVERY),
            P(seg, dp, None),
            P(seg, dp, None),
            P(seg, dp),
            P(seg, dp),
            P(seg, dp),
            P(seg, dp),
        ),
        out_specs=(
            P(EVERY, None, None, None),
            P(EVERY, None, None, None),
            P(seg, dp, None),
            P(seg, dp, None),
            P(seg, dp),
            P(seg, dp),
            P(seg, dp),
            P(seg, dp),
        ),
        check_vma=False,
    )
```

```python
import functools

import jax
import jax.numpy as jnp
from jax import lax
from jax.experimental import pallas as pl
from jax.experimental.pallas import tpu as pltpu
from jax.sharding import Mesh, PartitionSpec as P

eps = 1e-05
PLANE = ("y", "x", "c")
EVERY = ("z", "y", "x", "c")
BF = jnp.bfloat16
F32 = jnp.float32


def nt(a, b):
    return lax.dot_general(a, b, (((1,), (1,)), ((), ())), preferred_element_type=F32)


def nn(a, b):
    return lax.dot_general(a, b, (((1,), (0,)), ((), ())), preferred_element_type=F32)


VMEM_CAP = 56 * 1024 * 1024
ANY = pl.BlockSpec(memory_space=pl.ANY)


def call(body, outs, scratch, flops, *args, deps=(), far=(), far_outs=()):
    moved = sum(a.size * a.dtype.itemsize for a in args) + sum(
        o.size * o.dtype.itemsize for o in outs
    )
    n = len(deps)

    def spec(a):
        return pl.BlockSpec(memory_space=pltpu.SMEM if a.dtype == jnp.int32 else pltpu.VMEM)

    return pl.pallas_call(
        lambda *refs: body(*refs[n:]),
        out_shape=outs,
        in_specs=[ANY] * n + [ANY if i in far else spec(a) for i, a in enumerate(args)],
        out_specs=[ANY if i in far_outs else spec(o) for i, o in enumerate(outs)],
        scratch_shapes=scratch,
        compiler_params=pltpu.CompilerParams(vmem_limit_bytes=VMEM_CAP),
        cost_estimate=pl.CostEstimate(flops=flops, bytes_accessed=moved, transcendentals=0),
    )(*deps, *args)


def chunk(i, size):
    return pl.ds(pl.multiple_of(i * size, 16), size)


def clear_borders(pad_ref, side, plane, nf):
    zrow = jnp.zeros(pad_ref.shape[1:], BF)
    pad_ref[0] = zrow
    pad_ref[side + 1] = zrow
    zcol = jnp.zeros((nf, pad_ref.shape[2]), BF)
    for i in range(side):
        pad_ref[i + 1, 0:nf] = zcol
        pad_ref[i + 1, nf + plane : 2 * nf + plane] = zcol


def by_rank(slices, rank):
    odd = lax.rem(rank, 2) == 1
    for p in range(len(slices) // 2):
        a, b = slices[2 * p], slices[2 * p + 1]
        yield lax.bitwise_xor(rank // 2, p), odd, a, b


def halves(odd, own, mate):
    low = lax.broadcasted_iota(jnp.int32, own.shape, 1) < 64
    own, mate = own.astype(F32), mate.astype(F32)
    a, b = jnp.where(odd, mate, own), jnp.where(odd, own, mate)
    top = jnp.where(low, a, pltpu.roll(b, 64, 1))
    bottom = jnp.where(low, pltpu.roll(a, 64, 1), b)
    return top, bottom


def store_packed(rank, mate_ref, keep_ref, part, k, step, low):
    rows_now = chunk(k, step)
    odd = lax.rem(rank, 2) == 1
    for q in range(keep_ref.shape[0]):
        x = part[:step, 128 * q : 128 * q + 128]
        y = part[step:, 128 * q : 128 * q + 128]
        even_slice = jnp.where(low, x, pltpu.roll(y, 64, 1))
        odd_slice = jnp.where(low, pltpu.roll(x, 64, 1), y)
        p = lax.bitwise_xor(rank // 2, q)
        keep_ref[p, rows_now, :] = jnp.where(odd, odd_slice, even_slice).astype(BF)
        mate_ref[p, rows_now, :] = jnp.where(odd, even_slice, odd_slice).astype(BF)


def fetch_kernels(w_ref, ktm_ref, lw_ref, sems):
    nz, _, width = w_ref.shape
    hc = ktm_ref.shape[0]
    copies = []
    for z in range(nz):
        copies.append(pltpu.make_async_copy(
            w_ref.at[z, pl.ds(0, hc)], ktm_ref.at[:, pl.ds(z * width, width)], sems.at[2 * z]))
        copies.append(pltpu.make_async_copy(
            w_ref.at[z, pl.ds(hc, lw_ref.shape[1])], lw_ref.at[z], sems.at[2 * z + 1]))
    for copy in copies:
        copy.start()
    return copies


def join_temporal(lw_ref, lf_ref, ltm_ref):
    ch = ltm_ref.shape[1]
    width = lw_ref.shape[2] // 2
    count = 2 * lw_ref.shape[0]
    size = ltm_ref.shape[0] // count
    for z in range(lw_ref.shape[0]):
        first = lw_ref[z, :, 0:ch].astype(F32)
        off = width % 128
        second = lw_ref[z, :, width - off : width - off + ch + 128].astype(F32)
        second = pltpu.roll(second, ch + 128 - off, 1)[:, 0:ch]
        for b, block in ((2 * z, first), (2 * z + 1, second)):
            lf_ref[b * size : b * size + block.shape[0], :] = block
    ltm_ref[...] = lf_ref[0 : ltm_ref.shape[0], :].astype(BF)


def prepare_body(w_ref, kn_out, l_out, lt_out, rows_out, ktm_ref, lw_ref, lf_ref, sems):
    hc, ch = ktm_ref.shape[0], l_out.shape[1]
    for copy in fetch_kernels(w_ref, ktm_ref, lw_ref, sems):
        copy.wait()
    for t in range(9):
        kn_out[t] = ktm_ref[:, t * ch : (t + 1) * ch].astype(F32).T.astype(BF)
    join_temporal(lw_ref, lf_ref, l_out)
    rows_out[...] = lw_ref[:, lw_ref.shape[1] - rows_out.shape[1] :, :]
    for t in range(3):
        lt_out[t] = lf_ref[t * hc : (t + 1) * hc].T.astype(BF)


def prepare(w, hc, ch, deps=()):
    outs = [
        jax.ShapeDtypeStruct((9, ch, hc), BF),
        jax.ShapeDtypeStruct((3 * hc, ch), BF),
        jax.ShapeDtypeStruct((3, ch, hc), BF),
        jax.ShapeDtypeStruct((w.shape[0], 16, w.shape[2]), BF),
    ]
    tall = w.shape[1] - hc
    scratch = [
        pltpu.VMEM((hc, 9 * ch), BF),
        pltpu.VMEM((w.shape[0], tall, w.shape[2]), BF),
        pltpu.VMEM((3 * hc + tall, ch), F32),
        pltpu.SemaphoreType.DMA((2 * w.shape[0],)),
    ]
    return call(prepare_body, outs, scratch, 2 * w.size * 512, w, deps=deps, far=(0,))


def conv_body(side, first, rank_ref, *refs):
    n = 1 if first else 8
    slices = refs[:n]
    (kn_in, ltm_ref, vec_ref, before_ref, after_ref,
     pad_out, hid_out, xhat_out, rs_ref, mate_ref, keep_ref,
     pad_ref, hid_ref, xhat_ref, sp_ref, kn_ref, sems) = refs[n:]
    rank = rank_ref[0]
    kn_copy = pltpu.make_async_copy(kn_in, kn_ref, sems.at[0])
    kn_copy.start()
    ch, hc = pad_ref.shape[2], hid_ref.shape[1]
    rows = hid_ref.shape[0]
    plane = rows // side
    nf = plane // side
    step = plane // 2
    clear_borders(pad_ref, side, plane, nf)
    if first:
        for i in range(side):
            pad_ref[i + 1, nf : nf + plane] = slices[0][i * plane : (i + 1) * plane]
    else:
        def place(k, carry):
            for q, odd, a_ref, b_ref in by_rank(slices, rank):
                top, bottom = halves(odd, a_ref[chunk(k, step), :], b_ref[chunk(k, step), :])
                lanes = pl.ds(pl.multiple_of(128 * q, 128), 128)
                for piece, kk in ((top, k), (bottom, k + side)):
                    at = nf + lax.rem(kk, 2) * step
                    pad_ref[1 + kk // 2, pl.ds(pl.multiple_of(at, 16), step), lanes] = piece.astype(BF)
            return carry

        lax.fori_loop(0, side, place, 0, unroll=True)
    pad_copy = pltpu.make_async_copy(pad_ref, pad_out, sems.at[1])
    pad_copy.start()
    kn_copy.wait()

    def conv(i, total):
        acc = jnp.zeros((plane, hc), F32)
        for t in range(9):
            r, c = t // 3, t % 3
            acc += nn(pad_ref[i + r, c * nf : c * nf + plane, :], kn_ref[t])
        sp_ref[i] = acc
        return total + jnp.sum(acc, axis=0, keepdims=True)

    mean = lax.fori_loop(0, side, conv, jnp.zeros((1, hc), F32), unroll=True) / rows

    def square(i, total):
        cen = sp_ref[i] - mean
        return total + jnp.sum(cen * cen, axis=0, keepdims=True)

    var = lax.fori_loop(0, side, square, jnp.zeros((1, hc), F32), unroll=True) / rows
    rs = lax.rsqrt(var + eps)
    rs_ref[...] = rs
    gain, bias = vec_ref[0:1, :], vec_ref[1:2, :]

    def act(i, carry):
        xhat = (sp_ref[i] - mean) * rs
        xhat_ref[i] = xhat
        v = xhat * gain + bias
        v = v * jax.nn.sigmoid(v)
        sp_ref[i] = v
        hid_ref[chunk(i, plane), :] = v.astype(BF)
        return carry

    lax.fori_loop(0, side, act, 0, unroll=True)
    late = [
        pltpu.make_async_copy(hid_ref, hid_out, sems.at[2]),
        pltpu.make_async_copy(xhat_ref, xhat_out, sems.at[3]),
    ]
    for copy in late:
        copy.start()
    low = lax.broadcasted_iota(jnp.int32, (step, 128), 1) < 64

    def temporal(k, carry):
        pieces = []
        for kk in (k, k + side):
            par = lax.rem(kk, 2)
            h = sp_ref[kk // 2, pl.ds(pl.multiple_of(par * step, 8), step), :]
            at = pl.multiple_of(par * (step % nf), 8)
            pieces.append((
                (pltpu.roll(h, 1, 0) * before_ref[pl.ds(at, step), :]).astype(BF),
                h.astype(BF),
                (pltpu.roll(h, step - 1, 0) * after_ref[pl.ds(at, step), :]).astype(BF),
            ))
        part = sum(
            nn(jnp.concatenate([x, y], axis=0), ltm_ref[t * hc : (t + 1) * hc])
            for t, (x, y) in enumerate(zip(*pieces))
        )
        store_packed(rank, mate_ref, keep_ref, part, k, step, low)
        return carry

    lax.fori_loop(0, side, temporal, 0, unroll=True)
    for copy in [pad_copy] + late:
        copy.wait()


def conv_forward(rank, g, kn, lt, vec, before, after, side, pixels, ch, deps=()):
    hc = vec.shape[1]
    plane = pixels // side
    nf = plane // side
    n = len(g)
    shapes = [
        ((side + 2, plane + 2 * nf, ch), BF),
        ((pixels, hc), BF),
        ((side, plane, hc), F32),
    ]
    outs = [jax.ShapeDtypeStruct(*s) for s in shapes] + [
        jax.ShapeDtypeStruct((1, hc), F32),
        jax.ShapeDtypeStruct((4, pixels // 2, 128), BF),
        jax.ShapeDtypeStruct((4, pixels // 2, 128), BF),
    ]
    scratch = [pltpu.VMEM(*s) for s in shapes] + [
        pltpu.VMEM((side, plane, hc), F32),
        pltpu.VMEM((9, ch, hc), BF),
        pltpu.SemaphoreType.DMA((4,)),
    ]
    flops = 2 * pixels * hc * 12 * ch
    return call(functools.partial(conv_body, side, n == 1), outs, scratch, flops,
                rank, *g, kn, lt, vec, before, after,
                deps=deps, far=(n + 1,), far_outs=(0, 1, 2))


def fold(v):
    return v + pltpu.roll(v, 64, 1)


def total_of(refs):
    t = refs[0][...].astype(F32)
    for ref in refs[1:]:
        t += ref[...].astype(F32)
    return t


def pair_sum_body(keep_ref, mate_ref, *out_refs):
    for p, ref in enumerate(out_refs):
        ref[...] = (keep_ref[p].astype(F32) + mate_ref[p].astype(F32)).astype(ref.dtype)


def pair_sum(keep, arrived, deps=()):
    shape = keep.shape[1:]
    outs = [jax.ShapeDtypeStruct(shape, BF)] * keep.shape[0]
    return call(pair_sum_body, outs, [], keep.size, keep, arrived, deps=deps)


def out_norm_body(n, has_skip, *refs):
    parts, refs = refs[:n], refs[n:]
    if has_skip:
        vec_ref, skip_ref, xhat_ref, rs_ref, pre_ref, res_ref = refs
    else:
        vec_ref, xhat_ref, rs_ref, pre_ref, res_ref = refs
    t = total_of(parts)
    pixels = 2 * t.shape[0]
    mean = fold(jnp.sum(t, axis=0, keepdims=True)) / pixels
    cen = t - mean
    rs = lax.rsqrt(fold(jnp.sum(cen * cen, axis=0, keepdims=True)) / pixels + eps)
    xhat = cen * rs
    pre = xhat * vec_ref[0:1, :] + vec_ref[1:2, :]
    if has_skip:
        pre = pre + skip_ref[...].astype(F32)
    xhat_ref[...] = xhat
    rs_ref[...] = rs
    pre_ref[...] = pre
    res_ref[...] = (pre * jax.nn.sigmoid(pre)).astype(BF)


def out_norm(parts, vec, skip, deps=()):
    half = parts[0].shape[0]
    outs = [
        jax.ShapeDtypeStruct((half, 128), F32),
        jax.ShapeDtypeStruct((1, 128), F32),
        jax.ShapeDtypeStruct((half, 128), F32),
        jax.ShapeDtypeStruct((half, 128), BF),
    ]
    args = (*parts, vec) + (() if skip is None else (skip,))
    body = functools.partial(out_norm_body, len(parts), skip is not None)
    return call(body, outs, [], half * 128 * 10, *args, deps=deps)


def out_back_body(n, *refs):
    parts, (pre_ref, xhat_ref, rs_ref, vec_ref, dpre_ref, dt_ref, sums_ref) = refs[:n], refs[n:]
    g = total_of(parts)
    pre, xhat = pre_ref[...], xhat_ref[...]
    sig = jax.nn.sigmoid(pre)
    dpre = g * (sig * (1.0 + pre * (1.0 - sig)))
    pixels = 2 * pre.shape[0]
    sb = fold(jnp.sum(dpre, axis=0, keepdims=True))
    sg = fold(jnp.sum(dpre * xhat, axis=0, keepdims=True))
    dpre_ref[...] = dpre.astype(BF)
    scale = vec_ref[0:1, :] * rs_ref[...]
    dt_ref[...] = (scale * (dpre - sb / pixels - xhat * (sg / pixels))).astype(BF)
    sums_ref[0:1, :] = sg
    sums_ref[1:2, :] = sb


def out_back(parts, pre, xhat, rs, vec, deps=()):
    half = pre.shape[0]
    outs = [
        jax.ShapeDtypeStruct((half, 128), BF),
        jax.ShapeDtypeStruct((half, 128), BF),
        jax.ShapeDtypeStruct((2, 128), F32),
    ]
    args = (*parts, pre, xhat, rs, vec)
    return call(functools.partial(out_back_body, len(parts)), outs, [], half * 1280, *args, deps=deps)


def conv_back_body(side, rank_ref, *refs):
    slices, (xhat_in, rs_ref, w_ref, lnt_ref, vec_ref, before_ref, after_ref,
             dt_out, ds_out, sums_ref, mate_ref, keep_ref,
             dt_ref, ds_ref, xhat_ref, dy_ref, pad_ref, ktm_ref, sems) = refs[:8], refs[8:]
    half = slices[0].shape[0]
    rank = rank_ref[0]
    nz, _, width = w_ref.shape
    rows = 2 * half
    plane = rows // side
    nf = plane // side
    step = plane // 2
    hc = ds_ref.shape[1]
    ch = dt_ref.shape[1]
    fetched = [
        pltpu.make_async_copy(
            w_ref.at[z, pl.ds(0, hc)], ktm_ref.at[:, pl.ds(z * width, width)], sems.at[z])
        for z in range(nz)
    ]
    xhat_copy = pltpu.make_async_copy(xhat_in, xhat_ref, sems.at[nz])
    for copy in fetched + [xhat_copy]:
        copy.start()
    clear_borders(pad_ref, side, plane, nf)

    def place(k, carry):
        for q, odd, a_ref, b_ref in by_rank(slices, rank):
            top, bottom = halves(odd, a_ref[chunk(k, step), :], b_ref[chunk(k, step), :])
            lanes = pl.ds(pl.multiple_of(128 * q, 128), 128)
            dt_ref[chunk(k, step), lanes] = top.astype(BF)
            dt_ref[pl.ds(pl.multiple_of(half + k * step, 16), step), lanes] = bottom.astype(BF)
        return carry

    lax.fori_loop(0, side, place, 0, unroll=True)
    dt_copy = pltpu.make_async_copy(dt_ref, dt_out, sems.at[nz + 1])
    dt_copy.start()
    xhat_copy.wait()
    gain, bias = vec_ref[0:1, :], vec_ref[1:2, :]

    def hidden_grad(i, sums):
        dt = dt_ref[chunk(i, plane), :]
        early = nn(dt, lnt_ref[0]) * before_ref[0:plane, :]
        late = nn(dt, lnt_ref[2]) * after_ref[0:plane, :]
        dh = nn(dt, lnt_ref[1]) + pltpu.roll(early, plane - 1, 0) + pltpu.roll(late, 1, 0)
        xhat = xhat_ref[i]
        v = xhat * gain + bias
        sig = jax.nn.sigmoid(v)
        dy = dh * (sig * (1.0 + v * (1.0 - sig)))
        dy_ref[i] = dy
        return (
            sums[0] + jnp.sum(dy * xhat, axis=0, keepdims=True),
            sums[1] + jnp.sum(dy, axis=0, keepdims=True),
        )

    zero = jnp.zeros((1, hc), F32)
    sg, sb = lax.fori_loop(0, side, hidden_grad, (zero, zero), unroll=True)
    sums_ref[0:1, :] = sg
    sums_ref[1:2, :] = sb
    scale = gain * rs_ref[...]

    def spatial_grad(i, carry):
        ds = (scale * (dy_ref[i] - sb / rows - xhat_ref[i] * (sg / rows))).astype(BF)
        pad_ref[i + 1, nf : nf + plane] = ds
        ds_ref[chunk(i, plane), :] = ds
        return carry

    lax.fori_loop(0, side, spatial_grad, 0, unroll=True)
    ds_copy = pltpu.make_async_copy(ds_ref, ds_out, sems.at[nz + 2])
    ds_copy.start()
    for copy in fetched:
        copy.wait()
    low = lax.broadcasted_iota(jnp.int32, (step, 128), 1) < 64

    def back(k, carry):
        acc = jnp.zeros((2 * step, ch), F32)
        for t in range(9):
            r, c = 2 - t // 3, 2 - t % 3
            pieces = []
            for kk in (k, k + side):
                at = c * nf + lax.rem(kk, 2) * step
                pieces.append(pad_ref[kk // 2 + r, pl.ds(pl.multiple_of(at, 16), step), :])
            acc += nn(jnp.concatenate(pieces, axis=0), ktm_ref[:, t * ch : (t + 1) * ch])
        store_packed(rank, mate_ref, keep_ref, acc, k, step, low)
        return carry

    lax.fori_loop(0, side, back, 0, unroll=True)
    dt_copy.wait()
    ds_copy.wait()


def conv_back(rank, g, xhat, rs, w, lnt, vec, before, after, side, deps=()):
    half = g[0].shape[0]
    hc = vec.shape[1]
    ch = len(g) * 64
    pixels = 2 * half
    plane = pixels // side
    nf = plane // side
    outs = [
        jax.ShapeDtypeStruct((pixels, ch), BF),
        jax.ShapeDtypeStruct((pixels, hc), BF),
        jax.ShapeDtypeStruct((2, hc), F32),
        jax.ShapeDtypeStruct((4, half, 128), BF),
        jax.ShapeDtypeStruct((4, half, 128), BF),
    ]
    scratch = [
        pltpu.VMEM((pixels, ch), BF),
        pltpu.VMEM((pixels, hc), BF),
        pltpu.VMEM((side, plane, hc), F32),
        pltpu.VMEM((side, plane, hc), F32),
        pltpu.VMEM((side + 2, plane + 2 * nf, hc), BF),
        pltpu.VMEM((hc, 9 * ch), BF),
        pltpu.SemaphoreType.DMA((w.shape[0] + 3,)),
    ]
    flops = 2 * pixels * hc * 12 * ch
    return call(functools.partial(conv_back_body, side), outs, scratch, flops,
                rank, *g, xhat, rs, w, lnt, vec, before, after,
                deps=deps, far=(9, 11), far_outs=(0, 1))


def grads_body(side, pad_ref, hid_ref, ds_ref, dt_ref, before_ref, after_ref, mid_ref, out_ref,
               sg_ref, dst_ref, taps_ref, tg_ref, vec_ref):
    ch = pad_ref.shape[2]
    hc = hid_ref.shape[1]
    plane = hid_ref.shape[0] // side
    nf = plane // side
    for i in (0, 1, side + 2, side + 3):
        dst_ref[i] = jnp.zeros(dst_ref.shape[1:], BF)
    for i in range(side):
        at = slice(i * plane, (i + 1) * plane)
        h = hid_ref[at, :].astype(F32)
        taps_ref[i, 0:hc] = (pltpu.roll(h, 1, 0) * before_ref[0:plane, :]).T.astype(BF)
        taps_ref[i, hc : 2 * hc] = h.T.astype(BF)
        taps_ref[i, 2 * hc : 3 * hc] = (pltpu.roll(h, plane - 1, 0) * after_ref[0:plane, :]).T.astype(BF)
        dst_ref[i + 2] = ds_ref[at, :].astype(F32).T.astype(BF)
    tg_ref[0 : 3 * hc, :] = sum(
        nn(taps_ref[i], dt_ref[i * plane : (i + 1) * plane, :]) for i in range(side)
    )
    tg_ref[3 * hc :, :] = jnp.zeros((tg_ref.shape[0] - 3 * hc, ch), F32)
    nz, _, width = sg_ref.shape
    size = 3 * hc // (2 * nz)
    vec_ref[...] = jnp.zeros(vec_ref.shape, F32)
    vec_ref[size : size + 2, 0:hc] = mid_ref[...]
    vec_ref[size + 2 : size + 4, 0:128] = out_ref[...]
    tall = vec_ref.shape[0]
    inside = lax.broadcasted_iota(jnp.int32, (tall, ch), 0) < size
    off = (width // 2) % 128
    for z in range(nz):
        first, second = [
            jnp.where(inside, tg_ref[b * size : b * size + tall, :], vec_ref[...])
            for b in (2 * z, 2 * z + 1)
        ]
        start = width // 2 - off
        sg_ref[z, hc : hc + tall, 0:ch] = first.astype(BF)
        second = pltpu.roll(jnp.concatenate([second, jnp.zeros((tall, 128), F32)], axis=1), off, 1)
        sg_ref[z, hc : hc + tall, start : start + ch + 128] = second.astype(BF)
    for c in range(3):
        acc = sum(
            nn(dst_ref[i : i + 3].reshape(3 * hc, plane), pad_ref[i, c * nf : c * nf + plane, :])
            for i in range(1, side + 1)
        )
        for r in range(3):
            first = (3 * r + c) * ch
            end = first + ch
            at = (2 - r) * hc
            done = 0
            while first < end:
                z = first // width
                last = min(end, (z + 1) * width)
                sg_ref[z, 0:hc, first - z * width : last - z * width] = (
                    acc[at : at + hc, done : done + last - first].astype(BF)
                )
                done += last - first
                first = last


def kernel_grads(pad, hidden, ds, dt, before, after, mid, out, side, shape, deps=()):
    pixels, hc = hidden.shape
    ch = dt.shape[1]
    plane = pixels // side
    outs = [jax.ShapeDtypeStruct(shape, BF)]
    tall = shape[1] - hc
    scratch = [
        pltpu.VMEM((side + 4, hc, plane), BF),
        pltpu.VMEM((side, 3 * hc, plane), BF),
        pltpu.VMEM((3 * hc + tall, ch), F32),
        pltpu.VMEM((tall, ch), F32),
    ]
    flops = 2 * pixels * hc * 12 * ch
    return call(functools.partial(grads_body, side), outs, scratch, flops,
                pad, hidden, ds, dt, before, after, mid, out, deps=deps)[0]


def pass_on_body(*refs):
    pass


def after_all(v, *deps):
    n = len(deps)
    return pl.pallas_call(
        pass_on_body,
        out_shape=jax.ShapeDtypeStruct(v.shape, v.dtype),
        in_specs=[ANY] * (n + 1),
        out_specs=ANY,
        input_output_aliases={n: 0},
        cost_estimate=pl.CostEstimate(flops=0, bytes_accessed=0, transcendentals=0),
    )(*deps, v)


def pack_kernels_body(kt_ref, lt_ref, vec_ref, out_ref, low_ref):
    ranks, _, width = out_ref.shape
    hc = kt_ref.shape[0] // ranks
    blocks = lt_ref.shape[0] // hc
    q = hc // ranks
    low_ref[...] = jnp.zeros(low_ref.shape, F32)
    for r in range(ranks):
        out_ref[r, 0:hc, :] = kt_ref[r * hc : (r + 1) * hc, :]
        for b in range(blocks):
            low_ref[r, b * q : (b + 1) * q, 0 : lt_ref.shape[1]] = (
                lt_ref[b * hc + r * q : b * hc + (r + 1) * q, :]
            )
        low_ref[r, blocks * q : blocks * q + 1, :] = vec_ref[...]
        out_ref[r, hc:, :] = low_ref[r].astype(BF)


def pack_kernels(kt, lt, vec, ranks, tall, deps):
    width = kt.shape[1]
    outs = [jax.ShapeDtypeStruct((ranks, kt.shape[0] // ranks + tall, width), BF)]
    scratch = [pltpu.VMEM((ranks, tall, width), F32)]
    return call(pack_kernels_body, outs, scratch, kt.size * 8, kt, lt, vec, deps=deps)[0]


def call(body, outs, scratch, flops, *args, deps=(), far=(), far_outs=()):
    moved = sum(a.size * a.dtype.itemsize for a in args) + sum(
        o.size * o.dtype.itemsize for o in outs
    )
    n = len(deps)

    def spec(a):
        return pl.BlockSpec(memory_space=pltpu.SMEM if a.dtype == jnp.int32 else pltpu.VMEM)

    return pl.pallas_call(
        lambda *refs: body(*refs[n:]),
        out_shape=outs,
        in_specs=[ANY] * n + [ANY if i in far else spec(a) for i, a in enumerate(args)],
        out_specs=[ANY if i in far_outs else spec(o) for i, o in enumerate(outs)],
        scratch_shapes=scratch,
        compiler_params=pltpu.CompilerParams(vmem_limit_bytes=VMEM_CAP),
        cost_estimate=pl.CostEstimate(flops=flops, bytes_accessed=moved, transcendentals=0),
    )(*deps, *args)


def chunk(i, size):
    return pl.ds(pl.multiple_of(i * size, 16), size)


def clear_borders(pad_ref, side, plane, nf):
    zrow = jnp.zeros(pad_ref.shape[1:], BF)
    pad_ref[0] = zrow
    pad_ref[side + 1] = zrow
    zcol = jnp.zeros((nf, pad_ref.shape[2]), BF)
    for i in range(side):
        pad_ref[i + 1, 0:nf] = zcol
        pad_ref[i + 1, nf + plane : 2 * nf + plane] = zcol


def by_rank(slices, rank):
    odd = lax.rem(rank, 2) == 1
    for p in range(len(slices) // 2):
        a, b = slices[2 * p], slices[2 * p + 1]
        yield lax.bitwise_xor(rank // 2, p), odd, a, b


def halves(odd, own, mate):
    low = lax.broadcasted_iota(jnp.int32, own.shape, 1) < 64
    own, mate = own.astype(F32), mate.astype(F32)
    a, b = jnp.where(odd, mate, own), jnp.where(odd, own, mate)
    top = jnp.where(low, a, pltpu.roll(b, 64, 1))
    bottom = jnp.where(low, pltpu.roll(a, 64, 1), b)
    return top, bottom


def store_packed(rank, mate_ref, keep_ref, part, k, step, low):
    rows_now = chunk(k, step)
    odd = lax.rem(rank, 2) == 1
    for q in range(keep_ref.shape[0]):
        x = part[:step, 128 * q : 128 * q + 128]
        y = part[step:, 128 * q : 128 * q + 128]
        even_slice = jnp.where(low, x, pltpu.roll(y, 64, 1))
        odd_slice = jnp.where(low, pltpu.roll(x, 64, 1), y)
        p = lax.bitwise_xor(rank // 2, q)
        keep_ref[p, rows_now, :] = jnp.where(odd, odd_slice, even_slice).astype(BF)
        mate_ref[p, rows_now, :] = jnp.where(odd, even_slice, odd_slice).astype(BF)


def fetch_kernels(w_ref, ktm_ref, lw_ref, sems):
    nz, _, width = w_ref.shape
    hc = ktm_ref.shape[0]
    copies = []
    for z in range(nz):
        copies.append(pltpu.make_async_copy(
            w_ref.at[z, pl.ds(0, hc)], ktm_ref.at[:, pl.ds(z * width, width)], sems.at[2 * z]))
        copies.append(pltpu.make_async_copy(
            w_ref.at[z, pl.ds(hc, lw_ref.shape[1])], lw_ref.at[z], sems.at[2 * z + 1]))
    for copy in copies:
        copy.start()
    return copies


def join_temporal(lw_ref, lf_ref, ltm_ref):
    ch = ltm_ref.shape[1]
    width = lw_ref.shape[2] // 2
    count = 2 * lw_ref.shape[0]
    size = ltm_ref.shape[0] // count
    for z in range(lw_ref.shape[0]):
        first = lw_ref[z, :, 0:ch].astype(F32)
        off = width % 128
        second = lw_ref[z, :, width - off : width - off + ch + 128].astype(F32)
        second = pltpu.roll(second, ch + 128 - off, 1)[:, 0:ch]
        for b, block in ((2 * z, first), (2 * z + 1, second)):
            lf_ref[b * size : b * size + block.shape[0], :] = block
    ltm_ref[...] = lf_ref[0 : ltm_ref.shape[0], :].astype(BF)


def prepare_body(w_ref, kn_out, l_out, lt_out, rows_out, ktm_ref, lw_ref, lf_ref, sems):
    hc, ch = ktm_ref.shape[0], l_out.shape[1]
    for copy in fetch_kernels(w_ref, ktm_ref, lw_ref, sems):
        copy.wait()
    for t in range(9):
        kn_out[t] = ktm_ref[:, t * ch : (t + 1) * ch].astype(F32).T.astype(BF)
    join_temporal(lw_ref, lf_ref, l_out)
    rows_out[...] = lw_ref[:, lw_ref.shape[1] - rows_out.shape[1] :, :]
    for t in range(3):
        lt_out[t] = lf_ref[t * hc : (t + 1) * hc].T.astype(BF)


def prepare(w, hc, ch, deps=()):
    outs = [
        jax.ShapeDtypeStruct((9, ch, hc), BF),
        jax.ShapeDtypeStruct((3 * hc, ch), BF),
        jax.ShapeDtypeStruct((3, ch, hc), BF),
        jax.ShapeDtypeStruct((w.shape[0], 16, w.shape[2]), BF),
    ]
    tall = w.shape[1] - hc
    scratch = [
        pltpu.VMEM((hc, 9 * ch), BF),
        pltpu.VMEM((w.shape[0], tall, w.shape[2]), BF),
        pltpu.VMEM((3 * hc + tall, ch), F32),
        pltpu.SemaphoreType.DMA((2 * w.shape[0],)),
    ]
    return call(prepare_body, outs, scratch, 2 * w.size * 512, w, deps=deps, far=(0,))


def conv_body(side, first, rank_ref, *refs):
    n = 1 if first else 8
    slices = refs[:n]
    (kn_in, ltm_ref, vec_ref, before_ref, after_ref,
     pad_out, hid_out, xhat_out, rs_ref, mate_ref, keep_ref,
     pad_ref, hid_ref, xhat_ref, sp_ref, kn_ref, sems) = refs[n:]
    rank = rank_ref[0]
    kn_copy = pltpu.make_async_copy(kn_in, kn_ref, sems.at[0])
    kn_copy.start()
    ch, hc = pad_ref.shape[2], hid_ref.shape[1]
    rows = hid_ref.shape[0]
    plane = rows // side
    nf = plane // side
    step = plane // 2
    clear_borders(pad_ref, side, plane, nf)
    if first:
        for i in range(side):
            pad_ref[i + 1, nf : nf + plane] = slices[0][i * plane : (i + 1) * plane]
    else:
        def place(k, carry):
            for q, odd, a_ref, b_ref in by_rank(slices, rank):
                top, bottom = halves(odd, a_ref[chunk(k, step), :], b_ref[chunk(k, step), :])
                lanes = pl.ds(pl.multiple_of(128 * q, 128), 128)
                for piece, kk in ((top, k), (bottom, k + side)):
                    at = nf + lax.rem(kk, 2) * step
                    pad_ref[1 + kk // 2, pl.ds(pl.multiple_of(at, 16), step), lanes] = piece.astype(BF)
            return carry

        lax.fori_loop(0, side, place, 0, unroll=True)
    pad_copy = pltpu.make_async_copy(pad_ref, pad_out, sems.at[1])
    pad_copy.start()
    kn_copy.wait()

    def conv(i, total):
        acc = jnp.zeros((plane, hc), F32)
        for t in range(9):
            r, c = t // 3, t % 3
            acc += nn(pad_ref[i + r, c * nf : c * nf + plane, :], kn_ref[t])
        sp_ref[i] = acc
        return total + jnp.sum(acc, axis=0, keepdims=True)

    mean = lax.fori_loop(0, side, conv, jnp.zeros((1, hc), F32), unroll=True) / rows

    def square(i, total):
        cen = sp_ref[i] - mean
        return total + jnp.sum(cen * cen, axis=0, keepdims=True)

    var = lax.fori_loop(0, side, square, jnp.zeros((1, hc), F32), unroll=True) / rows
    rs = lax.rsqrt(var + eps)
    rs_ref[...] = rs
    gain, bias = vec_ref[0:1, :], vec_ref[1:2, :]

    def act(i, carry):
        xhat = (sp_ref[i] - mean) * rs
        xhat_ref[i] = xhat
        v = xhat * gain + bias
        v = v * jax.nn.sigmoid(v)
        sp_ref[i] = v
        hid_ref[chunk(i, plane), :] = v.astype(BF)
        return carry

    lax.fori_loop(0, side, act, 0, unroll=True)
    late = [
        pltpu.make_async_copy(hid_ref, hid_out, sems.at[2]),
        pltpu.make_async_copy(xhat_ref, xhat_out, sems.at[3]),
    ]
    for copy in late:
        copy.start()
    low = lax.broadcasted_iota(jnp.int32, (step, 128), 1) < 64

    def temporal(k, carry):
        pieces = []
        for kk in (k, k + side):
            par = lax.rem(kk, 2)
            h = sp_ref[kk // 2, pl.ds(pl.multiple_of(par * step, 8), step), :]
            at = pl.multiple_of(par * (step % nf), 8)
            pieces.append((
                (pltpu.roll(h, 1, 0) * before_ref[pl.ds(at, step), :]).astype(BF),
                h.astype(BF),
                (pltpu.roll(h, step - 1, 0) * after_ref[pl.ds(at, step), :]).astype(BF),
            ))
        part = sum(
            nn(jnp.concatenate([x, y], axis=0), ltm_ref[t * hc : (t + 1) * hc])
            for t, (x, y) in enumerate(zip(*pieces))
        )
        store_packed(rank, mate_ref, keep_ref, part, k, step, low)
        return carry

    lax.fori_loop(0, side, temporal, 0, unroll=True)
    for copy in [pad_copy] + late:
        copy.wait()


def conv_forward(rank, g, kn, lt, vec, before, after, side, pixels, ch, deps=()):
    hc = vec.shape[1]
    plane = pixels // side
    nf = plane // side
    n = len(g)
    shapes = [
        ((side + 2, plane + 2 * nf, ch), BF),
        ((pixels, hc), BF),
        ((side, plane, hc), F32),
    ]
    outs = [jax.ShapeDtypeStruct(*s) for s in shapes] + [
        jax.ShapeDtypeStruct((1, hc), F32),
        jax.ShapeDtypeStruct((4, pixels // 2, 128), BF),
        jax.ShapeDtypeStruct((4, pixels // 2, 128), BF),
    ]
    scratch = [pltpu.VMEM(*s) for s in shapes] + [
        pltpu.VMEM((side, plane, hc), F32),
        pltpu.VMEM((9, ch, hc), BF),
        pltpu.SemaphoreType.DMA((4,)),
    ]
    flops = 2 * pixels * hc * 12 * ch
    return call(functools.partial(conv_body, side, n == 1), outs, scratch, flops,
                rank, *g, kn, lt, vec, before, after,
                deps=deps, far=(n + 1,), far_outs=(0, 1, 2))


def fold(v):
    return v + pltpu.roll(v, 64, 1)


def total_of(refs):
    t = refs[0][...].astype(F32)
    for ref in refs[1:]:
        t += ref[...].astype(F32)
    return t


def pair_sum_body(keep_ref, mate_ref, *out_refs):
    for p, ref in enumerate(out_refs):
        ref[...] = (keep_ref[p].astype(F32) + mate_ref[p].astype(F32)).astype(ref.dtype)


def pair_sum(keep, arrived, deps=()):
    shape = keep.shape[1:]
    outs = [jax.ShapeDtypeStruct(shape, BF)] * keep.shape[0]
    return call(pair_sum_body, outs, [], keep.size, keep, arrived, deps=deps)


def out_norm_body(n, has_skip, *refs):
    parts, refs = refs[:n], refs[n:]
    if has_skip:
        vec_ref, skip_ref, xhat_ref, rs_ref, pre_ref, res_ref = refs
    else:
        vec_ref, xhat_ref, rs_ref, pre_ref, res_ref = refs
    t = total_of(parts)
    pixels = 2 * t.shape[0]
    mean = fold(jnp.sum(t, axis=0, keepdims=True)) / pixels
    cen = t - mean
    rs = lax.rsqrt(fold(jnp.sum(cen * cen, axis=0, keepdims=True)) / pixels + eps)
    xhat = cen * rs
    pre = xhat * vec_ref[0:1, :] + vec_ref[1:2, :]
    if has_skip:
        pre = pre + skip_ref[...].astype(F32)
    xhat_ref[...] = xhat
    rs_ref[...] = rs
    pre_ref[...] = pre
    res_ref[...] = (pre * jax.nn.sigmoid(pre)).astype(BF)


def out_norm(parts, vec, skip, deps=()):
    half = parts[0].shape[0]
    outs = [
        jax.ShapeDtypeStruct((half, 128), F32),
        jax.ShapeDtypeStruct((1, 128), F32),
        jax.ShapeDtypeStruct((half, 128), F32),
        jax.ShapeDtypeStruct((half, 128), BF),
    ]
    args = (*parts, vec) + (() if skip is None else (skip,))
    body = functools.partial(out_norm_body, len(parts), skip is not None)
    return call(body, outs, [], half * 128 * 10, *args, deps=deps)


def out_back_body(n, *refs):
    parts, (pre_ref, xhat_ref, rs_ref, vec_ref, dpre_ref, dt_ref, sums_ref) = refs[:n], refs[n:]
    g = total_of(parts)
    pre, xhat = pre_ref[...], xhat_ref[...]
    sig = jax.nn.sigmoid(pre)
    dpre = g * (sig * (1.0 + pre * (1.0 - sig)))
    pixels = 2 * pre.shape[0]
    sb = fold(jnp.sum(dpre, axis=0, keepdims=True))
    sg = fold(jnp.sum(dpre * xhat, axis=0, keepdims=True))
    dpre_ref[...] = dpre.astype(BF)
    scale = vec_ref[0:1, :] * rs_ref[...]
    dt_ref[...] = (scale * (dpre - sb / pixels - xhat * (sg / pixels))).astype(BF)
    sums_ref[0:1, :] = sg
    sums_ref[1:2, :] = sb


def out_back(parts, pre, xhat, rs, vec, deps=()):
    half = pre.shape[0]
    outs = [
        jax.ShapeDtypeStruct((half, 128), BF),
        jax.ShapeDtypeStruct((half, 128), BF),
        jax.ShapeDtypeStruct((2, 128), F32),
    ]
    args = (*parts, pre, xhat, rs, vec)
    return call(functools.partial(out_back_body, len(parts)), outs, [], half * 1280, *args, deps=deps)


def conv_back_body(side, rank_ref, *refs):
    slices, (xhat_in, rs_ref, w_ref, lnt_ref, vec_ref, before_ref, after_ref,
             dt_out, ds_out, sums_ref, mate_ref, keep_ref,
             dt_ref, ds_ref, xhat_ref, dy_ref, pad_ref, ktm_ref, sems) = refs[:8], refs[8:]
    half = slices[0].shape[0]
    rank = rank_ref[0]
    nz, _, width = w_ref.shape
    rows = 2 * half
    plane = rows // side
    nf = plane // side
    step = plane // 2
    hc = ds_ref.shape[1]
    ch = dt_ref.shape[1]
    fetched = [
        pltpu.make_async_copy(
            w_ref.at[z, pl.ds(0, hc)], ktm_ref.at[:, pl.ds(z * width, width)], sems.at[z])
        for z in range(nz)
    ]
    xhat_copy = pltpu.make_async_copy(xhat_in, xhat_ref, sems.at[nz])
    for copy in fetched + [xhat_copy]:
        copy.start()
    clear_borders(pad_ref, side, plane, nf)

    def place(k, carry):
        for q, odd, a_ref, b_ref in by_rank(slices, rank):
            top, bottom = halves(odd, a_ref[chunk(k, step), :], b_ref[chunk(k, step), :])
            lanes = pl.ds(pl.multiple_of(128 * q, 128), 128)
            dt_ref[chunk(k, step), lanes] = top.astype(BF)
            dt_ref[pl.ds(pl.multiple_of(half + k * step, 16), step), lanes] = bottom.astype(BF)
        return carry

    lax.fori_loop(0, side, place, 0, unroll=True)
    dt_copy = pltpu.make_async_copy(dt_ref, dt_out, sems.at[nz + 1])
    dt_copy.start()
    xhat_copy.wait()
    gain, bias = vec_ref[0:1, :], vec_ref[1:2, :]

    def hidden_grad(i, sums):
        dt = dt_ref[chunk(i, plane), :]
        early = nn(dt, lnt_ref[0]) * before_ref[0:plane, :]
        late = nn(dt, lnt_ref[2]) * after_ref[0:plane, :]
        dh = nn(dt, lnt_ref[1]) + pltpu.roll(early, plane - 1, 0) + pltpu.roll(late, 1, 0)
        xhat = xhat_ref[i]
        v = xhat * gain + bias
        sig = jax.nn.sigmoid(v)
        dy = dh * (sig * (1.0 + v * (1.0 - sig)))
        dy_ref[i] = dy
        return (
            sums[0] + jnp.sum(dy * xhat, axis=0, keepdims=True),
            sums[1] + jnp.sum(dy, axis=0, keepdims=True),
        )

    zero = jnp.zeros((1, hc), F32)
    sg, sb = lax.fori_loop(0, side, hidden_grad, (zero, zero), unroll=True)
    sums_ref[0:1, :] = sg
    sums_ref[1:2, :] = sb
    scale = gain * rs_ref[...]

    def spatial_grad(i, carry):
        ds = (scale * (dy_ref[i] - sb / rows - xhat_ref[i] * (sg / rows))).astype(BF)
        pad_ref[i + 1, nf : nf + plane] = ds
        ds_ref[chunk(i, plane), :] = ds
        return carry

    lax.fori_loop(0, side, spatial_grad, 0, unroll=True)
    ds_copy = pltpu.make_async_copy(ds_ref, ds_out, sems.at[nz + 2])
    ds_copy.start()
    for copy in fetched:
        copy.wait()
    low = lax.broadcasted_iota(jnp.int32, (step, 128), 1) < 64

    def back(k, carry):
        acc = jnp.zeros((2 * step, ch), F32)
        for t in range(9):
            r, c = 2 - t // 3, 2 - t % 3
            pieces = []
            for kk in (k, k + side):
                at = c * nf + lax.rem(kk, 2) * step
                pieces.append(pad_ref[kk // 2 + r, pl.ds(pl.multiple_of(at, 16), step), :])
            acc += nn(jnp.concatenate(pieces, axis=0), ktm_ref[:, t * ch : (t + 1) * ch])
        store_packed(rank, mate_ref, keep_ref, acc, k, step, low)
        return carry

    lax.fori_loop(0, side, back, 0, unroll=True)
    dt_copy.wait()
    ds_copy.wait()


def conv_back(rank, g, xhat, rs, w, lnt, vec, before, after, side, deps=()):
    half = g[0].shape[0]
    hc = vec.shape[1]
    ch = len(g) * 64
    pixels = 2 * half
    plane = pixels // side
    nf = plane // side
    outs = [
        jax.ShapeDtypeStruct((pixels, ch), BF),
        jax.ShapeDtypeStruct((pixels, hc), BF),
        jax.ShapeDtypeStruct((2, hc), F32),
        jax.ShapeDtypeStruct((4, half, 128), BF),
        jax.ShapeDtypeStruct((4, half, 128), BF),
    ]
    scratch = [
        pltpu.VMEM((pixels, ch), BF),
        pltpu.VMEM((pixels, hc), BF),
        pltpu.VMEM((side, plane, hc), F32),
        pltpu.VMEM((side, plane, hc), F32),
        pltpu.VMEM((side + 2, plane + 2 * nf, hc), BF),
        pltpu.VMEM((hc, 9 * ch), BF),
        pltpu.SemaphoreType.DMA((w.shape[0] + 3,)),
    ]
    flops = 2 * pixels * hc * 12 * ch
    return call(functools.partial(conv_back_body, side), outs, scratch, flops,
                rank, *g, xhat, rs, w, lnt, vec, before, after,
                deps=deps, far=(9, 11), far_outs=(0, 1))


def grads_body(side, pad_ref, hid_ref, ds_ref, dt_ref, before_ref, after_ref, mid_ref, out_ref,
               sg_ref, dst_ref, taps_ref, tg_ref, vec_ref):
    ch = pad_ref.shape[2]
    hc = hid_ref.shape[1]
    plane = hid_ref.shape[0] // side
    nf = plane // side
    for i in (0, 1, side + 2, side + 3):
        dst_ref[i] = jnp.zeros(dst_ref.shape[1:], BF)
    for i in range(side):
        at = slice(i * plane, (i + 1) * plane)
        h = hid_ref[at, :].astype(F32)
        taps_ref[i, 0:hc] = (pltpu.roll(h, 1, 0) * before_ref[0:plane, :]).T.astype(BF)
        taps_ref[i, hc : 2 * hc] = h.T.astype(BF)
        taps_ref[i, 2 * hc : 3 * hc] = (pltpu.roll(h, plane - 1, 0) * after_ref[0:plane, :]).T.astype(BF)
        dst_ref[i + 2] = ds_ref[at, :].astype(F32).T.astype(BF)
    tg_ref[0 : 3 * hc, :] = sum(
        nn(taps_ref[i], dt_ref[i * plane : (i + 1) * plane, :]) for i in range(side)
    )
    tg_ref[3 * hc :, :] = jnp.zeros((tg_ref.shape[0] - 3 * hc, ch), F32)
    nz, _, width = sg_ref.shape
    size = 3 * hc // (2 * nz)
    vec_ref[...] = jnp.zeros(vec_ref.shape, F32)
    vec_ref[size : size + 2, 0:hc] = mid_ref[...]
    vec_ref[size + 2 : size + 4, 0:128] = out_ref[...]
    tall = vec_ref.shape[0]
    inside = lax.broadcasted_iota(jnp.int32, (tall, ch), 0) < size
    off = (width // 2) % 128
    for z in range(nz):
        first, second = [
            jnp.where(inside, tg_ref[b * size : b * size + tall, :], vec_ref[...])
            for b in (2 * z, 2 * z + 1)
        ]
        start = width // 2 - off
        sg_ref[z, hc : hc + tall, 0:ch] = first.astype(BF)
        second = pltpu.roll(jnp.concatenate([second, jnp.zeros((tall, 128), F32)], axis=1), off, 1)
        sg_ref[z, hc : hc + tall, start : start + ch + 128] = second.astype(BF)
    for c in range(3):
        acc = sum(
            nn(dst_ref[i : i + 3].reshape(3 * hc, plane), pad_ref[i, c * nf : c * nf + plane, :])
            for i in range(1, side + 1)
        )
        for r in range(3):
            first = (3 * r + c) * ch
            end = first + ch
            at = (2 - r) * hc
            done = 0
            while first < end:
                z = first // width
                last = min(end, (z + 1) * width)
                sg_ref[z, 0:hc, first - z * width : last - z * width] = (
                    acc[at : at + hc, done : done + last - first].astype(BF)
                )
                done += last - first
                first = last


def kernel_grads(pad, hidden, ds, dt, before, after, mid, out, side, shape, deps=()):
    pixels, hc = hidden.shape
    ch = dt.shape[1]
    plane = pixels // side
    outs = [jax.ShapeDtypeStruct(shape, BF)]
    tall = shape[1] - hc
    scratch = [
        pltpu.VMEM((side + 4, hc, plane), BF),
        pltpu.VMEM((side, 3 * hc, plane), BF),
        pltpu.VMEM((3 * hc + tall, ch), F32),
        pltpu.VMEM((tall, ch), F32),
    ]
    flops = 2 * pixels * hc * 12 * ch
    return call(functools.partial(grads_body, side), outs, scratch, flops,
                pad, hidden, ds, dt, before, after, mid, out, deps=deps)[0]


def pass_on_body(*refs):
    pass


def after_all(v, *deps):
    n = len(deps)
    return pl.pallas_call(
        pass_on_body,
        out_shape=jax.ShapeDtypeStruct(v.shape, v.dtype),
        in_specs=[ANY] * (n + 1),
        out_specs=ANY,
        input_output_aliases={n: 0},
        cost_estimate=pl.CostEstimate(flops=0, bytes_accessed=0, transcendentals=0),
    )(*deps, v)


def pack_kernels_body(kt_ref, lt_ref, vec_ref, out_ref, low_ref):
    ranks, _, width = out_ref.shape
    hc = kt_ref.shape[0] // ranks
    blocks = lt_ref.shape[0] // hc
    q = hc // ranks
    low_ref[...] = jnp.zeros(low_ref.shape, F32)
    for r in range(ranks):
        out_ref[r, 0:hc, :] = kt_ref[r * hc : (r + 1) * hc, :]
        for b in range(blocks):
            low_ref[r, b * q : (b + 1) * q, 0 : lt_ref.shape[1]] = (
                lt_ref[b * hc + r * q : b * hc + (r + 1) * q, :]
            )
        low_ref[r, blocks * q : blocks * q + 1, :] = vec_ref[...]
        out_ref[r, hc:, :] = low_ref[r].astype(BF)


def pack_kernels(kt, lt, vec, ranks, tall, deps):
    width = kt.shape[1]
    outs = [jax.ShapeDtypeStruct((ranks, kt.shape[0] // ranks + tall, width), BF)]
    scratch = [pltpu.VMEM((ranks, tall, width), F32)]
    return call(pack_kernels_body, outs, scratch, kt.size * 8, kt, lt, vec, deps=deps)[0]


def hop(v, k):
    n = 1
    for name in EVERY:
        n *= lax.axis_size(name)
    return lax.ppermute(v, EVERY, [(i, i ^ k) for i in range(n)])


def plane_gather(v, aside=()):
    got = {0: v}
    for k in (6, 2, 4):
        got[k] = hop(v, k)
    got[1] = hop(after_all(v, *aside) if aside else v, 1)
    for k in (2, 4, 6):
        got[k ^ 1] = hop(got[k], 1)
    return [got[k] for k in range(8)]


def plane_reduce(mate, keep, deps=()):
    sums = pair_sum(keep, hop(mate, 1), deps)
    arrived = {k: hop(sums[k // 2], k) for k in (6, 2, 4)}
    return [sums[0], arrived[2], arrived[4], arrived[6]]


def on_device(frames, cot, starts, ks, ktm, mg, mb, og, ob):
    nz, n_rank, n_seg = lax.axis_size("z"), 8, 4
    n_dp = nz * 2
    fr, side, ch = frames.shape[0], frames.shape[1], frames.shape[3]
    area = side * side
    hid = ks.shape[2]
    hc, cc = hid // n_rank, ch // n_rank
    q = hc // n_rank
    rank = lax.axis_index(PLANE)
    rank_now = rank.astype(jnp.int32).reshape(1)
    d_index = lax.axis_index(("z", "y"))
    nf = n_dp * fr
    pixels = area * nf
    half = pixels // 2

    def keeper(d, s):
        v = (d // 2) ^ s
        return (d % 2) * 4 + (v % 2) * 2 + v // 2

    to_plane = [
        (d * n_seg + s, s * n_rank + keeper(d, s)) for d in range(n_dp) for s in range(n_seg)
    ]
    from_plane = [(b, a) for a, b in to_plane]
    rows = fr * area
    flag_row = jnp.pad(starts.astype(BF)[None], ((0, 11), (0, ch - fr)))
    lead = rows + 12
    moving = jnp.concatenate([frames.reshape(rows, ch), flag_row, cot.reshape(rows, ch)], axis=0)
    moving = lax.ppermute(moving, EVERY, to_plane)

    perm = (jnp.arange(hid).reshape(n_rank, n_rank, q).transpose(1, 0, 2).reshape(hid)[:, None]
            == jnp.arange(hid)[None, :]).astype(BF)
    kt = lax.dot_general(perm, ks[0].astype(BF), (((1,), (1,)), ((), ())),
                         preferred_element_type=F32).astype(BF)
    lrows, width = ktm.shape[1] // n_rank, ks.shape[1]
    tall = -(-(lrows + 4) // 16) * 16
    extra = jnp.concatenate([mg, mb, og, ob], axis=1)
    extra = jnp.pad(extra, ((0, 0), (0, width - extra.shape[1])))
    w = pack_kernels(kt, ktm[0], extra, n_rank, tall, deps=(moving,))
    w = lax.all_to_all(w, PLANE, 0, 0)
    here = w
    high = hc + tall

    w = w.reshape(2, n_seg, high, width).transpose(1, 2, 0, 3).reshape(n_seg, high, 2 * width)
    ws = [lax.all_gather(w[s], "z", axis=0) for s in range(n_seg)]

    group = 7
    own = moving[lead:].reshape(group, rows // group, n_rank, cc).transpose(2, 1, 0, 3)
    own = own.reshape(n_rank, rows // group, group * cc)
    own = jnp.pad(own, ((0, 0), (0, 4), (0, ch - group * cc)))
    own = jnp.concatenate([jnp.broadcast_to(moving[:lead], (n_rank, lead, ch)), own], axis=1)
    gathered = lax.all_to_all(after_all(own, here), PLANE, 0, 0)


    def norm_rows(rows_now):
        row = rows_now[:, (lrows - tall) % 16].reshape(n_dp, width).astype(F32)
        mid = jnp.stack([
            lax.dynamic_slice_in_dim(row[:, i * hc : (i + 1) * hc], rank * q, q, axis=1).reshape(hc)
            for i in range(2)])
        own = lax.dynamic_index_in_dim(row, rank, 0, keepdims=False)
        out = jnp.stack([
            jnp.tile(own[2 * hc + i * cc : 2 * hc + (i + 1) * cc], 2) for i in range(2)])
        return mid, out

    def by_pixel(v):
        width = v.shape[2]
        v = v.reshape(n_rank * fr, area, width).transpose(1, 0, 2)
        return v.reshape(pixels, width)

    def packed(v):
        return jnp.concatenate([v[:half], v[half:]], axis=1)

    a0 = by_pixel(gathered[:, :rows])
    flags = gathered[:, rows, :fr].reshape(nf) > 0.5
    slot = jnp.arange(nf) % fr
    before = jnp.where(flags | (slot == 0), 0.0, 1.0)
    after = jnp.where(jnp.roll(flags, -1) | (slot == fr - 1), 0.0, 1.0)
    spread = (side * nf + nf, hc)
    before = jnp.broadcast_to(jnp.tile(before, side + 1)[:, None], spread)
    after = jnp.broadcast_to(jnp.tile(after, side + 1)[:, None], spread)
    skip = packed(lax.dynamic_slice_in_dim(a0, rank * cc, cc, axis=1))

    def across(*slices):
        n = len(slices)
        v = jnp.stack([jnp.concatenate([v[:, :cc], v[:, cc:]], axis=0) for v in slices])
        v = v.reshape(n, area, n_rank, fr, cc).transpose(2, 0, 1, 3, 4).reshape(n_rank, n * rows, cc)
        return lax.all_to_all(v, PLANE, 0, 0)

    def home(v):
        n = v.shape[1] // rows
        v = v.transpose(1, 0, 2).reshape(n * rows, ch)
        v = lax.ppermute(v, EVERY, from_plane).reshape(n, area, fr, ch).transpose(0, 2, 1, 3)
        return v.reshape(n, *frames.shape)

    saved = []
    g = [a0]
    ready = prepare(ws[0], hc, ch)
    for s in range(n_seg):
        kn, lt, lnt, rows_now = ready
        mid, out = norm_rows(rows_now)
        pad, hidden, xm, rm, mate, keep = conv_forward(
            rank_now, g, kn, lt, mid, before, after, side, pixels, ch)
        parts = plane_reduce(mate, keep)
        xo, ro, pre, res = out_norm(parts, out, skip if s % 2 == 1 else None)
        saved.append((pad, hidden, xm, rm, xo, ro, pre, lnt, mid, out))
        if s % 2 == 1:
            skip = res
        if s < n_seg - 1:
            ready = prepare(ws[s + 1], hc, ch, deps=(res,))
            g = plane_gather(res, ready[:1])
    cot_own = gathered[:, lead : lead + rows // group, : group * cc]
    cot_own = cot_own.reshape(n_rank, rows // group, group, cc).transpose(0, 2, 1, 3)
    cot_own = packed(by_pixel(cot_own.reshape(n_rank, rows, cc)))

    parts = [cot_own]
    skip_grad = None

    grads, raw = [], None
    for s in reversed(range(n_seg)):
        pad, hidden, xm, rm, xo, ro, pre, lnt, mid, out = saved[s]
        if s == 1:
            parts = parts + [skip_grad]
        deps = () if raw is None else (raw, *grads[len(grads) - 1 :])
        dpre, dt, osum = out_back(parts, pre, xo, ro, out, deps=deps)
        if raw is not None:
            grads.append(lax.psum_scatter(after_all(raw, dt), "z", scatter_dimension=0))
        if s % 2 == 1:
            skip_grad = dpre
        dtf, ds, msum, mate, keep = conv_back(
            rank_now, plane_gather(dt), xm, rm, ws[s], lnt, mid, before, after, side)
        if s > 0:
            parts = plane_reduce(mate, keep)
        raw = kernel_grads(pad, hidden, ds, dtf, before, after, msum, osum, side, ws[s].shape,
                           deps=parts[:1] if s > 0 else ())
    last = lax.psum_scatter(raw, "z", scatter_dimension=0)
    parts = plane_reduce(mate, keep, deps=(raw,))

    da = sum(p.astype(F32) for p in parts) + skip_grad.astype(F32)
    home_now = home(across(res, da.astype(BF)))
    output, frames_grad = home_now[0], home_now[1].astype(F32)

    def by_row(v):
        return v.reshape(high, 2, width).transpose(1, 0, 2)

    g = jnp.stack([by_row(v) for v in [last] + grads[::-1]], axis=1).reshape(n_rank, high, width)
    g = lax.all_to_all(g, PLANE, 0, 0)
    space_grad = lax.dot_general(g[:, :hc].reshape(hid, width), perm, (((0,), (0,)), ((), ())),
                                 preferred_element_type=F32)
    tg = g[:, hc : hc + lrows, :ch].reshape(n_rank, -1, q, ch)
    time_grad = tg.transpose(1, 0, 2, 3).reshape(-1, ch).astype(F32)
    sums = g[:, hc + lrows : hc + lrows + 4].astype(F32)

    def mid_own(v):
        return lax.dynamic_slice_in_dim(v[:, :hc], d_index * q, q, axis=1).reshape(1, hc)

    own = lax.dynamic_index_in_dim(sums, d_index, 0, keepdims=False)
    return (
        output,
        frames_grad,
        space_grad[None],
        time_grad[None],
        mid_own(sums[:, 0]),
        mid_own(sums[:, 1]),
        own[2:3, :cc],
        own[3:4, :cc],
    )


def from_behind(value, axis, steps):
    count = lax.axis_size(axis)
    leading, last = (max(0, -steps), min(count, count - steps))
    return lax.ppermute(value, axis, [(source, source + steps) for source in range(leading, last)])


def space_apply(current, kernel):
    frame_side = current.shape[1]
    padded = jnp.pad(current, ((0, 0), (1, 1), (1, 1), (0, 0)))
    stacked = jnp.concatenate(
        [
            padded[:, row_shift : row_shift + frame_side, col_shift : col_shift + frame_side, :]
            for row_shift in range(3)
            for col_shift in range(3)
        ],
        axis=-1,
    )
    return (
        stacked,
        jnp.einsum("fijc,co->fijo", stacked, kernel, preferred_element_type=jnp.float32),
    )


def space_back(gradient, kernel):
    frame_side = gradient.shape[1]
    channels = kernel.shape[0] // 9
    spread = jnp.einsum("fijo,co->fijc", gradient, kernel, preferred_element_type=jnp.float32)
    total = jnp.zeros((gradient.shape[0], frame_side + 2, frame_side + 2, channels), jnp.float32)
    for tap_index in range(9):
        row_shift = tap_index // 3
        col_shift = tap_index % 3
        piece_now = spread[..., tap_index * channels : (tap_index + 1) * channels]
        total = total + jnp.pad(
            piece_now, ((0, 0), (row_shift, 2 - row_shift), (col_shift, 2 - col_shift), (0, 0))
        )
    return total[:, 1 : frame_side + 1, 1 : frame_side + 1, :]


def time_apply(current, kernel, before_mask, after_mask):
    blanks = jnp.zeros_like(current[:1])
    earlier = jnp.concatenate([blanks, current[:-1]], axis=0) * before_mask[
        :, None, None, None
    ].astype(current.dtype)
    later = jnp.concatenate([current[1:], blanks], axis=0) * after_mask[:, None, None, None].astype(
        current.dtype
    )
    stacked = jnp.concatenate([earlier, current, later], axis=-1)
    return (
        stacked,
        jnp.einsum("fijc,co->fijo", stacked, kernel, preferred_element_type=jnp.float32),
    )


def time_back(gradient, kernel, before_mask, after_mask):
    channels = kernel.shape[0] // 3
    spread = jnp.einsum("fijo,co->fijc", gradient, kernel, preferred_element_type=jnp.float32)
    early_part = spread[..., :channels] * before_mask[:, None, None, None]
    late_part = spread[..., 2 * channels :] * after_mask[:, None, None, None]
    blanks = jnp.zeros_like(early_part[:1])
    moved_early = jnp.concatenate([early_part[1:], blanks], axis=0)
    moved_late = jnp.concatenate([blanks, late_part[:-1]], axis=0)
    return spread[..., channels : 2 * channels] + moved_early + moved_late


def moments(values, pixel_count):
    average = lax.psum(jnp.sum(values, axis=(0, 1, 2)), "dp") / pixel_count
    centered = values - average
    spread = lax.psum(jnp.sum(centered * centered, axis=(0, 1, 2)), "dp") / pixel_count
    return (average, lax.rsqrt(spread + eps))


def reduce_back(gradient, normed):
    return lax.psum(
        (jnp.sum(gradient, axis=(0, 1, 2)), jnp.sum(gradient * normed, axis=(0, 1, 2))), "dp"
    )


def silu_slope(values):
    sigmoid_now = jax.nn.sigmoid(values)
    return sigmoid_now * (1.0 + values * (1.0 - sigmoid_now))


def pick_slot(stack, slot_index):
    return lax.dynamic_index_in_dim(stack, slot_index, 0, keepdims=False)


def store_slot(stack, value, slot_index, usable):
    previous = pick_slot(stack, slot_index)
    return lax.dynamic_update_index_in_dim(stack, jnp.where(usable, value, previous), slot_index, 0)


def on_device_general(
    frames, cotangent, starts, space_kernel, time_kernel, mid_gain, mid_bias, out_gain, out_bias
):
    n_segment = lax.axis_size("segment")
    n_data = lax.axis_size("dp")
    segment_index = lax.axis_index("segment")
    odd_segment = segment_index % 2 == 1
    last_segment = segment_index == n_segment - 1
    first_segment = segment_index == 0
    frame_count = frames.shape[0]
    frame_side = frames.shape[1]
    channels = frames.shape[3]
    hidden_units = mid_gain.shape[1] * n_data
    pixel_count = n_data * frame_count * frame_side * frame_side
    turns = 2 * n_segment - 1
    block_shape = (n_segment,) + frames.shape
    all_frames, all_cot, all_starts = (
        lax.all_gather(frames, "segment", axis=0, tiled=True),
        lax.all_gather(cotangent, "segment", axis=0, tiled=True),
        lax.all_gather(starts.astype(jnp.bfloat16), "segment", axis=0, tiled=True),
    )
    frame_stack = all_frames.reshape(block_shape)
    cot_stack = all_cot.reshape(block_shape)
    clip_flags = all_starts.astype(jnp.float32).reshape(n_segment, frame_count)
    positions = jnp.arange(frame_count)
    before_mask = jnp.where((clip_flags > 0.5) | (positions == 0), 0.0, 1.0)
    following = jnp.concatenate([clip_flags[:, 1:], jnp.ones((n_segment, 1), jnp.float32)], axis=1)
    after_mask = jnp.where(following > 0.5, 0.0, 1.0)
    gathered = (
        lax.all_gather(space_kernel[0].astype(jnp.bfloat16), "dp", axis=0, tiled=True),
        lax.all_gather(time_kernel[0].astype(jnp.bfloat16), "dp", axis=0, tiled=True),
        lax.all_gather(mid_gain[0].astype(jnp.bfloat16), "dp", axis=0, tiled=True),
        lax.all_gather(mid_bias[0].astype(jnp.bfloat16), "dp", axis=0, tiled=True),
        lax.all_gather(out_gain[0].astype(jnp.bfloat16), "dp", axis=0, tiled=True),
        lax.all_gather(out_bias[0].astype(jnp.bfloat16), "dp", axis=0, tiled=True),
    )
    space_low, time_low = (gathered[0], gathered[1])
    mid_gain_now = gathered[2].astype(jnp.float32)
    mid_bias_now = gathered[3].astype(jnp.float32)
    out_gain_now = gathered[4].astype(jnp.float32)
    out_bias_now = gathered[5].astype(jnp.float32)
    incoming = jnp.zeros_like(frames)
    carried = jnp.zeros_like(frames)
    kept_input = jnp.zeros(block_shape, jnp.bfloat16)
    kept_skip = jnp.zeros(block_shape, jnp.bfloat16)
    kept_mid_mean = jnp.zeros((n_segment, hidden_units), jnp.float32)
    kept_mid_scale = jnp.zeros((n_segment, hidden_units), jnp.float32)
    kept_out_mean = jnp.zeros((n_segment, channels), jnp.float32)
    kept_out_scale = jnp.zeros((n_segment, channels), jnp.float32)
    results = jnp.zeros(block_shape, jnp.float32)
    for turn_index in range(turns):
        micro_index = turn_index - segment_index
        usable = (micro_index >= 0) & (micro_index < n_segment)
        slot_index = jnp.clip(micro_index, 0, n_segment - 1)
        current = jnp.where(first_segment, pick_slot(frame_stack, slot_index), incoming)
        skip_input = carried
        _, spatial = space_apply(current, space_low)
        mid_mean, mid_scale = moments(spatial, pixel_count)
        hidden_act = jax.nn.silu(
            (spatial - mid_mean) * mid_scale * mid_gain_now + mid_bias_now
        ).astype(jnp.bfloat16)
        _, temporal = time_apply(
            hidden_act,
            time_low,
            pick_slot(before_mask, slot_index),
            pick_slot(after_mask, slot_index),
        )
        out_mean, out_scale = moments(temporal, pixel_count)
        pre_act = (
            (temporal - out_mean) * out_scale * out_gain_now
            + out_bias_now
            + jnp.where(odd_segment, skip_input.astype(jnp.float32), 0.0)
        )
        result = jax.nn.silu(pre_act).astype(jnp.bfloat16)
        kept_input = store_slot(kept_input, current, slot_index, usable)
        kept_skip = store_slot(kept_skip, skip_input, slot_index, usable)
        kept_mid_mean = store_slot(kept_mid_mean, mid_mean, slot_index, usable)
        kept_mid_scale = store_slot(kept_mid_scale, mid_scale, slot_index, usable)
        kept_out_mean = store_slot(kept_out_mean, out_mean, slot_index, usable)
        kept_out_scale = store_slot(kept_out_scale, out_scale, slot_index, usable)
        results = store_slot(results, result.astype(jnp.float32), slot_index, usable)
        if turn_index < turns - 1:
            incoming, carried = from_behind(
                (result, jnp.where(odd_segment, result, current)), "segment", 1
            )
    gathered = (
        lax.all_gather(space_kernel[0].astype(jnp.bfloat16), "dp", axis=0, tiled=True),
        lax.all_gather(time_kernel[0].astype(jnp.bfloat16), "dp", axis=0, tiled=True),
        lax.all_gather(mid_gain[0].astype(jnp.bfloat16), "dp", axis=0, tiled=True),
        lax.all_gather(mid_bias[0].astype(jnp.bfloat16), "dp", axis=0, tiled=True),
        lax.all_gather(out_gain[0].astype(jnp.bfloat16), "dp", axis=0, tiled=True),
        lax.all_gather(out_bias[0].astype(jnp.bfloat16), "dp", axis=0, tiled=True),
    )
    space_low, time_low = (gathered[0], gathered[1])
    mid_gain_now = gathered[2].astype(jnp.float32)
    mid_bias_now = gathered[3].astype(jnp.float32)
    out_gain_now = gathered[4].astype(jnp.float32)
    out_bias_now = gathered[5].astype(jnp.float32)
    grad_input = jnp.zeros_like(frames)
    grad_skip = jnp.zeros_like(frames)
    space_acc = jnp.zeros(space_low.shape, jnp.float32)
    time_acc = jnp.zeros(time_low.shape, jnp.float32)
    mid_gain_acc = jnp.zeros((hidden_units,), jnp.float32)
    mid_bias_acc = jnp.zeros((hidden_units,), jnp.float32)
    out_gain_acc = jnp.zeros((channels,), jnp.float32)
    out_bias_acc = jnp.zeros((channels,), jnp.float32)
    input_grads = jnp.zeros(block_shape, jnp.float32)
    for turn_index in range(turns):
        micro_index = n_segment - 1 - (turn_index - (n_segment - 1 - segment_index))
        usable = (micro_index >= 0) & (micro_index < n_segment)
        usable_weight = usable.astype(jnp.float32)
        slot_index = jnp.clip(micro_index, 0, n_segment - 1)
        current = pick_slot(kept_input, slot_index)
        skip_input = pick_slot(kept_skip, slot_index)
        before_now = pick_slot(before_mask, slot_index)
        after_now = pick_slot(after_mask, slot_index)
        space_taps, spatial = space_apply(current, space_low)
        mid_normed = (spatial - pick_slot(kept_mid_mean, slot_index)) * pick_slot(
            kept_mid_scale, slot_index
        )
        mid_pre = mid_normed * mid_gain_now + mid_bias_now
        hidden_act = jax.nn.silu(mid_pre).astype(jnp.bfloat16)
        time_taps, temporal = time_apply(hidden_act, time_low, before_now, after_now)
        out_scale = pick_slot(kept_out_scale, slot_index)
        out_normed = (temporal - pick_slot(kept_out_mean, slot_index)) * out_scale
        pre_act = (
            out_normed * out_gain_now
            + out_bias_now
            + jnp.where(odd_segment, skip_input.astype(jnp.float32), 0.0)
        )
        grad_result = jnp.where(
            last_segment,
            pick_slot(cot_stack, slot_index).astype(jnp.float32),
            grad_input.astype(jnp.float32)
            + jnp.where(odd_segment, grad_skip.astype(jnp.float32), 0.0),
        )
        grad_pre = grad_result * silu_slope(pre_act)
        out_bias_sum, out_gain_sum = reduce_back(grad_pre, out_normed)
        grad_temporal = (
            out_gain_now
            * out_scale
            * (grad_pre - out_bias_sum / pixel_count - out_normed * out_gain_sum / pixel_count)
        ).astype(jnp.bfloat16)
        time_acc = time_acc + usable_weight * jnp.einsum(
            "fijc,fijo->co", time_taps, grad_temporal, preferred_element_type=jnp.float32
        )
        grad_hidden = time_back(grad_temporal, time_low, before_now, after_now)
        grad_mid = grad_hidden * silu_slope(mid_pre)
        mid_bias_sum, mid_gain_sum = reduce_back(grad_mid, mid_normed)
        mid_scale = pick_slot(kept_mid_scale, slot_index)
        grad_spatial = (
            mid_gain_now
            * mid_scale
            * (grad_mid - mid_bias_sum / pixel_count - mid_normed * mid_gain_sum / pixel_count)
        ).astype(jnp.bfloat16)
        space_acc = space_acc + usable_weight * jnp.einsum(
            "fijc,fijo->co", space_taps, grad_spatial, preferred_element_type=jnp.float32
        )
        grad_current = space_back(grad_spatial, space_low)
        mid_gain_acc = mid_gain_acc + usable_weight * mid_gain_sum
        mid_bias_acc = mid_bias_acc + usable_weight * mid_bias_sum
        out_gain_acc = out_gain_acc + usable_weight * out_gain_sum
        out_bias_acc = out_bias_acc + usable_weight * out_bias_sum
        input_grads = store_slot(
            input_grads, grad_current + grad_skip.astype(jnp.float32), slot_index, usable
        )
        if turn_index < turns - 1:
            grad_input, grad_skip = from_behind(
                (
                    grad_current.astype(jnp.bfloat16),
                    jnp.where(odd_segment, grad_pre.astype(jnp.bfloat16), grad_skip),
                ),
                "segment",
                -1,
            )
    space_grad, time_grad = (
        lax.psum_scatter(space_acc, "dp", scatter_dimension=0, tiled=True),
        lax.psum_scatter(time_acc, "dp", scatter_dimension=0, tiled=True),
    )
    data_index = lax.axis_index("dp")

    def own_share(full_vector):
        share = full_vector.shape[0] // n_data
        return lax.dynamic_slice_in_dim(full_vector, data_index * share, share)[None]

    flat_shape = (n_segment * frame_count,) + frames.shape[1:]
    arrived_out, arrived_grads = (
        lax.all_to_all(
            results.reshape(flat_shape).astype(jnp.bfloat16),
            "segment",
            split_axis=0,
            concat_axis=0,
            tiled=True,
        ).astype(jnp.float32),
        lax.all_to_all(
            input_grads.reshape(flat_shape).astype(jnp.bfloat16),
            "segment",
            split_axis=0,
            concat_axis=0,
            tiled=True,
        ).astype(jnp.float32),
    )
    output = arrived_out[(n_segment - 1) * frame_count :].astype(jnp.bfloat16)
    frames_grad = arrived_grads[:frame_count]
    return (
        output,
        frames_grad,
        space_grad[None],
        time_grad[None],
        own_share(mid_gain_acc),
        own_share(mid_bias_acc),
        own_share(out_gain_acc),
        own_share(out_bias_acc),
    )


def general(mesh):
    return jax.shard_map(
        on_device_general,
        mesh=mesh,
        in_specs=(
            P(("dp", "segment"), None, None, None),
            P(("dp", "segment"), None, None, None),
            P(("dp", "segment")),
            P("segment", "dp", None),
            P("segment", "dp", None),
            P("segment", "dp"),
            P("segment", "dp"),
            P("segment", "dp"),
            P("segment", "dp"),
        ),
        out_specs=(
            P(("dp", "segment"), None, None, None),
            P(("dp", "segment"), None, None, None),
            P("segment", "dp", None),
            P("segment", "dp", None),
            P("segment", "dp"),
            P("segment", "dp"),
            P("segment", "dp"),
            P("segment", "dp"),
        ),
        check_vma=False,
    )


def solution(mesh):
    if mesh.shape["dp"] != 8 or mesh.shape["segment"] != 4:
        return general(mesh)
    n_dp, n_seg = mesh.shape["dp"], mesh.shape["segment"]
    fine = Mesh(mesh.devices.reshape(n_dp // 2, 2, 2, n_seg // 2), EVERY)
    dp, seg = ("z", "y"), ("x", "c")
    return jax.shard_map(
        on_device,
        mesh=fine,
        in_specs=(
            P(EVERY, None, None, None),
            P(EVERY, None, None, None),
            P(EVERY),
            P(seg, dp, None),
            P(seg, dp, None),
            P(seg, dp),
            P(seg, dp),
            P(seg, dp),
            P(seg, dp),
        ),
        out_specs=(
            P(EVERY, None, None, None),
            P(EVERY, None, None, None),
            P(seg, dp, None),
            P(seg, dp, None),
            P(seg, dp),
            P(seg, dp),
            P(seg, dp),
            P(seg, dp),
        ),
        check_vma=False,
    )
```

```python
import functools

import jax
import jax.numpy as jnp
from jax import lax
from jax.experimental import pallas as pl
from jax.experimental.pallas import tpu as pltpu
from jax.sharding import Mesh, PartitionSpec as P

eps = 1e-05
PLANE = ("y", "x", "c")
EVERY = ("z", "y", "x", "c")
BF = jnp.bfloat16
F32 = jnp.float32


def nt(a, b):
    return lax.dot_general(a, b, (((1,), (1,)), ((), ())), preferred_element_type=F32)


def nn(a, b):
    return lax.dot_general(a, b, (((1,), (0,)), ((), ())), preferred_element_type=F32)


VMEM_CAP = 56 * 1024 * 1024
ANY = pl.BlockSpec(memory_space=pl.ANY)


def call(body, outs, scratch, flops, *args, deps=(), far=(), far_outs=()):
    moved = sum(a.size * a.dtype.itemsize for a in args) + sum(
        o.size * o.dtype.itemsize for o in outs
    )
    n = len(deps)

    def spec(a):
        return pl.BlockSpec(memory_space=pltpu.SMEM if a.dtype == jnp.int32 else pltpu.VMEM)

    return pl.pallas_call(
        lambda *refs: body(*refs[n:]),
        out_shape=outs,
        in_specs=[ANY] * n + [ANY if i in far else spec(a) for i, a in enumerate(args)],
        out_specs=[ANY if i in far_outs else spec(o) for i, o in enumerate(outs)],
        scratch_shapes=scratch,
        compiler_params=pltpu.CompilerParams(vmem_limit_bytes=VMEM_CAP),
        cost_estimate=pl.CostEstimate(flops=flops, bytes_accessed=moved, transcendentals=0),
    )(*deps, *args)


def chunk(i, size):
    return pl.ds(pl.multiple_of(i * size, 16), size)


def clear_borders(pad_ref, side, plane, nf):
    zrow = jnp.zeros(pad_ref.shape[1:], BF)
    pad_ref[0] = zrow
    pad_ref[side + 1] = zrow
    zcol = jnp.zeros((nf, pad_ref.shape[2]), BF)
    for i in range(side):
        pad_ref[i + 1, 0:nf] = zcol
        pad_ref[i + 1, nf + plane : 2 * nf + plane] = zcol


def by_rank(slices, rank):
    odd = lax.rem(rank, 2) == 1
    for p in range(len(slices) // 2):
        a, b = slices[2 * p], slices[2 * p + 1]
        yield lax.bitwise_xor(rank // 2, p), odd, a, b


def halves(odd, own, mate):
    low = lax.broadcasted_iota(jnp.int32, own.shape, 1) < 64
    own, mate = own.astype(F32), mate.astype(F32)
    a, b = jnp.where(odd, mate, own), jnp.where(odd, own, mate)
    top = jnp.where(low, a, pltpu.roll(b, 64, 1))
    bottom = jnp.where(low, pltpu.roll(a, 64, 1), b)
    return top, bottom


def store_packed(rank, mate_ref, keep_ref, part, k, step, low):
    rows_now = chunk(k, step)
    odd = lax.rem(rank, 2) == 1
    for q in range(keep_ref.shape[0]):
        x = part[:step, 128 * q : 128 * q + 128]
        y = part[step:, 128 * q : 128 * q + 128]
        even_slice = jnp.where(low, x, pltpu.roll(y, 64, 1))
        odd_slice = jnp.where(low, pltpu.roll(x, 64, 1), y)
        p = lax.bitwise_xor(rank // 2, q)
        keep_ref[p, rows_now, :] = jnp.where(odd, odd_slice, even_slice).astype(BF)
        mate_ref[p, rows_now, :] = jnp.where(odd, even_slice, odd_slice).astype(BF)


def fetch_kernels(w_ref, ktm_ref, lw_ref, sems):
    nz, _, width = w_ref.shape
    hc = ktm_ref.shape[0]
    copies = []
    for z in range(nz):
        copies.append(pltpu.make_async_copy(
            w_ref.at[z, pl.ds(0, hc)], ktm_ref.at[:, pl.ds(z * width, width)], sems.at[2 * z]))
        copies.append(pltpu.make_async_copy(
            w_ref.at[z, pl.ds(hc, lw_ref.shape[1])], lw_ref.at[z], sems.at[2 * z + 1]))
    for copy in copies:
        copy.start()
    return copies


def join_temporal(lw_ref, lf_ref, ltm_ref):
    ch = ltm_ref.shape[1]
    width = lw_ref.shape[2] // 2
    count = 2 * lw_ref.shape[0]
    size = ltm_ref.shape[0] // count
    for z in range(lw_ref.shape[0]):
        first = lw_ref[z, :, 0:ch].astype(F32)
        off = width % 128
        second = lw_ref[z, :, width - off : width - off + ch + 128].astype(F32)
        second = pltpu.roll(second, ch + 128 - off, 1)[:, 0:ch]
        for b, block in ((2 * z, first), (2 * z + 1, second)):
            lf_ref[b * size : b * size + block.shape[0], :] = block
    ltm_ref[...] = lf_ref[0 : ltm_ref.shape[0], :].astype(BF)


def prepare_body(w_ref, kn_out, l_out, lt_out, rows_out, ktm_ref, lw_ref, lf_ref, sems):
    hc, ch = ktm_ref.shape[0], l_out.shape[1]
    for copy in fetch_kernels(w_ref, ktm_ref, lw_ref, sems):
        copy.wait()
    for t in range(9):
        kn_out[t] = ktm_ref[:, t * ch : (t + 1) * ch].astype(F32).T.astype(BF)
    join_temporal(lw_ref, lf_ref, l_out)
    rows_out[...] = lw_ref[:, lw_ref.shape[1] - rows_out.shape[1] :, :]
    for t in range(3):
        lt_out[t] = lf_ref[t * hc : (t + 1) * hc].T.astype(BF)


def prepare(w, hc, ch, deps=()):
    outs = [
        jax.ShapeDtypeStruct((9, ch, hc), BF),
        jax.ShapeDtypeStruct((3 * hc, ch), BF),
        jax.ShapeDtypeStruct((3, ch, hc), BF),
        jax.ShapeDtypeStruct((w.shape[0], 16, w.shape[2]), BF),
    ]
    tall = w.shape[1] - hc
    scratch = [
        pltpu.VMEM((hc, 9 * ch), BF),
        pltpu.VMEM((w.shape[0], tall, w.shape[2]), BF),
        pltpu.VMEM((3 * hc + tall, ch), F32),
        pltpu.SemaphoreType.DMA((2 * w.shape[0],)),
    ]
    return call(prepare_body, outs, scratch, 2 * w.size * 512, w, deps=deps, far=(0,))


def conv_body(side, first, rank_ref, *refs):
    n = 1 if first else 8
    slices = refs[:n]
    (kn_in, ltm_ref, vec_ref, before_ref, after_ref,
     pad_out, hid_out, xhat_out, rs_ref, mate_ref, keep_ref,
     pad_ref, hid_ref, xhat_ref, sp_ref, kn_ref, sems) = refs[n:]
    rank = rank_ref[0]
    kn_copy = pltpu.make_async_copy(kn_in, kn_ref, sems.at[0])
    kn_copy.start()
    ch, hc = pad_ref.shape[2], hid_ref.shape[1]
    rows = hid_ref.shape[0]
    plane = rows // side
    nf = plane // side
    step = plane // 2
    clear_borders(pad_ref, side, plane, nf)
    if first:
        for i in range(side):
            pad_ref[i + 1, nf : nf + plane] = slices[0][i * plane : (i + 1) * plane]
    else:
        def place(k, carry):
            for q, odd, a_ref, b_ref in by_rank(slices, rank):
                top, bottom = halves(odd, a_ref[chunk(k, step), :], b_ref[chunk(k, step), :])
                lanes = pl.ds(pl.multiple_of(128 * q, 128), 128)
                for piece, kk in ((top, k), (bottom, k + side)):
                    at = nf + lax.rem(kk, 2) * step
                    pad_ref[1 + kk // 2, pl.ds(pl.multiple_of(at, 16), step), lanes] = piece.astype(BF)
            return carry

        lax.fori_loop(0, side, place, 0, unroll=True)
    pad_copy = pltpu.make_async_copy(pad_ref, pad_out, sems.at[1])
    pad_copy.start()
    kn_copy.wait()

    def conv(i, total):
        acc = jnp.zeros((plane, hc), F32)
        for t in range(9):
            r, c = t // 3, t % 3
            acc += nn(pad_ref[i + r, c * nf : c * nf + plane, :], kn_ref[t])
        sp_ref[i] = acc
        return total + jnp.sum(acc, axis=0, keepdims=True)

    mean = lax.fori_loop(0, side, conv, jnp.zeros((1, hc), F32), unroll=True) / rows

    def square(i, total):
        cen = sp_ref[i] - mean
        return total + jnp.sum(cen * cen, axis=0, keepdims=True)

    var = lax.fori_loop(0, side, square, jnp.zeros((1, hc), F32), unroll=True) / rows
    rs = lax.rsqrt(var + eps)
    rs_ref[...] = rs
    gain, bias = vec_ref[0:1, :], vec_ref[1:2, :]

    def act(i, carry):
        xhat = (sp_ref[i] - mean) * rs
        xhat_ref[i] = xhat
        v = xhat * gain + bias
        v = v * jax.nn.sigmoid(v)
        sp_ref[i] = v
        hid_ref[chunk(i, plane), :] = v.astype(BF)
        return carry

    lax.fori_loop(0, side, act, 0, unroll=True)
    late = [
        pltpu.make_async_copy(hid_ref, hid_out, sems.at[2]),
        pltpu.make_async_copy(xhat_ref, xhat_out, sems.at[3]),
    ]
    for copy in late:
        copy.start()
    low = lax.broadcasted_iota(jnp.int32, (step, 128), 1) < 64

    def temporal(k, carry):
        pieces = []
        for kk in (k, k + side):
            par = lax.rem(kk, 2)
            h = sp_ref[kk // 2, pl.ds(pl.multiple_of(par * step, 8), step), :]
            at = pl.multiple_of(par * (step % nf), 8)
            pieces.append((
                (pltpu.roll(h, 1, 0) * before_ref[pl.ds(at, step), :]).astype(BF),
                h.astype(BF),
                (pltpu.roll(h, step - 1, 0) * after_ref[pl.ds(at, step), :]).astype(BF),
            ))
        part = sum(
            nn(jnp.concatenate([x, y], axis=0), ltm_ref[t * hc : (t + 1) * hc])
            for t, (x, y) in enumerate(zip(*pieces))
        )
        store_packed(rank, mate_ref, keep_ref, part, k, step, low)
        return carry

    lax.fori_loop(0, side, temporal, 0, unroll=True)
    for copy in [pad_copy] + late:
        copy.wait()


def conv_forward(rank, g, kn, lt, vec, before, after, side, pixels, ch, deps=()):
    hc = vec.shape[1]
    plane = pixels // side
    nf = plane // side
    n = len(g)
    shapes = [
        ((side + 2, plane + 2 * nf, ch), BF),
        ((pixels, hc), BF),
        ((side, plane, hc), F32),
    ]
    outs = [jax.ShapeDtypeStruct(*s) for s in shapes] + [
        jax.ShapeDtypeStruct((1, hc), F32),
        jax.ShapeDtypeStruct((4, pixels // 2, 128), BF),
        jax.ShapeDtypeStruct((4, pixels // 2, 128), BF),
    ]
    scratch = [pltpu.VMEM(*s) for s in shapes] + [
        pltpu.VMEM((side, plane, hc), F32),
        pltpu.VMEM((9, ch, hc), BF),
        pltpu.SemaphoreType.DMA((4,)),
    ]
    flops = 2 * pixels * hc * 12 * ch
    return call(functools.partial(conv_body, side, n == 1), outs, scratch, flops,
                rank, *g, kn, lt, vec, before, after,
                deps=deps, far=(n + 1,), far_outs=(0, 1, 2))


def fold(v):
    return v + pltpu.roll(v, 64, 1)


def total_of(refs):
    t = refs[0][...].astype(F32)
    for ref in refs[1:]:
        t += ref[...].astype(F32)
    return t


def pair_sum_body(keep_ref, mate_ref, *out_refs):
    for p, ref in enumerate(out_refs):
        ref[...] = (keep_ref[p].astype(F32) + mate_ref[p].astype(F32)).astype(ref.dtype)


def pair_sum(keep, arrived, deps=()):
    shape = keep.shape[1:]
    outs = [jax.ShapeDtypeStruct(shape, BF)] * keep.shape[0]
    return call(pair_sum_body, outs, [], keep.size, keep, arrived, deps=deps)


def out_norm_body(n, has_skip, *refs):
    parts, refs = refs[:n], refs[n:]
    if has_skip:
        vec_ref, skip_ref, xhat_ref, rs_ref, pre_ref, res_ref = refs
    else:
        vec_ref, xhat_ref, rs_ref, pre_ref, res_ref = refs
    t = total_of(parts)
    pixels = 2 * t.shape[0]
    mean = fold(jnp.sum(t, axis=0, keepdims=True)) / pixels
    cen = t - mean
    rs = lax.rsqrt(fold(jnp.sum(cen * cen, axis=0, keepdims=True)) / pixels + eps)
    xhat = cen * rs
    pre = xhat * vec_ref[0:1, :] + vec_ref[1:2, :]
    if has_skip:
        pre = pre + skip_ref[...].astype(F32)
    xhat_ref[...] = xhat
    rs_ref[...] = rs
    pre_ref[...] = pre
    res_ref[...] = (pre * jax.nn.sigmoid(pre)).astype(BF)


def out_norm(parts, vec, skip, deps=()):
    half = parts[0].shape[0]
    outs = [
        jax.ShapeDtypeStruct((half, 128), F32),
        jax.ShapeDtypeStruct((1, 128), F32),
        jax.ShapeDtypeStruct((half, 128), F32),
        jax.ShapeDtypeStruct((half, 128), BF),
    ]
    args = (*parts, vec) + (() if skip is None else (skip,))
    body = functools.partial(out_norm_body, len(parts), skip is not None)
    return call(body, outs, [], half * 128 * 10, *args, deps=deps)


def out_back_body(n, *refs):
    parts, (pre_ref, xhat_ref, rs_ref, vec_ref, dpre_ref, dt_ref, sums_ref) = refs[:n], refs[n:]
    g = total_of(parts)
    pre, xhat = pre_ref[...], xhat_ref[...]
    sig = jax.nn.sigmoid(pre)
    dpre = g * (sig * (1.0 + pre * (1.0 - sig)))
    pixels = 2 * pre.shape[0]
    sb = fold(jnp.sum(dpre, axis=0, keepdims=True))
    sg = fold(jnp.sum(dpre * xhat, axis=0, keepdims=True))
    dpre_ref[...] = dpre.astype(BF)
    scale = vec_ref[0:1, :] * rs_ref[...]
    dt_ref[...] = (scale * (dpre - sb / pixels - xhat * (sg / pixels))).astype(BF)
    sums_ref[0:1, :] = sg
    sums_ref[1:2, :] = sb


def out_back(parts, pre, xhat, rs, vec, deps=()):
    half = pre.shape[0]
    outs = [
        jax.ShapeDtypeStruct((half, 128), BF),
        jax.ShapeDtypeStruct((half, 128), BF),
        jax.ShapeDtypeStruct((2, 128), F32),
    ]
    args = (*parts, pre, xhat, rs, vec)
    return call(functools.partial(out_back_body, len(parts)), outs, [], half * 1280, *args, deps=deps)


def conv_back_body(side, rank_ref, *refs):
    slices, (xhat_in, rs_ref, w_ref, lnt_ref, vec_ref, before_ref, after_ref,
             dt_out, ds_out, sums_ref, mate_ref, keep_ref,
             dt_ref, ds_ref, xhat_ref, dy_ref, pad_ref, ktm_ref, sems) = refs[:8], refs[8:]
    half = slices[0].shape[0]
    rank = rank_ref[0]
    nz, _, width = w_ref.shape
    rows = 2 * half
    plane = rows // side
    nf = plane // side
    step = plane // 2
    hc = ds_ref.shape[1]
    ch = dt_ref.shape[1]
    fetched = [
        pltpu.make_async_copy(
            w_ref.at[z, pl.ds(0, hc)], ktm_ref.at[:, pl.ds(z * width, width)], sems.at[z])
        for z in range(nz)
    ]
    xhat_copy = pltpu.make_async_copy(xhat_in, xhat_ref, sems.at[nz])
    for copy in fetched + [xhat_copy]:
        copy.start()
    clear_borders(pad_ref, side, plane, nf)

    def place(k, carry):
        for q, odd, a_ref, b_ref in by_rank(slices, rank):
            top, bottom = halves(odd, a_ref[chunk(k, step), :], b_ref[chunk(k, step), :])
            lanes = pl.ds(pl.multiple_of(128 * q, 128), 128)
            dt_ref[chunk(k, step), lanes] = top.astype(BF)
            dt_ref[pl.ds(pl.multiple_of(half + k * step, 16), step), lanes] = bottom.astype(BF)
        return carry

    lax.fori_loop(0, side, place, 0, unroll=True)
    dt_copy = pltpu.make_async_copy(dt_ref, dt_out, sems.at[nz + 1])
    dt_copy.start()
    xhat_copy.wait()
    gain, bias = vec_ref[0:1, :], vec_ref[1:2, :]

    def hidden_grad(i, sums):
        dt = dt_ref[chunk(i, plane), :]
        early = nn(dt, lnt_ref[0]) * before_ref[0:plane, :]
        late = nn(dt, lnt_ref[2]) * after_ref[0:plane, :]
        dh = nn(dt, lnt_ref[1]) + pltpu.roll(early, plane - 1, 0) + pltpu.roll(late, 1, 0)
        xhat = xhat_ref[i]
        v = xhat * gain + bias
        sig = jax.nn.sigmoid(v)
        dy = dh * (sig * (1.0 + v * (1.0 - sig)))
        dy_ref[i] = dy
        return (
            sums[0] + jnp.sum(dy * xhat, axis=0, keepdims=True),
            sums[1] + jnp.sum(dy, axis=0, keepdims=True),
        )

    zero = jnp.zeros((1, hc), F32)
    sg, sb = lax.fori_loop(0, side, hidden_grad, (zero, zero), unroll=True)
    sums_ref[0:1, :] = sg
    sums_ref[1:2, :] = sb
    scale = gain * rs_ref[...]

    def spatial_grad(i, carry):
        ds = (scale * (dy_ref[i] - sb / rows - xhat_ref[i] * (sg / rows))).astype(BF)
        pad_ref[i + 1, nf : nf + plane] = ds
        ds_ref[chunk(i, plane), :] = ds
        return carry

    lax.fori_loop(0, side, spatial_grad, 0, unroll=True)
    ds_copy = pltpu.make_async_copy(ds_ref, ds_out, sems.at[nz + 2])
    ds_copy.start()
    for copy in fetched:
        copy.wait()
    low = lax.broadcasted_iota(jnp.int32, (step, 128), 1) < 64

    def back(k, carry):
        acc = jnp.zeros((2 * step, ch), F32)
        for t in range(9):
            r, c = 2 - t // 3, 2 - t % 3
            pieces = []
            for kk in (k, k + side):
                at = c * nf + lax.rem(kk, 2) * step
                pieces.append(pad_ref[kk // 2 + r, pl.ds(pl.multiple_of(at, 16), step), :])
            acc += nn(jnp.concatenate(pieces, axis=0), ktm_ref[:, t * ch : (t + 1) * ch])
        store_packed(rank, mate_ref, keep_ref, acc, k, step, low)
        return carry

    lax.fori_loop(0, side, back, 0, unroll=True)
    dt_copy.wait()
    ds_copy.wait()


def conv_back(rank, g, xhat, rs, w, lnt, vec, before, after, side, deps=()):
    half = g[0].shape[0]
    hc = vec.shape[1]
    ch = len(g) * 64
    pixels = 2 * half
    plane = pixels // side
    nf = plane // side
    outs = [
        jax.ShapeDtypeStruct((pixels, ch), BF),
        jax.ShapeDtypeStruct((pixels, hc), BF),
        jax.ShapeDtypeStruct((2, hc), F32),
        jax.ShapeDtypeStruct((4, half, 128), BF),
        jax.ShapeDtypeStruct((4, half, 128), BF),
    ]
    scratch = [
        pltpu.VMEM((pixels, ch), BF),
        pltpu.VMEM((pixels, hc), BF),
        pltpu.VMEM((side, plane, hc), F32),
        pltpu.VMEM((side, plane, hc), F32),
        pltpu.VMEM((side + 2, plane + 2 * nf, hc), BF),
        pltpu.VMEM((hc, 9 * ch), BF),
        pltpu.SemaphoreType.DMA((w.shape[0] + 3,)),
    ]
    flops = 2 * pixels * hc * 12 * ch
    return call(functools.partial(conv_back_body, side), outs, scratch, flops,
                rank, *g, xhat, rs, w, lnt, vec, before, after,
                deps=deps, far=(9, 11), far_outs=(0, 1))


def grads_body(side, pad_ref, hid_ref, ds_ref, dt_ref, before_ref, after_ref, mid_ref, out_ref,
               sg_ref, dst_ref, taps_ref, tg_ref, vec_ref):
    ch = pad_ref.shape[2]
    hc = hid_ref.shape[1]
    plane = hid_ref.shape[0] // side
    nf = plane // side
    for i in (0, 1, side + 2, side + 3):
        dst_ref[i] = jnp.zeros(dst_ref.shape[1:], BF)
    for i in range(side):
        at = slice(i * plane, (i + 1) * plane)
        h = hid_ref[at, :].astype(F32)
        taps_ref[i, 0:hc] = (pltpu.roll(h, 1, 0) * before_ref[0:plane, :]).T.astype(BF)
        taps_ref[i, hc : 2 * hc] = h.T.astype(BF)
        taps_ref[i, 2 * hc : 3 * hc] = (pltpu.roll(h, plane - 1, 0) * after_ref[0:plane, :]).T.astype(BF)
        dst_ref[i + 2] = ds_ref[at, :].astype(F32).T.astype(BF)
    tg_ref[0 : 3 * hc, :] = sum(
        nn(taps_ref[i], dt_ref[i * plane : (i + 1) * plane, :]) for i in range(side)
    )
    tg_ref[3 * hc :, :] = jnp.zeros((tg_ref.shape[0] - 3 * hc, ch), F32)
    nz, _, width = sg_ref.shape
    size = 3 * hc // (2 * nz)
    vec_ref[...] = jnp.zeros(vec_ref.shape, F32)
    vec_ref[size : size + 2, 0:hc] = mid_ref[...]
    vec_ref[size + 2 : size + 4, 0:128] = out_ref[...]
    tall = vec_ref.shape[0]
    inside = lax.broadcasted_iota(jnp.int32, (tall, ch), 0) < size
    off = (width // 2) % 128
    for z in range(nz):
        first, second = [
            jnp.where(inside, tg_ref[b * size : b * size + tall, :], vec_ref[...])
            for b in (2 * z, 2 * z + 1)
        ]
        start = width // 2 - off
        sg_ref[z, hc : hc + tall, 0:ch] = first.astype(BF)
        second = pltpu.roll(jnp.concatenate([second, jnp.zeros((tall, 128), F32)], axis=1), off, 1)
        sg_ref[z, hc : hc + tall, start : start + ch + 128] = second.astype(BF)
    for c in range(3):
        acc = sum(
            nn(dst_ref[i : i + 3].reshape(3 * hc, plane), pad_ref[i, c * nf : c * nf + plane, :])
            for i in range(1, side + 1)
        )
        for r in range(3):
            first = (3 * r + c) * ch
            end = first + ch
            at = (2 - r) * hc
            done = 0
            while first < end:
                z = first // width
                last = min(end, (z + 1) * width)
                sg_ref[z, 0:hc, first - z * width : last - z * width] = (
                    acc[at : at + hc, done : done + last - first].astype(BF)
                )
                done += last - first
                first = last


def kernel_grads(pad, hidden, ds, dt, before, after, mid, out, side, shape, deps=()):
    pixels, hc = hidden.shape
    ch = dt.shape[1]
    plane = pixels // side
    outs = [jax.ShapeDtypeStruct(shape, BF)]
    tall = shape[1] - hc
    scratch = [
        pltpu.VMEM((side + 4, hc, plane), BF),
        pltpu.VMEM((side, 3 * hc, plane), BF),
        pltpu.VMEM((3 * hc + tall, ch), F32),
        pltpu.VMEM((tall, ch), F32),
    ]
    flops = 2 * pixels * hc * 12 * ch
    return call(functools.partial(grads_body, side), outs, scratch, flops,
                pad, hidden, ds, dt, before, after, mid, out, deps=deps)[0]


def pass_on_body(*refs):
    pass


def after_all(v, *deps):
    n = len(deps)
    return pl.pallas_call(
        pass_on_body,
        out_shape=jax.ShapeDtypeStruct(v.shape, v.dtype),
        in_specs=[ANY] * (n + 1),
        out_specs=ANY,
        input_output_aliases={n: 0},
        cost_estimate=pl.CostEstimate(flops=0, bytes_accessed=0, transcendentals=0),
    )(*deps, v)


def pack_kernels_body(kt_ref, lt_ref, vec_ref, out_ref, low_ref):
    ranks, _, width = out_ref.shape
    hc = kt_ref.shape[0] // ranks
    blocks = lt_ref.shape[0] // hc
    q = hc // ranks
    low_ref[...] = jnp.zeros(low_ref.shape, F32)
    for r in range(ranks):
        out_ref[r, 0:hc, :] = kt_ref[r * hc : (r + 1) * hc, :]
        for b in range(blocks):
            low_ref[r, b * q : (b + 1) * q, 0 : lt_ref.shape[1]] = (
                lt_ref[b * hc + r * q : b * hc + (r + 1) * q, :]
            )
        low_ref[r, blocks * q : blocks * q + 1, :] = vec_ref[...]
        out_ref[r, hc:, :] = low_ref[r].astype(BF)


def pack_kernels(kt, lt, vec, ranks, tall, deps):
    width = kt.shape[1]
    outs = [jax.ShapeDtypeStruct((ranks, kt.shape[0] // ranks + tall, width), BF)]
    scratch = [pltpu.VMEM((ranks, tall, width), F32)]
    return call(pack_kernels_body, outs, scratch, kt.size * 8, kt, lt, vec, deps=deps)[0]


def call(body, outs, scratch, flops, *args, deps=(), far=(), far_outs=()):
    moved = sum(a.size * a.dtype.itemsize for a in args) + sum(
        o.size * o.dtype.itemsize for o in outs
    )
    n = len(deps)

    def spec(a):
        return pl.BlockSpec(memory_space=pltpu.SMEM if a.dtype == jnp.int32 else pltpu.VMEM)

    return pl.pallas_call(
        lambda *refs: body(*refs[n:]),
        out_shape=outs,
        in_specs=[ANY] * n + [ANY if i in far else spec(a) for i, a in enumerate(args)],
        out_specs=[ANY if i in far_outs else spec(o) for i, o in enumerate(outs)],
        scratch_shapes=scratch,
        compiler_params=pltpu.CompilerParams(vmem_limit_bytes=VMEM_CAP),
        cost_estimate=pl.CostEstimate(flops=flops, bytes_accessed=moved, transcendentals=0),
    )(*deps, *args)


def chunk(i, size):
    return pl.ds(pl.multiple_of(i * size, 16), size)


def clear_borders(pad_ref, side, plane, nf):
    zrow = jnp.zeros(pad_ref.shape[1:], BF)
    pad_ref[0] = zrow
    pad_ref[side + 1] = zrow
    zcol = jnp.zeros((nf, pad_ref.shape[2]), BF)
    for i in range(side):
        pad_ref[i + 1, 0:nf] = zcol
        pad_ref[i + 1, nf + plane : 2 * nf + plane] = zcol


def by_rank(slices, rank):
    odd = lax.rem(rank, 2) == 1
    for p in range(len(slices) // 2):
        a, b = slices[2 * p], slices[2 * p + 1]
        yield lax.bitwise_xor(rank // 2, p), odd, a, b


def halves(odd, own, mate):
    low = lax.broadcasted_iota(jnp.int32, own.shape, 1) < 64
    own, mate = own.astype(F32), mate.astype(F32)
    a, b = jnp.where(odd, mate, own), jnp.where(odd, own, mate)
    top = jnp.where(low, a, pltpu.roll(b, 64, 1))
    bottom = jnp.where(low, pltpu.roll(a, 64, 1), b)
    return top, bottom


def store_packed(rank, mate_ref, keep_ref, part, k, step, low):
    rows_now = chunk(k, step)
    odd = lax.rem(rank, 2) == 1
    for q in range(keep_ref.shape[0]):
        x = part[:step, 128 * q : 128 * q + 128]
        y = part[step:, 128 * q : 128 * q + 128]
        even_slice = jnp.where(low, x, pltpu.roll(y, 64, 1))
        odd_slice = jnp.where(low, pltpu.roll(x, 64, 1), y)
        p = lax.bitwise_xor(rank // 2, q)
        keep_ref[p, rows_now, :] = jnp.where(odd, odd_slice, even_slice).astype(BF)
        mate_ref[p, rows_now, :] = jnp.where(odd, even_slice, odd_slice).astype(BF)


def fetch_kernels(w_ref, ktm_ref, lw_ref, sems):
    nz, _, width = w_ref.shape
    hc = ktm_ref.shape[0]
    copies = []
    for z in range(nz):
        copies.append(pltpu.make_async_copy(
            w_ref.at[z, pl.ds(0, hc)], ktm_ref.at[:, pl.ds(z * width, width)], sems.at[2 * z]))
        copies.append(pltpu.make_async_copy(
            w_ref.at[z, pl.ds(hc, lw_ref.shape[1])], lw_ref.at[z], sems.at[2 * z + 1]))
    for copy in copies:
        copy.start()
    return copies


def join_temporal(lw_ref, lf_ref, ltm_ref):
    ch = ltm_ref.shape[1]
    width = lw_ref.shape[2] // 2
    count = 2 * lw_ref.shape[0]
    size = ltm_ref.shape[0] // count
    for z in range(lw_ref.shape[0]):
        first = lw_ref[z, :, 0:ch].astype(F32)
        off = width % 128
        second = lw_ref[z, :, width - off : width - off + ch + 128].astype(F32)
        second = pltpu.roll(second, ch + 128 - off, 1)[:, 0:ch]
        for b, block in ((2 * z, first), (2 * z + 1, second)):
            lf_ref[b * size : b * size + block.shape[0], :] = block
    ltm_ref[...] = lf_ref[0 : ltm_ref.shape[0], :].astype(BF)


def prepare_body(w_ref, kn_out, l_out, lt_out, rows_out, ktm_ref, lw_ref, lf_ref, sems):
    hc, ch = ktm_ref.shape[0], l_out.shape[1]
    for copy in fetch_kernels(w_ref, ktm_ref, lw_ref, sems):
        copy.wait()
    for t in range(9):
        kn_out[t] = ktm_ref[:, t * ch : (t + 1) * ch].astype(F32).T.astype(BF)
    join_temporal(lw_ref, lf_ref, l_out)
    rows_out[...] = lw_ref[:, lw_ref.shape[1] - rows_out.shape[1] :, :]
    for t in range(3):
        lt_out[t] = lf_ref[t * hc : (t + 1) * hc].T.astype(BF)


def prepare(w, hc, ch, deps=()):
    outs = [
        jax.ShapeDtypeStruct((9, ch, hc), BF),
        jax.ShapeDtypeStruct((3 * hc, ch), BF),
        jax.ShapeDtypeStruct((3, ch, hc), BF),
        jax.ShapeDtypeStruct((w.shape[0], 16, w.shape[2]), BF),
    ]
    tall = w.shape[1] - hc
    scratch = [
        pltpu.VMEM((hc, 9 * ch), BF),
        pltpu.VMEM((w.shape[0], tall, w.shape[2]), BF),
        pltpu.VMEM((3 * hc + tall, ch), F32),
        pltpu.SemaphoreType.DMA((2 * w.shape[0],)),
    ]
    return call(prepare_body, outs, scratch, 2 * w.size * 512, w, deps=deps, far=(0,))


def conv_body(side, first, rank_ref, *refs):
    n = 1 if first else 8
    slices = refs[:n]
    (kn_in, ltm_ref, vec_ref, before_ref, after_ref,
     pad_out, hid_out, xhat_out, rs_ref, mate_ref, keep_ref,
     pad_ref, hid_ref, xhat_ref, sp_ref, kn_ref, sems) = refs[n:]
    rank = rank_ref[0]
    kn_copy = pltpu.make_async_copy(kn_in, kn_ref, sems.at[0])
    kn_copy.start()
    ch, hc = pad_ref.shape[2], hid_ref.shape[1]
    rows = hid_ref.shape[0]
    plane = rows // side
    nf = plane // side
    step = plane // 2
    clear_borders(pad_ref, side, plane, nf)
    if first:
        for i in range(side):
            pad_ref[i + 1, nf : nf + plane] = slices[0][i * plane : (i + 1) * plane]
    else:
        def place(k, carry):
            for q, odd, a_ref, b_ref in by_rank(slices, rank):
                top, bottom = halves(odd, a_ref[chunk(k, step), :], b_ref[chunk(k, step), :])
                lanes = pl.ds(pl.multiple_of(128 * q, 128), 128)
                for piece, kk in ((top, k), (bottom, k + side)):
                    at = nf + lax.rem(kk, 2) * step
                    pad_ref[1 + kk // 2, pl.ds(pl.multiple_of(at, 16), step), lanes] = piece.astype(BF)
            return carry

        lax.fori_loop(0, side, place, 0, unroll=True)
    pad_copy = pltpu.make_async_copy(pad_ref, pad_out, sems.at[1])
    pad_copy.start()
    kn_copy.wait()

    def conv(i, total):
        acc = jnp.zeros((plane, hc), F32)
        for t in range(9):
            r, c = t // 3, t % 3
            acc += nn(pad_ref[i + r, c * nf : c * nf + plane, :], kn_ref[t])
        sp_ref[i] = acc
        return total + jnp.sum(acc, axis=0, keepdims=True)

    mean = lax.fori_loop(0, side, conv, jnp.zeros((1, hc), F32), unroll=True) / rows

    def square(i, total):
        cen = sp_ref[i] - mean
        return total + jnp.sum(cen * cen, axis=0, keepdims=True)

    var = lax.fori_loop(0, side, square, jnp.zeros((1, hc), F32), unroll=True) / rows
    rs = lax.rsqrt(var + eps)
    rs_ref[...] = rs
    gain, bias = vec_ref[0:1, :], vec_ref[1:2, :]

    def act(i, carry):
        xhat = (sp_ref[i] - mean) * rs
        xhat_ref[i] = xhat
        v = xhat * gain + bias
        v = v * jax.nn.sigmoid(v)
        sp_ref[i] = v
        hid_ref[chunk(i, plane), :] = v.astype(BF)
        return carry

    lax.fori_loop(0, side, act, 0, unroll=True)
    late = [
        pltpu.make_async_copy(hid_ref, hid_out, sems.at[2]),
        pltpu.make_async_copy(xhat_ref, xhat_out, sems.at[3]),
    ]
    for copy in late:
        copy.start()
    low = lax.broadcasted_iota(jnp.int32, (step, 128), 1) < 64

    def temporal(k, carry):
        pieces = []
        for kk in (k, k + side):
            par = lax.rem(kk, 2)
            h = sp_ref[kk // 2, pl.ds(pl.multiple_of(par * step, 8), step), :]
            at = pl.multiple_of(par * (step % nf), 8)
            pieces.append((
                (pltpu.roll(h, 1, 0) * before_ref[pl.ds(at, step), :]).astype(BF),
                h.astype(BF),
                (pltpu.roll(h, step - 1, 0) * after_ref[pl.ds(at, step), :]).astype(BF),
            ))
        part = sum(
            nn(jnp.concatenate([x, y], axis=0), ltm_ref[t * hc : (t + 1) * hc])
            for t, (x, y) in enumerate(zip(*pieces))
        )
        store_packed(rank, mate_ref, keep_ref, part, k, step, low)
        return carry

    lax.fori_loop(0, side, temporal, 0, unroll=True)
    for copy in [pad_copy] + late:
        copy.wait()


def conv_forward(rank, g, kn, lt, vec, before, after, side, pixels, ch, deps=()):
    hc = vec.shape[1]
    plane = pixels // side
    nf = plane // side
    n = len(g)
    shapes = [
        ((side + 2, plane + 2 * nf, ch), BF),
        ((pixels, hc), BF),
        ((side, plane, hc), F32),
    ]
    outs = [jax.ShapeDtypeStruct(*s) for s in shapes] + [
        jax.ShapeDtypeStruct((1, hc), F32),
        jax.ShapeDtypeStruct((4, pixels // 2, 128), BF),
        jax.ShapeDtypeStruct((4, pixels // 2, 128), BF),
    ]
    scratch = [pltpu.VMEM(*s) for s in shapes] + [
        pltpu.VMEM((side, plane, hc), F32),
        pltpu.VMEM((9, ch, hc), BF),
        pltpu.SemaphoreType.DMA((4,)),
    ]
    flops = 2 * pixels * hc * 12 * ch
    return call(functools.partial(conv_body, side, n == 1), outs, scratch, flops,
                rank, *g, kn, lt, vec, before, after,
                deps=deps, far=(n + 1,), far_outs=(0, 1, 2))


def fold(v):
    return v + pltpu.roll(v, 64, 1)


def total_of(refs):
    t = refs[0][...].astype(F32)
    for ref in refs[1:]:
        t += ref[...].astype(F32)
    return t


def pair_sum_body(keep_ref, mate_ref, *out_refs):
    for p, ref in enumerate(out_refs):
        ref[...] = (keep_ref[p].astype(F32) + mate_ref[p].astype(F32)).astype(ref.dtype)


def pair_sum(keep, arrived, deps=()):
    shape = keep.shape[1:]
    outs = [jax.ShapeDtypeStruct(shape, BF)] * keep.shape[0]
    return call(pair_sum_body, outs, [], keep.size, keep, arrived, deps=deps)


def out_norm_body(n, has_skip, *refs):
    parts, refs = refs[:n], refs[n:]
    if has_skip:
        vec_ref, skip_ref, xhat_ref, rs_ref, pre_ref, res_ref = refs
    else:
        vec_ref, xhat_ref, rs_ref, pre_ref, res_ref = refs
    t = total_of(parts)
    pixels = 2 * t.shape[0]
    mean = fold(jnp.sum(t, axis=0, keepdims=True)) / pixels
    cen = t - mean
    rs = lax.rsqrt(fold(jnp.sum(cen * cen, axis=0, keepdims=True)) / pixels + eps)
    xhat = cen * rs
    pre = xhat * vec_ref[0:1, :] + vec_ref[1:2, :]
    if has_skip:
        pre = pre + skip_ref[...].astype(F32)
    xhat_ref[...] = xhat
    rs_ref[...] = rs
    pre_ref[...] = pre
    res_ref[...] = (pre * jax.nn.sigmoid(pre)).astype(BF)


def out_norm(parts, vec, skip, deps=()):
    half = parts[0].shape[0]
    outs = [
        jax.ShapeDtypeStruct((half, 128), F32),
        jax.ShapeDtypeStruct((1, 128), F32),
        jax.ShapeDtypeStruct((half, 128), F32),
        jax.ShapeDtypeStruct((half, 128), BF),
    ]
    args = (*parts, vec) + (() if skip is None else (skip,))
    body = functools.partial(out_norm_body, len(parts), skip is not None)
    return call(body, outs, [], half * 128 * 10, *args, deps=deps)


def out_back_body(n, *refs):
    parts, (pre_ref, xhat_ref, rs_ref, vec_ref, dpre_ref, dt_ref, sums_ref) = refs[:n], refs[n:]
    g = total_of(parts)
    pre, xhat = pre_ref[...], xhat_ref[...]
    sig = jax.nn.sigmoid(pre)
    dpre = g * (sig * (1.0 + pre * (1.0 - sig)))
    pixels = 2 * pre.shape[0]
    sb = fold(jnp.sum(dpre, axis=0, keepdims=True))
    sg = fold(jnp.sum(dpre * xhat, axis=0, keepdims=True))
    dpre_ref[...] = dpre.astype(BF)
    scale = vec_ref[0:1, :] * rs_ref[...]
    dt_ref[...] = (scale * (dpre - sb / pixels - xhat * (sg / pixels))).astype(BF)
    sums_ref[0:1, :] = sg
    sums_ref[1:2, :] = sb


def out_back(parts, pre, xhat, rs, vec, deps=()):
    half = pre.shape[0]
    outs = [
        jax.ShapeDtypeStruct((half, 128), BF),
        jax.ShapeDtypeStruct((half, 128), BF),
        jax.ShapeDtypeStruct((2, 128), F32),
    ]
    args = (*parts, pre, xhat, rs, vec)
    return call(functools.partial(out_back_body, len(parts)), outs, [], half * 1280, *args, deps=deps)


def conv_back_body(side, rank_ref, *refs):
    slices, (xhat_in, rs_ref, w_ref, lnt_ref, vec_ref, before_ref, after_ref,
             dt_out, ds_out, sums_ref, mate_ref, keep_ref,
             dt_ref, ds_ref, xhat_ref, dy_ref, pad_ref, ktm_ref, sems) = refs[:8], refs[8:]
    half = slices[0].shape[0]
    rank = rank_ref[0]
    nz, _, width = w_ref.shape
    rows = 2 * half
    plane = rows // side
    nf = plane // side
    step = plane // 2
    hc = ds_ref.shape[1]
    ch = dt_ref.shape[1]
    fetched = [
        pltpu.make_async_copy(
            w_ref.at[z, pl.ds(0, hc)], ktm_ref.at[:, pl.ds(z * width, width)], sems.at[z])
        for z in range(nz)
    ]
    xhat_copy = pltpu.make_async_copy(xhat_in, xhat_ref, sems.at[nz])
    for copy in fetched + [xhat_copy]:
        copy.start()
    clear_borders(pad_ref, side, plane, nf)

    def place(k, carry):
        for q, odd, a_ref, b_ref in by_rank(slices, rank):
            top, bottom = halves(odd, a_ref[chunk(k, step), :], b_ref[chunk(k, step), :])
            lanes = pl.ds(pl.multiple_of(128 * q, 128), 128)
            dt_ref[chunk(k, step), lanes] = top.astype(BF)
            dt_ref[pl.ds(pl.multiple_of(half + k * step, 16), step), lanes] = bottom.astype(BF)
        return carry

    lax.fori_loop(0, side, place, 0, unroll=True)
    dt_copy = pltpu.make_async_copy(dt_ref, dt_out, sems.at[nz + 1])
    dt_copy.start()
    xhat_copy.wait()
    gain, bias = vec_ref[0:1, :], vec_ref[1:2, :]

    def hidden_grad(i, sums):
        dt = dt_ref[chunk(i, plane), :]
        early = nn(dt, lnt_ref[0]) * before_ref[0:plane, :]
        late = nn(dt, lnt_ref[2]) * after_ref[0:plane, :]
        dh = nn(dt, lnt_ref[1]) + pltpu.roll(early, plane - 1, 0) + pltpu.roll(late, 1, 0)
        xhat = xhat_ref[i]
        v = xhat * gain + bias
        sig = jax.nn.sigmoid(v)
        dy = dh * (sig * (1.0 + v * (1.0 - sig)))
        dy_ref[i] = dy
        return (
            sums[0] + jnp.sum(dy * xhat, axis=0, keepdims=True),
            sums[1] + jnp.sum(dy, axis=0, keepdims=True),
        )

    zero = jnp.zeros((1, hc), F32)
    sg, sb = lax.fori_loop(0, side, hidden_grad, (zero, zero), unroll=True)
    sums_ref[0:1, :] = sg
    sums_ref[1:2, :] = sb
    scale = gain * rs_ref[...]

    def spatial_grad(i, carry):
        ds = (scale * (dy_ref[i] - sb / rows - xhat_ref[i] * (sg / rows))).astype(BF)
        pad_ref[i + 1, nf : nf + plane] = ds
        ds_ref[chunk(i, plane), :] = ds
        return carry

    lax.fori_loop(0, side, spatial_grad, 0, unroll=True)
    ds_copy = pltpu.make_async_copy(ds_ref, ds_out, sems.at[nz + 2])
    ds_copy.start()
    for copy in fetched:
        copy.wait()
    low = lax.broadcasted_iota(jnp.int32, (step, 128), 1) < 64

    def back(k, carry):
        acc = jnp.zeros((2 * step, ch), F32)
        for t in range(9):
            r, c = 2 - t // 3, 2 - t % 3
            pieces = []
            for kk in (k, k + side):
                at = c * nf + lax.rem(kk, 2) * step
                pieces.append(pad_ref[kk // 2 + r, pl.ds(pl.multiple_of(at, 16), step), :])
            acc += nn(jnp.concatenate(pieces, axis=0), ktm_ref[:, t * ch : (t + 1) * ch])
        store_packed(rank, mate_ref, keep_ref, acc, k, step, low)
        return carry

    lax.fori_loop(0, side, back, 0, unroll=True)
    dt_copy.wait()
    ds_copy.wait()


def conv_back(rank, g, xhat, rs, w, lnt, vec, before, after, side, deps=()):
    half = g[0].shape[0]
    hc = vec.shape[1]
    ch = len(g) * 64
    pixels = 2 * half
    plane = pixels // side
    nf = plane // side
    outs = [
        jax.ShapeDtypeStruct((pixels, ch), BF),
        jax.ShapeDtypeStruct((pixels, hc), BF),
        jax.ShapeDtypeStruct((2, hc), F32),
        jax.ShapeDtypeStruct((4, half, 128), BF),
        jax.ShapeDtypeStruct((4, half, 128), BF),
    ]
    scratch = [
        pltpu.VMEM((pixels, ch), BF),
        pltpu.VMEM((pixels, hc), BF),
        pltpu.VMEM((side, plane, hc), F32),
        pltpu.VMEM((side, plane, hc), F32),
        pltpu.VMEM((side + 2, plane + 2 * nf, hc), BF),
        pltpu.VMEM((hc, 9 * ch), BF),
        pltpu.SemaphoreType.DMA((w.shape[0] + 3,)),
    ]
    flops = 2 * pixels * hc * 12 * ch
    return call(functools.partial(conv_back_body, side), outs, scratch, flops,
                rank, *g, xhat, rs, w, lnt, vec, before, after,
                deps=deps, far=(9, 11), far_outs=(0, 1))


def grads_body(side, pad_ref, hid_ref, ds_ref, dt_ref, before_ref, after_ref, mid_ref, out_ref,
               sg_ref, dst_ref, taps_ref, tg_ref, vec_ref):
    ch = pad_ref.shape[2]
    hc = hid_ref.shape[1]
    plane = hid_ref.shape[0] // side
    nf = plane // side
    for i in (0, 1, side + 2, side + 3):
        dst_ref[i] = jnp.zeros(dst_ref.shape[1:], BF)
    for i in range(side):
        at = slice(i * plane, (i + 1) * plane)
        h = hid_ref[at, :].astype(F32)
        taps_ref[i, 0:hc] = (pltpu.roll(h, 1, 0) * before_ref[0:plane, :]).T.astype(BF)
        taps_ref[i, hc : 2 * hc] = h.T.astype(BF)
        taps_ref[i, 2 * hc : 3 * hc] = (pltpu.roll(h, plane - 1, 0) * after_ref[0:plane, :]).T.astype(BF)
        dst_ref[i + 2] = ds_ref[at, :].astype(F32).T.astype(BF)
    tg_ref[0 : 3 * hc, :] = sum(
        nn(taps_ref[i], dt_ref[i * plane : (i + 1) * plane, :]) for i in range(side)
    )
    tg_ref[3 * hc :, :] = jnp.zeros((tg_ref.shape[0] - 3 * hc, ch), F32)
    nz, _, width = sg_ref.shape
    size = 3 * hc // (2 * nz)
    vec_ref[...] = jnp.zeros(vec_ref.shape, F32)
    vec_ref[size : size + 2, 0:hc] = mid_ref[...]
    vec_ref[size + 2 : size + 4, 0:128] = out_ref[...]
    tall = vec_ref.shape[0]
    inside = lax.broadcasted_iota(jnp.int32, (tall, ch), 0) < size
    off = (width // 2) % 128
    for z in range(nz):
        first, second = [
            jnp.where(inside, tg_ref[b * size : b * size + tall, :], vec_ref[...])
            for b in (2 * z, 2 * z + 1)
        ]
        start = width // 2 - off
        sg_ref[z, hc : hc + tall, 0:ch] = first.astype(BF)
        second = pltpu.roll(jnp.concatenate([second, jnp.zeros((tall, 128), F32)], axis=1), off, 1)
        sg_ref[z, hc : hc + tall, start : start + ch + 128] = second.astype(BF)
    for c in range(3):
        acc = sum(
            nn(dst_ref[i : i + 3].reshape(3 * hc, plane), pad_ref[i, c * nf : c * nf + plane, :])
            for i in range(1, side + 1)
        )
        for r in range(3):
            first = (3 * r + c) * ch
            end = first + ch
            at = (2 - r) * hc
            done = 0
            while first < end:
                z = first // width
                last = min(end, (z + 1) * width)
                sg_ref[z, 0:hc, first - z * width : last - z * width] = (
                    acc[at : at + hc, done : done + last - first].astype(BF)
                )
                done += last - first
                first = last


def kernel_grads(pad, hidden, ds, dt, before, after, mid, out, side, shape, deps=()):
    pixels, hc = hidden.shape
    ch = dt.shape[1]
    plane = pixels // side
    outs = [jax.ShapeDtypeStruct(shape, BF)]
    tall = shape[1] - hc
    scratch = [
        pltpu.VMEM((side + 4, hc, plane), BF),
        pltpu.VMEM((side, 3 * hc, plane), BF),
        pltpu.VMEM((3 * hc + tall, ch), F32),
        pltpu.VMEM((tall, ch), F32),
    ]
    flops = 2 * pixels * hc * 12 * ch
    return call(functools.partial(grads_body, side), outs, scratch, flops,
                pad, hidden, ds, dt, before, after, mid, out, deps=deps)[0]


def pass_on_body(*refs):
    pass


def after_all(v, *deps):
    n = len(deps)
    return pl.pallas_call(
        pass_on_body,
        out_shape=jax.ShapeDtypeStruct(v.shape, v.dtype),
        in_specs=[ANY] * (n + 1),
        out_specs=ANY,
        input_output_aliases={n: 0},
        cost_estimate=pl.CostEstimate(flops=0, bytes_accessed=0, transcendentals=0),
    )(*deps, v)


def pack_kernels_body(kt_ref, lt_ref, vec_ref, out_ref, low_ref):
    ranks, _, width = out_ref.shape
    hc = kt_ref.shape[0] // ranks
    blocks = lt_ref.shape[0] // hc
    q = hc // ranks
    low_ref[...] = jnp.zeros(low_ref.shape, F32)
    for r in range(ranks):
        out_ref[r, 0:hc, :] = kt_ref[r * hc : (r + 1) * hc, :]
        for b in range(blocks):
            low_ref[r, b * q : (b + 1) * q, 0 : lt_ref.shape[1]] = (
                lt_ref[b * hc + r * q : b * hc + (r + 1) * q, :]
            )
        low_ref[r, blocks * q : blocks * q + 1, :] = vec_ref[...]
        out_ref[r, hc:, :] = low_ref[r].astype(BF)


def pack_kernels(kt, lt, vec, ranks, tall, deps):
    width = kt.shape[1]
    outs = [jax.ShapeDtypeStruct((ranks, kt.shape[0] // ranks + tall, width), BF)]
    scratch = [pltpu.VMEM((ranks, tall, width), F32)]
    return call(pack_kernels_body, outs, scratch, kt.size * 8, kt, lt, vec, deps=deps)[0]


def hop(v, k):
    n = 1
    for name in EVERY:
        n *= lax.axis_size(name)
    return lax.ppermute(v, EVERY, [(i, i ^ k) for i in range(n)])


def plane_gather(v, aside=()):
    got = {0: v}
    for k in (6, 2, 4):
        got[k] = hop(v, k)
    got[1] = hop(after_all(v, *aside) if aside else v, 1)
    for k in (2, 4, 6):
        got[k ^ 1] = hop(got[k], 1)
    return [got[k] for k in range(8)]


def plane_reduce(mate, keep, deps=()):
    sums = pair_sum(keep, hop(mate, 1), deps)
    arrived = {k: hop(sums[k // 2], k) for k in (6, 2, 4)}
    return [sums[0], arrived[2], arrived[4], arrived[6]]


def on_device(frames, cot, starts, ks, ktm, mg, mb, og, ob):
    nz, n_rank, n_seg = lax.axis_size("z"), 8, 4
    n_dp = nz * 2
    fr, side, ch = frames.shape[0], frames.shape[1], frames.shape[3]
    area = side * side
    hid = ks.shape[2]
    hc, cc = hid // n_rank, ch // n_rank
    q = hc // n_rank
    rank = lax.axis_index(PLANE)
    rank_now = rank.astype(jnp.int32).reshape(1)
    d_index = lax.axis_index(("z", "y"))
    nf = n_dp * fr
    pixels = area * nf
    half = pixels // 2

    def keeper(d, s):
        v = (d // 2) ^ s
        return (d % 2) * 4 + (v % 2) * 2 + v // 2

    to_plane = [
        (d * n_seg + s, s * n_rank + keeper(d, s)) for d in range(n_dp) for s in range(n_seg)
    ]
    from_plane = [(b, a) for a, b in to_plane]
    rows = fr * area
    flag_row = jnp.pad(starts.astype(BF)[None], ((0, 11), (0, ch - fr)))
    lead = rows + 12
    moving = jnp.concatenate([frames.reshape(rows, ch), flag_row, cot.reshape(rows, ch)], axis=0)
    moving = lax.ppermute(moving, EVERY, to_plane)

    perm = (jnp.arange(hid).reshape(n_rank, n_rank, q).transpose(1, 0, 2).reshape(hid)[:, None]
            == jnp.arange(hid)[None, :]).astype(BF)
    kt = lax.dot_general(perm, ks[0].astype(BF), (((1,), (1,)), ((), ())),
                         preferred_element_type=F32).astype(BF)
    lrows, width = ktm.shape[1] // n_rank, ks.shape[1]
    tall = -(-(lrows + 4) // 16) * 16
    extra = jnp.concatenate([mg, mb, og, ob], axis=1)
    extra = jnp.pad(extra, ((0, 0), (0, width - extra.shape[1])))
    w = pack_kernels(kt, ktm[0], extra, n_rank, tall, deps=(moving,))
    w = lax.all_to_all(w, PLANE, 0, 0)
    here = w
    high = hc + tall

    w = w.reshape(2, n_seg, high, width).transpose(1, 2, 0, 3).reshape(n_seg, high, 2 * width)
    ws = [lax.all_gather(w[s], "z", axis=0) for s in range(n_seg)]

    group = 7
    own = moving[lead:].reshape(group, rows // group, n_rank, cc).transpose(2, 1, 0, 3)
    own = own.reshape(n_rank, rows // group, group * cc)
    own = jnp.pad(own, ((0, 0), (0, 4), (0, ch - group * cc)))
    own = jnp.concatenate([jnp.broadcast_to(moving[:lead], (n_rank, lead, ch)), own], axis=1)
    gathered = lax.all_to_all(after_all(own, here), PLANE, 0, 0)


    def norm_rows(rows_now):
        row = rows_now[:, (lrows - tall) % 16].reshape(n_dp, width).astype(F32)
        mid = jnp.stack([
            lax.dynamic_slice_in_dim(row[:, i * hc : (i + 1) * hc], rank * q, q, axis=1).reshape(hc)
            for i in range(2)])
        own = lax.dynamic_index_in_dim(row, rank, 0, keepdims=False)
        out = jnp.stack([
            jnp.tile(own[2 * hc + i * cc : 2 * hc + (i + 1) * cc], 2) for i in range(2)])
        return mid, out

    def by_pixel(v):
        width = v.shape[2]
        v = v.reshape(n_rank * fr, area, width).transpose(1, 0, 2)
        return v.reshape(pixels, width)

    def packed(v):
        return jnp.concatenate([v[:half], v[half:]], axis=1)

    a0 = by_pixel(gathered[:, :rows])
    flags = gathered[:, rows, :fr].reshape(nf) > 0.5
    slot = jnp.arange(nf) % fr
    before = jnp.where(flags | (slot == 0), 0.0, 1.0)
    after = jnp.where(jnp.roll(flags, -1) | (slot == fr - 1), 0.0, 1.0)
    spread = (side * nf + nf, hc)
    before = jnp.broadcast_to(jnp.tile(before, side + 1)[:, None], spread)
    after = jnp.broadcast_to(jnp.tile(after, side + 1)[:, None], spread)
    skip = packed(lax.dynamic_slice_in_dim(a0, rank * cc, cc, axis=1))

    def across(*slices):
        n = len(slices)
        v = jnp.stack([jnp.concatenate([v[:, :cc], v[:, cc:]], axis=0) for v in slices])
        v = v.reshape(n, area, n_rank, fr, cc).transpose(2, 0, 1, 3, 4).reshape(n_rank, n * rows, cc)
        return lax.all_to_all(v, PLANE, 0, 0)

    def home(v):
        n = v.shape[1] // rows
        v = v.transpose(1, 0, 2).reshape(n * rows, ch)
        v = lax.ppermute(v, EVERY, from_plane).reshape(n, area, fr, ch).transpose(0, 2, 1, 3)
        return v.reshape(n, *frames.shape)

    saved = []
    g = [a0]
    ready = prepare(ws[0], hc, ch, deps=(before, after))
    for s in range(n_seg):
        kn, lt, lnt, rows_now = ready
        mid, out = norm_rows(rows_now)
        pad, hidden, xm, rm, mate, keep = conv_forward(
            rank_now, g, kn, lt, mid, before, after, side, pixels, ch)
        parts = plane_reduce(mate, keep)
        xo, ro, pre, res = out_norm(parts, out, skip if s % 2 == 1 else None)
        saved.append((pad, hidden, xm, rm, xo, ro, pre, lnt, mid, out))
        if s % 2 == 1:
            skip = res
        if s < n_seg - 1:
            ready = prepare(ws[s + 1], hc, ch, deps=(res,))
            g = plane_gather(res, ready[:1])
    cot_own = gathered[:, lead : lead + rows // group, : group * cc]
    cot_own = cot_own.reshape(n_rank, rows // group, group, cc).transpose(0, 2, 1, 3)
    cot_own = packed(by_pixel(cot_own.reshape(n_rank, rows, cc)))

    parts = [cot_own]
    skip_grad = None

    grads, raw = [], None
    for s in reversed(range(n_seg)):
        pad, hidden, xm, rm, xo, ro, pre, lnt, mid, out = saved[s]
        if s == 1:
            parts = parts + [skip_grad]
        deps = () if raw is None else (raw, *grads[-2:-1])
        dpre, dt, osum = out_back(parts, pre, xo, ro, out, deps=deps)
        if s % 2 == 1:
            skip_grad = dpre
        dtf, ds, msum, mate, keep = conv_back(
            rank_now, plane_gather(dt), xm, rm, ws[s], lnt, mid, before, after, side)
        if s > 0:
            parts = plane_reduce(mate, keep)
        raw = kernel_grads(pad, hidden, ds, dtf, before, after, msum, osum, side, ws[s].shape,
                           deps=parts[:1] if s > 0 else ())
        if s > 0:
            grads.append(lax.psum_scatter(after_all(raw, parts[3]), "z", scatter_dimension=0))
    last = lax.psum_scatter(raw, "z", scatter_dimension=0)
    parts = plane_reduce(mate, keep, deps=(raw,))

    da = sum(p.astype(F32) for p in parts) + skip_grad.astype(F32)
    home_now = home(across(res, da.astype(BF)))
    output, frames_grad = home_now[0], home_now[1].astype(F32)

    def by_row(v):
        return v.reshape(high, 2, width).transpose(1, 0, 2)

    g = jnp.stack([by_row(v) for v in [last] + grads[::-1]], axis=1).reshape(n_rank, high, width)
    g = lax.all_to_all(g, PLANE, 0, 0)
    space_grad = lax.dot_general(g[:, :hc].reshape(hid, width), perm, (((0,), (0,)), ((), ())),
                                 preferred_element_type=F32)
    tg = g[:, hc : hc + lrows, :ch].reshape(n_rank, -1, q, ch)
    time_grad = tg.transpose(1, 0, 2, 3).reshape(-1, ch).astype(F32)
    sums = g[:, hc + lrows : hc + lrows + 4].astype(F32)

    def mid_own(v):
        return lax.dynamic_slice_in_dim(v[:, :hc], d_index * q, q, axis=1).reshape(1, hc)

    own = lax.dynamic_index_in_dim(sums, d_index, 0, keepdims=False)
    return (
        output,
        frames_grad,
        space_grad[None],
        time_grad[None],
        mid_own(sums[:, 0]),
        mid_own(sums[:, 1]),
        own[2:3, :cc],
        own[3:4, :cc],
    )


def from_behind(value, axis, steps):
    count = lax.axis_size(axis)
    leading, last = (max(0, -steps), min(count, count - steps))
    return lax.ppermute(value, axis, [(source, source + steps) for source in range(leading, last)])


def space_apply(current, kernel):
    frame_side = current.shape[1]
    padded = jnp.pad(current, ((0, 0), (1, 1), (1, 1), (0, 0)))
    stacked = jnp.concatenate(
        [
            padded[:, row_shift : row_shift + frame_side, col_shift : col_shift + frame_side, :]
            for row_shift in range(3)
            for col_shift in range(3)
        ],
        axis=-1,
    )
    return (
        stacked,
        jnp.einsum("fijc,co->fijo", stacked, kernel, preferred_element_type=jnp.float32),
    )


def space_back(gradient, kernel):
    frame_side = gradient.shape[1]
    channels = kernel.shape[0] // 9
    spread = jnp.einsum("fijo,co->fijc", gradient, kernel, preferred_element_type=jnp.float32)
    total = jnp.zeros((gradient.shape[0], frame_side + 2, frame_side + 2, channels), jnp.float32)
    for tap_index in range(9):
        row_shift = tap_index // 3
        col_shift = tap_index % 3
        piece_now = spread[..., tap_index * channels : (tap_index + 1) * channels]
        total = total + jnp.pad(
            piece_now, ((0, 0), (row_shift, 2 - row_shift), (col_shift, 2 - col_shift), (0, 0))
        )
    return total[:, 1 : frame_side + 1, 1 : frame_side + 1, :]


def time_apply(current, kernel, before_mask, after_mask):
    blanks = jnp.zeros_like(current[:1])
    earlier = jnp.concatenate([blanks, current[:-1]], axis=0) * before_mask[
        :, None, None, None
    ].astype(current.dtype)
    later = jnp.concatenate([current[1:], blanks], axis=0) * after_mask[:, None, None, None].astype(
        current.dtype
    )
    stacked = jnp.concatenate([earlier, current, later], axis=-1)
    return (
        stacked,
        jnp.einsum("fijc,co->fijo", stacked, kernel, preferred_element_type=jnp.float32),
    )


def time_back(gradient, kernel, before_mask, after_mask):
    channels = kernel.shape[0] // 3
    spread = jnp.einsum("fijo,co->fijc", gradient, kernel, preferred_element_type=jnp.float32)
    early_part = spread[..., :channels] * before_mask[:, None, None, None]
    late_part = spread[..., 2 * channels :] * after_mask[:, None, None, None]
    blanks = jnp.zeros_like(early_part[:1])
    moved_early = jnp.concatenate([early_part[1:], blanks], axis=0)
    moved_late = jnp.concatenate([blanks, late_part[:-1]], axis=0)
    return spread[..., channels : 2 * channels] + moved_early + moved_late


def moments(values, pixel_count):
    average = lax.psum(jnp.sum(values, axis=(0, 1, 2)), "dp") / pixel_count
    centered = values - average
    spread = lax.psum(jnp.sum(centered * centered, axis=(0, 1, 2)), "dp") / pixel_count
    return (average, lax.rsqrt(spread + eps))


def reduce_back(gradient, normed):
    return lax.psum(
        (jnp.sum(gradient, axis=(0, 1, 2)), jnp.sum(gradient * normed, axis=(0, 1, 2))), "dp"
    )


def silu_slope(values):
    sigmoid_now = jax.nn.sigmoid(values)
    return sigmoid_now * (1.0 + values * (1.0 - sigmoid_now))


def pick_slot(stack, slot_index):
    return lax.dynamic_index_in_dim(stack, slot_index, 0, keepdims=False)


def store_slot(stack, value, slot_index, usable):
    previous = pick_slot(stack, slot_index)
    return lax.dynamic_update_index_in_dim(stack, jnp.where(usable, value, previous), slot_index, 0)


def on_device_general(
    frames, cotangent, starts, space_kernel, time_kernel, mid_gain, mid_bias, out_gain, out_bias
):
    n_segment = lax.axis_size("segment")
    n_data = lax.axis_size("dp")
    segment_index = lax.axis_index("segment")
    odd_segment = segment_index % 2 == 1
    last_segment = segment_index == n_segment - 1
    first_segment = segment_index == 0
    frame_count = frames.shape[0]
    frame_side = frames.shape[1]
    channels = frames.shape[3]
    hidden_units = mid_gain.shape[1] * n_data
    pixel_count = n_data * frame_count * frame_side * frame_side
    turns = 2 * n_segment - 1
    block_shape = (n_segment,) + frames.shape
    all_frames, all_cot, all_starts = (
        lax.all_gather(frames, "segment", axis=0, tiled=True),
        lax.all_gather(cotangent, "segment", axis=0, tiled=True),
        lax.all_gather(starts.astype(jnp.bfloat16), "segment", axis=0, tiled=True),
    )
    frame_stack = all_frames.reshape(block_shape)
    cot_stack = all_cot.reshape(block_shape)
    clip_flags = all_starts.astype(jnp.float32).reshape(n_segment, frame_count)
    positions = jnp.arange(frame_count)
    before_mask = jnp.where((clip_flags > 0.5) | (positions == 0), 0.0, 1.0)
    following = jnp.concatenate([clip_flags[:, 1:], jnp.ones((n_segment, 1), jnp.float32)], axis=1)
    after_mask = jnp.where(following > 0.5, 0.0, 1.0)
    gathered = (
        lax.all_gather(space_kernel[0].astype(jnp.bfloat16), "dp", axis=0, tiled=True),
        lax.all_gather(time_kernel[0].astype(jnp.bfloat16), "dp", axis=0, tiled=True),
        lax.all_gather(mid_gain[0].astype(jnp.bfloat16), "dp", axis=0, tiled=True),
        lax.all_gather(mid_bias[0].astype(jnp.bfloat16), "dp", axis=0, tiled=True),
        lax.all_gather(out_gain[0].astype(jnp.bfloat16), "dp", axis=0, tiled=True),
        lax.all_gather(out_bias[0].astype(jnp.bfloat16), "dp", axis=0, tiled=True),
    )
    space_low, time_low = (gathered[0], gathered[1])
    mid_gain_now = gathered[2].astype(jnp.float32)
    mid_bias_now = gathered[3].astype(jnp.float32)
    out_gain_now = gathered[4].astype(jnp.float32)
    out_bias_now = gathered[5].astype(jnp.float32)
    incoming = jnp.zeros_like(frames)
    carried = jnp.zeros_like(frames)
    kept_input = jnp.zeros(block_shape, jnp.bfloat16)
    kept_skip = jnp.zeros(block_shape, jnp.bfloat16)
    kept_mid_mean = jnp.zeros((n_segment, hidden_units), jnp.float32)
    kept_mid_scale = jnp.zeros((n_segment, hidden_units), jnp.float32)
    kept_out_mean = jnp.zeros((n_segment, channels), jnp.float32)
    kept_out_scale = jnp.zeros((n_segment, channels), jnp.float32)
    results = jnp.zeros(block_shape, jnp.float32)
    for turn_index in range(turns):
        micro_index = turn_index - segment_index
        usable = (micro_index >= 0) & (micro_index < n_segment)
        slot_index = jnp.clip(micro_index, 0, n_segment - 1)
        current = jnp.where(first_segment, pick_slot(frame_stack, slot_index), incoming)
        skip_input = carried
        _, spatial = space_apply(current, space_low)
        mid_mean, mid_scale = moments(spatial, pixel_count)
        hidden_act = jax.nn.silu(
            (spatial - mid_mean) * mid_scale * mid_gain_now + mid_bias_now
        ).astype(jnp.bfloat16)
        _, temporal = time_apply(
            hidden_act,
            time_low,
            pick_slot(before_mask, slot_index),
            pick_slot(after_mask, slot_index),
        )
        out_mean, out_scale = moments(temporal, pixel_count)
        pre_act = (
            (temporal - out_mean) * out_scale * out_gain_now
            + out_bias_now
            + jnp.where(odd_segment, skip_input.astype(jnp.float32), 0.0)
        )
        result = jax.nn.silu(pre_act).astype(jnp.bfloat16)
        kept_input = store_slot(kept_input, current, slot_index, usable)
        kept_skip = store_slot(kept_skip, skip_input, slot_index, usable)
        kept_mid_mean = store_slot(kept_mid_mean, mid_mean, slot_index, usable)
        kept_mid_scale = store_slot(kept_mid_scale, mid_scale, slot_index, usable)
        kept_out_mean = store_slot(kept_out_mean, out_mean, slot_index, usable)
        kept_out_scale = store_slot(kept_out_scale, out_scale, slot_index, usable)
        results = store_slot(results, result.astype(jnp.float32), slot_index, usable)
        if turn_index < turns - 1:
            incoming, carried = from_behind(
                (result, jnp.where(odd_segment, result, current)), "segment", 1
            )
    gathered = (
        lax.all_gather(space_kernel[0].astype(jnp.bfloat16), "dp", axis=0, tiled=True),
        lax.all_gather(time_kernel[0].astype(jnp.bfloat16), "dp", axis=0, tiled=True),
        lax.all_gather(mid_gain[0].astype(jnp.bfloat16), "dp", axis=0, tiled=True),
        lax.all_gather(mid_bias[0].astype(jnp.bfloat16), "dp", axis=0, tiled=True),
        lax.all_gather(out_gain[0].astype(jnp.bfloat16), "dp", axis=0, tiled=True),
        lax.all_gather(out_bias[0].astype(jnp.bfloat16), "dp", axis=0, tiled=True),
    )
    space_low, time_low = (gathered[0], gathered[1])
    mid_gain_now = gathered[2].astype(jnp.float32)
    mid_bias_now = gathered[3].astype(jnp.float32)
    out_gain_now = gathered[4].astype(jnp.float32)
    out_bias_now = gathered[5].astype(jnp.float32)
    grad_input = jnp.zeros_like(frames)
    grad_skip = jnp.zeros_like(frames)
    space_acc = jnp.zeros(space_low.shape, jnp.float32)
    time_acc = jnp.zeros(time_low.shape, jnp.float32)
    mid_gain_acc = jnp.zeros((hidden_units,), jnp.float32)
    mid_bias_acc = jnp.zeros((hidden_units,), jnp.float32)
    out_gain_acc = jnp.zeros((channels,), jnp.float32)
    out_bias_acc = jnp.zeros((channels,), jnp.float32)
    input_grads = jnp.zeros(block_shape, jnp.float32)
    for turn_index in range(turns):
        micro_index = n_segment - 1 - (turn_index - (n_segment - 1 - segment_index))
        usable = (micro_index >= 0) & (micro_index < n_segment)
        usable_weight = usable.astype(jnp.float32)
        slot_index = jnp.clip(micro_index, 0, n_segment - 1)
        current = pick_slot(kept_input, slot_index)
        skip_input = pick_slot(kept_skip, slot_index)
        before_now = pick_slot(before_mask, slot_index)
        after_now = pick_slot(after_mask, slot_index)
        space_taps, spatial = space_apply(current, space_low)
        mid_normed = (spatial - pick_slot(kept_mid_mean, slot_index)) * pick_slot(
            kept_mid_scale, slot_index
        )
        mid_pre = mid_normed * mid_gain_now + mid_bias_now
        hidden_act = jax.nn.silu(mid_pre).astype(jnp.bfloat16)
        time_taps, temporal = time_apply(hidden_act, time_low, before_now, after_now)
        out_scale = pick_slot(kept_out_scale, slot_index)
        out_normed = (temporal - pick_slot(kept_out_mean, slot_index)) * out_scale
        pre_act = (
            out_normed * out_gain_now
            + out_bias_now
            + jnp.where(odd_segment, skip_input.astype(jnp.float32), 0.0)
        )
        grad_result = jnp.where(
            last_segment,
            pick_slot(cot_stack, slot_index).astype(jnp.float32),
            grad_input.astype(jnp.float32)
            + jnp.where(odd_segment, grad_skip.astype(jnp.float32), 0.0),
        )
        grad_pre = grad_result * silu_slope(pre_act)
        out_bias_sum, out_gain_sum = reduce_back(grad_pre, out_normed)
        grad_temporal = (
            out_gain_now
            * out_scale
            * (grad_pre - out_bias_sum / pixel_count - out_normed * out_gain_sum / pixel_count)
        ).astype(jnp.bfloat16)
        time_acc = time_acc + usable_weight * jnp.einsum(
            "fijc,fijo->co", time_taps, grad_temporal, preferred_element_type=jnp.float32
        )
        grad_hidden = time_back(grad_temporal, time_low, before_now, after_now)
        grad_mid = grad_hidden * silu_slope(mid_pre)
        mid_bias_sum, mid_gain_sum = reduce_back(grad_mid, mid_normed)
        mid_scale = pick_slot(kept_mid_scale, slot_index)
        grad_spatial = (
            mid_gain_now
            * mid_scale
            * (grad_mid - mid_bias_sum / pixel_count - mid_normed * mid_gain_sum / pixel_count)
        ).astype(jnp.bfloat16)
        space_acc = space_acc + usable_weight * jnp.einsum(
            "fijc,fijo->co", space_taps, grad_spatial, preferred_element_type=jnp.float32
        )
        grad_current = space_back(grad_spatial, space_low)
        mid_gain_acc = mid_gain_acc + usable_weight * mid_gain_sum
        mid_bias_acc = mid_bias_acc + usable_weight * mid_bias_sum
        out_gain_acc = out_gain_acc + usable_weight * out_gain_sum
        out_bias_acc = out_bias_acc + usable_weight * out_bias_sum
        input_grads = store_slot(
            input_grads, grad_current + grad_skip.astype(jnp.float32), slot_index, usable
        )
        if turn_index < turns - 1:
            grad_input, grad_skip = from_behind(
                (
                    grad_current.astype(jnp.bfloat16),
                    jnp.where(odd_segment, grad_pre.astype(jnp.bfloat16), grad_skip),
                ),
                "segment",
                -1,
            )
    space_grad, time_grad = (
        lax.psum_scatter(space_acc, "dp", scatter_dimension=0, tiled=True),
        lax.psum_scatter(time_acc, "dp", scatter_dimension=0, tiled=True),
    )
    data_index = lax.axis_index("dp")

    def own_share(full_vector):
        share = full_vector.shape[0] // n_data
        return lax.dynamic_slice_in_dim(full_vector, data_index * share, share)[None]

    flat_shape = (n_segment * frame_count,) + frames.shape[1:]
    arrived_out, arrived_grads = (
        lax.all_to_all(
            results.reshape(flat_shape).astype(jnp.bfloat16),
            "segment",
            split_axis=0,
            concat_axis=0,
            tiled=True,
        ).astype(jnp.float32),
        lax.all_to_all(
            input_grads.reshape(flat_shape).astype(jnp.bfloat16),
            "segment",
            split_axis=0,
            concat_axis=0,
            tiled=True,
        ).astype(jnp.float32),
    )
    output = arrived_out[(n_segment - 1) * frame_count :].astype(jnp.bfloat16)
    frames_grad = arrived_grads[:frame_count]
    return (
        output,
        frames_grad,
        space_grad[None],
        time_grad[None],
        own_share(mid_gain_acc),
        own_share(mid_bias_acc),
        own_share(out_gain_acc),
        own_share(out_bias_acc),
    )


def general(mesh):
    return jax.shard_map(
        on_device_general,
        mesh=mesh,
        in_specs=(
            P(("dp", "segment"), None, None, None),
            P(("dp", "segment"), None, None, None),
            P(("dp", "segment")),
            P("segment", "dp", None),
            P("segment", "dp", None),
            P("segment", "dp"),
            P("segment", "dp"),
            P("segment", "dp"),
            P("segment", "dp"),
        ),
        out_specs=(
            P(("dp", "segment"), None, None, None),
            P(("dp", "segment"), None, None, None),
            P("segment", "dp", None),
            P("segment", "dp", None),
            P("segment", "dp"),
            P("segment", "dp"),
            P("segment", "dp"),
            P("segment", "dp"),
        ),
        check_vma=False,
    )


def solution(mesh):
    if mesh.shape["dp"] != 8 or mesh.shape["segment"] != 4:
        return general(mesh)
    n_dp, n_seg = mesh.shape["dp"], mesh.shape["segment"]
    fine = Mesh(mesh.devices.reshape(n_dp // 2, 2, 2, n_seg // 2), EVERY)
    dp, seg = ("z", "y"), ("x", "c")
    return jax.shard_map(
        on_device,
        mesh=fine,
        in_specs=(
            P(EVERY, None, None, None),
            P(EVERY, None, None, None),
            P(EVERY),
            P(seg, dp, None),
            P(seg, dp, None),
            P(seg, dp),
            P(seg, dp),
            P(seg, dp),
            P(seg, dp),
        ),
        out_specs=(
            P(EVERY, None, None, None),
            P(EVERY, None, None, None),
            P(seg, dp, None),
            P(seg, dp, None),
            P(seg, dp),
            P(seg, dp),
            P(seg, dp),
            P(seg, dp),
        ),
        check_vma=False,
    )
```

```python
import functools

import jax
import jax.numpy as jnp
from jax import lax
from jax.experimental import pallas as pl
from jax.experimental.pallas import tpu as pltpu
from jax.sharding import Mesh, PartitionSpec as P

eps = 1e-05
PLANE = ("y", "x", "c")
EVERY = ("z", "y", "x", "c")
BF = jnp.bfloat16
F32 = jnp.float32


def nt(a, b):
    return lax.dot_general(a, b, (((1,), (1,)), ((), ())), preferred_element_type=F32)


def nn(a, b):
    return lax.dot_general(a, b, (((1,), (0,)), ((), ())), preferred_element_type=F32)


VMEM_CAP = 56 * 1024 * 1024
SMALL_CAP = 16 * 1024 * 1024
ANY = pl.BlockSpec(memory_space=pl.ANY)


def call(body, outs, scratch, flops, *args, deps=(), far=(), far_outs=(), cap=VMEM_CAP):
    moved = sum(a.size * a.dtype.itemsize for a in args) + sum(
        o.size * o.dtype.itemsize for o in outs
    )
    n = len(deps)

    def spec(a):
        return pl.BlockSpec(memory_space=pltpu.SMEM if a.dtype == jnp.int32 else pltpu.VMEM)

    return pl.pallas_call(
        lambda *refs: body(*refs[n:]),
        out_shape=outs,
        in_specs=[ANY] * n + [ANY if i in far else spec(a) for i, a in enumerate(args)],
        out_specs=[ANY if i in far_outs else spec(o) for i, o in enumerate(outs)],
        scratch_shapes=scratch,
        compiler_params=pltpu.CompilerParams(vmem_limit_bytes=cap),
        cost_estimate=pl.CostEstimate(flops=flops, bytes_accessed=moved, transcendentals=0),
    )(*deps, *args)


def chunk(i, size):
    return pl.ds(pl.multiple_of(i * size, 16), size)


def clear_borders(pad_ref, side, plane, nf):
    zrow = jnp.zeros(pad_ref.shape[1:], BF)
    pad_ref[0] = zrow
    pad_ref[side + 1] = zrow
    zcol = jnp.zeros((nf, pad_ref.shape[2]), BF)
    for i in range(side):
        pad_ref[i + 1, 0:nf] = zcol
        pad_ref[i + 1, nf + plane : 2 * nf + plane] = zcol


def by_rank(slices, rank):
    odd = lax.rem(rank, 2) == 1
    for p in range(len(slices) // 2):
        a, b = slices[2 * p], slices[2 * p + 1]
        yield lax.bitwise_xor(rank // 2, p), odd, a, b


def halves(odd, own, mate):
    low = lax.broadcasted_iota(jnp.int32, own.shape, 1) < 64
    own, mate = own.astype(F32), mate.astype(F32)
    a, b = jnp.where(odd, mate, own), jnp.where(odd, own, mate)
    top = jnp.where(low, a, pltpu.roll(b, 64, 1))
    bottom = jnp.where(low, pltpu.roll(a, 64, 1), b)
    return top, bottom


def store_packed(rank, mate_ref, keep_ref, part, k, step, low):
    rows_now = chunk(k, step)
    odd = lax.rem(rank, 2) == 1
    for q in range(keep_ref.shape[0]):
        x = part[:step, 128 * q : 128 * q + 128]
        y = part[step:, 128 * q : 128 * q + 128]
        even_slice = jnp.where(low, x, pltpu.roll(y, 64, 1))
        odd_slice = jnp.where(low, pltpu.roll(x, 64, 1), y)
        p = lax.bitwise_xor(rank // 2, q)
        keep_ref[p, rows_now, :] = jnp.where(odd, odd_slice, even_slice).astype(BF)
        mate_ref[p, rows_now, :] = jnp.where(odd, even_slice, odd_slice).astype(BF)


def fetch_kernels(w_ref, ktm_ref, lw_ref, sems):
    nz, _, width = w_ref.shape
    hc = ktm_ref.shape[0]
    copies = []
    for z in range(nz):
        copies.append(pltpu.make_async_copy(
            w_ref.at[z, pl.ds(0, hc)], ktm_ref.at[:, pl.ds(z * width, width)], sems.at[2 * z]))
        copies.append(pltpu.make_async_copy(
            w_ref.at[z, pl.ds(hc, lw_ref.shape[1])], lw_ref.at[z], sems.at[2 * z + 1]))
    for copy in copies:
        copy.start()
    return copies


def join_temporal(lw_ref, lf_ref, ltm_ref):
    ch = ltm_ref.shape[1]
    width = lw_ref.shape[2] // 2
    count = 2 * lw_ref.shape[0]
    size = ltm_ref.shape[0] // count
    for z in range(lw_ref.shape[0]):
        first = lw_ref[z, :, 0:ch].astype(F32)
        off = width % 128
        second = lw_ref[z, :, width - off : width - off + ch + 128].astype(F32)
        second = pltpu.roll(second, ch + 128 - off, 1)[:, 0:ch]
        for b, block in ((2 * z, first), (2 * z + 1, second)):
            lf_ref[b * size : b * size + block.shape[0], :] = block
    ltm_ref[...] = lf_ref[0 : ltm_ref.shape[0], :].astype(BF)


def prepare_body(w_ref, kn_out, l_out, lt_out, rows_out, ktm_ref, lw_ref, lf_ref, sems):
    hc, ch = ktm_ref.shape[0], l_out.shape[1]
    for copy in fetch_kernels(w_ref, ktm_ref, lw_ref, sems):
        copy.wait()
    for t in range(9):
        kn_out[t] = ktm_ref[:, t * ch : (t + 1) * ch].astype(F32).T.astype(BF)
    join_temporal(lw_ref, lf_ref, l_out)
    rows_out[...] = lw_ref[:, lw_ref.shape[1] - rows_out.shape[1] :, :]
    for t in range(3):
        lt_out[t] = lf_ref[t * hc : (t + 1) * hc].T.astype(BF)


def prepare(w, hc, ch, deps=()):
    outs = [
        jax.ShapeDtypeStruct((9, ch, hc), BF),
        jax.ShapeDtypeStruct((3 * hc, ch), BF),
        jax.ShapeDtypeStruct((3, ch, hc), BF),
        jax.ShapeDtypeStruct((w.shape[0], 16, w.shape[2]), BF),
    ]
    tall = w.shape[1] - hc
    scratch = [
        pltpu.VMEM((hc, 9 * ch), BF),
        pltpu.VMEM((w.shape[0], tall, w.shape[2]), BF),
        pltpu.VMEM((3 * hc + tall, ch), F32),
        pltpu.SemaphoreType.DMA((2 * w.shape[0],)),
    ]
    return call(prepare_body, outs, scratch, 2 * w.size * 512, w, deps=deps, far=(0,))


def conv_body(side, first, rank_ref, *refs):
    n = 1 if first else 8
    slices = refs[:n]
    (kn_in, ltm_ref, vec_ref, before_ref, after_ref,
     pad_out, hid_out, xhat_out, rs_ref, mate_ref, keep_ref,
     pad_ref, hid_ref, xhat_ref, sp_ref, kn_ref, sems) = refs[n:]
    rank = rank_ref[0]
    kn_copy = pltpu.make_async_copy(kn_in, kn_ref, sems.at[0])
    kn_copy.start()
    ch, hc = pad_ref.shape[2], hid_ref.shape[1]
    rows = hid_ref.shape[0]
    plane = rows // side
    nf = plane // side
    step = plane // 2
    clear_borders(pad_ref, side, plane, nf)
    if first:
        for i in range(side):
            pad_ref[i + 1, nf : nf + plane] = slices[0][i * plane : (i + 1) * plane]
    else:
        def place(k, carry):
            for q, odd, a_ref, b_ref in by_rank(slices, rank):
                top, bottom = halves(odd, a_ref[chunk(k, step), :], b_ref[chunk(k, step), :])
                lanes = pl.ds(pl.multiple_of(128 * q, 128), 128)
                for piece, kk in ((top, k), (bottom, k + side)):
                    at = nf + lax.rem(kk, 2) * step
                    pad_ref[1 + kk // 2, pl.ds(pl.multiple_of(at, 16), step), lanes] = piece.astype(BF)
            return carry

        lax.fori_loop(0, side, place, 0, unroll=True)
    pad_copy = pltpu.make_async_copy(pad_ref, pad_out, sems.at[1])
    pad_copy.start()
    kn_copy.wait()

    def conv(i, total):
        acc = jnp.zeros((plane, hc), F32)
        for t in range(9):
            r, c = t // 3, t % 3
            acc += nn(pad_ref[i + r, c * nf : c * nf + plane, :], kn_ref[t])
        sp_ref[i] = acc
        return total + jnp.sum(acc, axis=0, keepdims=True)

    mean = lax.fori_loop(0, side, conv, jnp.zeros((1, hc), F32), unroll=True) / rows

    def square(i, total):
        cen = sp_ref[i] - mean
        return total + jnp.sum(cen * cen, axis=0, keepdims=True)

    var = lax.fori_loop(0, side, square, jnp.zeros((1, hc), F32), unroll=True) / rows
    rs = lax.rsqrt(var + eps)
    rs_ref[...] = rs
    gain, bias = vec_ref[0:1, :], vec_ref[1:2, :]

    def act(i, carry):
        xhat = (sp_ref[i] - mean) * rs
        xhat_ref[i] = xhat
        v = xhat * gain + bias
        v = v * jax.nn.sigmoid(v)
        sp_ref[i] = v
        hid_ref[chunk(i, plane), :] = v.astype(BF)
        return carry

    lax.fori_loop(0, side, act, 0, unroll=True)
    late = [
        pltpu.make_async_copy(hid_ref, hid_out, sems.at[2]),
        pltpu.make_async_copy(xhat_ref, xhat_out, sems.at[3]),
    ]
    for copy in late:
        copy.start()
    low = lax.broadcasted_iota(jnp.int32, (step, 128), 1) < 64

    def temporal(k, carry):
        pieces = []
        for kk in (k, k + side):
            par = lax.rem(kk, 2)
            h = sp_ref[kk // 2, pl.ds(pl.multiple_of(par * step, 8), step), :]
            at = pl.multiple_of(par * (step % nf), 8)
            pieces.append((
                (pltpu.roll(h, 1, 0) * before_ref[pl.ds(at, step), :]).astype(BF),
                h.astype(BF),
                (pltpu.roll(h, step - 1, 0) * after_ref[pl.ds(at, step), :]).astype(BF),
            ))
        part = sum(
            nn(jnp.concatenate([x, y], axis=0), ltm_ref[t * hc : (t + 1) * hc])
            for t, (x, y) in enumerate(zip(*pieces))
        )
        store_packed(rank, mate_ref, keep_ref, part, k, step, low)
        return carry

    lax.fori_loop(0, side, temporal, 0, unroll=True)
    for copy in [pad_copy] + late:
        copy.wait()


def conv_forward(rank, g, kn, lt, vec, before, after, side, pixels, ch, deps=()):
    hc = vec.shape[1]
    plane = pixels // side
    nf = plane // side
    n = len(g)
    shapes = [
        ((side + 2, plane + 2 * nf, ch), BF),
        ((pixels, hc), BF),
        ((side, plane, hc), F32),
    ]
    outs = [jax.ShapeDtypeStruct(*s) for s in shapes] + [
        jax.ShapeDtypeStruct((1, hc), F32),
        jax.ShapeDtypeStruct((4, pixels // 2, 128), BF),
        jax.ShapeDtypeStruct((4, pixels // 2, 128), BF),
    ]
    scratch = [pltpu.VMEM(*s) for s in shapes] + [
        pltpu.VMEM((side, plane, hc), F32),
        pltpu.VMEM((9, ch, hc), BF),
        pltpu.SemaphoreType.DMA((4,)),
    ]
    flops = 2 * pixels * hc * 12 * ch
    return call(functools.partial(conv_body, side, n == 1), outs, scratch, flops,
                rank, *g, kn, lt, vec, before, after,
                deps=deps, far=(n + 1,), far_outs=(0, 1, 2))


def fold(v):
    return v + pltpu.roll(v, 64, 1)


def total_of(refs):
    t = refs[0][...].astype(F32)
    for ref in refs[1:]:
        t += ref[...].astype(F32)
    return t


def pair_sum_body(keep_ref, mate_ref, *out_refs):
    for p, ref in enumerate(out_refs):
        ref[...] = (keep_ref[p].astype(F32) + mate_ref[p].astype(F32)).astype(ref.dtype)


def pair_sum(keep, arrived, deps=()):
    shape = keep.shape[1:]
    outs = [jax.ShapeDtypeStruct(shape, BF)] * keep.shape[0]
    return call(pair_sum_body, outs, [], keep.size, keep, arrived, deps=deps, cap=SMALL_CAP)


def out_norm_body(n, has_skip, *refs):
    parts, refs = refs[:n], refs[n:]
    if has_skip:
        vec_ref, skip_ref, xhat_ref, rs_ref, pre_ref, res_ref = refs
    else:
        vec_ref, xhat_ref, rs_ref, pre_ref, res_ref = refs
    t = total_of(parts)
    pixels = 2 * t.shape[0]
    mean = fold(jnp.sum(t, axis=0, keepdims=True)) / pixels
    cen = t - mean
    rs = lax.rsqrt(fold(jnp.sum(cen * cen, axis=0, keepdims=True)) / pixels + eps)
    xhat = cen * rs
    pre = xhat * vec_ref[0:1, :] + vec_ref[1:2, :]
    if has_skip:
        pre = pre + skip_ref[...].astype(F32)
    xhat_ref[...] = xhat
    rs_ref[...] = rs
    pre_ref[...] = pre
    res_ref[...] = (pre * jax.nn.sigmoid(pre)).astype(BF)


def out_norm(parts, vec, skip, deps=()):
    half = parts[0].shape[0]
    outs = [
        jax.ShapeDtypeStruct((half, 128), F32),
        jax.ShapeDtypeStruct((1, 128), F32),
        jax.ShapeDtypeStruct((half, 128), F32),
        jax.ShapeDtypeStruct((half, 128), BF),
    ]
    args = (*parts, vec) + (() if skip is None else (skip,))
    body = functools.partial(out_norm_body, len(parts), skip is not None)
    return call(body, outs, [], half * 128 * 10, *args, deps=deps, cap=SMALL_CAP)


def out_back_body(n, *refs):
    parts, (pre_ref, xhat_ref, rs_ref, vec_ref, dpre_ref, dt_ref, sums_ref) = refs[:n], refs[n:]
    g = total_of(parts)
    pre, xhat = pre_ref[...], xhat_ref[...]
    sig = jax.nn.sigmoid(pre)
    dpre = g * (sig * (1.0 + pre * (1.0 - sig)))
    pixels = 2 * pre.shape[0]
    sb = fold(jnp.sum(dpre, axis=0, keepdims=True))
    sg = fold(jnp.sum(dpre * xhat, axis=0, keepdims=True))
    dpre_ref[...] = dpre.astype(BF)
    scale = vec_ref[0:1, :] * rs_ref[...]
    dt_ref[...] = (scale * (dpre - sb / pixels - xhat * (sg / pixels))).astype(BF)
    sums_ref[0:1, :] = sg
    sums_ref[1:2, :] = sb


def out_back(parts, pre, xhat, rs, vec, deps=()):
    half = pre.shape[0]
    outs = [
        jax.ShapeDtypeStruct((half, 128), BF),
        jax.ShapeDtypeStruct((half, 128), BF),
        jax.ShapeDtypeStruct((2, 128), F32),
    ]
    args = (*parts, pre, xhat, rs, vec)
    return call(functools.partial(out_back_body, len(parts)), outs, [], half * 1280, *args, deps=deps,
                cap=SMALL_CAP)


def conv_back_body(side, rank_ref, *refs):
    slices, (xhat_in, rs_ref, w_ref, lnt_ref, vec_ref, before_ref, after_ref,
             dt_out, ds_out, sums_ref, mate_ref, keep_ref,
             dt_ref, ds_ref, xhat_ref, dy_ref, pad_ref, ktm_ref, sems) = refs[:8], refs[8:]
    half = slices[0].shape[0]
    rank = rank_ref[0]
    nz, _, width = w_ref.shape
    rows = 2 * half
    plane = rows // side
    nf = plane // side
    step = plane // 2
    hc = ds_ref.shape[1]
    ch = dt_ref.shape[1]
    fetched = [
        pltpu.make_async_copy(
            w_ref.at[z, pl.ds(0, hc)], ktm_ref.at[:, pl.ds(z * width, width)], sems.at[z])
        for z in range(nz)
    ]
    xhat_copy = pltpu.make_async_copy(xhat_in, xhat_ref, sems.at[nz])
    for copy in fetched + [xhat_copy]:
        copy.start()
    clear_borders(pad_ref, side, plane, nf)

    def place(k, carry):
        for q, odd, a_ref, b_ref in by_rank(slices, rank):
            top, bottom = halves(odd, a_ref[chunk(k, step), :], b_ref[chunk(k, step), :])
            lanes = pl.ds(pl.multiple_of(128 * q, 128), 128)
            dt_ref[chunk(k, step), lanes] = top.astype(BF)
            dt_ref[pl.ds(pl.multiple_of(half + k * step, 16), step), lanes] = bottom.astype(BF)
        return carry

    lax.fori_loop(0, side, place, 0, unroll=True)
    dt_copy = pltpu.make_async_copy(dt_ref, dt_out, sems.at[nz + 1])
    dt_copy.start()
    xhat_copy.wait()
    gain, bias = vec_ref[0:1, :], vec_ref[1:2, :]

    def hidden_grad(i, sums):
        dt = dt_ref[chunk(i, plane), :]
        early = nn(dt, lnt_ref[0]) * before_ref[0:plane, :]
        late = nn(dt, lnt_ref[2]) * after_ref[0:plane, :]
        dh = nn(dt, lnt_ref[1]) + pltpu.roll(early, plane - 1, 0) + pltpu.roll(late, 1, 0)
        xhat = xhat_ref[i]
        v = xhat * gain + bias
        sig = jax.nn.sigmoid(v)
        dy = dh * (sig * (1.0 + v * (1.0 - sig)))
        dy_ref[i] = dy
        return (
            sums[0] + jnp.sum(dy * xhat, axis=0, keepdims=True),
            sums[1] + jnp.sum(dy, axis=0, keepdims=True),
        )

    zero = jnp.zeros((1, hc), F32)
    sg, sb = lax.fori_loop(0, side, hidden_grad, (zero, zero), unroll=True)
    sums_ref[0:1, :] = sg
    sums_ref[1:2, :] = sb
    scale = gain * rs_ref[...]

    def spatial_grad(i, carry):
        ds = (scale * (dy_ref[i] - sb / rows - xhat_ref[i] * (sg / rows))).astype(BF)
        pad_ref[i + 1, nf : nf + plane] = ds
        ds_ref[chunk(i, plane), :] = ds
        return carry

    lax.fori_loop(0, side, spatial_grad, 0, unroll=True)
    ds_copy = pltpu.make_async_copy(ds_ref, ds_out, sems.at[nz + 2])
    ds_copy.start()
    for copy in fetched:
        copy.wait()
    low = lax.broadcasted_iota(jnp.int32, (step, 128), 1) < 64

    def back(k, carry):
        acc = jnp.zeros((2 * step, ch), F32)
        for t in range(9):
            r, c = 2 - t // 3, 2 - t % 3
            pieces = []
            for kk in (k, k + side):
                at = c * nf + lax.rem(kk, 2) * step
                pieces.append(pad_ref[kk // 2 + r, pl.ds(pl.multiple_of(at, 16), step), :])
            acc += nn(jnp.concatenate(pieces, axis=0), ktm_ref[:, t * ch : (t + 1) * ch])
        store_packed(rank, mate_ref, keep_ref, acc, k, step, low)
        return carry

    lax.fori_loop(0, side, back, 0, unroll=True)
    dt_copy.wait()
    ds_copy.wait()


def conv_back(rank, g, xhat, rs, w, lnt, vec, before, after, side, deps=()):
    half = g[0].shape[0]
    hc = vec.shape[1]
    ch = len(g) * 64
    pixels = 2 * half
    plane = pixels // side
    nf = plane // side
    outs = [
        jax.ShapeDtypeStruct((pixels, ch), BF),
        jax.ShapeDtypeStruct((pixels, hc), BF),
        jax.ShapeDtypeStruct((2, hc), F32),
        jax.ShapeDtypeStruct((4, half, 128), BF),
        jax.ShapeDtypeStruct((4, half, 128), BF),
    ]
    scratch = [
        pltpu.VMEM((pixels, ch), BF),
        pltpu.VMEM((pixels, hc), BF),
        pltpu.VMEM((side, plane, hc), F32),
        pltpu.VMEM((side, plane, hc), F32),
        pltpu.VMEM((side + 2, plane + 2 * nf, hc), BF),
        pltpu.VMEM((hc, 9 * ch), BF),
        pltpu.SemaphoreType.DMA((w.shape[0] + 3,)),
    ]
    flops = 2 * pixels * hc * 12 * ch
    return call(functools.partial(conv_back_body, side), outs, scratch, flops,
                rank, *g, xhat, rs, w, lnt, vec, before, after,
                deps=deps, far=(9, 11), far_outs=(0, 1))


def grads_body(side, pad_ref, hid_ref, ds_ref, dt_ref, before_ref, after_ref, mid_ref, out_ref,
               sg_ref, dst_ref, taps_ref, tg_ref, vec_ref):
    ch = pad_ref.shape[2]
    hc = hid_ref.shape[1]
    plane = hid_ref.shape[0] // side
    nf = plane // side
    for i in (0, 1, side + 2, side + 3):
        dst_ref[i] = jnp.zeros(dst_ref.shape[1:], BF)
    for i in range(side):
        at = slice(i * plane, (i + 1) * plane)
        h = hid_ref[at, :].astype(F32)
        taps_ref[i, 0:hc] = (pltpu.roll(h, 1, 0) * before_ref[0:plane, :]).T.astype(BF)
        taps_ref[i, hc : 2 * hc] = h.T.astype(BF)
        taps_ref[i, 2 * hc : 3 * hc] = (pltpu.roll(h, plane - 1, 0) * after_ref[0:plane, :]).T.astype(BF)
        dst_ref[i + 2] = ds_ref[at, :].astype(F32).T.astype(BF)
    tg_ref[0 : 3 * hc, :] = sum(
        nn(taps_ref[i], dt_ref[i * plane : (i + 1) * plane, :]) for i in range(side)
    )
    tg_ref[3 * hc :, :] = jnp.zeros((tg_ref.shape[0] - 3 * hc, ch), F32)
    nz, _, width = sg_ref.shape
    size = 3 * hc // (2 * nz)
    vec_ref[...] = jnp.zeros(vec_ref.shape, F32)
    vec_ref[size : size + 2, 0:hc] = mid_ref[...]
    vec_ref[size + 2 : size + 4, 0:128] = out_ref[...]
    tall = vec_ref.shape[0]
    inside = lax.broadcasted_iota(jnp.int32, (tall, ch), 0) < size
    off = (width // 2) % 128
    for z in range(nz):
        first, second = [
            jnp.where(inside, tg_ref[b * size : b * size + tall, :], vec_ref[...])
            for b in (2 * z, 2 * z + 1)
        ]
        start = width // 2 - off
        sg_ref[z, hc : hc + tall, 0:ch] = first.astype(BF)
        second = pltpu.roll(jnp.concatenate([second, jnp.zeros((tall, 128), F32)], axis=1), off, 1)
        sg_ref[z, hc : hc + tall, start : start + ch + 128] = second.astype(BF)
    for c in range(3):
        acc = sum(
            nn(dst_ref[i : i + 3].reshape(3 * hc, plane), pad_ref[i, c * nf : c * nf + plane, :])
            for i in range(1, side + 1)
        )
        for r in range(3):
            first = (3 * r + c) * ch
            end = first + ch
            at = (2 - r) * hc
            done = 0
            while first < end:
                z = first // width
                last = min(end, (z + 1) * width)
                sg_ref[z, 0:hc, first - z * width : last - z * width] = (
                    acc[at : at + hc, done : done + last - first].astype(BF)
                )
                done += last - first
                first = last


def kernel_grads(pad, hidden, ds, dt, before, after, mid, out, side, shape, deps=()):
    pixels, hc = hidden.shape
    ch = dt.shape[1]
    plane = pixels // side
    outs = [jax.ShapeDtypeStruct(shape, BF)]
    tall = shape[1] - hc
    scratch = [
        pltpu.VMEM((side + 4, hc, plane), BF),
        pltpu.VMEM((side, 3 * hc, plane), BF),
        pltpu.VMEM((3 * hc + tall, ch), F32),
        pltpu.VMEM((tall, ch), F32),
    ]
    flops = 2 * pixels * hc * 12 * ch
    return call(functools.partial(grads_body, side), outs, scratch, flops,
                pad, hidden, ds, dt, before, after, mid, out, deps=deps)[0]


def pass_on_body(*refs):
    pass


def after_all(v, *deps):
    n = len(deps)
    return pl.pallas_call(
        pass_on_body,
        out_shape=jax.ShapeDtypeStruct(v.shape, v.dtype),
        in_specs=[ANY] * (n + 1),
        out_specs=ANY,
        input_output_aliases={n: 0},
        cost_estimate=pl.CostEstimate(flops=0, bytes_accessed=0, transcendentals=0),
    )(*deps, v)


def pack_kernels_body(kt_ref, lt_ref, vec_ref, out_ref, low_ref):
    ranks, _, width = out_ref.shape
    hc = kt_ref.shape[0] // ranks
    blocks = lt_ref.shape[0] // hc
    q = hc // ranks
    low_ref[...] = jnp.zeros(low_ref.shape, F32)
    for r in range(ranks):
        out_ref[r, 0:hc, :] = kt_ref[r * hc : (r + 1) * hc, :]
        for b in range(blocks):
            low_ref[r, b * q : (b + 1) * q, 0 : lt_ref.shape[1]] = (
                lt_ref[b * hc + r * q : b * hc + (r + 1) * q, :]
            )
        low_ref[r, blocks * q : blocks * q + 1, :] = vec_ref[...]
        out_ref[r, hc:, :] = low_ref[r].astype(BF)


def pack_kernels(kt, lt, vec, ranks, tall, deps):
    width = kt.shape[1]
    outs = [jax.ShapeDtypeStruct((ranks, kt.shape[0] // ranks + tall, width), BF)]
    scratch = [pltpu.VMEM((ranks, tall, width), F32)]
    return call(pack_kernels_body, outs, scratch, kt.size * 8, kt, lt, vec, deps=deps)[0]


def call(body, outs, scratch, flops, *args, deps=(), far=(), far_outs=(), cap=VMEM_CAP):
    moved = sum(a.size * a.dtype.itemsize for a in args) + sum(
        o.size * o.dtype.itemsize for o in outs
    )
    n = len(deps)

    def spec(a):
        return pl.BlockSpec(memory_space=pltpu.SMEM if a.dtype == jnp.int32 else pltpu.VMEM)

    return pl.pallas_call(
        lambda *refs: body(*refs[n:]),
        out_shape=outs,
        in_specs=[ANY] * n + [ANY if i in far else spec(a) for i, a in enumerate(args)],
        out_specs=[ANY if i in far_outs else spec(o) for i, o in enumerate(outs)],
        scratch_shapes=scratch,
        compiler_params=pltpu.CompilerParams(vmem_limit_bytes=cap),
        cost_estimate=pl.CostEstimate(flops=flops, bytes_accessed=moved, transcendentals=0),
    )(*deps, *args)


def chunk(i, size):
    return pl.ds(pl.multiple_of(i * size, 16), size)


def clear_borders(pad_ref, side, plane, nf):
    zrow = jnp.zeros(pad_ref.shape[1:], BF)
    pad_ref[0] = zrow
    pad_ref[side + 1] = zrow
    zcol = jnp.zeros((nf, pad_ref.shape[2]), BF)
    for i in range(side):
        pad_ref[i + 1, 0:nf] = zcol
        pad_ref[i + 1, nf + plane : 2 * nf + plane] = zcol


def by_rank(slices, rank):
    odd = lax.rem(rank, 2) == 1
    for p in range(len(slices) // 2):
        a, b = slices[2 * p], slices[2 * p + 1]
        yield lax.bitwise_xor(rank // 2, p), odd, a, b


def halves(odd, own, mate):
    low = lax.broadcasted_iota(jnp.int32, own.shape, 1) < 64
    own, mate = own.astype(F32), mate.astype(F32)
    a, b = jnp.where(odd, mate, own), jnp.where(odd, own, mate)
    top = jnp.where(low, a, pltpu.roll(b, 64, 1))
    bottom = jnp.where(low, pltpu.roll(a, 64, 1), b)
    return top, bottom


def store_packed(rank, mate_ref, keep_ref, part, k, step, low):
    rows_now = chunk(k, step)
    odd = lax.rem(rank, 2) == 1
    for q in range(keep_ref.shape[0]):
        x = part[:step, 128 * q : 128 * q + 128]
        y = part[step:, 128 * q : 128 * q + 128]
        even_slice = jnp.where(low, x, pltpu.roll(y, 64, 1))
        odd_slice = jnp.where(low, pltpu.roll(x, 64, 1), y)
        p = lax.bitwise_xor(rank // 2, q)
        keep_ref[p, rows_now, :] = jnp.where(odd, odd_slice, even_slice).astype(BF)
        mate_ref[p, rows_now, :] = jnp.where(odd, even_slice, odd_slice).astype(BF)


def fetch_kernels(w_ref, ktm_ref, lw_ref, sems):
    nz, _, width = w_ref.shape
    hc = ktm_ref.shape[0]
    copies = []
    for z in range(nz):
        copies.append(pltpu.make_async_copy(
            w_ref.at[z, pl.ds(0, hc)], ktm_ref.at[:, pl.ds(z * width, width)], sems.at[2 * z]))
        copies.append(pltpu.make_async_copy(
            w_ref.at[z, pl.ds(hc, lw_ref.shape[1])], lw_ref.at[z], sems.at[2 * z + 1]))
    for copy in copies:
        copy.start()
    return copies


def join_temporal(lw_ref, lf_ref, ltm_ref):
    ch = ltm_ref.shape[1]
    width = lw_ref.shape[2] // 2
    count = 2 * lw_ref.shape[0]
    size = ltm_ref.shape[0] // count
    for z in range(lw_ref.shape[0]):
        first = lw_ref[z, :, 0:ch].astype(F32)
        off = width % 128
        second = lw_ref[z, :, width - off : width - off + ch + 128].astype(F32)
        second = pltpu.roll(second, ch + 128 - off, 1)[:, 0:ch]
        for b, block in ((2 * z, first), (2 * z + 1, second)):
            lf_ref[b * size : b * size + block.shape[0], :] = block
    ltm_ref[...] = lf_ref[0 : ltm_ref.shape[0], :].astype(BF)


def prepare_body(w_ref, kn_out, l_out, lt_out, rows_out, ktm_ref, lw_ref, lf_ref, sems):
    hc, ch = ktm_ref.shape[0], l_out.shape[1]
    for copy in fetch_kernels(w_ref, ktm_ref, lw_ref, sems):
        copy.wait()
    for t in range(9):
        kn_out[t] = ktm_ref[:, t * ch : (t + 1) * ch].astype(F32).T.astype(BF)
    join_temporal(lw_ref, lf_ref, l_out)
    rows_out[...] = lw_ref[:, lw_ref.shape[1] - rows_out.shape[1] :, :]
    for t in range(3):
        lt_out[t] = lf_ref[t * hc : (t + 1) * hc].T.astype(BF)


def prepare(w, hc, ch, deps=()):
    outs = [
        jax.ShapeDtypeStruct((9, ch, hc), BF),
        jax.ShapeDtypeStruct((3 * hc, ch), BF),
        jax.ShapeDtypeStruct((3, ch, hc), BF),
        jax.ShapeDtypeStruct((w.shape[0], 16, w.shape[2]), BF),
    ]
    tall = w.shape[1] - hc
    scratch = [
        pltpu.VMEM((hc, 9 * ch), BF),
        pltpu.VMEM((w.shape[0], tall, w.shape[2]), BF),
        pltpu.VMEM((3 * hc + tall, ch), F32),
        pltpu.SemaphoreType.DMA((2 * w.shape[0],)),
    ]
    return call(prepare_body, outs, scratch, 2 * w.size * 512, w, deps=deps, far=(0,))


def conv_body(side, first, rank_ref, *refs):
    n = 1 if first else 8
    slices = refs[:n]
    (kn_in, ltm_ref, vec_ref, before_ref, after_ref,
     pad_out, hid_out, xhat_out, rs_ref, mate_ref, keep_ref,
     pad_ref, hid_ref, xhat_ref, sp_ref, kn_ref, sems) = refs[n:]
    rank = rank_ref[0]
    kn_copy = pltpu.make_async_copy(kn_in, kn_ref, sems.at[0])
    kn_copy.start()
    ch, hc = pad_ref.shape[2], hid_ref.shape[1]
    rows = hid_ref.shape[0]
    plane = rows // side
    nf = plane // side
    step = plane // 2
    clear_borders(pad_ref, side, plane, nf)
    if first:
        for i in range(side):
            pad_ref[i + 1, nf : nf + plane] = slices[0][i * plane : (i + 1) * plane]
    else:
        def place(k, carry):
            for q, odd, a_ref, b_ref in by_rank(slices, rank):
                top, bottom = halves(odd, a_ref[chunk(k, step), :], b_ref[chunk(k, step), :])
                lanes = pl.ds(pl.multiple_of(128 * q, 128), 128)
                for piece, kk in ((top, k), (bottom, k + side)):
                    at = nf + lax.rem(kk, 2) * step
                    pad_ref[1 + kk // 2, pl.ds(pl.multiple_of(at, 16), step), lanes] = piece.astype(BF)
            return carry

        lax.fori_loop(0, side, place, 0, unroll=True)
    pad_copy = pltpu.make_async_copy(pad_ref, pad_out, sems.at[1])
    pad_copy.start()
    kn_copy.wait()

    def conv(i, total):
        acc = jnp.zeros((plane, hc), F32)
        for t in range(9):
            r, c = t // 3, t % 3
            acc += nn(pad_ref[i + r, c * nf : c * nf + plane, :], kn_ref[t])
        sp_ref[i] = acc
        return total + jnp.sum(acc, axis=0, keepdims=True)

    mean = lax.fori_loop(0, side, conv, jnp.zeros((1, hc), F32), unroll=True) / rows

    def square(i, total):
        cen = sp_ref[i] - mean
        return total + jnp.sum(cen * cen, axis=0, keepdims=True)

    var = lax.fori_loop(0, side, square, jnp.zeros((1, hc), F32), unroll=True) / rows
    rs = lax.rsqrt(var + eps)
    rs_ref[...] = rs
    gain, bias = vec_ref[0:1, :], vec_ref[1:2, :]

    def act(i, carry):
        xhat = (sp_ref[i] - mean) * rs
        xhat_ref[i] = xhat
        v = xhat * gain + bias
        v = v * jax.nn.sigmoid(v)
        sp_ref[i] = v
        hid_ref[chunk(i, plane), :] = v.astype(BF)
        return carry

    lax.fori_loop(0, side, act, 0, unroll=True)
    late = [
        pltpu.make_async_copy(hid_ref, hid_out, sems.at[2]),
        pltpu.make_async_copy(xhat_ref, xhat_out, sems.at[3]),
    ]
    for copy in late:
        copy.start()
    low = lax.broadcasted_iota(jnp.int32, (step, 128), 1) < 64

    def temporal(k, carry):
        pieces = []
        for kk in (k, k + side):
            par = lax.rem(kk, 2)
            h = sp_ref[kk // 2, pl.ds(pl.multiple_of(par * step, 8), step), :]
            at = pl.multiple_of(par * (step % nf), 8)
            pieces.append((
                (pltpu.roll(h, 1, 0) * before_ref[pl.ds(at, step), :]).astype(BF),
                h.astype(BF),
                (pltpu.roll(h, step - 1, 0) * after_ref[pl.ds(at, step), :]).astype(BF),
            ))
        part = sum(
            nn(jnp.concatenate([x, y], axis=0), ltm_ref[t * hc : (t + 1) * hc])
            for t, (x, y) in enumerate(zip(*pieces))
        )
        store_packed(rank, mate_ref, keep_ref, part, k, step, low)
        return carry

    lax.fori_loop(0, side, temporal, 0, unroll=True)
    for copy in [pad_copy] + late:
        copy.wait()


def conv_forward(rank, g, kn, lt, vec, before, after, side, pixels, ch, deps=()):
    hc = vec.shape[1]
    plane = pixels // side
    nf = plane // side
    n = len(g)
    shapes = [
        ((side + 2, plane + 2 * nf, ch), BF),
        ((pixels, hc), BF),
        ((side, plane, hc), F32),
    ]
    outs = [jax.ShapeDtypeStruct(*s) for s in shapes] + [
        jax.ShapeDtypeStruct((1, hc), F32),
        jax.ShapeDtypeStruct((4, pixels // 2, 128), BF),
        jax.ShapeDtypeStruct((4, pixels // 2, 128), BF),
    ]
    scratch = [pltpu.VMEM(*s) for s in shapes] + [
        pltpu.VMEM((side, plane, hc), F32),
        pltpu.VMEM((9, ch, hc), BF),
        pltpu.SemaphoreType.DMA((4,)),
    ]
    flops = 2 * pixels * hc * 12 * ch
    return call(functools.partial(conv_body, side, n == 1), outs, scratch, flops,
                rank, *g, kn, lt, vec, before, after,
                deps=deps, far=(n + 1,), far_outs=(0, 1, 2))


def fold(v):
    return v + pltpu.roll(v, 64, 1)


def total_of(refs):
    t = refs[0][...].astype(F32)
    for ref in refs[1:]:
        t += ref[...].astype(F32)
    return t


def pair_sum_body(keep_ref, mate_ref, *out_refs):
    for p, ref in enumerate(out_refs):
        ref[...] = (keep_ref[p].astype(F32) + mate_ref[p].astype(F32)).astype(ref.dtype)


def pair_sum(keep, arrived, deps=()):
    shape = keep.shape[1:]
    outs = [jax.ShapeDtypeStruct(shape, BF)] * keep.shape[0]
    return call(pair_sum_body, outs, [], keep.size, keep, arrived, deps=deps, cap=SMALL_CAP)


def out_norm_body(n, has_skip, *refs):
    parts, refs = refs[:n], refs[n:]
    if has_skip:
        vec_ref, skip_ref, xhat_ref, rs_ref, pre_ref, res_ref = refs
    else:
        vec_ref, xhat_ref, rs_ref, pre_ref, res_ref = refs
    t = total_of(parts)
    pixels = 2 * t.shape[0]
    mean = fold(jnp.sum(t, axis=0, keepdims=True)) / pixels
    cen = t - mean
    rs = lax.rsqrt(fold(jnp.sum(cen * cen, axis=0, keepdims=True)) / pixels + eps)
    xhat = cen * rs
    pre = xhat * vec_ref[0:1, :] + vec_ref[1:2, :]
    if has_skip:
        pre = pre + skip_ref[...].astype(F32)
    xhat_ref[...] = xhat
    rs_ref[...] = rs
    pre_ref[...] = pre
    res_ref[...] = (pre * jax.nn.sigmoid(pre)).astype(BF)


def out_norm(parts, vec, skip, deps=()):
    half = parts[0].shape[0]
    outs = [
        jax.ShapeDtypeStruct((half, 128), F32),
        jax.ShapeDtypeStruct((1, 128), F32),
        jax.ShapeDtypeStruct((half, 128), F32),
        jax.ShapeDtypeStruct((half, 128), BF),
    ]
    args = (*parts, vec) + (() if skip is None else (skip,))
    body = functools.partial(out_norm_body, len(parts), skip is not None)
    return call(body, outs, [], half * 128 * 10, *args, deps=deps, cap=SMALL_CAP)


def out_back_body(n, *refs):
    parts, (pre_ref, xhat_ref, rs_ref, vec_ref, dpre_ref, dt_ref, sums_ref) = refs[:n], refs[n:]
    g = total_of(parts)
    pre, xhat = pre_ref[...], xhat_ref[...]
    sig = jax.nn.sigmoid(pre)
    dpre = g * (sig * (1.0 + pre * (1.0 - sig)))
    pixels = 2 * pre.shape[0]
    sb = fold(jnp.sum(dpre, axis=0, keepdims=True))
    sg = fold(jnp.sum(dpre * xhat, axis=0, keepdims=True))
    dpre_ref[...] = dpre.astype(BF)
    scale = vec_ref[0:1, :] * rs_ref[...]
    dt_ref[...] = (scale * (dpre - sb / pixels - xhat * (sg / pixels))).astype(BF)
    sums_ref[0:1, :] = sg
    sums_ref[1:2, :] = sb


def out_back(parts, pre, xhat, rs, vec, deps=()):
    half = pre.shape[0]
    outs = [
        jax.ShapeDtypeStruct((half, 128), BF),
        jax.ShapeDtypeStruct((half, 128), BF),
        jax.ShapeDtypeStruct((2, 128), F32),
    ]
    args = (*parts, pre, xhat, rs, vec)
    return call(functools.partial(out_back_body, len(parts)), outs, [], half * 1280, *args, deps=deps,
                cap=SMALL_CAP)


def conv_back_body(side, rank_ref, *refs):
    slices, (xhat_in, rs_ref, w_ref, lnt_ref, vec_ref, before_ref, after_ref,
             dt_out, ds_out, sums_ref, mate_ref, keep_ref,
             dt_ref, ds_ref, xhat_ref, dy_ref, pad_ref, ktm_ref, sems) = refs[:8], refs[8:]
    half = slices[0].shape[0]
    rank = rank_ref[0]
    nz, _, width = w_ref.shape
    rows = 2 * half
    plane = rows // side
    nf = plane // side
    step = plane // 2
    hc = ds_ref.shape[1]
    ch = dt_ref.shape[1]
    fetched = [
        pltpu.make_async_copy(
            w_ref.at[z, pl.ds(0, hc)], ktm_ref.at[:, pl.ds(z * width, width)], sems.at[z])
        for z in range(nz)
    ]
    xhat_copy = pltpu.make_async_copy(xhat_in, xhat_ref, sems.at[nz])
    for copy in fetched + [xhat_copy]:
        copy.start()
    clear_borders(pad_ref, side, plane, nf)

    def place(k, carry):
        for q, odd, a_ref, b_ref in by_rank(slices, rank):
            top, bottom = halves(odd, a_ref[chunk(k, step), :], b_ref[chunk(k, step), :])
            lanes = pl.ds(pl.multiple_of(128 * q, 128), 128)
            dt_ref[chunk(k, step), lanes] = top.astype(BF)
            dt_ref[pl.ds(pl.multiple_of(half + k * step, 16), step), lanes] = bottom.astype(BF)
        return carry

    lax.fori_loop(0, side, place, 0, unroll=True)
    dt_copy = pltpu.make_async_copy(dt_ref, dt_out, sems.at[nz + 1])
    dt_copy.start()
    xhat_copy.wait()
    gain, bias = vec_ref[0:1, :], vec_ref[1:2, :]

    def hidden_grad(i, sums):
        dt = dt_ref[chunk(i, plane), :]
        early = nn(dt, lnt_ref[0]) * before_ref[0:plane, :]
        late = nn(dt, lnt_ref[2]) * after_ref[0:plane, :]
        dh = nn(dt, lnt_ref[1]) + pltpu.roll(early, plane - 1, 0) + pltpu.roll(late, 1, 0)
        xhat = xhat_ref[i]
        v = xhat * gain + bias
        sig = jax.nn.sigmoid(v)
        dy = dh * (sig * (1.0 + v * (1.0 - sig)))
        dy_ref[i] = dy
        return (
            sums[0] + jnp.sum(dy * xhat, axis=0, keepdims=True),
            sums[1] + jnp.sum(dy, axis=0, keepdims=True),
        )

    zero = jnp.zeros((1, hc), F32)
    sg, sb = lax.fori_loop(0, side, hidden_grad, (zero, zero), unroll=True)
    sums_ref[0:1, :] = sg
    sums_ref[1:2, :] = sb
    scale = gain * rs_ref[...]

    def spatial_grad(i, carry):
        ds = (scale * (dy_ref[i] - sb / rows - xhat_ref[i] * (sg / rows))).astype(BF)
        pad_ref[i + 1, nf : nf + plane] = ds
        ds_ref[chunk(i, plane), :] = ds
        return carry

    lax.fori_loop(0, side, spatial_grad, 0, unroll=True)
    ds_copy = pltpu.make_async_copy(ds_ref, ds_out, sems.at[nz + 2])
    ds_copy.start()
    for copy in fetched:
        copy.wait()
    low = lax.broadcasted_iota(jnp.int32, (step, 128), 1) < 64

    def back(k, carry):
        acc = jnp.zeros((2 * step, ch), F32)
        for t in range(9):
            r, c = 2 - t // 3, 2 - t % 3
            pieces = []
            for kk in (k, k + side):
                at = c * nf + lax.rem(kk, 2) * step
                pieces.append(pad_ref[kk // 2 + r, pl.ds(pl.multiple_of(at, 16), step), :])
            acc += nn(jnp.concatenate(pieces, axis=0), ktm_ref[:, t * ch : (t + 1) * ch])
        store_packed(rank, mate_ref, keep_ref, acc, k, step, low)
        return carry

    lax.fori_loop(0, side, back, 0, unroll=True)
    dt_copy.wait()
    ds_copy.wait()


def conv_back(rank, g, xhat, rs, w, lnt, vec, before, after, side, deps=()):
    half = g[0].shape[0]
    hc = vec.shape[1]
    ch = len(g) * 64
    pixels = 2 * half
    plane = pixels // side
    nf = plane // side
    outs = [
        jax.ShapeDtypeStruct((pixels, ch), BF),
        jax.ShapeDtypeStruct((pixels, hc), BF),
        jax.ShapeDtypeStruct((2, hc), F32),
        jax.ShapeDtypeStruct((4, half, 128), BF),
        jax.ShapeDtypeStruct((4, half, 128), BF),
    ]
    scratch = [
        pltpu.VMEM((pixels, ch), BF),
        pltpu.VMEM((pixels, hc), BF),
        pltpu.VMEM((side, plane, hc), F32),
        pltpu.VMEM((side, plane, hc), F32),
        pltpu.VMEM((side + 2, plane + 2 * nf, hc), BF),
        pltpu.VMEM((hc, 9 * ch), BF),
        pltpu.SemaphoreType.DMA((w.shape[0] + 3,)),
    ]
    flops = 2 * pixels * hc * 12 * ch
    return call(functools.partial(conv_back_body, side), outs, scratch, flops,
                rank, *g, xhat, rs, w, lnt, vec, before, after,
                deps=deps, far=(9, 11), far_outs=(0, 1))


def grads_body(side, pad_ref, hid_ref, ds_ref, dt_ref, before_ref, after_ref, mid_ref, out_ref,
               sg_ref, dst_ref, taps_ref, tg_ref, vec_ref):
    ch = pad_ref.shape[2]
    hc = hid_ref.shape[1]
    plane = hid_ref.shape[0] // side
    nf = plane // side
    for i in (0, 1, side + 2, side + 3):
        dst_ref[i] = jnp.zeros(dst_ref.shape[1:], BF)
    for i in range(side):
        at = slice(i * plane, (i + 1) * plane)
        h = hid_ref[at, :].astype(F32)
        taps_ref[i, 0:hc] = (pltpu.roll(h, 1, 0) * before_ref[0:plane, :]).T.astype(BF)
        taps_ref[i, hc : 2 * hc] = h.T.astype(BF)
        taps_ref[i, 2 * hc : 3 * hc] = (pltpu.roll(h, plane - 1, 0) * after_ref[0:plane, :]).T.astype(BF)
        dst_ref[i + 2] = ds_ref[at, :].astype(F32).T.astype(BF)
    tg_ref[0 : 3 * hc, :] = sum(
        nn(taps_ref[i], dt_ref[i * plane : (i + 1) * plane, :]) for i in range(side)
    )
    tg_ref[3 * hc :, :] = jnp.zeros((tg_ref.shape[0] - 3 * hc, ch), F32)
    nz, _, width = sg_ref.shape
    size = 3 * hc // (2 * nz)
    vec_ref[...] = jnp.zeros(vec_ref.shape, F32)
    vec_ref[size : size + 2, 0:hc] = mid_ref[...]
    vec_ref[size + 2 : size + 4, 0:128] = out_ref[...]
    tall = vec_ref.shape[0]
    inside = lax.broadcasted_iota(jnp.int32, (tall, ch), 0) < size
    off = (width // 2) % 128
    for z in range(nz):
        first, second = [
            jnp.where(inside, tg_ref[b * size : b * size + tall, :], vec_ref[...])
            for b in (2 * z, 2 * z + 1)
        ]
        start = width // 2 - off
        sg_ref[z, hc : hc + tall, 0:ch] = first.astype(BF)
        second = pltpu.roll(jnp.concatenate([second, jnp.zeros((tall, 128), F32)], axis=1), off, 1)
        sg_ref[z, hc : hc + tall, start : start + ch + 128] = second.astype(BF)
    for c in range(3):
        acc = sum(
            nn(dst_ref[i : i + 3].reshape(3 * hc, plane), pad_ref[i, c * nf : c * nf + plane, :])
            for i in range(1, side + 1)
        )
        for r in range(3):
            first = (3 * r + c) * ch
            end = first + ch
            at = (2 - r) * hc
            done = 0
            while first < end:
                z = first // width
                last = min(end, (z + 1) * width)
                sg_ref[z, 0:hc, first - z * width : last - z * width] = (
                    acc[at : at + hc, done : done + last - first].astype(BF)
                )
                done += last - first
                first = last


def kernel_grads(pad, hidden, ds, dt, before, after, mid, out, side, shape, deps=()):
    pixels, hc = hidden.shape
    ch = dt.shape[1]
    plane = pixels // side
    outs = [jax.ShapeDtypeStruct(shape, BF)]
    tall = shape[1] - hc
    scratch = [
        pltpu.VMEM((side + 4, hc, plane), BF),
        pltpu.VMEM((side, 3 * hc, plane), BF),
        pltpu.VMEM((3 * hc + tall, ch), F32),
        pltpu.VMEM((tall, ch), F32),
    ]
    flops = 2 * pixels * hc * 12 * ch
    return call(functools.partial(grads_body, side), outs, scratch, flops,
                pad, hidden, ds, dt, before, after, mid, out, deps=deps)[0]


def pass_on_body(*refs):
    pass


def after_all(v, *deps):
    n = len(deps)
    return pl.pallas_call(
        pass_on_body,
        out_shape=jax.ShapeDtypeStruct(v.shape, v.dtype),
        in_specs=[ANY] * (n + 1),
        out_specs=ANY,
        input_output_aliases={n: 0},
        cost_estimate=pl.CostEstimate(flops=0, bytes_accessed=0, transcendentals=0),
    )(*deps, v)


def pack_kernels_body(kt_ref, lt_ref, vec_ref, out_ref, low_ref):
    ranks, _, width = out_ref.shape
    hc = kt_ref.shape[0] // ranks
    blocks = lt_ref.shape[0] // hc
    q = hc // ranks
    low_ref[...] = jnp.zeros(low_ref.shape, F32)
    for r in range(ranks):
        out_ref[r, 0:hc, :] = kt_ref[r * hc : (r + 1) * hc, :]
        for b in range(blocks):
            low_ref[r, b * q : (b + 1) * q, 0 : lt_ref.shape[1]] = (
                lt_ref[b * hc + r * q : b * hc + (r + 1) * q, :]
            )
        low_ref[r, blocks * q : blocks * q + 1, :] = vec_ref[...]
        out_ref[r, hc:, :] = low_ref[r].astype(BF)


def pack_kernels(kt, lt, vec, ranks, tall, deps):
    width = kt.shape[1]
    outs = [jax.ShapeDtypeStruct((ranks, kt.shape[0] // ranks + tall, width), BF)]
    scratch = [pltpu.VMEM((ranks, tall, width), F32)]
    return call(pack_kernels_body, outs, scratch, kt.size * 8, kt, lt, vec, deps=deps)[0]


def hop(v, k):
    n = 1
    for name in EVERY:
        n *= lax.axis_size(name)
    return lax.ppermute(v, EVERY, [(i, i ^ k) for i in range(n)])


def plane_gather(v, aside=()):
    got = {0: v}
    for k in (6, 2, 4):
        got[k] = hop(v, k)
    got[1] = hop(after_all(v, *aside) if aside else v, 1)
    for k in (2, 4, 6):
        got[k ^ 1] = hop(got[k], 1)
    return [got[k] for k in range(8)]


def plane_reduce(mate, keep, deps=()):
    sums = pair_sum(keep, hop(mate, 1), deps)
    arrived = {k: hop(sums[k // 2], k) for k in (6, 2, 4)}
    return [sums[0], arrived[2], arrived[4], arrived[6]]


def on_device(frames, cot, starts, ks, ktm, mg, mb, og, ob):
    nz, n_rank, n_seg = lax.axis_size("z"), 8, 4
    n_dp = nz * 2
    fr, side, ch = frames.shape[0], frames.shape[1], frames.shape[3]
    area = side * side
    hid = ks.shape[2]
    hc, cc = hid // n_rank, ch // n_rank
    q = hc // n_rank
    rank = lax.axis_index(PLANE)
    rank_now = rank.astype(jnp.int32).reshape(1)
    d_index = lax.axis_index(("z", "y"))
    nf = n_dp * fr
    pixels = area * nf
    half = pixels // 2

    def keeper(d, s):
        v = (d // 2) ^ s
        return (d % 2) * 4 + (v % 2) * 2 + v // 2

    to_plane = [
        (d * n_seg + s, s * n_rank + keeper(d, s)) for d in range(n_dp) for s in range(n_seg)
    ]
    from_plane = [(b, a) for a, b in to_plane]
    rows = fr * area
    flag_row = jnp.pad(starts.astype(BF)[None], ((0, 11), (0, ch - fr)))
    lead = rows + 12
    moving = jnp.concatenate([frames.reshape(rows, ch), flag_row, cot.reshape(rows, ch)], axis=0)
    moving = lax.ppermute(moving, EVERY, to_plane)

    perm = (jnp.arange(hid).reshape(n_rank, n_rank, q).transpose(1, 0, 2).reshape(hid)[:, None]
            == jnp.arange(hid)[None, :]).astype(BF)
    kt = lax.dot_general(perm, ks[0].astype(BF), (((1,), (1,)), ((), ())),
                         preferred_element_type=F32).astype(BF)
    lrows, width = ktm.shape[1] // n_rank, ks.shape[1]
    tall = -(-(lrows + 4) // 16) * 16
    extra = jnp.concatenate([mg, mb, og, ob], axis=1)
    extra = jnp.pad(extra, ((0, 0), (0, width - extra.shape[1])))
    w = pack_kernels(kt, ktm[0], extra, n_rank, tall, deps=(moving,))
    w = lax.all_to_all(w, PLANE, 0, 0)
    here = w
    high = hc + tall

    w = w.reshape(2, n_seg, high, width).transpose(1, 2, 0, 3).reshape(n_seg, high, 2 * width)
    ws = [lax.all_gather(w[s], "z", axis=0) for s in range(n_seg)]

    group = 7
    own = moving[lead:].reshape(group, rows // group, n_rank, cc).transpose(2, 1, 0, 3)
    own = own.reshape(n_rank, rows // group, group * cc)
    own = jnp.pad(own, ((0, 0), (0, 4), (0, ch - group * cc)))
    own = jnp.concatenate([jnp.broadcast_to(moving[:lead], (n_rank, lead, ch)), own], axis=1)
    gathered = lax.all_to_all(after_all(own, here), PLANE, 0, 0)


    def norm_rows(rows_now):
        row = rows_now[:, (lrows - tall) % 16].reshape(n_dp, width).astype(F32)
        mid = jnp.stack([
            lax.dynamic_slice_in_dim(row[:, i * hc : (i + 1) * hc], rank * q, q, axis=1).reshape(hc)
            for i in range(2)])
        own = lax.dynamic_index_in_dim(row, rank, 0, keepdims=False)
        out = jnp.stack([
            jnp.tile(own[2 * hc + i * cc : 2 * hc + (i + 1) * cc], 2) for i in range(2)])
        return mid, out

    def by_pixel(v):
        width = v.shape[2]
        v = v.reshape(n_rank * fr, area, width).transpose(1, 0, 2)
        return v.reshape(pixels, width)

    def packed(v):
        return jnp.concatenate([v[:half], v[half:]], axis=1)

    a0 = by_pixel(gathered[:, :rows])
    flags = gathered[:, rows, :fr].reshape(nf) > 0.5
    slot = jnp.arange(nf) % fr
    before = jnp.where(flags | (slot == 0), 0.0, 1.0)
    after = jnp.where(jnp.roll(flags, -1) | (slot == fr - 1), 0.0, 1.0)
    spread = (side * nf + nf, hc)
    before = jnp.broadcast_to(jnp.tile(before, side + 1)[:, None], spread)
    after = jnp.broadcast_to(jnp.tile(after, side + 1)[:, None], spread)
    skip = packed(lax.dynamic_slice_in_dim(a0, rank * cc, cc, axis=1))

    def across(*slices):
        n = len(slices)
        v = jnp.stack([jnp.concatenate([v[:, :cc], v[:, cc:]], axis=0) for v in slices])
        v = v.reshape(n, area, n_rank, fr, cc).transpose(2, 0, 1, 3, 4).reshape(n_rank, n * rows, cc)
        return lax.all_to_all(v, PLANE, 0, 0)

    def home(v):
        n = v.shape[1] // rows
        v = v.transpose(1, 0, 2).reshape(n * rows, ch)
        v = lax.ppermute(v, EVERY, from_plane).reshape(n, area, fr, ch).transpose(0, 2, 1, 3)
        return v.reshape(n, *frames.shape)

    saved = []
    g = [a0]
    ready = prepare(ws[0], hc, ch, deps=(before, after))
    for s in range(n_seg):
        kn, lt, lnt, rows_now = ready
        mid, out = norm_rows(rows_now)
        pad, hidden, xm, rm, mate, keep = conv_forward(
            rank_now, g, kn, lt, mid, before, after, side, pixels, ch)
        parts = plane_reduce(mate, keep)
        xo, ro, pre, res = out_norm(parts, out, skip if s % 2 == 1 else None)
        saved.append((pad, hidden, xm, rm, xo, ro, pre, lnt, mid, out))
        if s % 2 == 1:
            skip = res
        if s < n_seg - 1:
            ready = prepare(ws[s + 1], hc, ch, deps=(res,))
            g = plane_gather(res, ready[:1])
    cot_own = gathered[:, lead : lead + rows // group, : group * cc]
    cot_own = cot_own.reshape(n_rank, rows // group, group, cc).transpose(0, 2, 1, 3)
    cot_own = packed(by_pixel(cot_own.reshape(n_rank, rows, cc)))

    parts = [cot_own]
    skip_grad = None

    grads, raw = [], None
    for s in reversed(range(n_seg)):
        pad, hidden, xm, rm, xo, ro, pre, lnt, mid, out = saved[s]
        if s == 1:
            parts = parts + [skip_grad]
        deps = () if raw is None else (raw, *grads[len(grads) - 1 :])
        dpre, dt, osum = out_back(parts, pre, xo, ro, out, deps=deps)
        if raw is not None:
            grads.append(lax.psum_scatter(after_all(raw, dt), "z", scatter_dimension=0))
        if s % 2 == 1:
            skip_grad = dpre
        dtf, ds, msum, mate, keep = conv_back(
            rank_now, plane_gather(dt), xm, rm, ws[s], lnt, mid, before, after, side)
        if s > 0:
            parts = plane_reduce(mate, keep)
        raw = kernel_grads(pad, hidden, ds, dtf, before, after, msum, osum, side, ws[s].shape,
                           deps=parts[:1] if s > 0 else ())
    last = lax.psum_scatter(raw, "z", scatter_dimension=0)
    parts = plane_reduce(mate, keep, deps=(raw,))

    da = sum(p.astype(F32) for p in parts) + skip_grad.astype(F32)
    home_now = home(across(res, da.astype(BF)))
    output, frames_grad = home_now[0], home_now[1].astype(F32)

    def by_row(v):
        return v.reshape(high, 2, width).transpose(1, 0, 2)

    g = jnp.stack([by_row(v) for v in [last] + grads[::-1]], axis=1).reshape(n_rank, high, width)
    g = lax.all_to_all(g, PLANE, 0, 0)
    space_grad = lax.dot_general(g[:, :hc].reshape(hid, width), perm, (((0,), (0,)), ((), ())),
                                 preferred_element_type=F32)
    tg = g[:, hc : hc + lrows, :ch].reshape(n_rank, -1, q, ch)
    time_grad = tg.transpose(1, 0, 2, 3).reshape(-1, ch).astype(F32)
    sums = g[:, hc + lrows : hc + lrows + 4].astype(F32)

    def mid_own(v):
        return lax.dynamic_slice_in_dim(v[:, :hc], d_index * q, q, axis=1).reshape(1, hc)

    own = lax.dynamic_index_in_dim(sums, d_index, 0, keepdims=False)
    return (
        output,
        frames_grad,
        space_grad[None],
        time_grad[None],
        mid_own(sums[:, 0]),
        mid_own(sums[:, 1]),
        own[2:3, :cc],
        own[3:4, :cc],
    )


def from_behind(value, axis, steps):
    count = lax.axis_size(axis)
    leading, last = (max(0, -steps), min(count, count - steps))
    return lax.ppermute(value, axis, [(source, source + steps) for source in range(leading, last)])


def space_apply(current, kernel):
    frame_side = current.shape[1]
    padded = jnp.pad(current, ((0, 0), (1, 1), (1, 1), (0, 0)))
    stacked = jnp.concatenate(
        [
            padded[:, row_shift : row_shift + frame_side, col_shift : col_shift + frame_side, :]
            for row_shift in range(3)
            for col_shift in range(3)
        ],
        axis=-1,
    )
    return (
        stacked,
        jnp.einsum("fijc,co->fijo", stacked, kernel, preferred_element_type=jnp.float32),
    )


def space_back(gradient, kernel):
    frame_side = gradient.shape[1]
    channels = kernel.shape[0] // 9
    spread = jnp.einsum("fijo,co->fijc", gradient, kernel, preferred_element_type=jnp.float32)
    total = jnp.zeros((gradient.shape[0], frame_side + 2, frame_side + 2, channels), jnp.float32)
    for tap_index in range(9):
        row_shift = tap_index // 3
        col_shift = tap_index % 3
        piece_now = spread[..., tap_index * channels : (tap_index + 1) * channels]
        total = total + jnp.pad(
            piece_now, ((0, 0), (row_shift, 2 - row_shift), (col_shift, 2 - col_shift), (0, 0))
        )
    return total[:, 1 : frame_side + 1, 1 : frame_side + 1, :]


def time_apply(current, kernel, before_mask, after_mask):
    blanks = jnp.zeros_like(current[:1])
    earlier = jnp.concatenate([blanks, current[:-1]], axis=0) * before_mask[
        :, None, None, None
    ].astype(current.dtype)
    later = jnp.concatenate([current[1:], blanks], axis=0) * after_mask[:, None, None, None].astype(
        current.dtype
    )
    stacked = jnp.concatenate([earlier, current, later], axis=-1)
    return (
        stacked,
        jnp.einsum("fijc,co->fijo", stacked, kernel, preferred_element_type=jnp.float32),
    )


def time_back(gradient, kernel, before_mask, after_mask):
    channels = kernel.shape[0] // 3
    spread = jnp.einsum("fijo,co->fijc", gradient, kernel, preferred_element_type=jnp.float32)
    early_part = spread[..., :channels] * before_mask[:, None, None, None]
    late_part = spread[..., 2 * channels :] * after_mask[:, None, None, None]
    blanks = jnp.zeros_like(early_part[:1])
    moved_early = jnp.concatenate([early_part[1:], blanks], axis=0)
    moved_late = jnp.concatenate([blanks, late_part[:-1]], axis=0)
    return spread[..., channels : 2 * channels] + moved_early + moved_late


def moments(values, pixel_count):
    average = lax.psum(jnp.sum(values, axis=(0, 1, 2)), "dp") / pixel_count
    centered = values - average
    spread = lax.psum(jnp.sum(centered * centered, axis=(0, 1, 2)), "dp") / pixel_count
    return (average, lax.rsqrt(spread + eps))


def reduce_back(gradient, normed):
    return lax.psum(
        (jnp.sum(gradient, axis=(0, 1, 2)), jnp.sum(gradient * normed, axis=(0, 1, 2))), "dp"
    )


def silu_slope(values):
    sigmoid_now = jax.nn.sigmoid(values)
    return sigmoid_now * (1.0 + values * (1.0 - sigmoid_now))


def pick_slot(stack, slot_index):
    return lax.dynamic_index_in_dim(stack, slot_index, 0, keepdims=False)


def store_slot(stack, value, slot_index, usable):
    previous = pick_slot(stack, slot_index)
    return lax.dynamic_update_index_in_dim(stack, jnp.where(usable, value, previous), slot_index, 0)


def on_device_general(
    frames, cotangent, starts, space_kernel, time_kernel, mid_gain, mid_bias, out_gain, out_bias
):
    n_segment = lax.axis_size("segment")
    n_data = lax.axis_size("dp")
    segment_index = lax.axis_index("segment")
    odd_segment = segment_index % 2 == 1
    last_segment = segment_index == n_segment - 1
    first_segment = segment_index == 0
    frame_count = frames.shape[0]
    frame_side = frames.shape[1]
    channels = frames.shape[3]
    hidden_units = mid_gain.shape[1] * n_data
    pixel_count = n_data * frame_count * frame_side * frame_side
    turns = 2 * n_segment - 1
    block_shape = (n_segment,) + frames.shape
    all_frames, all_cot, all_starts = (
        lax.all_gather(frames, "segment", axis=0, tiled=True),
        lax.all_gather(cotangent, "segment", axis=0, tiled=True),
        lax.all_gather(starts.astype(jnp.bfloat16), "segment", axis=0, tiled=True),
    )
    frame_stack = all_frames.reshape(block_shape)
    cot_stack = all_cot.reshape(block_shape)
    clip_flags = all_starts.astype(jnp.float32).reshape(n_segment, frame_count)
    positions = jnp.arange(frame_count)
    before_mask = jnp.where((clip_flags > 0.5) | (positions == 0), 0.0, 1.0)
    following = jnp.concatenate([clip_flags[:, 1:], jnp.ones((n_segment, 1), jnp.float32)], axis=1)
    after_mask = jnp.where(following > 0.5, 0.0, 1.0)
    gathered = (
        lax.all_gather(space_kernel[0].astype(jnp.bfloat16), "dp", axis=0, tiled=True),
        lax.all_gather(time_kernel[0].astype(jnp.bfloat16), "dp", axis=0, tiled=True),
        lax.all_gather(mid_gain[0].astype(jnp.bfloat16), "dp", axis=0, tiled=True),
        lax.all_gather(mid_bias[0].astype(jnp.bfloat16), "dp", axis=0, tiled=True),
        lax.all_gather(out_gain[0].astype(jnp.bfloat16), "dp", axis=0, tiled=True),
        lax.all_gather(out_bias[0].astype(jnp.bfloat16), "dp", axis=0, tiled=True),
    )
    space_low, time_low = (gathered[0], gathered[1])
    mid_gain_now = gathered[2].astype(jnp.float32)
    mid_bias_now = gathered[3].astype(jnp.float32)
    out_gain_now = gathered[4].astype(jnp.float32)
    out_bias_now = gathered[5].astype(jnp.float32)
    incoming = jnp.zeros_like(frames)
    carried = jnp.zeros_like(frames)
    kept_input = jnp.zeros(block_shape, jnp.bfloat16)
    kept_skip = jnp.zeros(block_shape, jnp.bfloat16)
    kept_mid_mean = jnp.zeros((n_segment, hidden_units), jnp.float32)
    kept_mid_scale = jnp.zeros((n_segment, hidden_units), jnp.float32)
    kept_out_mean = jnp.zeros((n_segment, channels), jnp.float32)
    kept_out_scale = jnp.zeros((n_segment, channels), jnp.float32)
    results = jnp.zeros(block_shape, jnp.float32)
    for turn_index in range(turns):
        micro_index = turn_index - segment_index
        usable = (micro_index >= 0) & (micro_index < n_segment)
        slot_index = jnp.clip(micro_index, 0, n_segment - 1)
        current = jnp.where(first_segment, pick_slot(frame_stack, slot_index), incoming)
        skip_input = carried
        _, spatial = space_apply(current, space_low)
        mid_mean, mid_scale = moments(spatial, pixel_count)
        hidden_act = jax.nn.silu(
            (spatial - mid_mean) * mid_scale * mid_gain_now + mid_bias_now
        ).astype(jnp.bfloat16)
        _, temporal = time_apply(
            hidden_act,
            time_low,
            pick_slot(before_mask, slot_index),
            pick_slot(after_mask, slot_index),
        )
        out_mean, out_scale = moments(temporal, pixel_count)
        pre_act = (
            (temporal - out_mean) * out_scale * out_gain_now
            + out_bias_now
            + jnp.where(odd_segment, skip_input.astype(jnp.float32), 0.0)
        )
        result = jax.nn.silu(pre_act).astype(jnp.bfloat16)
        kept_input = store_slot(kept_input, current, slot_index, usable)
        kept_skip = store_slot(kept_skip, skip_input, slot_index, usable)
        kept_mid_mean = store_slot(kept_mid_mean, mid_mean, slot_index, usable)
        kept_mid_scale = store_slot(kept_mid_scale, mid_scale, slot_index, usable)
        kept_out_mean = store_slot(kept_out_mean, out_mean, slot_index, usable)
        kept_out_scale = store_slot(kept_out_scale, out_scale, slot_index, usable)
        results = store_slot(results, result.astype(jnp.float32), slot_index, usable)
        if turn_index < turns - 1:
            incoming, carried = from_behind(
                (result, jnp.where(odd_segment, result, current)), "segment", 1
            )
    gathered = (
        lax.all_gather(space_kernel[0].astype(jnp.bfloat16), "dp", axis=0, tiled=True),
        lax.all_gather(time_kernel[0].astype(jnp.bfloat16), "dp", axis=0, tiled=True),
        lax.all_gather(mid_gain[0].astype(jnp.bfloat16), "dp", axis=0, tiled=True),
        lax.all_gather(mid_bias[0].astype(jnp.bfloat16), "dp", axis=0, tiled=True),
        lax.all_gather(out_gain[0].astype(jnp.bfloat16), "dp", axis=0, tiled=True),
        lax.all_gather(out_bias[0].astype(jnp.bfloat16), "dp", axis=0, tiled=True),
    )
    space_low, time_low = (gathered[0], gathered[1])
    mid_gain_now = gathered[2].astype(jnp.float32)
    mid_bias_now = gathered[3].astype(jnp.float32)
    out_gain_now = gathered[4].astype(jnp.float32)
    out_bias_now = gathered[5].astype(jnp.float32)
    grad_input = jnp.zeros_like(frames)
    grad_skip = jnp.zeros_like(frames)
    space_acc = jnp.zeros(space_low.shape, jnp.float32)
    time_acc = jnp.zeros(time_low.shape, jnp.float32)
    mid_gain_acc = jnp.zeros((hidden_units,), jnp.float32)
    mid_bias_acc = jnp.zeros((hidden_units,), jnp.float32)
    out_gain_acc = jnp.zeros((channels,), jnp.float32)
    out_bias_acc = jnp.zeros((channels,), jnp.float32)
    input_grads = jnp.zeros(block_shape, jnp.float32)
    for turn_index in range(turns):
        micro_index = n_segment - 1 - (turn_index - (n_segment - 1 - segment_index))
        usable = (micro_index >= 0) & (micro_index < n_segment)
        usable_weight = usable.astype(jnp.float32)
        slot_index = jnp.clip(micro_index, 0, n_segment - 1)
        current = pick_slot(kept_input, slot_index)
        skip_input = pick_slot(kept_skip, slot_index)
        before_now = pick_slot(before_mask, slot_index)
        after_now = pick_slot(after_mask, slot_index)
        space_taps, spatial = space_apply(current, space_low)
        mid_normed = (spatial - pick_slot(kept_mid_mean, slot_index)) * pick_slot(
            kept_mid_scale, slot_index
        )
        mid_pre = mid_normed * mid_gain_now + mid_bias_now
        hidden_act = jax.nn.silu(mid_pre).astype(jnp.bfloat16)
        time_taps, temporal = time_apply(hidden_act, time_low, before_now, after_now)
        out_scale = pick_slot(kept_out_scale, slot_index)
        out_normed = (temporal - pick_slot(kept_out_mean, slot_index)) * out_scale
        pre_act = (
            out_normed * out_gain_now
            + out_bias_now
            + jnp.where(odd_segment, skip_input.astype(jnp.float32), 0.0)
        )
        grad_result = jnp.where(
            last_segment,
            pick_slot(cot_stack, slot_index).astype(jnp.float32),
            grad_input.astype(jnp.float32)
            + jnp.where(odd_segment, grad_skip.astype(jnp.float32), 0.0),
        )
        grad_pre = grad_result * silu_slope(pre_act)
        out_bias_sum, out_gain_sum = reduce_back(grad_pre, out_normed)
        grad_temporal = (
            out_gain_now
            * out_scale
            * (grad_pre - out_bias_sum / pixel_count - out_normed * out_gain_sum / pixel_count)
        ).astype(jnp.bfloat16)
        time_acc = time_acc + usable_weight * jnp.einsum(
            "fijc,fijo->co", time_taps, grad_temporal, preferred_element_type=jnp.float32
        )
        grad_hidden = time_back(grad_temporal, time_low, before_now, after_now)
        grad_mid = grad_hidden * silu_slope(mid_pre)
        mid_bias_sum, mid_gain_sum = reduce_back(grad_mid, mid_normed)
        mid_scale = pick_slot(kept_mid_scale, slot_index)
        grad_spatial = (
            mid_gain_now
            * mid_scale
            * (grad_mid - mid_bias_sum / pixel_count - mid_normed * mid_gain_sum / pixel_count)
        ).astype(jnp.bfloat16)
        space_acc = space_acc + usable_weight * jnp.einsum(
            "fijc,fijo->co", space_taps, grad_spatial, preferred_element_type=jnp.float32
        )
        grad_current = space_back(grad_spatial, space_low)
        mid_gain_acc = mid_gain_acc + usable_weight * mid_gain_sum
        mid_bias_acc = mid_bias_acc + usable_weight * mid_bias_sum
        out_gain_acc = out_gain_acc + usable_weight * out_gain_sum
        out_bias_acc = out_bias_acc + usable_weight * out_bias_sum
        input_grads = store_slot(
            input_grads, grad_current + grad_skip.astype(jnp.float32), slot_index, usable
        )
        if turn_index < turns - 1:
            grad_input, grad_skip = from_behind(
                (
                    grad_current.astype(jnp.bfloat16),
                    jnp.where(odd_segment, grad_pre.astype(jnp.bfloat16), grad_skip),
                ),
                "segment",
                -1,
            )
    space_grad, time_grad = (
        lax.psum_scatter(space_acc, "dp", scatter_dimension=0, tiled=True),
        lax.psum_scatter(time_acc, "dp", scatter_dimension=0, tiled=True),
    )
    data_index = lax.axis_index("dp")

    def own_share(full_vector):
        share = full_vector.shape[0] // n_data
        return lax.dynamic_slice_in_dim(full_vector, data_index * share, share)[None]

    flat_shape = (n_segment * frame_count,) + frames.shape[1:]
    arrived_out, arrived_grads = (
        lax.all_to_all(
            results.reshape(flat_shape).astype(jnp.bfloat16),
            "segment",
            split_axis=0,
            concat_axis=0,
            tiled=True,
        ).astype(jnp.float32),
        lax.all_to_all(
            input_grads.reshape(flat_shape).astype(jnp.bfloat16),
            "segment",
            split_axis=0,
            concat_axis=0,
            tiled=True,
        ).astype(jnp.float32),
    )
    output = arrived_out[(n_segment - 1) * frame_count :].astype(jnp.bfloat16)
    frames_grad = arrived_grads[:frame_count]
    return (
        output,
        frames_grad,
        space_grad[None],
        time_grad[None],
        own_share(mid_gain_acc),
        own_share(mid_bias_acc),
        own_share(out_gain_acc),
        own_share(out_bias_acc),
    )


def general(mesh):
    return jax.shard_map(
        on_device_general,
        mesh=mesh,
        in_specs=(
            P(("dp", "segment"), None, None, None),
            P(("dp", "segment"), None, None, None),
            P(("dp", "segment")),
            P("segment", "dp", None),
            P("segment", "dp", None),
            P("segment", "dp"),
            P("segment", "dp"),
            P("segment", "dp"),
            P("segment", "dp"),
        ),
        out_specs=(
            P(("dp", "segment"), None, None, None),
            P(("dp", "segment"), None, None, None),
            P("segment", "dp", None),
            P("segment", "dp", None),
            P("segment", "dp"),
            P("segment", "dp"),
            P("segment", "dp"),
            P("segment", "dp"),
        ),
        check_vma=False,
    )


def solution(mesh):
    if mesh.shape["dp"] != 8 or mesh.shape["segment"] != 4:
        return general(mesh)
    n_dp, n_seg = mesh.shape["dp"], mesh.shape["segment"]
    fine = Mesh(mesh.devices.reshape(n_dp // 2, 2, 2, n_seg // 2), EVERY)
    dp, seg = ("z", "y"), ("x", "c")
    return jax.shard_map(
        on_device,
        mesh=fine,
        in_specs=(
            P(EVERY, None, None, None),
            P(EVERY, None, None, None),
            P(EVERY),
            P(seg, dp, None),
            P(seg, dp, None),
            P(seg, dp),
            P(seg, dp),
            P(seg, dp),
            P(seg, dp),
        ),
        out_specs=(
            P(EVERY, None, None, None),
            P(EVERY, None, None, None),
            P(seg, dp, None),
            P(seg, dp, None),
            P(seg, dp),
            P(seg, dp),
            P(seg, dp),
            P(seg, dp),
        ),
        check_vma=False,
    )
```
